32 devices in a mesh: gx: 4 (over x, core), gy: 8 (over z, y).
Axes of the slice: x: 2, y: 2, z: 4, core: 2. Of those that a mesh axis runs over, the one named last changes fastest.
Arguments:
- state: float32 [2, 8, 128, 512], P(None, None, 'gy', 'gx'), may hold values from 0 to 1, as said below
- previous: float32 [2, 8, 128, 512], P(None, None, 'gy', 'gx'), may hold values from 0 to 1
- feed: float32 [8, 128, 512], P(None, 'gy', 'gx'), may hold values from 0.01 to 0.1
- kill: float32 [8, 128, 512], P(None, 'gy', 'gx'), may hold values from 0.03 to 0.1
Outputs:
- correction: float32 [2, 8, 128, 512], P(None, None, 'gy', 'gx')
The draws below stay inside these ranges and needn't reach their ends.
Inputs may be any that keep to these rules, and one draw needn't show every extreme that they name: `state`: u and v of every cell lie in the stated range.
All inputs are finite; a program needn't handle non-finite values.
Results may differ from the reference program's by a relative error of at most 0.0001.
Values sent between devices are 32-bit elements; how exact they have to be, the bound alone decides.
No kernel may reach another device: no remote copies, remote signals or barrier semaphores. Data moves between devices by JAX's collectives and lax.ppermute only.
A program may use at most 128 MiB of HBM per device.

```python
import math
import jax
import jax.numpy as jnp

NX = 512
NY = 128
NZ = 8


def draw_state(key, part):
    first_key = jax.random.fold_in(key, 11)
    second_key = jax.random.fold_in(key, 23)
    shape = (NZ, NY, NX)
    cols = jnp.arange(NX, dtype=jnp.float32).reshape(1, 1, NX)
    rows = jnp.arange(NY, dtype=jnp.float32).reshape(1, NY, 1)
    across = 0.5 + 0.5 * jnp.cos(2.0 * math.pi * cols / NX)
    down = 0.5 + 0.5 * jnp.cos(2.0 * math.pi * rows / NY)
    envelope = 0.08 + 0.92 * across * down
    substrate = jax.random.uniform(first_key, shape, jnp.float32)
    catalyst = envelope * jax.random.uniform(second_key, shape, jnp.float32)
    return jnp.stack([substrate, catalyst]).astype(jnp.float32)


def level_of(key, dims, shards, least, largest):
    gain = 1.0
    for axis_at, parts in shards:
        draws = jax.random.uniform(jax.random.fold_in(jax.random.fold_in(key, 6), axis_at), (parts,), jnp.float32, least / len(shards), largest / len(shards))
        gain = gain * jnp.repeat(jnp.exp(draws), dims[axis_at] // parts).reshape((-1,) + (1,) * (len(dims) - 1 - axis_at))
    return gain


def setup_inputs(seed: int = 0) -> dict:
    seeds = jax.random.split(jax.random.key(seed), 5)
    return {
        "state": draw_state(jax.random.fold_in(seeds[4], 71), 0),
        "previous": jnp.clip(1.0 * jax.random.uniform(seeds[1], (2, NZ, NY, NX), jnp.float32) ** level_of(seeds[1], (2, NZ, NY, NX), ((2, 8), (3, 4)), -0.2, 0.2), 0.0, 1.0),
        "feed": jnp.clip(jnp.exp(math.log(0.1) - 2.3025851 * jax.random.uniform(seeds[2], (NZ, NY, NX), jnp.float32) ** level_of(seeds[2], (NZ, NY, NX), ((1, 8), (2, 4)), -0.2, 0.2)), 0.01, 0.1),
        "kill": jnp.clip(jnp.exp(math.log(0.1) - 1.2039728 * jax.random.uniform(seeds[3], (NZ, NY, NX), jnp.float32) ** level_of(seeds[3], (NZ, NY, NX), ((1, 8), (2, 4)), -0.2, 0.2)), 0.03, 0.1),
    }


substrate_diffusion = 40.0
catalyst_diffusion = 20.0
inverse_step = 2.0
lower_fraction = 0.25
coarsenings = 2


def neighbour_sum(field):
    along_x = jnp.roll(field, 1, 3) + jnp.roll(field, -1, 3)
    along_y = jnp.roll(field, 1, 2) + jnp.roll(field, -1, 2)
    along_z = jnp.roll(field, 1, 1) + jnp.roll(field, -1, 1)
    return along_x + along_y + along_z


def restrict(field):
    lead, depth, rows, cols = field.shape
    blocks = field.reshape(lead, depth // 2, 2, rows // 2, 2, cols // 2, 2)
    return jnp.mean(blocks, axis=(2, 4, 6))


def prolong(field):
    return jnp.repeat(jnp.repeat(jnp.repeat(field, 2, 1), 2, 2), 2, 3)


def diffusions(level):
    scale = 0.25 ** level
    return jnp.array([substrate_diffusion * scale, catalyst_diffusion * scale], jnp.float32).reshape(2, 1, 1, 1)


def coefficients(fields, level):
    scale = 0.25 ** level
    diff_first = substrate_diffusion * scale
    diff_second = catalyst_diffusion * scale
    substrate, catalyst, feed_rate, kill_rate = fields[0], fields[1], fields[2], fields[3]
    product = substrate * catalyst
    squared = catalyst * catalyst
    self_first = inverse_step + squared + feed_rate + 6.0 * diff_first
    cross_first = 2.0 * product
    cross_second = -squared
    self_second = inverse_step + feed_rate + kill_rate - 2.0 * product + 6.0 * diff_second
    coeff = jnp.stack([self_first, cross_first, cross_second, self_second])
    spread = jnp.maximum(jnp.max((6.0 * diff_first + cross_first) / self_first),
                         jnp.max((6.0 * diff_second + squared) / self_second))
    return coeff, spread


def apply_operator(coeff, field, neighbours, level):
    first = coeff[0] * field[0] + coeff[1] * field[1]
    second = coeff[2] * field[0] + coeff[3] * field[1]
    return jnp.stack([first, second]) - diffusions(level) * neighbours


def chebyshev(operate, coeff, source, start, spread):
    upper = 1.0 + spread
    lower = lower_fraction * upper
    centre = (upper + lower) / 2.0
    half_width = (upper - lower) / 2.0
    ratio = centre / half_width
    damping = 1.0 / ratio
    diagonal = jnp.stack([coeff[0], coeff[3]])
    if start is None:
        resid = source / diagonal
        update = resid / centre
        iterate = update
    else:
        resid = (source - operate(start)) / diagonal
        update = resid / centre
        iterate = start + update
    for sweep in range(2):
        resid = (source - operate(iterate)) / diagonal
        damping_next = 1.0 / (2.0 * ratio - damping)
        update = damping_next * damping * update + (2.0 * damping_next / half_width) * resid
        iterate = iterate + update
        damping = damping_next
    return iterate


def vcycle(level, source, coeffs, spreads):
    coeff = coeffs[level]
    spread = spreads[level]

    def operate(field):
        return apply_operator(coeff, field, neighbour_sum(field), level)

    iterate = chebyshev(operate, coeff, source, None, spread)
    if level < coarsenings:
        resid = source - operate(iterate)
        iterate = iterate + prolong(vcycle(level + 1, restrict(resid), coeffs, spreads))
    return chebyshev(operate, coeff, source, iterate, spread)


def reference(state, previous, feed, kill):
    fields = jnp.concatenate([state, feed[None], kill[None]], 0)
    coeffs = []
    spreads = []
    for level in range(coarsenings + 1):
        coeff, spread = coefficients(fields, level)
        coeffs.append(coeff)
        spreads.append(spread)
        if level < coarsenings:
            fields = restrict(fields)
    substrate, catalyst = state[0], state[1]
    reaction = substrate * catalyst * catalyst
    laplace = neighbour_sum(state) - 6.0 * state
    local_terms = jnp.stack([reaction - feed * (1.0 - substrate), -reaction + (feed + kill) * catalyst])
    nonlinear = inverse_step * (state - previous) - diffusions(0) * laplace + local_terms
    return vcycle(0, -nonlinear, coeffs, spreads)
```

```python
import functools

import jax
import jax.numpy as jnp
from jax import lax
from jax.experimental import pallas as pl
from jax.experimental.pallas import tpu as pltpu
from jax.sharding import PartitionSpec as P

DIFF = (40.0, 20.0)
INV_STEP = 2.0
LOWER = 0.25

_CENTRE = (1.0 + LOWER) / 2.0
_HALF = (1.0 - LOWER) / 2.0
_SIGMA = _CENTRE / _HALF
_RHO0 = 1.0 / _SIGMA
_RHO1 = 1.0 / (2.0 * _SIGMA - _RHO0)
_RHO2 = 1.0 / (2.0 * _SIGMA - _RHO1)

Z = 8
X = 128
HALO0 = 4
WIDE = 42
PER = X // WIDE
EDGE = 3
CHUNK = 4


def lane_of():
    return lax.broadcasted_iota(jnp.int32, (1, Z, X), 2)


def sub_of():
    return lax.broadcasted_iota(jnp.int32, (1, Z, X), 1)


def roll_x(tile, shift):
    shift = shift % X
    return pltpu.roll(tile, shift, 2) if shift else tile


def roll_z(tile, shift):
    shift = shift % Z
    return pltpu.roll(tile, shift, 1) if shift else tile


def rows_loop(lo, hi, body, step=CHUNK):
    full = (hi - lo) // step
    if full == 1:
        body(lo, step)
    elif full > 1:

        def trip(i, carry):
            body(lo + i * step, step)
            return carry

        lax.fori_loop(0, full, trip, 0)
    rest = hi - lo - full * step
    if rest:
        body(hi - rest, rest)


def neighbour_sums(read, r, n, k):
    lane = lane_of()
    low, high = lane < k, lane >= X - k
    centre = [read(t, r, n) for t in (0, 1)]
    right = [roll_x(c, k) for c in centre]
    left = [roll_x(c, -k) for c in centre]
    sums = []
    for t in (0, 1):
        c = centre[t]
        along_x = jnp.where(low, right[1 - t], right[t]) + jnp.where(high, left[1 - t], left[t])
        along_y = read(t, r - 1, n) + read(t, r + 1, n)
        along_z = 2.0 * roll_z(c, k) if 2 * k == Z else roll_z(c, k) + roll_z(c, -k)
        sums.append(along_x + along_y + along_z)
    return centre, sums


def jacobian(u, v, f, k, level):
    scale = 0.25**level
    product = u * v
    squared = v * v
    first = INV_STEP + squared + f + 6.0 * DIFF[0] * scale
    second = INV_STEP + f + k - 2.0 * product + 6.0 * DIFF[1] * scale
    return 2.0 * product, squared, 1.0 / first, 1.0 / second, first, second


def cheb_step(level, keep, source, target, d, r, n, carry, gain):
    scale = 0.25**level
    k = 1 << level
    u, nb_u = neighbour_sums(lambda t, a, m: source[0, t, pl.ds(a, m)], r, n, k)
    v, nb_v = neighbour_sums(lambda t, a, m: source[1, t, pl.ds(a, m)], r, n, k)
    rows = pl.ds(r, n)
    for t in (0, 1):
        cross, squared, inv_u, inv_v = (keep[i, t, rows] for i in range(4))
        res_u = inv_u * (keep[4, t, rows] - cross * v[t] + DIFF[0] * scale * nb_u[t]) - u[t]
        res_v = inv_v * (keep[5, t, rows] + squared * u[t] + DIFF[1] * scale * nb_v[t]) - v[t]
        du, dv = gain * res_u, gain * res_v
        if carry is not None:
            du = du + carry * d[0, t, rows]
            dv = dv + carry * d[1, t, rows]
        d[0, t, rows] = du
        d[1, t, rows] = dv
        target[0, t, rows] = u[t] + du
        target[1, t, rows] = v[t] + dv


def cheb_first(keep, target, d, r, n, gain):
    rows = pl.ds(r, n)
    for t in (0, 1):
        for i in (0, 1):
            value = gain * keep[2 + i, t, rows] * keep[4 + i, t, rows]
            d[i, t, rows] = value
            target[i, t, rows] = value


def residual(level, keep, diag, source, r, n):
    scale = 0.25**level
    k = 1 << level
    u, nb_u = neighbour_sums(lambda t, a, m: source[0, t, pl.ds(a, m)], r, n, k)
    v, nb_v = neighbour_sums(lambda t, a, m: source[1, t, pl.ds(a, m)], r, n, k)
    rows = pl.ds(r, n)
    first, second = [], []
    for t in (0, 1):
        first.append(
            keep[4, t, rows] - diag[0, t, rows] * u[t] - keep[0, t, rows] * v[t] + DIFF[0] * scale * nb_u[t]
        )
        second.append(
            keep[5, t, rows] - diag[1, t, rows] * v[t] + keep[1, t, rows] * u[t] + DIFF[1] * scale * nb_v[t]
        )
    return first, second


def gains(spread, level):
    top = jnp.max(spread.reshape(-1, Z, X), axis=0)
    row = lax.broadcasted_iota(jnp.int32, (Z, X), 0)
    top = jnp.max(jnp.where(row == level, top, 0.0), axis=0, keepdims=True)
    tau = 1.0 / (1.0 + jnp.broadcast_to(top, (Z, X)))
    return tau / _CENTRE, (2.0 * _RHO1 / _HALF) * tau, (2.0 * _RHO2 / _HALF) * tau


CARRY1 = _RHO1 * _RHO0
CARRY2 = _RHO2 * _RHO1


def pair_rows(value):
    n = value.shape[0] // 2
    pairs = value.reshape(n, 2, Z, X)
    return pairs[:, 0] + pairs[:, 1]


def pair_partner_x(tile, k, phase):
    return tile + (roll_x(tile, k) if phase else roll_x(tile, -k))


def pair_partner_z(tile, k, phase):
    return tile + (roll_z(tile, k) if phase else roll_z(tile, -k))


def spread_x(tile, k, phase):
    lane = lane_of()
    return jnp.where((lane & k) == (k if phase else 0), tile, roll_x(tile, -k if phase else k))


def spread_z(tile, k, phase):
    sub = sub_of()
    return jnp.where((sub & k) == (k if phase else 0), tile, roll_z(tile, -k if phase else k))


def restrict_packed(levels, k, pick):
    width = 2 * k
    lane, sub = lane_of() & (width - 1), sub_of() & (width - 1)
    out = None
    for i in range(width):
        across = None
        for j in range(width):
            value = pair_partner_x(pick(i, j), k, j & k)
            across = value if across is None else jnp.where(lane == j, value, across)
        value = pair_partner_z(across, k, i & k)
        out = value if out is None else jnp.where(sub == i, value, out)
    return out * 0.125


def unpack(tile, k, i, j):
    bit = 1
    while bit < k:
        tile = spread_x(tile, bit, j & bit)
        tile = spread_z(tile, bit, i & bit)
        bit *= 2
    return tile


def plane(ref, f, y, rows):
    return ref[pl.ds(f * Z * rows + y, Z, stride=rows), :]


def pack_y_kernel(rows, state, previous, feed, kill, to_prev, to_next):
    fields = [(state, 0), (state, 1), (previous, 0), (previous, 1), (feed, 0), (kill, 0)]
    for i, (ref, f) in enumerate(fields):
        for j in range(HALO0):
            to_prev[i * HALO0 + j] = plane(ref, f, j, rows)
            to_next[i * HALO0 + j] = plane(ref, f, rows - HALO0 + j, rows)


def spread_kernel(rows, state, feed, kill, out, fields):
    for y in range(rows):
        fields[0, y] = plane(state, 0, y, rows)
        fields[1, y] = plane(state, 1, y, rows)
        fields[2, y] = plane(feed, 0, y, rows)
        fields[3, y] = plane(kill, 0, y, rows)
    result = jnp.zeros((Z, X), jnp.float32)
    row = lax.broadcasted_iota(jnp.int32, (Z, X), 0)
    for level in range(3):
        n = rows >> level
        u, v, f, k = (fields[i, 0:n] for i in range(4))
        scale = 0.25**level
        cross, squared, inv_u, inv_v, _, _ = jacobian(u, v, f, k, level)
        both = jnp.maximum((6.0 * DIFF[0] * scale + cross) * inv_u, (6.0 * DIFF[1] * scale + squared) * inv_v)
        top = jnp.max(both, axis=0)
        top = jnp.max(jnp.max(top, axis=1, keepdims=True), axis=0, keepdims=True)
        result = jnp.where(row == level, jnp.broadcast_to(top, (Z, X)), result)
        if level < 2:
            span = 1 << level
            for i in range(4):
                summed = pair_rows(fields[i, 0:n])
                lane, sub = lane_of(), sub_of()
                summed = jnp.where(
                    (lane & span) == 0, pair_partner_x(summed, span, 0), pair_partner_x(summed, span, span)
                )
                summed = jnp.where(
                    (sub & span) == 0, pair_partner_z(summed, span, 0), pair_partner_z(summed, span, span)
                )
                fields[i, 0 : n // 2] = summed * 0.125
    out[...] = result


def fill_main(rows, state, previous, feed, kill, from_prev, from_next, fields):
    sources = [(state, 0), (state, 1), (previous, 0), (previous, 1), (feed, 0), (kill, 0)]
    for i, (ref, f) in enumerate(sources):
        fields[i, 0, 0:HALO0] = from_prev[i * HALO0 : (i + 1) * HALO0]
        fields[i, 0, HALO0 + rows : rows + 2 * HALO0] = from_next[i * HALO0 : (i + 1) * HALO0]
        for y in range(rows):
            fields[i, 0, HALO0 + y] = plane(ref, f, y, rows)


def pack_x_kernel(rows, state, previous, feed, kill, from_prev, from_next, to_left, to_right, fields):
    fill_main(rows, state, previous, feed, kill, from_prev, from_next, fields)
    total = rows + 2 * HALO0
    group = total // PER
    lane = lane_of()
    for i in range(6):
        left, right = None, None
        for j in range(PER):
            part = fields[i, 0, j * group : (j + 1) * group]
            a = roll_x(part, WIDE * j)
            b = roll_x(part, WIDE + WIDE * j)
            if j == 0:
                left, right = a, b
            else:
                left = jnp.where(lane >= WIDE * j, a, left)
                right = jnp.where(lane >= WIDE * j, b, right)
        to_left[i * group : (i + 1) * group] = left
        to_right[i * group : (i + 1) * group] = right


def fill_halo(rows, from_left, from_right, fields):
    total = rows + 2 * HALO0
    group = total // PER
    lane = lane_of()
    for i in range(6):
        left = from_left[i * group : (i + 1) * group]
        right = from_right[i * group : (i + 1) * group]
        for j in range(PER):
            value = jnp.where(lane < X // 2, roll_x(right, -WIDE * j), roll_x(left, X - WIDE - WIDE * j))
            fields[i, 1, j * group : (j + 1) * group] = value


def level0_kernel(
    rows,
    state,
    previous,
    feed,
    kill,
    from_prev,
    from_next,
    from_left,
    from_right,
    spread,
    packet,
    edge_prev,
    edge_next,
    keep,
    fields,
    other,
    d,
    diag,
):
    total = rows + 2 * HALO0
    fill_main(rows, state, previous, feed, kill, from_prev, from_next, fields)
    fill_halo(rows, from_left, from_right, fields)
    g0, g1, g2 = gains(spread[...], 0)
    here = keep.at[6:8]

    def setup(r, n):
        at = pl.ds(r, n)
        u, nb_u = neighbour_sums(lambda t, a, m: fields[0, t, pl.ds(a, m)], r, n, 1)
        v, nb_v = neighbour_sums(lambda t, a, m: fields[1, t, pl.ds(a, m)], r, n, 1)
        for t in (0, 1):
            f, k = fields[4, t, at], fields[5, t, at]
            cross, squared, inv_u, inv_v, first, second = jacobian(u[t], v[t], f, k, 0)
            react = u[t] * squared
            b_u = (
                DIFF[0] * (nb_u[t] - 6.0 * u[t])
                - INV_STEP * (u[t] - fields[2, t, at])
                - react
                + f * (1.0 - u[t])
            )
            b_v = (
                DIFF[1] * (nb_v[t] - 6.0 * v[t]) - INV_STEP * (v[t] - fields[3, t, at]) + react - (f + k) * v[t]
            )
            for i, value in enumerate((cross, squared, inv_u, inv_v, b_u, b_v)):
                keep[i, t, at] = value
            diag[0, t, at] = first
            diag[1, t, at] = second
            for i, value in enumerate((g0 * inv_u * b_u, g0 * inv_v * b_v)):
                d[i, t, at] = value
                keep[6 + i, t, at] = value

    rows_loop(1, total - 1, setup)
    rows_loop(2, total - 2, lambda r, n: cheb_step(0, keep, here, other, d, r, n, CARRY1, g1))
    rows_loop(3, total - 3, lambda r, n: cheb_step(0, keep, other, here, d, r, n, CARRY2, g2))

    def down(r, n):
        first, second = residual(0, keep, diag, here, r, n)
        out = (r - HALO0) // 4
        for t in (0, 1):
            at = pl.ds(r, n)
            values = [first[t], second[t], fields[0, t, at], fields[1, t, at], fields[4, t, at], fields[5, t, at]]
            sums = [pair_rows(value) for value in values]
            for p in range(3):
                packed = restrict_packed(0, 1, lambda i, j: sums[2 * p + i][j : j + 1])
                packet[p, t, pl.ds(out, 1)] = packed

    rows_loop(HALO0, HALO0 + rows, down, 4)

    lane = lane_of()
    for edge, start in ((edge_prev, HALO0), (edge_next, HALO0 + rows - EDGE)):
        halo = None
        for i in (0, 1):
            for j in range(EDGE):
                at = i * EDGE + j
                edge[at] = keep[6 + i, 0, start + j]
                value = roll_x(keep[6 + i, 1, start + j : start + j + 1], 4 + 8 * at)
                halo = value if halo is None else jnp.where((lane >> 3) == at, value, halo)
        edge[2 * EDGE : 2 * EDGE + 1] = halo


def level1_kernel(
    rows, own, above, below, spread, edge_prev, edge_next, packet, to_prev, to_next, keep, other, d, diag, fields
):
    total = 3 * rows
    g0, g1, g2 = gains(spread[...], 1)
    here = keep.at[6:8]

    for part, ref in enumerate((above, own, below)):

        def take(r, n, part=part, ref=ref):
            for p in range(3):
                for t in (0, 1):
                    tile = ref[p, t, pl.ds(r, n)]
                    for i in (0, 1):
                        a = unpack(tile, 2, i, 0)
                        b = unpack(tile, 2, i, 1)
                        value = jnp.stack([a, b], axis=1).reshape(2 * n, Z, X)
                        at = pl.ds(part * rows + 2 * r, 2 * n)
                        if p == 0:
                            keep[4 + i, t, at] = value
                        else:
                            fields[2 * (p - 1) + i, t, at] = value

        rows_loop(0, rows // 2, take, 2)

    def setup(r, n):
        at = pl.ds(r, n)
        for t in (0, 1):
            u, v, f, k = (fields[i, t, at] for i in range(4))
            cross, squared, inv_u, inv_v, first, second = jacobian(u, v, f, k, 1)
            for i, value in enumerate((cross, squared, inv_u, inv_v)):
                keep[i, t, at] = value
            diag[0, t, at] = first
            diag[1, t, at] = second
            for i, value in enumerate((g0 * inv_u * keep[4, t, at], g0 * inv_v * keep[5, t, at])):
                d[i, t, at] = value
                keep[6 + i, t, at] = value

    rows_loop(1, total - 1, setup)
    rows_loop(2, total - 2, lambda r, n: cheb_step(1, keep, here, other, d, r, n, CARRY1, g1))
    rows_loop(3, total - 3, lambda r, n: cheb_step(1, keep, other, here, d, r, n, CARRY2, g2))

    first, second = residual(1, keep, diag, here, rows, rows)
    for t in (0, 1):
        sums = [pair_rows(value) for value in (first[t], second[t])]
        sums += [pair_rows(fields[i, t, rows : 2 * rows]) for i in range(4)]
        for p in (0, 1):
            names = (2, 3, 4, 5) if p == 0 else (0, 1, 0, 1)
            value = restrict_packed(1, 2, lambda i, j: sums[names[i]][j : j + 1])
            for ref in (packet, to_prev, to_next):
                ref[2 * p + t : 2 * p + t + 1] = value
    to_prev[4 : 4 + 2 * EDGE + 1] = edge_prev[...]
    to_next[4 : 4 + 2 * EDGE + 1] = edge_next[...]


def level2_kernel(
    rows, spread, own, far_prev, near_prev, near_next, far_next, keep0, keep1, out, keep2, x2, y2, d2, x1, y1, x0, y0, d0
):
    rows1, rows2 = rows // 2, rows // 4
    total = 5 * rows2
    g0, g1, g2 = gains(spread[...], 2)

    for part, ref in enumerate((far_prev, near_prev, own, near_next, far_next)):
        for t in (0, 1):
            fields = []
            for i in range(4):
                parts = [unpack(ref[t : t + 1], 4, i, j) for j in range(rows2)]
                fields.append(jnp.concatenate(parts, axis=0))
            cross, squared, inv_u, inv_v, _, _ = jacobian(*fields, 2)
            at = slice(part * rows2, (part + 1) * rows2)
            for i, value in enumerate((cross, squared, inv_u, inv_v)):
                keep2[i, t, at] = value
            for i in (0, 1):
                parts = [unpack(ref[2 + t : 3 + t], 4, i, j) for j in range(rows2)]
                keep2[4 + i, t, at] = jnp.concatenate(parts, axis=0)

    rows_loop(0, total, lambda r, n: cheb_first(keep2, x2, d2, r, n, g0))
    rows_loop(1, total - 1, lambda r, n: cheb_step(2, keep2, x2, y2, d2, r, n, CARRY1, g1))
    rows_loop(2, total - 2, lambda r, n: cheb_step(2, keep2, y2, x2, d2, r, n, CARRY2, g2))
    rows_loop(3, total - 3, lambda r, n: cheb_step(2, keep2, x2, y2, d2, r, n, None, g0))
    rows_loop(4, total - 4, lambda r, n: cheb_step(2, keep2, y2, x2, d2, r, n, CARRY1, g1))
    rows_loop(5, total - 5, lambda r, n: cheb_step(2, keep2, x2, y2, d2, r, n, CARRY2, g2))

    g0, g1, g2 = gains(spread[...], 1)
    base1 = rows1 - 6
    for i in (0, 1):
        for t in (0, 1):
            coarse = y2[i, t, 2 * rows2 - 3 : 3 * rows2 + 3]
            n = rows2 + 6
            fine = jnp.broadcast_to(coarse[:, None], (n, 2, Z, X)).reshape(2 * n, Z, X)
            x1[i, t, base1 : base1 + 2 * n] = keep1[6 + i, t, base1 : base1 + 2 * n] + fine
    total = 3 * rows1
    rows_loop(4, total - 4, lambda r, n: cheb_step(1, keep1, x1, y1, d2, r, n, None, g0))
    rows_loop(5, total - 5, lambda r, n: cheb_step(1, keep1, y1, x1, d2, r, n, CARRY1, g1))
    rows_loop(6, total - 6, lambda r, n: cheb_step(1, keep1, x1, y1, d2, r, n, CARRY2, g2))

    g0, g1, g2 = gains(spread[...], 0)
    for i in (0, 1):
        for t in (0, 1):
            for at, ref in ((HALO0 - EDGE, near_prev), (HALO0 + rows, near_next)):
                if t == 0:
                    x0[i, t, at : at + EDGE] = ref[4 + i * EDGE : 4 + (i + 1) * EDGE]
                else:
                    for j in range(EDGE):
                        value = ref[4 + 2 * EDGE : 5 + 2 * EDGE]
                        x0[i, t, at + j : at + j + 1] = roll_x(value, -(4 + 8 * (i * EDGE + j)))
            x0[i, t, HALO0 : HALO0 + rows] = keep0[6 + i, t, HALO0 : HALO0 + rows]
            n = rows1 + 4
            coarse = y1[i, t, rows1 - 2 : 2 * rows1 + 2]
            fine = jnp.broadcast_to(coarse[:, None], (n, 2, Z, X)).reshape(2 * n, Z, X)
            at = slice(HALO0 - EDGE, HALO0 + rows + EDGE)
            x0[i, t, at] = x0[i, t, at] + fine[1 : 2 * n - 1]
    total = rows + 2 * HALO0
    rows_loop(2, total - 2, lambda r, n: cheb_step(0, keep0, x0, y0, d0, r, n, None, g0))
    rows_loop(3, total - 3, lambda r, n: cheb_step(0, keep0, y0, x0, d0, r, n, CARRY1, g1))
    rows_loop(4, total - 4, lambda r, n: cheb_step(0, keep0, x0, y0, d0, r, n, CARRY2, g2))
    for i in (0, 1):
        for y in range(rows):
            out[pl.ds(i * Z * rows + y, Z, stride=rows), :] = y0[i, 0, HALO0 + y]


def call(kernel, out_shapes, scratch, *args):
    out = [jax.ShapeDtypeStruct(shape, jnp.float32) for shape in out_shapes]
    return pl.pallas_call(
        kernel,
        out_shape=out,
        in_specs=[pl.BlockSpec(memory_space=pltpu.VMEM)] * len(args),
        out_specs=[pl.BlockSpec(memory_space=pltpu.VMEM)] * len(out),
        scratch_shapes=[pltpu.VMEM(shape, jnp.float32) for shape in scratch],
        compiler_params=pltpu.CompilerParams(vmem_limit_bytes=24 * 2**20),
    )(*args)


def shifted(value, axis, shift):
    count = lax.axis_size(axis)
    return lax.ppermute(value, axis, [((i + shift) % count, i) for i in range(count)])


def body(state, previous, feed, kill):
    _, depth, rows, cols = state.shape
    assert depth == Z and cols == X and rows % 8 == 0 and rows >= 16
    rows1 = rows // 2
    total0, total1, total2 = rows + 2 * HALO0, 3 * rows1, 5 * rows // 4
    state = state.reshape(2 * Z * rows, X)
    previous = previous.reshape(2 * Z * rows, X)
    feed = feed.reshape(Z * rows, X)
    kill = kill.reshape(Z * rows, X)
    inputs = (state, previous, feed, kill)

    strip = (6 * HALO0, Z, X)
    to_prev, to_next = call(functools.partial(pack_y_kernel, rows), [strip, strip], [], *inputs)
    from_next = shifted(to_prev, "gy", 1)
    from_prev = shifted(to_next, "gy", -1)

    (spread,) = call(functools.partial(spread_kernel, rows), [(Z, X)], [(4, rows, Z, X)], state, feed, kill)
    spread = lax.all_gather(spread, ("gx", "gy"), tiled=True)

    strip = (6 * (total0 // PER), Z, X)
    to_left, to_right = call(
        functools.partial(pack_x_kernel, rows),
        [strip, strip],
        [(6, 1, total0, Z, X)],
        *inputs,
        from_prev,
        from_next,
    )
    from_right = shifted(to_left, "gx", 1)
    from_left = shifted(to_right, "gx", -1)

    edge = (2 * EDGE + 1, Z, X)
    pair0 = (2, 2, total0, Z, X)
    packet1, edge_prev, edge_next, keep0 = call(
        functools.partial(level0_kernel, rows),
        [(3, 2, rows1 // 2, Z, X), edge, edge, (8, 2, total0, Z, X)],
        [(6, 2, total0, Z, X), pair0, pair0, pair0],
        *inputs,
        from_prev,
        from_next,
        from_left,
        from_right,
        spread,
    )
    below = shifted(packet1, "gy", 1)
    above = shifted(packet1, "gy", -1)

    pair1 = (2, 2, total1, Z, X)
    near = (4 + 2 * EDGE + 1, Z, X)
    packet2, to_prev, to_next, keep1 = call(
        functools.partial(level1_kernel, rows1),
        [(4, Z, X), near, near, (8, 2, total1, Z, X)],
        [pair1, pair1, pair1, (4, 2, total1, Z, X)],
        packet1,
        above,
        below,
        spread,
        edge_prev,
        edge_next,
    )
    near_next = shifted(to_prev, "gy", 1)
    near_prev = shifted(to_next, "gy", -1)
    far_next = shifted(packet2, "gy", 2)
    far_prev = shifted(packet2, "gy", -2)

    pair2 = (2, 2, total2, Z, X)
    (out,) = call(
        functools.partial(level2_kernel, rows),
        [(2 * Z * rows, X)],
        [(6, 2, total2, Z, X), pair2, pair2, pair1, pair1, pair1, pair0, pair0, pair0],
        spread,
        packet2,
        far_prev,
        near_prev,
        near_next,
        far_next,
        keep0,
        keep1,
    )
    return out.reshape(2, Z, rows, X)


def solution(mesh):
    placed = (
        P(None, None, "gy", "gx"),
        P(None, None, "gy", "gx"),
        P(None, "gy", "gx"),
        P(None, "gy", "gx"),
    )
    return jax.shard_map(
        body, mesh=mesh, in_specs=placed, out_specs=P(None, None, "gy", "gx"), check_vma=False
    )
```

```python
import functools

import jax
import jax.numpy as jnp
from jax import lax
from jax.experimental import pallas as pl
from jax.experimental.pallas import tpu as pltpu
from jax.sharding import PartitionSpec as P

DIFF = (40.0, 20.0)
INV_STEP = 2.0
LOWER = 0.25

_CENTRE = (1.0 + LOWER) / 2.0
_HALF = (1.0 - LOWER) / 2.0
_SIGMA = _CENTRE / _HALF
_RHO0 = 1.0 / _SIGMA
_RHO1 = 1.0 / (2.0 * _SIGMA - _RHO0)
_RHO2 = 1.0 / (2.0 * _SIGMA - _RHO1)

Z = 8
X = 128
HALO0 = 4
WIDE = 42
PER = X // WIDE
EDGE = 3
CHUNK = 4


def lane_of():
    return lax.broadcasted_iota(jnp.int32, (1, Z, X), 2)


def sub_of():
    return lax.broadcasted_iota(jnp.int32, (1, Z, X), 1)


def roll_x(tile, shift):
    shift = shift % X
    return pltpu.roll(tile, shift, 2) if shift else tile


def roll_z(tile, shift):
    shift = shift % Z
    return pltpu.roll(tile, shift, 1) if shift else tile


def rows_loop(lo, hi, body, step=CHUNK):
    full = (hi - lo) // step
    if full == 1:
        body(lo, step)
    elif full > 1:

        def trip(i, carry):
            body(lo + i * step, step)
            return carry

        lax.fori_loop(0, full, trip, 0)
    rest = hi - lo - full * step
    if rest:
        body(hi - rest, rest)


def neighbour_sums(read, r, n, k):
    lane = lane_of()
    low, high = lane < k, lane >= X - k
    centre = [read(t, r, n) for t in (0, 1)]
    right = [roll_x(c, k) for c in centre]
    left = [roll_x(c, -k) for c in centre]
    sums = []
    for t in (0, 1):
        c = centre[t]
        along_x = jnp.where(low, right[1 - t], right[t]) + jnp.where(high, left[1 - t], left[t])
        along_y = read(t, r - 1, n) + read(t, r + 1, n)
        along_z = 2.0 * roll_z(c, k) if 2 * k == Z else roll_z(c, k) + roll_z(c, -k)
        sums.append(along_x + along_y + along_z)
    return centre, sums


def jacobian(u, v, f, k, level):
    scale = 0.25**level
    product = u * v
    squared = v * v
    first = INV_STEP + squared + f + 6.0 * DIFF[0] * scale
    second = INV_STEP + f + k - 2.0 * product + 6.0 * DIFF[1] * scale
    return 2.0 * product, squared, 1.0 / first, 1.0 / second, first, second


def cheb_step(level, keep, source, target, d, r, n, carry, gain):
    scale = 0.25**level
    k = 1 << level
    u, nb_u = neighbour_sums(lambda t, a, m: source[0, t, pl.ds(a, m)], r, n, k)
    v, nb_v = neighbour_sums(lambda t, a, m: source[1, t, pl.ds(a, m)], r, n, k)
    rows = pl.ds(r, n)
    for t in (0, 1):
        cross, squared, inv_u, inv_v = (keep[i, t, rows] for i in range(4))
        res_u = inv_u * (keep[4, t, rows] - cross * v[t] + DIFF[0] * scale * nb_u[t]) - u[t]
        res_v = inv_v * (keep[5, t, rows] + squared * u[t] + DIFF[1] * scale * nb_v[t]) - v[t]
        du, dv = gain * res_u, gain * res_v
        if carry is not None:
            du = du + carry * d[0, t, rows]
            dv = dv + carry * d[1, t, rows]
        d[0, t, rows] = du
        d[1, t, rows] = dv
        target[0, t, rows] = u[t] + du
        target[1, t, rows] = v[t] + dv


def cheb_first(keep, target, d, r, n, gain):
    rows = pl.ds(r, n)
    for t in (0, 1):
        for i in (0, 1):
            value = gain * keep[2 + i, t, rows] * keep[4 + i, t, rows]
            d[i, t, rows] = value
            target[i, t, rows] = value


def residual(level, keep, diag, source, r, n):
    scale = 0.25**level
    k = 1 << level
    u, nb_u = neighbour_sums(lambda t, a, m: source[0, t, pl.ds(a, m)], r, n, k)
    v, nb_v = neighbour_sums(lambda t, a, m: source[1, t, pl.ds(a, m)], r, n, k)
    rows = pl.ds(r, n)
    first, second = [], []
    for t in (0, 1):
        first.append(
            keep[4, t, rows] - diag[0, t, rows] * u[t] - keep[0, t, rows] * v[t] + DIFF[0] * scale * nb_u[t]
        )
        second.append(
            keep[5, t, rows] - diag[1, t, rows] * v[t] + keep[1, t, rows] * u[t] + DIFF[1] * scale * nb_v[t]
        )
    return first, second


def gains(spread, level):
    top = jnp.max(spread.reshape(-1, Z, X), axis=0)
    row = lax.broadcasted_iota(jnp.int32, (Z, X), 0)
    top = jnp.max(jnp.where(row == level, top, 0.0), axis=0, keepdims=True)
    tau = 1.0 / (1.0 + jnp.broadcast_to(top, (Z, X)))
    return tau / _CENTRE, (2.0 * _RHO1 / _HALF) * tau, (2.0 * _RHO2 / _HALF) * tau


CARRY1 = _RHO1 * _RHO0
CARRY2 = _RHO2 * _RHO1


def pair_rows(value):
    n = value.shape[0] // 2
    pairs = value.reshape(n, 2, Z, X)
    return pairs[:, 0] + pairs[:, 1]


def pair_partner_x(tile, k, phase):
    return tile + (roll_x(tile, k) if phase else roll_x(tile, -k))


def pair_partner_z(tile, k, phase):
    return tile + (roll_z(tile, k) if phase else roll_z(tile, -k))


def spread_x(tile, k, phase):
    lane = lane_of()
    return jnp.where((lane & k) == (k if phase else 0), tile, roll_x(tile, -k if phase else k))


def spread_z(tile, k, phase):
    sub = sub_of()
    return jnp.where((sub & k) == (k if phase else 0), tile, roll_z(tile, -k if phase else k))


def restrict_packed(levels, k, pick):
    width = 2 * k
    lane, sub = lane_of() & (width - 1), sub_of() & (width - 1)
    out = None
    for i in range(width):
        across = None
        for j in range(width):
            value = pair_partner_x(pick(i, j), k, j & k)
            across = value if across is None else jnp.where(lane == j, value, across)
        value = pair_partner_z(across, k, i & k)
        out = value if out is None else jnp.where(sub == i, value, out)
    return out * 0.125


def unpack(tile, k, i, j):
    bit = 1
    while bit < k:
        tile = spread_x(tile, bit, j & bit)
        tile = spread_z(tile, bit, i & bit)
        bit *= 2
    return tile


def plane(ref, f, y, rows):
    return ref[pl.ds(f * Z * rows + y, Z, stride=rows), :]


def pack_y_kernel(rows, state, previous, feed, kill, to_prev, to_next):
    fields = [(state, 0), (state, 1), (previous, 0), (previous, 1), (feed, 0), (kill, 0)]
    for i, (ref, f) in enumerate(fields):
        for j in range(HALO0):
            to_prev[i * HALO0 + j] = plane(ref, f, j, rows)
            to_next[i * HALO0 + j] = plane(ref, f, rows - HALO0 + j, rows)


def spread_kernel(rows, state, feed, kill, out, fields):
    for y in range(rows):
        fields[0, y] = plane(state, 0, y, rows)
        fields[1, y] = plane(state, 1, y, rows)
        fields[2, y] = plane(feed, 0, y, rows)
        fields[3, y] = plane(kill, 0, y, rows)
    result = jnp.zeros((Z, X), jnp.float32)
    row = lax.broadcasted_iota(jnp.int32, (Z, X), 0)
    for level in range(3):
        n = rows >> level
        u, v, f, k = (fields[i, 0:n] for i in range(4))
        scale = 0.25**level
        cross, squared, inv_u, inv_v, _, _ = jacobian(u, v, f, k, level)
        both = jnp.maximum((6.0 * DIFF[0] * scale + cross) * inv_u, (6.0 * DIFF[1] * scale + squared) * inv_v)
        top = jnp.max(both, axis=0)
        top = jnp.max(jnp.max(top, axis=1, keepdims=True), axis=0, keepdims=True)
        result = jnp.where(row == level, jnp.broadcast_to(top, (Z, X)), result)
        if level < 2:
            span = 1 << level
            for i in range(4):
                summed = pair_rows(fields[i, 0:n])
                lane, sub = lane_of(), sub_of()
                summed = jnp.where(
                    (lane & span) == 0, pair_partner_x(summed, span, 0), pair_partner_x(summed, span, span)
                )
                summed = jnp.where(
                    (sub & span) == 0, pair_partner_z(summed, span, 0), pair_partner_z(summed, span, span)
                )
                fields[i, 0 : n // 2] = summed * 0.125
    out[...] = result


def fill_main(rows, state, previous, feed, kill, from_prev, from_next, fields):
    sources = [(state, 0), (state, 1), (previous, 0), (previous, 1), (feed, 0), (kill, 0)]
    for i, (ref, f) in enumerate(sources):
        fields[i, 0, 0:HALO0] = from_prev[i * HALO0 : (i + 1) * HALO0]
        fields[i, 0, HALO0 + rows : rows + 2 * HALO0] = from_next[i * HALO0 : (i + 1) * HALO0]
        for y in range(rows):
            fields[i, 0, HALO0 + y] = plane(ref, f, y, rows)


def pack_x_kernel(rows, state, previous, feed, kill, from_prev, from_next, to_left, to_right, fields):
    fill_main(rows, state, previous, feed, kill, from_prev, from_next, fields)
    total = rows + 2 * HALO0
    group = total // PER
    lane = lane_of()
    for i in range(6):
        left, right = None, None
        for j in range(PER):
            part = fields[i, 0, j * group : (j + 1) * group]
            a = roll_x(part, WIDE * j)
            b = roll_x(part, WIDE + WIDE * j)
            if j == 0:
                left, right = a, b
            else:
                left = jnp.where(lane >= WIDE * j, a, left)
                right = jnp.where(lane >= WIDE * j, b, right)
        to_left[i * group : (i + 1) * group] = left
        to_right[i * group : (i + 1) * group] = right


def fill_halo(rows, from_left, from_right, fields):
    total = rows + 2 * HALO0
    group = total // PER
    lane = lane_of()
    for i in range(6):
        left = from_left[i * group : (i + 1) * group]
        right = from_right[i * group : (i + 1) * group]
        for j in range(PER):
            value = jnp.where(lane < X // 2, roll_x(right, -WIDE * j), roll_x(left, X - WIDE - WIDE * j))
            fields[i, 1, j * group : (j + 1) * group] = value


def level0_kernel(
    rows,
    state,
    previous,
    feed,
    kill,
    from_prev,
    from_next,
    from_left,
    from_right,
    spread,
    packet,
    edge_prev,
    edge_next,
    keep,
    fields,
    other,
    d,
    diag,
):
    total = rows + 2 * HALO0
    fill_main(rows, state, previous, feed, kill, from_prev, from_next, fields)
    fill_halo(rows, from_left, from_right, fields)
    g0, g1, g2 = gains(spread[...], 0)
    here = keep.at[6:8]

    def setup(r, n):
        at = pl.ds(r, n)
        u, nb_u = neighbour_sums(lambda t, a, m: fields[0, t, pl.ds(a, m)], r, n, 1)
        v, nb_v = neighbour_sums(lambda t, a, m: fields[1, t, pl.ds(a, m)], r, n, 1)
        for t in (0, 1):
            f, k = fields[4, t, at], fields[5, t, at]
            cross, squared, inv_u, inv_v, first, second = jacobian(u[t], v[t], f, k, 0)
            react = u[t] * squared
            b_u = (
                DIFF[0] * (nb_u[t] - 6.0 * u[t])
                - INV_STEP * (u[t] - fields[2, t, at])
                - react
                + f * (1.0 - u[t])
            )
            b_v = (
                DIFF[1] * (nb_v[t] - 6.0 * v[t]) - INV_STEP * (v[t] - fields[3, t, at]) + react - (f + k) * v[t]
            )
            for i, value in enumerate((cross, squared, inv_u, inv_v, b_u, b_v)):
                keep[i, t, at] = value
            diag[0, t, at] = first
            diag[1, t, at] = second
            for i, value in enumerate((g0 * inv_u * b_u, g0 * inv_v * b_v)):
                d[i, t, at] = value
                keep[6 + i, t, at] = value

    rows_loop(1, total - 1, setup)
    rows_loop(2, total - 2, lambda r, n: cheb_step(0, keep, here, other, d, r, n, CARRY1, g1))
    rows_loop(3, total - 3, lambda r, n: cheb_step(0, keep, other, here, d, r, n, CARRY2, g2))

    def down(r, n):
        first, second = residual(0, keep, diag, here, r, n)
        out = (r - HALO0) // 4
        for t in (0, 1):
            at = pl.ds(r, n)
            values = [first[t], second[t], fields[0, t, at], fields[1, t, at], fields[4, t, at], fields[5, t, at]]
            sums = [pair_rows(value) for value in values]
            for p in range(3):
                packed = restrict_packed(0, 1, lambda i, j: sums[2 * p + i][j : j + 1])
                packet[p, t, pl.ds(out, 1)] = packed

    rows_loop(HALO0, HALO0 + rows, down, 4)

    lane = lane_of()
    for edge, start in ((edge_prev, HALO0), (edge_next, HALO0 + rows - EDGE)):
        halo = None
        for i in (0, 1):
            for j in range(EDGE):
                at = i * EDGE + j
                edge[at] = keep[6 + i, 0, start + j]
                value = roll_x(keep[6 + i, 1, start + j : start + j + 1], 4 + 8 * at)
                halo = value if halo is None else jnp.where((lane >> 3) == at, value, halo)
        edge[2 * EDGE : 2 * EDGE + 1] = halo


def level1_kernel(
    rows, own, above, below, spread, edge_prev, edge_next, packet, to_prev, to_next, keep, other, d, diag, fields
):
    total = 3 * rows
    g0, g1, g2 = gains(spread[...], 1)
    here = keep.at[6:8]

    for part, ref in enumerate((above, own, below)):

        def take(r, n, part=part, ref=ref):
            for p in range(3):
                for t in (0, 1):
                    tile = ref[p, t, pl.ds(r, n)]
                    for i in (0, 1):
                        a = unpack(tile, 2, i, 0)
                        b = unpack(tile, 2, i, 1)
                        value = jnp.stack([a, b], axis=1).reshape(2 * n, Z, X)
                        at = pl.ds(part * rows + 2 * r, 2 * n)
                        if p == 0:
                            keep[4 + i, t, at] = value
                        else:
                            fields[2 * (p - 1) + i, t, at] = value

        rows_loop(0, rows // 2, take, 2)

    def setup(r, n):
        at = pl.ds(r, n)
        for t in (0, 1):
            u, v, f, k = (fields[i, t, at] for i in range(4))
            cross, squared, inv_u, inv_v, first, second = jacobian(u, v, f, k, 1)
            for i, value in enumerate((cross, squared, inv_u, inv_v)):
                keep[i, t, at] = value
            diag[0, t, at] = first
            diag[1, t, at] = second
            for i, value in enumerate((g0 * inv_u * keep[4, t, at], g0 * inv_v * keep[5, t, at])):
                d[i, t, at] = value
                keep[6 + i, t, at] = value

    rows_loop(1, total - 1, setup)
    rows_loop(2, total - 2, lambda r, n: cheb_step(1, keep, here, other, d, r, n, CARRY1, g1))
    rows_loop(3, total - 3, lambda r, n: cheb_step(1, keep, other, here, d, r, n, CARRY2, g2))

    first, second = residual(1, keep, diag, here, rows, rows)
    for t in (0, 1):
        sums = [pair_rows(value) for value in (first[t], second[t])]
        sums += [pair_rows(fields[i, t, rows : 2 * rows]) for i in range(4)]
        for p in (0, 1):
            names = (2, 3, 4, 5) if p == 0 else (0, 1, 0, 1)
            value = restrict_packed(1, 2, lambda i, j: sums[names[i]][j : j + 1])
            for ref in (packet, to_prev, to_next):
                ref[2 * p + t : 2 * p + t + 1] = value
    to_prev[4 : 4 + 2 * EDGE + 1] = edge_prev[...]
    to_next[4 : 4 + 2 * EDGE + 1] = edge_next[...]


def level2_kernel(
    rows, spread, own, far_prev, near_prev, near_next, far_next, keep0, keep1, out, keep2, x2, y2, d2, x1, y1, x0, y0, d0
):
    rows1, rows2 = rows // 2, rows // 4
    total = 5 * rows2
    g0, g1, g2 = gains(spread[...], 2)

    for part, ref in enumerate((far_prev, near_prev, own, near_next, far_next)):
        for t in (0, 1):
            fields = []
            for i in range(4):
                parts = [unpack(ref[t : t + 1], 4, i, j) for j in range(rows2)]
                fields.append(jnp.concatenate(parts, axis=0))
            cross, squared, inv_u, inv_v, _, _ = jacobian(*fields, 2)
            at = slice(part * rows2, (part + 1) * rows2)
            for i, value in enumerate((cross, squared, inv_u, inv_v)):
                keep2[i, t, at] = value
            for i in (0, 1):
                parts = [unpack(ref[2 + t : 3 + t], 4, i, j) for j in range(rows2)]
                keep2[4 + i, t, at] = jnp.concatenate(parts, axis=0)

    rows_loop(0, total, lambda r, n: cheb_first(keep2, x2, d2, r, n, g0))
    rows_loop(1, total - 1, lambda r, n: cheb_step(2, keep2, x2, y2, d2, r, n, CARRY1, g1))
    rows_loop(2, total - 2, lambda r, n: cheb_step(2, keep2, y2, x2, d2, r, n, CARRY2, g2))
    rows_loop(3, total - 3, lambda r, n: cheb_step(2, keep2, x2, y2, d2, r, n, None, g0))
    rows_loop(4, total - 4, lambda r, n: cheb_step(2, keep2, y2, x2, d2, r, n, CARRY1, g1))
    rows_loop(5, total - 5, lambda r, n: cheb_step(2, keep2, x2, y2, d2, r, n, CARRY2, g2))

    g0, g1, g2 = gains(spread[...], 1)
    base1 = rows1 - 6
    for i in (0, 1):
        for t in (0, 1):
            coarse = y2[i, t, 2 * rows2 - 3 : 3 * rows2 + 3]
            n = rows2 + 6
            fine = jnp.broadcast_to(coarse[:, None], (n, 2, Z, X)).reshape(2 * n, Z, X)
            x1[i, t, base1 : base1 + 2 * n] = keep1[6 + i, t, base1 : base1 + 2 * n] + fine
    total = 3 * rows1
    rows_loop(4, total - 4, lambda r, n: cheb_step(1, keep1, x1, y1, d2, r, n, None, g0))
    rows_loop(5, total - 5, lambda r, n: cheb_step(1, keep1, y1, x1, d2, r, n, CARRY1, g1))
    rows_loop(6, total - 6, lambda r, n: cheb_step(1, keep1, x1, y1, d2, r, n, CARRY2, g2))

    g0, g1, g2 = gains(spread[...], 0)
    for i in (0, 1):
        for t in (0, 1):
            for at, ref in ((HALO0 - EDGE, near_prev), (HALO0 + rows, near_next)):
                if t == 0:
                    x0[i, t, at : at + EDGE] = ref[4 + i * EDGE : 4 + (i + 1) * EDGE]
                else:
                    for j in range(EDGE):
                        value = ref[4 + 2 * EDGE : 5 + 2 * EDGE]
                        x0[i, t, at + j : at + j + 1] = roll_x(value, -(4 + 8 * (i * EDGE + j)))
            x0[i, t, HALO0 : HALO0 + rows] = keep0[6 + i, t, HALO0 : HALO0 + rows]
            n = rows1 + 4
            coarse = y1[i, t, rows1 - 2 : 2 * rows1 + 2]
            fine = jnp.broadcast_to(coarse[:, None], (n, 2, Z, X)).reshape(2 * n, Z, X)
            at = slice(HALO0 - EDGE, HALO0 + rows + EDGE)
            x0[i, t, at] = x0[i, t, at] + fine[1 : 2 * n - 1]
    total = rows + 2 * HALO0
    rows_loop(2, total - 2, lambda r, n: cheb_step(0, keep0, x0, y0, d0, r, n, None, g0))
    rows_loop(3, total - 3, lambda r, n: cheb_step(0, keep0, y0, x0, d0, r, n, CARRY1, g1))
    rows_loop(4, total - 4, lambda r, n: cheb_step(0, keep0, x0, y0, d0, r, n, CARRY2, g2))
    for i in (0, 1):
        for y in range(rows):
            out[pl.ds(i * Z * rows + y, Z, stride=rows), :] = y0[i, 0, HALO0 + y]


def call(kernel, out_shapes, scratch, *args):
    out = [jax.ShapeDtypeStruct(shape, jnp.float32) for shape in out_shapes]
    return pl.pallas_call(
        kernel,
        out_shape=out,
        in_specs=[pl.BlockSpec(memory_space=pltpu.VMEM)] * len(args),
        out_specs=[pl.BlockSpec(memory_space=pltpu.VMEM)] * len(out),
        scratch_shapes=[pltpu.VMEM(shape, jnp.float32) for shape in scratch],
        compiler_params=pltpu.CompilerParams(vmem_limit_bytes=24 * 2**20),
    )(*args)


def shifted(value, axis, shift):
    count = lax.axis_size(axis)
    return lax.ppermute(value, axis, [((i + shift) % count, i) for i in range(count)])


def body(state, previous, feed, kill):
    _, depth, rows, cols = state.shape
    assert depth == Z and cols == X and rows % 8 == 0 and rows >= 16
    rows1 = rows // 2
    total0, total1, total2 = rows + 2 * HALO0, 3 * rows1, 5 * rows // 4
    state = state.reshape(2 * Z * rows, X)
    previous = previous.reshape(2 * Z * rows, X)
    feed = feed.reshape(Z * rows, X)
    kill = kill.reshape(Z * rows, X)
    inputs = (state, previous, feed, kill)

    strip = (6 * HALO0, Z, X)
    to_prev, to_next = call(functools.partial(pack_y_kernel, rows), [strip, strip], [], *inputs)
    from_next = shifted(to_prev, "gy", 1)
    from_prev = shifted(to_next, "gy", -1)

    (spread,) = call(functools.partial(spread_kernel, rows), [(Z, X)], [(4, rows, Z, X)], state, feed, kill)
    count = lax.axis_size("gx") * lax.axis_size("gy")
    copies = jnp.broadcast_to(spread[None], (count, Z, X))
    spread = lax.all_to_all(copies, ("gx", "gy"), 0, 0, tiled=True)

    strip = (6 * (total0 // PER), Z, X)
    to_left, to_right = call(
        functools.partial(pack_x_kernel, rows),
        [strip, strip],
        [(6, 1, total0, Z, X)],
        *inputs,
        from_prev,
        from_next,
    )
    from_right = shifted(to_left, "gx", 1)
    from_left = shifted(to_right, "gx", -1)

    edge = (2 * EDGE + 1, Z, X)
    pair0 = (2, 2, total0, Z, X)
    packet1, edge_prev, edge_next, keep0 = call(
        functools.partial(level0_kernel, rows),
        [(3, 2, rows1 // 2, Z, X), edge, edge, (8, 2, total0, Z, X)],
        [(6, 2, total0, Z, X), pair0, pair0, pair0],
        *inputs,
        from_prev,
        from_next,
        from_left,
        from_right,
        spread,
    )
    below = shifted(packet1, "gy", 1)
    above = shifted(packet1, "gy", -1)

    pair1 = (2, 2, total1, Z, X)
    near = (4 + 2 * EDGE + 1, Z, X)
    packet2, to_prev, to_next, keep1 = call(
        functools.partial(level1_kernel, rows1),
        [(4, Z, X), near, near, (8, 2, total1, Z, X)],
        [pair1, pair1, pair1, (4, 2, total1, Z, X)],
        packet1,
        above,
        below,
        spread,
        edge_prev,
        edge_next,
    )
    near_next = shifted(to_prev, "gy", 1)
    near_prev = shifted(to_next, "gy", -1)
    far_next = shifted(packet2, "gy", 2)
    far_prev = shifted(packet2, "gy", -2)

    pair2 = (2, 2, total2, Z, X)
    (out,) = call(
        functools.partial(level2_kernel, rows),
        [(2 * Z * rows, X)],
        [(6, 2, total2, Z, X), pair2, pair2, pair1, pair1, pair1, pair0, pair0, pair0],
        spread,
        packet2,
        far_prev,
        near_prev,
        near_next,
        far_next,
        keep0,
        keep1,
    )
    return out.reshape(2, Z, rows, X)


def solution(mesh):
    placed = (
        P(None, None, "gy", "gx"),
        P(None, None, "gy", "gx"),
        P(None, "gy", "gx"),
        P(None, "gy", "gx"),
    )
    return jax.shard_map(
        body, mesh=mesh, in_specs=placed, out_specs=P(None, None, "gy", "gx"), check_vma=False
    )
```

```python
import functools

import jax
import jax.numpy as jnp
from jax import lax
from jax.experimental import pallas as pl
from jax.experimental.pallas import tpu as pltpu
from jax.sharding import PartitionSpec as P

DIFF = (40.0, 20.0)
INV_STEP = 2.0
LOWER = 0.25

_CENTRE = (1.0 + LOWER) / 2.0
_HALF = (1.0 - LOWER) / 2.0
_SIGMA = _CENTRE / _HALF
_RHO0 = 1.0 / _SIGMA
_RHO1 = 1.0 / (2.0 * _SIGMA - _RHO0)
_RHO2 = 1.0 / (2.0 * _SIGMA - _RHO1)

Z = 8
X = 128
HALO0 = 4
WIDE = 42
PER = X // WIDE
EDGE = 3
CHUNK = 4

LO1, HI1 = -10, 14
LO2, HI2 = -2, 3
LO_UP, HI_UP = -3, 7
SIZE1, SIZE2, SIZE_UP = HI1 - LO1 + 2, HI2 - LO2 + 2, HI_UP - LO_UP + 2
OWN = 4


def lane_of():
    return lax.broadcasted_iota(jnp.int32, (1, Z, X), 2)


def sub_of():
    return lax.broadcasted_iota(jnp.int32, (1, Z, X), 1)


def roll_x(tile, shift):
    shift = shift % X
    return pltpu.roll(tile, shift, 2) if shift else tile


def roll_z(tile, shift):
    shift = shift % Z
    return pltpu.roll(tile, shift, 1) if shift else tile


def rows_loop(lo, hi, body, step=CHUNK):
    full = (hi - lo) // step
    if full == 1:
        body(lo, step)
    elif full > 1:

        def trip(i, carry):
            body(lo + i * step, step)
            return carry

        lax.fori_loop(0, full, trip, 0)
    rest = hi - lo - full * step
    if rest:
        body(hi - rest, rest)


def neighbour_sums(read, r, n, k):
    lane = lane_of()
    low, high = lane < k, lane >= X - k
    centre = [read(t, r, n) for t in (0, 1)]
    right = [roll_x(c, k) for c in centre]
    left = [roll_x(c, -k) for c in centre]
    sums = []
    for t in (0, 1):
        c = centre[t]
        along_x = jnp.where(low, right[1 - t], right[t]) + jnp.where(high, left[1 - t], left[t])
        along_y = read(t, r - 1, n) + read(t, r + 1, n)
        along_z = 2.0 * roll_z(c, k) if 2 * k == Z else roll_z(c, k) + roll_z(c, -k)
        sums.append(along_x + along_y + along_z)
    return centre, sums


def jacobian(u, v, f, k, level):
    scale = 0.25**level
    product = u * v
    squared = v * v
    first = INV_STEP + squared + f + 6.0 * DIFF[0] * scale
    second = INV_STEP + f + k - 2.0 * product + 6.0 * DIFF[1] * scale
    return 2.0 * product, squared, 1.0 / first, 1.0 / second, first, second


def cheb_step(level, keep, source, target, d, r, n, carry, gain):
    scale = 0.25**level
    k = 1 << level
    u, nb_u = neighbour_sums(lambda t, a, m: source[0, t, pl.ds(a, m)], r, n, k)
    v, nb_v = neighbour_sums(lambda t, a, m: source[1, t, pl.ds(a, m)], r, n, k)
    rows = pl.ds(r, n)
    for t in (0, 1):
        cross, squared, inv_u, inv_v = (keep[i, t, rows] for i in range(4))
        res_u = inv_u * (keep[4, t, rows] - cross * v[t] + DIFF[0] * scale * nb_u[t]) - u[t]
        res_v = inv_v * (keep[5, t, rows] + squared * u[t] + DIFF[1] * scale * nb_v[t]) - v[t]
        du, dv = gain * res_u, gain * res_v
        if carry is not None:
            du = du + carry * d[0, t, rows]
            dv = dv + carry * d[1, t, rows]
        d[0, t, rows] = du
        d[1, t, rows] = dv
        target[0, t, rows] = u[t] + du
        target[1, t, rows] = v[t] + dv


def residual(level, keep, diag, source, r, n):
    scale = 0.25**level
    k = 1 << level
    u, nb_u = neighbour_sums(lambda t, a, m: source[0, t, pl.ds(a, m)], r, n, k)
    v, nb_v = neighbour_sums(lambda t, a, m: source[1, t, pl.ds(a, m)], r, n, k)
    rows = pl.ds(r, n)
    first, second = [], []
    for t in (0, 1):
        first.append(
            keep[4, t, rows] - diag[0, t, rows] * u[t] - keep[0, t, rows] * v[t] + DIFF[0] * scale * nb_u[t]
        )
        second.append(
            keep[5, t, rows] - diag[1, t, rows] * v[t] + keep[1, t, rows] * u[t] + DIFF[1] * scale * nb_v[t]
        )
    return first, second


CARRY1 = _RHO1 * _RHO0
CARRY2 = _RHO2 * _RHO1


def write_gains(spread, out):
    row = lax.broadcasted_iota(jnp.int32, (Z, X), 0)
    for level in range(3):
        top = jnp.max(jnp.where(row == level, spread, 0.0), axis=0, keepdims=True)
        tau = 1.0 / (1.0 + jnp.broadcast_to(top, (Z, X)))
        for i, factor in enumerate((1.0 / _CENTRE, 2.0 * _RHO1 / _HALF, 2.0 * _RHO2 / _HALF)):
            out[3 * level + i] = factor * tau


def pair_rows(value):
    n = value.shape[0] // 2
    pairs = value.reshape(n, 2, Z, X)
    return pairs[:, 0] + pairs[:, 1]


def restrict_01(first, second):
    lane, sub = lane_of(), sub_of()
    across = []
    for value in (first, second):
        a, b = value[0:1], value[1:2]
        across.append(jnp.where((lane & 1) == 0, a + roll_x(a, -1), b + roll_x(b, 1)))
    a, b = across
    return 0.125 * jnp.where((sub & 1) == 0, a + roll_z(a, -1), b + roll_z(b, 1))


def restrict_12(groups):
    lane, sub = lane_of(), sub_of()
    out = None
    for p, value in enumerate(groups):
        value = value + roll_x(value, 1 if p & 1 else -1)
        value = value + roll_x(value, 2 if p & 2 else -2)
        out = value if out is None else jnp.where((lane & 3) == p, value, out)
    return 0.125 * (out + jnp.where((sub & 2) == 0, roll_z(out, -2), roll_z(out, 2)))


def spread_x(tile, k, phase):
    return jnp.where((lane_of() & k) == phase, tile, roll_x(tile, -k if phase else k))


def packed_jacobian(uv, fk, level):
    scale = 0.25**level
    even = (sub_of() & 1) == 0
    u, v = jnp.where(even, uv, roll_z(uv, 1)), jnp.where(even, roll_z(uv, -1), uv)
    f, k = jnp.where(even, fk, roll_z(fk, 1)), jnp.where(even, roll_z(fk, -1), fk)
    product, squared = u * v, v * v
    diag = jnp.where(
        even,
        INV_STEP + squared + f + 6.0 * DIFF[0] * scale,
        INV_STEP + f + k - 2.0 * product + 6.0 * DIFF[1] * scale,
    )
    return 1.0 / diag, jnp.where(even, -2.0 * product, squared), diag


def packed_spread(uv, fk, level):
    scale = 0.25**level
    even = (sub_of() & 1) == 0
    inverse, other, _ = packed_jacobian(uv, fk, level)
    return jnp.where(even, 6.0 * DIFF[0] * scale - other, 6.0 * DIFF[1] * scale + other) * inverse


def packed_terms(source, g, n, level):
    k = 1 << level
    lane, sub = lane_of(), sub_of()
    even = (sub & 1) == 0
    first, last = (lane & (k - 1)) == 0, (lane & (k - 1)) == k - 1
    low, high = lane < k, lane >= X - k
    diff = jnp.where(even, DIFF[0] * 0.25**level, DIFF[1] * 0.25**level)
    wide = [source[t, pl.ds(g - 1, n + 2)] for t in (0, 1)]
    centre = [w[1 : n + 1] for w in wide]
    right = [roll_x(c, k) for c in centre]
    left = [roll_x(c, -k) for c in centre]
    out = []
    for t in (0, 1):
        c, w = centre[t], wide[t]
        total = jnp.where(low, right[1 - t], right[t]) + jnp.where(high, left[1 - t], left[t])
        if k == 2:
            ahead, back = roll_x(w, 1), roll_x(w, -1)
            total = total + jnp.where(first, back[0:n], ahead[1 : n + 1])
            total = total + jnp.where(last, ahead[2 : n + 2], back[1 : n + 1])
            total = total + roll_z(c, 2) + roll_z(c, -2)
        else:
            total = total + jnp.where(first, roll_x(w[0:n], -(k - 1)), roll_x(c, 1))
            total = total + jnp.where(last, roll_x(w[2 : n + 2], k - 1), roll_x(c, -1))
            total = total + 2.0 * roll_z(c, 4)
        other = jnp.where(even, roll_z(c, -1), roll_z(c, 1))
        out.append((c, other, diff * total))
    return out


def packed_first(coef, shift, b, target, d, g, n, gain):
    for t in (0, 1):
        value = gain * coef[0, t, pl.ds(g + shift, n)] * b[t, pl.ds(g + shift, n)]
        d[t, pl.ds(g, n)] = value
        target[t, pl.ds(g, n)] = value


def packed_step(level, coef, shift, b, source, target, d, g, n, carry, gain):
    for t, (c, other, spread) in enumerate(packed_terms(source, g, n, level)):
        at = pl.ds(g + shift, n)
        res = coef[0, t, at] * (b[t, at] + coef[1, t, at] * other + spread) - c
        delta = gain * res
        if carry is not None:
            delta = delta + carry * d[t, pl.ds(g, n)]
        d[t, pl.ds(g, n)] = delta
        target[t, pl.ds(g, n)] = c + delta


def plane(ref, f, y, rows):
    return ref[pl.ds(f * Z * rows + y, Z, stride=rows), :]


def pack_y_kernel(rows, state, previous, feed, kill, to_prev, to_next, main, *scratch):
    sources, sems = scratch[:4], scratch[4]
    copies = [
        pltpu.make_async_copy(ref, held, sems.at[i])
        for i, (ref, held) in enumerate(zip((state, previous, feed, kill), sources))
    ]
    for copy in copies:
        copy.start()
    for copy in copies:
        copy.wait()
    state, previous, feed, kill = sources
    fields = [(state, 0), (state, 1), (previous, 0), (previous, 1), (feed, 0), (kill, 0)]
    for i, (ref, f) in enumerate(fields):
        for y in range(rows):
            value = plane(ref, f, y, rows)
            main[i, y] = value
            if y < HALO0:
                to_prev[i * HALO0 + y] = value
            if y >= rows - HALO0:
                to_next[i * HALO0 + y - rows + HALO0] = value


CHUNK1 = 2 * OWN + 1


def fields_kernel(count, rows, main, packet):
    row = lax.broadcasted_iota(jnp.int32, (Z, X), 0)
    u, v, f, k = (main[i] for i in (0, 1, 4, 5))
    cross, squared, inv_u, inv_v, _, _ = jacobian(u, v, f, k, 0)
    tops = [jnp.max(jnp.maximum((6.0 * DIFF[0] + cross) * inv_u, (6.0 * DIFF[1] + squared) * inv_v), axis=0)]
    sums = [pair_rows(value) for value in (u, v, f, k)]
    pairs = []
    for p in (0, 1):
        pairs.append(
            [restrict_01(sums[2 * p][2 * j : 2 * j + 2], sums[2 * p + 1][2 * j : 2 * j + 2]) for j in range(OWN)]
        )
    for c in range(count):
        for p in (0, 1):
            for j in range(OWN):
                packet[c * CHUNK1 + p * OWN + j] = pairs[p][j][0]
    tops.append(jnp.max(jnp.concatenate([packed_spread(a, b, 1) for a, b in zip(*pairs)], axis=0), axis=0))
    tops.append(packed_spread(restrict_12(pairs[0]), restrict_12(pairs[1]), 2)[0])
    result = jnp.zeros((Z, X), jnp.float32)
    for level, top in enumerate(tops):
        top = jnp.max(jnp.max(top, axis=1, keepdims=True), axis=0, keepdims=True)
        result = jnp.where(row == level, jnp.broadcast_to(top, (Z, X)), result)
    for c in range(count):
        packet[c * CHUNK1 + 2 * OWN] = result


def block_at(count, chunk, relative):
    me = lax.axis_index("gy")
    return lax.rem(me + relative + count * 4, count) * chunk


def runs():
    out = []
    g = LO1
    while g < HI1:
        n = min(OWN - g % OWN, HI1 - g)
        out.append((g // OWN, g % OWN, n, g - LO1))
        g += n
    return out


GROUPS1 = HI1 - LO1


def pack_three(parts):
    lane = lane_of()
    left, right = None, None
    for j, part in enumerate(parts):
        a, b = roll_x(part, WIDE * j), roll_x(part, WIDE + WIDE * j)
        left = a if left is None else jnp.where(lane >= WIDE * j, a, left)
        right = b if right is None else jnp.where(lane >= WIDE * j, b, right)
    return left, right


def unpack_three(from_left, from_right, j):
    return jnp.where(lane_of() < X // 2, roll_x(from_right, -WIDE * j), roll_x(from_left, X - WIDE - WIDE * j))


def pack_x_kernel(count, rows, main, from_prev, from_next, gathered, to_left, to_right, spread, held):
    total = rows + 2 * HALO0
    group = total // PER
    for i in range(6):
        strip = slice(i * HALO0, (i + 1) * HALO0)
        whole = jnp.concatenate([from_prev[strip], main[i], from_next[strip]], axis=0)
        left, right = pack_three([whole[j * group : (j + 1) * group] for j in range(PER)])
        to_left[i * group : (i + 1) * group] = left
        to_right[i * group : (i + 1) * group] = right
    for relative, first, n, where in runs():
        base = block_at(count, CHUNK1, relative)
        for p in (0, 1):
            held[p * GROUPS1 + where : p * GROUPS1 + where + n] = gathered[pl.ds(base + p * OWN + first, n)]
    share = 2 * GROUPS1 // PER
    left, right = pack_three([held[j * share : (j + 1) * share] for j in range(PER)])
    at = 6 * group
    to_left[at : at + share] = left
    to_right[at : at + share] = right
    top = gathered[2 * OWN]
    for c in range(1, count):
        top = jnp.maximum(top, gathered[c * CHUNK1 + 2 * OWN])
    to_left[at + share] = top
    to_right[at + share] = top
    spread[...] = top


def level0_kernel(count, rows, main, from_prev, from_next, from_left, from_right, *refs):
    spreads, (packet, edge_prev, edge_next, keep, gain_out, fields, other, d, diag) = refs[:-9], refs[-9:]
    total = rows + 2 * HALO0
    group = total // PER
    top = jnp.maximum(from_left[from_left.shape[0] - 1], from_right[from_right.shape[0] - 1])
    for ref in spreads:
        top = jnp.maximum(top, ref[...])
    write_gains(top, gain_out)
    g0, g1, g2 = (gain_out[i] for i in range(3))
    for i in range(6):
        strip = slice(i * HALO0, (i + 1) * HALO0)
        fields[i, 0, 0:HALO0] = from_prev[strip]
        fields[i, 0, HALO0 : HALO0 + rows] = main[i]
        fields[i, 0, HALO0 + rows : total] = from_next[strip]
        strip = slice(i * group, (i + 1) * group)
        left, right = from_left[strip], from_right[strip]
        for j in range(PER):
            fields[i, 1, j * group : (j + 1) * group] = unpack_three(left, right, j)
    here = keep.at[6:8]

    def setup(r, n):
        at = pl.ds(r, n)
        u, nb_u = neighbour_sums(lambda t, a, m: fields[0, t, pl.ds(a, m)], r, n, 1)
        v, nb_v = neighbour_sums(lambda t, a, m: fields[1, t, pl.ds(a, m)], r, n, 1)
        for t in (0, 1):
            f, k = fields[4, t, at], fields[5, t, at]
            cross, squared, inv_u, inv_v, first, second = jacobian(u[t], v[t], f, k, 0)
            react = u[t] * squared
            b_u = (
                DIFF[0] * (nb_u[t] - 6.0 * u[t])
                - INV_STEP * (u[t] - fields[2, t, at])
                - react
                + f * (1.0 - u[t])
            )
            b_v = (
                DIFF[1] * (nb_v[t] - 6.0 * v[t]) - INV_STEP * (v[t] - fields[3, t, at]) + react - (f + k) * v[t]
            )
            for i, value in enumerate((cross, squared, inv_u, inv_v, b_u, b_v)):
                keep[i, t, at] = value
            diag[0, t, at] = first
            diag[1, t, at] = second
            for i, value in enumerate((g0 * inv_u * b_u, g0 * inv_v * b_v)):
                d[i, t, at] = value
                keep[6 + i, t, at] = value

    rows_loop(1, total - 1, setup)
    rows_loop(2, total - 2, lambda r, n: cheb_step(0, keep, here, other, d, r, n, CARRY1, g1))
    rows_loop(3, total - 3, lambda r, n: cheb_step(0, keep, other, here, d, r, n, CARRY2, g2))

    def down(r, n):
        first, second = residual(0, keep, diag, here, r, n)
        out = (r - HALO0) // 4
        for t in (0, 1):
            value = restrict_01(pair_rows(first[t]), pair_rows(second[t]))
            for c in range(count):
                packet[pl.ds(c * 2 * OWN + t * OWN + out, 1)] = value

    rows_loop(HALO0, HALO0 + rows, down, 4)

    lane = lane_of()
    for edge, start in ((edge_prev, HALO0), (edge_next, HALO0 + rows - EDGE)):
        halo = None
        for i in (0, 1):
            for j in range(EDGE):
                at = i * EDGE + j
                edge[at] = keep[6 + i, 0, start + j]
                value = roll_x(keep[6 + i, 1, start + j : start + j + 1], 4 + 8 * at)
                halo = value if halo is None else jnp.where((lane >> 3) == at, value, halo)
        edge[2 * EDGE : 2 * EDGE + 1] = halo


def coarse_kernel(count, rows, gathered, from_left, from_right, gain, coef1, coef2, fields):
    del gain
    for relative, first, n, where in runs():
        base = block_at(count, CHUNK1, relative)
        for p in (0, 1):
            at = p * GROUPS1 + where
            fields[0, at : at + n] = gathered[pl.ds(base + p * OWN + first, n)]
    share = 2 * GROUPS1 // PER
    base = 6 * ((rows + 2 * HALO0) // PER)
    left, right = from_left[base : base + share], from_right[base : base + share]
    for j in range(PER):
        fields[1, j * share : (j + 1) * share] = unpack_three(left, right, j)

    for t in (0, 1):

        def level1(g, n, t=t):
            uv, fk = fields[t, pl.ds(g, n)], fields[t, pl.ds(GROUPS1 + g, n)]
            for i, value in enumerate(packed_jacobian(uv, fk, 1)):
                coef1[i, t, pl.ds(1 + g, n)] = value

        rows_loop(0, GROUPS1, level1, 6)
        pairs = []
        for p in (0, 1):
            start = p * GROUPS1 + OWN * LO2 - LO1
            pairs.append(
                jnp.concatenate(
                    [
                        restrict_12([fields[t, start + OWN * q + j : start + OWN * q + j + 1] for j in range(OWN)])
                        for q in range(HI2 - LO2)
                    ],
                    axis=0,
                )
            )
        inverse, other, _ = packed_jacobian(*pairs, 2)
        coef2[0, t, 1 : SIZE2 - 1] = inverse
        coef2[1, t, 1 : SIZE2 - 1] = other


def rest_kernel(
    count,
    rows,
    gathered,
    gain,
    coef1,
    coef2,
    keep0,
    from_prev,
    from_next,
    out,
    b1,
    x1,
    y1,
    d1,
    b2,
    x2,
    y2,
    d2,
    xu,
    yu,
    x0,
    y0,
    d0,
):
    lane, sub = lane_of(), sub_of()
    even = (sub & 1) == 0

    for relative, first, n, where in runs():
        base = block_at(count, 2 * OWN, relative)
        for t in (0, 1):
            b1[t, 1 + where : 1 + where + n] = gathered[pl.ds(base + t * OWN + first, n)]
    g0, g1, g2 = (gain[3 + i] for i in range(3))
    rows_loop(1, SIZE1 - 1, lambda g, n: packed_first(coef1, 0, b1, x1, d1, g, n, g0), 6)
    rows_loop(1, SIZE1 - 1, lambda g, n: packed_step(1, coef1, 0, b1, x1, y1, d1, g, n, CARRY1, g1), 6)
    rows_loop(1, SIZE1 - 1, lambda g, n: packed_step(1, coef1, 0, b1, y1, x1, d1, g, n, CARRY2, g2), 6)

    def down(q, n):
        at = OWN * q + OWN * LO2 - LO1 + 1
        for t, (c, other, spread) in enumerate(packed_terms(x1, at, OWN, 1)):
            here = pl.ds(at, OWN)
            res = b1[t, here] - coef1[2, t, here] * c + coef1[1, t, here] * other + spread
            b2[t, pl.ds(1 + q, 1)] = restrict_12([res[j : j + 1] for j in range(OWN)])

    rows_loop(0, HI2 - LO2, down, 1)

    n = HI2 - LO2
    g0, g1, g2 = (gain[6 + i] for i in range(3))
    packed_first(coef2, 0, b2, x2, d2, 1, n, g0)
    packed_step(2, coef2, 0, b2, x2, y2, d2, 1, n, CARRY1, g1)
    packed_step(2, coef2, 0, b2, y2, x2, d2, 1, n, CARRY2, g2)
    packed_step(2, coef2, 0, b2, x2, y2, d2, 1, n, None, g0)
    packed_step(2, coef2, 0, b2, y2, x2, d2, 1, n, CARRY1, g1)
    packed_step(2, coef2, 0, b2, x2, y2, d2, 1, n, CARRY2, g2)

    g0, g1, g2 = (gain[3 + i] for i in range(3))
    shift = LO_UP - LO1
    for t in (0, 1):
        for g in range(LO_UP, HI_UP):
            p = g % 4
            value = y2[t, g // 4 - LO2 + 1 : g // 4 - LO2 + 2]
            value = spread_x(spread_x(value, 1, p & 1), 2, p & 2)
            at = g - LO_UP + 1
            xu[t, at : at + 1] = x1[t, at + shift : at + shift + 1] + value
    n = HI_UP - LO_UP
    packed_step(1, coef1, shift, b1, xu, yu, d1, 1, n, None, g0)
    packed_step(1, coef1, shift, b1, yu, xu, d1, 1, n, CARRY1, g1)
    packed_step(1, coef1, shift, b1, xu, yu, d1, 1, n, CARRY2, g2)

    g0, g1, g2 = (gain[i] for i in range(3))
    for i in (0, 1):
        for at, ref in ((HALO0 - EDGE, from_prev), (HALO0 + rows, from_next)):
            x0[i, 0, at : at + EDGE] = ref[i * EDGE : (i + 1) * EDGE]
            for j in range(EDGE):
                x0[i, 1, at + j : at + j + 1] = roll_x(ref[2 * EDGE : 2 * EDGE + 1], -(4 + 8 * (i * EDGE + j)))
        for t in (0, 1):
            x0[i, t, HALO0 : HALO0 + rows] = keep0[6 + i, t, HALO0 : HALO0 + rows]
    for t in (0, 1):
        for row in range(-2, rows // 2 + 2):
            at = row // 2 - LO_UP + 1
            value = spread_x(yu[t, at : at + 1], 1, row & 1)
            for i, fine in enumerate((jnp.where(even, value, roll_z(value, 1)), jnp.where(even, roll_z(value, -1), value))):
                for y in (2 * row, 2 * row + 1):
                    if -EDGE <= y < rows + EDGE:
                        x0[i, t, y + HALO0 : y + HALO0 + 1] = x0[i, t, y + HALO0 : y + HALO0 + 1] + fine
    total = rows + 2 * HALO0
    rows_loop(2, total - 2, lambda r, n: cheb_step(0, keep0, x0, y0, d0, r, n, None, g0))
    rows_loop(3, total - 3, lambda r, n: cheb_step(0, keep0, y0, x0, d0, r, n, CARRY1, g1))
    rows_loop(4, total - 4, lambda r, n: cheb_step(0, keep0, x0, y0, d0, r, n, CARRY2, g2))
    for i in (0, 1):
        for y in range(rows):
            out[pl.ds(i * Z * rows + y, Z, stride=rows), :] = y0[i, 0, HALO0 + y]


def call(kernel, out_shapes, scratch, *args, space=pltpu.VMEM):
    out = [jax.ShapeDtypeStruct(shape, jnp.float32) for shape in out_shapes]
    return pl.pallas_call(
        kernel,
        out_shape=out,
        in_specs=[pl.BlockSpec(memory_space=space)] * len(args),
        out_specs=[pl.BlockSpec(memory_space=pltpu.VMEM)] * len(out),
        scratch_shapes=[pltpu.VMEM(s, jnp.float32) if isinstance(s, tuple) else s for s in scratch],
        compiler_params=pltpu.CompilerParams(vmem_limit_bytes=24 * 2**20),
    )(*args)


def shifted(value, axis, shift):
    count = lax.axis_size(axis)
    return lax.ppermute(value, axis, [((i + shift) % count, i) for i in range(count)])


def body(state, previous, feed, kill):
    _, depth, rows, cols = state.shape
    assert depth == Z and cols == X and rows == 4 * OWN
    across, count = lax.axis_size("gx"), lax.axis_size("gy")
    total0 = rows + 2 * HALO0
    state = state.reshape(2 * Z * rows, X)
    previous = previous.reshape(2 * Z * rows, X)
    feed = feed.reshape(Z * rows, X)
    kill = kill.reshape(Z * rows, X)
    inputs = (state, previous, feed, kill)

    strip = (6 * HALO0, Z, X)
    to_prev, to_next, main = call(
        functools.partial(pack_y_kernel, rows),
        [strip, strip, (6, rows, Z, X)],
        [*(a.shape for a in inputs), pltpu.SemaphoreType.DMA((4,))],
        *inputs,
        space=pl.ANY,
    )
    from_next = shifted(to_prev, "gy", 1)
    from_prev = shifted(to_next, "gy", -1)

    (packet,) = call(functools.partial(fields_kernel, count, rows), [(count * CHUNK1, Z, X)], [], main)
    gathered = lax.all_to_all(packet, "gy", 0, 0, tiled=True)

    strip = (6 * (total0 // PER) + 2 * GROUPS1 // PER + 1, Z, X)
    to_left, to_right, spread = call(
        functools.partial(pack_x_kernel, count, rows),
        [strip, strip, (Z, X)],
        [(2 * GROUPS1, Z, X)],
        main,
        from_prev,
        from_next,
        gathered,
    )
    from_right = shifted(to_left, "gx", 1)
    from_left = shifted(to_right, "gx", -1)
    spreads = [spread] + [shifted(spread, "gx", i) for i in range(2, across - 1)]

    edge = (2 * EDGE + 1, Z, X)
    pair0 = (2, 2, total0, Z, X)
    packet, to_prev, to_next, keep0, gain = call(
        functools.partial(level0_kernel, count, rows),
        [(count * 2 * OWN, Z, X), edge, edge, (8, 2, total0, Z, X), (9, Z, X)],
        [(6, 2, total0, Z, X), pair0, pair0, pair0],
        main,
        from_prev,
        from_next,
        from_left,
        from_right,
        *spreads,
    )
    sources = lax.all_to_all(packet, "gy", 0, 0, tiled=True)
    from_next = shifted(to_prev, "gy", 1)
    from_prev = shifted(to_next, "gy", -1)

    coef1, coef2 = call(
        functools.partial(coarse_kernel, count, rows),
        [(3, 2, SIZE1, Z, X), (2, 2, SIZE2, Z, X)],
        [(2, 2 * GROUPS1, Z, X)],
        gathered,
        from_left,
        from_right,
        gain,
    )

    one, two, up = (2, SIZE1, Z, X), (2, SIZE2, Z, X), (2, SIZE_UP, Z, X)
    (out,) = call(
        functools.partial(rest_kernel, count, rows),
        [(2 * Z * rows, X)],
        [one, one, one, one, two, two, two, two, up, up, pair0, pair0, pair0],
        sources,
        gain,
        coef1,
        coef2,
        keep0,
        from_prev,
        from_next,
    )
    return out.reshape(2, Z, rows, X)


def solution(mesh):
    placed = (
        P(None, None, "gy", "gx"),
        P(None, None, "gy", "gx"),
        P(None, "gy", "gx"),
        P(None, "gy", "gx"),
    )
    return jax.shard_map(
        body, mesh=mesh, in_specs=placed, out_specs=P(None, None, "gy", "gx"), check_vma=False
    )
```

```python
import functools

import jax
import jax.numpy as jnp
from jax import lax
from jax.experimental import pallas as pl
from jax.experimental.pallas import tpu as pltpu
from jax.sharding import PartitionSpec as P

DIFF = (40.0, 20.0)
INV_STEP = 2.0
LOWER = 0.25

_CENTRE = (1.0 + LOWER) / 2.0
_HALF = (1.0 - LOWER) / 2.0
_SIGMA = _CENTRE / _HALF
_RHO0 = 1.0 / _SIGMA
_RHO1 = 1.0 / (2.0 * _SIGMA - _RHO0)
_RHO2 = 1.0 / (2.0 * _SIGMA - _RHO1)

Z = 8
X = 128
HALO0 = 4
WIDE = 18
PER = X // WIDE
WIDE2 = 32
EDGE = 3
CHUNK = 4

LO1, HI1 = -4, 8
LO2, HI2 = -2, 3
LO_UP, HI_UP = -3, 7
SIZE1, SIZE2, SIZE_UP = HI1 - LO1 + 2, HI2 - LO2 + 2, HI_UP - LO_UP + 2
OWN = 4


def lane_of():
    return lax.broadcasted_iota(jnp.int32, (1, Z, X), 2)


def sub_of():
    return lax.broadcasted_iota(jnp.int32, (1, Z, X), 1)


def roll_x(tile, shift):
    shift = shift % X
    return pltpu.roll(tile, shift, 2) if shift else tile


def roll_z(tile, shift):
    shift = shift % Z
    return pltpu.roll(tile, shift, 1) if shift else tile


def rows_loop(lo, hi, body, step=CHUNK):
    full = (hi - lo) // step
    if full == 1:
        body(lo, step)
    elif full > 1:

        def trip(i, carry):
            body(lo + i * step, step)
            return carry

        lax.fori_loop(0, full, trip, 0)
    rest = hi - lo - full * step
    if rest:
        body(hi - rest, rest)


def neighbour_sums(read, r, n, k):
    lane = lane_of()
    low, high = lane < k, lane >= X - k
    centre = [read(t, r, n) for t in (0, 1)]
    right = [roll_x(c, k) for c in centre]
    left = [roll_x(c, -k) for c in centre]
    sums = []
    for t in (0, 1):
        c = centre[t]
        along_x = jnp.where(low, right[1 - t], right[t]) + jnp.where(high, left[1 - t], left[t])
        along_y = read(t, r - 1, n) + read(t, r + 1, n)
        along_z = 2.0 * roll_z(c, k) if 2 * k == Z else roll_z(c, k) + roll_z(c, -k)
        sums.append(along_x + along_y + along_z)
    return centre, sums


def jacobian(u, v, f, k, level):
    scale = 0.25**level
    product = u * v
    squared = v * v
    first = INV_STEP + squared + f + 6.0 * DIFF[0] * scale
    second = INV_STEP + f + k - 2.0 * product + 6.0 * DIFF[1] * scale
    return 2.0 * product, squared, 1.0 / first, 1.0 / second, first, second


def cheb_step(level, keep, source, target, d, r, n, carry, gain):
    scale = 0.25**level
    k = 1 << level
    u, nb_u = neighbour_sums(lambda t, a, m: source[0, t, pl.ds(a, m)], r, n, k)
    v, nb_v = neighbour_sums(lambda t, a, m: source[1, t, pl.ds(a, m)], r, n, k)
    rows = pl.ds(r, n)
    for t in (0, 1):
        cross, squared, inv_u, inv_v = (keep[i, t, rows] for i in range(4))
        res_u = inv_u * (keep[4, t, rows] - cross * v[t] + DIFF[0] * scale * nb_u[t]) - u[t]
        res_v = inv_v * (keep[5, t, rows] + squared * u[t] + DIFF[1] * scale * nb_v[t]) - v[t]
        du, dv = gain * res_u, gain * res_v
        if carry is not None:
            du = du + carry * d[0, t, rows]
            dv = dv + carry * d[1, t, rows]
        d[0, t, rows] = du
        d[1, t, rows] = dv
        target[0, t, rows] = u[t] + du
        target[1, t, rows] = v[t] + dv


def residual(level, keep, diag, source, r, n):
    scale = 0.25**level
    k = 1 << level
    u, nb_u = neighbour_sums(lambda t, a, m: source[0, t, pl.ds(a, m)], r, n, k)
    v, nb_v = neighbour_sums(lambda t, a, m: source[1, t, pl.ds(a, m)], r, n, k)
    rows = pl.ds(r, n)
    first, second = [], []
    for t in (0, 1):
        first.append(
            keep[4, t, rows] - diag[0, t, rows] * u[t] - keep[0, t, rows] * v[t] + DIFF[0] * scale * nb_u[t]
        )
        second.append(
            keep[5, t, rows] - diag[1, t, rows] * v[t] + keep[1, t, rows] * u[t] + DIFF[1] * scale * nb_v[t]
        )
    return first, second


CARRY1 = _RHO1 * _RHO0
CARRY2 = _RHO2 * _RHO1


def write_gains(spread, out):
    row = lax.broadcasted_iota(jnp.int32, (Z, X), 0)
    for level in range(3):
        top = jnp.max(jnp.where(row == level, spread, 0.0), axis=0, keepdims=True)
        tau = 1.0 / (1.0 + jnp.broadcast_to(top, (Z, X)))
        for i, factor in enumerate((1.0 / _CENTRE, 2.0 * _RHO1 / _HALF, 2.0 * _RHO2 / _HALF)):
            out[3 * level + i] = factor * tau


def pair_rows(value):
    n = value.shape[0] // 2
    pairs = value.reshape(n, 2, Z, X)
    return pairs[:, 0] + pairs[:, 1]


def restrict_01(first, second):
    lane, sub = lane_of(), sub_of()
    across = []
    for value in (first, second):
        a, b = value[0:1], value[1:2]
        across.append(jnp.where((lane & 1) == 0, a + roll_x(a, -1), b + roll_x(b, 1)))
    a, b = across
    return 0.125 * jnp.where((sub & 1) == 0, a + roll_z(a, -1), b + roll_z(b, 1))


def restrict_12(groups):
    lane, sub = lane_of(), sub_of()
    out = None
    for p, value in enumerate(groups):
        value = value + roll_x(value, 1 if p & 1 else -1)
        value = value + roll_x(value, 2 if p & 2 else -2)
        out = value if out is None else jnp.where((lane & 3) == p, value, out)
    return 0.125 * (out + jnp.where((sub & 2) == 0, roll_z(out, -2), roll_z(out, 2)))


def spread_x(tile, k, phase):
    return jnp.where((lane_of() & k) == phase, tile, roll_x(tile, -k if phase else k))


def packed_jacobian(uv, fk, level):
    scale = 0.25**level
    even = (sub_of() & 1) == 0
    u, v = jnp.where(even, uv, roll_z(uv, 1)), jnp.where(even, roll_z(uv, -1), uv)
    f, k = jnp.where(even, fk, roll_z(fk, 1)), jnp.where(even, roll_z(fk, -1), fk)
    product, squared = u * v, v * v
    diag = jnp.where(
        even,
        INV_STEP + squared + f + 6.0 * DIFF[0] * scale,
        INV_STEP + f + k - 2.0 * product + 6.0 * DIFF[1] * scale,
    )
    return 1.0 / diag, jnp.where(even, -2.0 * product, squared), diag


def packed_spread(uv, fk, level):
    scale = 0.25**level
    even = (sub_of() & 1) == 0
    inverse, other, _ = packed_jacobian(uv, fk, level)
    return jnp.where(even, 6.0 * DIFF[0] * scale - other, 6.0 * DIFF[1] * scale + other) * inverse


def packed_terms(source, g, n, level):
    k = 1 << level
    lane, sub = lane_of(), sub_of()
    even = (sub & 1) == 0
    first, last = (lane & (k - 1)) == 0, (lane & (k - 1)) == k - 1
    low, high = lane < k, lane >= X - k
    diff = jnp.where(even, DIFF[0] * 0.25**level, DIFF[1] * 0.25**level)
    wide = [source[t, pl.ds(g - 1, n + 2)] for t in (0, 1)]
    centre = [w[1 : n + 1] for w in wide]
    right = [roll_x(c, k) for c in centre]
    left = [roll_x(c, -k) for c in centre]
    out = []
    for t in (0, 1):
        c, w = centre[t], wide[t]
        total = jnp.where(low, right[1 - t], right[t]) + jnp.where(high, left[1 - t], left[t])
        if k == 2:
            ahead, back = roll_x(w, 1), roll_x(w, -1)
            total = total + jnp.where(first, back[0:n], ahead[1 : n + 1])
            total = total + jnp.where(last, ahead[2 : n + 2], back[1 : n + 1])
            total = total + roll_z(c, 2) + roll_z(c, -2)
        else:
            total = total + jnp.where(first, roll_x(w[0:n], -(k - 1)), roll_x(c, 1))
            total = total + jnp.where(last, roll_x(w[2 : n + 2], k - 1), roll_x(c, -1))
            total = total + 2.0 * roll_z(c, 4)
        other = jnp.where(even, roll_z(c, -1), roll_z(c, 1))
        out.append((c, other, diff * total))
    return out


def packed_first(coef, shift, b, target, d, g, n, gain):
    for t in (0, 1):
        value = gain * coef[0, t, pl.ds(g + shift, n)] * b[t, pl.ds(g + shift, n)]
        d[t, pl.ds(g, n)] = value
        target[t, pl.ds(g, n)] = value


def packed_step(level, coef, shift, b, source, target, d, g, n, carry, gain):
    for t, (c, other, spread) in enumerate(packed_terms(source, g, n, level)):
        at = pl.ds(g + shift, n)
        res = coef[0, t, at] * (b[t, at] + coef[1, t, at] * other + spread) - c
        delta = gain * res
        if carry is not None:
            delta = delta + carry * d[t, pl.ds(g, n)]
        d[t, pl.ds(g, n)] = delta
        target[t, pl.ds(g, n)] = c + delta


def plane(ref, f, y, rows):
    return ref[pl.ds(f * Z * rows + y, Z, stride=rows), :]


FIELDS1 = 6 * HALO0


def pack_y_kernel(rows, state, previous, feed, kill, to_prev, to_next, main, coarse, *scratch):
    sources, sems = scratch[:4], scratch[4]
    copies = [
        pltpu.make_async_copy(ref, held, sems.at[i])
        for i, (ref, held) in enumerate(zip((state, previous, feed, kill), sources))
    ]
    for copy in copies:
        copy.start()
    for copy in copies:
        copy.wait()
    state, previous, feed, kill = sources
    fields = [(state, 0), (state, 1), (previous, 0), (previous, 1), (feed, 0), (kill, 0)]
    for i, (ref, f) in enumerate(fields):
        for y in range(rows):
            value = plane(ref, f, y, rows)
            main[i, y] = value
            if y < HALO0:
                to_prev[i * HALO0 + y] = value
            if y >= rows - HALO0:
                to_next[i * HALO0 + y - rows + HALO0] = value
    for p, (i, j) in enumerate(((0, 1), (4, 5))):
        first, second = pair_rows(main[i]), pair_rows(main[j])
        for g in range(OWN):
            value = restrict_01(first[2 * g : 2 * g + 2], second[2 * g : 2 * g + 2])[0]
            for ref, at in ((coarse, 0), (to_prev, FIELDS1), (to_next, FIELDS1)):
                ref[at + p * OWN + g] = value


def fields_kernel(count, main, coarse, packet):
    row = lax.broadcasted_iota(jnp.int32, (Z, X), 0)
    u, v, f, k = (main[i] for i in (0, 1, 4, 5))
    cross, squared, inv_u, inv_v, _, _ = jacobian(u, v, f, k, 0)
    tops = [jnp.max(jnp.maximum((6.0 * DIFF[0] + cross) * inv_u, (6.0 * DIFF[1] + squared) * inv_v), axis=0)]
    pairs = [coarse[p * OWN : (p + 1) * OWN] for p in (0, 1)]
    tops.append(jnp.max(packed_spread(*pairs, 1), axis=0))
    uv, fk = (restrict_12([pair[j : j + 1] for j in range(OWN)]) for pair in pairs)
    tops.append(packed_spread(uv, fk, 2)[0])
    fields = jnp.where((sub_of() & 2) == 0, uv, fk)[0]
    result = jnp.zeros((Z, X), jnp.float32)
    for level, top in enumerate(tops):
        top = jnp.max(jnp.max(top, axis=1, keepdims=True), axis=0, keepdims=True)
        result = jnp.where(row == level, jnp.broadcast_to(top, (Z, X)), result)
    for c in range(count):
        packet[2 * c] = fields
        packet[2 * c + 1] = result


def block_at(count, chunk, relative):
    me = lax.axis_index("gy")
    return lax.rem(me + relative + count * 4, count) * chunk


GROUPS1 = HI1 - LO1
GROUPS2 = HI2 - LO2


def pack_slots(parts, width):
    lane = lane_of()
    left, right = None, None
    for j, part in enumerate(parts):
        a, b = roll_x(part, width * j), roll_x(part, width + width * j)
        left = a if left is None else jnp.where(lane >= width * j, a, left)
        right = b if right is None else jnp.where(lane >= width * j, b, right)
    return left, right


def unpack_slot(from_left, from_right, j, width):
    return jnp.where(lane_of() < X // 2, roll_x(from_right, -width * j), roll_x(from_left, X - width - width * j))


def pack_x_kernel(count, rows, main, coarse, from_prev, from_next, gathered, to_left, to_right, spread, held):
    total = rows + 2 * HALO0
    share = held.shape[0] // PER
    for i in range(6):
        strip = slice(i * HALO0, (i + 1) * HALO0)
        held[i * total : i * total + HALO0] = from_prev[strip]
        held[i * total + HALO0 : i * total + HALO0 + rows] = main[i]
        held[i * total + HALO0 + rows : (i + 1) * total] = from_next[strip]
    for p in (0, 1):
        for part, (ref, at) in enumerate(((from_prev, FIELDS1), (coarse, 0), (from_next, FIELDS1))):
            to = 6 * total + p * GROUPS1 + part * OWN
            held[to : to + OWN] = ref[at + p * OWN : at + (p + 1) * OWN]
    left, right = pack_slots([held[j * share : (j + 1) * share] for j in range(PER)], WIDE)
    to_left[0:share] = left
    to_right[0:share] = right
    slots = X // WIDE2
    parts = [gathered[pl.ds(block_at(count, 2, LO2 + q), 1)] for q in range(GROUPS2)]
    for i in range(0, GROUPS2, slots):
        left, right = pack_slots(parts[i : i + slots], WIDE2)
        at = share + i // slots
        to_left[at : at + 1] = left
        to_right[at : at + 1] = right
    top = gathered[1]
    for c in range(1, count):
        top = jnp.maximum(top, gathered[2 * c + 1])
    to_left[to_left.shape[0] - 1] = top
    to_right[to_right.shape[0] - 1] = top
    spread[...] = top


HALO1 = X // (2 * OWN)
EDGES = OWN + 1


def level0_kernel(rows, main, from_prev, from_next, from_left, from_right, *refs):
    spreads, (own, to_prev, to_next, keep, gain_out, fields, other, d, diag) = refs[:-9], refs[-9:]
    total = rows + 2 * HALO0
    share = (6 * total + 2 * GROUPS1) // PER
    top = jnp.maximum(from_left[from_left.shape[0] - 1], from_right[from_right.shape[0] - 1])
    for ref in spreads:
        top = jnp.maximum(top, ref[...])
    write_gains(top, gain_out)
    g0, g1, g2 = (gain_out[i] for i in range(3))
    for i in range(6):
        strip = slice(i * HALO0, (i + 1) * HALO0)
        fields[i, 0, 0:HALO0] = from_prev[strip]
        fields[i, 0, HALO0 : HALO0 + rows] = main[i]
        fields[i, 0, HALO0 + rows : total] = from_next[strip]
        for j in range(PER):
            lo, hi = max(i * total, j * share), min((i + 1) * total, (j + 1) * share)
            if lo < hi:
                strip = slice(lo - j * share, hi - j * share)
                fields[i, 1, lo - i * total : hi - i * total] = unpack_slot(from_left[strip], from_right[strip], j, WIDE)
    here = keep.at[6:8]

    def setup(r, n):
        at = pl.ds(r, n)
        u, nb_u = neighbour_sums(lambda t, a, m: fields[0, t, pl.ds(a, m)], r, n, 1)
        v, nb_v = neighbour_sums(lambda t, a, m: fields[1, t, pl.ds(a, m)], r, n, 1)
        for t in (0, 1):
            f, k = fields[4, t, at], fields[5, t, at]
            cross, squared, inv_u, inv_v, first, second = jacobian(u[t], v[t], f, k, 0)
            react = u[t] * squared
            b_u = (
                DIFF[0] * (nb_u[t] - 6.0 * u[t])
                - INV_STEP * (u[t] - fields[2, t, at])
                - react
                + f * (1.0 - u[t])
            )
            b_v = (
                DIFF[1] * (nb_v[t] - 6.0 * v[t]) - INV_STEP * (v[t] - fields[3, t, at]) + react - (f + k) * v[t]
            )
            for i, value in enumerate((cross, squared, inv_u, inv_v, b_u, b_v)):
                keep[i, t, at] = value
            diag[0, t, at] = first
            diag[1, t, at] = second
            for i, value in enumerate((g0 * inv_u * b_u, g0 * inv_v * b_v)):
                d[i, t, at] = value
                keep[6 + i, t, at] = value

    rows_loop(1, total - 1, setup)
    rows_loop(2, total - 2, lambda r, n: cheb_step(0, keep, here, other, d, r, n, CARRY1, g1))
    rows_loop(3, total - 3, lambda r, n: cheb_step(0, keep, other, here, d, r, n, CARRY2, g2))

    def down(r, n):
        first, second = residual(0, keep, diag, here, r, n)
        out = (r - HALO0) // 4
        for t in (0, 1):
            value = restrict_01(pair_rows(first[t]), pair_rows(second[t]))
            own[t, pl.ds(out, 1)] = value
            if t == 0:
                to_prev[pl.ds(out, 1)] = value
                to_next[pl.ds(out, 1)] = value

    rows_loop(HALO0, HALO0 + rows, down, 4)

    lane = lane_of()
    sides = None
    for j in range(OWN):
        value = roll_x(own[1, j : j + 1], HALO1 + 2 * HALO1 * j)
        sides = value if sides is None else jnp.where(lane // (2 * HALO1) == j, value, sides)
    for edge, start in ((to_prev, HALO0), (to_next, HALO0 + rows - EDGE)):
        edge[OWN : OWN + 1] = sides
        halo = None
        for i in (0, 1):
            for j in range(EDGE):
                at = i * EDGE + j
                edge[EDGES + at] = keep[6 + i, 0, start + j]
                value = roll_x(keep[6 + i, 1, start + j : start + j + 1], 4 + 8 * at)
                halo = value if halo is None else jnp.where((lane >> 3) == at, value, halo)
        edge[EDGES + 2 * EDGE : EDGES + 2 * EDGE + 1] = halo


def coarse_kernel(count, rows, coarse, from_prev, from_next, from_left, from_right, gathered, gain, coef1, coef2, fields):
    del gain
    share = (6 * (rows + 2 * HALO0) + 2 * GROUPS1) // PER
    base = 6 * (rows + 2 * HALO0) - (PER - 1) * share
    for p in (0, 1):
        for part, (ref, at) in enumerate(((from_prev, FIELDS1), (coarse, 0), (from_next, FIELDS1))):
            to = p * GROUPS1 + part * OWN
            fields[0, to : to + OWN] = ref[at + p * OWN : at + (p + 1) * OWN]
    fields[1] = unpack_slot(from_left[base:share], from_right[base:share], PER - 1, WIDE)
    for t in (0, 1):
        for i, value in enumerate(packed_jacobian(fields[t, 0:GROUPS1], fields[t, GROUPS1 : 2 * GROUPS1], 1)):
            coef1[i, t, 1 : SIZE1 - 1] = value

    sub = sub_of()
    slots = X // WIDE2
    for t in (0, 1):
        parts = []
        for q in range(GROUPS2):
            if t == 0:
                parts.append(gathered[pl.ds(block_at(count, 2, LO2 + q), 1)])
            else:
                at = share + q // slots
                parts.append(unpack_slot(from_left[at : at + 1], from_right[at : at + 1], q % slots, WIDE2))
        both = jnp.concatenate(parts, axis=0)
        uv = jnp.where((sub & 2) == 0, both, roll_z(both, 2))
        fk = jnp.where((sub & 2) == 0, roll_z(both, -2), both)
        inverse, other, _ = packed_jacobian(uv, fk, 2)
        coef2[0, t, 1 : SIZE2 - 1] = inverse
        coef2[1, t, 1 : SIZE2 - 1] = other


def level1_kernel(own, from_prev, from_next, coef1, gain, packet, keep, y1, d1):
    b1, x1 = keep.at[0], keep.at[1]
    for t in (0, 1):
        b1[t, 1 + OWN : 1 + 2 * OWN] = own[t]
        for ref, at in ((from_prev, 1), (from_next, 1 + 2 * OWN)):
            if t == 0:
                b1[t, at : at + OWN] = ref[0:OWN]
            else:
                for j in range(OWN):
                    b1[t, at + j : at + j + 1] = roll_x(ref[OWN : OWN + 1], -(HALO1 + 2 * HALO1 * j))
    g0, g1, g2 = (gain[3 + i] for i in range(3))
    n = GROUPS1
    packed_first(coef1, 0, b1, x1, d1, 1, n, g0)
    packed_step(1, coef1, 0, b1, x1, y1, d1, 1, n, CARRY1, g1)
    packed_step(1, coef1, 0, b1, y1, x1, d1, 1, n, CARRY2, g2)
    here = pl.ds(1 + OWN, OWN)
    c, other, spread = packed_terms(x1, 1 + OWN, OWN, 1)[0]
    res = b1[0, here] - coef1[2, 0, here] * c + coef1[1, 0, here] * other + spread
    value = restrict_12([res[j : j + 1] for j in range(OWN)])
    for c in range(packet.shape[0]):
        packet[c : c + 1] = value


def rest_kernel(
    across, count, gathered, gain, coef1, coef2, keep0, keep1, from_prev, from_next, out, d1, b2, x2, y2, d2, xu, yu, x0, y0, d0
):
    rows = out.shape[0] // (2 * Z)
    lane, sub = lane_of(), sub_of()
    even = (sub & 1) == 0
    b1, x1 = keep1.at[0], keep1.at[1]

    gx, gy = lax.axis_index("gx"), lax.axis_index("gy")
    columns = [lax.rem(gx + i + across, across) * count for i in (-1, 0, 1)]
    for q in range(GROUPS2):
        row = lax.rem(gy + LO2 + q + 4 * count, count)
        left, centre, right = (gathered[pl.ds(column + row, 1)] for column in columns)
        b2[0, 1 + q : 2 + q] = centre
        b2[1, 1 + q : 2 + q] = jnp.where(lane < X // 2, right, left)

    n = HI2 - LO2
    g0, g1, g2 = (gain[6 + i] for i in range(3))
    packed_first(coef2, 0, b2, x2, d2, 1, n, g0)
    packed_step(2, coef2, 0, b2, x2, y2, d2, 1, n, CARRY1, g1)
    packed_step(2, coef2, 0, b2, y2, x2, d2, 1, n, CARRY2, g2)
    packed_step(2, coef2, 0, b2, x2, y2, d2, 1, n, None, g0)
    packed_step(2, coef2, 0, b2, y2, x2, d2, 1, n, CARRY1, g1)
    packed_step(2, coef2, 0, b2, x2, y2, d2, 1, n, CARRY2, g2)

    g0, g1, g2 = (gain[3 + i] for i in range(3))
    shift = LO_UP - LO1
    for t in (0, 1):
        for g in range(LO_UP, HI_UP):
            p = g % 4
            value = y2[t, g // 4 - LO2 + 1 : g // 4 - LO2 + 2]
            value = spread_x(spread_x(value, 1, p & 1), 2, p & 2)
            at = g - LO_UP + 1
            xu[t, at : at + 1] = x1[t, at + shift : at + shift + 1] + value
    n = HI_UP - LO_UP
    packed_step(1, coef1, shift, b1, xu, yu, d1, 1, n, None, g0)
    packed_step(1, coef1, shift, b1, yu, xu, d1, 1, n, CARRY1, g1)
    packed_step(1, coef1, shift, b1, xu, yu, d1, 1, n, CARRY2, g2)

    g0, g1, g2 = (gain[i] for i in range(3))
    last = EDGES + 2 * EDGE
    for i in (0, 1):
        for at, ref in ((HALO0 - EDGE, from_prev), (HALO0 + rows, from_next)):
            x0[i, 0, at : at + EDGE] = ref[EDGES + i * EDGE : EDGES + (i + 1) * EDGE]
            for j in range(EDGE):
                x0[i, 1, at + j : at + j + 1] = roll_x(ref[last : last + 1], -(4 + 8 * (i * EDGE + j)))
        for t in (0, 1):
            x0[i, t, HALO0 : HALO0 + rows] = keep0[6 + i, t, HALO0 : HALO0 + rows]
    for t in (0, 1):
        for row in range(-2, rows // 2 + 2):
            at = row // 2 - LO_UP + 1
            value = spread_x(yu[t, at : at + 1], 1, row & 1)
            for i, fine in enumerate((jnp.where(even, value, roll_z(value, 1)), jnp.where(even, roll_z(value, -1), value))):
                for y in (2 * row, 2 * row + 1):
                    if -EDGE <= y < rows + EDGE:
                        x0[i, t, y + HALO0 : y + HALO0 + 1] = x0[i, t, y + HALO0 : y + HALO0 + 1] + fine
    total = rows + 2 * HALO0
    rows_loop(2, total - 2, lambda r, n: cheb_step(0, keep0, x0, y0, d0, r, n, None, g0))
    rows_loop(3, total - 3, lambda r, n: cheb_step(0, keep0, y0, x0, d0, r, n, CARRY1, g1))
    rows_loop(4, total - 4, lambda r, n: cheb_step(0, keep0, x0, y0, d0, r, n, CARRY2, g2))
    for i in (0, 1):
        for y in range(rows):
            out[pl.ds(i * Z * rows + y, Z, stride=rows), :] = y0[i, 0, HALO0 + y]


def call(kernel, out_shapes, scratch, *args, space=pltpu.VMEM):
    out = [jax.ShapeDtypeStruct(shape, jnp.float32) for shape in out_shapes]
    return pl.pallas_call(
        kernel,
        out_shape=out,
        in_specs=[pl.BlockSpec(memory_space=space)] * len(args),
        out_specs=[pl.BlockSpec(memory_space=pltpu.VMEM)] * len(out),
        scratch_shapes=[pltpu.VMEM(s, jnp.float32) if isinstance(s, tuple) else s for s in scratch],
        compiler_params=pltpu.CompilerParams(vmem_limit_bytes=24 * 2**20),
    )(*args)


def shifted(value, axis, shift):
    count = lax.axis_size(axis)
    return lax.ppermute(value, axis, [((i + shift) % count, i) for i in range(count)])


def body(state, previous, feed, kill):
    _, depth, rows, cols = state.shape
    assert depth == Z and cols == X and rows == 4 * OWN
    across, count = lax.axis_size("gx"), lax.axis_size("gy")
    total0 = rows + 2 * HALO0
    state = state.reshape(2 * Z * rows, X)
    previous = previous.reshape(2 * Z * rows, X)
    feed = feed.reshape(Z * rows, X)
    kill = kill.reshape(Z * rows, X)
    inputs = (state, previous, feed, kill)

    strip = (FIELDS1 + 2 * OWN, Z, X)
    to_prev, to_next, main, coarse = call(
        functools.partial(pack_y_kernel, rows),
        [strip, strip, (6, rows, Z, X), (2 * OWN, Z, X)],
        [*(a.shape for a in inputs), pltpu.SemaphoreType.DMA((4,))],
        *inputs,
        space=pltpu.HBM,
    )
    from_next = shifted(to_prev, "gy", 1)
    from_prev = shifted(to_next, "gy", -1)

    (packet,) = call(functools.partial(fields_kernel, count), [(2 * count, Z, X)], [], main, coarse)
    gathered = lax.all_to_all(packet, "gy", 0, 0, tiled=True)

    entries = 6 * total0 + 2 * GROUPS1
    assert entries % PER == 0
    strip = (entries // PER + -(-GROUPS2 * WIDE2 // X) + 1, Z, X)
    to_left, to_right, spread = call(
        functools.partial(pack_x_kernel, count, rows),
        [strip, strip, (Z, X)],
        [(entries, Z, X)],
        main,
        coarse,
        from_prev,
        from_next,
        gathered,
    )
    from_right = shifted(to_left, "gx", 1)
    from_left = shifted(to_right, "gx", -1)
    spreads = [spread] + [shifted(spread, "gx", i) for i in range(2, across - 1)]

    strip = (EDGES + 2 * EDGE + 1, Z, X)
    pair0 = (2, 2, total0, Z, X)
    own, to_prev, to_next, keep0, gain = call(
        functools.partial(level0_kernel, rows),
        [(2, OWN, Z, X), strip, strip, (8, 2, total0, Z, X), (9, Z, X)],
        [(6, 2, total0, Z, X), pair0, pair0, pair0],
        main,
        from_prev,
        from_next,
        from_left,
        from_right,
        *spreads,
    )
    coef1, coef2 = call(
        functools.partial(coarse_kernel, count, rows),
        [(3, 2, SIZE1, Z, X), (2, 2, SIZE2, Z, X)],
        [(2, 2 * GROUPS1, Z, X)],
        coarse,
        from_prev,
        from_next,
        from_left,
        from_right,
        gathered,
        gain,
    )
    from_next = shifted(to_prev, "gy", 1)
    from_prev = shifted(to_next, "gy", -1)

    one, two, up = (2, SIZE1, Z, X), (2, SIZE2, Z, X), (2, SIZE_UP, Z, X)
    packet, keep1 = call(
        level1_kernel, [(across * count, Z, X), (2, *one)], [one, one], own, from_prev, from_next, coef1, gain
    )
    gathered = lax.all_to_all(packet, ("gx", "gy"), 0, 0, tiled=True)

    (out,) = call(
        functools.partial(rest_kernel, across, count),
        [(2 * Z * rows, X)],
        [one, two, two, two, two, up, up, pair0, pair0, pair0],
        gathered,
        gain,
        coef1,
        coef2,
        keep0,
        keep1,
        from_prev,
        from_next,
    )
    return out.reshape(2, Z, rows, X)


def solution(mesh):
    placed = (
        P(None, None, "gy", "gx"),
        P(None, None, "gy", "gx"),
        P(None, "gy", "gx"),
        P(None, "gy", "gx"),
    )
    return jax.shard_map(
        body, mesh=mesh, in_specs=placed, out_specs=P(None, None, "gy", "gx"), check_vma=False
    )
```

```python
import functools

import jax
import jax.numpy as jnp
from jax import lax
from jax.experimental import pallas as pl
from jax.experimental.pallas import tpu as pltpu
from jax.sharding import PartitionSpec as P

DIFF = (40.0, 20.0)
INV_STEP = 2.0
LOWER = 0.25

_CENTRE = (1.0 + LOWER) / 2.0
_HALF = (1.0 - LOWER) / 2.0
_SIGMA = _CENTRE / _HALF
_RHO0 = 1.0 / _SIGMA
_RHO1 = 1.0 / (2.0 * _SIGMA - _RHO0)
_RHO2 = 1.0 / (2.0 * _SIGMA - _RHO1)

Z = 8
X = 128
HALO0 = 4
WIDE = 18
PER = X // WIDE
EDGE = 3
CHUNK = 4

LO1, HI1 = -4, 8
LO2, HI2 = -2, 3
LO_UP, HI_UP = -3, 7
SIZE1, SIZE2, SIZE_UP = HI1 - LO1 + 2, HI2 - LO2 + 2, HI_UP - LO_UP + 2
OWN = 4


def lane_of():
    return lax.broadcasted_iota(jnp.int32, (1, Z, X), 2)


def sub_of():
    return lax.broadcasted_iota(jnp.int32, (1, Z, X), 1)


def roll_x(tile, shift):
    shift = shift % X
    return pltpu.roll(tile, shift, 2) if shift else tile


def roll_z(tile, shift):
    shift = shift % Z
    return pltpu.roll(tile, shift, 1) if shift else tile


def rows_loop(lo, hi, body, step=CHUNK):
    full = (hi - lo) // step
    if full == 1:
        body(lo, step)
    elif full > 1:

        def trip(i, carry):
            body(lo + i * step, step)
            return carry

        lax.fori_loop(0, full, trip, 0)
    rest = hi - lo - full * step
    if rest:
        body(hi - rest, rest)


def neighbour_sums(read, r, n, k):
    lane = lane_of()
    low, high = lane < k, lane >= X - k
    centre = [read(t, r, n) for t in (0, 1)]
    right = [roll_x(c, k) for c in centre]
    left = [roll_x(c, -k) for c in centre]
    sums = []
    for t in (0, 1):
        c = centre[t]
        along_x = jnp.where(low, right[1 - t], right[t]) + jnp.where(high, left[1 - t], left[t])
        along_y = read(t, r - 1, n) + read(t, r + 1, n)
        along_z = 2.0 * roll_z(c, k) if 2 * k == Z else roll_z(c, k) + roll_z(c, -k)
        sums.append(along_x + along_y + along_z)
    return centre, sums


def jacobian(u, v, f, k, level):
    scale = 0.25**level
    product = u * v
    squared = v * v
    first = INV_STEP + squared + f + 6.0 * DIFF[0] * scale
    second = INV_STEP + f + k - 2.0 * product + 6.0 * DIFF[1] * scale
    return 2.0 * product, squared, 1.0 / first, 1.0 / second, first, second


def cheb_step(level, keep, source, target, d, r, n, carry, gain):
    scale = 0.25**level
    k = 1 << level
    u, nb_u = neighbour_sums(lambda t, a, m: source[0, t, pl.ds(a, m)], r, n, k)
    v, nb_v = neighbour_sums(lambda t, a, m: source[1, t, pl.ds(a, m)], r, n, k)
    rows = pl.ds(r, n)
    for t in (0, 1):
        cross, squared, inv_u, inv_v = (keep[i, t, rows] for i in range(4))
        res_u = inv_u * (keep[4, t, rows] - cross * v[t] + DIFF[0] * scale * nb_u[t]) - u[t]
        res_v = inv_v * (keep[5, t, rows] + squared * u[t] + DIFF[1] * scale * nb_v[t]) - v[t]
        du, dv = gain * res_u, gain * res_v
        if carry is not None:
            du = du + carry * d[0, t, rows]
            dv = dv + carry * d[1, t, rows]
        d[0, t, rows] = du
        d[1, t, rows] = dv
        target[0, t, rows] = u[t] + du
        target[1, t, rows] = v[t] + dv


def residual(level, keep, diag, source, r, n):
    scale = 0.25**level
    k = 1 << level
    u, nb_u = neighbour_sums(lambda t, a, m: source[0, t, pl.ds(a, m)], r, n, k)
    v, nb_v = neighbour_sums(lambda t, a, m: source[1, t, pl.ds(a, m)], r, n, k)
    rows = pl.ds(r, n)
    first, second = [], []
    for t in (0, 1):
        first.append(
            keep[4, t, rows] - diag[0, t, rows] * u[t] - keep[0, t, rows] * v[t] + DIFF[0] * scale * nb_u[t]
        )
        second.append(
            keep[5, t, rows] - diag[1, t, rows] * v[t] + keep[1, t, rows] * u[t] + DIFF[1] * scale * nb_v[t]
        )
    return first, second


CARRY1 = _RHO1 * _RHO0
CARRY2 = _RHO2 * _RHO1


def write_gains(spread, out):
    row = lax.broadcasted_iota(jnp.int32, (Z, X), 0)
    for level in range(3):
        top = jnp.max(jnp.where(row == level, spread, 0.0), axis=0, keepdims=True)
        tau = 1.0 / (1.0 + jnp.broadcast_to(top, (Z, X)))
        for i, factor in enumerate((1.0 / _CENTRE, 2.0 * _RHO1 / _HALF, 2.0 * _RHO2 / _HALF)):
            out[3 * level + i] = factor * tau


def pair_rows(value):
    n = value.shape[0] // 2
    pairs = value.reshape(n, 2, Z, X)
    return pairs[:, 0] + pairs[:, 1]


def restrict_01(first, second):
    lane, sub = lane_of(), sub_of()
    across = []
    for value in (first, second):
        a, b = value[0:1], value[1:2]
        across.append(jnp.where((lane & 1) == 0, a + roll_x(a, -1), b + roll_x(b, 1)))
    a, b = across
    return 0.125 * jnp.where((sub & 1) == 0, a + roll_z(a, -1), b + roll_z(b, 1))


def restrict_12(groups):
    lane, sub = lane_of(), sub_of()
    out = None
    for p, value in enumerate(groups):
        value = value + roll_x(value, 1 if p & 1 else -1)
        value = value + roll_x(value, 2 if p & 2 else -2)
        out = value if out is None else jnp.where((lane & 3) == p, value, out)
    return 0.125 * (out + jnp.where((sub & 2) == 0, roll_z(out, -2), roll_z(out, 2)))


def spread_x(tile, k, phase):
    return jnp.where((lane_of() & k) == phase, tile, roll_x(tile, -k if phase else k))


def packed_jacobian(uv, fk, level):
    scale = 0.25**level
    even = (sub_of() & 1) == 0
    u, v = jnp.where(even, uv, roll_z(uv, 1)), jnp.where(even, roll_z(uv, -1), uv)
    f, k = jnp.where(even, fk, roll_z(fk, 1)), jnp.where(even, roll_z(fk, -1), fk)
    product, squared = u * v, v * v
    diag = jnp.where(
        even,
        INV_STEP + squared + f + 6.0 * DIFF[0] * scale,
        INV_STEP + f + k - 2.0 * product + 6.0 * DIFF[1] * scale,
    )
    return 1.0 / diag, jnp.where(even, -2.0 * product, squared), diag


def packed_spread(uv, fk, level):
    scale = 0.25**level
    even = (sub_of() & 1) == 0
    inverse, other, _ = packed_jacobian(uv, fk, level)
    return jnp.where(even, 6.0 * DIFF[0] * scale - other, 6.0 * DIFF[1] * scale + other) * inverse


def packed_terms(source, g, n, level):
    k = 1 << level
    lane, sub = lane_of(), sub_of()
    even = (sub & 1) == 0
    first, last = (lane & (k - 1)) == 0, (lane & (k - 1)) == k - 1
    low, high = lane < k, lane >= X - k
    diff = jnp.where(even, DIFF[0] * 0.25**level, DIFF[1] * 0.25**level)
    wide = [source[t, pl.ds(g - 1, n + 2)] for t in (0, 1)]
    centre = [w[1 : n + 1] for w in wide]
    right = [roll_x(c, k) for c in centre]
    left = [roll_x(c, -k) for c in centre]
    out = []
    for t in (0, 1):
        c, w = centre[t], wide[t]
        total = jnp.where(low, right[1 - t], right[t]) + jnp.where(high, left[1 - t], left[t])
        if k == 2:
            ahead, back = roll_x(w, 1), roll_x(w, -1)
            total = total + jnp.where(first, back[0:n], ahead[1 : n + 1])
            total = total + jnp.where(last, ahead[2 : n + 2], back[1 : n + 1])
            total = total + roll_z(c, 2) + roll_z(c, -2)
        else:
            total = total + jnp.where(first, roll_x(w[0:n], -(k - 1)), roll_x(c, 1))
            total = total + jnp.where(last, roll_x(w[2 : n + 2], k - 1), roll_x(c, -1))
            total = total + 2.0 * roll_z(c, 4)
        other = jnp.where(even, roll_z(c, -1), roll_z(c, 1))
        out.append((c, other, diff * total))
    return out


def packed_first(coef, shift, b, target, d, g, n, gain):
    for t in (0, 1):
        value = gain * coef[0, t, pl.ds(g + shift, n)] * b[t, pl.ds(g + shift, n)]
        d[t, pl.ds(g, n)] = value
        target[t, pl.ds(g, n)] = value


def packed_step(level, coef, shift, b, source, target, d, g, n, carry, gain):
    for t, (c, other, spread) in enumerate(packed_terms(source, g, n, level)):
        at = pl.ds(g + shift, n)
        res = coef[0, t, at] * (b[t, at] + coef[1, t, at] * other + spread) - c
        delta = gain * res
        if carry is not None:
            delta = delta + carry * d[t, pl.ds(g, n)]
        d[t, pl.ds(g, n)] = delta
        target[t, pl.ds(g, n)] = c + delta


def plane(ref, f, y, rows):
    return ref[pl.ds(f * Z * rows + y, Z, stride=rows), :]


FIELDS1 = 6 * HALO0


def is_even(axis):
    return lax.rem(lax.axis_index(axis), 2) == 0


def prev_of(even, first, second, at):
    return jnp.where(even, first[at], second[at])


def next_of(even, first, second, at):
    return jnp.where(even, second[at], first[at])


def first_kernel(rows, state, previous, feed, kill, first, second, main, coarse, packet, *scratch):
    sources, sems = scratch[:4], scratch[4]
    copies = [
        pltpu.make_async_copy(ref, held, sems.at[i])
        for i, (ref, held) in enumerate(zip((state, previous, feed, kill), sources))
    ]
    for copy in copies:
        copy.start()
    for copy in copies:
        copy.wait()
    even = is_even("gy")
    state, previous, feed, kill = sources
    fields = [(state, 0), (state, 1), (previous, 0), (previous, 1), (feed, 0), (kill, 0)]
    for i, (ref, f) in enumerate(fields):
        for y in range(rows):
            main[i, y] = plane(ref, f, y, rows)
        top, bottom = main[i, 0:HALO0], main[i, rows - HALO0 : rows]
        at = slice(i * HALO0, (i + 1) * HALO0)
        first[at] = jnp.where(even, top, bottom)
        second[at] = jnp.where(even, bottom, top)
    u, v, f, k = (main[i] for i in (0, 1, 4, 5))
    sums = [pair_rows(value) for value in (u, v, f, k)]
    pairs = []
    for p in (0, 1):
        values = [
            restrict_01(sums[2 * p][2 * g : 2 * g + 2], sums[2 * p + 1][2 * g : 2 * g + 2]) for g in range(OWN)
        ]
        pairs.append(jnp.concatenate(values, axis=0))
        coarse[p * OWN : (p + 1) * OWN] = pairs[p]
        for ref in (first, second):
            ref[FIELDS1 + p * OWN : FIELDS1 + (p + 1) * OWN] = pairs[p]

    row = lax.broadcasted_iota(jnp.int32, (Z, X), 0)
    cross, squared, inv_u, inv_v, _, _ = jacobian(u, v, f, k, 0)
    tops = [jnp.max(jnp.maximum((6.0 * DIFF[0] + cross) * inv_u, (6.0 * DIFF[1] + squared) * inv_v), axis=0)]
    tops.append(jnp.max(packed_spread(*pairs, 1), axis=0))
    uv, fk = (restrict_12([pair[j : j + 1] for j in range(OWN)]) for pair in pairs)
    tops.append(packed_spread(uv, fk, 2)[0])
    both = jnp.where((sub_of() & 2) == 0, uv, fk)[0]
    result = jnp.zeros((Z, X), jnp.float32)
    for level, top in enumerate(tops):
        top = jnp.max(jnp.max(top, axis=1, keepdims=True), axis=0, keepdims=True)
        result = jnp.where(row == level, jnp.broadcast_to(top, (Z, X)), result)
    for c in range(packet.shape[0] // 2):
        packet[2 * c] = both
        packet[2 * c + 1] = result


def around(across, count, gathered, chunk):
    lane = lane_of()
    gx, gy = lax.axis_index("gx"), lax.axis_index("gy")
    columns = [lax.rem(gx + i + across, across) * count for i in (-1, 0, 1)]
    out = [[], []]
    for q in range(LO2, HI2):
        row = lax.rem(gy + q + 4 * count, count)
        left, centre, right = (gathered[pl.ds((column + row) * chunk, 1)] for column in columns)
        out[0].append(centre)
        out[1].append(jnp.where(lane < X // 2, right, left))
    return [jnp.concatenate(groups, axis=0) for groups in out]


GROUPS1 = HI1 - LO1
GROUPS2 = HI2 - LO2


def pack_slots(parts, width):
    lane = lane_of()
    left, right = None, None
    for j, part in enumerate(parts):
        a, b = roll_x(part, width * j), roll_x(part, width + width * j)
        left = a if left is None else jnp.where(lane >= width * j, a, left)
        right = b if right is None else jnp.where(lane >= width * j, b, right)
    return left, right


def unpack_slot(from_left, from_right, j, width):
    return jnp.where(lane_of() < X // 2, roll_x(from_right, -width * j), roll_x(from_left, X - width - width * j))


def pack_x_kernel(rows, main, coarse, y_first, y_second, first, second, held):
    even = is_even("gy")
    total = rows + 2 * HALO0
    share = held.shape[0] // PER
    for i in range(6):
        strip = slice(i * HALO0, (i + 1) * HALO0)
        held[i * total : i * total + HALO0] = prev_of(even, y_first, y_second, strip)
        held[i * total + HALO0 : i * total + HALO0 + rows] = main[i]
        held[i * total + HALO0 + rows : (i + 1) * total] = next_of(even, y_first, y_second, strip)
    for p in (0, 1):
        to = 6 * total + p * GROUPS1
        strip = slice(FIELDS1 + p * OWN, FIELDS1 + (p + 1) * OWN)
        held[to : to + OWN] = prev_of(even, y_first, y_second, strip)
        held[to + OWN : to + 2 * OWN] = coarse[p * OWN : (p + 1) * OWN]
        held[to + 2 * OWN : to + 3 * OWN] = next_of(even, y_first, y_second, strip)
    left, right = pack_slots([held[j * share : (j + 1) * share] for j in range(PER)], WIDE)
    even = is_even("gx")
    first[...] = jnp.where(even, left, right)
    second[...] = jnp.where(even, right, left)


HALO1 = X // (2 * OWN)
EDGES = OWN + 1


def level0_kernel(
    rows, main, y_first, y_second, x_first, x_second, gathered, own, first, second, keep, gain_out, fields, other, d, diag
):
    even, even_x = is_even("gy"), is_even("gx")
    total = rows + 2 * HALO0
    share = (6 * total + 2 * GROUPS1) // PER
    top = gathered[1]
    for c in range(1, gathered.shape[0] // 2):
        top = jnp.maximum(top, gathered[2 * c + 1])
    write_gains(top, gain_out)
    g0, g1, g2 = (gain_out[i] for i in range(3))
    for i in range(6):
        strip = slice(i * HALO0, (i + 1) * HALO0)
        fields[i, 0, 0:HALO0] = prev_of(even, y_first, y_second, strip)
        fields[i, 0, HALO0 : HALO0 + rows] = main[i]
        fields[i, 0, HALO0 + rows : total] = next_of(even, y_first, y_second, strip)
        for j in range(PER):
            lo, hi = max(i * total, j * share), min((i + 1) * total, (j + 1) * share)
            if lo < hi:
                strip = slice(lo - j * share, hi - j * share)
                left, right = prev_of(even_x, x_first, x_second, strip), next_of(even_x, x_first, x_second, strip)
                fields[i, 1, lo - i * total : hi - i * total] = unpack_slot(left, right, j, WIDE)
    here = keep.at[6:8]

    def setup(r, n):
        at = pl.ds(r, n)
        u, nb_u = neighbour_sums(lambda t, a, m: fields[0, t, pl.ds(a, m)], r, n, 1)
        v, nb_v = neighbour_sums(lambda t, a, m: fields[1, t, pl.ds(a, m)], r, n, 1)
        for t in (0, 1):
            f, k = fields[4, t, at], fields[5, t, at]
            cross, squared, inv_u, inv_v, first, second = jacobian(u[t], v[t], f, k, 0)
            react = u[t] * squared
            b_u = (
                DIFF[0] * (nb_u[t] - 6.0 * u[t])
                - INV_STEP * (u[t] - fields[2, t, at])
                - react
                + f * (1.0 - u[t])
            )
            b_v = (
                DIFF[1] * (nb_v[t] - 6.0 * v[t]) - INV_STEP * (v[t] - fields[3, t, at]) + react - (f + k) * v[t]
            )
            for i, value in enumerate((cross, squared, inv_u, inv_v, b_u, b_v)):
                keep[i, t, at] = value
            diag[0, t, at] = first
            diag[1, t, at] = second
            for i, value in enumerate((g0 * inv_u * b_u, g0 * inv_v * b_v)):
                d[i, t, at] = value
                keep[6 + i, t, at] = value

    rows_loop(1, total - 1, setup)
    rows_loop(2, total - 2, lambda r, n: cheb_step(0, keep, here, other, d, r, n, CARRY1, g1))
    rows_loop(3, total - 3, lambda r, n: cheb_step(0, keep, other, here, d, r, n, CARRY2, g2))

    def down(r, n):
        res = residual(0, keep, diag, here, r, n)
        out = (r - HALO0) // 4
        for t in (0, 1):
            value = restrict_01(pair_rows(res[0][t]), pair_rows(res[1][t]))
            own[t, pl.ds(out, 1)] = value
            if t == 0:
                first[pl.ds(out, 1)] = value
                second[pl.ds(out, 1)] = value

    rows_loop(HALO0, HALO0 + rows, down, 4)

    lane = lane_of()
    sides = None
    for j in range(OWN):
        value = roll_x(own[1, j : j + 1], HALO1 + 2 * HALO1 * j)
        sides = value if sides is None else jnp.where(lane // (2 * HALO1) == j, value, sides)
    edges = []
    for start in (HALO0, HALO0 + rows - EDGE):
        halo = None
        for i in (0, 1):
            for j in range(EDGE):
                at = i * EDGE + j
                value = roll_x(keep[6 + i, 1, start + j : start + j + 1], 4 + 8 * at)
                halo = value if halo is None else jnp.where((lane >> 3) == at, value, halo)
        edges.append([keep[6, 0, start : start + EDGE], keep[7, 0, start : start + EDGE], halo])
    top, bottom = (jnp.concatenate(parts, axis=0) for parts in edges)
    for ref in (first, second):
        ref[OWN : OWN + 1] = sides
    first[EDGES : EDGES + 2 * EDGE + 1] = jnp.where(even, top, bottom)
    second[EDGES : EDGES + 2 * EDGE + 1] = jnp.where(even, bottom, top)


def coarse_kernel(
    across, count, rows, coarse, y_first, y_second, x_first, x_second, gathered, gain, coef1, coef2, fields
):
    del gain
    even, even_x = is_even("gy"), is_even("gx")
    share = (6 * (rows + 2 * HALO0) + 2 * GROUPS1) // PER
    base = 6 * (rows + 2 * HALO0) - (PER - 1) * share
    for p in (0, 1):
        to = p * GROUPS1
        strip = slice(FIELDS1 + p * OWN, FIELDS1 + (p + 1) * OWN)
        fields[0, to : to + OWN] = prev_of(even, y_first, y_second, strip)
        fields[0, to + OWN : to + 2 * OWN] = coarse[p * OWN : (p + 1) * OWN]
        fields[0, to + 2 * OWN : to + 3 * OWN] = next_of(even, y_first, y_second, strip)
    strip = slice(base, share)
    left, right = prev_of(even_x, x_first, x_second, strip), next_of(even_x, x_first, x_second, strip)
    fields[1] = unpack_slot(left, right, PER - 1, WIDE)
    for t in (0, 1):
        for i, value in enumerate(packed_jacobian(fields[t, 0:GROUPS1], fields[t, GROUPS1 : 2 * GROUPS1], 1)):
            coef1[i, t, 1 : SIZE1 - 1] = value

    sub = sub_of()
    for t, both in enumerate(around(across, count, gathered, 2)):
        uv = jnp.where((sub & 2) == 0, both, roll_z(both, 2))
        fk = jnp.where((sub & 2) == 0, roll_z(both, -2), both)
        inverse, other, _ = packed_jacobian(uv, fk, 2)
        coef2[0, t, 1 : SIZE2 - 1] = inverse
        coef2[1, t, 1 : SIZE2 - 1] = other


def level1_kernel(own, first, second, coef1, gain, packet, keep, y1, d1):
    b1, x1 = keep.at[0], keep.at[1]
    even = is_even("gy")
    for t in (0, 1):
        b1[t, 1 + OWN : 1 + 2 * OWN] = own[t]
        for take, at in ((prev_of, 1), (next_of, 1 + 2 * OWN)):
            if t == 0:
                b1[t, at : at + OWN] = take(even, first, second, slice(0, OWN))
            else:
                sides = take(even, first, second, slice(OWN, OWN + 1))
                for j in range(OWN):
                    b1[t, at + j : at + j + 1] = roll_x(sides, -(HALO1 + 2 * HALO1 * j))
    g0, g1, g2 = (gain[3 + i] for i in range(3))
    n = GROUPS1
    packed_first(coef1, 0, b1, x1, d1, 1, n, g0)
    packed_step(1, coef1, 0, b1, x1, y1, d1, 1, n, CARRY1, g1)
    packed_step(1, coef1, 0, b1, y1, x1, d1, 1, n, CARRY2, g2)
    here = pl.ds(1 + OWN, OWN)
    c, other, spread = packed_terms(x1, 1 + OWN, OWN, 1)[0]
    res = b1[0, here] - coef1[2, 0, here] * c + coef1[1, 0, here] * other + spread
    value = restrict_12([res[j : j + 1] for j in range(OWN)])
    for c in range(packet.shape[0]):
        packet[c : c + 1] = value


def rest_kernel(
    across, count, gathered, gain, coef1, coef2, keep0, keep1, first, second, out, d1, b2, x2, y2, d2, xu, yu, x0, y0, d0
):
    rows = out.shape[0] // (2 * Z)
    even = (sub_of() & 1) == 0
    b1, x1 = keep1.at[0], keep1.at[1]

    for t, groups in enumerate(around(across, count, gathered, 1)):
        b2[t, 1 : SIZE2 - 1] = groups

    n = HI2 - LO2
    g0, g1, g2 = (gain[6 + i] for i in range(3))
    packed_first(coef2, 0, b2, x2, d2, 1, n, g0)
    packed_step(2, coef2, 0, b2, x2, y2, d2, 1, n, CARRY1, g1)
    packed_step(2, coef2, 0, b2, y2, x2, d2, 1, n, CARRY2, g2)
    packed_step(2, coef2, 0, b2, x2, y2, d2, 1, n, None, g0)
    packed_step(2, coef2, 0, b2, y2, x2, d2, 1, n, CARRY1, g1)
    packed_step(2, coef2, 0, b2, x2, y2, d2, 1, n, CARRY2, g2)

    g0, g1, g2 = (gain[3 + i] for i in range(3))
    shift = LO_UP - LO1
    for t in (0, 1):
        for g in range(LO_UP, HI_UP):
            p = g % 4
            value = y2[t, g // 4 - LO2 + 1 : g // 4 - LO2 + 2]
            value = spread_x(spread_x(value, 1, p & 1), 2, p & 2)
            at = g - LO_UP + 1
            xu[t, at : at + 1] = x1[t, at + shift : at + shift + 1] + value
    n = HI_UP - LO_UP
    packed_step(1, coef1, shift, b1, xu, yu, d1, 1, n, None, g0)
    packed_step(1, coef1, shift, b1, yu, xu, d1, 1, n, CARRY1, g1)
    packed_step(1, coef1, shift, b1, xu, yu, d1, 1, n, CARRY2, g2)

    g0, g1, g2 = (gain[i] for i in range(3))
    last = EDGES + 2 * EDGE
    even_y = is_even("gy")
    for i in (0, 1):
        for at, take in ((HALO0 - EDGE, prev_of), (HALO0 + rows, next_of)):
            strip = slice(EDGES + i * EDGE, EDGES + (i + 1) * EDGE)
            x0[i, 0, at : at + EDGE] = take(even_y, first, second, strip)
            sides = take(even_y, first, second, slice(last, last + 1))
            for j in range(EDGE):
                x0[i, 1, at + j : at + j + 1] = roll_x(sides, -(4 + 8 * (i * EDGE + j)))
        for t in (0, 1):
            x0[i, t, HALO0 : HALO0 + rows] = keep0[6 + i, t, HALO0 : HALO0 + rows]
    for t in (0, 1):
        for row in range(-2, rows // 2 + 2):
            at = row // 2 - LO_UP + 1
            value = spread_x(yu[t, at : at + 1], 1, row & 1)
            for i, fine in enumerate((jnp.where(even, value, roll_z(value, 1)), jnp.where(even, roll_z(value, -1), value))):
                for y in (2 * row, 2 * row + 1):
                    if -EDGE <= y < rows + EDGE:
                        x0[i, t, y + HALO0 : y + HALO0 + 1] = x0[i, t, y + HALO0 : y + HALO0 + 1] + fine
    total = rows + 2 * HALO0
    rows_loop(2, total - 2, lambda r, n: cheb_step(0, keep0, x0, y0, d0, r, n, None, g0))
    rows_loop(3, total - 3, lambda r, n: cheb_step(0, keep0, y0, x0, d0, r, n, CARRY1, g1))
    rows_loop(4, total - 4, lambda r, n: cheb_step(0, keep0, x0, y0, d0, r, n, CARRY2, g2))
    for i in (0, 1):
        for y in range(rows):
            out[pl.ds(i * Z * rows + y, Z, stride=rows), :] = y0[i, 0, HALO0 + y]


def call(kernel, out_shapes, scratch, *args, space=pltpu.VMEM):
    out = [jax.ShapeDtypeStruct(shape, jnp.float32) for shape in out_shapes]
    return pl.pallas_call(
        kernel,
        out_shape=out,
        in_specs=[pl.BlockSpec(memory_space=space)] * len(args),
        out_specs=[pl.BlockSpec(memory_space=pltpu.VMEM)] * len(out),
        scratch_shapes=[pltpu.VMEM(s, jnp.float32) if isinstance(s, tuple) else s for s in scratch],
        compiler_params=pltpu.CompilerParams(vmem_limit_bytes=24 * 2**20),
    )(*args)


def swap(value, axis, step):
    count = lax.axis_size(axis)
    assert count % 2 == 0
    pairs = [(i, (i + step) % count) for i in range(0, count, 2)]
    return lax.ppermute(value, axis, pairs + [(j, i) for i, j in pairs])


def exchange(first, second, axis):
    return swap(first, axis, -1), swap(second, axis, 1)


def body(state, previous, feed, kill):
    _, depth, rows, cols = state.shape
    assert depth == Z and cols == X and rows == 4 * OWN
    across, count = lax.axis_size("gx"), lax.axis_size("gy")
    total0 = rows + 2 * HALO0
    state = state.reshape(2 * Z * rows, X)
    previous = previous.reshape(2 * Z * rows, X)
    feed = feed.reshape(Z * rows, X)
    kill = kill.reshape(Z * rows, X)
    inputs = (state, previous, feed, kill)

    strip = (FIELDS1 + 2 * OWN, Z, X)
    first, second, main, coarse, packet = call(
        functools.partial(first_kernel, rows),
        [strip, strip, (6, rows, Z, X), (2 * OWN, Z, X), (2 * across * count, Z, X)],
        [*(a.shape for a in inputs), pltpu.SemaphoreType.DMA((4,))],
        *(pltpu.with_memory_space_constraint(a, pltpu.HBM) for a in inputs),
        space=pltpu.HBM,
    )
    fields2 = lax.all_to_all(packet, ("gx", "gy"), 0, 0, tiled=True)
    y_packets = exchange(first, second, "gy")

    entries = 6 * total0 + 2 * GROUPS1
    assert entries % PER == 0
    strip = (entries // PER, Z, X)
    first, second = call(
        functools.partial(pack_x_kernel, rows), [strip, strip], [(entries, Z, X)], main, coarse, *y_packets
    )
    x_packets = exchange(first, second, "gx")

    strip = (EDGES + 2 * EDGE + 1, Z, X)
    pair0 = (2, 2, total0, Z, X)
    own, first, second, keep0, gain = call(
        functools.partial(level0_kernel, rows),
        [(2, OWN, Z, X), strip, strip, (8, 2, total0, Z, X), (9, Z, X)],
        [(6, 2, total0, Z, X), pair0, pair0, pair0],
        main,
        *y_packets,
        *x_packets,
        fields2,
    )
    coef1, coef2 = call(
        functools.partial(coarse_kernel, across, count, rows),
        [(3, 2, SIZE1, Z, X), (2, 2, SIZE2, Z, X)],
        [(2, 2 * GROUPS1, Z, X)],
        coarse,
        *y_packets,
        *x_packets,
        fields2,
        gain,
    )
    b_packets = exchange(first, second, "gy")

    one, two, up = (2, SIZE1, Z, X), (2, SIZE2, Z, X), (2, SIZE_UP, Z, X)
    packet, keep1 = call(
        level1_kernel, [(across * count, Z, X), (2, *one)], [one, one], own, *b_packets, coef1, gain
    )
    gathered = lax.all_to_all(packet, ("gx", "gy"), 0, 0, tiled=True)

    (out,) = call(
        functools.partial(rest_kernel, across, count),
        [(2 * Z * rows, X)],
        [one, two, two, two, two, up, up, pair0, pair0, pair0],
        gathered,
        gain,
        coef1,
        coef2,
        keep0,
        keep1,
        *b_packets,
    )
    return out.reshape(2, Z, rows, X)


def solution(mesh):
    placed = (
        P(None, None, "gy", "gx"),
        P(None, None, "gy", "gx"),
        P(None, "gy", "gx"),
        P(None, "gy", "gx"),
    )
    return jax.shard_map(
        body, mesh=mesh, in_specs=placed, out_specs=P(None, None, "gy", "gx"), check_vma=False
    )
```

```python
import functools

import jax
import jax.numpy as jnp
from jax import lax
from jax.experimental import pallas as pl
from jax.experimental.pallas import tpu as pltpu
from jax.sharding import PartitionSpec as P

DIFF = (40.0, 20.0)
INV_STEP = 2.0
LOWER = 0.25

_CENTRE = (1.0 + LOWER) / 2.0
_HALF = (1.0 - LOWER) / 2.0
_SIGMA = _CENTRE / _HALF
_RHO0 = 1.0 / _SIGMA
_RHO1 = 1.0 / (2.0 * _SIGMA - _RHO0)
_RHO2 = 1.0 / (2.0 * _SIGMA - _RHO1)

Z = 8
X = 128
HALO0 = 4
HALOS = (4, 4, 3, 3, 3, 3)
STARTS = tuple(sum(HALOS[:i]) for i in range(6))
FIELDS1 = sum(HALOS)
FIELDS2 = FIELDS1 + 8
WIDE = 18
PER = X // WIDE
WIDE2 = 32
EDGE = 3
CHUNK = 4

LO1, HI1 = -4, 8
LO2, HI2 = -2, 3
LO_UP, HI_UP = -3, 7
SIZE1, SIZE2, SIZE_UP = HI1 - LO1 + 2, HI2 - LO2 + 2, HI_UP - LO_UP + 2
OWN = 4


def lane_of():
    return lax.broadcasted_iota(jnp.int32, (1, Z, X), 2)


def sub_of():
    return lax.broadcasted_iota(jnp.int32, (1, Z, X), 1)


def roll_x(tile, shift):
    shift = shift % X
    return pltpu.roll(tile, shift, 2) if shift else tile


def roll_z(tile, shift):
    shift = shift % Z
    return pltpu.roll(tile, shift, 1) if shift else tile


def rows_loop(lo, hi, body, step=CHUNK):
    full = (hi - lo) // step
    if full == 1:
        body(lo, step)
    elif full > 1:

        def trip(i, carry):
            body(lo + i * step, step)
            return carry

        lax.fori_loop(0, full, trip, 0)
    rest = hi - lo - full * step
    if rest:
        body(hi - rest, rest)


def neighbour_sums(read, r, n, k):
    lane = lane_of()
    low, high = lane < k, lane >= X - k
    centre = [read(t, r, n) for t in (0, 1)]
    right = [roll_x(c, k) for c in centre]
    left = [roll_x(c, -k) for c in centre]
    sums = []
    for t in (0, 1):
        c = centre[t]
        along_x = jnp.where(low, right[1 - t], right[t]) + jnp.where(high, left[1 - t], left[t])
        along_y = read(t, r - 1, n) + read(t, r + 1, n)
        along_z = 2.0 * roll_z(c, k) if 2 * k == Z else roll_z(c, k) + roll_z(c, -k)
        sums.append(along_x + along_y + along_z)
    return centre, sums


def jacobian(u, v, f, k, level):
    scale = 0.25**level
    product = u * v
    squared = v * v
    first = INV_STEP + squared + f + 6.0 * DIFF[0] * scale
    second = INV_STEP + f + k - 2.0 * product + 6.0 * DIFF[1] * scale
    return 2.0 * product, squared, 1.0 / first, 1.0 / second, first, second


def cheb_step(level, keep, source, target, d, r, n, carry, gain):
    scale = 0.25**level
    k = 1 << level
    u, nb_u = neighbour_sums(lambda t, a, m: source[0, t, pl.ds(a, m)], r, n, k)
    v, nb_v = neighbour_sums(lambda t, a, m: source[1, t, pl.ds(a, m)], r, n, k)
    rows = pl.ds(r, n)
    for t in (0, 1):
        cross, squared, inv_u, inv_v = (keep[i, t, rows] for i in range(4))
        res_u = inv_u * (keep[4, t, rows] - cross * v[t] + DIFF[0] * scale * nb_u[t]) - u[t]
        res_v = inv_v * (keep[5, t, rows] + squared * u[t] + DIFF[1] * scale * nb_v[t]) - v[t]
        du, dv = gain * res_u, gain * res_v
        if carry is not None:
            du = du + carry * d[0, t, rows]
            dv = dv + carry * d[1, t, rows]
        d[0, t, rows] = du
        d[1, t, rows] = dv
        target[0, t, rows] = u[t] + du
        target[1, t, rows] = v[t] + dv


def residual(level, keep, diag, source, r, n):
    scale = 0.25**level
    k = 1 << level
    u, nb_u = neighbour_sums(lambda t, a, m: source[0, t, pl.ds(a, m)], r, n, k)
    v, nb_v = neighbour_sums(lambda t, a, m: source[1, t, pl.ds(a, m)], r, n, k)
    rows = pl.ds(r, n)
    first, second = [], []
    for t in (0, 1):
        first.append(
            keep[4, t, rows] - diag[0, t, rows] * u[t] - keep[0, t, rows] * v[t] + DIFF[0] * scale * nb_u[t]
        )
        second.append(
            keep[5, t, rows] - diag[1, t, rows] * v[t] + keep[1, t, rows] * u[t] + DIFF[1] * scale * nb_v[t]
        )
    return first, second


CARRY1 = _RHO1 * _RHO0
CARRY2 = _RHO2 * _RHO1


def write_gains(spread, out):
    lane = lax.broadcasted_iota(jnp.int32, (1, X), 1)
    for level in range(3):
        top = jnp.max(jnp.where(lane == level, spread, 0.0), axis=1, keepdims=True)
        tau = 1.0 / (1.0 + jnp.broadcast_to(top, (Z, X)))
        for i, factor in enumerate((1.0 / _CENTRE, 2.0 * _RHO1 / _HALF, 2.0 * _RHO2 / _HALF)):
            out[3 * level + i] = factor * tau


def pair_rows(value):
    n = value.shape[0] // 2
    pairs = value.reshape(n, 2, Z, X)
    return pairs[:, 0] + pairs[:, 1]


def restrict_01(first, second):
    lane, sub = lane_of(), sub_of()
    across = []
    for value in (first, second):
        a, b = value[0:1], value[1:2]
        across.append(jnp.where((lane & 1) == 0, a + roll_x(a, -1), b + roll_x(b, 1)))
    a, b = across
    return 0.125 * jnp.where((sub & 1) == 0, a + roll_z(a, -1), b + roll_z(b, 1))


def restrict_12(groups):
    lane, sub = lane_of(), sub_of()
    out = None
    for p, value in enumerate(groups):
        value = value + roll_x(value, 1 if p & 1 else -1)
        value = value + roll_x(value, 2 if p & 2 else -2)
        out = value if out is None else jnp.where((lane & 3) == p, value, out)
    return 0.125 * (out + jnp.where((sub & 2) == 0, roll_z(out, -2), roll_z(out, 2)))


def spread_x(tile, k, phase):
    return jnp.where((lane_of() & k) == phase, tile, roll_x(tile, -k if phase else k))


def packed_jacobian(uv, fk, level):
    scale = 0.25**level
    even = (sub_of() & 1) == 0
    u, v = jnp.where(even, uv, roll_z(uv, 1)), jnp.where(even, roll_z(uv, -1), uv)
    f, k = jnp.where(even, fk, roll_z(fk, 1)), jnp.where(even, roll_z(fk, -1), fk)
    product, squared = u * v, v * v
    diag = jnp.where(
        even,
        INV_STEP + squared + f + 6.0 * DIFF[0] * scale,
        INV_STEP + f + k - 2.0 * product + 6.0 * DIFF[1] * scale,
    )
    return 1.0 / diag, jnp.where(even, -2.0 * product, squared), diag


def packed_spread(uv, fk, level):
    scale = 0.25**level
    even = (sub_of() & 1) == 0
    inverse, other, _ = packed_jacobian(uv, fk, level)
    return jnp.where(even, 6.0 * DIFF[0] * scale - other, 6.0 * DIFF[1] * scale + other) * inverse


def packed_terms(source, g, n, level):
    k = 1 << level
    lane, sub = lane_of(), sub_of()
    even = (sub & 1) == 0
    first, last = (lane & (k - 1)) == 0, (lane & (k - 1)) == k - 1
    low, high = lane < k, lane >= X - k
    diff = jnp.where(even, DIFF[0] * 0.25**level, DIFF[1] * 0.25**level)
    wide = [source[t, pl.ds(g - 1, n + 2)] for t in (0, 1)]
    centre = [w[1 : n + 1] for w in wide]
    right = [roll_x(c, k) for c in centre]
    left = [roll_x(c, -k) for c in centre]
    out = []
    for t in (0, 1):
        c, w = centre[t], wide[t]
        total = jnp.where(low, right[1 - t], right[t]) + jnp.where(high, left[1 - t], left[t])
        if k == 2:
            ahead, back = roll_x(w, 1), roll_x(w, -1)
            total = total + jnp.where(first, back[0:n], ahead[1 : n + 1])
            total = total + jnp.where(last, ahead[2 : n + 2], back[1 : n + 1])
            total = total + roll_z(c, 2) + roll_z(c, -2)
        else:
            total = total + jnp.where(first, roll_x(w[0:n], -(k - 1)), roll_x(c, 1))
            total = total + jnp.where(last, roll_x(w[2 : n + 2], k - 1), roll_x(c, -1))
            total = total + 2.0 * roll_z(c, 4)
        other = jnp.where(even, roll_z(c, -1), roll_z(c, 1))
        out.append((c, other, diff * total))
    return out


def packed_first(coef, shift, b, target, d, g, n, gain):
    for t in (0, 1):
        value = gain * coef[0, t, pl.ds(g + shift, n)] * b[t, pl.ds(g + shift, n)]
        d[t, pl.ds(g, n)] = value
        target[t, pl.ds(g, n)] = value


def packed_step(level, coef, shift, b, source, target, d, g, n, carry, gain):
    for t, (c, other, spread) in enumerate(packed_terms(source, g, n, level)):
        at = pl.ds(g + shift, n)
        res = coef[0, t, at] * (b[t, at] + coef[1, t, at] * other + spread) - c
        delta = gain * res
        if carry is not None:
            delta = delta + carry * d[t, pl.ds(g, n)]
        d[t, pl.ds(g, n)] = delta
        target[t, pl.ds(g, n)] = c + delta


def plane(ref, f, y, rows):
    return ref[pl.ds(f * Z * rows + y, Z, stride=rows), :]


def is_even(axis):
    return lax.rem(lax.axis_index(axis), 2) == 0


def prev_of(even, first, second, at):
    return jnp.where(even, first[at], second[at])


def next_of(even, first, second, at):
    return jnp.where(even, second[at], first[at])


def first_kernel(rows, state, previous, feed, kill, first, second, main, coarse, *scratch):
    sources, sems = scratch[:4], scratch[4]
    copies = [
        pltpu.make_async_copy(ref, held, sems.at[i])
        for i, (ref, held) in enumerate(zip((state, previous, feed, kill), sources))
    ]
    for copy in copies:
        copy.start()
    for copy in copies:
        copy.wait()
    even = is_even("gy")
    state, previous, feed, kill = sources
    fields = [(state, 0), (state, 1), (previous, 0), (previous, 1), (feed, 0), (kill, 0)]
    for i, (ref, f) in enumerate(fields):
        for y in range(rows):
            main[i, y] = plane(ref, f, y, rows)
        top, bottom = main[i, 0 : HALOS[i]], main[i, rows - HALOS[i] : rows]
        at = slice(STARTS[i], STARTS[i] + HALOS[i])
        first[at] = jnp.where(even, top, bottom)
        second[at] = jnp.where(even, bottom, top)
    u, v, f, k = (main[i] for i in (0, 1, 4, 5))
    sums = [pair_rows(value) for value in (u, v, f, k)]
    pairs = []
    for p in (0, 1):
        values = [
            restrict_01(sums[2 * p][2 * g : 2 * g + 2], sums[2 * p + 1][2 * g : 2 * g + 2]) for g in range(OWN)
        ]
        pairs.append(jnp.concatenate(values, axis=0))
        coarse[p * OWN : (p + 1) * OWN] = pairs[p]
        for ref in (first, second):
            ref[FIELDS1 + p * OWN : FIELDS1 + (p + 1) * OWN] = pairs[p]

    uv, fk = (restrict_12([pair[j : j + 1] for j in range(OWN)]) for pair in pairs)
    both = jnp.where((sub_of() & 2) == 0, uv, fk)
    coarse[2 * OWN : 2 * OWN + 1] = both
    for ref in (first, second):
        ref[FIELDS2 : FIELDS2 + 1] = both


def split_fields2(both):
    low = (sub_of() & 2) == 0
    return jnp.where(low, both, roll_z(both, 2)), jnp.where(low, roll_z(both, -2), both)


def spread_kernel(main, coarse, out):
    lane = lax.broadcasted_iota(jnp.int32, (1, X), 1)
    u, v, f, k = (main[i] for i in (0, 1, 4, 5))
    cross, squared, inv_u, inv_v, _, _ = jacobian(u, v, f, k, 0)
    tops = [jnp.max(jnp.maximum((6.0 * DIFF[0] + cross) * inv_u, (6.0 * DIFF[1] + squared) * inv_v), axis=0)]
    tops.append(jnp.max(packed_spread(coarse[0:OWN], coarse[OWN : 2 * OWN], 1), axis=0))
    tops.append(packed_spread(*split_fields2(coarse[2 * OWN : 2 * OWN + 1]), 2)[0])
    result = jnp.zeros((1, X), jnp.float32)
    for level, top in enumerate(tops):
        top = jnp.max(jnp.max(top, axis=0, keepdims=True), axis=1, keepdims=True)
        result = jnp.where(lane == level, jnp.broadcast_to(top, (1, X)), result)
    out[...] = jnp.broadcast_to(result[None], out.shape)


def around(across, count, gathered):
    lane = lane_of()
    gx, gy = lax.axis_index("gx"), lax.axis_index("gy")
    columns = [lax.rem(gx + i + across, across) * count for i in (-1, 0, 1)]
    out = [[], []]
    for q in range(LO2, HI2):
        row = lax.rem(gy + q + 4 * count, count)
        left, centre, right = (gathered[pl.ds(column + row, 1)] for column in columns)
        out[0].append(centre)
        out[1].append(jnp.where(lane < X // 2, right, left))
    return [jnp.concatenate(groups, axis=0) for groups in out]


GROUPS1 = HI1 - LO1
GROUPS2 = HI2 - LO2


def entry(rows, i):
    starts = [0]
    for halo in HALOS:
        starts.append(starts[-1] + rows + 2 * halo)
    return (starts + [starts[-1] + 2 * GROUPS1])[i]


def entry_tiles(rows):
    return -(-entry(rows, 7) // PER)


def pack_slots(parts, width):
    lane = lane_of()
    left, right = None, None
    for j, part in enumerate(parts):
        a, b = roll_x(part, width * j), roll_x(part, width + width * j)
        left = a if left is None else jnp.where(lane >= width * j, a, left)
        right = b if right is None else jnp.where(lane >= width * j, b, right)
    return left, right


def unpack_slot(from_left, from_right, j, width):
    return jnp.where(lane_of() < X // 2, roll_x(from_right, -width * j), roll_x(from_left, X - width - width * j))


def unpack_entries(even_x, x_first, x_second, share, lo, hi):
    out = []
    for j in range(PER):
        a, b = max(lo, j * share), min(hi, (j + 1) * share)
        if a < b:
            strip = slice(a - j * share, b - j * share)
            left, right = prev_of(even_x, x_first, x_second, strip), next_of(even_x, x_first, x_second, strip)
            out.append((a - lo, b - lo, unpack_slot(left, right, j, WIDE)))
    return out


def unpack_fields2(even_x, x_first, x_second, share, j):
    strip = slice(share, share + 1)
    left, right = prev_of(even_x, x_first, x_second, strip), next_of(even_x, x_first, x_second, strip)
    return unpack_slot(left, right, j, WIDE2)


def pack_x_kernel(rows, main, coarse, y_first, y_second, first, second, held):
    even = is_even("gy")
    share = entry_tiles(rows)
    for i, halo in enumerate(HALOS):
        strip = slice(STARTS[i], STARTS[i] + halo)
        to = entry(rows, i)
        held[to : to + halo] = prev_of(even, y_first, y_second, strip)
        held[to + halo : to + halo + rows] = main[i]
        held[to + halo + rows : to + 2 * halo + rows] = next_of(even, y_first, y_second, strip)
    for p in (0, 1):
        to = entry(rows, 6) + p * GROUPS1
        strip = slice(FIELDS1 + p * OWN, FIELDS1 + (p + 1) * OWN)
        held[to : to + OWN] = prev_of(even, y_first, y_second, strip)
        held[to + OWN : to + 2 * OWN] = coarse[p * OWN : (p + 1) * OWN]
        held[to + 2 * OWN : to + 3 * OWN] = next_of(even, y_first, y_second, strip)
    left, right = pack_slots([held[j * share : (j + 1) * share] for j in range(PER)], WIDE)
    strip = slice(FIELDS2, FIELDS2 + 1)
    own = coarse[2 * OWN : 2 * OWN + 1]
    parts = [prev_of(even, y_first, y_second, strip), own, next_of(even, y_first, y_second, strip)]
    left2, right2 = pack_slots(parts, WIDE2)
    even = is_even("gx")
    first[0:share] = jnp.where(even, left, right)
    second[0:share] = jnp.where(even, right, left)
    first[share : share + 1] = jnp.where(even, left2, right2)
    second[share : share + 1] = jnp.where(even, right2, left2)


HALO1 = X // (2 * OWN)
EDGES = OWN + 1
FAR = EDGES + 2 * EDGE + 1


def level0_kernel(
    rows, main, y_first, y_second, x_first, x_second, gathered, own, first, second, keep, gain_out, fields, other, d, diag
):
    even, even_x = is_even("gy"), is_even("gx")
    total = rows + 2 * HALO0
    share = entry_tiles(rows)
    top = gathered[0]
    for c in range(1, gathered.shape[0]):
        top = jnp.maximum(top, gathered[c])
    write_gains(top, gain_out)
    g0, g1, g2 = (gain_out[i] for i in range(3))
    for i, halo in enumerate(HALOS):
        strip = slice(STARTS[i], STARTS[i] + halo)
        skip = HALO0 - halo
        fields[i, 0, skip:HALO0] = prev_of(even, y_first, y_second, strip)
        fields[i, 0, HALO0 : HALO0 + rows] = main[i]
        fields[i, 0, HALO0 + rows : total - skip] = next_of(even, y_first, y_second, strip)
        for a, b, value in unpack_entries(even_x, x_first, x_second, share, entry(rows, i), entry(rows, i + 1)):
            fields[i, 1, a + skip : b + skip] = value
    here = keep.at[6:8]

    def setup(r, n):
        at = pl.ds(r, n)
        u, nb_u = neighbour_sums(lambda t, a, m: fields[0, t, pl.ds(a, m)], r, n, 1)
        v, nb_v = neighbour_sums(lambda t, a, m: fields[1, t, pl.ds(a, m)], r, n, 1)
        for t in (0, 1):
            f, k = fields[4, t, at], fields[5, t, at]
            cross, squared, inv_u, inv_v, first, second = jacobian(u[t], v[t], f, k, 0)
            react = u[t] * squared
            b_u = (
                DIFF[0] * (nb_u[t] - 6.0 * u[t])
                - INV_STEP * (u[t] - fields[2, t, at])
                - react
                + f * (1.0 - u[t])
            )
            b_v = (
                DIFF[1] * (nb_v[t] - 6.0 * v[t]) - INV_STEP * (v[t] - fields[3, t, at]) + react - (f + k) * v[t]
            )
            for i, value in enumerate((cross, squared, inv_u, inv_v, b_u, b_v)):
                keep[i, t, at] = value
            diag[0, t, at] = first
            diag[1, t, at] = second
            for i, value in enumerate((g0 * inv_u * b_u, g0 * inv_v * b_v)):
                d[i, t, at] = value
                keep[6 + i, t, at] = value

    rows_loop(1, total - 1, setup)
    rows_loop(2, total - 2, lambda r, n: cheb_step(0, keep, here, other, d, r, n, CARRY1, g1))
    rows_loop(3, total - 3, lambda r, n: cheb_step(0, keep, other, here, d, r, n, CARRY2, g2))

    def down(r, n):
        res = residual(0, keep, diag, here, r, n)
        out = (r - HALO0) // 4
        for t in (0, 1):
            value = restrict_01(pair_rows(res[0][t]), pair_rows(res[1][t]))
            own[t, pl.ds(out, 1)] = value
            if t == 0:
                first[pl.ds(out, 1)] = value
                second[pl.ds(out, 1)] = value

    rows_loop(HALO0, HALO0 + rows, down, 4)

    lane = lane_of()
    sides = None
    for j in range(OWN):
        value = roll_x(own[1, j : j + 1], HALO1 + 2 * HALO1 * j)
        sides = value if sides is None else jnp.where(lane // (2 * HALO1) == j, value, sides)
    edges = []
    for start in (HALO0, HALO0 + rows - EDGE):
        halo = None
        for i in (0, 1):
            for j in range(EDGE):
                at = i * EDGE + j
                value = roll_x(keep[6 + i, 1, start + j : start + j + 1], 4 + 8 * at)
                halo = value if halo is None else jnp.where((lane >> 3) == at, value, halo)
        edges.append([keep[6, 0, start : start + EDGE], keep[7, 0, start : start + EDGE], halo])
    top, bottom = (jnp.concatenate(parts, axis=0) for parts in edges)
    for ref in (first, second):
        ref[OWN : OWN + 1] = sides
    strip = slice(FIELDS2, FIELDS2 + 1)
    for t in (0, 1):
        if t == 0:
            before, after = prev_of(even, y_first, y_second, strip), next_of(even, y_first, y_second, strip)
        else:
            before, after = (unpack_fields2(even_x, x_first, x_second, share, j) for j in (0, 2))
        first[FAR + t : FAR + t + 1] = jnp.where(even, after, before)
        second[FAR + t : FAR + t + 1] = jnp.where(even, before, after)
    first[EDGES : EDGES + 2 * EDGE + 1] = jnp.where(even, top, bottom)
    second[EDGES : EDGES + 2 * EDGE + 1] = jnp.where(even, bottom, top)


def coarse1_kernel(rows, coarse, y_first, y_second, x_first, x_second, gain, coef, fields):
    del gain
    even, even_x = is_even("gy"), is_even("gx")
    share = entry_tiles(rows)
    for p in (0, 1):
        to = p * GROUPS1
        strip = slice(FIELDS1 + p * OWN, FIELDS1 + (p + 1) * OWN)
        fields[0, to : to + OWN] = prev_of(even, y_first, y_second, strip)
        fields[0, to + OWN : to + 2 * OWN] = coarse[p * OWN : (p + 1) * OWN]
        fields[0, to + 2 * OWN : to + 3 * OWN] = next_of(even, y_first, y_second, strip)
    for a, b, value in unpack_entries(even_x, x_first, x_second, share, entry(rows, 6), entry(rows, 7)):
        fields[1, a:b] = value
    for t in (0, 1):
        for i, value in enumerate(packed_jacobian(fields[t, 0:GROUPS1], fields[t, GROUPS1 : 2 * GROUPS1], 1)):
            coef[i, t, 1 : SIZE1 - 1] = value


def coarse2_kernel(rows, coarse, y_first, y_second, x_first, x_second, b_first, b_second, coef):
    even, even_x = is_even("gy"), is_even("gx")
    share = entry_tiles(rows)
    near = slice(FIELDS2, FIELDS2 + 1)
    for t in (0, 1):
        far = slice(FAR + t, FAR + t + 1)
        if t == 0:
            middle = [
                prev_of(even, y_first, y_second, near),
                coarse[2 * OWN : 2 * OWN + 1],
                next_of(even, y_first, y_second, near),
            ]
        else:
            middle = [unpack_fields2(even_x, x_first, x_second, share, j) for j in range(3)]
        parts = [prev_of(even, b_first, b_second, far), *middle, next_of(even, b_first, b_second, far)]
        inverse, other, _ = packed_jacobian(*split_fields2(jnp.concatenate(parts, axis=0)), 2)
        coef[0, t, 1 : SIZE2 - 1] = inverse
        coef[1, t, 1 : SIZE2 - 1] = other


def level1_kernel(own, first, second, coef1, gain, packet, keep, y1, d1):
    b1, x1 = keep.at[0], keep.at[1]
    even = is_even("gy")
    for t in (0, 1):
        b1[t, 1 + OWN : 1 + 2 * OWN] = own[t]
        for take, at in ((prev_of, 1), (next_of, 1 + 2 * OWN)):
            if t == 0:
                b1[t, at : at + OWN] = take(even, first, second, slice(0, OWN))
            else:
                sides = take(even, first, second, slice(OWN, OWN + 1))
                for j in range(OWN):
                    b1[t, at + j : at + j + 1] = roll_x(sides, -(HALO1 + 2 * HALO1 * j))
    g0, g1, g2 = (gain[3 + i] for i in range(3))
    n = GROUPS1
    packed_first(coef1, 0, b1, x1, d1, 1, n, g0)
    packed_step(1, coef1, 0, b1, x1, y1, d1, 1, n, CARRY1, g1)
    packed_step(1, coef1, 0, b1, y1, x1, d1, 1, n, CARRY2, g2)
    here = pl.ds(1 + OWN, OWN)
    c, other, spread = packed_terms(x1, 1 + OWN, OWN, 1)[0]
    res = b1[0, here] - coef1[2, 0, here] * c + coef1[1, 0, here] * other + spread
    value = restrict_12([res[j : j + 1] for j in range(OWN)])
    for c in range(packet.shape[0]):
        packet[c : c + 1] = value


def rest_kernel(
    across, count, gathered, gain, coef1, coef2, keep0, keep1, first, second, out, d1, b2, x2, y2, d2, xu, yu, x0, y0, d0
):
    rows = out.shape[0] // (2 * Z)
    even = (sub_of() & 1) == 0
    b1, x1 = keep1.at[0], keep1.at[1]

    for t, groups in enumerate(around(across, count, gathered)):
        b2[t, 1 : SIZE2 - 1] = groups

    n = HI2 - LO2
    g0, g1, g2 = (gain[6 + i] for i in range(3))
    packed_first(coef2, 0, b2, x2, d2, 1, n, g0)
    packed_step(2, coef2, 0, b2, x2, y2, d2, 1, n, CARRY1, g1)
    packed_step(2, coef2, 0, b2, y2, x2, d2, 1, n, CARRY2, g2)
    packed_step(2, coef2, 0, b2, x2, y2, d2, 1, n, None, g0)
    packed_step(2, coef2, 0, b2, y2, x2, d2, 1, n, CARRY1, g1)
    packed_step(2, coef2, 0, b2, x2, y2, d2, 1, n, CARRY2, g2)

    g0, g1, g2 = (gain[3 + i] for i in range(3))
    shift = LO_UP - LO1
    for t in (0, 1):
        for g in range(LO_UP, HI_UP):
            p = g % 4
            value = y2[t, g // 4 - LO2 + 1 : g // 4 - LO2 + 2]
            value = spread_x(spread_x(value, 1, p & 1), 2, p & 2)
            at = g - LO_UP + 1
            xu[t, at : at + 1] = x1[t, at + shift : at + shift + 1] + value
    n = HI_UP - LO_UP
    packed_step(1, coef1, shift, b1, xu, yu, d1, 1, n, None, g0)
    packed_step(1, coef1, shift, b1, yu, xu, d1, 1, n, CARRY1, g1)
    packed_step(1, coef1, shift, b1, xu, yu, d1, 1, n, CARRY2, g2)

    g0, g1, g2 = (gain[i] for i in range(3))
    last = EDGES + 2 * EDGE
    even_y = is_even("gy")
    for i in (0, 1):
        for at, take in ((HALO0 - EDGE, prev_of), (HALO0 + rows, next_of)):
            strip = slice(EDGES + i * EDGE, EDGES + (i + 1) * EDGE)
            x0[i, 0, at : at + EDGE] = take(even_y, first, second, strip)
            sides = take(even_y, first, second, slice(last, last + 1))
            for j in range(EDGE):
                x0[i, 1, at + j : at + j + 1] = roll_x(sides, -(4 + 8 * (i * EDGE + j)))
        for t in (0, 1):
            x0[i, t, HALO0 : HALO0 + rows] = keep0[6 + i, t, HALO0 : HALO0 + rows]
    for t in (0, 1):
        for row in range(-2, rows // 2 + 2):
            at = row // 2 - LO_UP + 1
            value = spread_x(yu[t, at : at + 1], 1, row & 1)
            for i, fine in enumerate((jnp.where(even, value, roll_z(value, 1)), jnp.where(even, roll_z(value, -1), value))):
                for y in (2 * row, 2 * row + 1):
                    if -EDGE <= y < rows + EDGE:
                        x0[i, t, y + HALO0 : y + HALO0 + 1] = x0[i, t, y + HALO0 : y + HALO0 + 1] + fine
    total = rows + 2 * HALO0
    rows_loop(2, total - 2, lambda r, n: cheb_step(0, keep0, x0, y0, d0, r, n, None, g0))
    rows_loop(3, total - 3, lambda r, n: cheb_step(0, keep0, y0, x0, d0, r, n, CARRY1, g1))
    rows_loop(4, total - 4, lambda r, n: cheb_step(0, keep0, x0, y0, d0, r, n, CARRY2, g2))
    for i in (0, 1):
        for y in range(rows):
            out[pl.ds(i * Z * rows + y, Z, stride=rows), :] = y0[i, 0, HALO0 + y]


def call(kernel, out_shapes, scratch, *args, space=pltpu.VMEM):
    out = [jax.ShapeDtypeStruct(shape, jnp.float32) for shape in out_shapes]
    return pl.pallas_call(
        kernel,
        out_shape=out,
        in_specs=[pl.BlockSpec(memory_space=space)] * len(args),
        out_specs=[pl.BlockSpec(memory_space=pltpu.VMEM)] * len(out),
        scratch_shapes=[pltpu.VMEM(s, jnp.float32) if isinstance(s, tuple) else s for s in scratch],
        compiler_params=pltpu.CompilerParams(vmem_limit_bytes=24 * 2**20),
    )(*args)


def swap(value, axis, step):
    count = lax.axis_size(axis)
    assert count % 2 == 0
    pairs = [(i, (i + step) % count) for i in range(0, count, 2)]
    return lax.ppermute(value, axis, pairs + [(j, i) for i, j in pairs])


def exchange(first, second, axis):
    return swap(first, axis, -1), swap(second, axis, 1)


def body(state, previous, feed, kill):
    _, depth, rows, cols = state.shape
    assert depth == Z and cols == X and rows == 4 * OWN
    across, count = lax.axis_size("gx"), lax.axis_size("gy")
    total0 = rows + 2 * HALO0
    state = state.reshape(2 * Z * rows, X)
    previous = previous.reshape(2 * Z * rows, X)
    feed = feed.reshape(Z * rows, X)
    kill = kill.reshape(Z * rows, X)
    inputs = (state, previous, feed, kill)

    strip = (FIELDS2 + 1, Z, X)
    first, second, main, coarse = call(
        functools.partial(first_kernel, rows),
        [strip, strip, (6, rows, Z, X), (2 * OWN + 1, Z, X)],
        [*(a.shape for a in inputs), pltpu.SemaphoreType.DMA((4,))],
        *(pltpu.with_memory_space_constraint(a, pltpu.HBM) for a in inputs),
        space=pltpu.HBM,
    )
    y_packets = exchange(first, second, "gy")
    (spread,) = call(spread_kernel, [(across * count, 1, X)], [], main, coarse)
    spread = lax.all_to_all(spread, ("gx", "gy"), 0, 0, tiled=True)

    strip = (entry_tiles(rows) + 1, Z, X)
    first, second = call(
        functools.partial(pack_x_kernel, rows),
        [strip, strip],
        [(PER * entry_tiles(rows), Z, X)],
        main,
        coarse,
        *y_packets,
    )
    x_packets = exchange(first, second, "gx")

    strip = (FAR + 2, Z, X)
    pair0 = (2, 2, total0, Z, X)
    own, first, second, keep0, gain = call(
        functools.partial(level0_kernel, rows),
        [(2, OWN, Z, X), strip, strip, (8, 2, total0, Z, X), (9, Z, X)],
        [(6, 2, total0, Z, X), pair0, pair0, pair0],
        main,
        *y_packets,
        *x_packets,
        spread,
    )
    (coef1,) = call(
        functools.partial(coarse1_kernel, rows),
        [(3, 2, SIZE1, Z, X)],
        [(2, 2 * GROUPS1, Z, X)],
        coarse,
        *y_packets,
        *x_packets,
        gain,
    )
    b_packets = exchange(first, second, "gy")

    one, two, up = (2, SIZE1, Z, X), (2, SIZE2, Z, X), (2, SIZE_UP, Z, X)
    packet, keep1 = call(
        level1_kernel, [(across * count, Z, X), (2, *one)], [one, one], own, *b_packets, coef1, gain
    )
    gathered = lax.all_to_all(packet, ("gx", "gy"), 0, 0, tiled=True)
    (coef2,) = call(
        functools.partial(coarse2_kernel, rows),
        [(2, 2, SIZE2, Z, X)],
        [],
        coarse,
        *y_packets,
        *x_packets,
        *b_packets,
    )

    (out,) = call(
        functools.partial(rest_kernel, across, count),
        [(2 * Z * rows, X)],
        [one, two, two, two, two, up, up, pair0, pair0, pair0],
        gathered,
        gain,
        coef1,
        coef2,
        keep0,
        keep1,
        *b_packets,
    )
    return out.reshape(2, Z, rows, X)


def solution(mesh):
    placed = (
        P(None, None, "gy", "gx"),
        P(None, None, "gy", "gx"),
        P(None, "gy", "gx"),
        P(None, "gy", "gx"),
    )
    return jax.shard_map(
        body, mesh=mesh, in_specs=placed, out_specs=P(None, None, "gy", "gx"), check_vma=False
    )
```

```python
import functools

import jax
import jax.numpy as jnp
from jax import lax
from jax.experimental import pallas as pl
from jax.experimental.pallas import tpu as pltpu
from jax.sharding import PartitionSpec as P

DIFF = (40.0, 20.0)
INV_STEP = 2.0
LOWER = 0.25

_CENTRE = (1.0 + LOWER) / 2.0
_HALF = (1.0 - LOWER) / 2.0
_SIGMA = _CENTRE / _HALF
_RHO0 = 1.0 / _SIGMA
_RHO1 = 1.0 / (2.0 * _SIGMA - _RHO0)
_RHO2 = 1.0 / (2.0 * _SIGMA - _RHO1)

Z = 8
X = 128
HALO0 = 4
HALOS = (4, 4, 3, 3, 3, 3)
STARTS = tuple(sum(HALOS[:i]) for i in range(6))
FIELDS1 = sum(HALOS)
FIELDS2 = FIELDS1 + 8
WIDE = 18
PER = X // WIDE
WIDE2 = 32
EDGE = 3
CHUNK = 4

LO1, HI1 = -4, 8
LO2, HI2 = -2, 3
LO_UP, HI_UP = -3, 7
SIZE1, SIZE2, SIZE_UP = HI1 - LO1 + 2, HI2 - LO2 + 2, HI_UP - LO_UP + 2
OWN = 4


def lane_of():
    return lax.broadcasted_iota(jnp.int32, (1, Z, X), 2)


def sub_of():
    return lax.broadcasted_iota(jnp.int32, (1, Z, X), 1)


def roll_x(tile, shift):
    shift = shift % X
    return pltpu.roll(tile, shift, 2) if shift else tile


def roll_z(tile, shift):
    shift = shift % Z
    return pltpu.roll(tile, shift, 1) if shift else tile


def rows_loop(lo, hi, body, step=CHUNK):
    full = (hi - lo) // step
    if full == 1:
        body(lo, step)
    elif full > 1:

        def trip(i, carry):
            body(lo + i * step, step)
            return carry

        lax.fori_loop(0, full, trip, 0)
    rest = hi - lo - full * step
    if rest:
        body(hi - rest, rest)


def neighbour_sums(read, r, n, k):
    lane = lane_of()
    low, high = lane < k, lane >= X - k
    centre = [read(t, r, n) for t in (0, 1)]
    right = [roll_x(c, k) for c in centre]
    left = [roll_x(c, -k) for c in centre]
    sums = []
    for t in (0, 1):
        c = centre[t]
        along_x = jnp.where(low, right[1 - t], right[t]) + jnp.where(high, left[1 - t], left[t])
        along_y = read(t, r - 1, n) + read(t, r + 1, n)
        along_z = 2.0 * roll_z(c, k) if 2 * k == Z else roll_z(c, k) + roll_z(c, -k)
        sums.append(along_x + along_y + along_z)
    return centre, sums


def jacobian(u, v, f, k, level):
    scale = 0.25**level
    product = u * v
    squared = v * v
    first = INV_STEP + squared + f + 6.0 * DIFF[0] * scale
    second = INV_STEP + f + k - 2.0 * product + 6.0 * DIFF[1] * scale
    return 2.0 * product, squared, 1.0 / first, 1.0 / second, first, second


def cheb_step(level, keep, source, target, d, r, n, carry, gain):
    scale = 0.25**level
    k = 1 << level
    u, nb_u = neighbour_sums(lambda t, a, m: source[0, t, pl.ds(a, m)], r, n, k)
    v, nb_v = neighbour_sums(lambda t, a, m: source[1, t, pl.ds(a, m)], r, n, k)
    rows = pl.ds(r, n)
    for t in (0, 1):
        cross, squared, inv_u, inv_v = (keep[i, t, rows] for i in range(4))
        res_u = inv_u * (keep[4, t, rows] - cross * v[t] + DIFF[0] * scale * nb_u[t]) - u[t]
        res_v = inv_v * (keep[5, t, rows] + squared * u[t] + DIFF[1] * scale * nb_v[t]) - v[t]
        du, dv = gain * res_u, gain * res_v
        if carry is not None:
            du = du + carry * d[0, t, rows]
            dv = dv + carry * d[1, t, rows]
        d[0, t, rows] = du
        d[1, t, rows] = dv
        target[0, t, rows] = u[t] + du
        target[1, t, rows] = v[t] + dv


def residual(level, keep, diag, source, r, n):
    scale = 0.25**level
    k = 1 << level
    u, nb_u = neighbour_sums(lambda t, a, m: source[0, t, pl.ds(a, m)], r, n, k)
    v, nb_v = neighbour_sums(lambda t, a, m: source[1, t, pl.ds(a, m)], r, n, k)
    rows = pl.ds(r, n)
    first, second = [], []
    for t in (0, 1):
        first.append(
            keep[4, t, rows] - diag[0, t, rows] * u[t] - keep[0, t, rows] * v[t] + DIFF[0] * scale * nb_u[t]
        )
        second.append(
            keep[5, t, rows] - diag[1, t, rows] * v[t] + keep[1, t, rows] * u[t] + DIFF[1] * scale * nb_v[t]
        )
    return first, second


CARRY1 = _RHO1 * _RHO0
CARRY2 = _RHO2 * _RHO1


def write_gains(spread, out):
    lane = lax.broadcasted_iota(jnp.int32, (1, X), 1)
    for level in range(3):
        top = jnp.max(jnp.where(lane == level, spread, 0.0), axis=1, keepdims=True)
        tau = 1.0 / (1.0 + jnp.broadcast_to(top, (Z, X)))
        for i, factor in enumerate((1.0 / _CENTRE, 2.0 * _RHO1 / _HALF, 2.0 * _RHO2 / _HALF)):
            out[3 * level + i] = factor * tau


def pair_rows(value):
    n = value.shape[0] // 2
    pairs = value.reshape(n, 2, Z, X)
    return pairs[:, 0] + pairs[:, 1]


def restrict_01(first, second):
    lane, sub = lane_of(), sub_of()
    across = []
    for value in (first, second):
        a, b = value[0:1], value[1:2]
        across.append(jnp.where((lane & 1) == 0, a + roll_x(a, -1), b + roll_x(b, 1)))
    a, b = across
    return 0.125 * jnp.where((sub & 1) == 0, a + roll_z(a, -1), b + roll_z(b, 1))


def restrict_12(groups):
    lane, sub = lane_of(), sub_of()
    out = None
    for p, value in enumerate(groups):
        value = value + roll_x(value, 1 if p & 1 else -1)
        value = value + roll_x(value, 2 if p & 2 else -2)
        out = value if out is None else jnp.where((lane & 3) == p, value, out)
    return 0.125 * (out + jnp.where((sub & 2) == 0, roll_z(out, -2), roll_z(out, 2)))


def spread_x(tile, k, phase):
    return jnp.where((lane_of() & k) == phase, tile, roll_x(tile, -k if phase else k))


def packed_jacobian(uv, fk, level):
    scale = 0.25**level
    even = (sub_of() & 1) == 0
    u, v = jnp.where(even, uv, roll_z(uv, 1)), jnp.where(even, roll_z(uv, -1), uv)
    f, k = jnp.where(even, fk, roll_z(fk, 1)), jnp.where(even, roll_z(fk, -1), fk)
    product, squared = u * v, v * v
    diag = jnp.where(
        even,
        INV_STEP + squared + f + 6.0 * DIFF[0] * scale,
        INV_STEP + f + k - 2.0 * product + 6.0 * DIFF[1] * scale,
    )
    return 1.0 / diag, jnp.where(even, -2.0 * product, squared), diag


def packed_spread(uv, fk, level):
    scale = 0.25**level
    even = (sub_of() & 1) == 0
    inverse, other, _ = packed_jacobian(uv, fk, level)
    return jnp.where(even, 6.0 * DIFF[0] * scale - other, 6.0 * DIFF[1] * scale + other) * inverse


def packed_terms(source, g, n, level):
    k = 1 << level
    lane, sub = lane_of(), sub_of()
    even = (sub & 1) == 0
    first, last = (lane & (k - 1)) == 0, (lane & (k - 1)) == k - 1
    low, high = lane < k, lane >= X - k
    diff = jnp.where(even, DIFF[0] * 0.25**level, DIFF[1] * 0.25**level)
    wide = [source[t, pl.ds(g - 1, n + 2)] for t in (0, 1)]
    centre = [w[1 : n + 1] for w in wide]
    right = [roll_x(c, k) for c in centre]
    left = [roll_x(c, -k) for c in centre]
    out = []
    for t in (0, 1):
        c, w = centre[t], wide[t]
        total = jnp.where(low, right[1 - t], right[t]) + jnp.where(high, left[1 - t], left[t])
        if k == 2:
            ahead, back = roll_x(w, 1), roll_x(w, -1)
            total = total + jnp.where(first, back[0:n], ahead[1 : n + 1])
            total = total + jnp.where(last, ahead[2 : n + 2], back[1 : n + 1])
            total = total + roll_z(c, 2) + roll_z(c, -2)
        else:
            total = total + jnp.where(first, roll_x(w[0:n], -(k - 1)), roll_x(c, 1))
            total = total + jnp.where(last, roll_x(w[2 : n + 2], k - 1), roll_x(c, -1))
            total = total + 2.0 * roll_z(c, 4)
        other = jnp.where(even, roll_z(c, -1), roll_z(c, 1))
        out.append((c, other, diff * total))
    return out


def packed_first(coef, shift, b, target, d, g, n, gain):
    for t in (0, 1):
        value = gain * coef[0, t, pl.ds(g + shift, n)] * b[t, pl.ds(g + shift, n)]
        d[t, pl.ds(g, n)] = value
        target[t, pl.ds(g, n)] = value


def packed_step(level, coef, shift, b, source, target, d, g, n, carry, gain):
    for t, (c, other, spread) in enumerate(packed_terms(source, g, n, level)):
        at = pl.ds(g + shift, n)
        res = coef[0, t, at] * (b[t, at] + coef[1, t, at] * other + spread) - c
        delta = gain * res
        if carry is not None:
            delta = delta + carry * d[t, pl.ds(g, n)]
        d[t, pl.ds(g, n)] = delta
        target[t, pl.ds(g, n)] = c + delta


def plane(ref, f, y, rows):
    return ref[pl.ds(f * Z * rows + y, Z, stride=rows), :]


def is_even(axis):
    return lax.rem(lax.axis_index(axis), 2) == 0


def prev_of(even, first, second, at):
    return jnp.where(even, first[at], second[at])


def next_of(even, first, second, at):
    return jnp.where(even, second[at], first[at])


def first_kernel(rows, state, previous, feed, kill, first, second, main, coarse, *scratch):
    sources, sems = scratch[:4], scratch[4]
    copies = [
        pltpu.make_async_copy(ref, held, sems.at[i])
        for i, (ref, held) in enumerate(zip((state, previous, feed, kill), sources))
    ]
    for copy in copies:
        copy.start()
    for copy in copies:
        copy.wait()
    even = is_even("gy")
    state, previous, feed, kill = sources
    fields = [(state, 0), (state, 1), (previous, 0), (previous, 1), (feed, 0), (kill, 0)]
    for i, (ref, f) in enumerate(fields):
        for y in range(rows):
            main[i, y] = plane(ref, f, y, rows)
        top, bottom = main[i, 0 : HALOS[i]], main[i, rows - HALOS[i] : rows]
        at = slice(STARTS[i], STARTS[i] + HALOS[i])
        first[at] = jnp.where(even, top, bottom)
        second[at] = jnp.where(even, bottom, top)
    u, v, f, k = (main[i] for i in (0, 1, 4, 5))
    sums = [pair_rows(value) for value in (u, v, f, k)]
    pairs = []
    for p in (0, 1):
        values = [
            restrict_01(sums[2 * p][2 * g : 2 * g + 2], sums[2 * p + 1][2 * g : 2 * g + 2]) for g in range(OWN)
        ]
        pairs.append(jnp.concatenate(values, axis=0))
        coarse[p * OWN : (p + 1) * OWN] = pairs[p]
        for ref in (first, second):
            ref[FIELDS1 + p * OWN : FIELDS1 + (p + 1) * OWN] = pairs[p]

    uv, fk = (restrict_12([pair[j : j + 1] for j in range(OWN)]) for pair in pairs)
    both = jnp.where((sub_of() & 2) == 0, uv, fk)
    coarse[2 * OWN : 2 * OWN + 1] = both
    for ref in (first, second):
        ref[FIELDS2 : FIELDS2 + 1] = both


def split_fields2(both):
    low = (sub_of() & 2) == 0
    return jnp.where(low, both, roll_z(both, 2)), jnp.where(low, roll_z(both, -2), both)


def spread_kernel(main, coarse, out):
    lane = lax.broadcasted_iota(jnp.int32, (1, X), 1)
    u, v, f, k = (main[i] for i in (0, 1, 4, 5))
    cross, squared, inv_u, inv_v, _, _ = jacobian(u, v, f, k, 0)
    tops = [jnp.max(jnp.maximum((6.0 * DIFF[0] + cross) * inv_u, (6.0 * DIFF[1] + squared) * inv_v), axis=0)]
    tops.append(jnp.max(packed_spread(coarse[0:OWN], coarse[OWN : 2 * OWN], 1), axis=0))
    tops.append(packed_spread(*split_fields2(coarse[2 * OWN : 2 * OWN + 1]), 2)[0])
    result = jnp.zeros((1, X), jnp.float32)
    for level, top in enumerate(tops):
        top = jnp.max(jnp.max(top, axis=0, keepdims=True), axis=1, keepdims=True)
        result = jnp.where(lane == level, jnp.broadcast_to(top, (1, X)), result)
    out[...] = jnp.broadcast_to(result[None], out.shape)


def around(across, count, gathered):
    lane = lane_of()
    gx, gy = lax.axis_index("gx"), lax.axis_index("gy")
    columns = [lax.rem(gx + i + across, across) * count for i in (-1, 0, 1)]
    out = [[], []]
    for q in range(LO2, HI2):
        row = lax.rem(gy + q + 4 * count, count)
        left, centre, right = (gathered[pl.ds(column + row, 1)] for column in columns)
        out[0].append(centre)
        out[1].append(jnp.where(lane < X // 2, right, left))
    return [jnp.concatenate(groups, axis=0) for groups in out]


GROUPS1 = HI1 - LO1
GROUPS2 = HI2 - LO2


def entry(rows, i):
    starts = [0]
    for halo in HALOS:
        starts.append(starts[-1] + rows + 2 * halo)
    return (starts + [starts[-1] + 2 * GROUPS1])[i]


def entry_tiles(rows):
    return -(-entry(rows, 7) // PER)


def pack_slots(parts, width):
    lane = lane_of()
    left, right = None, None
    for j, part in enumerate(parts):
        a, b = roll_x(part, width * j), roll_x(part, width + width * j)
        left = a if left is None else jnp.where(lane >= width * j, a, left)
        right = b if right is None else jnp.where(lane >= width * j, b, right)
    return left, right


def unpack_slot(from_left, from_right, j, width):
    return jnp.where(lane_of() < X // 2, roll_x(from_right, -width * j), roll_x(from_left, X - width - width * j))


def unpack_entries(even_x, x_first, x_second, share, lo, hi):
    out = []
    for j in range(PER):
        a, b = max(lo, j * share), min(hi, (j + 1) * share)
        if a < b:
            strip = slice(a - j * share, b - j * share)
            left, right = prev_of(even_x, x_first, x_second, strip), next_of(even_x, x_first, x_second, strip)
            out.append((a - lo, b - lo, unpack_slot(left, right, j, WIDE)))
    return out


def unpack_fields2(even_x, x_first, x_second, share, j):
    strip = slice(share, share + 1)
    left, right = prev_of(even_x, x_first, x_second, strip), next_of(even_x, x_first, x_second, strip)
    return unpack_slot(left, right, j, WIDE2)


def pack_x_kernel(rows, main, coarse, y_first, y_second, first, second, held):
    even = is_even("gy")
    share = entry_tiles(rows)
    for i, halo in enumerate(HALOS):
        strip = slice(STARTS[i], STARTS[i] + halo)
        to = entry(rows, i)
        held[to : to + halo] = prev_of(even, y_first, y_second, strip)
        held[to + halo : to + halo + rows] = main[i]
        held[to + halo + rows : to + 2 * halo + rows] = next_of(even, y_first, y_second, strip)
    for p in (0, 1):
        to = entry(rows, 6) + p * GROUPS1
        strip = slice(FIELDS1 + p * OWN, FIELDS1 + (p + 1) * OWN)
        held[to : to + OWN] = prev_of(even, y_first, y_second, strip)
        held[to + OWN : to + 2 * OWN] = coarse[p * OWN : (p + 1) * OWN]
        held[to + 2 * OWN : to + 3 * OWN] = next_of(even, y_first, y_second, strip)
    left, right = pack_slots([held[j * share : (j + 1) * share] for j in range(PER)], WIDE)
    strip = slice(FIELDS2, FIELDS2 + 1)
    own = coarse[2 * OWN : 2 * OWN + 1]
    parts = [prev_of(even, y_first, y_second, strip), own, next_of(even, y_first, y_second, strip)]
    left2, right2 = pack_slots(parts, WIDE2)
    even = is_even("gx")
    first[0:share] = jnp.where(even, left, right)
    second[0:share] = jnp.where(even, right, left)
    first[share : share + 1] = jnp.where(even, left2, right2)
    second[share : share + 1] = jnp.where(even, right2, left2)


HALO1 = X // (2 * OWN)
EDGES = OWN + 1
FAR = EDGES + 2 * EDGE + 1


def level0_kernel(
    rows, main, y_first, y_second, x_first, x_second, gathered, own, first, second, keep, gain_out, fields, other, d, diag
):
    even, even_x = is_even("gy"), is_even("gx")
    total = rows + 2 * HALO0
    share = entry_tiles(rows)
    top = jnp.max(gathered[...], axis=0)
    write_gains(top[0:1], gain_out)
    g0, g1, g2 = (gain_out[i] for i in range(3))
    for i, halo in enumerate(HALOS):
        strip = slice(STARTS[i], STARTS[i] + halo)
        skip = HALO0 - halo
        fields[i, 0, skip:HALO0] = prev_of(even, y_first, y_second, strip)
        fields[i, 0, HALO0 : HALO0 + rows] = main[i]
        fields[i, 0, HALO0 + rows : total - skip] = next_of(even, y_first, y_second, strip)
        for a, b, value in unpack_entries(even_x, x_first, x_second, share, entry(rows, i), entry(rows, i + 1)):
            fields[i, 1, a + skip : b + skip] = value
    here = keep.at[6:8]

    def setup(r, n):
        at = pl.ds(r, n)
        u, nb_u = neighbour_sums(lambda t, a, m: fields[0, t, pl.ds(a, m)], r, n, 1)
        v, nb_v = neighbour_sums(lambda t, a, m: fields[1, t, pl.ds(a, m)], r, n, 1)
        for t in (0, 1):
            f, k = fields[4, t, at], fields[5, t, at]
            cross, squared, inv_u, inv_v, first, second = jacobian(u[t], v[t], f, k, 0)
            react = u[t] * squared
            b_u = (
                DIFF[0] * (nb_u[t] - 6.0 * u[t])
                - INV_STEP * (u[t] - fields[2, t, at])
                - react
                + f * (1.0 - u[t])
            )
            b_v = (
                DIFF[1] * (nb_v[t] - 6.0 * v[t]) - INV_STEP * (v[t] - fields[3, t, at]) + react - (f + k) * v[t]
            )
            for i, value in enumerate((cross, squared, inv_u, inv_v, b_u, b_v)):
                keep[i, t, at] = value
            diag[0, t, at] = first
            diag[1, t, at] = second
            for i, value in enumerate((g0 * inv_u * b_u, g0 * inv_v * b_v)):
                d[i, t, at] = value
                keep[6 + i, t, at] = value

    rows_loop(1, total - 1, setup)
    rows_loop(2, total - 2, lambda r, n: cheb_step(0, keep, here, other, d, r, n, CARRY1, g1))
    rows_loop(3, total - 3, lambda r, n: cheb_step(0, keep, other, here, d, r, n, CARRY2, g2))

    def down(r, n):
        res = residual(0, keep, diag, here, r, n)
        out = (r - HALO0) // 4
        for t in (0, 1):
            value = restrict_01(pair_rows(res[0][t]), pair_rows(res[1][t]))
            own[t, pl.ds(out, 1)] = value
            if t == 0:
                first[pl.ds(out, 1)] = value
                second[pl.ds(out, 1)] = value

    rows_loop(HALO0, HALO0 + rows, down, 4)

    lane = lane_of()
    sides = None
    for j in range(OWN):
        value = roll_x(own[1, j : j + 1], HALO1 + 2 * HALO1 * j)
        sides = value if sides is None else jnp.where(lane // (2 * HALO1) == j, value, sides)
    edges = []
    for start in (HALO0, HALO0 + rows - EDGE):
        halo = None
        for i in (0, 1):
            for j in range(EDGE):
                at = i * EDGE + j
                value = roll_x(keep[6 + i, 1, start + j : start + j + 1], 4 + 8 * at)
                halo = value if halo is None else jnp.where((lane >> 3) == at, value, halo)
        edges.append([keep[6, 0, start : start + EDGE], keep[7, 0, start : start + EDGE], halo])
    top, bottom = (jnp.concatenate(parts, axis=0) for parts in edges)
    for ref in (first, second):
        ref[OWN : OWN + 1] = sides
    strip = slice(FIELDS2, FIELDS2 + 1)
    for t in (0, 1):
        if t == 0:
            before, after = prev_of(even, y_first, y_second, strip), next_of(even, y_first, y_second, strip)
        else:
            before, after = (unpack_fields2(even_x, x_first, x_second, share, j) for j in (0, 2))
        first[FAR + t : FAR + t + 1] = jnp.where(even, after, before)
        second[FAR + t : FAR + t + 1] = jnp.where(even, before, after)
    first[EDGES : EDGES + 2 * EDGE + 1] = jnp.where(even, top, bottom)
    second[EDGES : EDGES + 2 * EDGE + 1] = jnp.where(even, bottom, top)


def coarse1_kernel(rows, coarse, y_first, y_second, x_first, x_second, gain, coef, fields):
    del gain
    even, even_x = is_even("gy"), is_even("gx")
    share = entry_tiles(rows)
    for p in (0, 1):
        to = p * GROUPS1
        strip = slice(FIELDS1 + p * OWN, FIELDS1 + (p + 1) * OWN)
        fields[0, to : to + OWN] = prev_of(even, y_first, y_second, strip)
        fields[0, to + OWN : to + 2 * OWN] = coarse[p * OWN : (p + 1) * OWN]
        fields[0, to + 2 * OWN : to + 3 * OWN] = next_of(even, y_first, y_second, strip)
    for a, b, value in unpack_entries(even_x, x_first, x_second, share, entry(rows, 6), entry(rows, 7)):
        fields[1, a:b] = value
    for t in (0, 1):
        for i, value in enumerate(packed_jacobian(fields[t, 0:GROUPS1], fields[t, GROUPS1 : 2 * GROUPS1], 1)):
            coef[i, t, 1 : SIZE1 - 1] = value


def coarse2_kernel(rows, coarse, y_first, y_second, x_first, x_second, b_first, b_second, coef):
    even, even_x = is_even("gy"), is_even("gx")
    share = entry_tiles(rows)
    near = slice(FIELDS2, FIELDS2 + 1)
    for t in (0, 1):
        far = slice(FAR + t, FAR + t + 1)
        if t == 0:
            middle = [
                prev_of(even, y_first, y_second, near),
                coarse[2 * OWN : 2 * OWN + 1],
                next_of(even, y_first, y_second, near),
            ]
        else:
            middle = [unpack_fields2(even_x, x_first, x_second, share, j) for j in range(3)]
        parts = [prev_of(even, b_first, b_second, far), *middle, next_of(even, b_first, b_second, far)]
        inverse, other, _ = packed_jacobian(*split_fields2(jnp.concatenate(parts, axis=0)), 2)
        coef[0, t, 1 : SIZE2 - 1] = inverse
        coef[1, t, 1 : SIZE2 - 1] = other


def level1_kernel(own, first, second, coef1, gain, packet, keep, y1, d1):
    b1, x1 = keep.at[0], keep.at[1]
    even = is_even("gy")
    for t in (0, 1):
        b1[t, 1 + OWN : 1 + 2 * OWN] = own[t]
        for take, at in ((prev_of, 1), (next_of, 1 + 2 * OWN)):
            if t == 0:
                b1[t, at : at + OWN] = take(even, first, second, slice(0, OWN))
            else:
                sides = take(even, first, second, slice(OWN, OWN + 1))
                for j in range(OWN):
                    b1[t, at + j : at + j + 1] = roll_x(sides, -(HALO1 + 2 * HALO1 * j))
    g0, g1, g2 = (gain[3 + i] for i in range(3))
    n = GROUPS1
    packed_first(coef1, 0, b1, x1, d1, 1, n, g0)
    packed_step(1, coef1, 0, b1, x1, y1, d1, 1, n, CARRY1, g1)
    packed_step(1, coef1, 0, b1, y1, x1, d1, 1, n, CARRY2, g2)
    here = pl.ds(1 + OWN, OWN)
    c, other, spread = packed_terms(x1, 1 + OWN, OWN, 1)[0]
    res = b1[0, here] - coef1[2, 0, here] * c + coef1[1, 0, here] * other + spread
    value = restrict_12([res[j : j + 1] for j in range(OWN)])
    for c in range(packet.shape[0]):
        packet[c : c + 1] = value


def rest_kernel(
    across, count, gathered, gain, coef1, coef2, keep0, keep1, first, second, out, d1, b2, x2, y2, d2, xu, yu, x0, y0, d0
):
    rows = out.shape[0] // (2 * Z)
    even = (sub_of() & 1) == 0
    b1, x1 = keep1.at[0], keep1.at[1]

    for t, groups in enumerate(around(across, count, gathered)):
        b2[t, 1 : SIZE2 - 1] = groups

    n = HI2 - LO2
    g0, g1, g2 = (gain[6 + i] for i in range(3))
    packed_first(coef2, 0, b2, x2, d2, 1, n, g0)
    packed_step(2, coef2, 0, b2, x2, y2, d2, 1, n, CARRY1, g1)
    packed_step(2, coef2, 0, b2, y2, x2, d2, 1, n, CARRY2, g2)
    packed_step(2, coef2, 0, b2, x2, y2, d2, 1, n, None, g0)
    packed_step(2, coef2, 0, b2, y2, x2, d2, 1, n, CARRY1, g1)
    packed_step(2, coef2, 0, b2, x2, y2, d2, 1, n, CARRY2, g2)

    g0, g1, g2 = (gain[3 + i] for i in range(3))
    shift = LO_UP - LO1
    for t in (0, 1):
        for g in range(LO_UP, HI_UP):
            p = g % 4
            value = y2[t, g // 4 - LO2 + 1 : g // 4 - LO2 + 2]
            value = spread_x(spread_x(value, 1, p & 1), 2, p & 2)
            at = g - LO_UP + 1
            xu[t, at : at + 1] = x1[t, at + shift : at + shift + 1] + value
    n = HI_UP - LO_UP
    packed_step(1, coef1, shift, b1, xu, yu, d1, 1, n, None, g0)
    packed_step(1, coef1, shift, b1, yu, xu, d1, 1, n, CARRY1, g1)
    packed_step(1, coef1, shift, b1, xu, yu, d1, 1, n, CARRY2, g2)

    g0, g1, g2 = (gain[i] for i in range(3))
    last = EDGES + 2 * EDGE
    even_y = is_even("gy")
    for i in (0, 1):
        for at, take in ((HALO0 - EDGE, prev_of), (HALO0 + rows, next_of)):
            strip = slice(EDGES + i * EDGE, EDGES + (i + 1) * EDGE)
            x0[i, 0, at : at + EDGE] = take(even_y, first, second, strip)
            sides = take(even_y, first, second, slice(last, last + 1))
            for j in range(EDGE):
                x0[i, 1, at + j : at + j + 1] = roll_x(sides, -(4 + 8 * (i * EDGE + j)))
        for t in (0, 1):
            x0[i, t, HALO0 : HALO0 + rows] = keep0[6 + i, t, HALO0 : HALO0 + rows]
    for t in (0, 1):
        for row in range(-2, rows // 2 + 2):
            at = row // 2 - LO_UP + 1
            value = spread_x(yu[t, at : at + 1], 1, row & 1)
            for i, fine in enumerate((jnp.where(even, value, roll_z(value, 1)), jnp.where(even, roll_z(value, -1), value))):
                for y in (2 * row, 2 * row + 1):
                    if -EDGE <= y < rows + EDGE:
                        x0[i, t, y + HALO0 : y + HALO0 + 1] = x0[i, t, y + HALO0 : y + HALO0 + 1] + fine
    total = rows + 2 * HALO0
    rows_loop(2, total - 2, lambda r, n: cheb_step(0, keep0, x0, y0, d0, r, n, None, g0))
    rows_loop(3, total - 3, lambda r, n: cheb_step(0, keep0, y0, x0, d0, r, n, CARRY1, g1))
    rows_loop(4, total - 4, lambda r, n: cheb_step(0, keep0, x0, y0, d0, r, n, CARRY2, g2))
    for i in (0, 1):
        for y in range(rows):
            out[pl.ds(i * Z * rows + y, Z, stride=rows), :] = y0[i, 0, HALO0 + y]


def call(kernel, out_shapes, scratch, *args, space=pltpu.VMEM):
    out = [jax.ShapeDtypeStruct(shape, jnp.float32) for shape in out_shapes]
    return pl.pallas_call(
        kernel,
        out_shape=out,
        in_specs=[pl.BlockSpec(memory_space=space)] * len(args),
        out_specs=[pl.BlockSpec(memory_space=pltpu.VMEM)] * len(out),
        scratch_shapes=[pltpu.VMEM(s, jnp.float32) if isinstance(s, tuple) else s for s in scratch],
        compiler_params=pltpu.CompilerParams(vmem_limit_bytes=24 * 2**20),
    )(*args)


def swap(value, axis, step):
    count = lax.axis_size(axis)
    assert count % 2 == 0
    pairs = [(i, (i + step) % count) for i in range(0, count, 2)]
    return lax.ppermute(value, axis, pairs + [(j, i) for i, j in pairs])


def exchange(first, second, axis):
    return swap(first, axis, -1), swap(second, axis, 1)


def body(state, previous, feed, kill):
    _, depth, rows, cols = state.shape
    assert depth == Z and cols == X and rows == 4 * OWN
    across, count = lax.axis_size("gx"), lax.axis_size("gy")
    total0 = rows + 2 * HALO0
    state = state.reshape(2 * Z * rows, X)
    previous = previous.reshape(2 * Z * rows, X)
    feed = feed.reshape(Z * rows, X)
    kill = kill.reshape(Z * rows, X)
    inputs = (state, previous, feed, kill)

    strip = (FIELDS2 + 1, Z, X)
    first, second, main, coarse = call(
        functools.partial(first_kernel, rows),
        [strip, strip, (6, rows, Z, X), (2 * OWN + 1, Z, X)],
        [*(a.shape for a in inputs), pltpu.SemaphoreType.DMA((4,))],
        *(pltpu.with_memory_space_constraint(a, pltpu.HBM) for a in inputs),
        space=pltpu.HBM,
    )
    y_packets = exchange(first, second, "gy")
    (spread,) = call(spread_kernel, [(across * count, Z, X)], [], main, coarse)
    spread = lax.all_to_all(spread, ("gx", "gy"), 0, 0, tiled=True)

    strip = (entry_tiles(rows) + 1, Z, X)
    first, second = call(
        functools.partial(pack_x_kernel, rows),
        [strip, strip],
        [(PER * entry_tiles(rows), Z, X)],
        main,
        coarse,
        *y_packets,
    )
    x_packets = exchange(first, second, "gx")

    strip = (FAR + 2, Z, X)
    pair0 = (2, 2, total0, Z, X)
    own, first, second, keep0, gain = call(
        functools.partial(level0_kernel, rows),
        [(2, OWN, Z, X), strip, strip, (8, 2, total0, Z, X), (9, Z, X)],
        [(6, 2, total0, Z, X), pair0, pair0, pair0],
        main,
        *y_packets,
        *x_packets,
        spread,
    )
    (coef1,) = call(
        functools.partial(coarse1_kernel, rows),
        [(3, 2, SIZE1, Z, X)],
        [(2, 2 * GROUPS1, Z, X)],
        coarse,
        *y_packets,
        *x_packets,
        gain,
    )
    b_packets = exchange(first, second, "gy")

    one, two, up = (2, SIZE1, Z, X), (2, SIZE2, Z, X), (2, SIZE_UP, Z, X)
    packet, keep1 = call(
        level1_kernel, [(across * count, Z, X), (2, *one)], [one, one], own, *b_packets, coef1, gain
    )
    gathered = lax.all_to_all(packet, ("gx", "gy"), 0, 0, tiled=True)
    (coef2,) = call(
        functools.partial(coarse2_kernel, rows),
        [(2, 2, SIZE2, Z, X)],
        [],
        coarse,
        *y_packets,
        *x_packets,
        *b_packets,
    )

    (out,) = call(
        functools.partial(rest_kernel, across, count),
        [(2 * Z * rows, X)],
        [one, two, two, two, two, up, up, pair0, pair0, pair0],
        gathered,
        gain,
        coef1,
        coef2,
        keep0,
        keep1,
        *b_packets,
    )
    return out.reshape(2, Z, rows, X)


def solution(mesh):
    placed = (
        P(None, None, "gy", "gx"),
        P(None, None, "gy", "gx"),
        P(None, "gy", "gx"),
        P(None, "gy", "gx"),
    )
    return jax.shard_map(
        body, mesh=mesh, in_specs=placed, out_specs=P(None, None, "gy", "gx"), check_vma=False
    )
```

```python
import functools

import jax
import jax.numpy as jnp
from jax import lax
from jax.experimental import pallas as pl
from jax.experimental.pallas import tpu as pltpu
from jax.sharding import PartitionSpec as P

DIFF = (40.0, 20.0)
INV_STEP = 2.0
LOWER = 0.25

_CENTRE = (1.0 + LOWER) / 2.0
_HALF = (1.0 - LOWER) / 2.0
_SIGMA = _CENTRE / _HALF
_RHO0 = 1.0 / _SIGMA
_RHO1 = 1.0 / (2.0 * _SIGMA - _RHO0)
_RHO2 = 1.0 / (2.0 * _SIGMA - _RHO1)

Z = 8
X = 128
HALO0 = 4
HALOS = (4, 4, 3, 3, 3, 3)
STARTS = tuple(sum(HALOS[:i]) for i in range(6))
FIELDS1 = sum(HALOS)
FIELDS2 = FIELDS1 + 8
WIDE = 18
PER = X // WIDE
WIDE2 = 32
EDGE = 3
CHUNK = 4

LO1, HI1 = -4, 8
LO2, HI2 = -2, 3
LO_UP, HI_UP = -3, 7
SIZE1, SIZE2, SIZE_UP = HI1 - LO1 + 2, HI2 - LO2 + 2, HI_UP - LO_UP + 2
OWN = 4


def lane_of():
    return lax.broadcasted_iota(jnp.int32, (1, Z, X), 2)


def sub_of():
    return lax.broadcasted_iota(jnp.int32, (1, Z, X), 1)


def roll_x(tile, shift):
    shift = shift % X
    return pltpu.roll(tile, shift, 2) if shift else tile


def roll_z(tile, shift):
    shift = shift % Z
    return pltpu.roll(tile, shift, 1) if shift else tile


def rows_loop(lo, hi, body, step=CHUNK):
    full = (hi - lo) // step
    if full == 1:
        body(lo, step)
    elif full > 1:

        def trip(i, carry):
            body(lo + i * step, step)
            return carry

        lax.fori_loop(0, full, trip, 0)
    rest = hi - lo - full * step
    if rest:
        body(hi - rest, rest)


def neighbour_sums(read, r, n, k):
    lane = lane_of()
    low, high = lane < k, lane >= X - k
    centre = [read(t, r, n) for t in (0, 1)]
    right = [roll_x(c, k) for c in centre]
    left = [roll_x(c, -k) for c in centre]
    sums = []
    for t in (0, 1):
        c = centre[t]
        along_x = jnp.where(low, right[1 - t], right[t]) + jnp.where(high, left[1 - t], left[t])
        along_y = read(t, r - 1, n) + read(t, r + 1, n)
        along_z = 2.0 * roll_z(c, k) if 2 * k == Z else roll_z(c, k) + roll_z(c, -k)
        sums.append(along_x + along_y + along_z)
    return centre, sums


def jacobian(u, v, f, k, level):
    scale = 0.25**level
    product = u * v
    squared = v * v
    first = INV_STEP + squared + f + 6.0 * DIFF[0] * scale
    second = INV_STEP + f + k - 2.0 * product + 6.0 * DIFF[1] * scale
    return 2.0 * product, squared, 1.0 / first, 1.0 / second, first, second


def cheb_step(level, keep, source, target, d, r, n, carry, gain):
    scale = 0.25**level
    k = 1 << level
    u, nb_u = neighbour_sums(lambda t, a, m: source[0, t, pl.ds(a, m)], r, n, k)
    v, nb_v = neighbour_sums(lambda t, a, m: source[1, t, pl.ds(a, m)], r, n, k)
    rows = pl.ds(r, n)
    for t in (0, 1):
        cross, squared, inv_u, inv_v = (keep[i, t, rows] for i in range(4))
        res_u = inv_u * (keep[4, t, rows] - cross * v[t] + DIFF[0] * scale * nb_u[t]) - u[t]
        res_v = inv_v * (keep[5, t, rows] + squared * u[t] + DIFF[1] * scale * nb_v[t]) - v[t]
        du, dv = gain * res_u, gain * res_v
        if carry is not None:
            du = du + carry * d[0, t, rows]
            dv = dv + carry * d[1, t, rows]
        d[0, t, rows] = du
        d[1, t, rows] = dv
        target[0, t, rows] = u[t] + du
        target[1, t, rows] = v[t] + dv


def residual(level, keep, diag, source, r, n):
    scale = 0.25**level
    k = 1 << level
    u, nb_u = neighbour_sums(lambda t, a, m: source[0, t, pl.ds(a, m)], r, n, k)
    v, nb_v = neighbour_sums(lambda t, a, m: source[1, t, pl.ds(a, m)], r, n, k)
    rows = pl.ds(r, n)
    first, second = [], []
    for t in (0, 1):
        first.append(
            keep[4, t, rows] - diag[0, t, rows] * u[t] - keep[0, t, rows] * v[t] + DIFF[0] * scale * nb_u[t]
        )
        second.append(
            keep[5, t, rows] - diag[1, t, rows] * v[t] + keep[1, t, rows] * u[t] + DIFF[1] * scale * nb_v[t]
        )
    return first, second


CARRY1 = _RHO1 * _RHO0
CARRY2 = _RHO2 * _RHO1


def write_gains(spread, out):
    lane = lax.broadcasted_iota(jnp.int32, (1, X), 1)
    for level in range(3):
        top = jnp.max(jnp.where(lane == level, spread, 0.0), axis=1, keepdims=True)
        tau = 1.0 / (1.0 + jnp.broadcast_to(top, (Z, X)))
        for i, factor in enumerate((1.0 / _CENTRE, 2.0 * _RHO1 / _HALF, 2.0 * _RHO2 / _HALF)):
            out[3 * level + i] = factor * tau


def pair_rows(value):
    n = value.shape[0] // 2
    pairs = value.reshape(n, 2, Z, X)
    return pairs[:, 0] + pairs[:, 1]


def restrict_01(first, second):
    lane, sub = lane_of(), sub_of()
    across = []
    for value in (first, second):
        a, b = value[0:1], value[1:2]
        across.append(jnp.where((lane & 1) == 0, a + roll_x(a, -1), b + roll_x(b, 1)))
    a, b = across
    return 0.125 * jnp.where((sub & 1) == 0, a + roll_z(a, -1), b + roll_z(b, 1))


def restrict_12(groups):
    lane, sub = lane_of(), sub_of()
    out = None
    for p, value in enumerate(groups):
        value = value + roll_x(value, 1 if p & 1 else -1)
        value = value + roll_x(value, 2 if p & 2 else -2)
        out = value if out is None else jnp.where((lane & 3) == p, value, out)
    return 0.125 * (out + jnp.where((sub & 2) == 0, roll_z(out, -2), roll_z(out, 2)))


def spread_x(tile, k, phase):
    return jnp.where((lane_of() & k) == phase, tile, roll_x(tile, -k if phase else k))


def packed_jacobian(uv, fk, level):
    scale = 0.25**level
    even = (sub_of() & 1) == 0
    u, v = jnp.where(even, uv, roll_z(uv, 1)), jnp.where(even, roll_z(uv, -1), uv)
    f, k = jnp.where(even, fk, roll_z(fk, 1)), jnp.where(even, roll_z(fk, -1), fk)
    product, squared = u * v, v * v
    diag = jnp.where(
        even,
        INV_STEP + squared + f + 6.0 * DIFF[0] * scale,
        INV_STEP + f + k - 2.0 * product + 6.0 * DIFF[1] * scale,
    )
    return 1.0 / diag, jnp.where(even, -2.0 * product, squared), diag


def packed_spread(uv, fk, level):
    scale = 0.25**level
    even = (sub_of() & 1) == 0
    inverse, other, _ = packed_jacobian(uv, fk, level)
    return jnp.where(even, 6.0 * DIFF[0] * scale - other, 6.0 * DIFF[1] * scale + other) * inverse


def packed_terms(source, g, n, level):
    k = 1 << level
    lane, sub = lane_of(), sub_of()
    even = (sub & 1) == 0
    first, last = (lane & (k - 1)) == 0, (lane & (k - 1)) == k - 1
    low, high = lane < k, lane >= X - k
    diff = jnp.where(even, DIFF[0] * 0.25**level, DIFF[1] * 0.25**level)
    wide = [source[t, pl.ds(g - 1, n + 2)] for t in (0, 1)]
    centre = [w[1 : n + 1] for w in wide]
    right = [roll_x(c, k) for c in centre]
    left = [roll_x(c, -k) for c in centre]
    out = []
    for t in (0, 1):
        c, w = centre[t], wide[t]
        total = jnp.where(low, right[1 - t], right[t]) + jnp.where(high, left[1 - t], left[t])
        if k == 2:
            ahead, back = roll_x(w, 1), roll_x(w, -1)
            total = total + jnp.where(first, back[0:n], ahead[1 : n + 1])
            total = total + jnp.where(last, ahead[2 : n + 2], back[1 : n + 1])
            total = total + roll_z(c, 2) + roll_z(c, -2)
        else:
            total = total + jnp.where(first, roll_x(w[0:n], -(k - 1)), roll_x(c, 1))
            total = total + jnp.where(last, roll_x(w[2 : n + 2], k - 1), roll_x(c, -1))
            total = total + 2.0 * roll_z(c, 4)
        other = jnp.where(even, roll_z(c, -1), roll_z(c, 1))
        out.append((c, other, diff * total))
    return out


def packed_first(coef, shift, b, target, d, g, n, gain):
    for t in (0, 1):
        value = gain * coef[0, t, pl.ds(g + shift, n)] * b[t, pl.ds(g + shift, n)]
        d[t, pl.ds(g, n)] = value
        target[t, pl.ds(g, n)] = value


def packed_step(level, coef, shift, b, source, target, d, g, n, carry, gain):
    for t, (c, other, spread) in enumerate(packed_terms(source, g, n, level)):
        at = pl.ds(g + shift, n)
        res = coef[0, t, at] * (b[t, at] + coef[1, t, at] * other + spread) - c
        delta = gain * res
        if carry is not None:
            delta = delta + carry * d[t, pl.ds(g, n)]
        d[t, pl.ds(g, n)] = delta
        target[t, pl.ds(g, n)] = c + delta


def plane(ref, f, y, rows):
    return ref[pl.ds(f * Z * rows + y, Z, stride=rows), :]


def is_even(axis):
    return lax.rem(lax.axis_index(axis), 2) == 0


def prev_of(even, first, second, at):
    return jnp.where(even, first[at], second[at])


def next_of(even, first, second, at):
    return jnp.where(even, second[at], first[at])


def first_kernel(rows, state, previous, feed, kill, first, second, main, coarse, *scratch):
    sources, sems = scratch[:4], scratch[4]
    copies = [
        pltpu.make_async_copy(ref, held, sems.at[i])
        for i, (ref, held) in enumerate(zip((state, previous, feed, kill), sources))
    ]
    for copy in copies:
        copy.start()
    for copy in copies:
        copy.wait()
    even = is_even("gy")
    state, previous, feed, kill = sources
    fields = [(state, 0), (state, 1), (previous, 0), (previous, 1), (feed, 0), (kill, 0)]
    for i, (ref, f) in enumerate(fields):
        for y in range(rows):
            main[i, y] = plane(ref, f, y, rows)
        top, bottom = main[i, 0 : HALOS[i]], main[i, rows - HALOS[i] : rows]
        at = slice(STARTS[i], STARTS[i] + HALOS[i])
        first[at] = jnp.where(even, top, bottom)
        second[at] = jnp.where(even, bottom, top)
    u, v, f, k = (main[i] for i in (0, 1, 4, 5))
    sums = [pair_rows(value) for value in (u, v, f, k)]
    pairs = []
    for p in (0, 1):
        values = [
            restrict_01(sums[2 * p][2 * g : 2 * g + 2], sums[2 * p + 1][2 * g : 2 * g + 2]) for g in range(OWN)
        ]
        pairs.append(jnp.concatenate(values, axis=0))
        coarse[p * OWN : (p + 1) * OWN] = pairs[p]
        for ref in (first, second):
            ref[FIELDS1 + p * OWN : FIELDS1 + (p + 1) * OWN] = pairs[p]

    uv, fk = (restrict_12([pair[j : j + 1] for j in range(OWN)]) for pair in pairs)
    both = jnp.where((sub_of() & 2) == 0, uv, fk)
    coarse[2 * OWN : 2 * OWN + 1] = both
    for ref in (first, second):
        ref[FIELDS2 : FIELDS2 + 1] = both


def split_fields2(both):
    low = (sub_of() & 2) == 0
    return jnp.where(low, both, roll_z(both, 2)), jnp.where(low, roll_z(both, -2), both)


def spread_kernel(main, coarse, out):
    lane = lax.broadcasted_iota(jnp.int32, (1, X), 1)
    u, v, f, k = (main[i] for i in (0, 1, 4, 5))
    cross, squared, inv_u, inv_v, _, _ = jacobian(u, v, f, k, 0)
    tops = [jnp.max(jnp.maximum((6.0 * DIFF[0] + cross) * inv_u, (6.0 * DIFF[1] + squared) * inv_v), axis=0)]
    tops.append(jnp.max(packed_spread(coarse[0:OWN], coarse[OWN : 2 * OWN], 1), axis=0))
    tops.append(packed_spread(*split_fields2(coarse[2 * OWN : 2 * OWN + 1]), 2)[0])
    result = jnp.zeros((1, X), jnp.float32)
    for level, top in enumerate(tops):
        top = jnp.max(jnp.max(top, axis=0, keepdims=True), axis=1, keepdims=True)
        result = jnp.where(lane == level, jnp.broadcast_to(top, (1, X)), result)
    out[...] = jnp.broadcast_to(result[None], out.shape)


def around(across, count, gathered):
    lane = lane_of()
    gx, gy = lax.axis_index("gx"), lax.axis_index("gy")
    columns = [lax.rem(gx + i + across, across) * count for i in (-1, 0, 1)]
    out = [[], []]
    for q in range(LO2, HI2):
        row = lax.rem(gy + q + 4 * count, count)
        left, centre, right = (gathered[pl.ds(column + row, 1)] for column in columns)
        out[0].append(centre)
        out[1].append(jnp.where(lane < X // 2, right, left))
    return [jnp.concatenate(groups, axis=0) for groups in out]


GROUPS1 = HI1 - LO1
GROUPS2 = HI2 - LO2


def entry(rows, i):
    starts = [0]
    for halo in HALOS:
        starts.append(starts[-1] + rows + 2 * halo)
    return (starts + [starts[-1] + 2 * GROUPS1])[i]


def entry_tiles(rows):
    return -(-entry(rows, 7) // PER)


def pack_slots(parts, width):
    lane = lane_of()
    left, right = None, None
    for j, part in enumerate(parts):
        a, b = roll_x(part, width * j), roll_x(part, width + width * j)
        left = a if left is None else jnp.where(lane >= width * j, a, left)
        right = b if right is None else jnp.where(lane >= width * j, b, right)
    return left, right


def unpack_slot(from_left, from_right, j, width):
    return jnp.where(lane_of() < X // 2, roll_x(from_right, -width * j), roll_x(from_left, X - width - width * j))


def unpack_entries(even_x, x_first, x_second, share, lo, hi):
    out = []
    for j in range(PER):
        a, b = max(lo, j * share), min(hi, (j + 1) * share)
        if a < b:
            strip = slice(a - j * share, b - j * share)
            left, right = prev_of(even_x, x_first, x_second, strip), next_of(even_x, x_first, x_second, strip)
            out.append((a - lo, b - lo, unpack_slot(left, right, j, WIDE)))
    return out


def unpack_fields2(even_x, x_first, x_second, share, j):
    strip = slice(share, share + 1)
    left, right = prev_of(even_x, x_first, x_second, strip), next_of(even_x, x_first, x_second, strip)
    return unpack_slot(left, right, j, WIDE2)


def pack_x_kernel(rows, main, coarse, y_first, y_second, first, second, held):
    even = is_even("gy")
    share = entry_tiles(rows)
    for i, halo in enumerate(HALOS):
        strip = slice(STARTS[i], STARTS[i] + halo)
        to = entry(rows, i)
        held[to : to + halo] = prev_of(even, y_first, y_second, strip)
        held[to + halo : to + halo + rows] = main[i]
        held[to + halo + rows : to + 2 * halo + rows] = next_of(even, y_first, y_second, strip)
    for p in (0, 1):
        to = entry(rows, 6) + p * GROUPS1
        strip = slice(FIELDS1 + p * OWN, FIELDS1 + (p + 1) * OWN)
        held[to : to + OWN] = prev_of(even, y_first, y_second, strip)
        held[to + OWN : to + 2 * OWN] = coarse[p * OWN : (p + 1) * OWN]
        held[to + 2 * OWN : to + 3 * OWN] = next_of(even, y_first, y_second, strip)
    left, right = pack_slots([held[j * share : (j + 1) * share] for j in range(PER)], WIDE)
    strip = slice(FIELDS2, FIELDS2 + 1)
    own = coarse[2 * OWN : 2 * OWN + 1]
    parts = [prev_of(even, y_first, y_second, strip), own, next_of(even, y_first, y_second, strip)]
    left2, right2 = pack_slots(parts, WIDE2)
    even = is_even("gx")
    first[0:share] = jnp.where(even, left, right)
    second[0:share] = jnp.where(even, right, left)
    first[share : share + 1] = jnp.where(even, left2, right2)
    second[share : share + 1] = jnp.where(even, right2, left2)


HALO1 = X // (2 * OWN)
EDGES = OWN + 1
FAR = EDGES + 2 * EDGE + 1


def level0_kernel(
    rows, main, y_first, y_second, x_first, x_second, gathered, own, first, second, keep, gain_out, fields, other, d, diag
):
    even, even_x = is_even("gy"), is_even("gx")
    total = rows + 2 * HALO0
    share = entry_tiles(rows)
    top = jnp.max(gathered[...], axis=0)
    write_gains(top[0:1], gain_out)
    g0, g1, g2 = (gain_out[i] for i in range(3))
    for i, halo in enumerate(HALOS):
        strip = slice(STARTS[i], STARTS[i] + halo)
        skip = HALO0 - halo
        fields[i, 0, skip:HALO0] = prev_of(even, y_first, y_second, strip)
        fields[i, 0, HALO0 : HALO0 + rows] = main[i]
        fields[i, 0, HALO0 + rows : total - skip] = next_of(even, y_first, y_second, strip)
        for a, b, value in unpack_entries(even_x, x_first, x_second, share, entry(rows, i), entry(rows, i + 1)):
            fields[i, 1, a + skip : b + skip] = value
    here = keep.at[6:8]

    def setup(r, n):
        at = pl.ds(r, n)
        u, nb_u = neighbour_sums(lambda t, a, m: fields[0, t, pl.ds(a, m)], r, n, 1)
        v, nb_v = neighbour_sums(lambda t, a, m: fields[1, t, pl.ds(a, m)], r, n, 1)
        for t in (0, 1):
            f, k = fields[4, t, at], fields[5, t, at]
            cross, squared, inv_u, inv_v, first, second = jacobian(u[t], v[t], f, k, 0)
            react = u[t] * squared
            b_u = (
                DIFF[0] * (nb_u[t] - 6.0 * u[t])
                - INV_STEP * (u[t] - fields[2, t, at])
                - react
                + f * (1.0 - u[t])
            )
            b_v = (
                DIFF[1] * (nb_v[t] - 6.0 * v[t]) - INV_STEP * (v[t] - fields[3, t, at]) + react - (f + k) * v[t]
            )
            for i, value in enumerate((cross, squared, inv_u, inv_v, b_u, b_v)):
                keep[i, t, at] = value
            diag[0, t, at] = first
            diag[1, t, at] = second
            for i, value in enumerate((g0 * inv_u * b_u, g0 * inv_v * b_v)):
                d[i, t, at] = value
                keep[6 + i, t, at] = value

    rows_loop(1, total - 1, setup)
    rows_loop(2, total - 2, lambda r, n: cheb_step(0, keep, here, other, d, r, n, CARRY1, g1))
    rows_loop(3, total - 3, lambda r, n: cheb_step(0, keep, other, here, d, r, n, CARRY2, g2))

    def down(r, n):
        res = residual(0, keep, diag, here, r, n)
        out = (r - HALO0) // 4
        for t in (0, 1):
            value = restrict_01(pair_rows(res[0][t]), pair_rows(res[1][t]))
            own[t, pl.ds(out, 1)] = value
            if t == 0:
                first[pl.ds(out, 1)] = value
                second[pl.ds(out, 1)] = value

    rows_loop(HALO0, HALO0 + rows, down, 4)

    lane = lane_of()
    sides = None
    for j in range(OWN):
        value = roll_x(own[1, j : j + 1], HALO1 + 2 * HALO1 * j)
        sides = value if sides is None else jnp.where(lane // (2 * HALO1) == j, value, sides)
    edges = []
    for start in (HALO0, HALO0 + rows - EDGE):
        halo = None
        for i in (0, 1):
            for j in range(EDGE):
                at = i * EDGE + j
                value = roll_x(keep[6 + i, 1, start + j : start + j + 1], 4 + 8 * at)
                halo = value if halo is None else jnp.where((lane >> 3) == at, value, halo)
        edges.append([keep[6, 0, start : start + EDGE], keep[7, 0, start : start + EDGE], halo])
    top, bottom = (jnp.concatenate(parts, axis=0) for parts in edges)
    for ref in (first, second):
        ref[OWN : OWN + 1] = sides
    strip = slice(FIELDS2, FIELDS2 + 1)
    for t in (0, 1):
        if t == 0:
            before, after = prev_of(even, y_first, y_second, strip), next_of(even, y_first, y_second, strip)
        else:
            before, after = (unpack_fields2(even_x, x_first, x_second, share, j) for j in (0, 2))
        first[FAR + t : FAR + t + 1] = jnp.where(even, after, before)
        second[FAR + t : FAR + t + 1] = jnp.where(even, before, after)
    first[EDGES : EDGES + 2 * EDGE + 1] = jnp.where(even, top, bottom)
    second[EDGES : EDGES + 2 * EDGE + 1] = jnp.where(even, bottom, top)


def coarse1_kernel(rows, coarse, y_first, y_second, x_first, x_second, gain, coef, fields):
    del gain
    even, even_x = is_even("gy"), is_even("gx")
    share = entry_tiles(rows)
    for p in (0, 1):
        to = p * GROUPS1
        strip = slice(FIELDS1 + p * OWN, FIELDS1 + (p + 1) * OWN)
        fields[0, to : to + OWN] = prev_of(even, y_first, y_second, strip)
        fields[0, to + OWN : to + 2 * OWN] = coarse[p * OWN : (p + 1) * OWN]
        fields[0, to + 2 * OWN : to + 3 * OWN] = next_of(even, y_first, y_second, strip)
    for a, b, value in unpack_entries(even_x, x_first, x_second, share, entry(rows, 6), entry(rows, 7)):
        fields[1, a:b] = value
    for t in (0, 1):
        for i, value in enumerate(packed_jacobian(fields[t, 0:GROUPS1], fields[t, GROUPS1 : 2 * GROUPS1], 1)):
            coef[i, t, 1 : SIZE1 - 1] = value


def coarse2_kernel(rows, coarse, y_first, y_second, x_first, x_second, b_first, b_second, coef):
    even, even_x = is_even("gy"), is_even("gx")
    share = entry_tiles(rows)
    near = slice(FIELDS2, FIELDS2 + 1)
    for t in (0, 1):
        far = slice(FAR + t, FAR + t + 1)
        if t == 0:
            middle = [
                prev_of(even, y_first, y_second, near),
                coarse[2 * OWN : 2 * OWN + 1],
                next_of(even, y_first, y_second, near),
            ]
        else:
            middle = [unpack_fields2(even_x, x_first, x_second, share, j) for j in range(3)]
        parts = [prev_of(even, b_first, b_second, far), *middle, next_of(even, b_first, b_second, far)]
        inverse, other, _ = packed_jacobian(*split_fields2(jnp.concatenate(parts, axis=0)), 2)
        coef[0, t, 1 : SIZE2 - 1] = inverse
        coef[1, t, 1 : SIZE2 - 1] = other


def level1_kernel(own, first, second, coef1, gain, packet, keep, y1, d1):
    b1, x1 = keep.at[0], keep.at[1]
    even = is_even("gy")
    for t in (0, 1):
        b1[t, 1 + OWN : 1 + 2 * OWN] = own[t]
        for take, at in ((prev_of, 1), (next_of, 1 + 2 * OWN)):
            if t == 0:
                b1[t, at : at + OWN] = take(even, first, second, slice(0, OWN))
            else:
                sides = take(even, first, second, slice(OWN, OWN + 1))
                for j in range(OWN):
                    b1[t, at + j : at + j + 1] = roll_x(sides, -(HALO1 + 2 * HALO1 * j))
    g0, g1, g2 = (gain[3 + i] for i in range(3))
    n = GROUPS1
    packed_first(coef1, 0, b1, x1, d1, 1, n, g0)
    packed_step(1, coef1, 0, b1, x1, y1, d1, 1, n, CARRY1, g1)
    packed_step(1, coef1, 0, b1, y1, x1, d1, 1, n, CARRY2, g2)
    here = pl.ds(1 + OWN, OWN)
    c, other, spread = packed_terms(x1, 1 + OWN, OWN, 1)[0]
    res = b1[0, here] - coef1[2, 0, here] * c + coef1[1, 0, here] * other + spread
    value = restrict_12([res[j : j + 1] for j in range(OWN)])
    for c in range(packet.shape[0]):
        packet[c : c + 1] = value


def rest_kernel(
    across, count, gathered, gain, coef1, coef2, keep0, keep1, first, second, out, d1, b2, x2, y2, d2, xu, yu, x0, y0, d0
):
    rows = out.shape[0] // (2 * Z)
    even = (sub_of() & 1) == 0
    b1, x1 = keep1.at[0], keep1.at[1]

    for t, groups in enumerate(around(across, count, gathered)):
        b2[t, 1 : SIZE2 - 1] = groups

    n = HI2 - LO2
    g0, g1, g2 = (gain[6 + i] for i in range(3))
    packed_first(coef2, 0, b2, x2, d2, 1, n, g0)
    packed_step(2, coef2, 0, b2, x2, y2, d2, 1, n, CARRY1, g1)
    packed_step(2, coef2, 0, b2, y2, x2, d2, 1, n, CARRY2, g2)
    packed_step(2, coef2, 0, b2, x2, y2, d2, 1, n, None, g0)
    packed_step(2, coef2, 0, b2, y2, x2, d2, 1, n, CARRY1, g1)
    packed_step(2, coef2, 0, b2, x2, y2, d2, 1, n, CARRY2, g2)

    g0, g1, g2 = (gain[3 + i] for i in range(3))
    shift = LO_UP - LO1
    for t in (0, 1):
        for g in range(LO_UP, HI_UP):
            p = g % 4
            value = y2[t, g // 4 - LO2 + 1 : g // 4 - LO2 + 2]
            value = spread_x(spread_x(value, 1, p & 1), 2, p & 2)
            at = g - LO_UP + 1
            xu[t, at : at + 1] = x1[t, at + shift : at + shift + 1] + value
    n = HI_UP - LO_UP
    packed_step(1, coef1, shift, b1, xu, yu, d1, 1, n, None, g0)
    packed_step(1, coef1, shift, b1, yu, xu, d1, 1, n, CARRY1, g1)
    packed_step(1, coef1, shift, b1, xu, yu, d1, 1, n, CARRY2, g2)

    g0, g1, g2 = (gain[i] for i in range(3))
    last = EDGES + 2 * EDGE
    even_y = is_even("gy")
    for i in (0, 1):
        for at, take in ((HALO0 - EDGE, prev_of), (HALO0 + rows, next_of)):
            strip = slice(EDGES + i * EDGE, EDGES + (i + 1) * EDGE)
            x0[i, 0, at : at + EDGE] = take(even_y, first, second, strip)
            sides = take(even_y, first, second, slice(last, last + 1))
            for j in range(EDGE):
                x0[i, 1, at + j : at + j + 1] = roll_x(sides, -(4 + 8 * (i * EDGE + j)))
        for t in (0, 1):
            x0[i, t, HALO0 : HALO0 + rows] = keep0[6 + i, t, HALO0 : HALO0 + rows]
    for t in (0, 1):
        for row in range(-2, rows // 2 + 2):
            at = row // 2 - LO_UP + 1
            value = spread_x(yu[t, at : at + 1], 1, row & 1)
            for i, fine in enumerate((jnp.where(even, value, roll_z(value, 1)), jnp.where(even, roll_z(value, -1), value))):
                for y in (2 * row, 2 * row + 1):
                    if -EDGE <= y < rows + EDGE:
                        x0[i, t, y + HALO0 : y + HALO0 + 1] = x0[i, t, y + HALO0 : y + HALO0 + 1] + fine
    total = rows + 2 * HALO0
    rows_loop(2, total - 2, lambda r, n: cheb_step(0, keep0, x0, y0, d0, r, n, None, g0))
    rows_loop(3, total - 3, lambda r, n: cheb_step(0, keep0, y0, x0, d0, r, n, CARRY1, g1))
    rows_loop(4, total - 4, lambda r, n: cheb_step(0, keep0, x0, y0, d0, r, n, CARRY2, g2))
    for i in (0, 1):
        for y in range(rows):
            out[pl.ds(i * Z * rows + y, Z, stride=rows), :] = y0[i, 0, HALO0 + y]


def call(kernel, out_shapes, scratch, *args, space=pltpu.VMEM):
    out = [jax.ShapeDtypeStruct(shape, jnp.float32) for shape in out_shapes]
    return pl.pallas_call(
        kernel,
        out_shape=out,
        in_specs=[pl.BlockSpec(memory_space=space)] * len(args),
        out_specs=[pl.BlockSpec(memory_space=pltpu.VMEM)] * len(out),
        scratch_shapes=[pltpu.VMEM(s, jnp.float32) if isinstance(s, tuple) else s for s in scratch],
        compiler_params=pltpu.CompilerParams(vmem_limit_bytes=24 * 2**20),
    )(*args)


def swap(value, axis, step):
    count = lax.axis_size(axis)
    assert count % 2 == 0
    pairs = [(i, (i + step) % count) for i in range(0, count, 2)]
    return lax.ppermute(value, axis, pairs + [(j, i) for i, j in pairs])


def exchange(first, second, axis):
    return swap(first, axis, -1), swap(second, axis, 1)


def body(state, previous, feed, kill):
    _, depth, rows, cols = state.shape
    assert depth == Z and cols == X and rows == 4 * OWN
    across, count = lax.axis_size("gx"), lax.axis_size("gy")
    total0 = rows + 2 * HALO0
    state = state.reshape(2 * Z * rows, X)
    previous = previous.reshape(2 * Z * rows, X)
    feed = feed.reshape(Z * rows, X)
    kill = kill.reshape(Z * rows, X)
    inputs = (state, previous, feed, kill)

    strip = (FIELDS2 + 1, Z, X)
    first, second, main, coarse = call(
        functools.partial(first_kernel, rows),
        [strip, strip, (6, rows, Z, X), (2 * OWN + 1, Z, X)],
        [*(a.shape for a in inputs), pltpu.SemaphoreType.DMA((4,))],
        *(pltpu.with_memory_space_constraint(a, pltpu.HBM) for a in inputs),
        space=pltpu.HBM,
    )
    y_packets = exchange(first, second, "gy")
    (spread,) = call(spread_kernel, [(across * count, Z // 2, X)], [], main, coarse)
    spread = lax.all_to_all(spread, ("gx", "gy"), 0, 0, tiled=True)

    strip = (entry_tiles(rows) + 1, Z, X)
    first, second = call(
        functools.partial(pack_x_kernel, rows),
        [strip, strip],
        [(PER * entry_tiles(rows), Z, X)],
        main,
        coarse,
        *y_packets,
    )
    x_packets = exchange(first, second, "gx")

    strip = (FAR + 2, Z, X)
    pair0 = (2, 2, total0, Z, X)
    own, first, second, keep0, gain = call(
        functools.partial(level0_kernel, rows),
        [(2, OWN, Z, X), strip, strip, (8, 2, total0, Z, X), (9, Z, X)],
        [(6, 2, total0, Z, X), pair0, pair0, pair0],
        main,
        *y_packets,
        *x_packets,
        spread,
    )
    (coef1,) = call(
        functools.partial(coarse1_kernel, rows),
        [(3, 2, SIZE1, Z, X)],
        [(2, 2 * GROUPS1, Z, X)],
        coarse,
        *y_packets,
        *x_packets,
        gain,
    )
    b_packets = exchange(first, second, "gy")

    one, two, up = (2, SIZE1, Z, X), (2, SIZE2, Z, X), (2, SIZE_UP, Z, X)
    packet, keep1 = call(
        level1_kernel, [(across * count, Z, X), (2, *one)], [one, one], own, *b_packets, coef1, gain
    )
    gathered = lax.all_to_all(packet, ("gx", "gy"), 0, 0, tiled=True)
    (coef2,) = call(
        functools.partial(coarse2_kernel, rows),
        [(2, 2, SIZE2, Z, X)],
        [],
        coarse,
        *y_packets,
        *x_packets,
        *b_packets,
    )

    (out,) = call(
        functools.partial(rest_kernel, across, count),
        [(2 * Z * rows, X)],
        [one, two, two, two, two, up, up, pair0, pair0, pair0],
        gathered,
        gain,
        coef1,
        coef2,
        keep0,
        keep1,
        *b_packets,
    )
    return out.reshape(2, Z, rows, X)


def solution(mesh):
    placed = (
        P(None, None, "gy", "gx"),
        P(None, None, "gy", "gx"),
        P(None, "gy", "gx"),
        P(None, "gy", "gx"),
    )
    return jax.shard_map(
        body, mesh=mesh, in_specs=placed, out_specs=P(None, None, "gy", "gx"), check_vma=False
    )
```

```python
import functools

import jax
import jax.numpy as jnp
from jax import lax
from jax.experimental import pallas as pl
from jax.experimental.pallas import tpu as pltpu
from jax.sharding import PartitionSpec as P

DIFF = (40.0, 20.0)
INV_STEP = 2.0
LOWER = 0.25

_CENTRE = (1.0 + LOWER) / 2.0
_HALF = (1.0 - LOWER) / 2.0
_SIGMA = _CENTRE / _HALF
_RHO0 = 1.0 / _SIGMA
_RHO1 = 1.0 / (2.0 * _SIGMA - _RHO0)
_RHO2 = 1.0 / (2.0 * _SIGMA - _RHO1)

Z = 8
X = 128
HALO0 = 4
HALOS = (4, 4, 3, 3, 3, 3)
STARTS = tuple(sum(HALOS[:i]) for i in range(6))
FIELDS1 = sum(HALOS)
FIELDS2 = FIELDS1 + 8
PACKET = FIELDS2 + 1
WIDE = 42
PER = X // WIDE
EDGE = 3
CHUNK = 4

LO1, HI1 = -4, 8
LO2, HI2 = -2, 3
LO_UP, HI_UP = -3, 7
SIZE1, SIZE2, SIZE_UP = HI1 - LO1 + 2, HI2 - LO2 + 2, HI_UP - LO_UP + 2
OWN = 4


def lane_of():
    return lax.broadcasted_iota(jnp.int32, (1, Z, X), 2)


def sub_of():
    return lax.broadcasted_iota(jnp.int32, (1, Z, X), 1)


def roll_x(tile, shift):
    shift = shift % X
    return pltpu.roll(tile, shift, 2) if shift else tile


def roll_z(tile, shift):
    shift = shift % Z
    return pltpu.roll(tile, shift, 1) if shift else tile


def rows_loop(lo, hi, body, step=CHUNK):
    full = (hi - lo) // step
    if full == 1:
        body(lo, step)
    elif full > 1:

        def trip(i, carry):
            body(lo + i * step, step)
            return carry

        lax.fori_loop(0, full, trip, 0)
    rest = hi - lo - full * step
    if rest:
        body(hi - rest, rest)


def neighbour_sums(read, r, n, k):
    lane = lane_of()
    low, high = lane < k, lane >= X - k
    centre = [read(t, r, n) for t in (0, 1)]
    right = [roll_x(c, k) for c in centre]
    left = [roll_x(c, -k) for c in centre]
    sums = []
    for t in (0, 1):
        c = centre[t]
        along_x = jnp.where(low, right[1 - t], right[t]) + jnp.where(high, left[1 - t], left[t])
        along_y = read(t, r - 1, n) + read(t, r + 1, n)
        along_z = 2.0 * roll_z(c, k) if 2 * k == Z else roll_z(c, k) + roll_z(c, -k)
        sums.append(along_x + along_y + along_z)
    return centre, sums


def jacobian(u, v, f, k, level):
    scale = 0.25**level
    product = u * v
    squared = v * v
    first = INV_STEP + squared + f + 6.0 * DIFF[0] * scale
    second = INV_STEP + f + k - 2.0 * product + 6.0 * DIFF[1] * scale
    return 2.0 * product, squared, 1.0 / first, 1.0 / second, first, second


def cheb_step(level, keep, source, target, d, r, n, carry, gain):
    scale = 0.25**level
    k = 1 << level
    u, nb_u = neighbour_sums(lambda t, a, m: source[0, t, pl.ds(a, m)], r, n, k)
    v, nb_v = neighbour_sums(lambda t, a, m: source[1, t, pl.ds(a, m)], r, n, k)
    rows = pl.ds(r, n)
    for t in (0, 1):
        cross, squared, inv_u, inv_v = (keep[i, t, rows] for i in range(4))
        res_u = inv_u * (keep[4, t, rows] - cross * v[t] + DIFF[0] * scale * nb_u[t]) - u[t]
        res_v = inv_v * (keep[5, t, rows] + squared * u[t] + DIFF[1] * scale * nb_v[t]) - v[t]
        du, dv = gain * res_u, gain * res_v
        if carry is not None:
            du = du + carry * d[0, t, rows]
            dv = dv + carry * d[1, t, rows]
        d[0, t, rows] = du
        d[1, t, rows] = dv
        target[0, t, rows] = u[t] + du
        target[1, t, rows] = v[t] + dv


def residual(level, keep, diag, source, r, n):
    scale = 0.25**level
    k = 1 << level
    u, nb_u = neighbour_sums(lambda t, a, m: source[0, t, pl.ds(a, m)], r, n, k)
    v, nb_v = neighbour_sums(lambda t, a, m: source[1, t, pl.ds(a, m)], r, n, k)
    rows = pl.ds(r, n)
    first, second = [], []
    for t in (0, 1):
        first.append(
            keep[4, t, rows] - diag[0, t, rows] * u[t] - keep[0, t, rows] * v[t] + DIFF[0] * scale * nb_u[t]
        )
        second.append(
            keep[5, t, rows] - diag[1, t, rows] * v[t] + keep[1, t, rows] * u[t] + DIFF[1] * scale * nb_v[t]
        )
    return first, second


CARRY1 = _RHO1 * _RHO0
CARRY2 = _RHO2 * _RHO1


def write_gains(spread, out):
    lane = lax.broadcasted_iota(jnp.int32, (1, X), 1)
    for level in range(3):
        top = jnp.max(jnp.where(lane == level, spread, 0.0), axis=1, keepdims=True)
        tau = 1.0 / (1.0 + jnp.broadcast_to(top, (Z, X)))
        for i, factor in enumerate((1.0 / _CENTRE, 2.0 * _RHO1 / _HALF, 2.0 * _RHO2 / _HALF)):
            out[3 * level + i] = factor * tau


def pair_rows(value):
    n = value.shape[0] // 2
    pairs = value.reshape(n, 2, Z, X)
    return pairs[:, 0] + pairs[:, 1]


def restrict_01(first, second):
    lane, sub = lane_of(), sub_of()
    across = []
    for value in (first, second):
        a, b = value[0:1], value[1:2]
        across.append(jnp.where((lane & 1) == 0, a + roll_x(a, -1), b + roll_x(b, 1)))
    a, b = across
    return 0.125 * jnp.where((sub & 1) == 0, a + roll_z(a, -1), b + roll_z(b, 1))


def restrict_12(groups):
    lane, sub = lane_of(), sub_of()
    out = None
    for p, value in enumerate(groups):
        value = value + roll_x(value, 1 if p & 1 else -1)
        value = value + roll_x(value, 2 if p & 2 else -2)
        out = value if out is None else jnp.where((lane & 3) == p, value, out)
    return 0.125 * (out + jnp.where((sub & 2) == 0, roll_z(out, -2), roll_z(out, 2)))


def spread_x(tile, k, phase):
    return jnp.where((lane_of() & k) == phase, tile, roll_x(tile, -k if phase else k))


def packed_jacobian(uv, fk, level):
    scale = 0.25**level
    even = (sub_of() & 1) == 0
    u, v = jnp.where(even, uv, roll_z(uv, 1)), jnp.where(even, roll_z(uv, -1), uv)
    f, k = jnp.where(even, fk, roll_z(fk, 1)), jnp.where(even, roll_z(fk, -1), fk)
    product, squared = u * v, v * v
    diag = jnp.where(
        even,
        INV_STEP + squared + f + 6.0 * DIFF[0] * scale,
        INV_STEP + f + k - 2.0 * product + 6.0 * DIFF[1] * scale,
    )
    return 1.0 / diag, jnp.where(even, -2.0 * product, squared), diag


def packed_spread(uv, fk, level):
    scale = 0.25**level
    even = (sub_of() & 1) == 0
    inverse, other, _ = packed_jacobian(uv, fk, level)
    return jnp.where(even, 6.0 * DIFF[0] * scale - other, 6.0 * DIFF[1] * scale + other) * inverse


def packed_terms(source, g, n, level):
    k = 1 << level
    lane, sub = lane_of(), sub_of()
    even = (sub & 1) == 0
    first, last = (lane & (k - 1)) == 0, (lane & (k - 1)) == k - 1
    low, high = lane < k, lane >= X - k
    diff = jnp.where(even, DIFF[0] * 0.25**level, DIFF[1] * 0.25**level)
    wide = [source[t, pl.ds(g - 1, n + 2)] for t in (0, 1)]
    centre = [w[1 : n + 1] for w in wide]
    right = [roll_x(c, k) for c in centre]
    left = [roll_x(c, -k) for c in centre]
    out = []
    for t in (0, 1):
        c, w = centre[t], wide[t]
        total = jnp.where(low, right[1 - t], right[t]) + jnp.where(high, left[1 - t], left[t])
        if k == 2:
            ahead, back = roll_x(w, 1), roll_x(w, -1)
            total = total + jnp.where(first, back[0:n], ahead[1 : n + 1])
            total = total + jnp.where(last, ahead[2 : n + 2], back[1 : n + 1])
            total = total + roll_z(c, 2) + roll_z(c, -2)
        else:
            total = total + jnp.where(first, roll_x(w[0:n], -(k - 1)), roll_x(c, 1))
            total = total + jnp.where(last, roll_x(w[2 : n + 2], k - 1), roll_x(c, -1))
            total = total + 2.0 * roll_z(c, 4)
        other = jnp.where(even, roll_z(c, -1), roll_z(c, 1))
        out.append((c, other, diff * total))
    return out


def packed_first(coef, shift, b, target, d, g, n, gain):
    for t in (0, 1):
        value = gain * coef[0, t, pl.ds(g + shift, n)] * b[t, pl.ds(g + shift, n)]
        d[t, pl.ds(g, n)] = value
        target[t, pl.ds(g, n)] = value


def packed_step(level, coef, shift, b, source, target, d, g, n, carry, gain):
    for t, (c, other, spread) in enumerate(packed_terms(source, g, n, level)):
        at = pl.ds(g + shift, n)
        res = coef[0, t, at] * (b[t, at] + coef[1, t, at] * other + spread) - c
        delta = gain * res
        if carry is not None:
            delta = delta + carry * d[t, pl.ds(g, n)]
        d[t, pl.ds(g, n)] = delta
        target[t, pl.ds(g, n)] = c + delta


def plane(ref, f, y, rows):
    return ref[pl.ds(f * Z * rows + y, Z, stride=rows), :]


def is_even(axis):
    return lax.rem(lax.axis_index(axis), 2) == 0


def prev_of(even, first, second, at):
    return jnp.where(even, first[at], second[at])


def next_of(even, first, second, at):
    return jnp.where(even, second[at], first[at])


def first_kernel(rows, state, previous, feed, kill, first, second, main, coarse, *scratch):
    sources, sems = scratch[:4], scratch[4]
    copies = [
        pltpu.make_async_copy(ref, held, sems.at[i])
        for i, (ref, held) in enumerate(zip((state, previous, feed, kill), sources))
    ]
    for copy in copies:
        copy.start()
    for copy in copies:
        copy.wait()
    even = is_even("gy")
    state, previous, feed, kill = sources
    fields = [(state, 0), (state, 1), (previous, 0), (previous, 1), (feed, 0), (kill, 0)]
    for i, (ref, f) in enumerate(fields):
        for y in range(rows):
            main[i, y] = plane(ref, f, y, rows)
        top, bottom = main[i, 0 : HALOS[i]], main[i, rows - HALOS[i] : rows]
        at = slice(STARTS[i], STARTS[i] + HALOS[i])
        first[at] = jnp.where(even, top, bottom)
        second[at] = jnp.where(even, bottom, top)
    u, v, f, k = (main[i] for i in (0, 1, 4, 5))
    sums = [pair_rows(value) for value in (u, v, f, k)]
    pairs = []
    for p in (0, 1):
        values = [
            restrict_01(sums[2 * p][2 * g : 2 * g + 2], sums[2 * p + 1][2 * g : 2 * g + 2]) for g in range(OWN)
        ]
        pairs.append(jnp.concatenate(values, axis=0))
        coarse[p * OWN : (p + 1) * OWN] = pairs[p]
        for ref in (first, second):
            ref[FIELDS1 + p * OWN : FIELDS1 + (p + 1) * OWN] = pairs[p]

    uv, fk = (restrict_12([pair[j : j + 1] for j in range(OWN)]) for pair in pairs)
    both = jnp.where((sub_of() & 2) == 0, uv, fk)
    coarse[2 * OWN : 2 * OWN + 1] = both
    for ref in (first, second):
        ref[FIELDS2 : FIELDS2 + 1] = both


def split_fields2(both):
    low = (sub_of() & 2) == 0
    return jnp.where(low, both, roll_z(both, 2)), jnp.where(low, roll_z(both, -2), both)


def spread_kernel(main, coarse, out):
    lane = lax.broadcasted_iota(jnp.int32, (1, X), 1)
    u, v, f, k = (main[i] for i in (0, 1, 4, 5))
    cross, squared, inv_u, inv_v, _, _ = jacobian(u, v, f, k, 0)
    tops = [jnp.max(jnp.maximum((6.0 * DIFF[0] + cross) * inv_u, (6.0 * DIFF[1] + squared) * inv_v), axis=0)]
    tops.append(jnp.max(packed_spread(coarse[0:OWN], coarse[OWN : 2 * OWN], 1), axis=0))
    tops.append(packed_spread(*split_fields2(coarse[2 * OWN : 2 * OWN + 1]), 2)[0])
    result = jnp.zeros((1, X), jnp.float32)
    for level, top in enumerate(tops):
        top = jnp.max(jnp.max(top, axis=0, keepdims=True), axis=1, keepdims=True)
        result = jnp.where(lane == level, jnp.broadcast_to(top, (1, X)), result)
    out[...] = jnp.broadcast_to(result[None], out.shape)


GROUPS1 = HI1 - LO1
GROUPS2 = HI2 - LO2


def tiles_for(entries):
    return -(-entries // PER)


def pack_edges(entries, even, first, second):
    lane = lane_of()
    share = first.shape[0]
    left, right = None, None
    for j in range(PER):
        part = entries[j * share : (j + 1) * share]
        a, b = roll_x(part, WIDE * j), roll_x(part, WIDE + WIDE * j)
        left = a if left is None else jnp.where(lane >= WIDE * j, a, left)
        right = b if right is None else jnp.where(lane >= WIDE * j, b, right)
    first[...] = jnp.where(even, left, right)
    second[...] = jnp.where(even, right, left)


def halo_tiles(even, packets, lo, hi):
    first, second = packets
    share = first.shape[0]
    lane = lane_of()
    out = []
    for j in range(PER):
        a, b = max(lo, j * share), min(hi, (j + 1) * share)
        if a < b:
            strip = slice(a - j * share, b - j * share)
            left, right = prev_of(even, first, second, strip), next_of(even, first, second, strip)
            value = jnp.where(lane < X // 2, roll_x(right, -WIDE * j), roll_x(left, X - WIDE - WIDE * j))
            out.append((a - lo, b - lo, value))
    return out


def pack_own_kernel(rows, main, coarse, first, second, held):
    for i in range(6):
        held[i * rows : (i + 1) * rows] = main[i]
    held[6 * rows : 6 * rows + 2 * OWN + 1] = coarse[...]
    pack_edges(held, is_even("gx"), first, second)


def pack_corner_kernel(y_first, y_second, first, second, held):
    even = is_even("gy")
    every = slice(0, PACKET)
    held[0:PACKET] = prev_of(even, y_first, y_second, every)
    held[PACKET : 2 * PACKET] = next_of(even, y_first, y_second, every)
    pack_edges(held, is_even("gx"), first, second)


EDGES = 2 * OWN
FAR = EDGES + 2 * EDGE + 1


def level0_kernel(
    rows, main, y_first, y_second, own_a, own_b, corner_a, corner_b, gathered, own, first, second, keep, gain_out, fields, other, d, diag
):
    even, even_x = is_even("gy"), is_even("gx")
    total = rows + 2 * HALO0
    own_x, corner_x = (own_a, own_b), (corner_a, corner_b)
    top = jnp.max(gathered[...], axis=0)
    write_gains(top[0:1], gain_out)
    g0, g1, g2 = (gain_out[i] for i in range(3))
    for i, halo in enumerate(HALOS):
        strip = slice(STARTS[i], STARTS[i] + halo)
        skip = HALO0 - halo
        fields[i, 0, skip:HALO0] = prev_of(even, y_first, y_second, strip)
        fields[i, 0, HALO0 : HALO0 + rows] = main[i]
        fields[i, 0, HALO0 + rows : total - skip] = next_of(even, y_first, y_second, strip)
        for packets, lo, n, at in (
            (corner_x, STARTS[i], halo, skip),
            (own_x, i * rows, rows, HALO0),
            (corner_x, PACKET + STARTS[i], halo, HALO0 + rows),
        ):
            for a, b, value in halo_tiles(even_x, packets, lo, lo + n):
                fields[i, 1, at + a : at + b] = value
    here = keep.at[6:8]

    def setup(r, n):
        at = pl.ds(r, n)
        u, nb_u = neighbour_sums(lambda t, a, m: fields[0, t, pl.ds(a, m)], r, n, 1)
        v, nb_v = neighbour_sums(lambda t, a, m: fields[1, t, pl.ds(a, m)], r, n, 1)
        for t in (0, 1):
            f, k = fields[4, t, at], fields[5, t, at]
            cross, squared, inv_u, inv_v, first, second = jacobian(u[t], v[t], f, k, 0)
            react = u[t] * squared
            b_u = (
                DIFF[0] * (nb_u[t] - 6.0 * u[t])
                - INV_STEP * (u[t] - fields[2, t, at])
                - react
                + f * (1.0 - u[t])
            )
            b_v = (
                DIFF[1] * (nb_v[t] - 6.0 * v[t]) - INV_STEP * (v[t] - fields[3, t, at]) + react - (f + k) * v[t]
            )
            for i, value in enumerate((cross, squared, inv_u, inv_v, b_u, b_v)):
                keep[i, t, at] = value
            diag[0, t, at] = first
            diag[1, t, at] = second
            for i, value in enumerate((g0 * inv_u * b_u, g0 * inv_v * b_v)):
                d[i, t, at] = value
                keep[6 + i, t, at] = value

    rows_loop(1, total - 1, setup)
    rows_loop(2, total - 2, lambda r, n: cheb_step(0, keep, here, other, d, r, n, CARRY1, g1))
    rows_loop(3, total - 3, lambda r, n: cheb_step(0, keep, other, here, d, r, n, CARRY2, g2))

    def down(r, n):
        res = residual(0, keep, diag, here, r, n)
        out = (r - HALO0) // 4
        for t in (0, 1):
            value = restrict_01(pair_rows(res[0][t]), pair_rows(res[1][t]))
            own[t, pl.ds(out, 1)] = value
            if t == 0:
                first[pl.ds(out, 1)] = value
                second[pl.ds(out, 1)] = value

    rows_loop(HALO0, HALO0 + rows, down, 4)

    lane = lane_of()
    edges = []
    for start in (HALO0, HALO0 + rows - EDGE):
        halo = None
        for i in (0, 1):
            for j in range(EDGE):
                at = i * EDGE + j
                value = roll_x(keep[6 + i, 1, start + j : start + j + 1], 4 + 8 * at)
                halo = value if halo is None else jnp.where((lane >> 3) == at, value, halo)
        edges.append([keep[6, 0, start : start + EDGE], keep[7, 0, start : start + EDGE], halo])
    top, bottom = (jnp.concatenate(parts, axis=0) for parts in edges)
    for ref in (first, second):
        ref[OWN : 2 * OWN] = own[1]
    strip = slice(FIELDS2, FIELDS2 + 1)
    for t in (0, 1):
        if t == 0:
            before, after = prev_of(even, y_first, y_second, strip), next_of(even, y_first, y_second, strip)
        else:
            before, after = (
                halo_tiles(even_x, corner_x, at + FIELDS2, at + FIELDS2 + 1)[0][2] for at in (0, PACKET)
            )
        first[FAR + t : FAR + t + 1] = jnp.where(even, after, before)
        second[FAR + t : FAR + t + 1] = jnp.where(even, before, after)
    first[EDGES : EDGES + 2 * EDGE + 1] = jnp.where(even, top, bottom)
    second[EDGES : EDGES + 2 * EDGE + 1] = jnp.where(even, bottom, top)


def coarse1_kernel(
    rows, coarse, y_first, y_second, own_a, own_b, corner_a, corner_b, gain, coef, fields
):
    del gain
    even, even_x = is_even("gy"), is_even("gx")
    own_x, corner_x = (own_a, own_b), (corner_a, corner_b)
    for p in (0, 1):
        to = p * GROUPS1
        strip = slice(FIELDS1 + p * OWN, FIELDS1 + (p + 1) * OWN)
        fields[0, to : to + OWN] = prev_of(even, y_first, y_second, strip)
        fields[0, to + OWN : to + 2 * OWN] = coarse[p * OWN : (p + 1) * OWN]
        fields[0, to + 2 * OWN : to + 3 * OWN] = next_of(even, y_first, y_second, strip)
        for part, (packets, lo) in enumerate(
            ((corner_x, FIELDS1), (own_x, 6 * rows), (corner_x, PACKET + FIELDS1))
        ):
            lo += p * OWN
            for a, b, value in halo_tiles(even_x, packets, lo, lo + OWN):
                fields[1, to + part * OWN + a : to + part * OWN + b] = value
    for t in (0, 1):
        for i, value in enumerate(packed_jacobian(fields[t, 0:GROUPS1], fields[t, GROUPS1 : 2 * GROUPS1], 1)):
            coef[i, t, 1 : SIZE1 - 1] = value


def coarse2_kernel(
    rows, coarse, y_first, y_second, own_a, own_b, corner_a, corner_b, b_first, b_second, coef
):
    even, even_x = is_even("gy"), is_even("gx")
    own_x, corner_x = (own_a, own_b), (corner_a, corner_b)
    near = slice(FIELDS2, FIELDS2 + 1)
    for t in (0, 1):
        far = slice(FAR + t, FAR + t + 1)
        if t == 0:
            middle = [
                prev_of(even, y_first, y_second, near),
                coarse[2 * OWN : 2 * OWN + 1],
                next_of(even, y_first, y_second, near),
            ]
        else:
            middle = [
                halo_tiles(even_x, packets, lo, lo + 1)[0][2]
                for packets, lo in ((corner_x, FIELDS2), (own_x, 6 * rows + 2 * OWN), (corner_x, PACKET + FIELDS2))
            ]
        parts = [prev_of(even, b_first, b_second, far), *middle, next_of(even, b_first, b_second, far)]
        inverse, other, _ = packed_jacobian(*split_fields2(jnp.concatenate(parts, axis=0)), 2)
        coef[0, t, 1 : SIZE2 - 1] = inverse
        coef[1, t, 1 : SIZE2 - 1] = other


def level1_kernel(own, first, second, coef1, gain, packet, keep, y1, d1):
    b1, x1 = keep.at[0], keep.at[1]
    even = is_even("gy")
    for t in (0, 1):
        b1[t, 1 + OWN : 1 + 2 * OWN] = own[t]
        strip = slice(t * OWN, (t + 1) * OWN)
        b1[t, 1 : 1 + OWN] = prev_of(even, first, second, strip)
        b1[t, 1 + 2 * OWN : 1 + 3 * OWN] = next_of(even, first, second, strip)
    g0, g1, g2 = (gain[3 + i] for i in range(3))
    n = GROUPS1
    packed_first(coef1, 0, b1, x1, d1, 1, n, g0)
    packed_step(1, coef1, 0, b1, x1, y1, d1, 1, n, CARRY1, g1)
    packed_step(1, coef1, 0, b1, y1, x1, d1, 1, n, CARRY2, g2)
    here = pl.ds(1 + OWN, OWN)
    for t, (c, other, spread) in enumerate(packed_terms(x1, 1 + OWN, OWN, 1)):
        res = b1[t, here] - coef1[2, t, here] * c + coef1[1, t, here] * other + spread
        packet[t : t + 1] = restrict_12([res[j : j + 1] for j in range(OWN)])


def rest_kernel(
    own2, near_a, near_b, far_a, far_b, gain, coef1, coef2, keep0, keep1, first, second, out, d1, b2, x2, y2, d2, xu, yu, x0, y0, d0
):
    rows = out.shape[0] // (2 * Z)
    even = (sub_of() & 1) == 0
    b1, x1 = keep1.at[0], keep1.at[1]

    even_y, low = is_even("gy"), lax.rem(lax.axis_index("gy"), 4) < 2
    for t in (0, 1):
        at = slice(t, t + 1)
        parts = [
            next_of(low, far_a, far_b, at),
            prev_of(even_y, near_a, near_b, at),
            own2[at],
            next_of(even_y, near_a, near_b, at),
            prev_of(low, far_a, far_b, at),
        ]
        b2[t, 1 : SIZE2 - 1] = jnp.concatenate(parts, axis=0)

    n = HI2 - LO2
    g0, g1, g2 = (gain[6 + i] for i in range(3))
    packed_first(coef2, 0, b2, x2, d2, 1, n, g0)
    packed_step(2, coef2, 0, b2, x2, y2, d2, 1, n, CARRY1, g1)
    packed_step(2, coef2, 0, b2, y2, x2, d2, 1, n, CARRY2, g2)
    packed_step(2, coef2, 0, b2, x2, y2, d2, 1, n, None, g0)
    packed_step(2, coef2, 0, b2, y2, x2, d2, 1, n, CARRY1, g1)
    packed_step(2, coef2, 0, b2, x2, y2, d2, 1, n, CARRY2, g2)

    g0, g1, g2 = (gain[3 + i] for i in range(3))
    shift = LO_UP - LO1
    for t in (0, 1):
        for g in range(LO_UP, HI_UP):
            p = g % 4
            value = y2[t, g // 4 - LO2 + 1 : g // 4 - LO2 + 2]
            value = spread_x(spread_x(value, 1, p & 1), 2, p & 2)
            at = g - LO_UP + 1
            xu[t, at : at + 1] = x1[t, at + shift : at + shift + 1] + value
    n = HI_UP - LO_UP
    packed_step(1, coef1, shift, b1, xu, yu, d1, 1, n, None, g0)
    packed_step(1, coef1, shift, b1, yu, xu, d1, 1, n, CARRY1, g1)
    packed_step(1, coef1, shift, b1, xu, yu, d1, 1, n, CARRY2, g2)

    g0, g1, g2 = (gain[i] for i in range(3))
    last = EDGES + 2 * EDGE
    for i in (0, 1):
        for at, take in ((HALO0 - EDGE, prev_of), (HALO0 + rows, next_of)):
            strip = slice(EDGES + i * EDGE, EDGES + (i + 1) * EDGE)
            x0[i, 0, at : at + EDGE] = take(even_y, first, second, strip)
            sides = take(even_y, first, second, slice(last, last + 1))
            for j in range(EDGE):
                x0[i, 1, at + j : at + j + 1] = roll_x(sides, -(4 + 8 * (i * EDGE + j)))
        for t in (0, 1):
            x0[i, t, HALO0 : HALO0 + rows] = keep0[6 + i, t, HALO0 : HALO0 + rows]
    for t in (0, 1):
        for row in range(-2, rows // 2 + 2):
            at = row // 2 - LO_UP + 1
            value = spread_x(yu[t, at : at + 1], 1, row & 1)
            for i, fine in enumerate((jnp.where(even, value, roll_z(value, 1)), jnp.where(even, roll_z(value, -1), value))):
                for y in (2 * row, 2 * row + 1):
                    if -EDGE <= y < rows + EDGE:
                        x0[i, t, y + HALO0 : y + HALO0 + 1] = x0[i, t, y + HALO0 : y + HALO0 + 1] + fine
    total = rows + 2 * HALO0
    rows_loop(2, total - 2, lambda r, n: cheb_step(0, keep0, x0, y0, d0, r, n, None, g0))
    rows_loop(3, total - 3, lambda r, n: cheb_step(0, keep0, y0, x0, d0, r, n, CARRY1, g1))
    rows_loop(4, total - 4, lambda r, n: cheb_step(0, keep0, x0, y0, d0, r, n, CARRY2, g2))
    for i in (0, 1):
        for y in range(rows):
            out[pl.ds(i * Z * rows + y, Z, stride=rows), :] = y0[i, 0, HALO0 + y]


def call(kernel, out_shapes, scratch, *args, space=pltpu.VMEM):
    out = [jax.ShapeDtypeStruct(shape, jnp.float32) for shape in out_shapes]
    return pl.pallas_call(
        kernel,
        out_shape=out,
        in_specs=[pl.BlockSpec(memory_space=space)] * len(args),
        out_specs=[pl.BlockSpec(memory_space=pltpu.VMEM)] * len(out),
        scratch_shapes=[pltpu.VMEM(s, jnp.float32) if isinstance(s, tuple) else s for s in scratch],
        compiler_params=pltpu.CompilerParams(vmem_limit_bytes=24 * 2**20),
    )(*args)


def swap(value, axis, step):
    count = lax.axis_size(axis)
    assert count % 2 == 0
    pairs = [(i, (i + step) % count) for i in range(0, count, 2)]
    return lax.ppermute(value, axis, pairs + [(j, i) for i, j in pairs])


def swap_far(value, axis, step):
    count = lax.axis_size(axis)
    assert count % 4 == 0
    pairs = [(i + j, (i + j + 2 * step) % count) for i in range(0, count, 4) for j in (0, 1)]
    return lax.ppermute(value, axis, pairs + [(j, i) for i, j in pairs])


def exchange(first, second, axis):
    return swap(first, axis, -1), swap(second, axis, 1)


def body(state, previous, feed, kill):
    _, depth, rows, cols = state.shape
    assert depth == Z and cols == X and rows == 4 * OWN
    across, count = lax.axis_size("gx"), lax.axis_size("gy")
    total0 = rows + 2 * HALO0
    state = state.reshape(2 * Z * rows, X)
    previous = previous.reshape(2 * Z * rows, X)
    feed = feed.reshape(Z * rows, X)
    kill = kill.reshape(Z * rows, X)
    inputs = (state, previous, feed, kill)

    strip = (FIELDS2 + 1, Z, X)
    first, second, main, coarse = call(
        functools.partial(first_kernel, rows),
        [strip, strip, (6, rows, Z, X), (2 * OWN + 1, Z, X)],
        [*(a.shape for a in inputs), pltpu.SemaphoreType.DMA((4,))],
        *(pltpu.with_memory_space_constraint(a, pltpu.HBM) for a in inputs),
        space=pltpu.HBM,
    )
    y_packets = exchange(first, second, "gy")
    (spread,) = call(spread_kernel, [(across * count, Z // 2, X)], [], main, coarse)
    spread = lax.all_to_all(spread, ("gx", "gy"), 0, 0, tiled=True)

    tiles = tiles_for(6 * rows + 2 * OWN + 1)
    own_x = exchange(
        *call(
            functools.partial(pack_own_kernel, rows),
            [(tiles, Z, X), (tiles, Z, X)],
            [(PER * tiles, Z, X)],
            main,
            coarse,
        ),
        "gx",
    )
    tiles = tiles_for(2 * PACKET)
    corner_x = exchange(
        *call(pack_corner_kernel, [(tiles, Z, X), (tiles, Z, X)], [(PER * tiles, Z, X)], *y_packets), "gx"
    )

    strip = (FAR + 2, Z, X)
    pair0 = (2, 2, total0, Z, X)
    own, first, second, keep0, gain = call(
        functools.partial(level0_kernel, rows),
        [(2, OWN, Z, X), strip, strip, (8, 2, total0, Z, X), (9, Z, X)],
        [(6, 2, total0, Z, X), pair0, pair0, pair0],
        main,
        *y_packets,
        *own_x,
        *corner_x,
        spread,
    )
    (coef1,) = call(
        functools.partial(coarse1_kernel, rows),
        [(3, 2, SIZE1, Z, X)],
        [(2, 2 * GROUPS1, Z, X)],
        coarse,
        *y_packets,
        *own_x,
        *corner_x,
        gain,
    )
    b_packets = exchange(first, second, "gy")

    one, two, up = (2, SIZE1, Z, X), (2, SIZE2, Z, X), (2, SIZE_UP, Z, X)
    packet, keep1 = call(
        level1_kernel, [(2, Z, X), (2, *one)], [one, one], own, *b_packets, coef1, gain
    )
    near = exchange(packet, packet, "gy")
    far = (swap_far(packet, "gy", 1), swap_far(packet, "gy", -1))
    (coef2,) = call(
        functools.partial(coarse2_kernel, rows),
        [(2, 2, SIZE2, Z, X)],
        [],
        coarse,
        *y_packets,
        *own_x,
        *corner_x,
        *b_packets,
    )

    (out,) = call(
        rest_kernel,
        [(2 * Z * rows, X)],
        [one, two, two, two, two, up, up, pair0, pair0, pair0],
        packet,
        *near,
        *far,
        gain,
        coef1,
        coef2,
        keep0,
        keep1,
        *b_packets,
    )
    return out.reshape(2, Z, rows, X)


def solution(mesh):
    placed = (
        P(None, None, "gy", "gx"),
        P(None, None, "gy", "gx"),
        P(None, "gy", "gx"),
        P(None, "gy", "gx"),
    )
    return jax.shard_map(
        body, mesh=mesh, in_specs=placed, out_specs=P(None, None, "gy", "gx"), check_vma=False
    )
```

```python
import functools

import jax
import jax.numpy as jnp
from jax import lax
from jax.experimental import pallas as pl
from jax.experimental.pallas import tpu as pltpu
from jax.sharding import PartitionSpec as P

DIFF = (40.0, 20.0)
INV_STEP = 2.0
LOWER = 0.25

_CENTRE = (1.0 + LOWER) / 2.0
_HALF = (1.0 - LOWER) / 2.0
_SIGMA = _CENTRE / _HALF
_RHO0 = 1.0 / _SIGMA
_RHO1 = 1.0 / (2.0 * _SIGMA - _RHO0)
_RHO2 = 1.0 / (2.0 * _SIGMA - _RHO1)

Z = 8
X = 128
HALO0 = 4
HALOS = (4, 4, 3, 3, 3, 3)
STARTS = tuple(sum(HALOS[:i]) for i in range(6))
FIELDS1 = sum(HALOS)
FIELDS2 = FIELDS1 + 8
PACKET = FIELDS2 + 1
WIDE = 42
PER = X // WIDE
EDGE = 3
CHUNK = 4

LO1, HI1 = -4, 8
LO2, HI2 = -2, 3
LO_UP, HI_UP = -3, 7
SIZE1, SIZE2, SIZE_UP = HI1 - LO1 + 2, HI2 - LO2 + 2, HI_UP - LO_UP + 2
OWN = 4


def lane_of():
    return lax.broadcasted_iota(jnp.int32, (1, Z, X), 2)


def sub_of():
    return lax.broadcasted_iota(jnp.int32, (1, Z, X), 1)


def roll_x(tile, shift):
    shift = shift % X
    return pltpu.roll(tile, shift, 2) if shift else tile


def roll_z(tile, shift):
    shift = shift % Z
    return pltpu.roll(tile, shift, 1) if shift else tile


def rows_loop(lo, hi, body, step=CHUNK):
    full = (hi - lo) // step
    if full == 1:
        body(lo, step)
    elif full > 1:

        def trip(i, carry):
            body(lo + i * step, step)
            return carry

        lax.fori_loop(0, full, trip, 0)
    rest = hi - lo - full * step
    if rest:
        body(hi - rest, rest)


def neighbour_sums(read, r, n, k):
    lane = lane_of()
    low, high = lane < k, lane >= X - k
    centre = [read(t, r, n) for t in (0, 1)]
    right = [roll_x(c, k) for c in centre]
    left = [roll_x(c, -k) for c in centre]
    sums = []
    for t in (0, 1):
        c = centre[t]
        along_x = jnp.where(low, right[1 - t], right[t]) + jnp.where(high, left[1 - t], left[t])
        along_y = read(t, r - 1, n) + read(t, r + 1, n)
        along_z = 2.0 * roll_z(c, k) if 2 * k == Z else roll_z(c, k) + roll_z(c, -k)
        sums.append(along_x + along_y + along_z)
    return centre, sums


def jacobian(u, v, f, k, level):
    scale = 0.25**level
    product = u * v
    squared = v * v
    first = INV_STEP + squared + f + 6.0 * DIFF[0] * scale
    second = INV_STEP + f + k - 2.0 * product + 6.0 * DIFF[1] * scale
    return 2.0 * product, squared, 1.0 / first, 1.0 / second, first, second


def cheb_step(level, keep, source, target, d, r, n, carry, gain):
    scale = 0.25**level
    k = 1 << level
    u, nb_u = neighbour_sums(lambda t, a, m: source[0, t, pl.ds(a, m)], r, n, k)
    v, nb_v = neighbour_sums(lambda t, a, m: source[1, t, pl.ds(a, m)], r, n, k)
    rows = pl.ds(r, n)
    for t in (0, 1):
        cross, squared, inv_u, inv_v = (keep[i, t, rows] for i in range(4))
        res_u = inv_u * (keep[4, t, rows] - cross * v[t] + DIFF[0] * scale * nb_u[t]) - u[t]
        res_v = inv_v * (keep[5, t, rows] + squared * u[t] + DIFF[1] * scale * nb_v[t]) - v[t]
        du, dv = gain * res_u, gain * res_v
        if carry is not None:
            du = du + carry * d[0, t, rows]
            dv = dv + carry * d[1, t, rows]
        d[0, t, rows] = du
        d[1, t, rows] = dv
        target[0, t, rows] = u[t] + du
        target[1, t, rows] = v[t] + dv


def residual(level, keep, diag, source, r, n):
    scale = 0.25**level
    k = 1 << level
    u, nb_u = neighbour_sums(lambda t, a, m: source[0, t, pl.ds(a, m)], r, n, k)
    v, nb_v = neighbour_sums(lambda t, a, m: source[1, t, pl.ds(a, m)], r, n, k)
    rows = pl.ds(r, n)
    first, second = [], []
    for t in (0, 1):
        first.append(
            keep[4, t, rows] - diag[0, t, rows] * u[t] - keep[0, t, rows] * v[t] + DIFF[0] * scale * nb_u[t]
        )
        second.append(
            keep[5, t, rows] - diag[1, t, rows] * v[t] + keep[1, t, rows] * u[t] + DIFF[1] * scale * nb_v[t]
        )
    return first, second


CARRY1 = _RHO1 * _RHO0
CARRY2 = _RHO2 * _RHO1


def write_gains(spread, out):
    lane = lax.broadcasted_iota(jnp.int32, (1, X), 1)
    for level in range(3):
        top = jnp.max(jnp.where(lane == level, spread, 0.0), axis=1, keepdims=True)
        tau = 1.0 / (1.0 + jnp.broadcast_to(top, (Z, X)))
        for i, factor in enumerate((1.0 / _CENTRE, 2.0 * _RHO1 / _HALF, 2.0 * _RHO2 / _HALF)):
            out[3 * level + i] = factor * tau


def pair_rows(value):
    n = value.shape[0] // 2
    pairs = value.reshape(n, 2, Z, X)
    return pairs[:, 0] + pairs[:, 1]


def restrict_01(first, second):
    lane, sub = lane_of(), sub_of()
    across = []
    for value in (first, second):
        a, b = value[0:1], value[1:2]
        across.append(jnp.where((lane & 1) == 0, a + roll_x(a, -1), b + roll_x(b, 1)))
    a, b = across
    return 0.125 * jnp.where((sub & 1) == 0, a + roll_z(a, -1), b + roll_z(b, 1))


def restrict_12(groups):
    lane, sub = lane_of(), sub_of()
    out = None
    for p, value in enumerate(groups):
        value = value + roll_x(value, 1 if p & 1 else -1)
        value = value + roll_x(value, 2 if p & 2 else -2)
        out = value if out is None else jnp.where((lane & 3) == p, value, out)
    return 0.125 * (out + jnp.where((sub & 2) == 0, roll_z(out, -2), roll_z(out, 2)))


def spread_x(tile, k, phase):
    return jnp.where((lane_of() & k) == phase, tile, roll_x(tile, -k if phase else k))


def packed_jacobian(uv, fk, level):
    scale = 0.25**level
    even = (sub_of() & 1) == 0
    u, v = jnp.where(even, uv, roll_z(uv, 1)), jnp.where(even, roll_z(uv, -1), uv)
    f, k = jnp.where(even, fk, roll_z(fk, 1)), jnp.where(even, roll_z(fk, -1), fk)
    product, squared = u * v, v * v
    diag = jnp.where(
        even,
        INV_STEP + squared + f + 6.0 * DIFF[0] * scale,
        INV_STEP + f + k - 2.0 * product + 6.0 * DIFF[1] * scale,
    )
    return 1.0 / diag, jnp.where(even, -2.0 * product, squared), diag


def packed_spread(uv, fk, level):
    scale = 0.25**level
    even = (sub_of() & 1) == 0
    inverse, other, _ = packed_jacobian(uv, fk, level)
    return jnp.where(even, 6.0 * DIFF[0] * scale - other, 6.0 * DIFF[1] * scale + other) * inverse


def packed_terms(source, g, n, level):
    k = 1 << level
    lane, sub = lane_of(), sub_of()
    even = (sub & 1) == 0
    first, last = (lane & (k - 1)) == 0, (lane & (k - 1)) == k - 1
    low, high = lane < k, lane >= X - k
    diff = jnp.where(even, DIFF[0] * 0.25**level, DIFF[1] * 0.25**level)
    wide = [source[t, pl.ds(g - 1, n + 2)] for t in (0, 1)]
    centre = [w[1 : n + 1] for w in wide]
    right = [roll_x(c, k) for c in centre]
    left = [roll_x(c, -k) for c in centre]
    out = []
    for t in (0, 1):
        c, w = centre[t], wide[t]
        total = jnp.where(low, right[1 - t], right[t]) + jnp.where(high, left[1 - t], left[t])
        if k == 2:
            ahead, back = roll_x(w, 1), roll_x(w, -1)
            total = total + jnp.where(first, back[0:n], ahead[1 : n + 1])
            total = total + jnp.where(last, ahead[2 : n + 2], back[1 : n + 1])
            total = total + roll_z(c, 2) + roll_z(c, -2)
        else:
            total = total + jnp.where(first, roll_x(w[0:n], -(k - 1)), roll_x(c, 1))
            total = total + jnp.where(last, roll_x(w[2 : n + 2], k - 1), roll_x(c, -1))
            total = total + 2.0 * roll_z(c, 4)
        other = jnp.where(even, roll_z(c, -1), roll_z(c, 1))
        out.append((c, other, diff * total))
    return out


def packed_first(coef, shift, b, target, d, g, n, gain):
    for t in (0, 1):
        value = gain * coef[0, t, pl.ds(g + shift, n)] * b[t, pl.ds(g + shift, n)]
        d[t, pl.ds(g, n)] = value
        target[t, pl.ds(g, n)] = value


def packed_step(level, coef, shift, b, source, target, d, g, n, carry, gain):
    for t, (c, other, spread) in enumerate(packed_terms(source, g, n, level)):
        at = pl.ds(g + shift, n)
        res = coef[0, t, at] * (b[t, at] + coef[1, t, at] * other + spread) - c
        delta = gain * res
        if carry is not None:
            delta = delta + carry * d[t, pl.ds(g, n)]
        d[t, pl.ds(g, n)] = delta
        target[t, pl.ds(g, n)] = c + delta


def plane(ref, f, y, rows):
    return ref[pl.ds(f * Z * rows + y, Z, stride=rows), :]


def is_even(axis):
    return lax.rem(lax.axis_index(axis), 2) == 0


def prev_of(even, first, second, at):
    return jnp.where(even, first[at], second[at])


def next_of(even, first, second, at):
    return jnp.where(even, second[at], first[at])


def first_kernel(rows, state, previous, feed, kill, first, second, main, coarse, *scratch):
    sources, sems = scratch[:4], scratch[4]
    copies = [
        pltpu.make_async_copy(ref, held, sems.at[i])
        for i, (ref, held) in enumerate(zip((state, previous, feed, kill), sources))
    ]
    for copy in copies:
        copy.start()
    for copy in copies:
        copy.wait()
    even = is_even("gy")
    state, previous, feed, kill = sources
    fields = [(state, 0), (state, 1), (previous, 0), (previous, 1), (feed, 0), (kill, 0)]
    for i, (ref, f) in enumerate(fields):
        for y in range(rows):
            main[i, y] = plane(ref, f, y, rows)
        top, bottom = main[i, 0 : HALOS[i]], main[i, rows - HALOS[i] : rows]
        at = slice(STARTS[i], STARTS[i] + HALOS[i])
        first[at] = jnp.where(even, top, bottom)
        second[at] = jnp.where(even, bottom, top)
    u, v, f, k = (main[i] for i in (0, 1, 4, 5))
    sums = [pair_rows(value) for value in (u, v, f, k)]
    pairs = []
    for p in (0, 1):
        values = [
            restrict_01(sums[2 * p][2 * g : 2 * g + 2], sums[2 * p + 1][2 * g : 2 * g + 2]) for g in range(OWN)
        ]
        pairs.append(jnp.concatenate(values, axis=0))
        coarse[p * OWN : (p + 1) * OWN] = pairs[p]
        for ref in (first, second):
            ref[FIELDS1 + p * OWN : FIELDS1 + (p + 1) * OWN] = pairs[p]

    uv, fk = (restrict_12([pair[j : j + 1] for j in range(OWN)]) for pair in pairs)
    both = jnp.where((sub_of() & 2) == 0, uv, fk)
    coarse[2 * OWN : 2 * OWN + 1] = both
    for ref in (first, second):
        ref[FIELDS2 : FIELDS2 + 1] = both


def split_fields2(both):
    low = (sub_of() & 2) == 0
    return jnp.where(low, both, roll_z(both, 2)), jnp.where(low, roll_z(both, -2), both)


def spread_kernel(main, coarse, out):
    lane = lax.broadcasted_iota(jnp.int32, (1, X), 1)
    u, v, f, k = (main[i] for i in (0, 1, 4, 5))
    cross, squared, inv_u, inv_v, _, _ = jacobian(u, v, f, k, 0)
    tops = [jnp.max(jnp.maximum((6.0 * DIFF[0] + cross) * inv_u, (6.0 * DIFF[1] + squared) * inv_v), axis=0)]
    tops.append(jnp.max(packed_spread(coarse[0:OWN], coarse[OWN : 2 * OWN], 1), axis=0))
    tops.append(packed_spread(*split_fields2(coarse[2 * OWN : 2 * OWN + 1]), 2)[0])
    result = jnp.zeros((1, X), jnp.float32)
    for level, top in enumerate(tops):
        top = jnp.max(jnp.max(top, axis=0, keepdims=True), axis=1, keepdims=True)
        result = jnp.where(lane == level, jnp.broadcast_to(top, (1, X)), result)
    out[...] = jnp.broadcast_to(result[None], out.shape)


GROUPS1 = HI1 - LO1
GROUPS2 = HI2 - LO2


def tiles_for(entries):
    return -(-entries // PER)


def pack_edges(entries, even, first, second):
    lane = lane_of()
    share = first.shape[0]
    left, right = None, None
    for j in range(PER):
        part = entries[j * share : (j + 1) * share]
        a, b = roll_x(part, WIDE * j), roll_x(part, WIDE + WIDE * j)
        left = a if left is None else jnp.where(lane >= WIDE * j, a, left)
        right = b if right is None else jnp.where(lane >= WIDE * j, b, right)
    first[...] = jnp.where(even, left, right)
    second[...] = jnp.where(even, right, left)


def halo_tiles(even, packets, lo, hi):
    first, second = packets
    share = first.shape[0]
    lane = lane_of()
    out = []
    for j in range(PER):
        a, b = max(lo, j * share), min(hi, (j + 1) * share)
        if a < b:
            strip = slice(a - j * share, b - j * share)
            left, right = prev_of(even, first, second, strip), next_of(even, first, second, strip)
            value = jnp.where(lane < X // 2, roll_x(right, -WIDE * j), roll_x(left, X - WIDE - WIDE * j))
            out.append((a - lo, b - lo, value))
    return out


def pack_own_kernel(rows, main, coarse, first, second, held):
    for i in range(6):
        held[i * rows : (i + 1) * rows] = main[i]
    held[6 * rows : 6 * rows + 2 * OWN + 1] = coarse[...]
    pack_edges(held, is_even("gx"), first, second)


def pack_corner_kernel(y_first, y_second, first, second, held):
    even = is_even("gy")
    every = slice(0, PACKET)
    held[0:PACKET] = prev_of(even, y_first, y_second, every)
    held[PACKET : 2 * PACKET] = next_of(even, y_first, y_second, every)
    pack_edges(held, is_even("gx"), first, second)


EDGES = 2 * OWN
FAR = EDGES + 2 * EDGE + 1


def level0_kernel(
    rows, main, y_first, y_second, own_a, own_b, corner_a, corner_b, gathered, own, first, second, keep, gain_out, fields, other, d, diag
):
    even, even_x = is_even("gy"), is_even("gx")
    total = rows + 2 * HALO0
    own_x, corner_x = (own_a, own_b), (corner_a, corner_b)
    top = jnp.max(gathered[...], axis=0)
    write_gains(top[0:1], gain_out)
    g0, g1, g2 = (gain_out[i] for i in range(3))
    for i, halo in enumerate(HALOS):
        strip = slice(STARTS[i], STARTS[i] + halo)
        skip = HALO0 - halo
        fields[i, 0, skip:HALO0] = prev_of(even, y_first, y_second, strip)
        fields[i, 0, HALO0 : HALO0 + rows] = main[i]
        fields[i, 0, HALO0 + rows : total - skip] = next_of(even, y_first, y_second, strip)
        for packets, lo, n, at in (
            (corner_x, STARTS[i], halo, skip),
            (own_x, i * rows, rows, HALO0),
            (corner_x, PACKET + STARTS[i], halo, HALO0 + rows),
        ):
            for a, b, value in halo_tiles(even_x, packets, lo, lo + n):
                fields[i, 1, at + a : at + b] = value
    here = keep.at[6:8]

    def setup(r, n):
        at = pl.ds(r, n)
        u, nb_u = neighbour_sums(lambda t, a, m: fields[0, t, pl.ds(a, m)], r, n, 1)
        v, nb_v = neighbour_sums(lambda t, a, m: fields[1, t, pl.ds(a, m)], r, n, 1)
        for t in (0, 1):
            f, k = fields[4, t, at], fields[5, t, at]
            cross, squared, inv_u, inv_v, first, second = jacobian(u[t], v[t], f, k, 0)
            react = u[t] * squared
            b_u = (
                DIFF[0] * (nb_u[t] - 6.0 * u[t])
                - INV_STEP * (u[t] - fields[2, t, at])
                - react
                + f * (1.0 - u[t])
            )
            b_v = (
                DIFF[1] * (nb_v[t] - 6.0 * v[t]) - INV_STEP * (v[t] - fields[3, t, at]) + react - (f + k) * v[t]
            )
            for i, value in enumerate((cross, squared, inv_u, inv_v, b_u, b_v)):
                keep[i, t, at] = value
            diag[0, t, at] = first
            diag[1, t, at] = second
            for i, value in enumerate((g0 * inv_u * b_u, g0 * inv_v * b_v)):
                d[i, t, at] = value
                keep[6 + i, t, at] = value

    rows_loop(1, total - 1, setup)
    rows_loop(2, total - 2, lambda r, n: cheb_step(0, keep, here, other, d, r, n, CARRY1, g1))
    rows_loop(3, total - 3, lambda r, n: cheb_step(0, keep, other, here, d, r, n, CARRY2, g2))

    def down(r, n):
        res = residual(0, keep, diag, here, r, n)
        out = (r - HALO0) // 4
        for t in (0, 1):
            value = restrict_01(pair_rows(res[0][t]), pair_rows(res[1][t]))
            own[t, pl.ds(out, 1)] = value
            if t == 0:
                first[pl.ds(out, 1)] = value
                second[pl.ds(out, 1)] = value

    rows_loop(HALO0, HALO0 + rows, down, 4)

    lane = lane_of()
    edges = []
    for start in (HALO0, HALO0 + rows - EDGE):
        halo = None
        for i in (0, 1):
            for j in range(EDGE):
                at = i * EDGE + j
                value = roll_x(keep[6 + i, 1, start + j : start + j + 1], 4 + 8 * at)
                halo = value if halo is None else jnp.where((lane >> 3) == at, value, halo)
        edges.append([keep[6, 0, start : start + EDGE], keep[7, 0, start : start + EDGE], halo])
    top, bottom = (jnp.concatenate(parts, axis=0) for parts in edges)
    for ref in (first, second):
        ref[OWN : 2 * OWN] = own[1]
    strip = slice(FIELDS2, FIELDS2 + 1)
    for t in (0, 1):
        if t == 0:
            before, after = prev_of(even, y_first, y_second, strip), next_of(even, y_first, y_second, strip)
        else:
            before, after = (
                halo_tiles(even_x, corner_x, at + FIELDS2, at + FIELDS2 + 1)[0][2] for at in (0, PACKET)
            )
        first[FAR + t : FAR + t + 1] = jnp.where(even, after, before)
        second[FAR + t : FAR + t + 1] = jnp.where(even, before, after)
    first[EDGES : EDGES + 2 * EDGE + 1] = jnp.where(even, top, bottom)
    second[EDGES : EDGES + 2 * EDGE + 1] = jnp.where(even, bottom, top)


def coarse1_kernel(
    rows, coarse, y_first, y_second, own_a, own_b, corner_a, corner_b, gain, coef, fields
):
    del gain
    even, even_x = is_even("gy"), is_even("gx")
    own_x, corner_x = (own_a, own_b), (corner_a, corner_b)
    for p in (0, 1):
        to = p * GROUPS1
        strip = slice(FIELDS1 + p * OWN, FIELDS1 + (p + 1) * OWN)
        fields[0, to : to + OWN] = prev_of(even, y_first, y_second, strip)
        fields[0, to + OWN : to + 2 * OWN] = coarse[p * OWN : (p + 1) * OWN]
        fields[0, to + 2 * OWN : to + 3 * OWN] = next_of(even, y_first, y_second, strip)
        for part, (packets, lo) in enumerate(
            ((corner_x, FIELDS1), (own_x, 6 * rows), (corner_x, PACKET + FIELDS1))
        ):
            lo += p * OWN
            for a, b, value in halo_tiles(even_x, packets, lo, lo + OWN):
                fields[1, to + part * OWN + a : to + part * OWN + b] = value
    for t in (0, 1):
        for i, value in enumerate(packed_jacobian(fields[t, 0:GROUPS1], fields[t, GROUPS1 : 2 * GROUPS1], 1)):
            coef[i, t, 1 : SIZE1 - 1] = value


def coarse2_kernel(
    rows, coarse, y_first, y_second, own_a, own_b, corner_a, corner_b, b_first, b_second, coef
):
    even, even_x = is_even("gy"), is_even("gx")
    own_x, corner_x = (own_a, own_b), (corner_a, corner_b)
    near = slice(FIELDS2, FIELDS2 + 1)
    for t in (0, 1):
        far = slice(FAR + t, FAR + t + 1)
        if t == 0:
            middle = [
                prev_of(even, y_first, y_second, near),
                coarse[2 * OWN : 2 * OWN + 1],
                next_of(even, y_first, y_second, near),
            ]
        else:
            middle = [
                halo_tiles(even_x, packets, lo, lo + 1)[0][2]
                for packets, lo in ((corner_x, FIELDS2), (own_x, 6 * rows + 2 * OWN), (corner_x, PACKET + FIELDS2))
            ]
        parts = [prev_of(even, b_first, b_second, far), *middle, next_of(even, b_first, b_second, far)]
        inverse, other, _ = packed_jacobian(*split_fields2(jnp.concatenate(parts, axis=0)), 2)
        coef[0, t, 1 : SIZE2 - 1] = inverse
        coef[1, t, 1 : SIZE2 - 1] = other


def level1_kernel(own, first, second, coef1, gain, packet, keep, y1, d1):
    b1, x1 = keep.at[0], keep.at[1]
    even = is_even("gy")
    for t in (0, 1):
        b1[t, 1 + OWN : 1 + 2 * OWN] = own[t]
        strip = slice(t * OWN, (t + 1) * OWN)
        b1[t, 1 : 1 + OWN] = prev_of(even, first, second, strip)
        b1[t, 1 + 2 * OWN : 1 + 3 * OWN] = next_of(even, first, second, strip)
    g0, g1, g2 = (gain[3 + i] for i in range(3))
    n = GROUPS1
    packed_first(coef1, 0, b1, x1, d1, 1, n, g0)
    packed_step(1, coef1, 0, b1, x1, y1, d1, 1, n, CARRY1, g1)
    packed_step(1, coef1, 0, b1, y1, x1, d1, 1, n, CARRY2, g2)
    here = pl.ds(1 + OWN, OWN)
    for t, (c, other, spread) in enumerate(packed_terms(x1, 1 + OWN, OWN, 1)):
        res = b1[t, here] - coef1[2, t, here] * c + coef1[1, t, here] * other + spread
        value = restrict_12([res[j : j + 1] for j in range(OWN)])
        for c in range(packet.shape[0] // 2):
            packet[2 * c + t : 2 * c + t + 1] = value


def rest_kernel(
    count, gathered, gain, coef1, coef2, keep0, keep1, first, second, out, d1, b2, x2, y2, d2, xu, yu, x0, y0, d0
):
    rows = out.shape[0] // (2 * Z)
    even = (sub_of() & 1) == 0
    b1, x1 = keep1.at[0], keep1.at[1]

    even_y, me = is_even("gy"), lax.axis_index("gy")
    for q in range(GROUPS2):
        at = lax.rem(me + LO2 + q + 4 * count, count) * 2
        for t in (0, 1):
            b2[t, 1 + q : 2 + q] = gathered[pl.ds(at + t, 1)]

    n = HI2 - LO2
    g0, g1, g2 = (gain[6 + i] for i in range(3))
    packed_first(coef2, 0, b2, x2, d2, 1, n, g0)
    packed_step(2, coef2, 0, b2, x2, y2, d2, 1, n, CARRY1, g1)
    packed_step(2, coef2, 0, b2, y2, x2, d2, 1, n, CARRY2, g2)
    packed_step(2, coef2, 0, b2, x2, y2, d2, 1, n, None, g0)
    packed_step(2, coef2, 0, b2, y2, x2, d2, 1, n, CARRY1, g1)
    packed_step(2, coef2, 0, b2, x2, y2, d2, 1, n, CARRY2, g2)

    g0, g1, g2 = (gain[3 + i] for i in range(3))
    shift = LO_UP - LO1
    for t in (0, 1):
        for g in range(LO_UP, HI_UP):
            p = g % 4
            value = y2[t, g // 4 - LO2 + 1 : g // 4 - LO2 + 2]
            value = spread_x(spread_x(value, 1, p & 1), 2, p & 2)
            at = g - LO_UP + 1
            xu[t, at : at + 1] = x1[t, at + shift : at + shift + 1] + value
    n = HI_UP - LO_UP
    packed_step(1, coef1, shift, b1, xu, yu, d1, 1, n, None, g0)
    packed_step(1, coef1, shift, b1, yu, xu, d1, 1, n, CARRY1, g1)
    packed_step(1, coef1, shift, b1, xu, yu, d1, 1, n, CARRY2, g2)

    g0, g1, g2 = (gain[i] for i in range(3))
    last = EDGES + 2 * EDGE
    for i in (0, 1):
        for at, take in ((HALO0 - EDGE, prev_of), (HALO0 + rows, next_of)):
            strip = slice(EDGES + i * EDGE, EDGES + (i + 1) * EDGE)
            x0[i, 0, at : at + EDGE] = take(even_y, first, second, strip)
            sides = take(even_y, first, second, slice(last, last + 1))
            for j in range(EDGE):
                x0[i, 1, at + j : at + j + 1] = roll_x(sides, -(4 + 8 * (i * EDGE + j)))
        for t in (0, 1):
            x0[i, t, HALO0 : HALO0 + rows] = keep0[6 + i, t, HALO0 : HALO0 + rows]
    for t in (0, 1):
        for row in range(-2, rows // 2 + 2):
            at = row // 2 - LO_UP + 1
            value = spread_x(yu[t, at : at + 1], 1, row & 1)
            for i, fine in enumerate((jnp.where(even, value, roll_z(value, 1)), jnp.where(even, roll_z(value, -1), value))):
                for y in (2 * row, 2 * row + 1):
                    if -EDGE <= y < rows + EDGE:
                        x0[i, t, y + HALO0 : y + HALO0 + 1] = x0[i, t, y + HALO0 : y + HALO0 + 1] + fine
    total = rows + 2 * HALO0
    rows_loop(2, total - 2, lambda r, n: cheb_step(0, keep0, x0, y0, d0, r, n, None, g0))
    rows_loop(3, total - 3, lambda r, n: cheb_step(0, keep0, y0, x0, d0, r, n, CARRY1, g1))
    rows_loop(4, total - 4, lambda r, n: cheb_step(0, keep0, x0, y0, d0, r, n, CARRY2, g2))
    for i in (0, 1):
        for y in range(rows):
            out[pl.ds(i * Z * rows + y, Z, stride=rows), :] = y0[i, 0, HALO0 + y]


def call(kernel, out_shapes, scratch, *args, space=pltpu.VMEM):
    out = [jax.ShapeDtypeStruct(shape, jnp.float32) for shape in out_shapes]
    return pl.pallas_call(
        kernel,
        out_shape=out,
        in_specs=[pl.BlockSpec(memory_space=space)] * len(args),
        out_specs=[pl.BlockSpec(memory_space=pltpu.VMEM)] * len(out),
        scratch_shapes=[pltpu.VMEM(s, jnp.float32) if isinstance(s, tuple) else s for s in scratch],
        compiler_params=pltpu.CompilerParams(vmem_limit_bytes=24 * 2**20),
    )(*args)


def swap(value, axis, step):
    count = lax.axis_size(axis)
    assert count % 2 == 0
    pairs = [(i, (i + step) % count) for i in range(0, count, 2)]
    return lax.ppermute(value, axis, pairs + [(j, i) for i, j in pairs])


def exchange(first, second, axis):
    return swap(first, axis, -1), swap(second, axis, 1)


def body(state, previous, feed, kill):
    _, depth, rows, cols = state.shape
    assert depth == Z and cols == X and rows == 4 * OWN
    across, count = lax.axis_size("gx"), lax.axis_size("gy")
    total0 = rows + 2 * HALO0
    state = state.reshape(2 * Z * rows, X)
    previous = previous.reshape(2 * Z * rows, X)
    feed = feed.reshape(Z * rows, X)
    kill = kill.reshape(Z * rows, X)
    inputs = (state, previous, feed, kill)

    strip = (FIELDS2 + 1, Z, X)
    first, second, main, coarse = call(
        functools.partial(first_kernel, rows),
        [strip, strip, (6, rows, Z, X), (2 * OWN + 1, Z, X)],
        [*(a.shape for a in inputs), pltpu.SemaphoreType.DMA((4,))],
        *(pltpu.with_memory_space_constraint(a, pltpu.HBM) for a in inputs),
        space=pltpu.HBM,
    )
    y_packets = exchange(first, second, "gy")
    (spread,) = call(spread_kernel, [(across * count, 6, X)], [], main, coarse)
    spread = lax.all_to_all(spread, ("gx", "gy"), 0, 0, tiled=True)

    tiles = tiles_for(6 * rows + 2 * OWN + 1)
    own_x = exchange(
        *call(
            functools.partial(pack_own_kernel, rows),
            [(tiles, Z, X), (tiles, Z, X)],
            [(PER * tiles, Z, X)],
            main,
            coarse,
        ),
        "gx",
    )
    tiles = tiles_for(2 * PACKET)
    corner_x = exchange(
        *call(pack_corner_kernel, [(tiles, Z, X), (tiles, Z, X)], [(PER * tiles, Z, X)], *y_packets), "gx"
    )

    strip = (FAR + 2, Z, X)
    pair0 = (2, 2, total0, Z, X)
    own, first, second, keep0, gain = call(
        functools.partial(level0_kernel, rows),
        [(2, OWN, Z, X), strip, strip, (8, 2, total0, Z, X), (9, Z, X)],
        [(6, 2, total0, Z, X), pair0, pair0, pair0],
        main,
        *y_packets,
        *own_x,
        *corner_x,
        spread,
    )
    (coef1,) = call(
        functools.partial(coarse1_kernel, rows),
        [(3, 2, SIZE1, Z, X)],
        [(2, 2 * GROUPS1, Z, X)],
        coarse,
        *y_packets,
        *own_x,
        *corner_x,
        gain,
    )
    b_packets = exchange(first, second, "gy")

    one, two, up = (2, SIZE1, Z, X), (2, SIZE2, Z, X), (2, SIZE_UP, Z, X)
    packet, keep1 = call(
        level1_kernel, [(2 * count, Z, X), (2, *one)], [one, one], own, *b_packets, coef1, gain
    )
    gathered = lax.all_to_all(packet, "gy", 0, 0, tiled=True)
    (coef2,) = call(
        functools.partial(coarse2_kernel, rows),
        [(2, 2, SIZE2, Z, X)],
        [],
        coarse,
        *y_packets,
        *own_x,
        *corner_x,
        *b_packets,
    )

    (out,) = call(
        functools.partial(rest_kernel, count),
        [(2 * Z * rows, X)],
        [one, two, two, two, two, up, up, pair0, pair0, pair0],
        gathered,
        gain,
        coef1,
        coef2,
        keep0,
        keep1,
        *b_packets,
    )
    return out.reshape(2, Z, rows, X)


def solution(mesh):
    placed = (
        P(None, None, "gy", "gx"),
        P(None, None, "gy", "gx"),
        P(None, "gy", "gx"),
        P(None, "gy", "gx"),
    )
    return jax.shard_map(
        body, mesh=mesh, in_specs=placed, out_specs=P(None, None, "gy", "gx"), check_vma=False
    )
```

```python
import functools

import jax
import jax.numpy as jnp
from jax import lax
from jax.experimental import pallas as pl
from jax.experimental.pallas import tpu as pltpu
from jax.sharding import PartitionSpec as P

DIFF = (40.0, 20.0)
INV_STEP = 2.0
LOWER = 0.25

_CENTRE = (1.0 + LOWER) / 2.0
_HALF = (1.0 - LOWER) / 2.0
_SIGMA = _CENTRE / _HALF
_RHO0 = 1.0 / _SIGMA
_RHO1 = 1.0 / (2.0 * _SIGMA - _RHO0)
_RHO2 = 1.0 / (2.0 * _SIGMA - _RHO1)

Z = 8
X = 128
HALO0 = 4
HALOS = (4, 4, 3, 3, 3, 3)
STARTS = tuple(sum(HALOS[:i]) for i in range(6))
FIELDS1 = sum(HALOS)
FIELDS2 = FIELDS1 + 8
PACKET = FIELDS2 + 1
WIDE = 42
PER = X // WIDE
EDGE = 3

LO1, HI1 = -4, 8
LO2, HI2 = -2, 3
LO_UP, HI_UP = -3, 7
SIZE1, SIZE2, SIZE_UP = HI1 - LO1 + 2, HI2 - LO2 + 2, HI_UP - LO_UP + 2
OWN = 4


def lane_of():
    return lax.broadcasted_iota(jnp.int32, (1, Z, X), 2)


def sub_of():
    return lax.broadcasted_iota(jnp.int32, (1, Z, X), 1)


def roll_x(tile, shift):
    shift = shift % X
    return pltpu.roll(tile, shift, 2) if shift else tile


def roll_z(tile, shift):
    shift = shift % Z
    return pltpu.roll(tile, shift, 1) if shift else tile


def rows_loop(lo, hi, body, step=None):
    step = step or (hi - lo) // 2
    full = (hi - lo) // step
    if full == 1:
        body(lo, step)
    elif full > 1:

        def trip(i, carry):
            body(lo + i * step, step)
            return carry

        lax.fori_loop(0, full, trip, 0)
    rest = hi - lo - full * step
    if rest:
        body(hi - rest, rest)


def neighbour_sums(read, r, n, k):
    lane = lane_of()
    low, high = lane < k, lane >= X - k
    centre = [read(t, r, n) for t in (0, 1)]
    right = [roll_x(c, k) for c in centre]
    left = [roll_x(c, -k) for c in centre]
    sums = []
    for t in (0, 1):
        c = centre[t]
        along_x = jnp.where(low, right[1 - t], right[t]) + jnp.where(high, left[1 - t], left[t])
        along_y = read(t, r - 1, n) + read(t, r + 1, n)
        along_z = 2.0 * roll_z(c, k) if 2 * k == Z else roll_z(c, k) + roll_z(c, -k)
        sums.append(along_x + along_y + along_z)
    return centre, sums


def jacobian(u, v, f, k, level):
    scale = 0.25**level
    product = u * v
    squared = v * v
    first = INV_STEP + squared + f + 6.0 * DIFF[0] * scale
    second = INV_STEP + f + k - 2.0 * product + 6.0 * DIFF[1] * scale
    return 2.0 * product, squared, 1.0 / first, 1.0 / second, first, second


def cheb_step(level, keep, source, target, d, r, n, carry, gain):
    scale = 0.25**level
    k = 1 << level
    u, nb_u = neighbour_sums(lambda t, a, m: source[0, t, pl.ds(a, m)], r, n, k)
    v, nb_v = neighbour_sums(lambda t, a, m: source[1, t, pl.ds(a, m)], r, n, k)
    rows = pl.ds(r, n)
    for t in (0, 1):
        cross, squared, inv_u, inv_v = (keep[i, t, rows] for i in range(4))
        res_u = inv_u * (keep[4, t, rows] - cross * v[t] + DIFF[0] * scale * nb_u[t]) - u[t]
        res_v = inv_v * (keep[5, t, rows] + squared * u[t] + DIFF[1] * scale * nb_v[t]) - v[t]
        du, dv = gain * res_u, gain * res_v
        if carry is not None:
            du = du + carry * d[0, t, rows]
            dv = dv + carry * d[1, t, rows]
        d[0, t, rows] = du
        d[1, t, rows] = dv
        target[0, t, rows] = u[t] + du
        target[1, t, rows] = v[t] + dv


def residual(level, keep, diag, source, r, n):
    scale = 0.25**level
    k = 1 << level
    u, nb_u = neighbour_sums(lambda t, a, m: source[0, t, pl.ds(a, m)], r, n, k)
    v, nb_v = neighbour_sums(lambda t, a, m: source[1, t, pl.ds(a, m)], r, n, k)
    rows = pl.ds(r, n)
    first, second = [], []
    for t in (0, 1):
        first.append(
            keep[4, t, rows] - diag[0, t, rows] * u[t] - keep[0, t, rows] * v[t] + DIFF[0] * scale * nb_u[t]
        )
        second.append(
            keep[5, t, rows] - diag[1, t, rows] * v[t] + keep[1, t, rows] * u[t] + DIFF[1] * scale * nb_v[t]
        )
    return first, second


CARRY1 = _RHO1 * _RHO0
CARRY2 = _RHO2 * _RHO1


def write_gains(spread, out):
    lane = lax.broadcasted_iota(jnp.int32, (1, X), 1)
    for level in range(3):
        top = jnp.max(jnp.where(lane == level, spread, 0.0), axis=1, keepdims=True)
        tau = 1.0 / (1.0 + jnp.broadcast_to(top, (Z, X)))
        for i, factor in enumerate((1.0 / _CENTRE, 2.0 * _RHO1 / _HALF, 2.0 * _RHO2 / _HALF)):
            out[3 * level + i] = factor * tau


def pair_rows(value):
    n = value.shape[0] // 2
    pairs = value.reshape(n, 2, Z, X)
    return pairs[:, 0] + pairs[:, 1]


def restrict_01(first, second):
    lane, sub = lane_of(), sub_of()
    across = []
    for value in (first, second):
        a, b = value[0:1], value[1:2]
        across.append(jnp.where((lane & 1) == 0, a + roll_x(a, -1), b + roll_x(b, 1)))
    a, b = across
    return 0.125 * jnp.where((sub & 1) == 0, a + roll_z(a, -1), b + roll_z(b, 1))


def restrict_12(groups):
    lane, sub = lane_of(), sub_of()
    out = None
    for p, value in enumerate(groups):
        value = value + roll_x(value, 1 if p & 1 else -1)
        value = value + roll_x(value, 2 if p & 2 else -2)
        out = value if out is None else jnp.where((lane & 3) == p, value, out)
    return 0.125 * (out + jnp.where((sub & 2) == 0, roll_z(out, -2), roll_z(out, 2)))


def spread_x(tile, k, phase):
    return jnp.where((lane_of() & k) == phase, tile, roll_x(tile, -k if phase else k))


def packed_jacobian(uv, fk, level):
    scale = 0.25**level
    even = (sub_of() & 1) == 0
    u, v = jnp.where(even, uv, roll_z(uv, 1)), jnp.where(even, roll_z(uv, -1), uv)
    f, k = jnp.where(even, fk, roll_z(fk, 1)), jnp.where(even, roll_z(fk, -1), fk)
    product, squared = u * v, v * v
    diag = jnp.where(
        even,
        INV_STEP + squared + f + 6.0 * DIFF[0] * scale,
        INV_STEP + f + k - 2.0 * product + 6.0 * DIFF[1] * scale,
    )
    return 1.0 / diag, jnp.where(even, -2.0 * product, squared), diag


def packed_spread(uv, fk, level):
    scale = 0.25**level
    even = (sub_of() & 1) == 0
    inverse, other, _ = packed_jacobian(uv, fk, level)
    return jnp.where(even, 6.0 * DIFF[0] * scale - other, 6.0 * DIFF[1] * scale + other) * inverse


def packed_terms(source, g, n, level):
    k = 1 << level
    lane, sub = lane_of(), sub_of()
    even = (sub & 1) == 0
    first, last = (lane & (k - 1)) == 0, (lane & (k - 1)) == k - 1
    low, high = lane < k, lane >= X - k
    diff = jnp.where(even, DIFF[0] * 0.25**level, DIFF[1] * 0.25**level)
    wide = [source[t, pl.ds(g - 1, n + 2)] for t in (0, 1)]
    centre = [w[1 : n + 1] for w in wide]
    right = [roll_x(c, k) for c in centre]
    left = [roll_x(c, -k) for c in centre]
    out = []
    for t in (0, 1):
        c, w = centre[t], wide[t]
        total = jnp.where(low, right[1 - t], right[t]) + jnp.where(high, left[1 - t], left[t])
        if k == 2:
            ahead, back = roll_x(w, 1), roll_x(w, -1)
            total = total + jnp.where(first, back[0:n], ahead[1 : n + 1])
            total = total + jnp.where(last, ahead[2 : n + 2], back[1 : n + 1])
            total = total + roll_z(c, 2) + roll_z(c, -2)
        else:
            total = total + jnp.where(first, roll_x(w[0:n], -(k - 1)), roll_x(c, 1))
            total = total + jnp.where(last, roll_x(w[2 : n + 2], k - 1), roll_x(c, -1))
            total = total + 2.0 * roll_z(c, 4)
        other = jnp.where(even, roll_z(c, -1), roll_z(c, 1))
        out.append((c, other, diff * total))
    return out


def packed_first(coef, shift, b, target, d, g, n, gain):
    for t in (0, 1):
        value = gain * coef[0, t, pl.ds(g + shift, n)] * b[t, pl.ds(g + shift, n)]
        d[t, pl.ds(g, n)] = value
        target[t, pl.ds(g, n)] = value


def packed_step(level, coef, shift, b, source, target, d, g, n, carry, gain):
    for t, (c, other, spread) in enumerate(packed_terms(source, g, n, level)):
        at = pl.ds(g + shift, n)
        res = coef[0, t, at] * (b[t, at] + coef[1, t, at] * other + spread) - c
        delta = gain * res
        if carry is not None:
            delta = delta + carry * d[t, pl.ds(g, n)]
        d[t, pl.ds(g, n)] = delta
        target[t, pl.ds(g, n)] = c + delta


def plane(ref, f, y, rows):
    return ref[pl.ds(f * Z * rows + y, Z, stride=rows), :]


def is_even(axis):
    return lax.rem(lax.axis_index(axis), 2) == 0


def prev_of(even, first, second, at):
    return jnp.where(even, first[at], second[at])


def next_of(even, first, second, at):
    return jnp.where(even, second[at], first[at])


def first_kernel(rows, state, previous, feed, kill, first, second, main, coarse, *scratch):
    sources, sems = scratch[:4], scratch[4]
    copies = [
        pltpu.make_async_copy(ref, held, sems.at[i])
        for i, (ref, held) in enumerate(zip((state, previous, feed, kill), sources))
    ]
    for copy in copies:
        copy.start()
    for copy in copies:
        copy.wait()
    even = is_even("gy")
    state, previous, feed, kill = sources
    fields = [(state, 0), (state, 1), (previous, 0), (previous, 1), (feed, 0), (kill, 0)]
    for i, (ref, f) in enumerate(fields):
        for y in range(rows):
            main[i, y] = plane(ref, f, y, rows)
        top, bottom = main[i, 0 : HALOS[i]], main[i, rows - HALOS[i] : rows]
        at = slice(STARTS[i], STARTS[i] + HALOS[i])
        first[at] = jnp.where(even, top, bottom)
        second[at] = jnp.where(even, bottom, top)
    u, v, f, k = (main[i] for i in (0, 1, 4, 5))
    sums = [pair_rows(value) for value in (u, v, f, k)]
    pairs = []
    for p in (0, 1):
        values = [
            restrict_01(sums[2 * p][2 * g : 2 * g + 2], sums[2 * p + 1][2 * g : 2 * g + 2]) for g in range(OWN)
        ]
        pairs.append(jnp.concatenate(values, axis=0))
        coarse[p * OWN : (p + 1) * OWN] = pairs[p]
        for ref in (first, second):
            ref[FIELDS1 + p * OWN : FIELDS1 + (p + 1) * OWN] = pairs[p]

    uv, fk = (restrict_12([pair[j : j + 1] for j in range(OWN)]) for pair in pairs)
    both = jnp.where((sub_of() & 2) == 0, uv, fk)
    coarse[2 * OWN : 2 * OWN + 1] = both
    for ref in (first, second):
        ref[FIELDS2 : FIELDS2 + 1] = both


def split_fields2(both):
    low = (sub_of() & 2) == 0
    return jnp.where(low, both, roll_z(both, 2)), jnp.where(low, roll_z(both, -2), both)


def spread_kernel(main, coarse, out):
    lane = lax.broadcasted_iota(jnp.int32, (1, X), 1)
    u, v, f, k = (main[i] for i in (0, 1, 4, 5))
    cross, squared, inv_u, inv_v, _, _ = jacobian(u, v, f, k, 0)
    tops = [jnp.max(jnp.maximum((6.0 * DIFF[0] + cross) * inv_u, (6.0 * DIFF[1] + squared) * inv_v), axis=0)]
    tops.append(jnp.max(packed_spread(coarse[0:OWN], coarse[OWN : 2 * OWN], 1), axis=0))
    tops.append(packed_spread(*split_fields2(coarse[2 * OWN : 2 * OWN + 1]), 2)[0])
    result = jnp.zeros((1, X), jnp.float32)
    for level, top in enumerate(tops):
        top = jnp.max(jnp.max(top, axis=0, keepdims=True), axis=1, keepdims=True)
        result = jnp.where(lane == level, jnp.broadcast_to(top, (1, X)), result)
    out[...] = jnp.broadcast_to(result[None], out.shape)


GROUPS1 = HI1 - LO1
GROUPS2 = HI2 - LO2


def tiles_for(entries):
    return -(-entries // PER)


def pack_edges(entries, even, first, second):
    lane = lane_of()
    share = first.shape[0]
    left, right = None, None
    for j in range(PER):
        part = entries[j * share : (j + 1) * share]
        a, b = roll_x(part, WIDE * j), roll_x(part, WIDE + WIDE * j)
        left = a if left is None else jnp.where(lane >= WIDE * j, a, left)
        right = b if right is None else jnp.where(lane >= WIDE * j, b, right)
    first[...] = jnp.where(even, left, right)
    second[...] = jnp.where(even, right, left)


def halo_tiles(even, packets, lo, hi):
    first, second = packets
    share = first.shape[0]
    lane = lane_of()
    out = []
    for j in range(PER):
        a, b = max(lo, j * share), min(hi, (j + 1) * share)
        if a < b:
            strip = slice(a - j * share, b - j * share)
            left, right = prev_of(even, first, second, strip), next_of(even, first, second, strip)
            value = jnp.where(lane < X // 2, roll_x(right, -WIDE * j), roll_x(left, X - WIDE - WIDE * j))
            out.append((a - lo, b - lo, value))
    return out


def pack_own_kernel(rows, main, coarse, first, second, held):
    for i in range(6):
        held[i * rows : (i + 1) * rows] = main[i]
    held[6 * rows : 6 * rows + 2 * OWN + 1] = coarse[...]
    pack_edges(held, is_even("gx"), first, second)


def pack_corner_kernel(y_first, y_second, first, second, held):
    even = is_even("gy")
    every = slice(0, PACKET)
    held[0:PACKET] = prev_of(even, y_first, y_second, every)
    held[PACKET : 2 * PACKET] = next_of(even, y_first, y_second, every)
    pack_edges(held, is_even("gx"), first, second)


FAR = 2 * OWN
EDGES = 2
EDGE_TILES = 2 * EDGE + 1


def level0_kernel(
    rows, main, y_first, y_second, own_a, own_b, corner_a, corner_b, gathered, own, first, second, edge_first, edge_second, keep, gain_out, fields, other, d, diag
):
    even, even_x = is_even("gy"), is_even("gx")
    total = rows + 2 * HALO0
    own_x, corner_x = (own_a, own_b), (corner_a, corner_b)
    top = jnp.max(gathered[...], axis=0)
    write_gains(top[0:1], gain_out)
    g0, g1, g2 = (gain_out[i] for i in range(3))
    for i, halo in enumerate(HALOS):
        strip = slice(STARTS[i], STARTS[i] + halo)
        skip = HALO0 - halo
        fields[i, 0, skip:HALO0] = prev_of(even, y_first, y_second, strip)
        fields[i, 0, HALO0 : HALO0 + rows] = main[i]
        fields[i, 0, HALO0 + rows : total - skip] = next_of(even, y_first, y_second, strip)
        for packets, lo, n, at in (
            (corner_x, STARTS[i], halo, skip),
            (own_x, i * rows, rows, HALO0),
            (corner_x, PACKET + STARTS[i], halo, HALO0 + rows),
        ):
            for a, b, value in halo_tiles(even_x, packets, lo, lo + n):
                fields[i, 1, at + a : at + b] = value
    here = keep.at[6:8]

    def setup(r, n):
        at = pl.ds(r, n)
        u, nb_u = neighbour_sums(lambda t, a, m: fields[0, t, pl.ds(a, m)], r, n, 1)
        v, nb_v = neighbour_sums(lambda t, a, m: fields[1, t, pl.ds(a, m)], r, n, 1)
        for t in (0, 1):
            f, k = fields[4, t, at], fields[5, t, at]
            cross, squared, inv_u, inv_v, first, second = jacobian(u[t], v[t], f, k, 0)
            react = u[t] * squared
            b_u = (
                DIFF[0] * (nb_u[t] - 6.0 * u[t])
                - INV_STEP * (u[t] - fields[2, t, at])
                - react
                + f * (1.0 - u[t])
            )
            b_v = (
                DIFF[1] * (nb_v[t] - 6.0 * v[t]) - INV_STEP * (v[t] - fields[3, t, at]) + react - (f + k) * v[t]
            )
            for i, value in enumerate((cross, squared, inv_u, inv_v, b_u, b_v)):
                keep[i, t, at] = value
            diag[0, t, at] = first
            diag[1, t, at] = second
            for i, value in enumerate((g0 * inv_u * b_u, g0 * inv_v * b_v)):
                d[i, t, at] = value
                keep[6 + i, t, at] = value

    rows_loop(1, total - 1, setup)
    rows_loop(2, total - 2, lambda r, n: cheb_step(0, keep, here, other, d, r, n, CARRY1, g1))
    rows_loop(3, total - 3, lambda r, n: cheb_step(0, keep, other, here, d, r, n, CARRY2, g2))

    def down(r, n):
        res = residual(0, keep, diag, here, r, n)
        for t in (0, 1):
            u, v = pair_rows(res[0][t]), pair_rows(res[1][t])
            for j in range(n // 4):
                value = restrict_01(u[2 * j : 2 * j + 2], v[2 * j : 2 * j + 2])
                for ref, at in ((own.at[t], 0), (first, t * OWN), (second, t * OWN)):
                    ref[pl.ds(at + (r - HALO0) // 4 + j, 1)] = value

    rows_loop(HALO0, HALO0 + rows, down, 8)

    lane = lane_of()
    edges = []
    for start in (HALO0, HALO0 + rows - EDGE):
        halo = None
        for i in (0, 1):
            for j in range(EDGE):
                at = i * EDGE + j
                value = roll_x(keep[6 + i, 1, start + j : start + j + 1], 4 + 8 * at)
                halo = value if halo is None else jnp.where((lane >> 3) == at, value, halo)
        edges.append([keep[6, 0, start : start + EDGE], keep[7, 0, start : start + EDGE], halo])
    top, bottom = (jnp.concatenate(parts, axis=0) for parts in edges)
    strip = slice(FIELDS2, FIELDS2 + 1)
    for t in (0, 1):
        if t == 0:
            before, after = prev_of(even, y_first, y_second, strip), next_of(even, y_first, y_second, strip)
        else:
            before, after = (
                halo_tiles(even_x, corner_x, at + FIELDS2, at + FIELDS2 + 1)[0][2] for at in (0, PACKET)
            )
        first[FAR + t : FAR + t + 1] = jnp.where(even, after, before)
        second[FAR + t : FAR + t + 1] = jnp.where(even, before, after)
    edge_first[...] = jnp.where(even, top, bottom)
    edge_second[...] = jnp.where(even, bottom, top)


def coarse1_kernel(
    rows, coarse, y_first, y_second, own_a, own_b, corner_a, corner_b, gain, coef, fields
):
    del gain
    even, even_x = is_even("gy"), is_even("gx")
    own_x, corner_x = (own_a, own_b), (corner_a, corner_b)
    for p in (0, 1):
        to = p * GROUPS1
        strip = slice(FIELDS1 + p * OWN, FIELDS1 + (p + 1) * OWN)
        fields[0, to : to + OWN] = prev_of(even, y_first, y_second, strip)
        fields[0, to + OWN : to + 2 * OWN] = coarse[p * OWN : (p + 1) * OWN]
        fields[0, to + 2 * OWN : to + 3 * OWN] = next_of(even, y_first, y_second, strip)
        for part, (packets, lo) in enumerate(
            ((corner_x, FIELDS1), (own_x, 6 * rows), (corner_x, PACKET + FIELDS1))
        ):
            lo += p * OWN
            for a, b, value in halo_tiles(even_x, packets, lo, lo + OWN):
                fields[1, to + part * OWN + a : to + part * OWN + b] = value
    for t in (0, 1):
        for i, value in enumerate(packed_jacobian(fields[t, 0:GROUPS1], fields[t, GROUPS1 : 2 * GROUPS1], 1)):
            coef[i, t, 1 : SIZE1 - 1] = value


def coarse2_kernel(
    rows, coarse, y_first, y_second, own_a, own_b, corner_a, corner_b, b_first, b_second, coef
):
    even, even_x = is_even("gy"), is_even("gx")
    own_x, corner_x = (own_a, own_b), (corner_a, corner_b)
    near = slice(FIELDS2, FIELDS2 + 1)
    for t in (0, 1):
        far = slice(FAR + t, FAR + t + 1)
        if t == 0:
            middle = [
                prev_of(even, y_first, y_second, near),
                coarse[2 * OWN : 2 * OWN + 1],
                next_of(even, y_first, y_second, near),
            ]
        else:
            middle = [
                halo_tiles(even_x, packets, lo, lo + 1)[0][2]
                for packets, lo in ((corner_x, FIELDS2), (own_x, 6 * rows + 2 * OWN), (corner_x, PACKET + FIELDS2))
            ]
        parts = [prev_of(even, b_first, b_second, far), *middle, next_of(even, b_first, b_second, far)]
        inverse, other, _ = packed_jacobian(*split_fields2(jnp.concatenate(parts, axis=0)), 2)
        coef[0, t, 1 : SIZE2 - 1] = inverse
        coef[1, t, 1 : SIZE2 - 1] = other


def level1_kernel(own, first, second, edge_a, edge_b, coef1, gain, packet, to_first, to_second, keep, y1, d1):
    b1, x1 = keep.at[0], keep.at[1]
    even = is_even("gy")
    for t in (0, 1):
        b1[t, 1 + OWN : 1 + 2 * OWN] = own[t]
        strip = slice(t * OWN, (t + 1) * OWN)
        b1[t, 1 : 1 + OWN] = prev_of(even, first, second, strip)
        b1[t, 1 + 2 * OWN : 1 + 3 * OWN] = next_of(even, first, second, strip)
    g0, g1, g2 = (gain[3 + i] for i in range(3))
    n = GROUPS1
    packed_first(coef1, 0, b1, x1, d1, 1, n, g0)
    packed_step(1, coef1, 0, b1, x1, y1, d1, 1, n, CARRY1, g1)
    packed_step(1, coef1, 0, b1, y1, x1, d1, 1, n, CARRY2, g2)
    here = pl.ds(1 + OWN, OWN)
    for t, (c, other, spread) in enumerate(packed_terms(x1, 1 + OWN, OWN, 1)):
        res = b1[t, here] - coef1[2, t, here] * c + coef1[1, t, here] * other + spread
        value = restrict_12([res[j : j + 1] for j in range(OWN)])
        for ref in (packet, to_first, to_second):
            ref[t : t + 1] = value
    to_first[EDGES : EDGES + EDGE_TILES] = edge_a[...]
    to_second[EDGES : EDGES + EDGE_TILES] = edge_b[...]


def rest_kernel(
    own2, near_a, near_b, far_a, far_b, gain, coef1, coef2, keep0, keep1, out, d1, b2, x2, y2, d2, xu, yu, x0, y0, d0
):
    rows = out.shape[0] // (2 * Z)
    even = (sub_of() & 1) == 0
    b1, x1 = keep1.at[0], keep1.at[1]

    even_y, low = is_even("gy"), lax.rem(lax.axis_index("gy"), 4) < 2
    for t in (0, 1):
        at = slice(t, t + 1)
        parts = [
            next_of(low, far_a, far_b, at),
            prev_of(even_y, near_a, near_b, at),
            own2[at],
            next_of(even_y, near_a, near_b, at),
            prev_of(low, far_a, far_b, at),
        ]
        b2[t, 1 : SIZE2 - 1] = jnp.concatenate(parts, axis=0)

    n = HI2 - LO2
    g0, g1, g2 = (gain[6 + i] for i in range(3))
    packed_first(coef2, 0, b2, x2, d2, 1, n, g0)
    packed_step(2, coef2, 0, b2, x2, y2, d2, 1, n, CARRY1, g1)
    packed_step(2, coef2, 0, b2, y2, x2, d2, 1, n, CARRY2, g2)
    packed_step(2, coef2, 0, b2, x2, y2, d2, 1, n, None, g0)
    packed_step(2, coef2, 0, b2, y2, x2, d2, 1, n, CARRY1, g1)
    packed_step(2, coef2, 0, b2, x2, y2, d2, 1, n, CARRY2, g2)

    g0, g1, g2 = (gain[3 + i] for i in range(3))
    shift = LO_UP - LO1
    for t in (0, 1):
        for g in range(LO_UP, HI_UP):
            p = g % 4
            value = y2[t, g // 4 - LO2 + 1 : g // 4 - LO2 + 2]
            value = spread_x(spread_x(value, 1, p & 1), 2, p & 2)
            at = g - LO_UP + 1
            xu[t, at : at + 1] = x1[t, at + shift : at + shift + 1] + value
    n = HI_UP - LO_UP
    packed_step(1, coef1, shift, b1, xu, yu, d1, 1, n, None, g0)
    packed_step(1, coef1, shift, b1, yu, xu, d1, 1, n, CARRY1, g1)
    packed_step(1, coef1, shift, b1, xu, yu, d1, 1, n, CARRY2, g2)

    g0, g1, g2 = (gain[i] for i in range(3))
    last = EDGES + 2 * EDGE
    for i in (0, 1):
        for at, take in ((HALO0 - EDGE, prev_of), (HALO0 + rows, next_of)):
            strip = slice(EDGES + i * EDGE, EDGES + (i + 1) * EDGE)
            x0[i, 0, at : at + EDGE] = take(even_y, near_a, near_b, strip)
            sides = take(even_y, near_a, near_b, slice(last, last + 1))
            for j in range(EDGE):
                x0[i, 1, at + j : at + j + 1] = roll_x(sides, -(4 + 8 * (i * EDGE + j)))
        for t in (0, 1):
            x0[i, t, HALO0 : HALO0 + rows] = keep0[6 + i, t, HALO0 : HALO0 + rows]
    for t in (0, 1):
        for row in range(-2, rows // 2 + 2):
            at = row // 2 - LO_UP + 1
            value = spread_x(yu[t, at : at + 1], 1, row & 1)
            for i, fine in enumerate((jnp.where(even, value, roll_z(value, 1)), jnp.where(even, roll_z(value, -1), value))):
                for y in (2 * row, 2 * row + 1):
                    if -EDGE <= y < rows + EDGE:
                        x0[i, t, y + HALO0 : y + HALO0 + 1] = x0[i, t, y + HALO0 : y + HALO0 + 1] + fine
    total = rows + 2 * HALO0
    rows_loop(2, total - 2, lambda r, n: cheb_step(0, keep0, x0, y0, d0, r, n, None, g0))
    rows_loop(3, total - 3, lambda r, n: cheb_step(0, keep0, y0, x0, d0, r, n, CARRY1, g1))
    rows_loop(4, total - 4, lambda r, n: cheb_step(0, keep0, x0, y0, d0, r, n, CARRY2, g2))
    for i in (0, 1):
        for y in range(rows):
            out[pl.ds(i * Z * rows + y, Z, stride=rows), :] = y0[i, 0, HALO0 + y]


def call(kernel, out_shapes, scratch, *args, space=pltpu.VMEM):
    out = [jax.ShapeDtypeStruct(shape, jnp.float32) for shape in out_shapes]
    return pl.pallas_call(
        kernel,
        out_shape=out,
        in_specs=[pl.BlockSpec(memory_space=space)] * len(args),
        out_specs=[pl.BlockSpec(memory_space=pltpu.VMEM)] * len(out),
        scratch_shapes=[pltpu.VMEM(s, jnp.float32) if isinstance(s, tuple) else s for s in scratch],
        compiler_params=pltpu.CompilerParams(vmem_limit_bytes=24 * 2**20),
    )(*args)


def swap(value, axis, step):
    count = lax.axis_size(axis)
    assert count % 2 == 0
    pairs = [(i, (i + step) % count) for i in range(0, count, 2)]
    return lax.ppermute(value, axis, pairs + [(j, i) for i, j in pairs])


def swap_far(value, axis, step):
    count = lax.axis_size(axis)
    assert count % 4 == 0
    pairs = [(i + j, (i + j + 2 * step) % count) for i in range(0, count, 4) for j in (0, 1)]
    return lax.ppermute(value, axis, pairs + [(j, i) for i, j in pairs])


def exchange(first, second, axis):
    return swap(first, axis, -1), swap(second, axis, 1)


def body(state, previous, feed, kill):
    _, depth, rows, cols = state.shape
    assert depth == Z and cols == X and rows == 4 * OWN
    across, count = lax.axis_size("gx"), lax.axis_size("gy")
    total0 = rows + 2 * HALO0
    state = state.reshape(2 * Z * rows, X)
    previous = previous.reshape(2 * Z * rows, X)
    feed = feed.reshape(Z * rows, X)
    kill = kill.reshape(Z * rows, X)
    inputs = (state, previous, feed, kill)

    strip = (FIELDS2 + 1, Z, X)
    first, second, main, coarse = call(
        functools.partial(first_kernel, rows),
        [strip, strip, (6, rows, Z, X), (2 * OWN + 1, Z, X)],
        [*(a.shape for a in inputs), pltpu.SemaphoreType.DMA((4,))],
        *(pltpu.with_memory_space_constraint(a, pltpu.HBM) for a in inputs),
        space=pltpu.HBM,
    )
    y_packets = exchange(first, second, "gy")
    (spread,) = call(spread_kernel, [(across * count, Z // 2, X)], [], main, coarse)
    spread = lax.all_to_all(spread, ("gx", "gy"), 0, 0, tiled=True)

    tiles = tiles_for(6 * rows + 2 * OWN + 1)
    own_x = exchange(
        *call(
            functools.partial(pack_own_kernel, rows),
            [(tiles, Z, X), (tiles, Z, X)],
            [(PER * tiles, Z, X)],
            main,
            coarse,
        ),
        "gx",
    )
    tiles = tiles_for(2 * PACKET)
    corner_x = exchange(
        *call(pack_corner_kernel, [(tiles, Z, X), (tiles, Z, X)], [(PER * tiles, Z, X)], *y_packets), "gx"
    )

    strip, edge = (FAR + 2, Z, X), (EDGE_TILES, Z, X)
    pair0 = (2, 2, total0, Z, X)
    own, first, second, edge_a, edge_b, keep0, gain = call(
        functools.partial(level0_kernel, rows),
        [(2, OWN, Z, X), strip, strip, edge, edge, (8, 2, total0, Z, X), (9, Z, X)],
        [(6, 2, total0, Z, X), pair0, pair0, pair0],
        main,
        *y_packets,
        *own_x,
        *corner_x,
        spread,
    )
    (coef1,) = call(
        functools.partial(coarse1_kernel, rows),
        [(3, 2, SIZE1, Z, X)],
        [(2, 2 * GROUPS1, Z, X)],
        coarse,
        *y_packets,
        *own_x,
        *corner_x,
        gain,
    )
    b_packets = exchange(first, second, "gy")

    one, two, up = (2, SIZE1, Z, X), (2, SIZE2, Z, X), (2, SIZE_UP, Z, X)
    near = (EDGES + EDGE_TILES, Z, X)
    packet, first, second, keep1 = call(
        level1_kernel,
        [(2, Z, X), near, near, (2, *one)],
        [one, one],
        own,
        *b_packets,
        edge_a,
        edge_b,
        coef1,
        gain,
    )
    far = (swap_far(packet, "gy", 1), swap_far(packet, "gy", -1))
    near = exchange(first, second, "gy")
    (coef2,) = call(
        functools.partial(coarse2_kernel, rows),
        [(2, 2, SIZE2, Z, X)],
        [],
        coarse,
        *y_packets,
        *own_x,
        *corner_x,
        *b_packets,
    )

    (out,) = call(
        rest_kernel,
        [(2 * Z * rows, X)],
        [one, two, two, two, two, up, up, pair0, pair0, pair0],
        packet,
        *near,
        *far,
        gain,
        coef1,
        coef2,
        keep0,
        keep1,
    )
    return out.reshape(2, Z, rows, X)


def solution(mesh):
    placed = (
        P(None, None, "gy", "gx"),
        P(None, None, "gy", "gx"),
        P(None, "gy", "gx"),
        P(None, "gy", "gx"),
    )
    return jax.shard_map(
        body, mesh=mesh, in_specs=placed, out_specs=P(None, None, "gy", "gx"), check_vma=False
    )
```

```python
import functools

import jax
import jax.numpy as jnp
from jax import lax
from jax.experimental import pallas as pl
from jax.experimental.pallas import tpu as pltpu
from jax.sharding import PartitionSpec as P

DIFF = (40.0, 20.0)
INV_STEP = 2.0
LOWER = 0.25

_CENTRE = (1.0 + LOWER) / 2.0
_HALF = (1.0 - LOWER) / 2.0
_SIGMA = _CENTRE / _HALF
_RHO0 = 1.0 / _SIGMA
_RHO1 = 1.0 / (2.0 * _SIGMA - _RHO0)
_RHO2 = 1.0 / (2.0 * _SIGMA - _RHO1)

Z = 8
X = 128
HALO0 = 4
HALOS = (4, 4, 3, 3, 3, 3)
STARTS = tuple(sum(HALOS[:i]) for i in range(6))
FIELDS1 = sum(HALOS)
FIELDS2 = FIELDS1 + 8
PACKET = FIELDS2 + 1
WIDE = 42
PER = X // WIDE
EDGE = 3

LO1, HI1 = -4, 8
LO2, HI2 = -2, 3
LO_UP, HI_UP = -3, 7
SIZE1, SIZE2, SIZE_UP = HI1 - LO1 + 2, HI2 - LO2 + 2, HI_UP - LO_UP + 2
OWN = 4


def lane_of():
    return lax.broadcasted_iota(jnp.int32, (1, Z, X), 2)


def sub_of():
    return lax.broadcasted_iota(jnp.int32, (1, Z, X), 1)


def roll_x(tile, shift):
    shift = shift % X
    return pltpu.roll(tile, shift, 2) if shift else tile


def roll_z(tile, shift):
    shift = shift % Z
    return pltpu.roll(tile, shift, 1) if shift else tile


def rows_loop(lo, hi, body, step=None):
    step = step or (hi - lo) // 2
    full = (hi - lo) // step
    if full == 1:
        body(lo, step)
    elif full > 1:

        def trip(i, carry):
            body(lo + i * step, step)
            return carry

        lax.fori_loop(0, full, trip, 0)
    rest = hi - lo - full * step
    if rest:
        body(hi - rest, rest)


def neighbour_sums(read, r, n, k):
    lane = lane_of()
    low, high = lane < k, lane >= X - k
    centre = [read(t, r, n) for t in (0, 1)]
    right = [roll_x(c, k) for c in centre]
    left = [roll_x(c, -k) for c in centre]
    sums = []
    for t in (0, 1):
        c = centre[t]
        along_x = jnp.where(low, right[1 - t], right[t]) + jnp.where(high, left[1 - t], left[t])
        along_y = read(t, r - 1, n) + read(t, r + 1, n)
        along_z = 2.0 * roll_z(c, k) if 2 * k == Z else roll_z(c, k) + roll_z(c, -k)
        sums.append(along_x + along_y + along_z)
    return centre, sums


def jacobian(u, v, f, k, level):
    scale = 0.25**level
    product = u * v
    squared = v * v
    first = INV_STEP + squared + f + 6.0 * DIFF[0] * scale
    second = INV_STEP + f + k - 2.0 * product + 6.0 * DIFF[1] * scale
    return 2.0 * product, squared, 1.0 / first, 1.0 / second, first, second


def cheb_step(level, keep, source, target, d, r, n, carry, gain):
    scale = 0.25**level
    k = 1 << level
    u, nb_u = neighbour_sums(lambda t, a, m: source[0, t, pl.ds(a, m)], r, n, k)
    v, nb_v = neighbour_sums(lambda t, a, m: source[1, t, pl.ds(a, m)], r, n, k)
    rows = pl.ds(r, n)
    for t in (0, 1):
        cross, squared, inv_u, inv_v = (keep[i, t, rows] for i in range(4))
        res_u = inv_u * (keep[4, t, rows] - cross * v[t] + DIFF[0] * scale * nb_u[t]) - u[t]
        res_v = inv_v * (keep[5, t, rows] + squared * u[t] + DIFF[1] * scale * nb_v[t]) - v[t]
        du, dv = gain * res_u, gain * res_v
        if carry is not None:
            du = du + carry * d[0, t, rows]
            dv = dv + carry * d[1, t, rows]
        d[0, t, rows] = du
        d[1, t, rows] = dv
        target[0, t, rows] = u[t] + du
        target[1, t, rows] = v[t] + dv


def next_power(keep, source, r, n):
    u, nb_u = neighbour_sums(lambda t, a, m: source[0, t, pl.ds(a, m)], r, n, 1)
    v, nb_v = neighbour_sums(lambda t, a, m: source[1, t, pl.ds(a, m)], r, n, 1)
    rows = pl.ds(r, n)
    first, second = [], []
    for t in (0, 1):
        cross, squared, inv_u, inv_v = (keep[i, t, rows] for i in range(4))
        first.append(u[t] + inv_u * (cross * v[t] - DIFF[0] * nb_u[t]))
        second.append(v[t] - inv_v * (squared * u[t] + DIFF[1] * nb_v[t]))
    return first, second


CARRY1 = _RHO1 * _RHO0
CARRY2 = _RHO2 * _RHO1


POWERS = 9


def write_gains(spread, out):
    lane = lax.broadcasted_iota(jnp.int32, (1, X), 1)
    for level in range(3):
        top = jnp.max(jnp.where(lane == level, spread, 0.0), axis=1, keepdims=True)
        tau = 1.0 / (1.0 + jnp.broadcast_to(top, (Z, X)))
        for i, factor in enumerate((1.0 / _CENTRE, 2.0 * _RHO1 / _HALF, 2.0 * _RHO2 / _HALF)):
            out[3 * level + i] = factor * tau
    g0, g1, g2 = (out[i] for i in range(3))
    first, second = g0 + CARRY1 * g0 + g1, g1 * g0
    out[POWERS] = first + CARRY2 * (CARRY1 * g0 + g1) + g2
    out[POWERS + 1] = second + CARRY2 * second + g2 * first
    out[POWERS + 2] = g2 * second


def pair_rows(value):
    n = value.shape[0] // 2
    pairs = value.reshape(n, 2, Z, X)
    return pairs[:, 0] + pairs[:, 1]


def restrict_01(first, second):
    lane, sub = lane_of(), sub_of()
    across = []
    for value in (first, second):
        a, b = value[0:1], value[1:2]
        across.append(jnp.where((lane & 1) == 0, a + roll_x(a, -1), b + roll_x(b, 1)))
    a, b = across
    return 0.125 * jnp.where((sub & 1) == 0, a + roll_z(a, -1), b + roll_z(b, 1))


def restrict_12(groups):
    lane, sub = lane_of(), sub_of()
    out = None
    for p, value in enumerate(groups):
        value = value + roll_x(value, 1 if p & 1 else -1)
        value = value + roll_x(value, 2 if p & 2 else -2)
        out = value if out is None else jnp.where((lane & 3) == p, value, out)
    return 0.125 * (out + jnp.where((sub & 2) == 0, roll_z(out, -2), roll_z(out, 2)))


def spread_x(tile, k, phase):
    return jnp.where((lane_of() & k) == phase, tile, roll_x(tile, -k if phase else k))


def packed_jacobian(uv, fk, level):
    scale = 0.25**level
    even = (sub_of() & 1) == 0
    u, v = jnp.where(even, uv, roll_z(uv, 1)), jnp.where(even, roll_z(uv, -1), uv)
    f, k = jnp.where(even, fk, roll_z(fk, 1)), jnp.where(even, roll_z(fk, -1), fk)
    product, squared = u * v, v * v
    diag = jnp.where(
        even,
        INV_STEP + squared + f + 6.0 * DIFF[0] * scale,
        INV_STEP + f + k - 2.0 * product + 6.0 * DIFF[1] * scale,
    )
    return 1.0 / diag, jnp.where(even, -2.0 * product, squared), diag


def packed_spread(uv, fk, level):
    scale = 0.25**level
    even = (sub_of() & 1) == 0
    inverse, other, _ = packed_jacobian(uv, fk, level)
    return jnp.where(even, 6.0 * DIFF[0] * scale - other, 6.0 * DIFF[1] * scale + other) * inverse


def packed_terms(source, g, n, level):
    k = 1 << level
    lane, sub = lane_of(), sub_of()
    even = (sub & 1) == 0
    first, last = (lane & (k - 1)) == 0, (lane & (k - 1)) == k - 1
    low, high = lane < k, lane >= X - k
    diff = jnp.where(even, DIFF[0] * 0.25**level, DIFF[1] * 0.25**level)
    wide = [source[t, pl.ds(g - 1, n + 2)] for t in (0, 1)]
    centre = [w[1 : n + 1] for w in wide]
    right = [roll_x(c, k) for c in centre]
    left = [roll_x(c, -k) for c in centre]
    out = []
    for t in (0, 1):
        c, w = centre[t], wide[t]
        total = jnp.where(low, right[1 - t], right[t]) + jnp.where(high, left[1 - t], left[t])
        if k == 2:
            ahead, back = roll_x(w, 1), roll_x(w, -1)
            total = total + jnp.where(first, back[0:n], ahead[1 : n + 1])
            total = total + jnp.where(last, ahead[2 : n + 2], back[1 : n + 1])
            total = total + roll_z(c, 2) + roll_z(c, -2)
        else:
            total = total + jnp.where(first, roll_x(w[0:n], -(k - 1)), roll_x(c, 1))
            total = total + jnp.where(last, roll_x(w[2 : n + 2], k - 1), roll_x(c, -1))
            total = total + 2.0 * roll_z(c, 4)
        other = jnp.where(even, roll_z(c, -1), roll_z(c, 1))
        out.append((c, other, diff * total))
    return out


def packed_first(coef, shift, b, target, d, g, n, gain):
    for t in (0, 1):
        value = gain * coef[0, t, pl.ds(g + shift, n)] * b[t, pl.ds(g + shift, n)]
        d[t, pl.ds(g, n)] = value
        target[t, pl.ds(g, n)] = value


def packed_step(level, coef, shift, b, source, target, d, g, n, carry, gain):
    for t, (c, other, spread) in enumerate(packed_terms(source, g, n, level)):
        at = pl.ds(g + shift, n)
        res = coef[0, t, at] * (b[t, at] + coef[1, t, at] * other + spread) - c
        delta = gain * res
        if carry is not None:
            delta = delta + carry * d[t, pl.ds(g, n)]
        d[t, pl.ds(g, n)] = delta
        target[t, pl.ds(g, n)] = c + delta


def plane(ref, f, y, rows):
    return ref[pl.ds(f * Z * rows + y, Z, stride=rows), :]


def is_even(axis):
    return lax.rem(lax.axis_index(axis), 2) == 0


def prev_of(even, first, second, at):
    return jnp.where(even, first[at], second[at])


def next_of(even, first, second, at):
    return jnp.where(even, second[at], first[at])


def first_kernel(rows, state, previous, feed, kill, first, second, main, coarse, *scratch):
    sources, sems = scratch[:4], scratch[4]
    copies = [
        pltpu.make_async_copy(ref, held, sems.at[i])
        for i, (ref, held) in enumerate(zip((state, previous, feed, kill), sources))
    ]
    for copy in copies:
        copy.start()
    for copy in copies:
        copy.wait()
    even = is_even("gy")
    state, previous, feed, kill = sources
    fields = [(state, 0), (state, 1), (previous, 0), (previous, 1), (feed, 0), (kill, 0)]
    for i, (ref, f) in enumerate(fields):
        for y in range(rows):
            main[i, y] = plane(ref, f, y, rows)
        top, bottom = main[i, 0 : HALOS[i]], main[i, rows - HALOS[i] : rows]
        at = slice(STARTS[i], STARTS[i] + HALOS[i])
        first[at] = jnp.where(even, top, bottom)
        second[at] = jnp.where(even, bottom, top)
    u, v, f, k = (main[i] for i in (0, 1, 4, 5))
    sums = [pair_rows(value) for value in (u, v, f, k)]
    pairs = []
    for p in (0, 1):
        values = [
            restrict_01(sums[2 * p][2 * g : 2 * g + 2], sums[2 * p + 1][2 * g : 2 * g + 2]) for g in range(OWN)
        ]
        pairs.append(jnp.concatenate(values, axis=0))
        coarse[p * OWN : (p + 1) * OWN] = pairs[p]
        for ref in (first, second):
            ref[FIELDS1 + p * OWN : FIELDS1 + (p + 1) * OWN] = pairs[p]

    uv, fk = (restrict_12([pair[j : j + 1] for j in range(OWN)]) for pair in pairs)
    both = jnp.where((sub_of() & 2) == 0, uv, fk)
    coarse[2 * OWN : 2 * OWN + 1] = both
    for ref in (first, second):
        ref[FIELDS2 : FIELDS2 + 1] = both


def split_fields2(both):
    low = (sub_of() & 2) == 0
    return jnp.where(low, both, roll_z(both, 2)), jnp.where(low, roll_z(both, -2), both)


def spread_kernel(main, coarse, out):
    lane = lax.broadcasted_iota(jnp.int32, (1, X), 1)
    u, v, f, k = (main[i] for i in (0, 1, 4, 5))
    cross, squared, inv_u, inv_v, _, _ = jacobian(u, v, f, k, 0)
    tops = [jnp.max(jnp.maximum((6.0 * DIFF[0] + cross) * inv_u, (6.0 * DIFF[1] + squared) * inv_v), axis=0)]
    tops.append(jnp.max(packed_spread(coarse[0:OWN], coarse[OWN : 2 * OWN], 1), axis=0))
    tops.append(packed_spread(*split_fields2(coarse[2 * OWN : 2 * OWN + 1]), 2)[0])
    result = jnp.zeros((1, X), jnp.float32)
    for level, top in enumerate(tops):
        top = jnp.max(jnp.max(top, axis=0, keepdims=True), axis=1, keepdims=True)
        result = jnp.where(lane == level, jnp.broadcast_to(top, (1, X)), result)
    out[...] = jnp.broadcast_to(result[None], out.shape)


GROUPS1 = HI1 - LO1
GROUPS2 = HI2 - LO2


def tiles_for(entries):
    return -(-entries // PER)


def pack_edges(entries, even, first, second):
    lane = lane_of()
    share = first.shape[0]
    left, right = None, None
    for j in range(PER):
        part = entries[j * share : (j + 1) * share]
        a, b = roll_x(part, WIDE * j), roll_x(part, WIDE + WIDE * j)
        left = a if left is None else jnp.where(lane >= WIDE * j, a, left)
        right = b if right is None else jnp.where(lane >= WIDE * j, b, right)
    first[...] = jnp.where(even, left, right)
    second[...] = jnp.where(even, right, left)


def halo_tiles(even, packets, lo, hi):
    first, second = packets
    share = first.shape[0]
    lane = lane_of()
    out = []
    for j in range(PER):
        a, b = max(lo, j * share), min(hi, (j + 1) * share)
        if a < b:
            strip = slice(a - j * share, b - j * share)
            left, right = prev_of(even, first, second, strip), next_of(even, first, second, strip)
            value = jnp.where(lane < X // 2, roll_x(right, -WIDE * j), roll_x(left, X - WIDE - WIDE * j))
            out.append((a - lo, b - lo, value))
    return out


def pack_own_kernel(rows, main, coarse, first, second, held):
    for i in range(6):
        held[i * rows : (i + 1) * rows] = main[i]
    held[6 * rows : 6 * rows + 2 * OWN + 1] = coarse[...]
    pack_edges(held, is_even("gx"), first, second)


def pack_corner_kernel(y_first, y_second, first, second, held):
    even = is_even("gy")
    every = slice(0, PACKET)
    held[0:PACKET] = prev_of(even, y_first, y_second, every)
    held[PACKET : 2 * PACKET] = next_of(even, y_first, y_second, every)
    pack_edges(held, is_even("gx"), first, second)


FAR = 2 * OWN
EDGES = 2
EDGE_TILES = 2 * EDGE + 1


def level0_kernel(
    rows, main, y_first, y_second, own_a, own_b, corner_a, corner_b, keep, powers, sources, fields, diag
):
    even, even_x = is_even("gy"), is_even("gx")
    total = rows + 2 * HALO0
    own_x, corner_x = (own_a, own_b), (corner_a, corner_b)
    for i, halo in enumerate(HALOS):
        strip = slice(STARTS[i], STARTS[i] + halo)
        skip = HALO0 - halo
        fields[i, 0, skip:HALO0] = prev_of(even, y_first, y_second, strip)
        fields[i, 0, HALO0 : HALO0 + rows] = main[i]
        fields[i, 0, HALO0 + rows : total - skip] = next_of(even, y_first, y_second, strip)
        for packets, lo, n, at in (
            (corner_x, STARTS[i], halo, skip),
            (own_x, i * rows, rows, HALO0),
            (corner_x, PACKET + STARTS[i], halo, HALO0 + rows),
        ):
            for a, b, value in halo_tiles(even_x, packets, lo, lo + n):
                fields[i, 1, at + a : at + b] = value

    def setup(r, n):
        at = pl.ds(r, n)
        u, nb_u = neighbour_sums(lambda t, a, m: fields[0, t, pl.ds(a, m)], r, n, 1)
        v, nb_v = neighbour_sums(lambda t, a, m: fields[1, t, pl.ds(a, m)], r, n, 1)
        for t in (0, 1):
            f, k = fields[4, t, at], fields[5, t, at]
            cross, squared, inv_u, inv_v, first, second = jacobian(u[t], v[t], f, k, 0)
            react = u[t] * squared
            b_u = (
                DIFF[0] * (nb_u[t] - 6.0 * u[t])
                - INV_STEP * (u[t] - fields[2, t, at])
                - react
                + f * (1.0 - u[t])
            )
            b_v = (
                DIFF[1] * (nb_v[t] - 6.0 * v[t]) - INV_STEP * (v[t] - fields[3, t, at]) + react - (f + k) * v[t]
            )
            for i, value in enumerate((cross, squared, inv_u, inv_v, b_u, b_v)):
                keep[i, t, at] = value
            diag[0, t, at] = first
            diag[1, t, at] = second
            powers[0, 0, t, at] = inv_u * b_u
            powers[0, 1, t, at] = inv_v * b_v

    rows_loop(1, total - 1, setup)
    for p in (0, 1):

        def power(r, n, p=p):
            for i, values in enumerate(next_power(keep, powers.at[p], r, n)):
                for t in (0, 1):
                    powers[p + 1, i, t, pl.ds(r, n)] = values[t]

        rows_loop(2 + p, total - 2 - p, power)

    def down(r, n):
        at = pl.ds(r, n)
        last = next_power(keep, powers.at[2], r, n)
        for t in (0, 1):
            both = [diag[i, t, at] for i in (0, 1)]
            parts = [[keep[4 + i, t, at] for i in (0, 1)]]
            parts += [[both[i] * powers[p, i, t, at] for i in (0, 1)] for p in (1, 2)]
            parts.append([both[i] * last[i][t] for i in (0, 1)])
            for q, part in enumerate(parts):
                u, v = (pair_rows(value) for value in part)
                for j in range(n // 4):
                    value = restrict_01(u[2 * j : 2 * j + 2], v[2 * j : 2 * j + 2])
                    sources[q, t, pl.ds((r - HALO0) // 4 + j, 1)] = value

    rows_loop(HALO0, HALO0 + rows, down, 8)


def combine_kernel(sources, y_first, y_second, corner_a, corner_b, spread, own, first, second, gain):
    even, even_x = is_even("gy"), is_even("gx")
    write_gains(jnp.max(spread[...], axis=0)[0:1], gain)
    p0, p1, p2 = (gain[POWERS + i] for i in range(3))
    for t in (0, 1):
        value = sources[0, t] - p0 * sources[1, t] + p1 * sources[2, t] - p2 * sources[3, t]
        own[t] = value
        for ref in (first, second):
            ref[t * OWN : (t + 1) * OWN] = value
    strip = slice(FIELDS2, FIELDS2 + 1)
    for t in (0, 1):
        if t == 0:
            before, after = prev_of(even, y_first, y_second, strip), next_of(even, y_first, y_second, strip)
        else:
            before, after = (
                halo_tiles(even_x, (corner_a, corner_b), at + FIELDS2, at + FIELDS2 + 1)[0][2] for at in (0, PACKET)
            )
        first[FAR + t : FAR + t + 1] = jnp.where(even, after, before)
        second[FAR + t : FAR + t + 1] = jnp.where(even, before, after)


def coarse1_kernel(
    rows, coarse, y_first, y_second, own_a, own_b, corner_a, corner_b, gain, powers, coef, x0, edge_first, edge_second, fields
):
    even, even_x = is_even("gy"), is_even("gx")
    own_x, corner_x = (own_a, own_b), (corner_a, corner_b)
    for p in (0, 1):
        to = p * GROUPS1
        strip = slice(FIELDS1 + p * OWN, FIELDS1 + (p + 1) * OWN)
        fields[0, to : to + OWN] = prev_of(even, y_first, y_second, strip)
        fields[0, to + OWN : to + 2 * OWN] = coarse[p * OWN : (p + 1) * OWN]
        fields[0, to + 2 * OWN : to + 3 * OWN] = next_of(even, y_first, y_second, strip)
        for part, (packets, lo) in enumerate(
            ((corner_x, FIELDS1), (own_x, 6 * rows), (corner_x, PACKET + FIELDS1))
        ):
            lo += p * OWN
            for a, b, value in halo_tiles(even_x, packets, lo, lo + OWN):
                fields[1, to + part * OWN + a : to + part * OWN + b] = value
    for t in (0, 1):
        for i, value in enumerate(packed_jacobian(fields[t, 0:GROUPS1], fields[t, GROUPS1 : 2 * GROUPS1], 1)):
            coef[i, t, 1 : SIZE1 - 1] = value

    p0, p1, p2 = (gain[POWERS + i] for i in range(3))
    for i in (0, 1):
        for t in (0, 1):
            y0, y1, y2 = (powers[p, i, t, HALO0 : HALO0 + rows] for p in range(3))
            x0[i, t] = p0 * y0 - p1 * y1 + p2 * y2
    lane = lane_of()
    edges = []
    for start in (0, rows - EDGE):
        halo = None
        for i in (0, 1):
            for j in range(EDGE):
                at = i * EDGE + j
                value = roll_x(x0[i, 1, start + j : start + j + 1], 4 + 8 * at)
                halo = value if halo is None else jnp.where((lane >> 3) == at, value, halo)
        edges.append([x0[0, 0, start : start + EDGE], x0[1, 0, start : start + EDGE], halo])
    top, bottom = (jnp.concatenate(parts, axis=0) for parts in edges)
    edge_first[...] = jnp.where(even, top, bottom)
    edge_second[...] = jnp.where(even, bottom, top)


def coarse2_kernel(
    rows, coarse, y_first, y_second, own_a, own_b, corner_a, corner_b, b_first, b_second, coef
):
    even, even_x = is_even("gy"), is_even("gx")
    own_x, corner_x = (own_a, own_b), (corner_a, corner_b)
    near = slice(FIELDS2, FIELDS2 + 1)
    for t in (0, 1):
        far = slice(FAR + t, FAR + t + 1)
        if t == 0:
            middle = [
                prev_of(even, y_first, y_second, near),
                coarse[2 * OWN : 2 * OWN + 1],
                next_of(even, y_first, y_second, near),
            ]
        else:
            middle = [
                halo_tiles(even_x, packets, lo, lo + 1)[0][2]
                for packets, lo in ((corner_x, FIELDS2), (own_x, 6 * rows + 2 * OWN), (corner_x, PACKET + FIELDS2))
            ]
        parts = [prev_of(even, b_first, b_second, far), *middle, next_of(even, b_first, b_second, far)]
        inverse, other, _ = packed_jacobian(*split_fields2(jnp.concatenate(parts, axis=0)), 2)
        coef[0, t, 1 : SIZE2 - 1] = inverse
        coef[1, t, 1 : SIZE2 - 1] = other


def level1_kernel(own, first, second, edge_a, edge_b, coef1, gain, packet, to_first, to_second, keep, y1, d1):
    b1, x1 = keep.at[0], keep.at[1]
    even = is_even("gy")
    for t in (0, 1):
        b1[t, 1 + OWN : 1 + 2 * OWN] = own[t]
        strip = slice(t * OWN, (t + 1) * OWN)
        b1[t, 1 : 1 + OWN] = prev_of(even, first, second, strip)
        b1[t, 1 + 2 * OWN : 1 + 3 * OWN] = next_of(even, first, second, strip)
    g0, g1, g2 = (gain[3 + i] for i in range(3))
    n = GROUPS1
    packed_first(coef1, 0, b1, x1, d1, 1, n, g0)
    packed_step(1, coef1, 0, b1, x1, y1, d1, 1, n, CARRY1, g1)
    packed_step(1, coef1, 0, b1, y1, x1, d1, 1, n, CARRY2, g2)
    here = pl.ds(1 + OWN, OWN)
    for t, (c, other, spread) in enumerate(packed_terms(x1, 1 + OWN, OWN, 1)):
        res = b1[t, here] - coef1[2, t, here] * c + coef1[1, t, here] * other + spread
        value = restrict_12([res[j : j + 1] for j in range(OWN)])
        for ref in (packet, to_first, to_second):
            ref[t : t + 1] = value
    to_first[EDGES : EDGES + EDGE_TILES] = edge_a[...]
    to_second[EDGES : EDGES + EDGE_TILES] = edge_b[...]


def rest_kernel(
    own2, near_a, near_b, far_a, far_b, gain, coef1, coef2, keep0, iterate, keep1, out, d1, b2, x2, y2, d2, xu, yu, x0, y0, d0
):
    rows = out.shape[0] // (2 * Z)
    even = (sub_of() & 1) == 0
    b1, x1 = keep1.at[0], keep1.at[1]

    even_y, low = is_even("gy"), lax.rem(lax.axis_index("gy"), 4) < 2
    for t in (0, 1):
        at = slice(t, t + 1)
        parts = [
            next_of(low, far_a, far_b, at),
            prev_of(even_y, near_a, near_b, at),
            own2[at],
            next_of(even_y, near_a, near_b, at),
            prev_of(low, far_a, far_b, at),
        ]
        b2[t, 1 : SIZE2 - 1] = jnp.concatenate(parts, axis=0)

    n = HI2 - LO2
    g0, g1, g2 = (gain[6 + i] for i in range(3))
    packed_first(coef2, 0, b2, x2, d2, 1, n, g0)
    packed_step(2, coef2, 0, b2, x2, y2, d2, 1, n, CARRY1, g1)
    packed_step(2, coef2, 0, b2, y2, x2, d2, 1, n, CARRY2, g2)
    packed_step(2, coef2, 0, b2, x2, y2, d2, 1, n, None, g0)
    packed_step(2, coef2, 0, b2, y2, x2, d2, 1, n, CARRY1, g1)
    packed_step(2, coef2, 0, b2, x2, y2, d2, 1, n, CARRY2, g2)

    g0, g1, g2 = (gain[3 + i] for i in range(3))
    shift = LO_UP - LO1
    for t in (0, 1):
        for g in range(LO_UP, HI_UP):
            p = g % 4
            value = y2[t, g // 4 - LO2 + 1 : g // 4 - LO2 + 2]
            value = spread_x(spread_x(value, 1, p & 1), 2, p & 2)
            at = g - LO_UP + 1
            xu[t, at : at + 1] = x1[t, at + shift : at + shift + 1] + value
    n = HI_UP - LO_UP
    packed_step(1, coef1, shift, b1, xu, yu, d1, 1, n, None, g0)
    packed_step(1, coef1, shift, b1, yu, xu, d1, 1, n, CARRY1, g1)
    packed_step(1, coef1, shift, b1, xu, yu, d1, 1, n, CARRY2, g2)

    g0, g1, g2 = (gain[i] for i in range(3))
    last = EDGES + 2 * EDGE
    for i in (0, 1):
        for at, take in ((HALO0 - EDGE, prev_of), (HALO0 + rows, next_of)):
            strip = slice(EDGES + i * EDGE, EDGES + (i + 1) * EDGE)
            x0[i, 0, at : at + EDGE] = take(even_y, near_a, near_b, strip)
            sides = take(even_y, near_a, near_b, slice(last, last + 1))
            for j in range(EDGE):
                x0[i, 1, at + j : at + j + 1] = roll_x(sides, -(4 + 8 * (i * EDGE + j)))
        for t in (0, 1):
            x0[i, t, HALO0 : HALO0 + rows] = iterate[i, t]
    for t in (0, 1):
        for row in range(-2, rows // 2 + 2):
            at = row // 2 - LO_UP + 1
            value = spread_x(yu[t, at : at + 1], 1, row & 1)
            for i, fine in enumerate((jnp.where(even, value, roll_z(value, 1)), jnp.where(even, roll_z(value, -1), value))):
                for y in (2 * row, 2 * row + 1):
                    if -EDGE <= y < rows + EDGE:
                        x0[i, t, y + HALO0 : y + HALO0 + 1] = x0[i, t, y + HALO0 : y + HALO0 + 1] + fine
    total = rows + 2 * HALO0
    rows_loop(2, total - 2, lambda r, n: cheb_step(0, keep0, x0, y0, d0, r, n, None, g0))
    rows_loop(3, total - 3, lambda r, n: cheb_step(0, keep0, y0, x0, d0, r, n, CARRY1, g1))
    rows_loop(4, total - 4, lambda r, n: cheb_step(0, keep0, x0, y0, d0, r, n, CARRY2, g2))
    for i in (0, 1):
        for y in range(rows):
            out[pl.ds(i * Z * rows + y, Z, stride=rows), :] = y0[i, 0, HALO0 + y]


def call(kernel, out_shapes, scratch, *args, space=pltpu.VMEM):
    out = [jax.ShapeDtypeStruct(shape, jnp.float32) for shape in out_shapes]
    return pl.pallas_call(
        kernel,
        out_shape=out,
        in_specs=[pl.BlockSpec(memory_space=space)] * len(args),
        out_specs=[pl.BlockSpec(memory_space=pltpu.VMEM)] * len(out),
        scratch_shapes=[pltpu.VMEM(s, jnp.float32) if isinstance(s, tuple) else s for s in scratch],
        compiler_params=pltpu.CompilerParams(vmem_limit_bytes=24 * 2**20),
    )(*args)


def swap(value, axis, step):
    count = lax.axis_size(axis)
    assert count % 2 == 0
    pairs = [(i, (i + step) % count) for i in range(0, count, 2)]
    return lax.ppermute(value, axis, pairs + [(j, i) for i, j in pairs])


def swap_far(value, axis, step):
    count = lax.axis_size(axis)
    assert count % 4 == 0
    pairs = [(i + j, (i + j + 2 * step) % count) for i in range(0, count, 4) for j in (0, 1)]
    return lax.ppermute(value, axis, pairs + [(j, i) for i, j in pairs])


def exchange(first, second, axis):
    return swap(first, axis, -1), swap(second, axis, 1)


def body(state, previous, feed, kill):
    _, depth, rows, cols = state.shape
    assert depth == Z and cols == X and rows == 4 * OWN
    across, count = lax.axis_size("gx"), lax.axis_size("gy")
    total0 = rows + 2 * HALO0
    state = state.reshape(2 * Z * rows, X)
    previous = previous.reshape(2 * Z * rows, X)
    feed = feed.reshape(Z * rows, X)
    kill = kill.reshape(Z * rows, X)
    inputs = (state, previous, feed, kill)

    strip = (FIELDS2 + 1, Z, X)
    first, second, main, coarse = call(
        functools.partial(first_kernel, rows),
        [strip, strip, (6, rows, Z, X), (2 * OWN + 1, Z, X)],
        [*(a.shape for a in inputs), pltpu.SemaphoreType.DMA((4,))],
        *(pltpu.with_memory_space_constraint(a, pltpu.HBM) for a in inputs),
        space=pltpu.HBM,
    )
    y_packets = exchange(first, second, "gy")
    (spread,) = call(spread_kernel, [(across * count, Z // 2, X)], [], main, coarse)
    spread = lax.all_to_all(spread, ("gx", "gy"), 0, 0, tiled=True)

    tiles = tiles_for(6 * rows + 2 * OWN + 1)
    own_x = exchange(
        *call(
            functools.partial(pack_own_kernel, rows),
            [(tiles, Z, X), (tiles, Z, X)],
            [(PER * tiles, Z, X)],
            main,
            coarse,
        ),
        "gx",
    )
    tiles = tiles_for(2 * PACKET)
    corner_x = exchange(
        *call(pack_corner_kernel, [(tiles, Z, X), (tiles, Z, X)], [(PER * tiles, Z, X)], *y_packets), "gx"
    )

    strip, edge = (FAR + 2, Z, X), (EDGE_TILES, Z, X)
    pair0 = (2, 2, total0, Z, X)
    keep0, powers, sources = call(
        functools.partial(level0_kernel, rows),
        [(6, 2, total0, Z, X), (3, *pair0), (4, 2, OWN, Z, X)],
        [(6, 2, total0, Z, X), pair0],
        main,
        *y_packets,
        *own_x,
        *corner_x,
    )
    own, first, second, gain = call(
        combine_kernel,
        [(2, OWN, Z, X), strip, strip, (POWERS + 3, Z, X)],
        [],
        sources,
        *y_packets,
        *corner_x,
        spread,
    )
    coef1, iterate, edge_a, edge_b = call(
        functools.partial(coarse1_kernel, rows),
        [(3, 2, SIZE1, Z, X), (2, 2, rows, Z, X), edge, edge],
        [(2, 2 * GROUPS1, Z, X)],
        coarse,
        *y_packets,
        *own_x,
        *corner_x,
        gain,
        powers,
    )
    b_packets = exchange(first, second, "gy")

    one, two, up = (2, SIZE1, Z, X), (2, SIZE2, Z, X), (2, SIZE_UP, Z, X)
    near = (EDGES + EDGE_TILES, Z, X)
    packet, first, second, keep1 = call(
        level1_kernel,
        [(2, Z, X), near, near, (2, *one)],
        [one, one],
        own,
        *b_packets,
        edge_a,
        edge_b,
        coef1,
        gain,
    )
    far = (swap_far(packet, "gy", 1), swap_far(packet, "gy", -1))
    near = exchange(first, second, "gy")
    (coef2,) = call(
        functools.partial(coarse2_kernel, rows),
        [(2, 2, SIZE2, Z, X)],
        [],
        coarse,
        *y_packets,
        *own_x,
        *corner_x,
        *b_packets,
    )

    (out,) = call(
        rest_kernel,
        [(2 * Z * rows, X)],
        [one, two, two, two, two, up, up, pair0, pair0, pair0],
        packet,
        *near,
        *far,
        gain,
        coef1,
        coef2,
        keep0,
        iterate,
        keep1,
    )
    return out.reshape(2, Z, rows, X)


def solution(mesh):
    placed = (
        P(None, None, "gy", "gx"),
        P(None, None, "gy", "gx"),
        P(None, "gy", "gx"),
        P(None, "gy", "gx"),
    )
    return jax.shard_map(
        body, mesh=mesh, in_specs=placed, out_specs=P(None, None, "gy", "gx"), check_vma=False
    )
```

```python
import functools

import jax
import jax.numpy as jnp
from jax import lax
from jax.experimental import pallas as pl
from jax.experimental.pallas import tpu as pltpu
from jax.sharding import PartitionSpec as P

DIFF = (40.0, 20.0)
INV_STEP = 2.0
LOWER = 0.25

_CENTRE = (1.0 + LOWER) / 2.0
_HALF = (1.0 - LOWER) / 2.0
_SIGMA = _CENTRE / _HALF
_RHO0 = 1.0 / _SIGMA
_RHO1 = 1.0 / (2.0 * _SIGMA - _RHO0)
_RHO2 = 1.0 / (2.0 * _SIGMA - _RHO1)

Z = 8
X = 128
HALO0 = 4
HALOS = (4, 4, 3, 3, 3, 3)
STARTS = tuple(sum(HALOS[:i]) for i in range(6))
FIELDS1 = sum(HALOS)
FIELDS2 = FIELDS1 + 8
PACKET = FIELDS2 + 1
WIDE = 42
PER = X // WIDE
EDGE = 3

LO1, HI1 = -4, 8
LO2, HI2 = -2, 3
LO_UP, HI_UP = -3, 7
SIZE1, SIZE2, SIZE_UP = HI1 - LO1 + 2, HI2 - LO2 + 2, HI_UP - LO_UP + 2
OWN = 4


def lane_of():
    return lax.broadcasted_iota(jnp.int32, (1, Z, X), 2)


def sub_of():
    return lax.broadcasted_iota(jnp.int32, (1, Z, X), 1)


def roll_x(tile, shift):
    shift = shift % X
    return pltpu.roll(tile, shift, 2) if shift else tile


def roll_z(tile, shift):
    shift = shift % Z
    return pltpu.roll(tile, shift, 1) if shift else tile


def rows_loop(lo, hi, body, step=None):
    step = step or (hi - lo) // 2
    full = (hi - lo) // step
    if full == 1:
        body(lo, step)
    elif full > 1:

        def trip(i, carry):
            body(lo + i * step, step)
            return carry

        lax.fori_loop(0, full, trip, 0)
    rest = hi - lo - full * step
    if rest:
        body(hi - rest, rest)


def neighbour_sums(read, r, n, k):
    lane = lane_of()
    low, high = lane < k, lane >= X - k
    centre = [read(t, r, n) for t in (0, 1)]
    right = [roll_x(c, k) for c in centre]
    left = [roll_x(c, -k) for c in centre]
    sums = []
    for t in (0, 1):
        c = centre[t]
        along_x = jnp.where(low, right[1 - t], right[t]) + jnp.where(high, left[1 - t], left[t])
        along_y = read(t, r - 1, n) + read(t, r + 1, n)
        along_z = 2.0 * roll_z(c, k) if 2 * k == Z else roll_z(c, k) + roll_z(c, -k)
        sums.append(along_x + along_y + along_z)
    return centre, sums


def jacobian(u, v, f, k, level):
    scale = 0.25**level
    product = u * v
    squared = v * v
    first = INV_STEP + squared + f + 6.0 * DIFF[0] * scale
    second = INV_STEP + f + k - 2.0 * product + 6.0 * DIFF[1] * scale
    return 2.0 * product, squared, 1.0 / first, 1.0 / second, first, second


def cheb_step(level, keep, source, target, d, r, n, carry, gain):
    scale = 0.25**level
    k = 1 << level
    u, nb_u = neighbour_sums(lambda t, a, m: source[0, t, pl.ds(a, m)], r, n, k)
    v, nb_v = neighbour_sums(lambda t, a, m: source[1, t, pl.ds(a, m)], r, n, k)
    rows = pl.ds(r, n)
    for t in (0, 1):
        cross, squared, inv_u, inv_v = (keep[i, t, rows] for i in range(4))
        res_u = inv_u * (keep[4, t, rows] - cross * v[t] + DIFF[0] * scale * nb_u[t]) - u[t]
        res_v = inv_v * (keep[5, t, rows] + squared * u[t] + DIFF[1] * scale * nb_v[t]) - v[t]
        du, dv = gain * res_u, gain * res_v
        if carry is not None:
            du = du + carry * d[0, t, rows]
            dv = dv + carry * d[1, t, rows]
        d[0, t, rows] = du
        d[1, t, rows] = dv
        target[0, t, rows] = u[t] + du
        target[1, t, rows] = v[t] + dv


def next_power(keep, source, r, n):
    u, nb_u = neighbour_sums(lambda t, a, m: source[0, t, pl.ds(a, m)], r, n, 1)
    v, nb_v = neighbour_sums(lambda t, a, m: source[1, t, pl.ds(a, m)], r, n, 1)
    rows = pl.ds(r, n)
    first, second = [], []
    for t in (0, 1):
        cross, squared, inv_u, inv_v = (keep[i, t, rows] for i in range(4))
        first.append(u[t] + inv_u * (cross * v[t] - DIFF[0] * nb_u[t]))
        second.append(v[t] - inv_v * (squared * u[t] + DIFF[1] * nb_v[t]))
    return first, second


CARRY1 = _RHO1 * _RHO0
CARRY2 = _RHO2 * _RHO1


POWERS = 9


def write_gains(spread, out):
    lane = lax.broadcasted_iota(jnp.int32, (1, X), 1)
    for level in range(3):
        top = jnp.max(jnp.where(lane == level, spread, 0.0), axis=1, keepdims=True)
        tau = 1.0 / (1.0 + jnp.broadcast_to(top, (Z, X)))
        for i, factor in enumerate((1.0 / _CENTRE, 2.0 * _RHO1 / _HALF, 2.0 * _RHO2 / _HALF)):
            out[3 * level + i] = factor * tau
    g0, g1, g2 = (out[i] for i in range(3))
    first, second = g0 + CARRY1 * g0 + g1, g1 * g0
    out[POWERS] = first + CARRY2 * (CARRY1 * g0 + g1) + g2
    out[POWERS + 1] = second + CARRY2 * second + g2 * first
    out[POWERS + 2] = g2 * second


def pair_rows(value):
    n = value.shape[0] // 2
    pairs = value.reshape(n, 2, Z, X)
    return pairs[:, 0] + pairs[:, 1]


def restrict_01(first, second):
    lane, sub = lane_of(), sub_of()
    across = []
    for value in (first, second):
        a, b = value[0:1], value[1:2]
        across.append(jnp.where((lane & 1) == 0, a + roll_x(a, -1), b + roll_x(b, 1)))
    a, b = across
    return 0.125 * jnp.where((sub & 1) == 0, a + roll_z(a, -1), b + roll_z(b, 1))


def restrict_12(groups):
    lane, sub = lane_of(), sub_of()
    out = None
    for p, value in enumerate(groups):
        value = value + roll_x(value, 1 if p & 1 else -1)
        value = value + roll_x(value, 2 if p & 2 else -2)
        out = value if out is None else jnp.where((lane & 3) == p, value, out)
    return 0.125 * (out + jnp.where((sub & 2) == 0, roll_z(out, -2), roll_z(out, 2)))


def spread_x(tile, k, phase):
    return jnp.where((lane_of() & k) == phase, tile, roll_x(tile, -k if phase else k))


def packed_jacobian(uv, fk, level):
    scale = 0.25**level
    even = (sub_of() & 1) == 0
    u, v = jnp.where(even, uv, roll_z(uv, 1)), jnp.where(even, roll_z(uv, -1), uv)
    f, k = jnp.where(even, fk, roll_z(fk, 1)), jnp.where(even, roll_z(fk, -1), fk)
    product, squared = u * v, v * v
    diag = jnp.where(
        even,
        INV_STEP + squared + f + 6.0 * DIFF[0] * scale,
        INV_STEP + f + k - 2.0 * product + 6.0 * DIFF[1] * scale,
    )
    return 1.0 / diag, jnp.where(even, -2.0 * product, squared), diag


def packed_spread(uv, fk, level):
    scale = 0.25**level
    even = (sub_of() & 1) == 0
    inverse, other, _ = packed_jacobian(uv, fk, level)
    return jnp.where(even, 6.0 * DIFF[0] * scale - other, 6.0 * DIFF[1] * scale + other) * inverse


def packed_terms(source, g, n, level):
    k = 1 << level
    lane, sub = lane_of(), sub_of()
    even = (sub & 1) == 0
    first, last = (lane & (k - 1)) == 0, (lane & (k - 1)) == k - 1
    low, high = lane < k, lane >= X - k
    diff = jnp.where(even, DIFF[0] * 0.25**level, DIFF[1] * 0.25**level)
    wide = [source[t, pl.ds(g - 1, n + 2)] for t in (0, 1)]
    centre = [w[1 : n + 1] for w in wide]
    right = [roll_x(c, k) for c in centre]
    left = [roll_x(c, -k) for c in centre]
    out = []
    for t in (0, 1):
        c, w = centre[t], wide[t]
        total = jnp.where(low, right[1 - t], right[t]) + jnp.where(high, left[1 - t], left[t])
        if k == 2:
            ahead, back = roll_x(w, 1), roll_x(w, -1)
            total = total + jnp.where(first, back[0:n], ahead[1 : n + 1])
            total = total + jnp.where(last, ahead[2 : n + 2], back[1 : n + 1])
            total = total + roll_z(c, 2) + roll_z(c, -2)
        else:
            total = total + jnp.where(first, roll_x(w[0:n], -(k - 1)), roll_x(c, 1))
            total = total + jnp.where(last, roll_x(w[2 : n + 2], k - 1), roll_x(c, -1))
            total = total + 2.0 * roll_z(c, 4)
        other = jnp.where(even, roll_z(c, -1), roll_z(c, 1))
        out.append((c, other, diff * total))
    return out


def packed_first(coef, shift, b, target, d, g, n, gain):
    for t in (0, 1):
        value = gain * coef[0, t, pl.ds(g + shift, n)] * b[t, pl.ds(g + shift, n)]
        d[t, pl.ds(g, n)] = value
        target[t, pl.ds(g, n)] = value


def packed_step(level, coef, shift, b, source, target, d, g, n, carry, gain):
    for t, (c, other, spread) in enumerate(packed_terms(source, g, n, level)):
        at = pl.ds(g + shift, n)
        res = coef[0, t, at] * (b[t, at] + coef[1, t, at] * other + spread) - c
        delta = gain * res
        if carry is not None:
            delta = delta + carry * d[t, pl.ds(g, n)]
        d[t, pl.ds(g, n)] = delta
        target[t, pl.ds(g, n)] = c + delta


def plane(ref, f, y, rows):
    return ref[pl.ds(f * Z * rows + y, Z, stride=rows), :]


def is_even(axis):
    return lax.rem(lax.axis_index(axis), 2) == 0


def prev_of(even, first, second, at):
    return jnp.where(even, first[at], second[at])


def next_of(even, first, second, at):
    return jnp.where(even, second[at], first[at])


def first_kernel(rows, state, previous, feed, kill, first, second, main, coarse, *scratch):
    sources, sems = scratch[:4], scratch[4]
    copies = [
        pltpu.make_async_copy(ref, held, sems.at[i])
        for i, (ref, held) in enumerate(zip((state, previous, feed, kill), sources))
    ]
    for copy in copies:
        copy.start()
    for copy in copies:
        copy.wait()
    even = is_even("gy")
    state, previous, feed, kill = sources
    fields = [(state, 0), (state, 1), (previous, 0), (previous, 1), (feed, 0), (kill, 0)]
    for i, (ref, f) in enumerate(fields):
        for y in range(rows):
            main[i, y] = plane(ref, f, y, rows)
        top, bottom = main[i, 0 : HALOS[i]], main[i, rows - HALOS[i] : rows]
        at = slice(STARTS[i], STARTS[i] + HALOS[i])
        first[at] = jnp.where(even, top, bottom)
        second[at] = jnp.where(even, bottom, top)
    u, v, f, k = (main[i] for i in (0, 1, 4, 5))
    sums = [pair_rows(value) for value in (u, v, f, k)]
    pairs = []
    for p in (0, 1):
        values = [
            restrict_01(sums[2 * p][2 * g : 2 * g + 2], sums[2 * p + 1][2 * g : 2 * g + 2]) for g in range(OWN)
        ]
        pairs.append(jnp.concatenate(values, axis=0))
        coarse[p * OWN : (p + 1) * OWN] = pairs[p]
        for ref in (first, second):
            ref[FIELDS1 + p * OWN : FIELDS1 + (p + 1) * OWN] = pairs[p]

    uv, fk = (restrict_12([pair[j : j + 1] for j in range(OWN)]) for pair in pairs)
    both = jnp.where((sub_of() & 2) == 0, uv, fk)
    coarse[2 * OWN : 2 * OWN + 1] = both
    for ref in (first, second):
        ref[FIELDS2 : FIELDS2 + 1] = both


def split_fields2(both):
    low = (sub_of() & 2) == 0
    return jnp.where(low, both, roll_z(both, 2)), jnp.where(low, roll_z(both, -2), both)


def spread_kernel(main, coarse, out):
    lane = lax.broadcasted_iota(jnp.int32, (1, X), 1)
    u, v, f, k = (main[i] for i in (0, 1, 4, 5))
    cross, squared, inv_u, inv_v, _, _ = jacobian(u, v, f, k, 0)
    tops = [jnp.max(jnp.maximum((6.0 * DIFF[0] + cross) * inv_u, (6.0 * DIFF[1] + squared) * inv_v), axis=0)]
    tops.append(jnp.max(packed_spread(coarse[0:OWN], coarse[OWN : 2 * OWN], 1), axis=0))
    tops.append(packed_spread(*split_fields2(coarse[2 * OWN : 2 * OWN + 1]), 2)[0])
    result = jnp.zeros((1, X), jnp.float32)
    for level, top in enumerate(tops):
        top = jnp.max(jnp.max(top, axis=0, keepdims=True), axis=1, keepdims=True)
        result = jnp.where(lane == level, jnp.broadcast_to(top, (1, X)), result)
    out[...] = jnp.broadcast_to(result[None], out.shape)


GROUPS1 = HI1 - LO1
GROUPS2 = HI2 - LO2


def tiles_for(entries):
    return -(-entries // PER)


def pack_edges(entries, even, first, second):
    lane = lane_of()
    share = first.shape[0]
    left, right = None, None
    for j in range(PER):
        part = entries[j * share : (j + 1) * share]
        a, b = roll_x(part, WIDE * j), roll_x(part, WIDE + WIDE * j)
        left = a if left is None else jnp.where(lane >= WIDE * j, a, left)
        right = b if right is None else jnp.where(lane >= WIDE * j, b, right)
    first[...] = jnp.where(even, left, right)
    second[...] = jnp.where(even, right, left)


def halo_tiles(even, packets, lo, hi):
    first, second = packets
    share = first.shape[0]
    lane = lane_of()
    out = []
    for j in range(PER):
        a, b = max(lo, j * share), min(hi, (j + 1) * share)
        if a < b:
            strip = slice(a - j * share, b - j * share)
            left, right = prev_of(even, first, second, strip), next_of(even, first, second, strip)
            value = jnp.where(lane < X // 2, roll_x(right, -WIDE * j), roll_x(left, X - WIDE - WIDE * j))
            out.append((a - lo, b - lo, value))
    return out


def pack_own_kernel(rows, main, coarse, first, second, held):
    for i in range(6):
        held[i * rows : (i + 1) * rows] = main[i]
    held[6 * rows : 6 * rows + 2 * OWN + 1] = coarse[...]
    pack_edges(held, is_even("gx"), first, second)


def pack_corner_kernel(y_first, y_second, first, second, held):
    even = is_even("gy")
    every = slice(0, PACKET)
    held[0:PACKET] = prev_of(even, y_first, y_second, every)
    held[PACKET : 2 * PACKET] = next_of(even, y_first, y_second, every)
    pack_edges(held, is_even("gx"), first, second)


FAR = 2 * OWN
EDGES = 2
EDGE_TILES = 2 * EDGE + 1


def level0_kernel(
    rows, main, y_first, y_second, own_a, own_b, corner_a, corner_b, keep, powers, sources, fields, diag, y0
):
    even, even_x = is_even("gy"), is_even("gx")
    total = rows + 2 * HALO0
    own_x, corner_x = (own_a, own_b), (corner_a, corner_b)
    for i, halo in enumerate(HALOS):
        strip = slice(STARTS[i], STARTS[i] + halo)
        skip = HALO0 - halo
        fields[i, 0, skip:HALO0] = prev_of(even, y_first, y_second, strip)
        fields[i, 0, HALO0 : HALO0 + rows] = main[i]
        fields[i, 0, HALO0 + rows : total - skip] = next_of(even, y_first, y_second, strip)
        for packets, lo, n, at in (
            (corner_x, STARTS[i], halo, skip),
            (own_x, i * rows, rows, HALO0),
            (corner_x, PACKET + STARTS[i], halo, HALO0 + rows),
        ):
            for a, b, value in halo_tiles(even_x, packets, lo, lo + n):
                fields[i, 1, at + a : at + b] = value

    def setup(r, n):
        at = pl.ds(r, n)
        u, nb_u = neighbour_sums(lambda t, a, m: fields[0, t, pl.ds(a, m)], r, n, 1)
        v, nb_v = neighbour_sums(lambda t, a, m: fields[1, t, pl.ds(a, m)], r, n, 1)
        for t in (0, 1):
            f, k = fields[4, t, at], fields[5, t, at]
            cross, squared, inv_u, inv_v, first, second = jacobian(u[t], v[t], f, k, 0)
            react = u[t] * squared
            b_u = (
                DIFF[0] * (nb_u[t] - 6.0 * u[t])
                - INV_STEP * (u[t] - fields[2, t, at])
                - react
                + f * (1.0 - u[t])
            )
            b_v = (
                DIFF[1] * (nb_v[t] - 6.0 * v[t]) - INV_STEP * (v[t] - fields[3, t, at]) + react - (f + k) * v[t]
            )
            for i, value in enumerate((cross, squared, inv_u, inv_v, b_u, b_v)):
                keep[i, t, at] = value
            diag[0, t, at] = first
            diag[1, t, at] = second
            y0[0, t, at] = inv_u * b_u
            y0[1, t, at] = inv_v * b_v

    rows_loop(1, total - 1, setup)
    for p in (0, 1):

        def power(r, n, p=p):
            for i, values in enumerate(next_power(keep, powers.at[0] if p else y0, r, n)):
                for t in (0, 1):
                    powers[p, i, t, pl.ds(r, n)] = values[t]

        rows_loop(2 + p, total - 2 - p, power)

    def down(r, n):
        at = pl.ds(r, n)
        last = next_power(keep, powers.at[1], r, n)
        for t in (0, 1):
            both = [diag[i, t, at] for i in (0, 1)]
            parts = [[keep[4 + i, t, at] for i in (0, 1)]]
            parts += [[both[i] * powers[p, i, t, at] for i in (0, 1)] for p in (0, 1)]
            parts.append([both[i] * last[i][t] for i in (0, 1)])
            for q, part in enumerate(parts):
                u, v = (pair_rows(value) for value in part)
                for j in range(n // 4):
                    value = restrict_01(u[2 * j : 2 * j + 2], v[2 * j : 2 * j + 2])
                    sources[q, t, pl.ds((r - HALO0) // 4 + j, 1)] = value

    rows_loop(HALO0, HALO0 + rows, down, 8)


def combine_kernel(sources, y_first, y_second, corner_a, corner_b, spread, own, first, second, gain):
    even, even_x = is_even("gy"), is_even("gx")
    write_gains(jnp.max(spread[...], axis=0)[0:1], gain)
    p0, p1, p2 = (gain[POWERS + i] for i in range(3))
    for t in (0, 1):
        value = sources[0, t] - p0 * sources[1, t] + p1 * sources[2, t] - p2 * sources[3, t]
        own[t] = value
        for ref in (first, second):
            ref[t * OWN : (t + 1) * OWN] = value
    strip = slice(FIELDS2, FIELDS2 + 1)
    for t in (0, 1):
        if t == 0:
            before, after = prev_of(even, y_first, y_second, strip), next_of(even, y_first, y_second, strip)
        else:
            before, after = (
                halo_tiles(even_x, (corner_a, corner_b), at + FIELDS2, at + FIELDS2 + 1)[0][2] for at in (0, PACKET)
            )
        first[FAR + t : FAR + t + 1] = jnp.where(even, after, before)
        second[FAR + t : FAR + t + 1] = jnp.where(even, before, after)


def coarse1_kernel(
    rows, coarse, y_first, y_second, own_a, own_b, corner_a, corner_b, gain, keep0, powers, coef, x0, edge_first, edge_second, fields
):
    even, even_x = is_even("gy"), is_even("gx")
    own_x, corner_x = (own_a, own_b), (corner_a, corner_b)
    for p in (0, 1):
        to = p * GROUPS1
        strip = slice(FIELDS1 + p * OWN, FIELDS1 + (p + 1) * OWN)
        fields[0, to : to + OWN] = prev_of(even, y_first, y_second, strip)
        fields[0, to + OWN : to + 2 * OWN] = coarse[p * OWN : (p + 1) * OWN]
        fields[0, to + 2 * OWN : to + 3 * OWN] = next_of(even, y_first, y_second, strip)
        for part, (packets, lo) in enumerate(
            ((corner_x, FIELDS1), (own_x, 6 * rows), (corner_x, PACKET + FIELDS1))
        ):
            lo += p * OWN
            for a, b, value in halo_tiles(even_x, packets, lo, lo + OWN):
                fields[1, to + part * OWN + a : to + part * OWN + b] = value
    for t in (0, 1):
        for i, value in enumerate(packed_jacobian(fields[t, 0:GROUPS1], fields[t, GROUPS1 : 2 * GROUPS1], 1)):
            coef[i, t, 1 : SIZE1 - 1] = value

    p0, p1, p2 = (gain[POWERS + i] for i in range(3))
    for i in (0, 1):
        for t in (0, 1):
            y0 = keep0[2 + i, t, HALO0 : HALO0 + rows] * keep0[4 + i, t, HALO0 : HALO0 + rows]
            y1, y2 = (powers[p, i, t, HALO0 : HALO0 + rows] for p in (0, 1))
            x0[i, t] = p0 * y0 - p1 * y1 + p2 * y2
    lane = lane_of()
    edges = []
    for start in (0, rows - EDGE):
        halo = None
        for i in (0, 1):
            for j in range(EDGE):
                at = i * EDGE + j
                value = roll_x(x0[i, 1, start + j : start + j + 1], 4 + 8 * at)
                halo = value if halo is None else jnp.where((lane >> 3) == at, value, halo)
        edges.append([x0[0, 0, start : start + EDGE], x0[1, 0, start : start + EDGE], halo])
    top, bottom = (jnp.concatenate(parts, axis=0) for parts in edges)
    edge_first[...] = jnp.where(even, top, bottom)
    edge_second[...] = jnp.where(even, bottom, top)


def coarse2_kernel(
    rows, coarse, y_first, y_second, own_a, own_b, corner_a, corner_b, b_first, b_second, coef
):
    even, even_x = is_even("gy"), is_even("gx")
    own_x, corner_x = (own_a, own_b), (corner_a, corner_b)
    near = slice(FIELDS2, FIELDS2 + 1)
    for t in (0, 1):
        far = slice(FAR + t, FAR + t + 1)
        if t == 0:
            middle = [
                prev_of(even, y_first, y_second, near),
                coarse[2 * OWN : 2 * OWN + 1],
                next_of(even, y_first, y_second, near),
            ]
        else:
            middle = [
                halo_tiles(even_x, packets, lo, lo + 1)[0][2]
                for packets, lo in ((corner_x, FIELDS2), (own_x, 6 * rows + 2 * OWN), (corner_x, PACKET + FIELDS2))
            ]
        parts = [prev_of(even, b_first, b_second, far), *middle, next_of(even, b_first, b_second, far)]
        inverse, other, _ = packed_jacobian(*split_fields2(jnp.concatenate(parts, axis=0)), 2)
        coef[0, t, 1 : SIZE2 - 1] = inverse
        coef[1, t, 1 : SIZE2 - 1] = other


def level1_kernel(own, first, second, edge_a, edge_b, coef1, gain, packet, to_first, to_second, keep, y1, d1):
    b1, x1 = keep.at[0], keep.at[1]
    even = is_even("gy")
    for t in (0, 1):
        b1[t, 1 + OWN : 1 + 2 * OWN] = own[t]
        strip = slice(t * OWN, (t + 1) * OWN)
        b1[t, 1 : 1 + OWN] = prev_of(even, first, second, strip)
        b1[t, 1 + 2 * OWN : 1 + 3 * OWN] = next_of(even, first, second, strip)
    g0, g1, g2 = (gain[3 + i] for i in range(3))
    n = GROUPS1
    packed_first(coef1, 0, b1, x1, d1, 1, n, g0)
    packed_step(1, coef1, 0, b1, x1, y1, d1, 1, n, CARRY1, g1)
    packed_step(1, coef1, 0, b1, y1, x1, d1, 1, n, CARRY2, g2)
    here = pl.ds(1 + OWN, OWN)
    for t, (c, other, spread) in enumerate(packed_terms(x1, 1 + OWN, OWN, 1)):
        res = b1[t, here] - coef1[2, t, here] * c + coef1[1, t, here] * other + spread
        value = restrict_12([res[j : j + 1] for j in range(OWN)])
        for ref in (packet, to_first, to_second):
            ref[t : t + 1] = value
    to_first[EDGES : EDGES + EDGE_TILES] = edge_a[...]
    to_second[EDGES : EDGES + EDGE_TILES] = edge_b[...]


def rest_kernel(
    own2, near_a, near_b, far_a, far_b, gain, coef1, coef2, keep0, iterate, keep1, out, d1, b2, x2, y2, d2, xu, yu, x0, y0, d0
):
    rows = out.shape[0] // (2 * Z)
    even = (sub_of() & 1) == 0
    b1, x1 = keep1.at[0], keep1.at[1]

    even_y, low = is_even("gy"), lax.rem(lax.axis_index("gy"), 4) < 2
    for t in (0, 1):
        at = slice(t, t + 1)
        parts = [
            next_of(low, far_a, far_b, at),
            prev_of(even_y, near_a, near_b, at),
            own2[at],
            next_of(even_y, near_a, near_b, at),
            prev_of(low, far_a, far_b, at),
        ]
        b2[t, 1 : SIZE2 - 1] = jnp.concatenate(parts, axis=0)

    n = HI2 - LO2
    g0, g1, g2 = (gain[6 + i] for i in range(3))
    packed_first(coef2, 0, b2, x2, d2, 1, n, g0)
    packed_step(2, coef2, 0, b2, x2, y2, d2, 1, n, CARRY1, g1)
    packed_step(2, coef2, 0, b2, y2, x2, d2, 1, n, CARRY2, g2)
    packed_step(2, coef2, 0, b2, x2, y2, d2, 1, n, None, g0)
    packed_step(2, coef2, 0, b2, y2, x2, d2, 1, n, CARRY1, g1)
    packed_step(2, coef2, 0, b2, x2, y2, d2, 1, n, CARRY2, g2)

    g0, g1, g2 = (gain[3 + i] for i in range(3))
    shift = LO_UP - LO1
    for t in (0, 1):
        for g in range(LO_UP, HI_UP):
            p = g % 4
            value = y2[t, g // 4 - LO2 + 1 : g // 4 - LO2 + 2]
            value = spread_x(spread_x(value, 1, p & 1), 2, p & 2)
            at = g - LO_UP + 1
            xu[t, at : at + 1] = x1[t, at + shift : at + shift + 1] + value
    n = HI_UP - LO_UP
    packed_step(1, coef1, shift, b1, xu, yu, d1, 1, n, None, g0)
    packed_step(1, coef1, shift, b1, yu, xu, d1, 1, n, CARRY1, g1)
    packed_step(1, coef1, shift, b1, xu, yu, d1, 1, n, CARRY2, g2)

    g0, g1, g2 = (gain[i] for i in range(3))
    last = EDGES + 2 * EDGE
    for i in (0, 1):
        for at, take in ((HALO0 - EDGE, prev_of), (HALO0 + rows, next_of)):
            strip = slice(EDGES + i * EDGE, EDGES + (i + 1) * EDGE)
            x0[i, 0, at : at + EDGE] = take(even_y, near_a, near_b, strip)
            sides = take(even_y, near_a, near_b, slice(last, last + 1))
            for j in range(EDGE):
                x0[i, 1, at + j : at + j + 1] = roll_x(sides, -(4 + 8 * (i * EDGE + j)))
        for t in (0, 1):
            x0[i, t, HALO0 : HALO0 + rows] = iterate[i, t]
    for t in (0, 1):
        for row in range(-2, rows // 2 + 2):
            at = row // 2 - LO_UP + 1
            value = spread_x(yu[t, at : at + 1], 1, row & 1)
            for i, fine in enumerate((jnp.where(even, value, roll_z(value, 1)), jnp.where(even, roll_z(value, -1), value))):
                for y in (2 * row, 2 * row + 1):
                    if -EDGE <= y < rows + EDGE:
                        x0[i, t, y + HALO0 : y + HALO0 + 1] = x0[i, t, y + HALO0 : y + HALO0 + 1] + fine
    total = rows + 2 * HALO0
    rows_loop(2, total - 2, lambda r, n: cheb_step(0, keep0, x0, y0, d0, r, n, None, g0))
    rows_loop(3, total - 3, lambda r, n: cheb_step(0, keep0, y0, x0, d0, r, n, CARRY1, g1))
    rows_loop(4, total - 4, lambda r, n: cheb_step(0, keep0, x0, y0, d0, r, n, CARRY2, g2))
    for i in (0, 1):
        for y in range(rows):
            out[pl.ds(i * Z * rows + y, Z, stride=rows), :] = y0[i, 0, HALO0 + y]


def call(kernel, out_shapes, scratch, *args, space=pltpu.VMEM):
    out = [jax.ShapeDtypeStruct(shape, jnp.float32) for shape in out_shapes]
    return pl.pallas_call(
        kernel,
        out_shape=out,
        in_specs=[pl.BlockSpec(memory_space=space)] * len(args),
        out_specs=[pl.BlockSpec(memory_space=pltpu.VMEM)] * len(out),
        scratch_shapes=[pltpu.VMEM(s, jnp.float32) if isinstance(s, tuple) else s for s in scratch],
        compiler_params=pltpu.CompilerParams(vmem_limit_bytes=24 * 2**20),
    )(*args)


def swap(value, axis, step):
    count = lax.axis_size(axis)
    assert count % 2 == 0
    pairs = [(i, (i + step) % count) for i in range(0, count, 2)]
    return lax.ppermute(value, axis, pairs + [(j, i) for i, j in pairs])


def swap_far(value, axis, step):
    count = lax.axis_size(axis)
    assert count % 4 == 0
    pairs = [(i + j, (i + j + 2 * step) % count) for i in range(0, count, 4) for j in (0, 1)]
    return lax.ppermute(value, axis, pairs + [(j, i) for i, j in pairs])


def exchange(first, second, axis):
    return swap(first, axis, -1), swap(second, axis, 1)


def body(state, previous, feed, kill):
    _, depth, rows, cols = state.shape
    assert depth == Z and cols == X and rows == 4 * OWN
    across, count = lax.axis_size("gx"), lax.axis_size("gy")
    total0 = rows + 2 * HALO0
    state = state.reshape(2 * Z * rows, X)
    previous = previous.reshape(2 * Z * rows, X)
    feed = feed.reshape(Z * rows, X)
    kill = kill.reshape(Z * rows, X)
    inputs = (state, previous, feed, kill)

    strip = (FIELDS2 + 1, Z, X)
    first, second, main, coarse = call(
        functools.partial(first_kernel, rows),
        [strip, strip, (6, rows, Z, X), (2 * OWN + 1, Z, X)],
        [*(a.shape for a in inputs), pltpu.SemaphoreType.DMA((4,))],
        *(pltpu.with_memory_space_constraint(a, pltpu.HBM) for a in inputs),
        space=pltpu.HBM,
    )
    y_packets = exchange(first, second, "gy")
    (spread,) = call(spread_kernel, [(across * count, Z // 2, X)], [], main, coarse)
    spread = lax.all_to_all(spread, ("gx", "gy"), 0, 0, tiled=True)

    tiles = tiles_for(6 * rows + 2 * OWN + 1)
    own_x = exchange(
        *call(
            functools.partial(pack_own_kernel, rows),
            [(tiles, Z, X), (tiles, Z, X)],
            [(PER * tiles, Z, X)],
            main,
            coarse,
        ),
        "gx",
    )
    tiles = tiles_for(2 * PACKET)
    corner_x = exchange(
        *call(pack_corner_kernel, [(tiles, Z, X), (tiles, Z, X)], [(PER * tiles, Z, X)], *y_packets), "gx"
    )

    strip, edge = (FAR + 2, Z, X), (EDGE_TILES, Z, X)
    pair0 = (2, 2, total0, Z, X)
    keep0, powers, sources = call(
        functools.partial(level0_kernel, rows),
        [(6, 2, total0, Z, X), (2, *pair0), (4, 2, OWN, Z, X)],
        [(6, 2, total0, Z, X), pair0, pair0],
        main,
        *y_packets,
        *own_x,
        *corner_x,
    )
    own, first, second, gain = call(
        combine_kernel,
        [(2, OWN, Z, X), strip, strip, (POWERS + 3, Z, X)],
        [],
        sources,
        *y_packets,
        *corner_x,
        spread,
    )
    coef1, iterate, edge_a, edge_b = call(
        functools.partial(coarse1_kernel, rows),
        [(3, 2, SIZE1, Z, X), (2, 2, rows, Z, X), edge, edge],
        [(2, 2 * GROUPS1, Z, X)],
        coarse,
        *y_packets,
        *own_x,
        *corner_x,
        gain,
        keep0,
        powers,
    )
    b_packets = exchange(first, second, "gy")

    one, two, up = (2, SIZE1, Z, X), (2, SIZE2, Z, X), (2, SIZE_UP, Z, X)
    near = (EDGES + EDGE_TILES, Z, X)
    packet, first, second, keep1 = call(
        level1_kernel,
        [(2, Z, X), near, near, (2, *one)],
        [one, one],
        own,
        *b_packets,
        edge_a,
        edge_b,
        coef1,
        gain,
    )
    far = (swap_far(packet, "gy", 1), swap_far(packet, "gy", -1))
    near = exchange(first, second, "gy")
    (coef2,) = call(
        functools.partial(coarse2_kernel, rows),
        [(2, 2, SIZE2, Z, X)],
        [],
        coarse,
        *y_packets,
        *own_x,
        *corner_x,
        *b_packets,
    )

    (out,) = call(
        rest_kernel,
        [(2 * Z * rows, X)],
        [one, two, two, two, two, up, up, pair0, pair0, pair0],
        packet,
        *near,
        *far,
        gain,
        coef1,
        coef2,
        keep0,
        iterate,
        keep1,
    )
    return out.reshape(2, Z, rows, X)


def solution(mesh):
    placed = (
        P(None, None, "gy", "gx"),
        P(None, None, "gy", "gx"),
        P(None, "gy", "gx"),
        P(None, "gy", "gx"),
    )
    return jax.shard_map(
        body, mesh=mesh, in_specs=placed, out_specs=P(None, None, "gy", "gx"), check_vma=False
    )
```

```python
import functools

import jax
import jax.numpy as jnp
from jax import lax
from jax.experimental import pallas as pl
from jax.experimental.pallas import tpu as pltpu
from jax.sharding import PartitionSpec as P

DIFF = (40.0, 20.0)
INV_STEP = 2.0
LOWER = 0.25

_CENTRE = (1.0 + LOWER) / 2.0
_HALF = (1.0 - LOWER) / 2.0
_SIGMA = _CENTRE / _HALF
_RHO0 = 1.0 / _SIGMA
_RHO1 = 1.0 / (2.0 * _SIGMA - _RHO0)
_RHO2 = 1.0 / (2.0 * _SIGMA - _RHO1)

Z = 8
X = 128
HALO0 = 4
HALOS = (4, 4, 3, 3, 3, 3)
STARTS = tuple(sum(HALOS[:i]) for i in range(6))
FIELDS1 = sum(HALOS)
FIELDS2 = FIELDS1 + 8
PACKET = FIELDS2 + 1
WIDE = 42
PER = X // WIDE
EDGE = 3

LO1, HI1 = -4, 8
LO2, HI2 = -2, 3
LO_UP, HI_UP = -3, 7
SIZE1, SIZE2, SIZE_UP = HI1 - LO1 + 2, HI2 - LO2 + 2, HI_UP - LO_UP + 2
OWN = 4


def lane_of():
    return lax.broadcasted_iota(jnp.int32, (1, Z, X), 2)


def sub_of():
    return lax.broadcasted_iota(jnp.int32, (1, Z, X), 1)


def roll_x(tile, shift):
    shift = shift % X
    return pltpu.roll(tile, shift, 2) if shift else tile


def roll_z(tile, shift):
    shift = shift % Z
    return pltpu.roll(tile, shift, 1) if shift else tile


def rows_loop(lo, hi, body, step=None):
    step = step or hi - lo
    full = (hi - lo) // step
    if full == 1:
        body(lo, step)
    elif full > 1:

        def trip(i, carry):
            body(lo + i * step, step)
            return carry

        lax.fori_loop(0, full, trip, 0)
    rest = hi - lo - full * step
    if rest:
        body(hi - rest, rest)


def neighbour_sums(read, r, n, k):
    lane = lane_of()
    low, high = lane < k, lane >= X - k
    centre = [read(t, r, n) for t in (0, 1)]
    right = [roll_x(c, k) for c in centre]
    left = [roll_x(c, -k) for c in centre]
    sums = []
    for t in (0, 1):
        c = centre[t]
        along_x = jnp.where(low, right[1 - t], right[t]) + jnp.where(high, left[1 - t], left[t])
        along_y = read(t, r - 1, n) + read(t, r + 1, n)
        along_z = 2.0 * roll_z(c, k) if 2 * k == Z else roll_z(c, k) + roll_z(c, -k)
        sums.append(along_x + along_y + along_z)
    return centre, sums


def jacobian(u, v, f, k, level):
    scale = 0.25**level
    product = u * v
    squared = v * v
    first = INV_STEP + squared + f + 6.0 * DIFF[0] * scale
    second = INV_STEP + f + k - 2.0 * product + 6.0 * DIFF[1] * scale
    return 2.0 * product, squared, 1.0 / first, 1.0 / second, first, second


def cheb_step(level, keep, source, target, d, r, n, carry, gain):
    scale = 0.25**level
    k = 1 << level
    u, nb_u = neighbour_sums(lambda t, a, m: source[0, t, pl.ds(a, m)], r, n, k)
    v, nb_v = neighbour_sums(lambda t, a, m: source[1, t, pl.ds(a, m)], r, n, k)
    rows = pl.ds(r, n)
    for t in (0, 1):
        cross, squared, inv_u, inv_v = (keep[i, t, rows] for i in range(4))
        res_u = inv_u * (keep[4, t, rows] - cross * v[t] + DIFF[0] * scale * nb_u[t]) - u[t]
        res_v = inv_v * (keep[5, t, rows] + squared * u[t] + DIFF[1] * scale * nb_v[t]) - v[t]
        du, dv = gain * res_u, gain * res_v
        if carry is not None:
            du = du + carry * d[0, t, rows]
            dv = dv + carry * d[1, t, rows]
        d[0, t, rows] = du
        d[1, t, rows] = dv
        target[0, t, rows] = u[t] + du
        target[1, t, rows] = v[t] + dv


def next_power(keep, source, r, n):
    u, nb_u = neighbour_sums(lambda t, a, m: source[0, t, pl.ds(a, m)], r, n, 1)
    v, nb_v = neighbour_sums(lambda t, a, m: source[1, t, pl.ds(a, m)], r, n, 1)
    rows = pl.ds(r, n)
    first, second = [], []
    for t in (0, 1):
        cross, squared, inv_u, inv_v = (keep[i, t, rows] for i in range(4))
        first.append(u[t] + inv_u * (cross * v[t] - DIFF[0] * nb_u[t]))
        second.append(v[t] - inv_v * (squared * u[t] + DIFF[1] * nb_v[t]))
    return first, second


CARRY1 = _RHO1 * _RHO0
CARRY2 = _RHO2 * _RHO1


POWERS = 9


def write_gains(spread, out):
    lane = lax.broadcasted_iota(jnp.int32, (1, X), 1)
    for level in range(3):
        top = jnp.max(jnp.where(lane == level, spread, 0.0), axis=1, keepdims=True)
        tau = 1.0 / (1.0 + jnp.broadcast_to(top, (Z, X)))
        for i, factor in enumerate((1.0 / _CENTRE, 2.0 * _RHO1 / _HALF, 2.0 * _RHO2 / _HALF)):
            out[3 * level + i] = factor * tau
    g0, g1, g2 = (out[i] for i in range(3))
    first, second = g0 + CARRY1 * g0 + g1, g1 * g0
    out[POWERS] = first + CARRY2 * (CARRY1 * g0 + g1) + g2
    out[POWERS + 1] = second + CARRY2 * second + g2 * first
    out[POWERS + 2] = g2 * second


def pair_rows(value):
    n = value.shape[0] // 2
    pairs = value.reshape(n, 2, Z, X)
    return pairs[:, 0] + pairs[:, 1]


def restrict_01(first, second):
    lane, sub = lane_of(), sub_of()
    across = []
    for value in (first, second):
        a, b = value[0:1], value[1:2]
        across.append(jnp.where((lane & 1) == 0, a + roll_x(a, -1), b + roll_x(b, 1)))
    a, b = across
    return 0.125 * jnp.where((sub & 1) == 0, a + roll_z(a, -1), b + roll_z(b, 1))


def restrict_12(groups):
    lane, sub = lane_of(), sub_of()
    out = None
    for p, value in enumerate(groups):
        value = value + roll_x(value, 1 if p & 1 else -1)
        value = value + roll_x(value, 2 if p & 2 else -2)
        out = value if out is None else jnp.where((lane & 3) == p, value, out)
    return 0.125 * (out + jnp.where((sub & 2) == 0, roll_z(out, -2), roll_z(out, 2)))


def spread_x(tile, k, phase):
    return jnp.where((lane_of() & k) == phase, tile, roll_x(tile, -k if phase else k))


def packed_jacobian(uv, fk, level):
    scale = 0.25**level
    even = (sub_of() & 1) == 0
    u, v = jnp.where(even, uv, roll_z(uv, 1)), jnp.where(even, roll_z(uv, -1), uv)
    f, k = jnp.where(even, fk, roll_z(fk, 1)), jnp.where(even, roll_z(fk, -1), fk)
    product, squared = u * v, v * v
    diag = jnp.where(
        even,
        INV_STEP + squared + f + 6.0 * DIFF[0] * scale,
        INV_STEP + f + k - 2.0 * product + 6.0 * DIFF[1] * scale,
    )
    return 1.0 / diag, jnp.where(even, -2.0 * product, squared), diag


def packed_spread(uv, fk, level):
    scale = 0.25**level
    even = (sub_of() & 1) == 0
    inverse, other, _ = packed_jacobian(uv, fk, level)
    return jnp.where(even, 6.0 * DIFF[0] * scale - other, 6.0 * DIFF[1] * scale + other) * inverse


def packed_terms(source, g, n, level):
    k = 1 << level
    lane, sub = lane_of(), sub_of()
    even = (sub & 1) == 0
    first, last = (lane & (k - 1)) == 0, (lane & (k - 1)) == k - 1
    low, high = lane < k, lane >= X - k
    diff = jnp.where(even, DIFF[0] * 0.25**level, DIFF[1] * 0.25**level)
    wide = [source[t, pl.ds(g - 1, n + 2)] for t in (0, 1)]
    centre = [w[1 : n + 1] for w in wide]
    right = [roll_x(c, k) for c in centre]
    left = [roll_x(c, -k) for c in centre]
    out = []
    for t in (0, 1):
        c, w = centre[t], wide[t]
        total = jnp.where(low, right[1 - t], right[t]) + jnp.where(high, left[1 - t], left[t])
        if k == 2:
            ahead, back = roll_x(w, 1), roll_x(w, -1)
            total = total + jnp.where(first, back[0:n], ahead[1 : n + 1])
            total = total + jnp.where(last, ahead[2 : n + 2], back[1 : n + 1])
            total = total + roll_z(c, 2) + roll_z(c, -2)
        else:
            total = total + jnp.where(first, roll_x(w[0:n], -(k - 1)), roll_x(c, 1))
            total = total + jnp.where(last, roll_x(w[2 : n + 2], k - 1), roll_x(c, -1))
            total = total + 2.0 * roll_z(c, 4)
        other = jnp.where(even, roll_z(c, -1), roll_z(c, 1))
        out.append((c, other, diff * total))
    return out


def packed_first(coef, shift, b, target, d, g, n, gain):
    for t in (0, 1):
        value = gain * coef[0, t, pl.ds(g + shift, n)] * b[t, pl.ds(g + shift, n)]
        d[t, pl.ds(g, n)] = value
        target[t, pl.ds(g, n)] = value


def packed_step(level, coef, shift, b, source, target, d, g, n, carry, gain):
    for t, (c, other, spread) in enumerate(packed_terms(source, g, n, level)):
        at = pl.ds(g + shift, n)
        res = coef[0, t, at] * (b[t, at] + coef[1, t, at] * other + spread) - c
        delta = gain * res
        if carry is not None:
            delta = delta + carry * d[t, pl.ds(g, n)]
        d[t, pl.ds(g, n)] = delta
        target[t, pl.ds(g, n)] = c + delta


def plane(ref, f, y, rows):
    return ref[pl.ds(f * Z * rows + y, Z, stride=rows), :]


def is_even(axis):
    return lax.rem(lax.axis_index(axis), 2) == 0


def prev_of(even, first, second, at):
    return jnp.where(even, first[at], second[at])


def next_of(even, first, second, at):
    return jnp.where(even, second[at], first[at])


def first_kernel(rows, state, previous, feed, kill, first, second, main, coarse, *scratch):
    sources, sems = scratch[:4], scratch[4]
    copies = [
        pltpu.make_async_copy(ref, held, sems.at[i])
        for i, (ref, held) in enumerate(zip((state, previous, feed, kill), sources))
    ]
    for copy in copies:
        copy.start()
    for copy in copies:
        copy.wait()
    even = is_even("gy")
    state, previous, feed, kill = sources
    fields = [(state, 0), (state, 1), (previous, 0), (previous, 1), (feed, 0), (kill, 0)]
    for i, (ref, f) in enumerate(fields):
        for y in range(rows):
            main[i, y] = plane(ref, f, y, rows)
        top, bottom = main[i, 0 : HALOS[i]], main[i, rows - HALOS[i] : rows]
        at = slice(STARTS[i], STARTS[i] + HALOS[i])
        first[at] = jnp.where(even, top, bottom)
        second[at] = jnp.where(even, bottom, top)
    u, v, f, k = (main[i] for i in (0, 1, 4, 5))
    sums = [pair_rows(value) for value in (u, v, f, k)]
    pairs = []
    for p in (0, 1):
        values = [
            restrict_01(sums[2 * p][2 * g : 2 * g + 2], sums[2 * p + 1][2 * g : 2 * g + 2]) for g in range(OWN)
        ]
        pairs.append(jnp.concatenate(values, axis=0))
        coarse[p * OWN : (p + 1) * OWN] = pairs[p]
        for ref in (first, second):
            ref[FIELDS1 + p * OWN : FIELDS1 + (p + 1) * OWN] = pairs[p]

    uv, fk = (restrict_12([pair[j : j + 1] for j in range(OWN)]) for pair in pairs)
    both = jnp.where((sub_of() & 2) == 0, uv, fk)
    coarse[2 * OWN : 2 * OWN + 1] = both
    for ref in (first, second):
        ref[FIELDS2 : FIELDS2 + 1] = both


def split_fields2(both):
    low = (sub_of() & 2) == 0
    return jnp.where(low, both, roll_z(both, 2)), jnp.where(low, roll_z(both, -2), both)


def spread_kernel(main, coarse, out):
    lane = lax.broadcasted_iota(jnp.int32, (1, X), 1)
    u, v, f, k = (main[i] for i in (0, 1, 4, 5))
    cross, squared, inv_u, inv_v, _, _ = jacobian(u, v, f, k, 0)
    tops = [jnp.max(jnp.maximum((6.0 * DIFF[0] + cross) * inv_u, (6.0 * DIFF[1] + squared) * inv_v), axis=0)]
    tops.append(jnp.max(packed_spread(coarse[0:OWN], coarse[OWN : 2 * OWN], 1), axis=0))
    tops.append(packed_spread(*split_fields2(coarse[2 * OWN : 2 * OWN + 1]), 2)[0])
    result = jnp.zeros((1, X), jnp.float32)
    for level, top in enumerate(tops):
        top = jnp.max(jnp.max(top, axis=0, keepdims=True), axis=1, keepdims=True)
        result = jnp.where(lane == level, jnp.broadcast_to(top, (1, X)), result)
    out[...] = jnp.broadcast_to(result[None], out.shape)


GROUPS1 = HI1 - LO1
GROUPS2 = HI2 - LO2


def tiles_for(entries):
    return -(-entries // PER)


def pack_edges(entries, even, first, second):
    lane = lane_of()
    share = first.shape[0]
    left, right = None, None
    for j in range(PER):
        part = entries[j * share : (j + 1) * share]
        a, b = roll_x(part, WIDE * j), roll_x(part, WIDE + WIDE * j)
        left = a if left is None else jnp.where(lane >= WIDE * j, a, left)
        right = b if right is None else jnp.where(lane >= WIDE * j, b, right)
    first[...] = jnp.where(even, left, right)
    second[...] = jnp.where(even, right, left)


def halo_tiles(even, packets, lo, hi):
    first, second = packets
    share = first.shape[0]
    lane = lane_of()
    out = []
    for j in range(PER):
        a, b = max(lo, j * share), min(hi, (j + 1) * share)
        if a < b:
            strip = slice(a - j * share, b - j * share)
            left, right = prev_of(even, first, second, strip), next_of(even, first, second, strip)
            value = jnp.where(lane < X // 2, roll_x(right, -WIDE * j), roll_x(left, X - WIDE - WIDE * j))
            out.append((a - lo, b - lo, value))
    return out


def pack_own_kernel(rows, main, coarse, first, second, held):
    for i in range(6):
        held[i * rows : (i + 1) * rows] = main[i]
    held[6 * rows : 6 * rows + 2 * OWN + 1] = coarse[...]
    pack_edges(held, is_even("gx"), first, second)


def pack_corner_kernel(y_first, y_second, first, second, held):
    even = is_even("gy")
    every = slice(0, PACKET)
    held[0:PACKET] = prev_of(even, y_first, y_second, every)
    held[PACKET : 2 * PACKET] = next_of(even, y_first, y_second, every)
    pack_edges(held, is_even("gx"), first, second)


FAR = 2
EDGES = 4
EDGE_TILES = 2 * EDGE + 1


def level0_kernel(
    rows, main, y_first, y_second, own_a, own_b, corner_a, corner_b, keep, powers, sources, fields, diag, y0
):
    even, even_x = is_even("gy"), is_even("gx")
    total = rows + 2 * HALO0
    own_x, corner_x = (own_a, own_b), (corner_a, corner_b)
    for i, halo in enumerate(HALOS):
        strip = slice(STARTS[i], STARTS[i] + halo)
        skip = HALO0 - halo
        fields[i, 0, skip:HALO0] = prev_of(even, y_first, y_second, strip)
        fields[i, 0, HALO0 : HALO0 + rows] = main[i]
        fields[i, 0, HALO0 + rows : total - skip] = next_of(even, y_first, y_second, strip)
        for packets, lo, n, at in (
            (corner_x, STARTS[i], halo, skip),
            (own_x, i * rows, rows, HALO0),
            (corner_x, PACKET + STARTS[i], halo, HALO0 + rows),
        ):
            for a, b, value in halo_tiles(even_x, packets, lo, lo + n):
                fields[i, 1, at + a : at + b] = value

    def setup(r, n):
        at = pl.ds(r, n)
        u, nb_u = neighbour_sums(lambda t, a, m: fields[0, t, pl.ds(a, m)], r, n, 1)
        v, nb_v = neighbour_sums(lambda t, a, m: fields[1, t, pl.ds(a, m)], r, n, 1)
        for t in (0, 1):
            f, k = fields[4, t, at], fields[5, t, at]
            cross, squared, inv_u, inv_v, first, second = jacobian(u[t], v[t], f, k, 0)
            react = u[t] * squared
            b_u = (
                DIFF[0] * (nb_u[t] - 6.0 * u[t])
                - INV_STEP * (u[t] - fields[2, t, at])
                - react
                + f * (1.0 - u[t])
            )
            b_v = (
                DIFF[1] * (nb_v[t] - 6.0 * v[t]) - INV_STEP * (v[t] - fields[3, t, at]) + react - (f + k) * v[t]
            )
            for i, value in enumerate((cross, squared, inv_u, inv_v, b_u, b_v)):
                keep[i, t, at] = value
            diag[0, t, at] = first
            diag[1, t, at] = second
            y0[0, t, at] = inv_u * b_u
            y0[1, t, at] = inv_v * b_v

    rows_loop(1, total - 1, setup)
    for p in (0, 1):

        def power(r, n, p=p):
            for i, values in enumerate(next_power(keep, powers.at[0] if p else y0, r, n)):
                for t in (0, 1):
                    powers[p, i, t, pl.ds(r, n)] = values[t]

        rows_loop(2 + p, total - 2 - p, power)

    def down(r, n):
        at = pl.ds(r, n)
        last = next_power(keep, powers.at[1], r, n)
        for t in (0, 1):
            both = [diag[i, t, at] for i in (0, 1)]
            parts = [[keep[4 + i, t, at] for i in (0, 1)]]
            parts += [[both[i] * powers[p, i, t, at] for i in (0, 1)] for p in (0, 1)]
            parts.append([both[i] * last[i][t] for i in (0, 1)])
            for q, part in enumerate(parts):
                u, v = (pair_rows(value) for value in part)
                for j in range(n // 4):
                    value = restrict_01(u[2 * j : 2 * j + 2], v[2 * j : 2 * j + 2])
                    sources[q, t, pl.ds((r - HALO0) // 4 + j, 1)] = value

    rows_loop(HALO0, HALO0 + rows, down)


def combine_kernel(sources, spread, own, first, second, gain):
    write_gains(jnp.max(spread[...], axis=0)[0:1], gain)
    p0, p1, p2 = (gain[POWERS + i] for i in range(3))
    for t in (0, 1):
        value = sources[0, t] - p0 * sources[1, t] + p1 * sources[2, t] - p2 * sources[3, t]
        own[t] = value
        for ref in (first, second):
            ref[t * OWN : (t + 1) * OWN] = value


def coarse1_kernel(
    rows, coarse, y_first, y_second, own_a, own_b, corner_a, corner_b, gain, keep0, powers, coef, x0, edge_first, edge_second, fields
):
    even, even_x = is_even("gy"), is_even("gx")
    own_x, corner_x = (own_a, own_b), (corner_a, corner_b)
    for p in (0, 1):
        to = p * GROUPS1
        strip = slice(FIELDS1 + p * OWN, FIELDS1 + (p + 1) * OWN)
        fields[0, to : to + OWN] = prev_of(even, y_first, y_second, strip)
        fields[0, to + OWN : to + 2 * OWN] = coarse[p * OWN : (p + 1) * OWN]
        fields[0, to + 2 * OWN : to + 3 * OWN] = next_of(even, y_first, y_second, strip)
        for part, (packets, lo) in enumerate(
            ((corner_x, FIELDS1), (own_x, 6 * rows), (corner_x, PACKET + FIELDS1))
        ):
            lo += p * OWN
            for a, b, value in halo_tiles(even_x, packets, lo, lo + OWN):
                fields[1, to + part * OWN + a : to + part * OWN + b] = value
    for t in (0, 1):
        for i, value in enumerate(packed_jacobian(fields[t, 0:GROUPS1], fields[t, GROUPS1 : 2 * GROUPS1], 1)):
            coef[i, t, 1 : SIZE1 - 1] = value

    p0, p1, p2 = (gain[POWERS + i] for i in range(3))
    for i in (0, 1):
        for t in (0, 1):
            y0 = keep0[2 + i, t, HALO0 : HALO0 + rows] * keep0[4 + i, t, HALO0 : HALO0 + rows]
            y1, y2 = (powers[p, i, t, HALO0 : HALO0 + rows] for p in (0, 1))
            x0[i, t] = p0 * y0 - p1 * y1 + p2 * y2
    lane = lane_of()
    edges = []
    for start in (0, rows - EDGE):
        halo = None
        for i in (0, 1):
            for j in range(EDGE):
                at = i * EDGE + j
                value = roll_x(x0[i, 1, start + j : start + j + 1], 4 + 8 * at)
                halo = value if halo is None else jnp.where((lane >> 3) == at, value, halo)
        edges.append([x0[0, 0, start : start + EDGE], x0[1, 0, start : start + EDGE], halo])
    top, bottom = (jnp.concatenate(parts, axis=0) for parts in edges)
    edge_first[2:] = jnp.where(even, top, bottom)
    edge_second[2:] = jnp.where(even, bottom, top)
    strip = slice(FIELDS2, FIELDS2 + 1)
    for t in (0, 1):
        if t == 0:
            before, after = prev_of(even, y_first, y_second, strip), next_of(even, y_first, y_second, strip)
        else:
            before, after = (
                halo_tiles(even_x, corner_x, at + FIELDS2, at + FIELDS2 + 1)[0][2] for at in (0, PACKET)
            )
        edge_first[t : t + 1] = jnp.where(even, after, before)
        edge_second[t : t + 1] = jnp.where(even, before, after)


def fields2_kernel(rows, coarse, y_first, y_second, own_a, own_b, corner_a, corner_b, out):
    even, even_x = is_even("gy"), is_even("gx")
    own_x, corner_x = (own_a, own_b), (corner_a, corner_b)
    near = slice(FIELDS2, FIELDS2 + 1)
    out[0, 0:1] = prev_of(even, y_first, y_second, near)
    out[0, 1:2] = coarse[2 * OWN : 2 * OWN + 1]
    out[0, 2:3] = next_of(even, y_first, y_second, near)
    for q, (packets, lo) in enumerate(
        ((corner_x, FIELDS2), (own_x, 6 * rows + 2 * OWN), (corner_x, PACKET + FIELDS2))
    ):
        out[1, q : q + 1] = halo_tiles(even_x, packets, lo, lo + 1)[0][2]


def level1_kernel(own, first, second, edge_a, edge_b, coef1, gain, packet, to_first, to_second, keep, y1, d1):
    b1, x1 = keep.at[0], keep.at[1]
    even = is_even("gy")
    for t in (0, 1):
        b1[t, 1 + OWN : 1 + 2 * OWN] = own[t]
        strip = slice(t * OWN, (t + 1) * OWN)
        b1[t, 1 : 1 + OWN] = prev_of(even, first, second, strip)
        b1[t, 1 + 2 * OWN : 1 + 3 * OWN] = next_of(even, first, second, strip)
    g0, g1, g2 = (gain[3 + i] for i in range(3))
    n = GROUPS1
    packed_first(coef1, 0, b1, x1, d1, 1, n, g0)
    packed_step(1, coef1, 0, b1, x1, y1, d1, 1, n, CARRY1, g1)
    packed_step(1, coef1, 0, b1, y1, x1, d1, 1, n, CARRY2, g2)
    here = pl.ds(1 + OWN, OWN)
    for t, (c, other, spread) in enumerate(packed_terms(x1, 1 + OWN, OWN, 1)):
        res = b1[t, here] - coef1[2, t, here] * c + coef1[1, t, here] * other + spread
        value = restrict_12([res[j : j + 1] for j in range(OWN)])
        for ref in (packet, to_first, to_second):
            ref[t : t + 1] = value
    to_first[FAR:] = edge_a[...]
    to_second[FAR:] = edge_b[...]


def rest_kernel(
    own2, near_a, near_b, far_a, far_b, gain, coef1, fields2, keep0, iterate, keep1, out, coef2, d1, b2, x2, y2, d2, xu, yu, x0, y0, d0
):
    rows = out.shape[0] // (2 * Z)
    even = (sub_of() & 1) == 0
    b1, x1 = keep1.at[0], keep1.at[1]

    even_y, low = is_even("gy"), lax.rem(lax.axis_index("gy"), 4) < 2
    for t in (0, 1):
        at = slice(t, t + 1)
        parts = [
            next_of(low, far_a, far_b, at),
            prev_of(even_y, near_a, near_b, at),
            own2[at],
            next_of(even_y, near_a, near_b, at),
            prev_of(low, far_a, far_b, at),
        ]
        b2[t, 1 : SIZE2 - 1] = jnp.concatenate(parts, axis=0)
        far = slice(FAR + t, FAR + t + 1)
        parts = [prev_of(even_y, near_a, near_b, far), fields2[t], next_of(even_y, near_a, near_b, far)]
        inverse, other, _ = packed_jacobian(*split_fields2(jnp.concatenate(parts, axis=0)), 2)
        coef2[0, t, 1 : SIZE2 - 1] = inverse
        coef2[1, t, 1 : SIZE2 - 1] = other

    n = HI2 - LO2
    g0, g1, g2 = (gain[6 + i] for i in range(3))
    packed_first(coef2, 0, b2, x2, d2, 1, n, g0)
    packed_step(2, coef2, 0, b2, x2, y2, d2, 1, n, CARRY1, g1)
    packed_step(2, coef2, 0, b2, y2, x2, d2, 1, n, CARRY2, g2)
    packed_step(2, coef2, 0, b2, x2, y2, d2, 1, n, None, g0)
    packed_step(2, coef2, 0, b2, y2, x2, d2, 1, n, CARRY1, g1)
    packed_step(2, coef2, 0, b2, x2, y2, d2, 1, n, CARRY2, g2)

    g0, g1, g2 = (gain[3 + i] for i in range(3))
    shift = LO_UP - LO1
    for t in (0, 1):
        for g in range(LO_UP, HI_UP):
            p = g % 4
            value = y2[t, g // 4 - LO2 + 1 : g // 4 - LO2 + 2]
            value = spread_x(spread_x(value, 1, p & 1), 2, p & 2)
            at = g - LO_UP + 1
            xu[t, at : at + 1] = x1[t, at + shift : at + shift + 1] + value
    n = HI_UP - LO_UP
    packed_step(1, coef1, shift, b1, xu, yu, d1, 1, n, None, g0)
    packed_step(1, coef1, shift, b1, yu, xu, d1, 1, n, CARRY1, g1)
    packed_step(1, coef1, shift, b1, xu, yu, d1, 1, n, CARRY2, g2)

    g0, g1, g2 = (gain[i] for i in range(3))
    last = EDGES + 2 * EDGE
    for i in (0, 1):
        for at, take in ((HALO0 - EDGE, prev_of), (HALO0 + rows, next_of)):
            strip = slice(EDGES + i * EDGE, EDGES + (i + 1) * EDGE)
            x0[i, 0, at : at + EDGE] = take(even_y, near_a, near_b, strip)
            sides = take(even_y, near_a, near_b, slice(last, last + 1))
            for j in range(EDGE):
                x0[i, 1, at + j : at + j + 1] = roll_x(sides, -(4 + 8 * (i * EDGE + j)))
        for t in (0, 1):
            x0[i, t, HALO0 : HALO0 + rows] = iterate[i, t]
    for t in (0, 1):
        for row in range(-2, rows // 2 + 2):
            at = row // 2 - LO_UP + 1
            value = spread_x(yu[t, at : at + 1], 1, row & 1)
            for i, fine in enumerate((jnp.where(even, value, roll_z(value, 1)), jnp.where(even, roll_z(value, -1), value))):
                for y in (2 * row, 2 * row + 1):
                    if -EDGE <= y < rows + EDGE:
                        x0[i, t, y + HALO0 : y + HALO0 + 1] = x0[i, t, y + HALO0 : y + HALO0 + 1] + fine
    total = rows + 2 * HALO0
    rows_loop(2, total - 2, lambda r, n: cheb_step(0, keep0, x0, y0, d0, r, n, None, g0))
    rows_loop(3, total - 3, lambda r, n: cheb_step(0, keep0, y0, x0, d0, r, n, CARRY1, g1))
    rows_loop(4, total - 4, lambda r, n: cheb_step(0, keep0, x0, y0, d0, r, n, CARRY2, g2))
    for i in (0, 1):
        for y in range(rows):
            out[pl.ds(i * Z * rows + y, Z, stride=rows), :] = y0[i, 0, HALO0 + y]


def call(kernel, out_shapes, scratch, *args, space=pltpu.VMEM):
    out = [jax.ShapeDtypeStruct(shape, jnp.float32) for shape in out_shapes]
    return pl.pallas_call(
        kernel,
        out_shape=out,
        in_specs=[pl.BlockSpec(memory_space=space)] * len(args),
        out_specs=[pl.BlockSpec(memory_space=pltpu.VMEM)] * len(out),
        scratch_shapes=[pltpu.VMEM(s, jnp.float32) if isinstance(s, tuple) else s for s in scratch],
        compiler_params=pltpu.CompilerParams(vmem_limit_bytes=24 * 2**20),
    )(*args)


def swap(value, axis, step):
    count = lax.axis_size(axis)
    assert count % 2 == 0
    pairs = [(i, (i + step) % count) for i in range(0, count, 2)]
    return lax.ppermute(value, axis, pairs + [(j, i) for i, j in pairs])


def swap_far(value, axis, step):
    count = lax.axis_size(axis)
    assert count % 4 == 0
    pairs = [(i + j, (i + j + 2 * step) % count) for i in range(0, count, 4) for j in (0, 1)]
    return lax.ppermute(value, axis, pairs + [(j, i) for i, j in pairs])


def exchange(first, second, axis):
    return swap(first, axis, -1), swap(second, axis, 1)


def body(state, previous, feed, kill):
    _, depth, rows, cols = state.shape
    assert depth == Z and cols == X and rows == 4 * OWN
    across, count = lax.axis_size("gx"), lax.axis_size("gy")
    total0 = rows + 2 * HALO0
    state = state.reshape(2 * Z * rows, X)
    previous = previous.reshape(2 * Z * rows, X)
    feed = feed.reshape(Z * rows, X)
    kill = kill.reshape(Z * rows, X)
    inputs = (state, previous, feed, kill)

    strip = (FIELDS2 + 1, Z, X)
    first, second, main, coarse = call(
        functools.partial(first_kernel, rows),
        [strip, strip, (6, rows, Z, X), (2 * OWN + 1, Z, X)],
        [*(a.shape for a in inputs), pltpu.SemaphoreType.DMA((4,))],
        *(pltpu.with_memory_space_constraint(a, pltpu.HBM) for a in inputs),
        space=pltpu.HBM,
    )
    y_packets = exchange(first, second, "gy")
    (spread,) = call(spread_kernel, [(across * count, Z // 2, X)], [], main, coarse)
    spread = lax.all_to_all(spread, ("gx", "gy"), 0, 0, tiled=True)

    tiles = tiles_for(6 * rows + 2 * OWN + 1)
    own_x = exchange(
        *call(
            functools.partial(pack_own_kernel, rows),
            [(tiles, Z, X), (tiles, Z, X)],
            [(PER * tiles, Z, X)],
            main,
            coarse,
        ),
        "gx",
    )
    tiles = tiles_for(2 * PACKET)
    corner_x = exchange(
        *call(pack_corner_kernel, [(tiles, Z, X), (tiles, Z, X)], [(PER * tiles, Z, X)], *y_packets), "gx"
    )

    strip, edge = (2 * OWN, Z, X), (2 + EDGE_TILES, Z, X)
    pair0 = (2, 2, total0, Z, X)
    keep0, powers, sources = call(
        functools.partial(level0_kernel, rows),
        [(6, 2, total0, Z, X), (2, *pair0), (4, 2, OWN, Z, X)],
        [(6, 2, total0, Z, X), pair0, pair0],
        main,
        *y_packets,
        *own_x,
        *corner_x,
    )
    own, first, second, gain = call(
        combine_kernel,
        [(2, OWN, Z, X), strip, strip, (POWERS + 3, Z, X)],
        [],
        sources,
        spread,
    )
    coef1, iterate, edge_a, edge_b = call(
        functools.partial(coarse1_kernel, rows),
        [(3, 2, SIZE1, Z, X), (2, 2, rows, Z, X), edge, edge],
        [(2, 2 * GROUPS1, Z, X)],
        coarse,
        *y_packets,
        *own_x,
        *corner_x,
        gain,
        keep0,
        powers,
    )
    (fields2,) = call(
        functools.partial(fields2_kernel, rows), [(2, 3, Z, X)], [], coarse, *y_packets, *own_x, *corner_x
    )
    b_packets = exchange(first, second, "gy")

    one, two, up = (2, SIZE1, Z, X), (2, SIZE2, Z, X), (2, SIZE_UP, Z, X)
    near = (EDGES + EDGE_TILES, Z, X)
    packet, first, second, keep1 = call(
        level1_kernel,
        [(2, Z, X), near, near, (2, *one)],
        [one, one],
        own,
        *b_packets,
        edge_a,
        edge_b,
        coef1,
        gain,
    )
    far = (swap_far(packet, "gy", 1), swap_far(packet, "gy", -1))
    near = exchange(first, second, "gy")

    (out,) = call(
        rest_kernel,
        [(2 * Z * rows, X)],
        [(2, *two), one, two, two, two, two, up, up, pair0, pair0, pair0],
        packet,
        *near,
        *far,
        gain,
        coef1,
        fields2,
        keep0,
        iterate,
        keep1,
    )
    return out.reshape(2, Z, rows, X)


def solution(mesh):
    placed = (
        P(None, None, "gy", "gx"),
        P(None, None, "gy", "gx"),
        P(None, "gy", "gx"),
        P(None, "gy", "gx"),
    )
    return jax.shard_map(
        body, mesh=mesh, in_specs=placed, out_specs=P(None, None, "gy", "gx"), check_vma=False
    )
```

```python
import functools

import jax
import jax.numpy as jnp
from jax import lax
from jax.experimental import pallas as pl
from jax.experimental.pallas import tpu as pltpu
from jax.sharding import PartitionSpec as P

DIFF = (40.0, 20.0)
INV_STEP = 2.0
LOWER = 0.25

_CENTRE = (1.0 + LOWER) / 2.0
_HALF = (1.0 - LOWER) / 2.0
_SIGMA = _CENTRE / _HALF
_RHO0 = 1.0 / _SIGMA
_RHO1 = 1.0 / (2.0 * _SIGMA - _RHO0)
_RHO2 = 1.0 / (2.0 * _SIGMA - _RHO1)

Z = 8
X = 128
HALO0 = 4
HALOS = (4, 4, 3, 3, 3, 3)
STARTS = tuple(sum(HALOS[:i]) for i in range(6))
FIELDS1 = sum(HALOS)
FIELDS2 = FIELDS1 + 8
PACKET = FIELDS2 + 1
WIDE = 42
PER = X // WIDE
EDGE = 3

LO1, HI1 = -4, 8
LO2, HI2 = -2, 3
LO_UP, HI_UP = -3, 7
SIZE1, SIZE2, SIZE_UP = HI1 - LO1 + 2, HI2 - LO2 + 2, HI_UP - LO_UP + 2
OWN = 4


def lane_of():
    return lax.broadcasted_iota(jnp.int32, (1, Z, X), 2)


def sub_of():
    return lax.broadcasted_iota(jnp.int32, (1, Z, X), 1)


def roll_x(tile, shift):
    shift = shift % X
    return pltpu.roll(tile, shift, 2) if shift else tile


def roll_z(tile, shift):
    shift = shift % Z
    return pltpu.roll(tile, shift, 1) if shift else tile


def rows_loop(lo, hi, body, step=None):
    step = step or hi - lo
    full = (hi - lo) // step
    if full == 1:
        body(lo, step)
    elif full > 1:

        def trip(i, carry):
            body(lo + i * step, step)
            return carry

        lax.fori_loop(0, full, trip, 0)
    rest = hi - lo - full * step
    if rest:
        body(hi - rest, rest)


def neighbour_sums(read, r, n, k):
    lane = lane_of()
    low, high = lane < k, lane >= X - k
    centre = [read(t, r, n) for t in (0, 1)]
    right = [roll_x(c, k) for c in centre]
    left = [roll_x(c, -k) for c in centre]
    sums = []
    for t in (0, 1):
        c = centre[t]
        along_x = jnp.where(low, right[1 - t], right[t]) + jnp.where(high, left[1 - t], left[t])
        along_y = read(t, r - 1, n) + read(t, r + 1, n)
        along_z = 2.0 * roll_z(c, k) if 2 * k == Z else roll_z(c, k) + roll_z(c, -k)
        sums.append(along_x + along_y + along_z)
    return centre, sums


def jacobian(u, v, f, k, level):
    scale = 0.25**level
    product = u * v
    squared = v * v
    first = INV_STEP + squared + f + 6.0 * DIFF[0] * scale
    second = INV_STEP + f + k - 2.0 * product + 6.0 * DIFF[1] * scale
    return 2.0 * product, squared, 1.0 / first, 1.0 / second, first, second


def cheb_step(level, keep, source, target, d, r, n, carry, gain):
    scale = 0.25**level
    k = 1 << level
    u, nb_u = neighbour_sums(lambda t, a, m: source[0, t, pl.ds(a, m)], r, n, k)
    v, nb_v = neighbour_sums(lambda t, a, m: source[1, t, pl.ds(a, m)], r, n, k)
    rows = pl.ds(r, n)
    for t in (0, 1):
        cross, squared, inv_u, inv_v = (keep[i, t, rows] for i in range(4))
        res_u = inv_u * (keep[4, t, rows] - cross * v[t] + DIFF[0] * scale * nb_u[t]) - u[t]
        res_v = inv_v * (keep[5, t, rows] + squared * u[t] + DIFF[1] * scale * nb_v[t]) - v[t]
        du, dv = gain * res_u, gain * res_v
        if carry is not None:
            du = du + carry * d[0, t, rows]
            dv = dv + carry * d[1, t, rows]
        d[0, t, rows] = du
        d[1, t, rows] = dv
        target[0, t, rows] = u[t] + du
        target[1, t, rows] = v[t] + dv


def next_power(keep, source, r, n):
    u, nb_u = neighbour_sums(lambda t, a, m: source[0, t, pl.ds(a, m)], r, n, 1)
    v, nb_v = neighbour_sums(lambda t, a, m: source[1, t, pl.ds(a, m)], r, n, 1)
    rows = pl.ds(r, n)
    first, second = [], []
    for t in (0, 1):
        cross, squared, inv_u, inv_v = (keep[i, t, rows] for i in range(4))
        first.append(u[t] + inv_u * (cross * v[t] - DIFF[0] * nb_u[t]))
        second.append(v[t] - inv_v * (squared * u[t] + DIFF[1] * nb_v[t]))
    return first, second


CARRY1 = _RHO1 * _RHO0
CARRY2 = _RHO2 * _RHO1


POWERS = 9


def write_gains(spread, out):
    lane = lax.broadcasted_iota(jnp.int32, (1, X), 1)
    for level in range(3):
        top = jnp.max(jnp.where(lane == level, spread, 0.0), axis=1, keepdims=True)
        tau = 1.0 / (1.0 + jnp.broadcast_to(top, (Z, X)))
        for i, factor in enumerate((1.0 / _CENTRE, 2.0 * _RHO1 / _HALF, 2.0 * _RHO2 / _HALF)):
            out[3 * level + i] = factor * tau
    g0, g1, g2 = (out[i] for i in range(3))
    first, second = g0 + CARRY1 * g0 + g1, g1 * g0
    out[POWERS] = first + CARRY2 * (CARRY1 * g0 + g1) + g2
    out[POWERS + 1] = second + CARRY2 * second + g2 * first
    out[POWERS + 2] = g2 * second


def pair_rows(value):
    n = value.shape[0] // 2
    pairs = value.reshape(n, 2, Z, X)
    return pairs[:, 0] + pairs[:, 1]


def restrict_01(first, second):
    lane, sub = lane_of(), sub_of()
    across = []
    for value in (first, second):
        a, b = value[0:1], value[1:2]
        across.append(jnp.where((lane & 1) == 0, a + roll_x(a, -1), b + roll_x(b, 1)))
    a, b = across
    return 0.125 * jnp.where((sub & 1) == 0, a + roll_z(a, -1), b + roll_z(b, 1))


def restrict_12(groups):
    lane, sub = lane_of(), sub_of()
    out = None
    for p, value in enumerate(groups):
        value = value + roll_x(value, 1 if p & 1 else -1)
        value = value + roll_x(value, 2 if p & 2 else -2)
        out = value if out is None else jnp.where((lane & 3) == p, value, out)
    return 0.125 * (out + jnp.where((sub & 2) == 0, roll_z(out, -2), roll_z(out, 2)))


def spread_x(tile, k, phase):
    return jnp.where((lane_of() & k) == phase, tile, roll_x(tile, -k if phase else k))


def packed_jacobian(uv, fk, level):
    scale = 0.25**level
    even = (sub_of() & 1) == 0
    u, v = jnp.where(even, uv, roll_z(uv, 1)), jnp.where(even, roll_z(uv, -1), uv)
    f, k = jnp.where(even, fk, roll_z(fk, 1)), jnp.where(even, roll_z(fk, -1), fk)
    product, squared = u * v, v * v
    diag = jnp.where(
        even,
        INV_STEP + squared + f + 6.0 * DIFF[0] * scale,
        INV_STEP + f + k - 2.0 * product + 6.0 * DIFF[1] * scale,
    )
    return 1.0 / diag, jnp.where(even, -2.0 * product, squared), diag


def packed_spread(uv, fk, level):
    scale = 0.25**level
    even = (sub_of() & 1) == 0
    inverse, other, _ = packed_jacobian(uv, fk, level)
    return jnp.where(even, 6.0 * DIFF[0] * scale - other, 6.0 * DIFF[1] * scale + other) * inverse


def packed_terms(source, g, n, level):
    k = 1 << level
    lane, sub = lane_of(), sub_of()
    even = (sub & 1) == 0
    first, last = (lane & (k - 1)) == 0, (lane & (k - 1)) == k - 1
    low, high = lane < k, lane >= X - k
    diff = jnp.where(even, DIFF[0] * 0.25**level, DIFF[1] * 0.25**level)
    wide = [source[t, pl.ds(g - 1, n + 2)] for t in (0, 1)]
    centre = [w[1 : n + 1] for w in wide]
    right = [roll_x(c, k) for c in centre]
    left = [roll_x(c, -k) for c in centre]
    out = []
    for t in (0, 1):
        c, w = centre[t], wide[t]
        total = jnp.where(low, right[1 - t], right[t]) + jnp.where(high, left[1 - t], left[t])
        if k == 2:
            ahead, back = roll_x(w, 1), roll_x(w, -1)
            total = total + jnp.where(first, back[0:n], ahead[1 : n + 1])
            total = total + jnp.where(last, ahead[2 : n + 2], back[1 : n + 1])
            total = total + roll_z(c, 2) + roll_z(c, -2)
        else:
            total = total + jnp.where(first, roll_x(w[0:n], -(k - 1)), roll_x(c, 1))
            total = total + jnp.where(last, roll_x(w[2 : n + 2], k - 1), roll_x(c, -1))
            total = total + 2.0 * roll_z(c, 4)
        other = jnp.where(even, roll_z(c, -1), roll_z(c, 1))
        out.append((c, other, diff * total))
    return out


def packed_first(coef, shift, b, target, d, g, n, gain):
    for t in (0, 1):
        value = gain * coef[0, t, pl.ds(g + shift, n)] * b[t, pl.ds(g + shift, n)]
        d[t, pl.ds(g, n)] = value
        target[t, pl.ds(g, n)] = value


def packed_step(level, coef, shift, b, source, target, d, g, n, carry, gain):
    for t, (c, other, spread) in enumerate(packed_terms(source, g, n, level)):
        at = pl.ds(g + shift, n)
        res = coef[0, t, at] * (b[t, at] + coef[1, t, at] * other + spread) - c
        delta = gain * res
        if carry is not None:
            delta = delta + carry * d[t, pl.ds(g, n)]
        d[t, pl.ds(g, n)] = delta
        target[t, pl.ds(g, n)] = c + delta


def plane(ref, f, y, rows):
    return ref[pl.ds(f * Z * rows + y, Z, stride=rows), :]


def is_even(axis):
    return lax.rem(lax.axis_index(axis), 2) == 0


def prev_of(even, first, second, at):
    return jnp.where(even, first[at], second[at])


def next_of(even, first, second, at):
    return jnp.where(even, second[at], first[at])


def first_kernel(rows, state, previous, feed, kill, first, second, main, coarse, *scratch):
    sources, sems = scratch[:4], scratch[4]
    copies = [
        pltpu.make_async_copy(ref, held, sems.at[i])
        for i, (ref, held) in enumerate(zip((state, previous, feed, kill), sources))
    ]
    for copy in copies:
        copy.start()
    for copy in copies:
        copy.wait()
    even = is_even("gy")
    state, previous, feed, kill = sources
    fields = [(state, 0), (state, 1), (previous, 0), (previous, 1), (feed, 0), (kill, 0)]
    for i, (ref, f) in enumerate(fields):
        for y in range(rows):
            main[i, y] = plane(ref, f, y, rows)
        top, bottom = main[i, 0 : HALOS[i]], main[i, rows - HALOS[i] : rows]
        at = slice(STARTS[i], STARTS[i] + HALOS[i])
        first[at] = jnp.where(even, top, bottom)
        second[at] = jnp.where(even, bottom, top)
    u, v, f, k = (main[i] for i in (0, 1, 4, 5))
    sums = [pair_rows(value) for value in (u, v, f, k)]
    pairs = []
    for p in (0, 1):
        values = [
            restrict_01(sums[2 * p][2 * g : 2 * g + 2], sums[2 * p + 1][2 * g : 2 * g + 2]) for g in range(OWN)
        ]
        pairs.append(jnp.concatenate(values, axis=0))
        coarse[p * OWN : (p + 1) * OWN] = pairs[p]
        for ref in (first, second):
            ref[FIELDS1 + p * OWN : FIELDS1 + (p + 1) * OWN] = pairs[p]

    uv, fk = (restrict_12([pair[j : j + 1] for j in range(OWN)]) for pair in pairs)
    both = jnp.where((sub_of() & 2) == 0, uv, fk)
    coarse[2 * OWN : 2 * OWN + 1] = both
    for ref in (first, second):
        ref[FIELDS2 : FIELDS2 + 1] = both


def split_fields2(both):
    low = (sub_of() & 2) == 0
    return jnp.where(low, both, roll_z(both, 2)), jnp.where(low, roll_z(both, -2), both)


def spread_kernel(main, coarse, out):
    lane = lax.broadcasted_iota(jnp.int32, (1, X), 1)
    u, v, f, k = (main[i] for i in (0, 1, 4, 5))
    cross, squared, inv_u, inv_v, _, _ = jacobian(u, v, f, k, 0)
    tops = [jnp.max(jnp.maximum((6.0 * DIFF[0] + cross) * inv_u, (6.0 * DIFF[1] + squared) * inv_v), axis=0)]
    tops.append(jnp.max(packed_spread(coarse[0:OWN], coarse[OWN : 2 * OWN], 1), axis=0))
    tops.append(packed_spread(*split_fields2(coarse[2 * OWN : 2 * OWN + 1]), 2)[0])
    result = jnp.zeros((1, X), jnp.float32)
    for level, top in enumerate(tops):
        top = jnp.max(jnp.max(top, axis=0, keepdims=True), axis=1, keepdims=True)
        result = jnp.where(lane == level, jnp.broadcast_to(top, (1, X)), result)
    out[...] = jnp.broadcast_to(result[None], out.shape)


GROUPS1 = HI1 - LO1
GROUPS2 = HI2 - LO2


def tiles_for(entries):
    return -(-entries // PER)


def pack_edges(entries, even, first, second):
    lane = lane_of()
    share = first.shape[0]
    left, right = None, None
    for j in range(PER):
        part = entries[j * share : (j + 1) * share]
        a, b = roll_x(part, WIDE * j), roll_x(part, WIDE + WIDE * j)
        left = a if left is None else jnp.where(lane >= WIDE * j, a, left)
        right = b if right is None else jnp.where(lane >= WIDE * j, b, right)
    first[...] = jnp.where(even, left, right)
    second[...] = jnp.where(even, right, left)


def halo_tiles(even, packets, lo, hi):
    first, second = packets
    share = first.shape[0]
    lane = lane_of()
    out = []
    for j in range(PER):
        a, b = max(lo, j * share), min(hi, (j + 1) * share)
        if a < b:
            strip = slice(a - j * share, b - j * share)
            left, right = prev_of(even, first, second, strip), next_of(even, first, second, strip)
            value = jnp.where(lane < X // 2, roll_x(right, -WIDE * j), roll_x(left, X - WIDE - WIDE * j))
            out.append((a - lo, b - lo, value))
    return out


def pack_own_kernel(rows, main, coarse, first, second, held):
    for i in range(6):
        held[i * rows : (i + 1) * rows] = main[i]
    held[6 * rows : 6 * rows + 2 * OWN + 1] = coarse[...]
    pack_edges(held, is_even("gx"), first, second)


def pack_corner_kernel(y_first, y_second, first, second, held):
    even = is_even("gy")
    every = slice(0, PACKET)
    held[0:PACKET] = prev_of(even, y_first, y_second, every)
    held[PACKET : 2 * PACKET] = next_of(even, y_first, y_second, every)
    pack_edges(held, is_even("gx"), first, second)


EDGE_TILES = 2 * EDGE + 1


def level0_kernel(
    rows, main, y_first, y_second, own_a, own_b, corner_a, corner_b, keep, powers, sources, fields, diag, y0
):
    even, even_x = is_even("gy"), is_even("gx")
    total = rows + 2 * HALO0
    own_x, corner_x = (own_a, own_b), (corner_a, corner_b)
    for i, halo in enumerate(HALOS):
        strip = slice(STARTS[i], STARTS[i] + halo)
        skip = HALO0 - halo
        fields[i, 0, skip:HALO0] = prev_of(even, y_first, y_second, strip)
        fields[i, 0, HALO0 : HALO0 + rows] = main[i]
        fields[i, 0, HALO0 + rows : total - skip] = next_of(even, y_first, y_second, strip)
        for packets, lo, n, at in (
            (corner_x, STARTS[i], halo, skip),
            (own_x, i * rows, rows, HALO0),
            (corner_x, PACKET + STARTS[i], halo, HALO0 + rows),
        ):
            for a, b, value in halo_tiles(even_x, packets, lo, lo + n):
                fields[i, 1, at + a : at + b] = value

    def setup(r, n):
        at = pl.ds(r, n)
        u, nb_u = neighbour_sums(lambda t, a, m: fields[0, t, pl.ds(a, m)], r, n, 1)
        v, nb_v = neighbour_sums(lambda t, a, m: fields[1, t, pl.ds(a, m)], r, n, 1)
        for t in (0, 1):
            f, k = fields[4, t, at], fields[5, t, at]
            cross, squared, inv_u, inv_v, first, second = jacobian(u[t], v[t], f, k, 0)
            react = u[t] * squared
            b_u = (
                DIFF[0] * (nb_u[t] - 6.0 * u[t])
                - INV_STEP * (u[t] - fields[2, t, at])
                - react
                + f * (1.0 - u[t])
            )
            b_v = (
                DIFF[1] * (nb_v[t] - 6.0 * v[t]) - INV_STEP * (v[t] - fields[3, t, at]) + react - (f + k) * v[t]
            )
            for i, value in enumerate((cross, squared, inv_u, inv_v, b_u, b_v)):
                keep[i, t, at] = value
            diag[0, t, at] = first
            diag[1, t, at] = second
            y0[0, t, at] = inv_u * b_u
            y0[1, t, at] = inv_v * b_v

    rows_loop(1, total - 1, setup)
    for p in (0, 1):

        def power(r, n, p=p):
            for i, values in enumerate(next_power(keep, powers.at[0] if p else y0, r, n)):
                for t in (0, 1):
                    powers[p, i, t, pl.ds(r, n)] = values[t]

        rows_loop(2 + p, total - 2 - p, power)

    def down(r, n):
        at = pl.ds(r, n)
        last = next_power(keep, powers.at[1], r, n)
        for t in (0, 1):
            both = [diag[i, t, at] for i in (0, 1)]
            parts = [[keep[4 + i, t, at] for i in (0, 1)]]
            parts += [[both[i] * powers[p, i, t, at] for i in (0, 1)] for p in (0, 1)]
            parts.append([both[i] * last[i][t] for i in (0, 1)])
            for q, part in enumerate(parts):
                u, v = (pair_rows(value) for value in part)
                for j in range(n // 4):
                    value = restrict_01(u[2 * j : 2 * j + 2], v[2 * j : 2 * j + 2])
                    sources[q, t, pl.ds((r - HALO0) // 4 + j, 1)] = value

    rows_loop(HALO0, HALO0 + rows, down)


def combine_kernel(sources, spread, own, first, second, gain):
    write_gains(jnp.max(spread[...], axis=0)[0:1], gain)
    p0, p1, p2 = (gain[POWERS + i] for i in range(3))
    for t in (0, 1):
        value = sources[0, t] - p0 * sources[1, t] + p1 * sources[2, t] - p2 * sources[3, t]
        own[t] = value
        for ref in (first, second):
            ref[t * OWN : (t + 1) * OWN] = value


def coarse1_kernel(
    rows, coarse, y_first, y_second, own_a, own_b, corner_a, corner_b, gain, keep0, powers, coef, x0, edge_first, edge_second, fields
):
    even, even_x = is_even("gy"), is_even("gx")
    own_x, corner_x = (own_a, own_b), (corner_a, corner_b)
    for p in (0, 1):
        to = p * GROUPS1
        strip = slice(FIELDS1 + p * OWN, FIELDS1 + (p + 1) * OWN)
        fields[0, to : to + OWN] = prev_of(even, y_first, y_second, strip)
        fields[0, to + OWN : to + 2 * OWN] = coarse[p * OWN : (p + 1) * OWN]
        fields[0, to + 2 * OWN : to + 3 * OWN] = next_of(even, y_first, y_second, strip)
        for part, (packets, lo) in enumerate(
            ((corner_x, FIELDS1), (own_x, 6 * rows), (corner_x, PACKET + FIELDS1))
        ):
            lo += p * OWN
            for a, b, value in halo_tiles(even_x, packets, lo, lo + OWN):
                fields[1, to + part * OWN + a : to + part * OWN + b] = value
    for t in (0, 1):
        for i, value in enumerate(packed_jacobian(fields[t, 0:GROUPS1], fields[t, GROUPS1 : 2 * GROUPS1], 1)):
            coef[i, t, 1 : SIZE1 - 1] = value

    p0, p1, p2 = (gain[POWERS + i] for i in range(3))
    for i in (0, 1):
        for t in (0, 1):
            y0 = keep0[2 + i, t, HALO0 : HALO0 + rows] * keep0[4 + i, t, HALO0 : HALO0 + rows]
            y1, y2 = (powers[p, i, t, HALO0 : HALO0 + rows] for p in (0, 1))
            x0[i, t] = p0 * y0 - p1 * y1 + p2 * y2
    lane = lane_of()
    edges = []
    for start in (0, rows - EDGE):
        halo = None
        for i in (0, 1):
            for j in range(EDGE):
                at = i * EDGE + j
                value = roll_x(x0[i, 1, start + j : start + j + 1], 4 + 8 * at)
                halo = value if halo is None else jnp.where((lane >> 3) == at, value, halo)
        edges.append([x0[0, 0, start : start + EDGE], x0[1, 0, start : start + EDGE], halo])
    top, bottom = (jnp.concatenate(parts, axis=0) for parts in edges)
    edge_first[...] = jnp.where(even, top, bottom)
    edge_second[...] = jnp.where(even, bottom, top)


def fields2_kernel(rows, coarse, y_first, y_second, own_a, own_b, corner_a, corner_b, out):
    even, even_x = is_even("gy"), is_even("gx")
    own_x, corner_x = (own_a, own_b), (corner_a, corner_b)
    near = slice(FIELDS2, FIELDS2 + 1)
    out[0, 0:1] = prev_of(even, y_first, y_second, near)
    out[0, 1:2] = coarse[2 * OWN : 2 * OWN + 1]
    out[0, 2:3] = next_of(even, y_first, y_second, near)
    for q, (packets, lo) in enumerate(
        ((corner_x, FIELDS2), (own_x, 6 * rows + 2 * OWN), (corner_x, PACKET + FIELDS2))
    ):
        out[1, q : q + 1] = halo_tiles(even_x, packets, lo, lo + 1)[0][2]


def level1_kernel(
    own, first, second, edge, edge_in, fields2, coef1, gain, packet, to_first, to_far, to_far2, edge_out, keep, y1, d1
):
    b1, x1 = keep.at[0], keep.at[1]
    even = is_even("gy")
    for t in (0, 1):
        b1[t, 1 + OWN : 1 + 2 * OWN] = own[t]
        strip = slice(t * OWN, (t + 1) * OWN)
        b1[t, 1 : 1 + OWN] = prev_of(even, first, second, strip)
        b1[t, 1 + 2 * OWN : 1 + 3 * OWN] = next_of(even, first, second, strip)
    g0, g1, g2 = (gain[3 + i] for i in range(3))
    n = GROUPS1
    packed_first(coef1, 0, b1, x1, d1, 1, n, g0)
    packed_step(1, coef1, 0, b1, x1, y1, d1, 1, n, CARRY1, g1)
    packed_step(1, coef1, 0, b1, y1, x1, d1, 1, n, CARRY2, g2)
    here = pl.ds(1 + OWN, OWN)
    for t, (c, other, spread) in enumerate(packed_terms(x1, 1 + OWN, OWN, 1)):
        res = b1[t, here] - coef1[2, t, here] * c + coef1[1, t, here] * other + spread
        value = restrict_12([res[j : j + 1] for j in range(OWN)])
        for ref in (packet, to_first, to_far, to_far2):
            ref[t : t + 1] = value
            if ref is to_far or ref is to_far2:
                ref[2 + t : 3 + t] = fields2[t, 1:2]
    to_far2[4:] = value
    to_first[2:] = edge[...]
    edge_out[...] = edge_in[...]


def rest_kernel(
    own2, near_a, near_b, far_a, far_b, edge_b, gain, coef1, fields2, keep0, iterate, keep1, out, coef2, d1, b2, x2, y2, d2, xu, yu, x0, y0, d0
):
    rows = out.shape[0] // (2 * Z)
    even = (sub_of() & 1) == 0
    b1, x1 = keep1.at[0], keep1.at[1]

    even_y, low = is_even("gy"), lax.rem(lax.axis_index("gy"), 4) < 2
    for t in (0, 1):
        at = slice(t, t + 1)
        parts = [
            next_of(low, far_a, far_b, at),
            prev_of(even_y, near_a, near_b, at),
            own2[at],
            next_of(even_y, near_a, near_b, at),
            prev_of(low, far_a, far_b, at),
        ]
        b2[t, 1 : SIZE2 - 1] = jnp.concatenate(parts, axis=0)
        at = slice(2 + t, 3 + t)
        parts = [next_of(low, far_a, far_b, at), fields2[t], prev_of(low, far_a, far_b, at)]
        inverse, other, _ = packed_jacobian(*split_fields2(jnp.concatenate(parts, axis=0)), 2)
        coef2[0, t, 1 : SIZE2 - 1] = inverse
        coef2[1, t, 1 : SIZE2 - 1] = other

    n = HI2 - LO2
    g0, g1, g2 = (gain[6 + i] for i in range(3))
    packed_first(coef2, 0, b2, x2, d2, 1, n, g0)
    packed_step(2, coef2, 0, b2, x2, y2, d2, 1, n, CARRY1, g1)
    packed_step(2, coef2, 0, b2, y2, x2, d2, 1, n, CARRY2, g2)
    packed_step(2, coef2, 0, b2, x2, y2, d2, 1, n, None, g0)
    packed_step(2, coef2, 0, b2, y2, x2, d2, 1, n, CARRY1, g1)
    packed_step(2, coef2, 0, b2, x2, y2, d2, 1, n, CARRY2, g2)

    g0, g1, g2 = (gain[3 + i] for i in range(3))
    shift = LO_UP - LO1
    for t in (0, 1):
        for g in range(LO_UP, HI_UP):
            p = g % 4
            value = y2[t, g // 4 - LO2 + 1 : g // 4 - LO2 + 2]
            value = spread_x(spread_x(value, 1, p & 1), 2, p & 2)
            at = g - LO_UP + 1
            xu[t, at : at + 1] = x1[t, at + shift : at + shift + 1] + value
    n = HI_UP - LO_UP
    packed_step(1, coef1, shift, b1, xu, yu, d1, 1, n, None, g0)
    packed_step(1, coef1, shift, b1, yu, xu, d1, 1, n, CARRY1, g1)
    packed_step(1, coef1, shift, b1, xu, yu, d1, 1, n, CARRY2, g2)

    g0, g1, g2 = (gain[i] for i in range(3))
    for i in (0, 1):
        for at, take in ((HALO0 - EDGE, prev_of), (HALO0 + rows, next_of)):
            whole = take(even_y, near_a.at[2:], edge_b, slice(0, EDGE_TILES))
            x0[i, 0, at : at + EDGE] = whole[i * EDGE : (i + 1) * EDGE]
            for j in range(EDGE):
                x0[i, 1, at + j : at + j + 1] = roll_x(whole[2 * EDGE :], -(4 + 8 * (i * EDGE + j)))
        for t in (0, 1):
            x0[i, t, HALO0 : HALO0 + rows] = iterate[i, t]
    for t in (0, 1):
        for row in range(-2, rows // 2 + 2):
            at = row // 2 - LO_UP + 1
            value = spread_x(yu[t, at : at + 1], 1, row & 1)
            for i, fine in enumerate((jnp.where(even, value, roll_z(value, 1)), jnp.where(even, roll_z(value, -1), value))):
                for y in (2 * row, 2 * row + 1):
                    if -EDGE <= y < rows + EDGE:
                        x0[i, t, y + HALO0 : y + HALO0 + 1] = x0[i, t, y + HALO0 : y + HALO0 + 1] + fine
    total = rows + 2 * HALO0
    rows_loop(2, total - 2, lambda r, n: cheb_step(0, keep0, x0, y0, d0, r, n, None, g0))
    rows_loop(3, total - 3, lambda r, n: cheb_step(0, keep0, y0, x0, d0, r, n, CARRY1, g1))
    rows_loop(4, total - 4, lambda r, n: cheb_step(0, keep0, x0, y0, d0, r, n, CARRY2, g2))
    for i in (0, 1):
        for y in range(rows):
            out[pl.ds(i * Z * rows + y, Z, stride=rows), :] = y0[i, 0, HALO0 + y]


def call(kernel, out_shapes, scratch, *args, space=pltpu.VMEM):
    out = [jax.ShapeDtypeStruct(shape, jnp.float32) for shape in out_shapes]
    return pl.pallas_call(
        kernel,
        out_shape=out,
        in_specs=[pl.BlockSpec(memory_space=space)] * len(args),
        out_specs=[pl.BlockSpec(memory_space=pltpu.VMEM)] * len(out),
        scratch_shapes=[pltpu.VMEM(s, jnp.float32) if isinstance(s, tuple) else s for s in scratch],
        compiler_params=pltpu.CompilerParams(vmem_limit_bytes=24 * 2**20),
    )(*args)


def swap(value, axis, step):
    count = lax.axis_size(axis)
    assert count % 2 == 0
    pairs = [(i, (i + step) % count) for i in range(0, count, 2)]
    return lax.ppermute(value, axis, pairs + [(j, i) for i, j in pairs])


def swap_far(value, axis, step):
    count = lax.axis_size(axis)
    assert count % 4 == 0
    pairs = [(i + j, (i + j + 2 * step) % count) for i in range(0, count, 4) for j in (0, 1)]
    return lax.ppermute(value, axis, pairs + [(j, i) for i, j in pairs])


def exchange(first, second, axis):
    return swap(first, axis, -1), swap(second, axis, 1)


def body(state, previous, feed, kill):
    _, depth, rows, cols = state.shape
    assert depth == Z and cols == X and rows == 4 * OWN
    across, count = lax.axis_size("gx"), lax.axis_size("gy")
    total0 = rows + 2 * HALO0
    state = state.reshape(2 * Z * rows, X)
    previous = previous.reshape(2 * Z * rows, X)
    feed = feed.reshape(Z * rows, X)
    kill = kill.reshape(Z * rows, X)
    inputs = (state, previous, feed, kill)

    strip = (FIELDS2 + 1, Z, X)
    first, second, main, coarse = call(
        functools.partial(first_kernel, rows),
        [strip, strip, (6, rows, Z, X), (2 * OWN + 1, Z, X)],
        [*(a.shape for a in inputs), pltpu.SemaphoreType.DMA((4,))],
        *(pltpu.with_memory_space_constraint(a, pltpu.HBM) for a in inputs),
        space=pltpu.HBM,
    )
    y_packets = exchange(first, second, "gy")
    (spread,) = call(spread_kernel, [(across * count, Z // 2, X)], [], main, coarse)
    spread = lax.all_to_all(spread, ("gx", "gy"), 0, 0, tiled=True)

    tiles = tiles_for(6 * rows + 2 * OWN + 1)
    own_x = exchange(
        *call(
            functools.partial(pack_own_kernel, rows),
            [(tiles, Z, X), (tiles, Z, X)],
            [(PER * tiles, Z, X)],
            main,
            coarse,
        ),
        "gx",
    )
    tiles = tiles_for(2 * PACKET)
    corner_x = exchange(
        *call(pack_corner_kernel, [(tiles, Z, X), (tiles, Z, X)], [(PER * tiles, Z, X)], *y_packets), "gx"
    )

    strip, edge = (2 * OWN, Z, X), (EDGE_TILES, Z, X)
    pair0 = (2, 2, total0, Z, X)
    keep0, powers, sources = call(
        functools.partial(level0_kernel, rows),
        [(6, 2, total0, Z, X), (2, *pair0), (4, 2, OWN, Z, X)],
        [(6, 2, total0, Z, X), pair0, pair0],
        main,
        *y_packets,
        *own_x,
        *corner_x,
    )
    own, first, second, gain = call(
        combine_kernel,
        [(2, OWN, Z, X), strip, strip, (POWERS + 3, Z, X)],
        [],
        sources,
        spread,
    )
    coef1, iterate, edge_a, edge_b = call(
        functools.partial(coarse1_kernel, rows),
        [(3, 2, SIZE1, Z, X), (2, 2, rows, Z, X), edge, edge],
        [(2, 2 * GROUPS1, Z, X)],
        coarse,
        *y_packets,
        *own_x,
        *corner_x,
        gain,
        keep0,
        powers,
    )
    (fields2,) = call(
        functools.partial(fields2_kernel, rows), [(2, 3, Z, X)], [], coarse, *y_packets, *own_x, *corner_x
    )
    b_packets = exchange(first, second, "gy")

    one, two, up = (2, SIZE1, Z, X), (2, SIZE2, Z, X), (2, SIZE_UP, Z, X)
    edge_in = swap(edge_b, "gy", 1)
    packet, first, to_far, to_far2, edge_out, keep1 = call(
        level1_kernel,
        [(2, Z, X), (2 + EDGE_TILES, Z, X), (4, Z, X), (5, Z, X), edge, (2, *one)],
        [one, one],
        own,
        *b_packets,
        edge_a,
        edge_in,
        fields2,
        coef1,
        gain,
    )
    near = (swap(first, "gy", -1), swap(packet, "gy", 1))
    far = (swap_far(to_far, "gy", 1), swap_far(to_far2, "gy", -1))

    (out,) = call(
        rest_kernel,
        [(2 * Z * rows, X)],
        [(2, *two), one, two, two, two, two, up, up, pair0, pair0, pair0],
        packet,
        *near,
        *far,
        edge_out,
        gain,
        coef1,
        fields2,
        keep0,
        iterate,
        keep1,
    )
    return out.reshape(2, Z, rows, X)


def solution(mesh):
    placed = (
        P(None, None, "gy", "gx"),
        P(None, None, "gy", "gx"),
        P(None, "gy", "gx"),
        P(None, "gy", "gx"),
    )
    return jax.shard_map(
        body, mesh=mesh, in_specs=placed, out_specs=P(None, None, "gy", "gx"), check_vma=False
    )
```

```python
import functools

import jax
import jax.numpy as jnp
from jax import lax
from jax.experimental import pallas as pl
from jax.experimental.pallas import tpu as pltpu
from jax.sharding import PartitionSpec as P

DIFF = (40.0, 20.0)
INV_STEP = 2.0
LOWER = 0.25

_CENTRE = (1.0 + LOWER) / 2.0
_HALF = (1.0 - LOWER) / 2.0
_SIGMA = _CENTRE / _HALF
_RHO0 = 1.0 / _SIGMA
_RHO1 = 1.0 / (2.0 * _SIGMA - _RHO0)
_RHO2 = 1.0 / (2.0 * _SIGMA - _RHO1)

Z = 8
X = 128
HALO0 = 4
HALOS = (4, 4, 3, 3, 3, 3)
STARTS = tuple(sum(HALOS[:i]) for i in range(6))
FIELDS1 = sum(HALOS)
FIELDS2 = FIELDS1 + 8
PACKET = FIELDS2 + 1
WIDE = 42
PER = X // WIDE
EDGE = 3

LO1, HI1 = -4, 8
LO2, HI2 = -2, 3
LO_UP, HI_UP = -3, 7
SIZE1, SIZE2, SIZE_UP = HI1 - LO1 + 2, HI2 - LO2 + 2, HI_UP - LO_UP + 2
OWN = 4


def lane_of():
    return lax.broadcasted_iota(jnp.int32, (1, Z, X), 2)


def sub_of():
    return lax.broadcasted_iota(jnp.int32, (1, Z, X), 1)


def roll_x(tile, shift):
    shift = shift % X
    return pltpu.roll(tile, shift, 2) if shift else tile


def roll_z(tile, shift):
    shift = shift % Z
    return pltpu.roll(tile, shift, 1) if shift else tile


def rows_loop(lo, hi, body, step=None):
    step = step or hi - lo
    full = (hi - lo) // step
    if full == 1:
        body(lo, step)
    elif full > 1:

        def trip(i, carry):
            body(lo + i * step, step)
            return carry

        lax.fori_loop(0, full, trip, 0)
    rest = hi - lo - full * step
    if rest:
        body(hi - rest, rest)


def neighbour_sums(read, r, n, k):
    lane = lane_of()
    low, high = lane < k, lane >= X - k
    centre = [read(t, r, n) for t in (0, 1)]
    right = [roll_x(c, k) for c in centre]
    left = [roll_x(c, -k) for c in centre]
    sums = []
    for t in (0, 1):
        c = centre[t]
        along_x = jnp.where(low, right[1 - t], right[t]) + jnp.where(high, left[1 - t], left[t])
        along_y = read(t, r - 1, n) + read(t, r + 1, n)
        along_z = 2.0 * roll_z(c, k) if 2 * k == Z else roll_z(c, k) + roll_z(c, -k)
        sums.append(along_x + along_y + along_z)
    return centre, sums


def jacobian(u, v, f, k, level):
    scale = 0.25**level
    product = u * v
    squared = v * v
    first = INV_STEP + squared + f + 6.0 * DIFF[0] * scale
    second = INV_STEP + f + k - 2.0 * product + 6.0 * DIFF[1] * scale
    return 2.0 * product, squared, 1.0 / first, 1.0 / second, first, second


def cheb_step(level, keep, source, target, d, r, n, carry, gain):
    scale = 0.25**level
    k = 1 << level
    u, nb_u = neighbour_sums(lambda t, a, m: source[0, t, pl.ds(a, m)], r, n, k)
    v, nb_v = neighbour_sums(lambda t, a, m: source[1, t, pl.ds(a, m)], r, n, k)
    rows = pl.ds(r, n)
    for t in (0, 1):
        cross, squared, inv_u, inv_v = (keep[i, t, rows] for i in range(4))
        res_u = inv_u * (keep[4, t, rows] - cross * v[t] + DIFF[0] * scale * nb_u[t]) - u[t]
        res_v = inv_v * (keep[5, t, rows] + squared * u[t] + DIFF[1] * scale * nb_v[t]) - v[t]
        du, dv = gain * res_u, gain * res_v
        if carry is not None:
            du = du + carry * d[0, t, rows]
            dv = dv + carry * d[1, t, rows]
        d[0, t, rows] = du
        d[1, t, rows] = dv
        target[0, t, rows] = u[t] + du
        target[1, t, rows] = v[t] + dv


def next_power(keep, source, r, n):
    u, nb_u = neighbour_sums(lambda t, a, m: source[0, t, pl.ds(a, m)], r, n, 1)
    v, nb_v = neighbour_sums(lambda t, a, m: source[1, t, pl.ds(a, m)], r, n, 1)
    rows = pl.ds(r, n)
    first, second = [], []
    for t in (0, 1):
        cross, squared, inv_u, inv_v = (keep[i, t, rows] for i in range(4))
        first.append(u[t] + inv_u * (cross * v[t] - DIFF[0] * nb_u[t]))
        second.append(v[t] - inv_v * (squared * u[t] + DIFF[1] * nb_v[t]))
    return first, second


CARRY1 = _RHO1 * _RHO0
CARRY2 = _RHO2 * _RHO1


POWERS = 9


def write_gains(spread, out):
    lane = lax.broadcasted_iota(jnp.int32, (1, X), 1)
    for level in range(3):
        top = jnp.max(jnp.where(lane == level, spread, 0.0), axis=1, keepdims=True)
        tau = 1.0 / (1.0 + jnp.broadcast_to(top, (Z, X)))
        for i, factor in enumerate((1.0 / _CENTRE, 2.0 * _RHO1 / _HALF, 2.0 * _RHO2 / _HALF)):
            out[3 * level + i] = factor * tau
    g0, g1, g2 = (out[i] for i in range(3))
    first, second = g0 + CARRY1 * g0 + g1, g1 * g0
    out[POWERS] = first + CARRY2 * (CARRY1 * g0 + g1) + g2
    out[POWERS + 1] = second + CARRY2 * second + g2 * first
    out[POWERS + 2] = g2 * second


def pair_rows(value):
    n = value.shape[0] // 2
    pairs = value.reshape(n, 2, Z, X)
    return pairs[:, 0] + pairs[:, 1]


def restrict_01(first, second):
    lane, sub = lane_of(), sub_of()
    across = []
    for value in (first, second):
        a, b = value[0:1], value[1:2]
        across.append(jnp.where((lane & 1) == 0, a + roll_x(a, -1), b + roll_x(b, 1)))
    a, b = across
    return 0.125 * jnp.where((sub & 1) == 0, a + roll_z(a, -1), b + roll_z(b, 1))


def restrict_12(groups):
    lane, sub = lane_of(), sub_of()
    out = None
    for p, value in enumerate(groups):
        value = value + roll_x(value, 1 if p & 1 else -1)
        value = value + roll_x(value, 2 if p & 2 else -2)
        out = value if out is None else jnp.where((lane & 3) == p, value, out)
    return 0.125 * (out + jnp.where((sub & 2) == 0, roll_z(out, -2), roll_z(out, 2)))


def spread_x(tile, k, phase):
    return jnp.where((lane_of() & k) == phase, tile, roll_x(tile, -k if phase else k))


def packed_jacobian(uv, fk, level):
    scale = 0.25**level
    even = (sub_of() & 1) == 0
    u, v = jnp.where(even, uv, roll_z(uv, 1)), jnp.where(even, roll_z(uv, -1), uv)
    f, k = jnp.where(even, fk, roll_z(fk, 1)), jnp.where(even, roll_z(fk, -1), fk)
    product, squared = u * v, v * v
    diag = jnp.where(
        even,
        INV_STEP + squared + f + 6.0 * DIFF[0] * scale,
        INV_STEP + f + k - 2.0 * product + 6.0 * DIFF[1] * scale,
    )
    return 1.0 / diag, jnp.where(even, -2.0 * product, squared), diag


def packed_spread(uv, fk, level):
    scale = 0.25**level
    even = (sub_of() & 1) == 0
    inverse, other, _ = packed_jacobian(uv, fk, level)
    return jnp.where(even, 6.0 * DIFF[0] * scale - other, 6.0 * DIFF[1] * scale + other) * inverse


def packed_terms(source, g, n, level):
    k = 1 << level
    lane, sub = lane_of(), sub_of()
    even = (sub & 1) == 0
    first, last = (lane & (k - 1)) == 0, (lane & (k - 1)) == k - 1
    low, high = lane < k, lane >= X - k
    diff = jnp.where(even, DIFF[0] * 0.25**level, DIFF[1] * 0.25**level)
    wide = [source[t, pl.ds(g - 1, n + 2)] for t in (0, 1)]
    centre = [w[1 : n + 1] for w in wide]
    right = [roll_x(c, k) for c in centre]
    left = [roll_x(c, -k) for c in centre]
    out = []
    for t in (0, 1):
        c, w = centre[t], wide[t]
        total = jnp.where(low, right[1 - t], right[t]) + jnp.where(high, left[1 - t], left[t])
        if k == 2:
            ahead, back = roll_x(w, 1), roll_x(w, -1)
            total = total + jnp.where(first, back[0:n], ahead[1 : n + 1])
            total = total + jnp.where(last, ahead[2 : n + 2], back[1 : n + 1])
            total = total + roll_z(c, 2) + roll_z(c, -2)
        else:
            total = total + jnp.where(first, roll_x(w[0:n], -(k - 1)), roll_x(c, 1))
            total = total + jnp.where(last, roll_x(w[2 : n + 2], k - 1), roll_x(c, -1))
            total = total + 2.0 * roll_z(c, 4)
        other = jnp.where(even, roll_z(c, -1), roll_z(c, 1))
        out.append((c, other, diff * total))
    return out


def packed_first(coef, shift, b, target, d, g, n, gain):
    for t in (0, 1):
        value = gain * coef[0, t, pl.ds(g + shift, n)] * b[t, pl.ds(g + shift, n)]
        d[t, pl.ds(g, n)] = value
        target[t, pl.ds(g, n)] = value


def packed_step(level, coef, shift, b, source, target, d, g, n, carry, gain):
    for t, (c, other, spread) in enumerate(packed_terms(source, g, n, level)):
        at = pl.ds(g + shift, n)
        res = coef[0, t, at] * (b[t, at] + coef[1, t, at] * other + spread) - c
        delta = gain * res
        if carry is not None:
            delta = delta + carry * d[t, pl.ds(g, n)]
        d[t, pl.ds(g, n)] = delta
        target[t, pl.ds(g, n)] = c + delta


def plane(ref, f, y, rows):
    return ref[pl.ds(f * Z * rows + y, Z, stride=rows), :]


def is_even(axis):
    return lax.rem(lax.axis_index(axis), 2) == 0


def prev_of(even, first, second, at):
    return jnp.where(even, first[at], second[at])


def next_of(even, first, second, at):
    return jnp.where(even, second[at], first[at])


def first_kernel(rows, state, previous, feed, kill, first, second, main, coarse, *scratch):
    sources, sems = scratch[:4], scratch[4]
    copies = [
        pltpu.make_async_copy(ref, held, sems.at[i])
        for i, (ref, held) in enumerate(zip((state, previous, feed, kill), sources))
    ]
    for copy in copies:
        copy.start()
    for copy in copies:
        copy.wait()
    even = is_even("gy")
    state, previous, feed, kill = sources
    fields = [(state, 0), (state, 1), (previous, 0), (previous, 1), (feed, 0), (kill, 0)]
    for i, (ref, f) in enumerate(fields):
        for y in range(rows):
            main[i, y] = plane(ref, f, y, rows)
        top, bottom = main[i, 0 : HALOS[i]], main[i, rows - HALOS[i] : rows]
        at = slice(STARTS[i], STARTS[i] + HALOS[i])
        first[at] = jnp.where(even, top, bottom)
        second[at] = jnp.where(even, bottom, top)
    u, v, f, k = (main[i] for i in (0, 1, 4, 5))
    sums = [pair_rows(value) for value in (u, v, f, k)]
    pairs = []
    for p in (0, 1):
        values = [
            restrict_01(sums[2 * p][2 * g : 2 * g + 2], sums[2 * p + 1][2 * g : 2 * g + 2]) for g in range(OWN)
        ]
        pairs.append(jnp.concatenate(values, axis=0))
        coarse[p * OWN : (p + 1) * OWN] = pairs[p]
        for ref in (first, second):
            ref[FIELDS1 + p * OWN : FIELDS1 + (p + 1) * OWN] = pairs[p]

    uv, fk = (restrict_12([pair[j : j + 1] for j in range(OWN)]) for pair in pairs)
    both = jnp.where((sub_of() & 2) == 0, uv, fk)
    coarse[2 * OWN : 2 * OWN + 1] = both
    for ref in (first, second):
        ref[FIELDS2 : FIELDS2 + 1] = both


def split_fields2(both):
    low = (sub_of() & 2) == 0
    return jnp.where(low, both, roll_z(both, 2)), jnp.where(low, roll_z(both, -2), both)


def write_spread(main, coarse, out):
    lane = lax.broadcasted_iota(jnp.int32, (1, X), 1)
    u, v, f, k = (main[i] for i in (0, 1, 4, 5))
    cross, squared, inv_u, inv_v, _, _ = jacobian(u, v, f, k, 0)
    tops = [jnp.max(jnp.maximum((6.0 * DIFF[0] + cross) * inv_u, (6.0 * DIFF[1] + squared) * inv_v), axis=0)]
    tops.append(jnp.max(packed_spread(coarse[0:OWN], coarse[OWN : 2 * OWN], 1), axis=0))
    tops.append(packed_spread(*split_fields2(coarse[2 * OWN : 2 * OWN + 1]), 2)[0])
    result = jnp.zeros((1, X), jnp.float32)
    for level, top in enumerate(tops):
        top = jnp.max(jnp.max(top, axis=0, keepdims=True), axis=1, keepdims=True)
        result = jnp.where(lane == level, jnp.broadcast_to(top, (1, X)), result)
    out[...] = jnp.broadcast_to(result[None], out.shape)


GROUPS1 = HI1 - LO1
GROUPS2 = HI2 - LO2


def tiles_for(entries):
    return -(-entries // PER)


def pack_edges(entries, even, first, second):
    lane = lane_of()
    share = first.shape[0]
    left, right = None, None
    for j in range(PER):
        part = entries[j * share : (j + 1) * share]
        a, b = roll_x(part, WIDE * j), roll_x(part, WIDE + WIDE * j)
        left = a if left is None else jnp.where(lane >= WIDE * j, a, left)
        right = b if right is None else jnp.where(lane >= WIDE * j, b, right)
    first[...] = jnp.where(even, left, right)
    second[...] = jnp.where(even, right, left)


def halo_tiles(even, packets, lo, hi):
    first, second = packets
    share = first.shape[0]
    lane = lane_of()
    out = []
    for j in range(PER):
        a, b = max(lo, j * share), min(hi, (j + 1) * share)
        if a < b:
            strip = slice(a - j * share, b - j * share)
            left, right = prev_of(even, first, second, strip), next_of(even, first, second, strip)
            value = jnp.where(lane < X // 2, roll_x(right, -WIDE * j), roll_x(left, X - WIDE - WIDE * j))
            out.append((a - lo, b - lo, value))
    return out


def pack_own_kernel(rows, main, coarse, first, second, spread, held, copies, sem):
    write_spread(main, coarse, copies)
    copy = pltpu.make_async_copy(copies, spread, sem)
    copy.start()
    for i in range(6):
        held[i * rows : (i + 1) * rows] = main[i]
    held[6 * rows : 6 * rows + 2 * OWN + 1] = coarse[...]
    pack_edges(held, is_even("gx"), first, second)
    copy.wait()


def pack_corner_kernel(y_first, y_second, first, second, held):
    even = is_even("gy")
    every = slice(0, PACKET)
    held[0:PACKET] = prev_of(even, y_first, y_second, every)
    held[PACKET : 2 * PACKET] = next_of(even, y_first, y_second, every)
    pack_edges(held, is_even("gx"), first, second)


EDGE_TILES = 2 * EDGE + 1


def level0_setup(fields, keep, diag, power, r, n):
    at = pl.ds(r, n)
    u, nb_u = neighbour_sums(lambda t, a, m: fields[0, t, pl.ds(a, m)], r, n, 1)
    v, nb_v = neighbour_sums(lambda t, a, m: fields[1, t, pl.ds(a, m)], r, n, 1)
    for t in (0, 1):
        f, k = fields[4, t, at], fields[5, t, at]
        cross, squared, inv_u, inv_v, first, second = jacobian(u[t], v[t], f, k, 0)
        react = u[t] * squared
        b_u = DIFF[0] * (nb_u[t] - 6.0 * u[t]) - INV_STEP * (u[t] - fields[2, t, at]) - react + f * (1.0 - u[t])
        b_v = DIFF[1] * (nb_v[t] - 6.0 * v[t]) - INV_STEP * (v[t] - fields[3, t, at]) + react - (f + k) * v[t]
        for i, value in enumerate((cross, squared, inv_u, inv_v, b_u, b_v)):
            keep[i, t, at] = value
        for i, value in enumerate((first, second)):
            diag[i, t, at] = value
        for i, value in enumerate((inv_u * b_u, inv_v * b_v)):
            power[i, t, at] = value


def level0_power(keep, source, target, r, n):
    for i, values in enumerate(next_power(keep, source, r, n)):
        for t in (0, 1):
            target[i, t, pl.ds(r, n)] = values[t]


def level0_down(keep, diag, y1, y2, sources, r, n):
    at = pl.ds(r, n)
    last = next_power(keep, y2, r, n)
    for t in (0, 1):
        both = [diag[i, t, at] for i in (0, 1)]
        parts = [[keep[4 + i, t, at] for i in (0, 1)]]
        parts += [[both[i] * power[i, t, at] for i in (0, 1)] for power in (y1, y2)]
        parts.append([both[i] * last[i][t] for i in (0, 1)])
        for q, part in enumerate(parts):
            u, v = (pair_rows(value) for value in part)
            for j in range(n // 4):
                value = restrict_01(u[2 * j : 2 * j + 2], v[2 * j : 2 * j + 2])
                sources[q, t, pl.ds((r - HALO0) // 4 + j, 1)] = value


def inner(rows, lost):
    return slice(HALO0 + lost, HALO0 + rows - lost)


def ends(rows, lo, hi):
    total = rows + 2 * HALO0
    return slice(lo, hi), slice(total - hi, total - lo)


def put_ends(target, rows, lo, hi, source):
    n = hi - lo
    for at, part in zip(ends(rows, lo, hi), (slice(0, n), slice(n, 2 * n))):
        for i in range(target.shape[0]):
            for t in (0, 1):
                target[i, t, at] = source[i, t, part]


def take_ends(source, rows, lo, hi, target):
    n = hi - lo
    for at, part in zip(ends(rows, lo, hi), (slice(0, n), slice(n, 2 * n))):
        for i in range(source.shape[0]):
            for t in (0, 1):
                target[i, t, part] = source[i, t, at]


def level0_inner_kernel(rows, main, own_a, own_b, keep_in, y0_in, y1_in, y2_in, diag_in, sources_in, *scratch):
    fields, keep, diag, y0, y1, y2 = scratch
    even_x = is_even("gx")
    for i in range(6):
        fields[i, 0, HALO0 : HALO0 + rows] = main[i]
        for a, b, value in halo_tiles(even_x, (own_a, own_b), i * rows, (i + 1) * rows):
            fields[i, 1, HALO0 + a : HALO0 + b] = value
    first = HALO0 + 1
    level0_setup(fields, keep, diag, y0, first, rows - 2)
    level0_power(keep, y0, y1, first + 1, rows - 4)
    level0_power(keep, y1, y2, first + 2, rows - 6)
    level0_down(keep, diag, y1, y2, sources_in, first + 3, rows - 8)
    for source, target, lost in ((keep, keep_in, 1), (y1, y1_in, 2), (y2, y2_in, 3)):
        for i in range(source.shape[0]):
            for t in (0, 1):
                target[i, t] = source[i, t, inner(rows, lost)]
    take_ends(y0, rows, HALO0 + 1, HALO0 + 3, y0_in)
    take_ends(diag, rows, HALO0 + 1, HALO0 + 4, diag_in)


def level0_outer_kernel(
    rows,
    main,
    y_first,
    y_second,
    own_a,
    own_b,
    corner_a,
    corner_b,
    keep_in,
    y0_in,
    y1_in,
    y2_in,
    diag_in,
    sources_in,
    keep_out,
    y1_out,
    y2_out,
    sources,
    edges,
    *scratch,
):
    fields, keep, diag, y0, y1, y2 = scratch
    even, even_x = is_even("gy"), is_even("gx")
    total = rows + 2 * HALO0
    near = HALO0 + 2
    for i, halo in enumerate(HALOS):
        strip = slice(STARTS[i], STARTS[i] + halo)
        skip = HALO0 - halo
        fields[i, 0, skip:HALO0] = prev_of(even, y_first, y_second, strip)
        fields[i, 0, HALO0:near] = main[i, 0:2]
        fields[i, 0, total - near : total - HALO0] = main[i, rows - 2 : rows]
        fields[i, 0, HALO0 + rows : total - skip] = next_of(even, y_first, y_second, strip)
        for packets, lo, n, at in (
            ((corner_a, corner_b), STARTS[i], halo, skip),
            ((own_a, own_b), i * rows, 2, HALO0),
            ((own_a, own_b), (i + 1) * rows - 2, 2, total - near),
            ((corner_a, corner_b), PACKET + STARTS[i], halo, HALO0 + rows),
        ):
            for a, b, value in halo_tiles(even_x, packets, lo, lo + n):
                fields[i, 1, at + a : at + b] = value
    for at, part in zip(ends(rows, 5, 8), (slice(0, 3), slice(rows - 5, rows - 2))):
        for i in range(6):
            for t in (0, 1):
                keep[i, t, at] = keep_in[i, t, part]
    put_ends(diag, rows, 5, 8, diag_in)
    put_ends(y0, rows, 5, 7, y0_in)
    for target, source, lost in ((y1, y1_in, 2), (y2, y2_in, 3)):
        n = rows - 2 * lost
        for at, part in zip(ends(rows, HALO0 + lost, HALO0 + lost + 2), (slice(0, 2), slice(n - 2, n))):
            for i in (0, 1):
                for t in (0, 1):
                    target[i, t, at] = source[i, t, part]
    for r in (1, total - 5):
        level0_setup(fields, keep, diag, y0, r, 4)
    for r in (2, total - 6):
        level0_power(keep, y0, y1, r, 4)
    for r in (3, total - 7):
        level0_power(keep, y1, y2, r, 4)
    for r in (4, total - 8):
        level0_down(keep, diag, y1, y2, sources, r, 4)
    for q in range(4):
        for t in (0, 1):
            sources[q, t, 1 : OWN - 1] = sources_in[q, t, 1 : OWN - 1]
    take_ends(keep, rows, 1, 5, keep_out)
    take_ends(y1, rows, 4, 6, y1_out)
    take_ends(y2, rows, 4, 7, y2_out)
    for p, power in enumerate((y0, y1, y2)):
        for side, start in enumerate((HALO0, HALO0 + rows - EDGE)):
            edges[p, side] = pack_rows(power, start)


def pack_rows(x, start):
    lane = lane_of()
    halo = None
    for i in (0, 1):
        for j in range(EDGE):
            at = i * EDGE + j
            value = roll_x(x[i, 1, start + j : start + j + 1], 4 + 8 * at)
            halo = value if halo is None else jnp.where((lane >> 3) == at, value, halo)
    return jnp.concatenate([x[i, 0, start : start + EDGE] for i in (0, 1)] + [halo], axis=0)


def combine_kernel(sources, edges, spread, own, first, second, edge_first, edge_second, gain):
    write_gains(jnp.max(spread[...], axis=0)[0:1], gain)
    p0, p1, p2 = (gain[POWERS + i] for i in range(3))
    for t in (0, 1):
        value = sources[0, t] - p0 * sources[1, t] + p1 * sources[2, t] - p2 * sources[3, t]
        own[t] = value
        for ref in (first, second):
            ref[t * OWN : (t + 1) * OWN] = value
    even = is_even("gy")
    top, bottom = (p0 * edges[0, side] - p1 * edges[1, side] + p2 * edges[2, side] for side in (0, 1))
    edge_first[...] = jnp.where(even, top, bottom)
    edge_second[...] = jnp.where(even, bottom, top)


def coarse1_kernel(
    rows, coarse, y_first, y_second, own_a, own_b, corner_a, corner_b, gain, keep_in, y1_in, y2_in, keep_out, y1_out, y2_out,
    coef, keep0, x0, fields
):
    even, even_x = is_even("gy"), is_even("gx")
    own_x, corner_x = (own_a, own_b), (corner_a, corner_b)
    for p in (0, 1):
        to = p * GROUPS1
        strip = slice(FIELDS1 + p * OWN, FIELDS1 + (p + 1) * OWN)
        fields[0, to : to + OWN] = prev_of(even, y_first, y_second, strip)
        fields[0, to + OWN : to + 2 * OWN] = coarse[p * OWN : (p + 1) * OWN]
        fields[0, to + 2 * OWN : to + 3 * OWN] = next_of(even, y_first, y_second, strip)
        for part, (packets, lo) in enumerate(
            ((corner_x, FIELDS1), (own_x, 6 * rows), (corner_x, PACKET + FIELDS1))
        ):
            lo += p * OWN
            for a, b, value in halo_tiles(even_x, packets, lo, lo + OWN):
                fields[1, to + part * OWN + a : to + part * OWN + b] = value
    for t in (0, 1):
        for i, value in enumerate(packed_jacobian(fields[t, 0:GROUPS1], fields[t, GROUPS1 : 2 * GROUPS1], 1)):
            coef[i, t, 1 : SIZE1 - 1] = value

    def whole(inside, outside):
        n = outside.shape[0] // 2
        return jnp.concatenate([outside[0:n], inside, outside[n:]], axis=0)

    for i in range(6):
        for t in (0, 1):
            keep0[i, t, 1 : rows + 2 * HALO0 - 1] = whole(keep_in[i, t], keep_out[i, t])
    p0, p1, p2 = (gain[POWERS + i] for i in range(3))
    for i in (0, 1):
        for t in (0, 1):
            y0 = keep0[2 + i, t, HALO0 : HALO0 + rows] * keep0[4 + i, t, HALO0 : HALO0 + rows]
            y1, y2 = (whole(a[i, t], b[i, t]) for a, b in ((y1_in, y1_out), (y2_in, y2_out)))
            x0[i, t] = p0 * y0 - p1 * y1 + p2 * y2


def fields2_kernel(rows, coarse, y_first, y_second, own_a, own_b, corner_a, corner_b, out):
    even, even_x = is_even("gy"), is_even("gx")
    own_x, corner_x = (own_a, own_b), (corner_a, corner_b)
    near = slice(FIELDS2, FIELDS2 + 1)
    out[0, 0:1] = prev_of(even, y_first, y_second, near)
    out[0, 1:2] = coarse[2 * OWN : 2 * OWN + 1]
    out[0, 2:3] = next_of(even, y_first, y_second, near)
    for q, (packets, lo) in enumerate(
        ((corner_x, FIELDS2), (own_x, 6 * rows + 2 * OWN), (corner_x, PACKET + FIELDS2))
    ):
        out[1, q : q + 1] = halo_tiles(even_x, packets, lo, lo + 1)[0][2]


def level1_kernel(
    own, first, second, edge_a, edge_b, fields2, coef1, gain, packet, to_first, to_second, to_far, keep, y1, d1
):
    b1, x1 = keep.at[0], keep.at[1]
    even = is_even("gy")
    for t in (0, 1):
        b1[t, 1 + OWN : 1 + 2 * OWN] = own[t]
        strip = slice(t * OWN, (t + 1) * OWN)
        b1[t, 1 : 1 + OWN] = prev_of(even, first, second, strip)
        b1[t, 1 + 2 * OWN : 1 + 3 * OWN] = next_of(even, first, second, strip)
    g0, g1, g2 = (gain[3 + i] for i in range(3))
    n = GROUPS1
    packed_first(coef1, 0, b1, x1, d1, 1, n, g0)
    packed_step(1, coef1, 0, b1, x1, y1, d1, 1, n, CARRY1, g1)
    packed_step(1, coef1, 0, b1, y1, x1, d1, 1, n, CARRY2, g2)
    here = pl.ds(1 + OWN, OWN)
    for t, (c, other, spread) in enumerate(packed_terms(x1, 1 + OWN, OWN, 1)):
        res = b1[t, here] - coef1[2, t, here] * c + coef1[1, t, here] * other + spread
        value = restrict_12([res[j : j + 1] for j in range(OWN)])
        for ref in (packet, to_first, to_second, to_far):
            ref[t : t + 1] = value
        to_far[2 + t : 3 + t] = fields2[t, 1:2]
    to_first[2:] = edge_a[...]
    to_second[2:] = edge_b[...]


def rest_kernel(
    own2, near_a, near_b, far_a, far_b, gain, coef1, fields2, keep0, iterate, keep1, out, coef2, d1, b2, x2, y2, d2, xu, yu, x0, y0, d0
):
    rows = out.shape[0] // (2 * Z)
    even = (sub_of() & 1) == 0
    b1, x1 = keep1.at[0], keep1.at[1]

    even_y, low = is_even("gy"), lax.rem(lax.axis_index("gy"), 4) < 2
    for t in (0, 1):
        at = slice(t, t + 1)
        parts = [
            next_of(low, far_a, far_b, at),
            prev_of(even_y, near_a, near_b, at),
            own2[at],
            next_of(even_y, near_a, near_b, at),
            prev_of(low, far_a, far_b, at),
        ]
        b2[t, 1 : SIZE2 - 1] = jnp.concatenate(parts, axis=0)
        at = slice(2 + t, 3 + t)
        parts = [next_of(low, far_a, far_b, at), fields2[t], prev_of(low, far_a, far_b, at)]
        inverse, other, _ = packed_jacobian(*split_fields2(jnp.concatenate(parts, axis=0)), 2)
        coef2[0, t, 1 : SIZE2 - 1] = inverse
        coef2[1, t, 1 : SIZE2 - 1] = other

    n = HI2 - LO2
    g0, g1, g2 = (gain[6 + i] for i in range(3))
    packed_first(coef2, 0, b2, x2, d2, 1, n, g0)
    packed_step(2, coef2, 0, b2, x2, y2, d2, 1, n, CARRY1, g1)
    packed_step(2, coef2, 0, b2, y2, x2, d2, 1, n, CARRY2, g2)
    packed_step(2, coef2, 0, b2, x2, y2, d2, 1, n, None, g0)
    packed_step(2, coef2, 0, b2, y2, x2, d2, 1, n, CARRY1, g1)
    packed_step(2, coef2, 0, b2, x2, y2, d2, 1, n, CARRY2, g2)

    g0, g1, g2 = (gain[3 + i] for i in range(3))
    shift = LO_UP - LO1
    for t in (0, 1):
        for g in range(LO_UP, HI_UP):
            p = g % 4
            value = y2[t, g // 4 - LO2 + 1 : g // 4 - LO2 + 2]
            value = spread_x(spread_x(value, 1, p & 1), 2, p & 2)
            at = g - LO_UP + 1
            xu[t, at : at + 1] = x1[t, at + shift : at + shift + 1] + value
    n = HI_UP - LO_UP
    packed_step(1, coef1, shift, b1, xu, yu, d1, 1, n, None, g0)
    packed_step(1, coef1, shift, b1, yu, xu, d1, 1, n, CARRY1, g1)
    packed_step(1, coef1, shift, b1, xu, yu, d1, 1, n, CARRY2, g2)

    g0, g1, g2 = (gain[i] for i in range(3))
    for i in (0, 1):
        for at, take in ((HALO0 - EDGE, prev_of), (HALO0 + rows, next_of)):
            whole = take(even_y, near_a, near_b, slice(2, 2 + EDGE_TILES))
            x0[i, 0, at : at + EDGE] = whole[i * EDGE : (i + 1) * EDGE]
            for j in range(EDGE):
                x0[i, 1, at + j : at + j + 1] = roll_x(whole[2 * EDGE :], -(4 + 8 * (i * EDGE + j)))
        for t in (0, 1):
            x0[i, t, HALO0 : HALO0 + rows] = iterate[i, t]
    for t in (0, 1):
        for row in range(-2, rows // 2 + 2):
            at = row // 2 - LO_UP + 1
            value = spread_x(yu[t, at : at + 1], 1, row & 1)
            for i, fine in enumerate((jnp.where(even, value, roll_z(value, 1)), jnp.where(even, roll_z(value, -1), value))):
                for y in (2 * row, 2 * row + 1):
                    if -EDGE <= y < rows + EDGE:
                        x0[i, t, y + HALO0 : y + HALO0 + 1] = x0[i, t, y + HALO0 : y + HALO0 + 1] + fine
    total = rows + 2 * HALO0
    rows_loop(2, total - 2, lambda r, n: cheb_step(0, keep0, x0, y0, d0, r, n, None, g0))
    rows_loop(3, total - 3, lambda r, n: cheb_step(0, keep0, y0, x0, d0, r, n, CARRY1, g1))
    rows_loop(4, total - 4, lambda r, n: cheb_step(0, keep0, x0, y0, d0, r, n, CARRY2, g2))
    for i in (0, 1):
        for y in range(rows):
            out[pl.ds(i * Z * rows + y, Z, stride=rows), :] = y0[i, 0, HALO0 + y]


def call(kernel, out_shapes, scratch, *args, space=pltpu.VMEM, outs=None):
    out = [jax.ShapeDtypeStruct(shape, jnp.float32) for shape in out_shapes]
    return pl.pallas_call(
        kernel,
        out_shape=out,
        in_specs=[pl.BlockSpec(memory_space=space)] * len(args),
        out_specs=[pl.BlockSpec(memory_space=m) for m in outs or [pltpu.VMEM] * len(out)],
        scratch_shapes=[pltpu.VMEM(s, jnp.float32) if isinstance(s, tuple) else s for s in scratch],
        compiler_params=pltpu.CompilerParams(vmem_limit_bytes=24 * 2**20),
    )(*args)


def swap(value, axis, step):
    count = lax.axis_size(axis)
    assert count % 2 == 0
    pairs = [(i, (i + step) % count) for i in range(0, count, 2)]
    return lax.ppermute(value, axis, pairs + [(j, i) for i, j in pairs])


def swap_far(value, axis, step):
    count = lax.axis_size(axis)
    assert count % 4 == 0
    pairs = [(i + j, (i + j + 2 * step) % count) for i in range(0, count, 4) for j in (0, 1)]
    return lax.ppermute(value, axis, pairs + [(j, i) for i, j in pairs])


def exchange(first, second, axis):
    return swap(first, axis, -1), swap(second, axis, 1)


def body(state, previous, feed, kill):
    _, depth, rows, cols = state.shape
    assert depth == Z and cols == X and rows == 4 * OWN
    across, count = lax.axis_size("gx"), lax.axis_size("gy")
    total0 = rows + 2 * HALO0
    state = state.reshape(2 * Z * rows, X)
    previous = previous.reshape(2 * Z * rows, X)
    feed = feed.reshape(Z * rows, X)
    kill = kill.reshape(Z * rows, X)
    inputs = (state, previous, feed, kill)

    strip = (FIELDS2 + 1, Z, X)
    first, second, main, coarse = call(
        functools.partial(first_kernel, rows),
        [strip, strip, (6, rows, Z, X), (2 * OWN + 1, Z, X)],
        [*(a.shape for a in inputs), pltpu.SemaphoreType.DMA((4,))],
        *(pltpu.with_memory_space_constraint(a, pltpu.HBM) for a in inputs),
        space=pltpu.HBM,
    )
    y_packets = exchange(first, second, "gy")
    tiles = tiles_for(6 * rows + 2 * OWN + 1)
    spread_shape = (across * count, Z // 2, X)
    first, second, spread = call(
        functools.partial(pack_own_kernel, rows),
        [(tiles, Z, X), (tiles, Z, X), spread_shape],
        [(PER * tiles, Z, X), spread_shape, pltpu.SemaphoreType.DMA],
        main,
        coarse,
        outs=[pltpu.VMEM, pltpu.VMEM, pltpu.HBM],
    )
    own_x = exchange(first, second, "gx")
    spread = lax.all_to_all(spread, ("gx", "gy"), 0, 0, tiled=True)
    tiles = tiles_for(2 * PACKET)
    corner_x = exchange(
        *call(pack_corner_kernel, [(tiles, Z, X), (tiles, Z, X)], [(PER * tiles, Z, X)], *y_packets), "gx"
    )

    strip, edge = (2 * OWN, Z, X), (EDGE_TILES, Z, X)
    pair0 = (2, 2, total0, Z, X)
    work = [(6, 2, total0, Z, X), (6, 2, total0, Z, X), pair0, pair0, pair0, pair0]
    four = (4, 2, OWN, Z, X)
    inside = call(
        functools.partial(level0_inner_kernel, rows),
        [
            (6, 2, rows - 2, Z, X),
            (2, 2, 4, Z, X),
            (2, 2, rows - 4, Z, X),
            (2, 2, rows - 6, Z, X),
            (2, 2, 6, Z, X),
            four,
        ],
        work,
        main,
        *own_x,
    )
    keep_in, _, y1_in, y2_in, _, _ = inside
    keep_out, y1_out, y2_out, sources, edges = call(
        functools.partial(level0_outer_kernel, rows),
        [(6, 2, 8, Z, X), (2, 2, 4, Z, X), (2, 2, 6, Z, X), four, (3, 2, *edge)],
        work,
        main,
        *y_packets,
        *own_x,
        *corner_x,
        *inside,
    )
    own, first, second, edge_a, edge_b, gain = call(
        combine_kernel,
        [(2, OWN, Z, X), strip, strip, edge, edge, (POWERS + 3, Z, X)],
        [],
        sources,
        edges,
        spread,
    )
    coef1, keep0, iterate = call(
        functools.partial(coarse1_kernel, rows),
        [(3, 2, SIZE1, Z, X), (6, 2, total0, Z, X), (2, 2, rows, Z, X)],
        [(2, 2 * GROUPS1, Z, X)],
        coarse,
        *y_packets,
        *own_x,
        *corner_x,
        gain,
        keep_in,
        y1_in,
        y2_in,
        keep_out,
        y1_out,
        y2_out,
    )
    (fields2,) = call(
        functools.partial(fields2_kernel, rows), [(2, 3, Z, X)], [], coarse, *y_packets, *own_x, *corner_x
    )
    b_packets = exchange(first, second, "gy")

    one, two, up = (2, SIZE1, Z, X), (2, SIZE2, Z, X), (2, SIZE_UP, Z, X)
    near = (2 + EDGE_TILES, Z, X)
    packet, first, second, to_far, keep1 = call(
        level1_kernel,
        [(2, Z, X), near, near, (4, Z, X), (2, *one)],
        [one, one],
        own,
        *b_packets,
        edge_a,
        edge_b,
        fields2,
        coef1,
        gain,
    )
    far = (swap_far(to_far, "gy", 1), swap_far(to_far, "gy", -1))
    near = exchange(first, second, "gy")

    (out,) = call(
        rest_kernel,
        [(2 * Z * rows, X)],
        [(2, *two), one, two, two, two, two, up, up, pair0, pair0, pair0],
        packet,
        *near,
        *far,
        gain,
        coef1,
        fields2,
        keep0,
        iterate,
        keep1,
    )
    return out.reshape(2, Z, rows, X)


def solution(mesh):
    placed = (
        P(None, None, "gy", "gx"),
        P(None, None, "gy", "gx"),
        P(None, "gy", "gx"),
        P(None, "gy", "gx"),
    )
    return jax.shard_map(
        body, mesh=mesh, in_specs=placed, out_specs=P(None, None, "gy", "gx"), check_vma=False
    )
```

```python
import functools

import jax
import jax.numpy as jnp
from jax import lax
from jax.experimental import pallas as pl
from jax.experimental.pallas import tpu as pltpu
from jax.sharding import PartitionSpec as P

DIFF = (40.0, 20.0)
INV_STEP = 2.0
LOWER = 0.25

_CENTRE = (1.0 + LOWER) / 2.0
_HALF = (1.0 - LOWER) / 2.0
_SIGMA = _CENTRE / _HALF
_RHO0 = 1.0 / _SIGMA
_RHO1 = 1.0 / (2.0 * _SIGMA - _RHO0)
_RHO2 = 1.0 / (2.0 * _SIGMA - _RHO1)

Z = 8
X = 128
HALO0 = 4
SENT = 3
FIELDS1 = 6 * SENT
FIELDS2 = FIELDS1 + 8
PACKET = FIELDS2 + 1
WIDE = 42
PER = X // WIDE
EDGE = 3

LO1, HI1 = -4, 8
LO2, HI2 = -2, 3
LO_UP, HI_UP = -3, 7
SIZE1, SIZE2, SIZE_UP = HI1 - LO1 + 2, HI2 - LO2 + 2, HI_UP - LO_UP + 2
OWN = 4


def lane_of():
    return lax.broadcasted_iota(jnp.int32, (1, Z, X), 2)


def sub_of():
    return lax.broadcasted_iota(jnp.int32, (1, Z, X), 1)


def roll_x(tile, shift):
    shift = shift % X
    return pltpu.roll(tile, shift, 2) if shift else tile


def roll_z(tile, shift):
    shift = shift % Z
    return pltpu.roll(tile, shift, 1) if shift else tile


def rows_loop(lo, hi, body, step=None):
    step = step or hi - lo
    full = (hi - lo) // step
    if full == 1:
        body(lo, step)
    elif full > 1:

        def trip(i, carry):
            body(lo + i * step, step)
            return carry

        lax.fori_loop(0, full, trip, 0)
    rest = hi - lo - full * step
    if rest:
        body(hi - rest, rest)


def neighbour_sums(read, r, n, k, tiles=(0, 1)):
    lane = lane_of()
    low, high = lane < k, lane >= X - k
    centre = [read(t, r, n) for t in (0, 1)]
    right = [roll_x(c, k) for c in centre]
    left = [roll_x(c, -k) for c in centre]
    sums = []
    for t in tiles:
        c = centre[t]
        along_x = jnp.where(low, right[1 - t], right[t]) + jnp.where(high, left[1 - t], left[t])
        along_y = read(t, r - 1, n) + read(t, r + 1, n)
        along_z = 2.0 * roll_z(c, k) if 2 * k == Z else roll_z(c, k) + roll_z(c, -k)
        sums.append(along_x + along_y + along_z)
    return centre, sums


def jacobian(u, v, f, k, level):
    scale = 0.25**level
    product = u * v
    squared = v * v
    first = INV_STEP + squared + f + 6.0 * DIFF[0] * scale
    second = INV_STEP + f + k - 2.0 * product + 6.0 * DIFF[1] * scale
    return 2.0 * product, squared, 1.0 / first, 1.0 / second, first, second


def cheb_step(level, keep, source, target, d, r, n, carry, gain, tiles=(0, 1)):
    scale = 0.25**level
    k = 1 << level
    u, nb_u = neighbour_sums(lambda t, a, m: source[0, t, pl.ds(a, m)], r, n, k, tiles)
    v, nb_v = neighbour_sums(lambda t, a, m: source[1, t, pl.ds(a, m)], r, n, k, tiles)
    rows = pl.ds(r, n)
    out = []
    for t in tiles:
        cross, squared, inv_u, inv_v = (keep[i, t, rows] for i in range(4))
        res_u = inv_u * (keep[4, t, rows] - cross * v[t] + DIFF[0] * scale * nb_u[t]) - u[t]
        res_v = inv_v * (keep[5, t, rows] + squared * u[t] + DIFF[1] * scale * nb_v[t]) - v[t]
        du, dv = gain * res_u, gain * res_v
        if carry is not None:
            du = du + carry * d[0, t, rows]
            dv = dv + carry * d[1, t, rows]
        if target is not None:
            d[0, t, rows] = du
            d[1, t, rows] = dv
            target[0, t, rows] = u[t] + du
            target[1, t, rows] = v[t] + dv
        out.append((u[t] + du, v[t] + dv))
    return out


def next_power(keep, source, r, n):
    u, nb_u = neighbour_sums(lambda t, a, m: source[0, t, pl.ds(a, m)], r, n, 1)
    v, nb_v = neighbour_sums(lambda t, a, m: source[1, t, pl.ds(a, m)], r, n, 1)
    rows = pl.ds(r, n)
    first, second = [], []
    for t in (0, 1):
        cross, squared, inv_u, inv_v = (keep[i, t, rows] for i in range(4))
        first.append(u[t] + inv_u * (cross * v[t] - DIFF[0] * nb_u[t]))
        second.append(v[t] - inv_v * (squared * u[t] + DIFF[1] * nb_v[t]))
    return first, second


CARRY1 = _RHO1 * _RHO0
CARRY2 = _RHO2 * _RHO1


POWERS = 9


def write_gains(spread, out):
    lane = lax.broadcasted_iota(jnp.int32, (1, X), 1)
    for level in range(3):
        top = jnp.max(jnp.where(lane == level, spread, 0.0), axis=1, keepdims=True)
        tau = 1.0 / (1.0 + jnp.broadcast_to(top, (Z, X)))
        for i, factor in enumerate((1.0 / _CENTRE, 2.0 * _RHO1 / _HALF, 2.0 * _RHO2 / _HALF)):
            out[3 * level + i] = factor * tau
    g0, g1, g2 = (out[i] for i in range(3))
    first, second = g0 + CARRY1 * g0 + g1, g1 * g0
    out[POWERS] = first + CARRY2 * (CARRY1 * g0 + g1) + g2
    out[POWERS + 1] = second + CARRY2 * second + g2 * first
    out[POWERS + 2] = g2 * second


def pair_rows(value):
    n = value.shape[0] // 2
    pairs = value.reshape(n, 2, Z, X)
    return pairs[:, 0] + pairs[:, 1]


def restrict_01(first, second):
    lane, sub = lane_of(), sub_of()
    across = []
    for value in (first, second):
        a, b = value[0:1], value[1:2]
        across.append(jnp.where((lane & 1) == 0, a + roll_x(a, -1), b + roll_x(b, 1)))
    a, b = across
    return 0.125 * jnp.where((sub & 1) == 0, a + roll_z(a, -1), b + roll_z(b, 1))


def restrict_12(groups):
    lane, sub = lane_of(), sub_of()
    out = None
    for p, value in enumerate(groups):
        value = value + roll_x(value, 1 if p & 1 else -1)
        value = value + roll_x(value, 2 if p & 2 else -2)
        out = value if out is None else jnp.where((lane & 3) == p, value, out)
    return 0.125 * (out + jnp.where((sub & 2) == 0, roll_z(out, -2), roll_z(out, 2)))


def spread_x(tile, k, phase):
    return jnp.where((lane_of() & k) == phase, tile, roll_x(tile, -k if phase else k))


def packed_jacobian(uv, fk, level):
    scale = 0.25**level
    even = (sub_of() & 1) == 0
    u, v = jnp.where(even, uv, roll_z(uv, 1)), jnp.where(even, roll_z(uv, -1), uv)
    f, k = jnp.where(even, fk, roll_z(fk, 1)), jnp.where(even, roll_z(fk, -1), fk)
    product, squared = u * v, v * v
    diag = jnp.where(
        even,
        INV_STEP + squared + f + 6.0 * DIFF[0] * scale,
        INV_STEP + f + k - 2.0 * product + 6.0 * DIFF[1] * scale,
    )
    return 1.0 / diag, jnp.where(even, -2.0 * product, squared), diag


def packed_spread(uv, fk, level):
    scale = 0.25**level
    even = (sub_of() & 1) == 0
    inverse, other, _ = packed_jacobian(uv, fk, level)
    return jnp.where(even, 6.0 * DIFF[0] * scale - other, 6.0 * DIFF[1] * scale + other) * inverse


def packed_terms(source, g, n, level):
    k = 1 << level
    lane, sub = lane_of(), sub_of()
    even = (sub & 1) == 0
    first, last = (lane & (k - 1)) == 0, (lane & (k - 1)) == k - 1
    low, high = lane < k, lane >= X - k
    diff = jnp.where(even, DIFF[0] * 0.25**level, DIFF[1] * 0.25**level)
    wide = [source[t, pl.ds(g - 1, n + 2)] for t in (0, 1)]
    centre = [w[1 : n + 1] for w in wide]
    right = [roll_x(c, k) for c in centre]
    left = [roll_x(c, -k) for c in centre]
    out = []
    for t in (0, 1):
        c, w = centre[t], wide[t]
        total = jnp.where(low, right[1 - t], right[t]) + jnp.where(high, left[1 - t], left[t])
        if k == 2:
            ahead, back = roll_x(w, 1), roll_x(w, -1)
            total = total + jnp.where(first, back[0:n], ahead[1 : n + 1])
            total = total + jnp.where(last, ahead[2 : n + 2], back[1 : n + 1])
            total = total + roll_z(c, 2) + roll_z(c, -2)
        else:
            total = total + jnp.where(first, roll_x(w[0:n], -(k - 1)), roll_x(c, 1))
            total = total + jnp.where(last, roll_x(w[2 : n + 2], k - 1), roll_x(c, -1))
            total = total + 2.0 * roll_z(c, 4)
        other = jnp.where(even, roll_z(c, -1), roll_z(c, 1))
        out.append((c, other, diff * total))
    return out


def packed_first(coef, shift, b, target, d, g, n, gain):
    for t in (0, 1):
        value = gain * coef[0, t, pl.ds(g + shift, n)] * b[t, pl.ds(g + shift, n)]
        d[t, pl.ds(g, n)] = value
        target[t, pl.ds(g, n)] = value


def packed_step(level, coef, shift, b, source, target, d, g, n, carry, gain):
    for t, (c, other, spread) in enumerate(packed_terms(source, g, n, level)):
        at = pl.ds(g + shift, n)
        res = coef[0, t, at] * (b[t, at] + coef[1, t, at] * other + spread) - c
        delta = gain * res
        if carry is not None:
            delta = delta + carry * d[t, pl.ds(g, n)]
        d[t, pl.ds(g, n)] = delta
        target[t, pl.ds(g, n)] = c + delta


def plane(ref, f, y, rows):
    return ref[pl.ds(f * Z * rows + y, Z, stride=rows), :]


def is_even(axis):
    return lax.rem(lax.axis_index(axis), 2) == 0


def prev_of(even, first, second, at):
    return jnp.where(even, first[at], second[at])


def next_of(even, first, second, at):
    return jnp.where(even, second[at], first[at])


SOURCES = ((0, 0), (0, 1), (1, 0), (1, 1), (2, 0), (3, 0))


def first_kernel(rows, state, previous, feed, kill, first, second, coarse, *rest):
    held, sems = rest[:4], rest[4]
    copies = [
        pltpu.make_async_copy(ref, to, sems.at[i]) for i, (ref, to) in enumerate(zip((state, previous, feed, kill), held))
    ]
    for copy in copies:
        copy.start()
    for copy in copies:
        copy.wait()
    even = is_even("gy")
    values = []
    for i, (j, f) in enumerate(SOURCES):
        wanted = range(rows) if i not in (2, 3) else [*range(SENT), *range(rows - SENT, rows)]
        values.append({y: plane(held[j], f, y, rows)[None] for y in wanted})
    for i in (2, 3):
        weight = DIFF[i - 2] / INV_STEP
        values[i][SENT - 1] = values[i][SENT - 1] + weight * values[i - 2][SENT]
        values[i][rows - SENT] = values[i][rows - SENT] + weight * values[i - 2][rows - SENT - 1]
    for i in range(6):
        for y in range(SENT):
            top, bottom = values[i][y], values[i][rows - SENT + y]
            at = slice(i * SENT + y, i * SENT + y + 1)
            first[at] = jnp.where(even, top, bottom)
            second[at] = jnp.where(even, bottom, top)
    pairs = []
    for p, (i, j) in enumerate(((0, 1), (4, 5))):
        parts = []
        for g in range(OWN):
            sums = [
                jnp.concatenate([value[4 * g + 2 * q] + value[4 * g + 2 * q + 1] for q in (0, 1)], axis=0)
                for value in (values[i], values[j])
            ]
            parts.append(restrict_01(*sums))
        pairs.append(jnp.concatenate(parts, axis=0))
        coarse[p * OWN : (p + 1) * OWN] = pairs[p]
        for ref in (first, second):
            ref[FIELDS1 + p * OWN : FIELDS1 + (p + 1) * OWN] = pairs[p]
    uv, fk = (restrict_12([pair[j : j + 1] for j in range(OWN)]) for pair in pairs)
    both = jnp.where((sub_of() & 2) == 0, uv, fk)
    coarse[2 * OWN : 2 * OWN + 1] = both
    for ref in (first, second):
        ref[FIELDS2 : FIELDS2 + 1] = both


def split_fields2(both):
    low = (sub_of() & 2) == 0
    return jnp.where(low, both, roll_z(both, 2)), jnp.where(low, roll_z(both, -2), both)


def write_spread(main, coarse, out):
    lane = lax.broadcasted_iota(jnp.int32, (1, X), 1)
    u, v, f, k = (main[i] for i in (0, 1, 4, 5))
    cross, squared, inv_u, inv_v, _, _ = jacobian(u, v, f, k, 0)
    tops = [jnp.max(jnp.maximum((6.0 * DIFF[0] + cross) * inv_u, (6.0 * DIFF[1] + squared) * inv_v), axis=0)]
    tops.append(jnp.max(packed_spread(coarse[0:OWN], coarse[OWN : 2 * OWN], 1), axis=0))
    tops.append(packed_spread(*split_fields2(coarse[2 * OWN : 2 * OWN + 1]), 2)[0])
    result = jnp.zeros((1, X), jnp.float32)
    for level, top in enumerate(tops):
        top = jnp.max(jnp.max(top, axis=0, keepdims=True), axis=1, keepdims=True)
        result = jnp.where(lane == level, jnp.broadcast_to(top, (1, X)), result)
    out[...] = jnp.broadcast_to(result[None], out.shape)


GROUPS1 = HI1 - LO1
GROUPS2 = HI2 - LO2


def tiles_for(entries):
    return -(-entries // PER)


def pack_edges(entries, even, first, second):
    lane = lane_of()
    share = first.shape[0]
    left, right = None, None
    for j in range(PER):
        part = entries[j * share : (j + 1) * share]
        a, b = roll_x(part, WIDE * j), roll_x(part, WIDE + WIDE * j)
        left = a if left is None else jnp.where(lane >= WIDE * j, a, left)
        right = b if right is None else jnp.where(lane >= WIDE * j, b, right)
    first[...] = jnp.where(even, left, right)
    second[...] = jnp.where(even, right, left)


def halo_tiles(even, packets, lo, hi):
    first, second = packets
    share = first.shape[0]
    lane = lane_of()
    out = []
    for j in range(PER):
        a, b = max(lo, j * share), min(hi, (j + 1) * share)
        if a < b:
            strip = slice(a - j * share, b - j * share)
            left, right = prev_of(even, first, second, strip), next_of(even, first, second, strip)
            value = jnp.where(lane < X // 2, roll_x(right, -WIDE * j), roll_x(left, X - WIDE - WIDE * j))
            out.append((a - lo, b - lo, value))
    return out


def pack_own_kernel(
    rows, state, previous, feed, kill, coarse, first, second, spread, main, held, copies, sem
):
    inputs = (state, previous, feed, kill)
    for i, (j, f) in enumerate(SOURCES):
        for y in range(rows):
            main[i, y] = plane(inputs[j], f, y, rows)
    write_spread(main, coarse, copies)
    copy = pltpu.make_async_copy(copies, spread, sem)
    copy.start()
    for i in range(6):
        held[i * rows : (i + 1) * rows] = main[i]
    held[6 * rows : 6 * rows + 2 * OWN + 1] = coarse[...]
    pack_edges(held, is_even("gx"), first, second)
    copy.wait()


def pack_corner_kernel(y_first, y_second, first, second, held):
    even = is_even("gy")
    every = slice(0, PACKET)
    held[0:PACKET] = prev_of(even, y_first, y_second, every)
    held[PACKET : 2 * PACKET] = next_of(even, y_first, y_second, every)
    pack_edges(held, is_even("gx"), first, second)


EDGE_TILES = 2 * EDGE + 1


def level0_setup(fields, keep, diag, power, r, n):
    at = pl.ds(r, n)
    u, nb_u = neighbour_sums(lambda t, a, m: fields[0, t, pl.ds(a, m)], r, n, 1)
    v, nb_v = neighbour_sums(lambda t, a, m: fields[1, t, pl.ds(a, m)], r, n, 1)
    for t in (0, 1):
        f, k = fields[4, t, at], fields[5, t, at]
        cross, squared, inv_u, inv_v, first, second = jacobian(u[t], v[t], f, k, 0)
        react = u[t] * squared
        b_u = DIFF[0] * (nb_u[t] - 6.0 * u[t]) - INV_STEP * (u[t] - fields[2, t, at]) - react + f * (1.0 - u[t])
        b_v = DIFF[1] * (nb_v[t] - 6.0 * v[t]) - INV_STEP * (v[t] - fields[3, t, at]) + react - (f + k) * v[t]
        for i, value in enumerate((cross, squared, inv_u, inv_v, b_u, b_v)):
            keep[i, t, at] = value
        for i, value in enumerate((first, second)):
            diag[i, t, at] = value
        for i, value in enumerate((inv_u * b_u, inv_v * b_v)):
            power[i, t, at] = value


def level0_power(keep, source, target, r, n):
    for i, values in enumerate(next_power(keep, source, r, n)):
        for t in (0, 1):
            target[i, t, pl.ds(r, n)] = values[t]


def level0_down(keep, diag, y1, y2, sources, r, n):
    at = pl.ds(r, n)
    last = next_power(keep, y2, r, n)
    for t in (0, 1):
        both = [diag[i, t, at] for i in (0, 1)]
        parts = [[keep[4 + i, t, at] for i in (0, 1)]]
        parts += [[both[i] * power[i, t, at] for i in (0, 1)] for power in (y1, y2)]
        parts.append([both[i] * last[i][t] for i in (0, 1)])
        for q, part in enumerate(parts):
            u, v = (pair_rows(value) for value in part)
            for j in range(n // 4):
                value = restrict_01(u[2 * j : 2 * j + 2], v[2 * j : 2 * j + 2])
                sources[q, t, pl.ds((r - HALO0) // 4 + j, 1)] = value


def inner(rows, lost):
    return slice(HALO0 + lost, HALO0 + rows - lost)


def ends(rows, lo, hi):
    total = rows + 2 * HALO0
    return slice(lo, hi), slice(total - hi, total - lo)


def put_ends(target, rows, lo, hi, source):
    n = hi - lo
    for at, part in zip(ends(rows, lo, hi), (slice(0, n), slice(n, 2 * n))):
        for i in range(target.shape[0]):
            for t in (0, 1):
                target[i, t, at] = source[i, t, part]


def take_ends(source, rows, lo, hi, target):
    n = hi - lo
    for at, part in zip(ends(rows, lo, hi), (slice(0, n), slice(n, 2 * n))):
        for i in range(source.shape[0]):
            for t in (0, 1):
                target[i, t, part] = source[i, t, at]


def level0_inner_kernel(rows, main, own_a, own_b, keep_in, y0_in, y1_in, y2_in, diag_in, sources_in, *scratch):
    fields, keep, diag, y0, y1, y2 = scratch
    even_x = is_even("gx")
    for i in range(6):
        fields[i, 0, HALO0 : HALO0 + rows] = main[i]
        for a, b, value in halo_tiles(even_x, (own_a, own_b), i * rows, (i + 1) * rows):
            fields[i, 1, HALO0 + a : HALO0 + b] = value
    first = HALO0 + 1
    level0_setup(fields, keep, diag, y0, first, rows - 2)
    level0_power(keep, y0, y1, first + 1, rows - 4)
    level0_power(keep, y1, y2, first + 2, rows - 6)
    level0_down(keep, diag, y1, y2, sources_in, first + 3, rows - 8)
    for source, target, lost in ((keep, keep_in, 1), (y1, y1_in, 2), (y2, y2_in, 3)):
        for i in range(source.shape[0]):
            for t in (0, 1):
                target[i, t] = source[i, t, inner(rows, lost)]
    take_ends(y0, rows, HALO0 + 1, HALO0 + 3, y0_in)
    take_ends(diag, rows, HALO0 + 1, HALO0 + 4, diag_in)


def level0_outer_kernel(
    rows,
    main,
    y_first,
    y_second,
    own_a,
    own_b,
    corner_a,
    corner_b,
    keep_in,
    y0_in,
    y1_in,
    y2_in,
    diag_in,
    sources_in,
    keep_out,
    y1_out,
    y2_out,
    sources,
    edges,
    *scratch,
):
    fields, keep, diag, y0, y1, y2 = scratch
    even, even_x = is_even("gy"), is_even("gx")
    total = rows + 2 * HALO0
    near, skip = HALO0 + 2, HALO0 - SENT
    for i in range(6):
        strip = slice(i * SENT, (i + 1) * SENT)
        fields[i, 0, skip:HALO0] = prev_of(even, y_first, y_second, strip)
        fields[i, 0, HALO0:near] = main[i, 0:2]
        fields[i, 0, total - near : total - HALO0] = main[i, rows - 2 : rows]
        fields[i, 0, HALO0 + rows : total - skip] = next_of(even, y_first, y_second, strip)
        for packets, lo, n, at in (
            ((corner_a, corner_b), i * SENT, SENT, skip),
            ((own_a, own_b), i * rows, 2, HALO0),
            ((own_a, own_b), (i + 1) * rows - 2, 2, total - near),
            ((corner_a, corner_b), PACKET + i * SENT, SENT, HALO0 + rows),
        ):
            for a, b, value in halo_tiles(even_x, packets, lo, lo + n):
                fields[i, 1, at + a : at + b] = value
    for i in (0, 1):
        for t in (0, 1):
            for at in (0, total - 1):
                fields[i, t, at] = jnp.zeros((Z, X), jnp.float32)
    for at, part in zip(ends(rows, 5, 8), (slice(0, 3), slice(rows - 5, rows - 2))):
        for i in range(6):
            for t in (0, 1):
                keep[i, t, at] = keep_in[i, t, part]
    put_ends(diag, rows, 5, 8, diag_in)
    put_ends(y0, rows, 5, 7, y0_in)
    for target, source, lost in ((y1, y1_in, 2), (y2, y2_in, 3)):
        n = rows - 2 * lost
        for at, part in zip(ends(rows, HALO0 + lost, HALO0 + lost + 2), (slice(0, 2), slice(n - 2, n))):
            for i in (0, 1):
                for t in (0, 1):
                    target[i, t, at] = source[i, t, part]
    for r in (1, total - 5):
        level0_setup(fields, keep, diag, y0, r, 4)
    for r in (2, total - 6):
        level0_power(keep, y0, y1, r, 4)
    for r in (3, total - 7):
        level0_power(keep, y1, y2, r, 4)
    for r in (4, total - 8):
        level0_down(keep, diag, y1, y2, sources, r, 4)
    for q in range(4):
        for t in (0, 1):
            sources[q, t, 1 : OWN - 1] = sources_in[q, t, 1 : OWN - 1]
    take_ends(keep, rows, 1, 5, keep_out)
    take_ends(y1, rows, 4, 6, y1_out)
    take_ends(y2, rows, 4, 7, y2_out)
    for p, power in enumerate((y0, y1, y2)):
        for side, start in enumerate((HALO0, HALO0 + rows - EDGE)):
            edges[p, side] = pack_rows(power, start)


def pack_rows(x, start):
    lane = lane_of()
    halo = None
    for i in (0, 1):
        for j in range(EDGE):
            at = i * EDGE + j
            value = roll_x(x[i, 1, start + j : start + j + 1], 4 + 8 * at)
            halo = value if halo is None else jnp.where((lane >> 3) == at, value, halo)
    return jnp.concatenate([x[i, 0, start : start + EDGE] for i in (0, 1)] + [halo], axis=0)


def combine_kernel(sources, edges, spread, own, first, second, edge_first, edge_second, gain):
    write_gains(jnp.max(spread[...], axis=0)[0:1], gain)
    p0, p1, p2 = (gain[POWERS + i] for i in range(3))
    for t in (0, 1):
        value = sources[0, t] - p0 * sources[1, t] + p1 * sources[2, t] - p2 * sources[3, t]
        own[t] = value
        for ref in (first, second):
            ref[t * OWN : (t + 1) * OWN] = value
    even = is_even("gy")
    top, bottom = (p0 * edges[0, side] - p1 * edges[1, side] + p2 * edges[2, side] for side in (0, 1))
    edge_first[...] = jnp.where(even, top, bottom)
    edge_second[...] = jnp.where(even, bottom, top)


def coarse1_kernel(
    rows, coarse, y_first, y_second, own_a, own_b, corner_a, corner_b, gain, keep_in, y1_in, y2_in, keep_out, y1_out, y2_out,
    coef, keep0, x0, fields
):
    even, even_x = is_even("gy"), is_even("gx")
    own_x, corner_x = (own_a, own_b), (corner_a, corner_b)
    for p in (0, 1):
        to = p * GROUPS1
        strip = slice(FIELDS1 + p * OWN, FIELDS1 + (p + 1) * OWN)
        fields[0, to : to + OWN] = prev_of(even, y_first, y_second, strip)
        fields[0, to + OWN : to + 2 * OWN] = coarse[p * OWN : (p + 1) * OWN]
        fields[0, to + 2 * OWN : to + 3 * OWN] = next_of(even, y_first, y_second, strip)
        for part, (packets, lo) in enumerate(
            ((corner_x, FIELDS1), (own_x, 6 * rows), (corner_x, PACKET + FIELDS1))
        ):
            lo += p * OWN
            for a, b, value in halo_tiles(even_x, packets, lo, lo + OWN):
                fields[1, to + part * OWN + a : to + part * OWN + b] = value
    for t in (0, 1):
        for i, value in enumerate(packed_jacobian(fields[t, 0:GROUPS1], fields[t, GROUPS1 : 2 * GROUPS1], 1)):
            coef[i, t, 1 : SIZE1 - 1] = value

    def whole(inside, outside):
        n = outside.shape[0] // 2
        return jnp.concatenate([outside[0:n], inside, outside[n:]], axis=0)

    for i in range(6):
        for t in (0, 1):
            keep0[i, t, 1 : rows + 2 * HALO0 - 1] = whole(keep_in[i, t], keep_out[i, t])
    p0, p1, p2 = (gain[POWERS + i] for i in range(3))
    for i in (0, 1):
        for t in (0, 1):
            y0 = keep0[2 + i, t, HALO0 : HALO0 + rows] * keep0[4 + i, t, HALO0 : HALO0 + rows]
            y1, y2 = (whole(a[i, t], b[i, t]) for a, b in ((y1_in, y1_out), (y2_in, y2_out)))
            x0[i, t] = p0 * y0 - p1 * y1 + p2 * y2


def fields2_kernel(rows, coarse, y_first, y_second, own_a, own_b, corner_a, corner_b, out):
    even, even_x = is_even("gy"), is_even("gx")
    own_x, corner_x = (own_a, own_b), (corner_a, corner_b)
    near = slice(FIELDS2, FIELDS2 + 1)
    out[0, 0:1] = prev_of(even, y_first, y_second, near)
    out[0, 1:2] = coarse[2 * OWN : 2 * OWN + 1]
    out[0, 2:3] = next_of(even, y_first, y_second, near)
    for q, (packets, lo) in enumerate(
        ((corner_x, FIELDS2), (own_x, 6 * rows + 2 * OWN), (corner_x, PACKET + FIELDS2))
    ):
        out[1, q : q + 1] = halo_tiles(even_x, packets, lo, lo + 1)[0][2]


def level1_kernel(
    own, first, second, edge_a, edge_b, fields2, coef1, gain, packet, to_first, to_second, to_far, keep, y1, d1
):
    b1, x1 = keep.at[0], keep.at[1]
    even = is_even("gy")
    for t in (0, 1):
        b1[t, 1 + OWN : 1 + 2 * OWN] = own[t]
        strip = slice(t * OWN, (t + 1) * OWN)
        b1[t, 1 : 1 + OWN] = prev_of(even, first, second, strip)
        b1[t, 1 + 2 * OWN : 1 + 3 * OWN] = next_of(even, first, second, strip)
    g0, g1, g2 = (gain[3 + i] for i in range(3))
    n = GROUPS1
    packed_first(coef1, 0, b1, x1, d1, 1, n, g0)
    packed_step(1, coef1, 0, b1, x1, y1, d1, 1, n, CARRY1, g1)
    packed_step(1, coef1, 0, b1, y1, x1, d1, 1, n, CARRY2, g2)
    here = pl.ds(1 + OWN, OWN)
    values = []
    for t, (c, other, spread) in enumerate(packed_terms(x1, 1 + OWN, OWN, 1)):
        res = b1[t, here] - coef1[2, t, here] * c + coef1[1, t, here] * other + spread
        values.append(restrict_12([res[j : j + 1] for j in range(OWN)]))
        to_far[1 + t : 2 + t] = fields2[t, 1:2]
    value = jnp.where((sub_of() & 2) == 0, values[0], values[1])
    for ref in (packet, to_first, to_second, to_far):
        ref[0:1] = value
    to_first[1:] = edge_a[...]
    to_second[1:] = edge_b[...]


def rest_kernel(
    own2, near_a, near_b, far_a, far_b, gain, coef1, fields2, keep0, iterate, keep1, out, coef2, d1, b2, x2, y2, d2, xu, yu, x0, y0, d0
):
    rows = out.shape[0] // (2 * Z)
    even = (sub_of() & 1) == 0
    b1, x1 = keep1.at[0], keep1.at[1]

    even_y, low = is_even("gy"), lax.rem(lax.axis_index("gy"), 4) < 2
    at = slice(0, 1)
    parts = [
        next_of(low, far_a, far_b, at),
        prev_of(even_y, near_a, near_b, at),
        own2[at],
        next_of(even_y, near_a, near_b, at),
        prev_of(low, far_a, far_b, at),
    ]
    for t, values in enumerate(split_fields2(jnp.concatenate(parts, axis=0))):
        b2[t, 1 : SIZE2 - 1] = values
        at = slice(1 + t, 2 + t)
        parts = [next_of(low, far_a, far_b, at), fields2[t], prev_of(low, far_a, far_b, at)]
        inverse, other, _ = packed_jacobian(*split_fields2(jnp.concatenate(parts, axis=0)), 2)
        coef2[0, t, 1 : SIZE2 - 1] = inverse
        coef2[1, t, 1 : SIZE2 - 1] = other

    n = HI2 - LO2
    g0, g1, g2 = (gain[6 + i] for i in range(3))
    packed_first(coef2, 0, b2, x2, d2, 1, n, g0)
    packed_step(2, coef2, 0, b2, x2, y2, d2, 1, n, CARRY1, g1)
    packed_step(2, coef2, 0, b2, y2, x2, d2, 1, n, CARRY2, g2)
    packed_step(2, coef2, 0, b2, x2, y2, d2, 1, n, None, g0)
    packed_step(2, coef2, 0, b2, y2, x2, d2, 1, n, CARRY1, g1)
    packed_step(2, coef2, 0, b2, x2, y2, d2, 1, n, CARRY2, g2)

    g0, g1, g2 = (gain[3 + i] for i in range(3))
    shift = LO_UP - LO1
    for t in (0, 1):
        for g in range(LO_UP, HI_UP):
            p = g % 4
            value = y2[t, g // 4 - LO2 + 1 : g // 4 - LO2 + 2]
            value = spread_x(spread_x(value, 1, p & 1), 2, p & 2)
            at = g - LO_UP + 1
            xu[t, at : at + 1] = x1[t, at + shift : at + shift + 1] + value
    n = HI_UP - LO_UP
    packed_step(1, coef1, shift, b1, xu, yu, d1, 1, n, None, g0)
    packed_step(1, coef1, shift, b1, yu, xu, d1, 1, n, CARRY1, g1)
    packed_step(1, coef1, shift, b1, xu, yu, d1, 1, n, CARRY2, g2)

    g0, g1, g2 = (gain[i] for i in range(3))
    for i in (0, 1):
        for at, take in ((HALO0 - EDGE, prev_of), (HALO0 + rows, next_of)):
            whole = take(even_y, near_a, near_b, slice(1, 1 + EDGE_TILES))
            x0[i, 0, at : at + EDGE] = whole[i * EDGE : (i + 1) * EDGE]
            for j in range(EDGE):
                x0[i, 1, at + j : at + j + 1] = roll_x(whole[2 * EDGE :], -(4 + 8 * (i * EDGE + j)))
        for t in (0, 1):
            x0[i, t, HALO0 : HALO0 + rows] = iterate[i, t]
    for t in (0, 1):
        for row in range(-2, rows // 2 + 2):
            at = row // 2 - LO_UP + 1
            value = spread_x(yu[t, at : at + 1], 1, row & 1)
            for i, fine in enumerate((jnp.where(even, value, roll_z(value, 1)), jnp.where(even, roll_z(value, -1), value))):
                for y in (2 * row, 2 * row + 1):
                    if -EDGE <= y < rows + EDGE:
                        x0[i, t, y + HALO0 : y + HALO0 + 1] = x0[i, t, y + HALO0 : y + HALO0 + 1] + fine
    total = rows + 2 * HALO0
    rows_loop(2, total - 2, lambda r, n: cheb_step(0, keep0, x0, y0, d0, r, n, None, g0))
    rows_loop(3, total - 3, lambda r, n: cheb_step(0, keep0, y0, x0, d0, r, n, CARRY1, g1))
    last = cheb_step(0, keep0, x0, None, d0, HALO0, rows, CARRY2, g2, (0,))[0]
    for i in (0, 1):
        for y in range(rows):
            out[pl.ds(i * Z * rows + y, Z, stride=rows), :] = last[i][y]


def call(kernel, out_shapes, scratch, *args, space=pltpu.VMEM, outs=None):
    out = [jax.ShapeDtypeStruct(shape, jnp.float32) for shape in out_shapes]
    return pl.pallas_call(
        kernel,
        out_shape=out,
        in_specs=[pl.BlockSpec(memory_space=space)] * len(args),
        out_specs=[pl.BlockSpec(memory_space=m) for m in outs or [pltpu.VMEM] * len(out)],
        scratch_shapes=[pltpu.VMEM(s, jnp.float32) if isinstance(s, tuple) else s for s in scratch],
        compiler_params=pltpu.CompilerParams(vmem_limit_bytes=24 * 2**20),
    )(*args)


def swap(value, axis, step):
    count = lax.axis_size(axis)
    assert count % 2 == 0
    pairs = [(i, (i + step) % count) for i in range(0, count, 2)]
    return lax.ppermute(value, axis, pairs + [(j, i) for i, j in pairs])


def swap_far(value, axis, step):
    count = lax.axis_size(axis)
    assert count % 4 == 0
    pairs = [(i + j, (i + j + 2 * step) % count) for i in range(0, count, 4) for j in (0, 1)]
    return lax.ppermute(value, axis, pairs + [(j, i) for i, j in pairs])


def exchange(first, second, axis):
    return swap(first, axis, -1), swap(second, axis, 1)


def body(state, previous, feed, kill):
    _, depth, rows, cols = state.shape
    assert depth == Z and cols == X and rows == 4 * OWN
    across, count = lax.axis_size("gx"), lax.axis_size("gy")
    total0 = rows + 2 * HALO0
    state = state.reshape(2 * Z * rows, X)
    previous = previous.reshape(2 * Z * rows, X)
    feed = feed.reshape(Z * rows, X)
    kill = kill.reshape(Z * rows, X)
    inputs = (state, previous, feed, kill)

    strip = (PACKET, Z, X)
    first, second, coarse, *inputs = call(
        functools.partial(first_kernel, rows),
        [strip, strip, (2 * OWN + 1, Z, X), *(a.shape for a in inputs)],
        [pltpu.SemaphoreType.DMA((4,))],
        *(pltpu.with_memory_space_constraint(a, pltpu.HBM) for a in inputs),
        space=pltpu.HBM,
    )
    y_packets = exchange(first, second, "gy")

    tiles = tiles_for(6 * rows + 2 * OWN + 1)
    spread_shape = (across * count, Z // 2, X)
    first, second, spread, main = call(
        functools.partial(pack_own_kernel, rows),
        [(tiles, Z, X), (tiles, Z, X), spread_shape, (6, rows, Z, X)],
        [(PER * tiles, Z, X), spread_shape, pltpu.SemaphoreType.DMA],
        *inputs,
        coarse,
        outs=[pltpu.VMEM, pltpu.VMEM, pltpu.HBM, pltpu.VMEM],
    )
    own_x = exchange(first, second, "gx")
    spread = lax.all_to_all(spread, ("gx", "gy"), 0, 0, tiled=True)
    tiles = tiles_for(2 * PACKET)
    corner_x = exchange(
        *call(pack_corner_kernel, [(tiles, Z, X), (tiles, Z, X)], [(PER * tiles, Z, X)], *y_packets), "gx"
    )

    strip, edge = (2 * OWN, Z, X), (EDGE_TILES, Z, X)
    pair0 = (2, 2, total0, Z, X)
    work = [(6, 2, total0, Z, X), (6, 2, total0, Z, X), pair0, pair0, pair0, pair0]
    four = (4, 2, OWN, Z, X)
    inside = call(
        functools.partial(level0_inner_kernel, rows),
        [
            (6, 2, rows - 2, Z, X),
            (2, 2, 4, Z, X),
            (2, 2, rows - 4, Z, X),
            (2, 2, rows - 6, Z, X),
            (2, 2, 6, Z, X),
            four,
        ],
        work,
        main,
        *own_x,
    )
    keep_in, _, y1_in, y2_in, _, _ = inside
    keep_out, y1_out, y2_out, sources, edges = call(
        functools.partial(level0_outer_kernel, rows),
        [(6, 2, 8, Z, X), (2, 2, 4, Z, X), (2, 2, 6, Z, X), four, (3, 2, *edge)],
        work,
        main,
        *y_packets,
        *own_x,
        *corner_x,
        *inside,
    )
    own, first, second, edge_a, edge_b, gain = call(
        combine_kernel,
        [(2, OWN, Z, X), strip, strip, edge, edge, (POWERS + 3, Z, X)],
        [],
        sources,
        edges,
        spread,
    )
    coef1, keep0, iterate = call(
        functools.partial(coarse1_kernel, rows),
        [(3, 2, SIZE1, Z, X), (6, 2, total0, Z, X), (2, 2, rows, Z, X)],
        [(2, 2 * GROUPS1, Z, X)],
        coarse,
        *y_packets,
        *own_x,
        *corner_x,
        gain,
        keep_in,
        y1_in,
        y2_in,
        keep_out,
        y1_out,
        y2_out,
    )
    (fields2,) = call(
        functools.partial(fields2_kernel, rows), [(2, 3, Z, X)], [], coarse, *y_packets, *own_x, *corner_x
    )
    b_packets = exchange(first, second, "gy")

    one, two, up = (2, SIZE1, Z, X), (2, SIZE2, Z, X), (2, SIZE_UP, Z, X)
    near = (1 + EDGE_TILES, Z, X)
    packet, first, second, to_far, keep1 = call(
        level1_kernel,
        [(1, Z, X), near, near, (3, Z, X), (2, *one)],
        [one, one],
        own,
        *b_packets,
        edge_a,
        edge_b,
        fields2,
        coef1,
        gain,
    )
    far = (swap_far(to_far, "gy", 1), swap_far(to_far, "gy", -1))
    near = exchange(first, second, "gy")

    (out,) = call(
        rest_kernel,
        [(2 * Z * rows, X)],
        [(2, *two), one, two, two, two, two, up, up, pair0, pair0, pair0],
        packet,
        *near,
        *far,
        gain,
        coef1,
        fields2,
        keep0,
        iterate,
        keep1,
    )
    return out.reshape(2, Z, rows, X)


def solution(mesh):
    placed = (
        P(None, None, "gy", "gx"),
        P(None, None, "gy", "gx"),
        P(None, "gy", "gx"),
        P(None, "gy", "gx"),
    )
    return jax.shard_map(
        body, mesh=mesh, in_specs=placed, out_specs=P(None, None, "gy", "gx"), check_vma=False
    )
```

```python
import functools

import jax
import jax.numpy as jnp
from jax import lax
from jax.experimental import pallas as pl
from jax.experimental.pallas import tpu as pltpu
from jax.sharding import PartitionSpec as P

DIFF = (40.0, 20.0)
INV_STEP = 2.0
LOWER = 0.25

_CENTRE = (1.0 + LOWER) / 2.0
_HALF = (1.0 - LOWER) / 2.0
_SIGMA = _CENTRE / _HALF
_RHO0 = 1.0 / _SIGMA
_RHO1 = 1.0 / (2.0 * _SIGMA - _RHO0)
_RHO2 = 1.0 / (2.0 * _SIGMA - _RHO1)

Z = 8
X = 128
HALO0 = 4
SENT = 3
FIELDS1 = 6 * SENT
FIELDS2 = FIELDS1 + 8
PACKET = FIELDS2 + 1
WIDE = 42
PER = X // WIDE
EDGE = 3

LO1, HI1 = -4, 8
LO2, HI2 = -2, 3
LO_UP, HI_UP = -3, 7
SIZE1, SIZE2, SIZE_UP = HI1 - LO1 + 2, HI2 - LO2 + 2, HI_UP - LO_UP + 2
OWN = 4


def lane_of():
    return lax.broadcasted_iota(jnp.int32, (1, Z, X), 2)


def sub_of():
    return lax.broadcasted_iota(jnp.int32, (1, Z, X), 1)


def roll_x(tile, shift):
    shift = shift % X
    return pltpu.roll(tile, shift, 2) if shift else tile


def roll_z(tile, shift):
    shift = shift % Z
    return pltpu.roll(tile, shift, 1) if shift else tile


def rows_loop(lo, hi, body, step=None):
    step = step or hi - lo
    full = (hi - lo) // step
    if full == 1:
        body(lo, step)
    elif full > 1:

        def trip(i, carry):
            body(lo + i * step, step)
            return carry

        lax.fori_loop(0, full, trip, 0)
    rest = hi - lo - full * step
    if rest:
        body(hi - rest, rest)


def neighbour_sums(read, r, n, k, tiles=(0, 1)):
    lane = lane_of()
    low, high = lane < k, lane >= X - k
    centre = [read(t, r, n) for t in (0, 1)]
    right = [roll_x(c, k) for c in centre]
    left = [roll_x(c, -k) for c in centre]
    sums = []
    for t in tiles:
        c = centre[t]
        along_x = jnp.where(low, right[1 - t], right[t]) + jnp.where(high, left[1 - t], left[t])
        along_y = read(t, r - 1, n) + read(t, r + 1, n)
        along_z = 2.0 * roll_z(c, k) if 2 * k == Z else roll_z(c, k) + roll_z(c, -k)
        sums.append(along_x + along_y + along_z)
    return centre, sums


def jacobian(u, v, f, k, level):
    scale = 0.25**level
    product = u * v
    squared = v * v
    first = INV_STEP + squared + f + 6.0 * DIFF[0] * scale
    second = INV_STEP + f + k - 2.0 * product + 6.0 * DIFF[1] * scale
    return 2.0 * product, squared, 1.0 / first, 1.0 / second, first, second


def cheb_step(level, keep, source, target, d, r, n, carry, gain, tiles=(0, 1)):
    scale = 0.25**level
    k = 1 << level
    u, nb_u = neighbour_sums(lambda t, a, m: source[0, t, pl.ds(a, m)], r, n, k, tiles)
    v, nb_v = neighbour_sums(lambda t, a, m: source[1, t, pl.ds(a, m)], r, n, k, tiles)
    rows = pl.ds(r, n)
    out = []
    for t in tiles:
        cross, squared, inv_u, inv_v = (keep[i, t, rows] for i in range(4))
        res_u = inv_u * (keep[4, t, rows] - cross * v[t] + DIFF[0] * scale * nb_u[t]) - u[t]
        res_v = inv_v * (keep[5, t, rows] + squared * u[t] + DIFF[1] * scale * nb_v[t]) - v[t]
        du, dv = gain * res_u, gain * res_v
        if carry is not None:
            du = du + carry * d[0, t, rows]
            dv = dv + carry * d[1, t, rows]
        if target is not None:
            d[0, t, rows] = du
            d[1, t, rows] = dv
            target[0, t, rows] = u[t] + du
            target[1, t, rows] = v[t] + dv
        out.append((u[t] + du, v[t] + dv))
    return out


def next_power(keep, source, r, n):
    u, nb_u = neighbour_sums(lambda t, a, m: source[0, t, pl.ds(a, m)], r, n, 1)
    v, nb_v = neighbour_sums(lambda t, a, m: source[1, t, pl.ds(a, m)], r, n, 1)
    rows = pl.ds(r, n)
    first, second = [], []
    for t in (0, 1):
        cross, squared, inv_u, inv_v = (keep[i, t, rows] for i in range(4))
        first.append(u[t] + inv_u * (cross * v[t] - DIFF[0] * nb_u[t]))
        second.append(v[t] - inv_v * (squared * u[t] + DIFF[1] * nb_v[t]))
    return first, second


CARRY1 = _RHO1 * _RHO0
CARRY2 = _RHO2 * _RHO1


POWERS = 9


def write_gains(spread, out):
    lane = lax.broadcasted_iota(jnp.int32, (1, X), 1)
    for level in range(3):
        top = jnp.max(jnp.where(lane == level, spread, 0.0), axis=1, keepdims=True)
        tau = 1.0 / (1.0 + jnp.broadcast_to(top, (Z, X)))
        for i, factor in enumerate((1.0 / _CENTRE, 2.0 * _RHO1 / _HALF, 2.0 * _RHO2 / _HALF)):
            out[3 * level + i] = factor * tau
    g0, g1, g2 = (out[i] for i in range(3))
    first, second = g0 + CARRY1 * g0 + g1, g1 * g0
    out[POWERS] = first + CARRY2 * (CARRY1 * g0 + g1) + g2
    out[POWERS + 1] = second + CARRY2 * second + g2 * first
    out[POWERS + 2] = g2 * second


def pair_rows(value):
    n = value.shape[0] // 2
    pairs = value.reshape(n, 2, Z, X)
    return pairs[:, 0] + pairs[:, 1]


def restrict_01(first, second):
    lane, sub = lane_of(), sub_of()
    across = []
    for value in (first, second):
        a, b = value[0:1], value[1:2]
        across.append(jnp.where((lane & 1) == 0, a + roll_x(a, -1), b + roll_x(b, 1)))
    a, b = across
    return 0.125 * jnp.where((sub & 1) == 0, a + roll_z(a, -1), b + roll_z(b, 1))


def restrict_12(groups):
    lane, sub = lane_of(), sub_of()
    out = None
    for p, value in enumerate(groups):
        value = value + roll_x(value, 1 if p & 1 else -1)
        value = value + roll_x(value, 2 if p & 2 else -2)
        out = value if out is None else jnp.where((lane & 3) == p, value, out)
    return 0.125 * (out + jnp.where((sub & 2) == 0, roll_z(out, -2), roll_z(out, 2)))


def spread_x(tile, k, phase):
    return jnp.where((lane_of() & k) == phase, tile, roll_x(tile, -k if phase else k))


def packed_jacobian(uv, fk, level):
    scale = 0.25**level
    even = (sub_of() & 1) == 0
    u, v = jnp.where(even, uv, roll_z(uv, 1)), jnp.where(even, roll_z(uv, -1), uv)
    f, k = jnp.where(even, fk, roll_z(fk, 1)), jnp.where(even, roll_z(fk, -1), fk)
    product, squared = u * v, v * v
    diag = jnp.where(
        even,
        INV_STEP + squared + f + 6.0 * DIFF[0] * scale,
        INV_STEP + f + k - 2.0 * product + 6.0 * DIFF[1] * scale,
    )
    return 1.0 / diag, jnp.where(even, -2.0 * product, squared), diag


def packed_spread(uv, fk, level):
    scale = 0.25**level
    even = (sub_of() & 1) == 0
    inverse, other, _ = packed_jacobian(uv, fk, level)
    return jnp.where(even, 6.0 * DIFF[0] * scale - other, 6.0 * DIFF[1] * scale + other) * inverse


def packed_terms(source, g, n, level):
    k = 1 << level
    lane, sub = lane_of(), sub_of()
    even = (sub & 1) == 0
    first, last = (lane & (k - 1)) == 0, (lane & (k - 1)) == k - 1
    low, high = lane < k, lane >= X - k
    diff = jnp.where(even, DIFF[0] * 0.25**level, DIFF[1] * 0.25**level)
    wide = [source[t, pl.ds(g - 1, n + 2)] for t in (0, 1)]
    centre = [w[1 : n + 1] for w in wide]
    right = [roll_x(c, k) for c in centre]
    left = [roll_x(c, -k) for c in centre]
    out = []
    for t in (0, 1):
        c, w = centre[t], wide[t]
        total = jnp.where(low, right[1 - t], right[t]) + jnp.where(high, left[1 - t], left[t])
        if k == 2:
            ahead, back = roll_x(w, 1), roll_x(w, -1)
            total = total + jnp.where(first, back[0:n], ahead[1 : n + 1])
            total = total + jnp.where(last, ahead[2 : n + 2], back[1 : n + 1])
            total = total + roll_z(c, 2) + roll_z(c, -2)
        else:
            total = total + jnp.where(first, roll_x(w[0:n], -(k - 1)), roll_x(c, 1))
            total = total + jnp.where(last, roll_x(w[2 : n + 2], k - 1), roll_x(c, -1))
            total = total + 2.0 * roll_z(c, 4)
        other = jnp.where(even, roll_z(c, -1), roll_z(c, 1))
        out.append((c, other, diff * total))
    return out


def packed_first(coef, shift, b, target, d, g, n, gain):
    for t in (0, 1):
        value = gain * coef[0, t, pl.ds(g + shift, n)] * b[t, pl.ds(g + shift, n)]
        d[t, pl.ds(g, n)] = value
        target[t, pl.ds(g, n)] = value


def packed_step(level, coef, shift, b, source, target, d, g, n, carry, gain):
    for t, (c, other, spread) in enumerate(packed_terms(source, g, n, level)):
        at = pl.ds(g + shift, n)
        res = coef[0, t, at] * (b[t, at] + coef[1, t, at] * other + spread) - c
        delta = gain * res
        if carry is not None:
            delta = delta + carry * d[t, pl.ds(g, n)]
        d[t, pl.ds(g, n)] = delta
        target[t, pl.ds(g, n)] = c + delta


def plane(ref, f, y, rows):
    return ref[pl.ds(f * Z * rows + y, Z, stride=rows), :]


def is_even(axis):
    return lax.rem(lax.axis_index(axis), 2) == 0


def prev_of(even, first, second, at):
    return jnp.where(even, first[at], second[at])


def next_of(even, first, second, at):
    return jnp.where(even, second[at], first[at])


SOURCES = ((0, 0), (0, 1), (1, 0), (1, 1), (2, 0), (3, 0))


def first_kernel(rows, state, previous, feed, kill, first, second, coarse, *rest):
    held, sems = rest[:4], rest[4]
    copies = [
        pltpu.make_async_copy(ref, to, sems.at[i]) for i, (ref, to) in enumerate(zip((state, previous, feed, kill), held))
    ]
    for copy in copies:
        copy.start()
    for copy in copies:
        copy.wait()
    even = is_even("gy")
    values = []
    for i, (j, f) in enumerate(SOURCES):
        wanted = range(rows) if i not in (2, 3) else [*range(SENT), *range(rows - SENT, rows)]
        values.append({y: plane(held[j], f, y, rows)[None] for y in wanted})
    for i in (2, 3):
        weight = DIFF[i - 2] / INV_STEP
        values[i][SENT - 1] = values[i][SENT - 1] + weight * values[i - 2][SENT]
        values[i][rows - SENT] = values[i][rows - SENT] + weight * values[i - 2][rows - SENT - 1]
    for i in range(6):
        for y in range(SENT):
            top, bottom = values[i][y], values[i][rows - SENT + y]
            at = slice(i * SENT + y, i * SENT + y + 1)
            first[at] = jnp.where(even, top, bottom)
            second[at] = jnp.where(even, bottom, top)
    pairs = []
    for p, (i, j) in enumerate(((0, 1), (4, 5))):
        parts = []
        for g in range(OWN):
            sums = [
                jnp.concatenate([value[4 * g + 2 * q] + value[4 * g + 2 * q + 1] for q in (0, 1)], axis=0)
                for value in (values[i], values[j])
            ]
            parts.append(restrict_01(*sums))
        pairs.append(jnp.concatenate(parts, axis=0))
        coarse[p * OWN : (p + 1) * OWN] = pairs[p]
        for ref in (first, second):
            ref[FIELDS1 + p * OWN : FIELDS1 + (p + 1) * OWN] = pairs[p]
    uv, fk = (restrict_12([pair[j : j + 1] for j in range(OWN)]) for pair in pairs)
    both = jnp.where((sub_of() & 2) == 0, uv, fk)
    coarse[2 * OWN : 2 * OWN + 1] = both
    for ref in (first, second):
        ref[FIELDS2 : FIELDS2 + 1] = both


def split_fields2(both):
    low = (sub_of() & 2) == 0
    return jnp.where(low, both, roll_z(both, 2)), jnp.where(low, roll_z(both, -2), both)


def write_spread(main, coarse, out):
    lane = lax.broadcasted_iota(jnp.int32, (1, X), 1)
    u, v, f, k = (main[i] for i in (0, 1, 4, 5))
    cross, squared, inv_u, inv_v, _, _ = jacobian(u, v, f, k, 0)
    tops = [jnp.max(jnp.maximum((6.0 * DIFF[0] + cross) * inv_u, (6.0 * DIFF[1] + squared) * inv_v), axis=0)]
    tops.append(jnp.max(packed_spread(coarse[0:OWN], coarse[OWN : 2 * OWN], 1), axis=0))
    tops.append(packed_spread(*split_fields2(coarse[2 * OWN : 2 * OWN + 1]), 2)[0])
    result = jnp.zeros((1, X), jnp.float32)
    for level, top in enumerate(tops):
        top = jnp.max(jnp.max(top, axis=0, keepdims=True), axis=1, keepdims=True)
        result = jnp.where(lane == level, jnp.broadcast_to(top, (1, X)), result)
    out[...] = jnp.broadcast_to(result[None], out.shape)


GROUPS1 = HI1 - LO1
GROUPS2 = HI2 - LO2


def tiles_for(entries):
    return -(-entries // PER)


def pack_edges(entries, even, first, second):
    lane = lane_of()
    share = first.shape[0]
    left, right = None, None
    for j in range(PER):
        part = entries[j * share : (j + 1) * share]
        a, b = roll_x(part, WIDE * j), roll_x(part, WIDE + WIDE * j)
        left = a if left is None else jnp.where(lane >= WIDE * j, a, left)
        right = b if right is None else jnp.where(lane >= WIDE * j, b, right)
    first[...] = jnp.where(even, left, right)
    second[...] = jnp.where(even, right, left)


def halo_tiles(even, packets, lo, hi):
    first, second = packets
    share = first.shape[0]
    lane = lane_of()
    out = []
    for j in range(PER):
        a, b = max(lo, j * share), min(hi, (j + 1) * share)
        if a < b:
            strip = slice(a - j * share, b - j * share)
            left, right = prev_of(even, first, second, strip), next_of(even, first, second, strip)
            value = jnp.where(lane < X // 2, roll_x(right, -WIDE * j), roll_x(left, X - WIDE - WIDE * j))
            out.append((a - lo, b - lo, value))
    return out


def pack_own_kernel(
    rows, state, previous, feed, kill, coarse, first, second, spread, main, held, copies, sem
):
    inputs = (state, previous, feed, kill)
    for i, (j, f) in enumerate(SOURCES):
        for y in range(rows):
            main[i, y] = plane(inputs[j], f, y, rows)
    write_spread(main, coarse, copies)
    copy = pltpu.make_async_copy(copies, spread, sem)
    copy.start()
    for i in range(6):
        held[i * rows : (i + 1) * rows] = main[i]
    held[6 * rows : 6 * rows + 2 * OWN + 1] = coarse[...]
    pack_edges(held, is_even("gx"), first, second)
    copy.wait()


def pack_corner_kernel(y_first, y_second, first, second, held):
    even = is_even("gy")
    every = slice(0, PACKET)
    held[0:PACKET] = prev_of(even, y_first, y_second, every)
    held[PACKET : 2 * PACKET] = next_of(even, y_first, y_second, every)
    pack_edges(held, is_even("gx"), first, second)


EDGE_TILES = 2 * EDGE + 1


def level0_setup(fields, keep, diag, power, r, n):
    at = pl.ds(r, n)
    u, nb_u = neighbour_sums(lambda t, a, m: fields[0, t, pl.ds(a, m)], r, n, 1)
    v, nb_v = neighbour_sums(lambda t, a, m: fields[1, t, pl.ds(a, m)], r, n, 1)
    for t in (0, 1):
        f, k = fields[4, t, at], fields[5, t, at]
        cross, squared, inv_u, inv_v, first, second = jacobian(u[t], v[t], f, k, 0)
        react = u[t] * squared
        b_u = DIFF[0] * (nb_u[t] - 6.0 * u[t]) - INV_STEP * (u[t] - fields[2, t, at]) - react + f * (1.0 - u[t])
        b_v = DIFF[1] * (nb_v[t] - 6.0 * v[t]) - INV_STEP * (v[t] - fields[3, t, at]) + react - (f + k) * v[t]
        for i, value in enumerate((cross, squared, inv_u, inv_v, b_u, b_v)):
            keep[i, t, at] = value
        for i, value in enumerate((first, second)):
            diag[i, t, at] = value
        for i, value in enumerate((inv_u * b_u, inv_v * b_v)):
            power[i, t, at] = value


def level0_power(keep, source, target, r, n):
    for i, values in enumerate(next_power(keep, source, r, n)):
        for t in (0, 1):
            target[i, t, pl.ds(r, n)] = values[t]


def level0_down(keep, diag, y1, y2, sources, r, n):
    at = pl.ds(r, n)
    last = next_power(keep, y2, r, n)
    for t in (0, 1):
        both = [diag[i, t, at] for i in (0, 1)]
        parts = [[keep[4 + i, t, at] for i in (0, 1)]]
        parts += [[both[i] * power[i, t, at] for i in (0, 1)] for power in (y1, y2)]
        parts.append([both[i] * last[i][t] for i in (0, 1)])
        for q, part in enumerate(parts):
            u, v = (pair_rows(value) for value in part)
            for j in range(n // 4):
                value = restrict_01(u[2 * j : 2 * j + 2], v[2 * j : 2 * j + 2])
                sources[q, t, pl.ds((r - HALO0) // 4 + j, 1)] = value


def inner(rows, lost):
    return slice(HALO0 + lost, HALO0 + rows - lost)


def ends(rows, lo, hi):
    total = rows + 2 * HALO0
    return slice(lo, hi), slice(total - hi, total - lo)


def put_ends(target, rows, lo, hi, source):
    n = hi - lo
    for at, part in zip(ends(rows, lo, hi), (slice(0, n), slice(n, 2 * n))):
        for i in range(target.shape[0]):
            for t in (0, 1):
                target[i, t, at] = source[i, t, part]


def take_ends(source, rows, lo, hi, target):
    n = hi - lo
    for at, part in zip(ends(rows, lo, hi), (slice(0, n), slice(n, 2 * n))):
        for i in range(source.shape[0]):
            for t in (0, 1):
                target[i, t, part] = source[i, t, at]


def level0_inner_kernel(rows, main, own_a, own_b, keep_in, y0_in, y1_in, y2_in, diag_in, sources_in, *scratch):
    fields, keep, diag, y0, y1, y2 = scratch
    even_x = is_even("gx")
    for i in range(6):
        fields[i, 0, HALO0 : HALO0 + rows] = main[i]
        for a, b, value in halo_tiles(even_x, (own_a, own_b), i * rows, (i + 1) * rows):
            fields[i, 1, HALO0 + a : HALO0 + b] = value
    first = HALO0 + 1
    level0_setup(fields, keep, diag, y0, first, rows - 2)
    level0_power(keep, y0, y1, first + 1, rows - 4)
    level0_power(keep, y1, y2, first + 2, rows - 6)
    level0_down(keep, diag, y1, y2, sources_in, first + 3, rows - 8)
    for source, target, lost in ((keep, keep_in, 1), (y1, y1_in, 2), (y2, y2_in, 3)):
        for i in range(source.shape[0]):
            for t in (0, 1):
                target[i, t] = source[i, t, inner(rows, lost)]
    take_ends(y0, rows, HALO0 + 1, HALO0 + 3, y0_in)
    take_ends(diag, rows, HALO0 + 1, HALO0 + 4, diag_in)


def level0_outer_kernel(
    rows,
    main,
    y_first,
    y_second,
    own_a,
    own_b,
    corner_a,
    corner_b,
    keep_in,
    y0_in,
    y1_in,
    y2_in,
    diag_in,
    sources_in,
    keep_out,
    y1_out,
    y2_out,
    sources,
    edges,
    *scratch,
):
    fields, keep, diag, y0, y1, y2 = scratch
    even, even_x = is_even("gy"), is_even("gx")
    total = rows + 2 * HALO0
    near, skip = HALO0 + 2, HALO0 - SENT
    for i in range(6):
        strip = slice(i * SENT, (i + 1) * SENT)
        fields[i, 0, skip:HALO0] = prev_of(even, y_first, y_second, strip)
        fields[i, 0, HALO0:near] = main[i, 0:2]
        fields[i, 0, total - near : total - HALO0] = main[i, rows - 2 : rows]
        fields[i, 0, HALO0 + rows : total - skip] = next_of(even, y_first, y_second, strip)
        for packets, lo, n, at in (
            ((corner_a, corner_b), i * SENT, SENT, skip),
            ((own_a, own_b), i * rows, 2, HALO0),
            ((own_a, own_b), (i + 1) * rows - 2, 2, total - near),
            ((corner_a, corner_b), PACKET + i * SENT, SENT, HALO0 + rows),
        ):
            for a, b, value in halo_tiles(even_x, packets, lo, lo + n):
                fields[i, 1, at + a : at + b] = value
    for i in (0, 1):
        for t in (0, 1):
            for at in (0, total - 1):
                fields[i, t, at] = jnp.zeros((Z, X), jnp.float32)
    for at, part in zip(ends(rows, 5, 8), (slice(0, 3), slice(rows - 5, rows - 2))):
        for i in range(6):
            for t in (0, 1):
                keep[i, t, at] = keep_in[i, t, part]
    put_ends(diag, rows, 5, 8, diag_in)
    put_ends(y0, rows, 5, 7, y0_in)
    for target, source, lost in ((y1, y1_in, 2), (y2, y2_in, 3)):
        n = rows - 2 * lost
        for at, part in zip(ends(rows, HALO0 + lost, HALO0 + lost + 2), (slice(0, 2), slice(n - 2, n))):
            for i in (0, 1):
                for t in (0, 1):
                    target[i, t, at] = source[i, t, part]
    for r in (1, total - 5):
        level0_setup(fields, keep, diag, y0, r, 4)
    for r in (2, total - 6):
        level0_power(keep, y0, y1, r, 4)
    for r in (3, total - 7):
        level0_power(keep, y1, y2, r, 4)
    for r in (4, total - 8):
        level0_down(keep, diag, y1, y2, sources, r, 4)
    for q in range(4):
        for t in (0, 1):
            sources[q, t, 1 : OWN - 1] = sources_in[q, t, 1 : OWN - 1]
    take_ends(keep, rows, 1, 5, keep_out)
    take_ends(y1, rows, 4, 6, y1_out)
    take_ends(y2, rows, 4, 7, y2_out)
    for p, power in enumerate((y0, y1, y2)):
        for side, start in enumerate((HALO0, HALO0 + rows - EDGE)):
            edges[p, side] = pack_rows(power, start)


def pack_rows(x, start):
    lane = lane_of()
    halo = None
    for i in (0, 1):
        for j in range(EDGE):
            at = i * EDGE + j
            value = roll_x(x[i, 1, start + j : start + j + 1], 4 + 8 * at)
            halo = value if halo is None else jnp.where((lane >> 3) == at, value, halo)
    return jnp.concatenate([x[i, 0, start : start + EDGE] for i in (0, 1)] + [halo], axis=0)


def combine_kernel(sources, edges, spread, own, first, second, edge_first, edge_second, gain):
    write_gains(jnp.max(spread[...], axis=0)[0:1], gain)
    p0, p1, p2 = (gain[POWERS + i] for i in range(3))
    for t in (0, 1):
        value = sources[0, t] - p0 * sources[1, t] + p1 * sources[2, t] - p2 * sources[3, t]
        own[t] = value
        for ref in (first, second):
            ref[t * OWN : (t + 1) * OWN] = value
    even = is_even("gy")
    top, bottom = (p0 * edges[0, side] - p1 * edges[1, side] + p2 * edges[2, side] for side in (0, 1))
    edge_first[...] = jnp.where(even, top, bottom)
    edge_second[...] = jnp.where(even, bottom, top)


def coarse1_kernel(
    rows, coarse, y_first, y_second, own_a, own_b, corner_a, corner_b, gain, keep_in, y1_in, y2_in, keep_out, y1_out, y2_out,
    coef, keep0, x0, fields
):
    even, even_x = is_even("gy"), is_even("gx")
    own_x, corner_x = (own_a, own_b), (corner_a, corner_b)
    for p in (0, 1):
        to = p * GROUPS1
        strip = slice(FIELDS1 + p * OWN, FIELDS1 + (p + 1) * OWN)
        fields[0, to : to + OWN] = prev_of(even, y_first, y_second, strip)
        fields[0, to + OWN : to + 2 * OWN] = coarse[p * OWN : (p + 1) * OWN]
        fields[0, to + 2 * OWN : to + 3 * OWN] = next_of(even, y_first, y_second, strip)
        for part, (packets, lo) in enumerate(
            ((corner_x, FIELDS1), (own_x, 6 * rows), (corner_x, PACKET + FIELDS1))
        ):
            lo += p * OWN
            for a, b, value in halo_tiles(even_x, packets, lo, lo + OWN):
                fields[1, to + part * OWN + a : to + part * OWN + b] = value
    for t in (0, 1):
        for i, value in enumerate(packed_jacobian(fields[t, 0:GROUPS1], fields[t, GROUPS1 : 2 * GROUPS1], 1)):
            coef[i, t, 1 : SIZE1 - 1] = value

    def whole(inside, outside):
        n = outside.shape[0] // 2
        return jnp.concatenate([outside[0:n], inside, outside[n:]], axis=0)

    for i in range(6):
        for t in (0, 1):
            keep0[i, t, 1 : rows + 2 * HALO0 - 1] = whole(keep_in[i, t], keep_out[i, t])
    p0, p1, p2 = (gain[POWERS + i] for i in range(3))
    for i in (0, 1):
        for t in (0, 1):
            y0 = keep0[2 + i, t, HALO0 : HALO0 + rows] * keep0[4 + i, t, HALO0 : HALO0 + rows]
            y1, y2 = (whole(a[i, t], b[i, t]) for a, b in ((y1_in, y1_out), (y2_in, y2_out)))
            x0[i, t] = p0 * y0 - p1 * y1 + p2 * y2


def fields2_kernel(rows, coarse, y_first, y_second, own_a, own_b, corner_a, corner_b, out):
    even, even_x = is_even("gy"), is_even("gx")
    own_x, corner_x = (own_a, own_b), (corner_a, corner_b)
    near = slice(FIELDS2, FIELDS2 + 1)
    out[0, 0:1] = prev_of(even, y_first, y_second, near)
    out[0, 1:2] = coarse[2 * OWN : 2 * OWN + 1]
    out[0, 2:3] = next_of(even, y_first, y_second, near)
    for q, (packets, lo) in enumerate(
        ((corner_x, FIELDS2), (own_x, 6 * rows + 2 * OWN), (corner_x, PACKET + FIELDS2))
    ):
        out[1, q : q + 1] = halo_tiles(even_x, packets, lo, lo + 1)[0][2]


def level1_kernel(
    own, first, second, edge_a, edge_b, fields2, coef1, gain, packet, to_first, to_second, to_far, keep, y1, d1
):
    b1, x1 = keep.at[0], keep.at[1]
    even = is_even("gy")
    for t in (0, 1):
        b1[t, 1 + OWN : 1 + 2 * OWN] = own[t]
        strip = slice(t * OWN, (t + 1) * OWN)
        b1[t, 1 : 1 + OWN] = prev_of(even, first, second, strip)
        b1[t, 1 + 2 * OWN : 1 + 3 * OWN] = next_of(even, first, second, strip)
    g0, g1, g2 = (gain[3 + i] for i in range(3))
    n = GROUPS1
    packed_first(coef1, 0, b1, x1, d1, 1, n, g0)
    packed_step(1, coef1, 0, b1, x1, y1, d1, 1, n, CARRY1, g1)
    packed_step(1, coef1, 0, b1, y1, x1, d1, 1, n, CARRY2, g2)
    here = pl.ds(1 + OWN, OWN)
    values = []
    for t, (c, other, spread) in enumerate(packed_terms(x1, 1 + OWN, OWN, 1)):
        res = b1[t, here] - coef1[2, t, here] * c + coef1[1, t, here] * other + spread
        values.append(restrict_12([res[j : j + 1] for j in range(OWN)]))
        to_far[1 + t : 2 + t] = fields2[t, 1:2]
    value = jnp.where((sub_of() & 2) == 0, values[0], values[1])
    for ref in (packet, to_first, to_second, to_far):
        ref[0:1] = value
    to_first[1:] = edge_a[...]
    to_second[1:] = edge_b[...]


def rest_kernel(
    own2, near_a, near_b, far_a, far_b, gain, coef1, fields2, keep0, iterate, keep1, out, coef2, d1, b2, x2, y2, d2, xu, yu, x0, y0, d0
):
    rows = out.shape[0] // (2 * Z)
    even = (sub_of() & 1) == 0
    b1, x1 = keep1.at[0], keep1.at[1]

    even_y, low = is_even("gy"), lax.rem(lax.axis_index("gy"), 4) < 2
    at = slice(0, 1)
    parts = [
        next_of(low, far_a, far_b, at),
        prev_of(even_y, near_a, near_b, at),
        own2[at],
        next_of(even_y, near_a, near_b, at),
        prev_of(low, far_a, far_b, at),
    ]
    for t, values in enumerate(split_fields2(jnp.concatenate(parts, axis=0))):
        b2[t, 1 : SIZE2 - 1] = values
        at = slice(1 + t, 2 + t)
        parts = [next_of(low, far_a, far_b, at), fields2[t], prev_of(low, far_a, far_b, at)]
        inverse, other, _ = packed_jacobian(*split_fields2(jnp.concatenate(parts, axis=0)), 2)
        coef2[0, t, 1 : SIZE2 - 1] = inverse
        coef2[1, t, 1 : SIZE2 - 1] = other

    n = HI2 - LO2
    g0, g1, g2 = (gain[6 + i] for i in range(3))
    packed_first(coef2, 0, b2, x2, d2, 1, n, g0)
    packed_step(2, coef2, 0, b2, x2, y2, d2, 1, n, CARRY1, g1)
    packed_step(2, coef2, 0, b2, y2, x2, d2, 1, n, CARRY2, g2)
    packed_step(2, coef2, 0, b2, x2, y2, d2, 1, n, None, g0)
    packed_step(2, coef2, 0, b2, y2, x2, d2, 1, n, CARRY1, g1)
    packed_step(2, coef2, 0, b2, x2, y2, d2, 1, n, CARRY2, g2)

    g0, g1, g2 = (gain[3 + i] for i in range(3))
    shift = LO_UP - LO1
    for t in (0, 1):
        for g in range(LO_UP, HI_UP):
            p = g % 4
            value = y2[t, g // 4 - LO2 + 1 : g // 4 - LO2 + 2]
            value = spread_x(spread_x(value, 1, p & 1), 2, p & 2)
            at = g - LO_UP + 1
            xu[t, at : at + 1] = x1[t, at + shift : at + shift + 1] + value
    n = HI_UP - LO_UP
    packed_step(1, coef1, shift, b1, xu, yu, d1, 1, n, None, g0)
    packed_step(1, coef1, shift, b1, yu, xu, d1, 1, n, CARRY1, g1)
    packed_step(1, coef1, shift, b1, xu, yu, d1, 1, n, CARRY2, g2)

    g0, g1, g2 = (gain[i] for i in range(3))
    for i in (0, 1):
        for at, take in ((HALO0 - EDGE, prev_of), (HALO0 + rows, next_of)):
            whole = take(even_y, near_a, near_b, slice(1, 1 + EDGE_TILES))
            x0[i, 0, at : at + EDGE] = whole[i * EDGE : (i + 1) * EDGE]
            for j in range(EDGE):
                x0[i, 1, at + j : at + j + 1] = roll_x(whole[2 * EDGE :], -(4 + 8 * (i * EDGE + j)))
        for t in (0, 1):
            x0[i, t, HALO0 : HALO0 + rows] = iterate[i, t]
    for t in (0, 1):
        for row in range(-2, rows // 2 + 2):
            at = row // 2 - LO_UP + 1
            value = spread_x(yu[t, at : at + 1], 1, row & 1)
            for i, fine in enumerate((jnp.where(even, value, roll_z(value, 1)), jnp.where(even, roll_z(value, -1), value))):
                for y in (2 * row, 2 * row + 1):
                    if -EDGE <= y < rows + EDGE:
                        x0[i, t, y + HALO0 : y + HALO0 + 1] = x0[i, t, y + HALO0 : y + HALO0 + 1] + fine
    total = rows + 2 * HALO0
    rows_loop(2, total - 2, lambda r, n: cheb_step(0, keep0, x0, y0, d0, r, n, None, g0))
    rows_loop(3, total - 3, lambda r, n: cheb_step(0, keep0, y0, x0, d0, r, n, CARRY1, g1))
    last = cheb_step(0, keep0, x0, None, d0, HALO0, rows, CARRY2, g2, (0,))[0]
    for i in (0, 1):
        for y in range(rows):
            out[pl.ds(i * Z * rows + y, Z, stride=rows), :] = last[i][y]


def call(kernel, out_shapes, scratch, *args, space=pltpu.VMEM, outs=None):
    out = [jax.ShapeDtypeStruct(shape, jnp.float32) for shape in out_shapes]
    return pl.pallas_call(
        kernel,
        out_shape=out,
        in_specs=[pl.BlockSpec(memory_space=space)] * len(args),
        out_specs=[pl.BlockSpec(memory_space=m) for m in outs or [pltpu.VMEM] * len(out)],
        scratch_shapes=[pltpu.VMEM(s, jnp.float32) if isinstance(s, tuple) else s for s in scratch],
        compiler_params=pltpu.CompilerParams(vmem_limit_bytes=24 * 2**20),
    )(*args)


def swap(value, axis, step):
    count = lax.axis_size(axis)
    assert count % 2 == 0
    pairs = [(i, (i + step) % count) for i in range(0, count, 2)]
    return lax.ppermute(value, axis, pairs + [(j, i) for i, j in pairs])


def swap_far(value, axis, step):
    count = lax.axis_size(axis)
    assert count % 4 == 0
    pairs = [(i + j, (i + j + 2 * step) % count) for i in range(0, count, 4) for j in (0, 1)]
    return lax.ppermute(value, axis, pairs + [(j, i) for i, j in pairs])


def exchange(first, second, axis):
    return swap(first, axis, -1), swap(second, axis, 1)


def body(state, previous, feed, kill):
    _, depth, rows, cols = state.shape
    assert depth == Z and cols == X and rows == 4 * OWN
    across, count = lax.axis_size("gx"), lax.axis_size("gy")
    total0 = rows + 2 * HALO0
    state = state.reshape(2 * Z * rows, X)
    previous = previous.reshape(2 * Z * rows, X)
    feed = feed.reshape(Z * rows, X)
    kill = kill.reshape(Z * rows, X)
    inputs = (state, previous, feed, kill)

    strip = (PACKET, Z, X)
    first, second, coarse, *inputs = call(
        functools.partial(first_kernel, rows),
        [strip, strip, (2 * OWN + 1, Z, X), *(a.shape for a in inputs)],
        [pltpu.SemaphoreType.DMA((4,))],
        *(pltpu.with_memory_space_constraint(a, pltpu.HBM) for a in inputs),
        space=pltpu.HBM,
    )
    y_packets = exchange(first, second, "gy")

    tiles = tiles_for(6 * rows + 2 * OWN + 1)
    spread_shape = (across * count, Z // 2, X)
    first, second, spread, main = call(
        functools.partial(pack_own_kernel, rows),
        [(tiles, Z, X), (tiles, Z, X), spread_shape, (6, rows, Z, X)],
        [(PER * tiles, Z, X), spread_shape, pltpu.SemaphoreType.DMA],
        *inputs,
        coarse,
        outs=[pltpu.VMEM, pltpu.VMEM, pltpu.HBM, pltpu.VMEM],
    )
    own_x = exchange(first, second, "gx")
    ranks = [(i + across // 2 * count + count // 2) % (across * count) for i in range(across * count)]
    spread = lax.all_to_all(spread, ("gx", "gy"), 0, 0, axis_index_groups=[ranks], tiled=True)
    tiles = tiles_for(2 * PACKET)
    corner_x = exchange(
        *call(pack_corner_kernel, [(tiles, Z, X), (tiles, Z, X)], [(PER * tiles, Z, X)], *y_packets), "gx"
    )

    strip, edge = (2 * OWN, Z, X), (EDGE_TILES, Z, X)
    pair0 = (2, 2, total0, Z, X)
    work = [(6, 2, total0, Z, X), (6, 2, total0, Z, X), pair0, pair0, pair0, pair0]
    four = (4, 2, OWN, Z, X)
    inside = call(
        functools.partial(level0_inner_kernel, rows),
        [
            (6, 2, rows - 2, Z, X),
            (2, 2, 4, Z, X),
            (2, 2, rows - 4, Z, X),
            (2, 2, rows - 6, Z, X),
            (2, 2, 6, Z, X),
            four,
        ],
        work,
        main,
        *own_x,
    )
    keep_in, _, y1_in, y2_in, _, _ = inside
    keep_out, y1_out, y2_out, sources, edges = call(
        functools.partial(level0_outer_kernel, rows),
        [(6, 2, 8, Z, X), (2, 2, 4, Z, X), (2, 2, 6, Z, X), four, (3, 2, *edge)],
        work,
        main,
        *y_packets,
        *own_x,
        *corner_x,
        *inside,
    )
    own, first, second, edge_a, edge_b, gain = call(
        combine_kernel,
        [(2, OWN, Z, X), strip, strip, edge, edge, (POWERS + 3, Z, X)],
        [],
        sources,
        edges,
        spread,
    )
    coef1, keep0, iterate = call(
        functools.partial(coarse1_kernel, rows),
        [(3, 2, SIZE1, Z, X), (6, 2, total0, Z, X), (2, 2, rows, Z, X)],
        [(2, 2 * GROUPS1, Z, X)],
        coarse,
        *y_packets,
        *own_x,
        *corner_x,
        gain,
        keep_in,
        y1_in,
        y2_in,
        keep_out,
        y1_out,
        y2_out,
    )
    (fields2,) = call(
        functools.partial(fields2_kernel, rows), [(2, 3, Z, X)], [], coarse, *y_packets, *own_x, *corner_x
    )
    b_packets = exchange(first, second, "gy")

    one, two, up = (2, SIZE1, Z, X), (2, SIZE2, Z, X), (2, SIZE_UP, Z, X)
    near = (1 + EDGE_TILES, Z, X)
    packet, first, second, to_far, keep1 = call(
        level1_kernel,
        [(1, Z, X), near, near, (3, Z, X), (2, *one)],
        [one, one],
        own,
        *b_packets,
        edge_a,
        edge_b,
        fields2,
        coef1,
        gain,
    )
    far = (swap_far(to_far, "gy", 1), swap_far(to_far, "gy", -1))
    near = exchange(first, second, "gy")

    (out,) = call(
        rest_kernel,
        [(2 * Z * rows, X)],
        [(2, *two), one, two, two, two, two, up, up, pair0, pair0, pair0],
        packet,
        *near,
        *far,
        gain,
        coef1,
        fields2,
        keep0,
        iterate,
        keep1,
    )
    return out.reshape(2, Z, rows, X)


def solution(mesh):
    placed = (
        P(None, None, "gy", "gx"),
        P(None, None, "gy", "gx"),
        P(None, "gy", "gx"),
        P(None, "gy", "gx"),
    )
    return jax.shard_map(
        body, mesh=mesh, in_specs=placed, out_specs=P(None, None, "gy", "gx"), check_vma=False
    )
```

```python
import functools

import jax
import jax.numpy as jnp
from jax import lax
from jax.experimental import pallas as pl
from jax.experimental.pallas import tpu as pltpu
from jax.sharding import PartitionSpec as P

DIFF = (40.0, 20.0)
INV_STEP = 2.0
LOWER = 0.25

_CENTRE = (1.0 + LOWER) / 2.0
_HALF = (1.0 - LOWER) / 2.0
_SIGMA = _CENTRE / _HALF
_RHO0 = 1.0 / _SIGMA
_RHO1 = 1.0 / (2.0 * _SIGMA - _RHO0)
_RHO2 = 1.0 / (2.0 * _SIGMA - _RHO1)

Z = 8
X = 128
HALO0 = 4
SENT = 3
FIELDS1 = 6 * SENT
FIELDS2 = FIELDS1 + 8
PACKET = FIELDS2 + 1
WIDE = 42
PER = X // WIDE
EDGE = 3

LO1, HI1 = -4, 8
LO2, HI2 = -2, 3
LO_UP, HI_UP = -3, 7
SIZE1, SIZE2, SIZE_UP = HI1 - LO1 + 2, HI2 - LO2 + 2, HI_UP - LO_UP + 2
OWN = 4


def lane_of():
    return lax.broadcasted_iota(jnp.int32, (1, Z, X), 2)


def sub_of():
    return lax.broadcasted_iota(jnp.int32, (1, Z, X), 1)


def roll_x(tile, shift):
    shift = shift % X
    return pltpu.roll(tile, shift, 2) if shift else tile


def roll_z(tile, shift):
    shift = shift % Z
    return pltpu.roll(tile, shift, 1) if shift else tile


def rows_loop(lo, hi, body, step=None):
    step = step or hi - lo
    full = (hi - lo) // step
    if full == 1:
        body(lo, step)
    elif full > 1:

        def trip(i, carry):
            body(lo + i * step, step)
            return carry

        lax.fori_loop(0, full, trip, 0)
    rest = hi - lo - full * step
    if rest:
        body(hi - rest, rest)


def neighbour_sums(read, r, n, k, tiles=(0, 1)):
    lane = lane_of()
    low, high = lane < k, lane >= X - k
    centre = [read(t, r, n) for t in (0, 1)]
    right = [roll_x(c, k) for c in centre]
    left = [roll_x(c, -k) for c in centre]
    sums = []
    for t in tiles:
        c = centre[t]
        along_x = jnp.where(low, right[1 - t], right[t]) + jnp.where(high, left[1 - t], left[t])
        along_y = read(t, r - 1, n) + read(t, r + 1, n)
        along_z = 2.0 * roll_z(c, k) if 2 * k == Z else roll_z(c, k) + roll_z(c, -k)
        sums.append(along_x + along_y + along_z)
    return centre, sums


def jacobian(u, v, f, k, level):
    scale = 0.25**level
    product = u * v
    squared = v * v
    first = INV_STEP + squared + f + 6.0 * DIFF[0] * scale
    second = INV_STEP + f + k - 2.0 * product + 6.0 * DIFF[1] * scale
    return 2.0 * product, squared, 1.0 / first, 1.0 / second, first, second


def cheb_step(level, keep, source, target, d, r, n, carry, gain, tiles=(0, 1)):
    scale = 0.25**level
    k = 1 << level
    u, nb_u = neighbour_sums(lambda t, a, m: source[0, t, pl.ds(a, m)], r, n, k, tiles)
    v, nb_v = neighbour_sums(lambda t, a, m: source[1, t, pl.ds(a, m)], r, n, k, tiles)
    rows = pl.ds(r, n)
    out = []
    for t in tiles:
        cross, squared, inv_u, inv_v = (keep[i, t, rows] for i in range(4))
        res_u = inv_u * (keep[4, t, rows] - cross * v[t] + DIFF[0] * scale * nb_u[t]) - u[t]
        res_v = inv_v * (keep[5, t, rows] + squared * u[t] + DIFF[1] * scale * nb_v[t]) - v[t]
        du, dv = gain * res_u, gain * res_v
        if carry is not None:
            du = du + carry * d[0, t, rows]
            dv = dv + carry * d[1, t, rows]
        if target is not None:
            d[0, t, rows] = du
            d[1, t, rows] = dv
            target[0, t, rows] = u[t] + du
            target[1, t, rows] = v[t] + dv
        out.append((u[t] + du, v[t] + dv))
    return out


def next_power(keep, source, r, n):
    u, nb_u = neighbour_sums(lambda t, a, m: source[0, t, pl.ds(a, m)], r, n, 1)
    v, nb_v = neighbour_sums(lambda t, a, m: source[1, t, pl.ds(a, m)], r, n, 1)
    rows = pl.ds(r, n)
    first, second = [], []
    for t in (0, 1):
        cross, squared, inv_u, inv_v = (keep[i, t, rows] for i in range(4))
        first.append(u[t] + inv_u * (cross * v[t] - DIFF[0] * nb_u[t]))
        second.append(v[t] - inv_v * (squared * u[t] + DIFF[1] * nb_v[t]))
    return first, second


CARRY1 = _RHO1 * _RHO0
CARRY2 = _RHO2 * _RHO1


POWERS = 9


def write_gains(spread, out):
    lane = lax.broadcasted_iota(jnp.int32, (1, X), 1)
    for level in range(3):
        top = jnp.max(jnp.where(lane == level, spread, 0.0), axis=1, keepdims=True)
        tau = 1.0 / (1.0 + jnp.broadcast_to(top, (Z, X)))
        for i, factor in enumerate((1.0 / _CENTRE, 2.0 * _RHO1 / _HALF, 2.0 * _RHO2 / _HALF)):
            out[3 * level + i] = factor * tau
    g0, g1, g2 = (out[i] for i in range(3))
    first, second = g0 + CARRY1 * g0 + g1, g1 * g0
    out[POWERS] = first + CARRY2 * (CARRY1 * g0 + g1) + g2
    out[POWERS + 1] = second + CARRY2 * second + g2 * first
    out[POWERS + 2] = g2 * second


def pair_rows(value):
    n = value.shape[0] // 2
    pairs = value.reshape(n, 2, Z, X)
    return pairs[:, 0] + pairs[:, 1]


def restrict_01(first, second):
    lane, sub = lane_of(), sub_of()
    across = []
    for value in (first, second):
        a, b = value[0:1], value[1:2]
        across.append(jnp.where((lane & 1) == 0, a + roll_x(a, -1), b + roll_x(b, 1)))
    a, b = across
    return 0.125 * jnp.where((sub & 1) == 0, a + roll_z(a, -1), b + roll_z(b, 1))


def restrict_12(groups):
    lane, sub = lane_of(), sub_of()
    out = None
    for p, value in enumerate(groups):
        value = value + roll_x(value, 1 if p & 1 else -1)
        value = value + roll_x(value, 2 if p & 2 else -2)
        out = value if out is None else jnp.where((lane & 3) == p, value, out)
    return 0.125 * (out + jnp.where((sub & 2) == 0, roll_z(out, -2), roll_z(out, 2)))


def spread_x(tile, k, phase):
    return jnp.where((lane_of() & k) == phase, tile, roll_x(tile, -k if phase else k))


def packed_jacobian(uv, fk, level):
    scale = 0.25**level
    even = (sub_of() & 1) == 0
    u, v = jnp.where(even, uv, roll_z(uv, 1)), jnp.where(even, roll_z(uv, -1), uv)
    f, k = jnp.where(even, fk, roll_z(fk, 1)), jnp.where(even, roll_z(fk, -1), fk)
    product, squared = u * v, v * v
    diag = jnp.where(
        even,
        INV_STEP + squared + f + 6.0 * DIFF[0] * scale,
        INV_STEP + f + k - 2.0 * product + 6.0 * DIFF[1] * scale,
    )
    return 1.0 / diag, jnp.where(even, -2.0 * product, squared), diag


def packed_spread(uv, fk, level):
    scale = 0.25**level
    even = (sub_of() & 1) == 0
    inverse, other, _ = packed_jacobian(uv, fk, level)
    return jnp.where(even, 6.0 * DIFF[0] * scale - other, 6.0 * DIFF[1] * scale + other) * inverse


def packed_terms(source, g, n, level):
    k = 1 << level
    lane, sub = lane_of(), sub_of()
    even = (sub & 1) == 0
    first, last = (lane & (k - 1)) == 0, (lane & (k - 1)) == k - 1
    low, high = lane < k, lane >= X - k
    diff = jnp.where(even, DIFF[0] * 0.25**level, DIFF[1] * 0.25**level)
    wide = [source[t, pl.ds(g - 1, n + 2)] for t in (0, 1)]
    centre = [w[1 : n + 1] for w in wide]
    right = [roll_x(c, k) for c in centre]
    left = [roll_x(c, -k) for c in centre]
    out = []
    for t in (0, 1):
        c, w = centre[t], wide[t]
        total = jnp.where(low, right[1 - t], right[t]) + jnp.where(high, left[1 - t], left[t])
        if k == 2:
            ahead, back = roll_x(w, 1), roll_x(w, -1)
            total = total + jnp.where(first, back[0:n], ahead[1 : n + 1])
            total = total + jnp.where(last, ahead[2 : n + 2], back[1 : n + 1])
            total = total + roll_z(c, 2) + roll_z(c, -2)
        else:
            total = total + jnp.where(first, roll_x(w[0:n], -(k - 1)), roll_x(c, 1))
            total = total + jnp.where(last, roll_x(w[2 : n + 2], k - 1), roll_x(c, -1))
            total = total + 2.0 * roll_z(c, 4)
        other = jnp.where(even, roll_z(c, -1), roll_z(c, 1))
        out.append((c, other, diff * total))
    return out


def packed_first(coef, shift, b, target, d, g, n, gain):
    for t in (0, 1):
        value = gain * coef[0, t, pl.ds(g + shift, n)] * b[t, pl.ds(g + shift, n)]
        d[t, pl.ds(g, n)] = value
        target[t, pl.ds(g, n)] = value


def packed_step(level, coef, shift, b, source, target, d, g, n, carry, gain):
    for t, (c, other, spread) in enumerate(packed_terms(source, g, n, level)):
        at = pl.ds(g + shift, n)
        res = coef[0, t, at] * (b[t, at] + coef[1, t, at] * other + spread) - c
        delta = gain * res
        if carry is not None:
            delta = delta + carry * d[t, pl.ds(g, n)]
        d[t, pl.ds(g, n)] = delta
        target[t, pl.ds(g, n)] = c + delta


def plane(ref, f, y, rows):
    return ref[pl.ds(f * Z * rows + y, Z, stride=rows), :]


def is_even(axis):
    return lax.rem(lax.axis_index(axis), 2) == 0


def prev_of(even, first, second, at):
    return jnp.where(even, first[at], second[at])


def next_of(even, first, second, at):
    return jnp.where(even, second[at], first[at])


SOURCES = ((0, 0), (0, 1), (1, 0), (1, 1), (2, 0), (3, 0))


def first_kernel(rows, state, previous, feed, kill, first, second, coarse, *rest):
    held, sems = rest[:4], rest[4]
    copies = [
        pltpu.make_async_copy(ref, to, sems.at[i]) for i, (ref, to) in enumerate(zip((state, previous, feed, kill), held))
    ]
    for copy in copies:
        copy.start()
    for copy in copies:
        copy.wait()
    even = is_even("gy")
    values = []
    for i, (j, f) in enumerate(SOURCES):
        wanted = range(rows) if i not in (2, 3) else [*range(SENT), *range(rows - SENT, rows)]
        values.append({y: plane(held[j], f, y, rows)[None] for y in wanted})
    for i in (2, 3):
        weight = DIFF[i - 2] / INV_STEP
        values[i][SENT - 1] = values[i][SENT - 1] + weight * values[i - 2][SENT]
        values[i][rows - SENT] = values[i][rows - SENT] + weight * values[i - 2][rows - SENT - 1]
    for i in range(6):
        for y in range(SENT):
            top, bottom = values[i][y], values[i][rows - SENT + y]
            at = slice(i * SENT + y, i * SENT + y + 1)
            first[at] = jnp.where(even, top, bottom)
            second[at] = jnp.where(even, bottom, top)
    pairs = []
    for p, (i, j) in enumerate(((0, 1), (4, 5))):
        parts = []
        for g in range(OWN):
            sums = [
                jnp.concatenate([value[4 * g + 2 * q] + value[4 * g + 2 * q + 1] for q in (0, 1)], axis=0)
                for value in (values[i], values[j])
            ]
            parts.append(restrict_01(*sums))
        pairs.append(jnp.concatenate(parts, axis=0))
        coarse[p * OWN : (p + 1) * OWN] = pairs[p]
        for ref in (first, second):
            ref[FIELDS1 + p * OWN : FIELDS1 + (p + 1) * OWN] = pairs[p]
    uv, fk = (restrict_12([pair[j : j + 1] for j in range(OWN)]) for pair in pairs)
    both = jnp.where((sub_of() & 2) == 0, uv, fk)
    coarse[2 * OWN : 2 * OWN + 1] = both
    for ref in (first, second):
        ref[FIELDS2 : FIELDS2 + 1] = both


def split_fields2(both):
    low = (sub_of() & 2) == 0
    return jnp.where(low, both, roll_z(both, 2)), jnp.where(low, roll_z(both, -2), both)


def write_spread(main, coarse, out):
    lane = lax.broadcasted_iota(jnp.int32, (1, X), 1)
    u, v, f, k = (main[i] for i in (0, 1, 4, 5))
    cross, squared, inv_u, inv_v, _, _ = jacobian(u, v, f, k, 0)
    tops = [jnp.max(jnp.maximum((6.0 * DIFF[0] + cross) * inv_u, (6.0 * DIFF[1] + squared) * inv_v), axis=0)]
    tops.append(jnp.max(packed_spread(coarse[0:OWN], coarse[OWN : 2 * OWN], 1), axis=0))
    tops.append(packed_spread(*split_fields2(coarse[2 * OWN : 2 * OWN + 1]), 2)[0])
    result = jnp.zeros((1, X), jnp.float32)
    for level, top in enumerate(tops):
        top = jnp.max(jnp.max(top, axis=0, keepdims=True), axis=1, keepdims=True)
        result = jnp.where(lane == level, jnp.broadcast_to(top, (1, X)), result)
    out[...] = jnp.broadcast_to(result[None], out.shape)


GROUPS1 = HI1 - LO1
GROUPS2 = HI2 - LO2


def tiles_for(entries):
    return -(-entries // PER)


def pack_edges(entries, even, first, second):
    lane = lane_of()
    share = first.shape[0]
    left, right = None, None
    for j in range(PER):
        part = entries[j * share : (j + 1) * share]
        a, b = roll_x(part, WIDE * j), roll_x(part, WIDE + WIDE * j)
        left = a if left is None else jnp.where(lane >= WIDE * j, a, left)
        right = b if right is None else jnp.where(lane >= WIDE * j, b, right)
    first[...] = jnp.where(even, left, right)
    second[...] = jnp.where(even, right, left)


def halo_tiles(even, packets, lo, hi):
    first, second = packets
    share = first.shape[0]
    lane = lane_of()
    out = []
    for j in range(PER):
        a, b = max(lo, j * share), min(hi, (j + 1) * share)
        if a < b:
            strip = slice(a - j * share, b - j * share)
            left, right = prev_of(even, first, second, strip), next_of(even, first, second, strip)
            value = jnp.where(lane < X // 2, roll_x(right, -WIDE * j), roll_x(left, X - WIDE - WIDE * j))
            out.append((a - lo, b - lo, value))
    return out


def pack_own_kernel(
    rows, state, previous, feed, kill, coarse, first, second, spread, main, held, copies, sem
):
    inputs = (state, previous, feed, kill)
    for i, (j, f) in enumerate(SOURCES):
        for y in range(rows):
            main[i, y] = plane(inputs[j], f, y, rows)
    write_spread(main, coarse, copies)
    copy = pltpu.make_async_copy(copies, spread, sem)
    copy.start()
    for i in range(6):
        held[i * rows : (i + 1) * rows] = main[i]
    held[6 * rows : 6 * rows + 2 * OWN + 1] = coarse[...]
    pack_edges(held, is_even("gx"), first, second)
    copy.wait()


def pack_corner_kernel(y_first, y_second, first, second, held):
    even = is_even("gy")
    every = slice(0, PACKET)
    held[0:PACKET] = prev_of(even, y_first, y_second, every)
    held[PACKET : 2 * PACKET] = next_of(even, y_first, y_second, every)
    pack_edges(held, is_even("gx"), first, second)


EDGE_TILES = 2 * EDGE + 1


def level0_setup(fields, keep, diag, power, r, n):
    at = pl.ds(r, n)
    u, nb_u = neighbour_sums(lambda t, a, m: fields[0, t, pl.ds(a, m)], r, n, 1)
    v, nb_v = neighbour_sums(lambda t, a, m: fields[1, t, pl.ds(a, m)], r, n, 1)
    for t in (0, 1):
        f, k = fields[4, t, at], fields[5, t, at]
        cross, squared, inv_u, inv_v, first, second = jacobian(u[t], v[t], f, k, 0)
        react = u[t] * squared
        b_u = DIFF[0] * (nb_u[t] - 6.0 * u[t]) - INV_STEP * (u[t] - fields[2, t, at]) - react + f * (1.0 - u[t])
        b_v = DIFF[1] * (nb_v[t] - 6.0 * v[t]) - INV_STEP * (v[t] - fields[3, t, at]) + react - (f + k) * v[t]
        for i, value in enumerate((cross, squared, inv_u, inv_v, b_u, b_v)):
            keep[i, t, at] = value
        for i, value in enumerate((first, second)):
            diag[i, t, at] = value
        for i, value in enumerate((inv_u * b_u, inv_v * b_v)):
            power[i, t, at] = value


def level0_power(keep, source, target, r, n):
    for i, values in enumerate(next_power(keep, source, r, n)):
        for t in (0, 1):
            target[i, t, pl.ds(r, n)] = values[t]


def level0_down(keep, diag, y1, y2, sources, r, n):
    at = pl.ds(r, n)
    last = next_power(keep, y2, r, n)
    for t in (0, 1):
        both = [diag[i, t, at] for i in (0, 1)]
        parts = [[keep[4 + i, t, at] for i in (0, 1)]]
        parts += [[both[i] * power[i, t, at] for i in (0, 1)] for power in (y1, y2)]
        parts.append([both[i] * last[i][t] for i in (0, 1)])
        for q, part in enumerate(parts):
            u, v = (pair_rows(value) for value in part)
            for j in range(n // 4):
                value = restrict_01(u[2 * j : 2 * j + 2], v[2 * j : 2 * j + 2])
                sources[q, t, pl.ds((r - HALO0) // 4 + j, 1)] = value


def inner(rows, lost):
    return slice(HALO0 + lost, HALO0 + rows - lost)


def ends(rows, lo, hi):
    total = rows + 2 * HALO0
    return slice(lo, hi), slice(total - hi, total - lo)


def put_ends(target, rows, lo, hi, source):
    n = hi - lo
    for at, part in zip(ends(rows, lo, hi), (slice(0, n), slice(n, 2 * n))):
        for i in range(target.shape[0]):
            for t in (0, 1):
                target[i, t, at] = source[i, t, part]


def take_ends(source, rows, lo, hi, target):
    n = hi - lo
    for at, part in zip(ends(rows, lo, hi), (slice(0, n), slice(n, 2 * n))):
        for i in range(source.shape[0]):
            for t in (0, 1):
                target[i, t, part] = source[i, t, at]


def level0_inner_kernel(rows, main, own_a, own_b, keep_in, y0_in, y1_in, y2_in, diag_in, sources_in, *scratch):
    fields, keep, diag, y0, y1, y2 = scratch
    even_x = is_even("gx")
    for i in range(6):
        fields[i, 0, HALO0 : HALO0 + rows] = main[i]
        for a, b, value in halo_tiles(even_x, (own_a, own_b), i * rows, (i + 1) * rows):
            fields[i, 1, HALO0 + a : HALO0 + b] = value
    first = HALO0 + 1
    level0_setup(fields, keep, diag, y0, first, rows - 2)
    level0_power(keep, y0, y1, first + 1, rows - 4)
    level0_power(keep, y1, y2, first + 2, rows - 6)
    level0_down(keep, diag, y1, y2, sources_in, first + 3, rows - 8)
    for source, target, lost in ((keep, keep_in, 1), (y1, y1_in, 2), (y2, y2_in, 3)):
        for i in range(source.shape[0]):
            for t in (0, 1):
                target[i, t] = source[i, t, inner(rows, lost)]
    take_ends(y0, rows, HALO0 + 1, HALO0 + 3, y0_in)
    take_ends(diag, rows, HALO0 + 1, HALO0 + 4, diag_in)


def level0_outer_kernel(
    rows,
    main,
    y_first,
    y_second,
    own_a,
    own_b,
    corner_a,
    corner_b,
    keep_in,
    y0_in,
    y1_in,
    y2_in,
    diag_in,
    sources_in,
    keep_out,
    y1_out,
    y2_out,
    sources,
    edges,
    *scratch,
):
    fields, keep, diag, y0, y1, y2 = scratch
    even, even_x = is_even("gy"), is_even("gx")
    total = rows + 2 * HALO0
    near, skip = HALO0 + 2, HALO0 - SENT
    for i in range(6):
        strip = slice(i * SENT, (i + 1) * SENT)
        fields[i, 0, skip:HALO0] = prev_of(even, y_first, y_second, strip)
        fields[i, 0, HALO0:near] = main[i, 0:2]
        fields[i, 0, total - near : total - HALO0] = main[i, rows - 2 : rows]
        fields[i, 0, HALO0 + rows : total - skip] = next_of(even, y_first, y_second, strip)
        for packets, lo, n, at in (
            ((corner_a, corner_b), i * SENT, SENT, skip),
            ((own_a, own_b), i * rows, 2, HALO0),
            ((own_a, own_b), (i + 1) * rows - 2, 2, total - near),
            ((corner_a, corner_b), PACKET + i * SENT, SENT, HALO0 + rows),
        ):
            for a, b, value in halo_tiles(even_x, packets, lo, lo + n):
                fields[i, 1, at + a : at + b] = value
    for i in (0, 1):
        for t in (0, 1):
            for at in (0, total - 1):
                fields[i, t, at] = jnp.zeros((Z, X), jnp.float32)
    for at, part in zip(ends(rows, 5, 8), (slice(0, 3), slice(rows - 5, rows - 2))):
        for i in range(6):
            for t in (0, 1):
                keep[i, t, at] = keep_in[i, t, part]
    put_ends(diag, rows, 5, 8, diag_in)
    put_ends(y0, rows, 5, 7, y0_in)
    for target, source, lost in ((y1, y1_in, 2), (y2, y2_in, 3)):
        n = rows - 2 * lost
        for at, part in zip(ends(rows, HALO0 + lost, HALO0 + lost + 2), (slice(0, 2), slice(n - 2, n))):
            for i in (0, 1):
                for t in (0, 1):
                    target[i, t, at] = source[i, t, part]
    for r in (1, total - 5):
        level0_setup(fields, keep, diag, y0, r, 4)
    for r in (2, total - 6):
        level0_power(keep, y0, y1, r, 4)
    for r in (3, total - 7):
        level0_power(keep, y1, y2, r, 4)
    for r in (4, total - 8):
        level0_down(keep, diag, y1, y2, sources, r, 4)
    for q in range(4):
        for t in (0, 1):
            sources[q, t, 1 : OWN - 1] = sources_in[q, t, 1 : OWN - 1]
    take_ends(keep, rows, 1, 5, keep_out)
    take_ends(y1, rows, 4, 6, y1_out)
    take_ends(y2, rows, 4, 7, y2_out)
    for p, power in enumerate((y0, y1, y2)):
        for side, start in enumerate((HALO0, HALO0 + rows - EDGE)):
            edges[p, side] = pack_rows(power, start)


def pack_rows(x, start):
    lane = lane_of()
    halo = None
    for i in (0, 1):
        for j in range(EDGE):
            at = i * EDGE + j
            value = roll_x(x[i, 1, start + j : start + j + 1], 4 + 8 * at)
            halo = value if halo is None else jnp.where((lane >> 3) == at, value, halo)
    return jnp.concatenate([x[i, 0, start : start + EDGE] for i in (0, 1)] + [halo], axis=0)


def squeeze(halo):
    lane = lane_of()
    last = halo[OWN - 1 : OWN]
    ahead = (lane >= WIDE) & (lane < 2 * WIDE)
    parts = [jnp.where(ahead, roll_x(last, WIDE), halo[0:1]), jnp.where(ahead, roll_x(last, 2 * WIDE - X), halo[1:2])]
    return jnp.concatenate(parts + [halo[2 : OWN - 1]], axis=0)


def unsqueeze(tiles):
    last = jnp.where(lane_of() < X // 2, roll_x(tiles[0:1], -WIDE), roll_x(tiles[1:2], X - 2 * WIDE))
    return jnp.concatenate([tiles, last], axis=0)


def combine_kernel(sources, edges, spread, own, first, second, edge_first, edge_second, gain):
    write_gains(jnp.max(spread[...], axis=0)[0:1], gain)
    p0, p1, p2 = (gain[POWERS + i] for i in range(3))
    for t in (0, 1):
        value = sources[0, t] - p0 * sources[1, t] + p1 * sources[2, t] - p2 * sources[3, t]
        own[t] = value
        for ref in (first, second):
            if t == 0:
                ref[0:OWN] = value
            else:
                ref[OWN:] = squeeze(value)
    even = is_even("gy")
    top, bottom = (p0 * edges[0, side] - p1 * edges[1, side] + p2 * edges[2, side] for side in (0, 1))
    edge_first[...] = jnp.where(even, top, bottom)
    edge_second[...] = jnp.where(even, bottom, top)


def coarse1_kernel(
    rows, coarse, y_first, y_second, own_a, own_b, corner_a, corner_b, gain, keep_in, y1_in, y2_in, keep_out, y1_out, y2_out,
    coef, keep0, x0, fields
):
    even, even_x = is_even("gy"), is_even("gx")
    own_x, corner_x = (own_a, own_b), (corner_a, corner_b)
    for p in (0, 1):
        to = p * GROUPS1
        strip = slice(FIELDS1 + p * OWN, FIELDS1 + (p + 1) * OWN)
        fields[0, to : to + OWN] = prev_of(even, y_first, y_second, strip)
        fields[0, to + OWN : to + 2 * OWN] = coarse[p * OWN : (p + 1) * OWN]
        fields[0, to + 2 * OWN : to + 3 * OWN] = next_of(even, y_first, y_second, strip)
        for part, (packets, lo) in enumerate(
            ((corner_x, FIELDS1), (own_x, 6 * rows), (corner_x, PACKET + FIELDS1))
        ):
            lo += p * OWN
            for a, b, value in halo_tiles(even_x, packets, lo, lo + OWN):
                fields[1, to + part * OWN + a : to + part * OWN + b] = value
    for t in (0, 1):
        for i, value in enumerate(packed_jacobian(fields[t, 0:GROUPS1], fields[t, GROUPS1 : 2 * GROUPS1], 1)):
            coef[i, t, 1 : SIZE1 - 1] = value

    def whole(inside, outside):
        n = outside.shape[0] // 2
        return jnp.concatenate([outside[0:n], inside, outside[n:]], axis=0)

    for i in range(6):
        for t in (0, 1):
            keep0[i, t, 1 : rows + 2 * HALO0 - 1] = whole(keep_in[i, t], keep_out[i, t])
    p0, p1, p2 = (gain[POWERS + i] for i in range(3))
    for i in (0, 1):
        for t in (0, 1):
            y0 = keep0[2 + i, t, HALO0 : HALO0 + rows] * keep0[4 + i, t, HALO0 : HALO0 + rows]
            y1, y2 = (whole(a[i, t], b[i, t]) for a, b in ((y1_in, y1_out), (y2_in, y2_out)))
            x0[i, t] = p0 * y0 - p1 * y1 + p2 * y2


def fields2_kernel(rows, coarse, y_first, y_second, own_a, own_b, corner_a, corner_b, out):
    even, even_x = is_even("gy"), is_even("gx")
    own_x, corner_x = (own_a, own_b), (corner_a, corner_b)
    near = slice(FIELDS2, FIELDS2 + 1)
    out[0, 0:1] = prev_of(even, y_first, y_second, near)
    out[0, 1:2] = coarse[2 * OWN : 2 * OWN + 1]
    out[0, 2:3] = next_of(even, y_first, y_second, near)
    for q, (packets, lo) in enumerate(
        ((corner_x, FIELDS2), (own_x, 6 * rows + 2 * OWN), (corner_x, PACKET + FIELDS2))
    ):
        out[1, q : q + 1] = halo_tiles(even_x, packets, lo, lo + 1)[0][2]


def level1_kernel(
    own, first, second, edge_a, edge_b, fields2, coef1, gain, packet, to_first, to_second, to_far, keep, y1, d1
):
    b1, x1 = keep.at[0], keep.at[1]
    even = is_even("gy")
    for t in (0, 1):
        b1[t, 1 + OWN : 1 + 2 * OWN] = own[t]
        for at, take in ((1, prev_of), (1 + 2 * OWN, next_of)):
            if t == 0:
                b1[t, at : at + OWN] = take(even, first, second, slice(0, OWN))
            else:
                b1[t, at : at + OWN] = unsqueeze(take(even, first, second, slice(OWN, 2 * OWN - 1)))
    g0, g1, g2 = (gain[3 + i] for i in range(3))
    n = GROUPS1
    packed_first(coef1, 0, b1, x1, d1, 1, n, g0)
    packed_step(1, coef1, 0, b1, x1, y1, d1, 2, n - 2, CARRY1, g1)
    packed_step(1, coef1, 0, b1, y1, x1, d1, 2, n - 2, CARRY2, g2)
    here = pl.ds(1 + OWN, OWN)
    values = []
    for t, (c, other, spread) in enumerate(packed_terms(x1, 1 + OWN, OWN, 1)):
        res = b1[t, here] - coef1[2, t, here] * c + coef1[1, t, here] * other + spread
        values.append(restrict_12([res[j : j + 1] for j in range(OWN)]))
        to_far[1 + t : 2 + t] = fields2[t, 1:2]
    value = jnp.where((sub_of() & 2) == 0, values[0], values[1])
    for ref in (packet, to_first, to_second, to_far):
        ref[0:1] = value
    to_first[1:] = edge_a[...]
    to_second[1:] = edge_b[...]


def rest_kernel(
    own2, near_a, near_b, far_a, far_b, gain, coef1, fields2, keep0, iterate, keep1, out, coef2, d1, b2, x2, y2, d2, xu, yu, x0, y0, d0
):
    rows = out.shape[0] // (2 * Z)
    even = (sub_of() & 1) == 0
    b1, x1 = keep1.at[0], keep1.at[1]

    even_y, low = is_even("gy"), lax.rem(lax.axis_index("gy"), 4) < 2
    at = slice(0, 1)
    parts = [
        next_of(low, far_a, far_b, at),
        prev_of(even_y, near_a, near_b, at),
        own2[at],
        next_of(even_y, near_a, near_b, at),
        prev_of(low, far_a, far_b, at),
    ]
    for t, values in enumerate(split_fields2(jnp.concatenate(parts, axis=0))):
        b2[t, 1 : SIZE2 - 1] = values
        at = slice(1 + t, 2 + t)
        parts = [next_of(low, far_a, far_b, at), fields2[t], prev_of(low, far_a, far_b, at)]
        inverse, other, _ = packed_jacobian(*split_fields2(jnp.concatenate(parts, axis=0)), 2)
        coef2[0, t, 1 : SIZE2 - 1] = inverse
        coef2[1, t, 1 : SIZE2 - 1] = other

    n = HI2 - LO2
    g0, g1, g2 = (gain[6 + i] for i in range(3))
    packed_first(coef2, 0, b2, x2, d2, 1, n, g0)
    packed_step(2, coef2, 0, b2, x2, y2, d2, 1, n, CARRY1, g1)
    packed_step(2, coef2, 0, b2, y2, x2, d2, 1, n, CARRY2, g2)
    packed_step(2, coef2, 0, b2, x2, y2, d2, 1, n, None, g0)
    packed_step(2, coef2, 0, b2, y2, x2, d2, 2, n - 2, CARRY1, g1)
    packed_step(2, coef2, 0, b2, x2, y2, d2, 2, n - 2, CARRY2, g2)

    g0, g1, g2 = (gain[3 + i] for i in range(3))
    shift = LO_UP - LO1
    for t in (0, 1):
        for g in range(LO_UP, HI_UP):
            p = g % 4
            value = y2[t, g // 4 - LO2 + 1 : g // 4 - LO2 + 2]
            value = spread_x(spread_x(value, 1, p & 1), 2, p & 2)
            at = g - LO_UP + 1
            xu[t, at : at + 1] = x1[t, at + shift : at + shift + 1] + value
    n = HI_UP - LO_UP
    packed_step(1, coef1, shift, b1, xu, yu, d1, 2, n - 2, None, g0)
    packed_step(1, coef1, shift, b1, yu, xu, d1, 2, n - 2, CARRY1, g1)
    packed_step(1, coef1, shift, b1, xu, yu, d1, 3, n - 4, CARRY2, g2)

    g0, g1, g2 = (gain[i] for i in range(3))
    for i in (0, 1):
        for at, take in ((HALO0 - EDGE, prev_of), (HALO0 + rows, next_of)):
            whole = take(even_y, near_a, near_b, slice(1, 1 + EDGE_TILES))
            x0[i, 0, at : at + EDGE] = whole[i * EDGE : (i + 1) * EDGE]
            for j in range(EDGE):
                x0[i, 1, at + j : at + j + 1] = roll_x(whole[2 * EDGE :], -(4 + 8 * (i * EDGE + j)))
        for t in (0, 1):
            x0[i, t, HALO0 : HALO0 + rows] = iterate[i, t]
    for t in (0, 1):
        for row in range(-2, rows // 2 + 2):
            at = row // 2 - LO_UP + 1
            value = spread_x(yu[t, at : at + 1], 1, row & 1)
            for i, fine in enumerate((jnp.where(even, value, roll_z(value, 1)), jnp.where(even, roll_z(value, -1), value))):
                for y in (2 * row, 2 * row + 1):
                    if -EDGE <= y < rows + EDGE:
                        x0[i, t, y + HALO0 : y + HALO0 + 1] = x0[i, t, y + HALO0 : y + HALO0 + 1] + fine
    total = rows + 2 * HALO0
    rows_loop(2, total - 2, lambda r, n: cheb_step(0, keep0, x0, y0, d0, r, n, None, g0))
    rows_loop(3, total - 3, lambda r, n: cheb_step(0, keep0, y0, x0, d0, r, n, CARRY1, g1))
    last = cheb_step(0, keep0, x0, None, d0, HALO0, rows, CARRY2, g2, (0,))[0]
    for i in (0, 1):
        for y in range(rows):
            out[pl.ds(i * Z * rows + y, Z, stride=rows), :] = last[i][y]


def call(kernel, out_shapes, scratch, *args, space=pltpu.VMEM, outs=None):
    out = [jax.ShapeDtypeStruct(shape, jnp.float32) for shape in out_shapes]
    return pl.pallas_call(
        kernel,
        out_shape=out,
        in_specs=[pl.BlockSpec(memory_space=space)] * len(args),
        out_specs=[pl.BlockSpec(memory_space=m) for m in outs or [pltpu.VMEM] * len(out)],
        scratch_shapes=[pltpu.VMEM(s, jnp.float32) if isinstance(s, tuple) else s for s in scratch],
        compiler_params=pltpu.CompilerParams(vmem_limit_bytes=24 * 2**20),
    )(*args)


def swap(value, axis, step):
    count = lax.axis_size(axis)
    assert count % 2 == 0
    pairs = [(i, (i + step) % count) for i in range(0, count, 2)]
    return lax.ppermute(value, axis, pairs + [(j, i) for i, j in pairs])


def swap_far(value, axis, step):
    count = lax.axis_size(axis)
    assert count % 4 == 0
    pairs = [(i + j, (i + j + 2 * step) % count) for i in range(0, count, 4) for j in (0, 1)]
    return lax.ppermute(value, axis, pairs + [(j, i) for i, j in pairs])


def exchange(first, second, axis):
    return swap(first, axis, -1), swap(second, axis, 1)


def body(state, previous, feed, kill):
    _, depth, rows, cols = state.shape
    assert depth == Z and cols == X and rows == 4 * OWN
    across, count = lax.axis_size("gx"), lax.axis_size("gy")
    total0 = rows + 2 * HALO0
    state = state.reshape(2 * Z * rows, X)
    previous = previous.reshape(2 * Z * rows, X)
    feed = feed.reshape(Z * rows, X)
    kill = kill.reshape(Z * rows, X)
    inputs = (state, previous, feed, kill)

    strip = (PACKET, Z, X)
    first, second, coarse, *inputs = call(
        functools.partial(first_kernel, rows),
        [strip, strip, (2 * OWN + 1, Z, X), *(a.shape for a in inputs)],
        [pltpu.SemaphoreType.DMA((4,))],
        *(pltpu.with_memory_space_constraint(a, pltpu.HBM) for a in inputs),
        space=pltpu.HBM,
    )
    y_packets = exchange(first, second, "gy")

    tiles = tiles_for(6 * rows + 2 * OWN + 1)
    spread_shape = (across * count, Z // 2, X)
    first, second, spread, main = call(
        functools.partial(pack_own_kernel, rows),
        [(tiles, Z, X), (tiles, Z, X), spread_shape, (6, rows, Z, X)],
        [(PER * tiles, Z, X), spread_shape, pltpu.SemaphoreType.DMA],
        *inputs,
        coarse,
        outs=[pltpu.VMEM, pltpu.VMEM, pltpu.HBM, pltpu.VMEM],
    )
    own_x = exchange(first, second, "gx")
    spread = lax.all_to_all(spread, ("gx", "gy"), 0, 0, tiled=True)
    tiles = tiles_for(2 * PACKET)
    corner_x = exchange(
        *call(pack_corner_kernel, [(tiles, Z, X), (tiles, Z, X)], [(PER * tiles, Z, X)], *y_packets), "gx"
    )

    strip, edge = (2 * OWN - 1, Z, X), (EDGE_TILES, Z, X)
    pair0 = (2, 2, total0, Z, X)
    work = [(6, 2, total0, Z, X), (6, 2, total0, Z, X), pair0, pair0, pair0, pair0]
    four = (4, 2, OWN, Z, X)
    inside = call(
        functools.partial(level0_inner_kernel, rows),
        [
            (6, 2, rows - 2, Z, X),
            (2, 2, 4, Z, X),
            (2, 2, rows - 4, Z, X),
            (2, 2, rows - 6, Z, X),
            (2, 2, 6, Z, X),
            four,
        ],
        work,
        main,
        *own_x,
    )
    keep_in, _, y1_in, y2_in, _, _ = inside
    keep_out, y1_out, y2_out, sources, edges = call(
        functools.partial(level0_outer_kernel, rows),
        [(6, 2, 8, Z, X), (2, 2, 4, Z, X), (2, 2, 6, Z, X), four, (3, 2, *edge)],
        work,
        main,
        *y_packets,
        *own_x,
        *corner_x,
        *inside,
    )
    own, first, second, edge_a, edge_b, gain = call(
        combine_kernel,
        [(2, OWN, Z, X), strip, strip, edge, edge, (POWERS + 3, Z, X)],
        [],
        sources,
        edges,
        spread,
    )
    coef1, keep0, iterate = call(
        functools.partial(coarse1_kernel, rows),
        [(3, 2, SIZE1, Z, X), (6, 2, total0, Z, X), (2, 2, rows, Z, X)],
        [(2, 2 * GROUPS1, Z, X)],
        coarse,
        *y_packets,
        *own_x,
        *corner_x,
        gain,
        keep_in,
        y1_in,
        y2_in,
        keep_out,
        y1_out,
        y2_out,
    )
    (fields2,) = call(
        functools.partial(fields2_kernel, rows), [(2, 3, Z, X)], [], coarse, *y_packets, *own_x, *corner_x
    )
    b_packets = exchange(first, second, "gy")

    one, two, up = (2, SIZE1, Z, X), (2, SIZE2, Z, X), (2, SIZE_UP, Z, X)
    near = (1 + EDGE_TILES, Z, X)
    packet, first, second, to_far, keep1 = call(
        level1_kernel,
        [(1, Z, X), near, near, (3, Z, X), (2, *one)],
        [one, one],
        own,
        *b_packets,
        edge_a,
        edge_b,
        fields2,
        coef1,
        gain,
    )
    far = (swap_far(to_far, "gy", 1), swap_far(to_far, "gy", -1))
    near = exchange(first, second, "gy")

    (out,) = call(
        rest_kernel,
        [(2 * Z * rows, X)],
        [(2, *two), one, two, two, two, two, up, up, pair0, pair0, pair0],
        packet,
        *near,
        *far,
        gain,
        coef1,
        fields2,
        keep0,
        iterate,
        keep1,
    )
    return out.reshape(2, Z, rows, X)


def solution(mesh):
    placed = (
        P(None, None, "gy", "gx"),
        P(None, None, "gy", "gx"),
        P(None, "gy", "gx"),
        P(None, "gy", "gx"),
    )
    return jax.shard_map(
        body, mesh=mesh, in_specs=placed, out_specs=P(None, None, "gy", "gx"), check_vma=False
    )
```

```python
import functools

import jax
import jax.numpy as jnp
from jax import lax
from jax.experimental import pallas as pl
from jax.experimental.pallas import tpu as pltpu
from jax.sharding import PartitionSpec as P

DIFF = (40.0, 20.0)
INV_STEP = 2.0
LOWER = 0.25

_CENTRE = (1.0 + LOWER) / 2.0
_HALF = (1.0 - LOWER) / 2.0
_SIGMA = _CENTRE / _HALF
_RHO0 = 1.0 / _SIGMA
_RHO1 = 1.0 / (2.0 * _SIGMA - _RHO0)
_RHO2 = 1.0 / (2.0 * _SIGMA - _RHO1)

Z = 8
X = 128
HALO0 = 4
SENT = 3
FIELDS1 = 6 * SENT
FIELDS2 = FIELDS1 + 8
PACKET = FIELDS2 + 1
WIDE = 42
PER = X // WIDE
EDGE = 3

LO1, HI1 = -4, 8
LO2, HI2 = -2, 3
LO_UP, HI_UP = -3, 7
SIZE1, SIZE2, SIZE_UP = HI1 - LO1 + 2, HI2 - LO2 + 2, HI_UP - LO_UP + 2
OWN = 4


def lane_of():
    return lax.broadcasted_iota(jnp.int32, (1, Z, X), 2)


def sub_of():
    return lax.broadcasted_iota(jnp.int32, (1, Z, X), 1)


def roll_x(tile, shift):
    shift = shift % X
    return pltpu.roll(tile, shift, 2) if shift else tile


def roll_z(tile, shift):
    shift = shift % Z
    return pltpu.roll(tile, shift, 1) if shift else tile


def chunks(lo, hi, step=4):
    return [(r, min(step, hi - r)) for r in range(lo, hi, step)]


def neighbour_sums(read, r, n, k, tiles=(0, 1)):
    lane = lane_of()
    low, high = lane < k, lane >= X - k
    centre = [read(t, r, n) for t in (0, 1)]
    right = [roll_x(c, k) for c in centre]
    left = [roll_x(c, -k) for c in centre]
    sums = []
    for t in tiles:
        c = centre[t]
        along_x = jnp.where(low, right[1 - t], right[t]) + jnp.where(high, left[1 - t], left[t])
        along_y = read(t, r - 1, n) + read(t, r + 1, n)
        along_z = 2.0 * roll_z(c, k) if 2 * k == Z else roll_z(c, k) + roll_z(c, -k)
        sums.append(along_x + along_y + along_z)
    return centre, sums


def jacobian(u, v, f, k, level):
    scale = 0.25**level
    product = u * v
    squared = v * v
    first = INV_STEP + squared + f + 6.0 * DIFF[0] * scale
    second = INV_STEP + f + k - 2.0 * product + 6.0 * DIFF[1] * scale
    return 2.0 * product, squared, 1.0 / first, 1.0 / second, first, second


def cheb_step(level, keep, source, target, d, r, n, carry, gain, tiles=(0, 1)):
    scale = 0.25**level
    k = 1 << level
    u, nb_u = neighbour_sums(lambda t, a, m: source[0, t, pl.ds(a, m)], r, n, k, tiles)
    v, nb_v = neighbour_sums(lambda t, a, m: source[1, t, pl.ds(a, m)], r, n, k, tiles)
    rows = pl.ds(r, n)
    out = []
    for t in tiles:
        cross, squared, inv_u, inv_v = (keep[i, t, rows] for i in range(4))
        res_u = inv_u * (keep[4, t, rows] - cross * v[t] + DIFF[0] * scale * nb_u[t]) - u[t]
        res_v = inv_v * (keep[5, t, rows] + squared * u[t] + DIFF[1] * scale * nb_v[t]) - v[t]
        du, dv = gain * res_u, gain * res_v
        if carry is not None:
            du = du + carry * d[0, t, rows]
            dv = dv + carry * d[1, t, rows]
        if target is not None:
            d[0, t, rows] = du
            d[1, t, rows] = dv
            target[0, t, rows] = u[t] + du
            target[1, t, rows] = v[t] + dv
        out.append((u[t] + du, v[t] + dv))
    return out


def next_power(keep, source, r, n):
    u, nb_u = neighbour_sums(lambda t, a, m: source[0, t, pl.ds(a, m)], r, n, 1)
    v, nb_v = neighbour_sums(lambda t, a, m: source[1, t, pl.ds(a, m)], r, n, 1)
    rows = pl.ds(r, n)
    first, second = [], []
    for t in (0, 1):
        cross, squared, inv_u, inv_v = (keep[i, t, rows] for i in range(4))
        first.append(u[t] + inv_u * (cross * v[t] - DIFF[0] * nb_u[t]))
        second.append(v[t] - inv_v * (squared * u[t] + DIFF[1] * nb_v[t]))
    return first, second


CARRY1 = _RHO1 * _RHO0
CARRY2 = _RHO2 * _RHO1


POWERS = 9


def write_gains(spread, out):
    lane = lax.broadcasted_iota(jnp.int32, (1, X), 1)
    for level in range(3):
        top = jnp.max(jnp.where(lane == level, spread, 0.0), axis=1, keepdims=True)
        tau = 1.0 / (1.0 + jnp.broadcast_to(top, (Z, X)))
        for i, factor in enumerate((1.0 / _CENTRE, 2.0 * _RHO1 / _HALF, 2.0 * _RHO2 / _HALF)):
            out[3 * level + i] = factor * tau
    g0, g1, g2 = (out[i] for i in range(3))
    first, second = g0 + CARRY1 * g0 + g1, g1 * g0
    out[POWERS] = first + CARRY2 * (CARRY1 * g0 + g1) + g2
    out[POWERS + 1] = second + CARRY2 * second + g2 * first
    out[POWERS + 2] = g2 * second


def pair_rows(value):
    n = value.shape[0] // 2
    pairs = value.reshape(n, 2, Z, X)
    return pairs[:, 0] + pairs[:, 1]


def restrict_01(first, second):
    lane, sub = lane_of(), sub_of()
    across = []
    for value in (first, second):
        a, b = value[0:1], value[1:2]
        across.append(jnp.where((lane & 1) == 0, a + roll_x(a, -1), b + roll_x(b, 1)))
    a, b = across
    return 0.125 * jnp.where((sub & 1) == 0, a + roll_z(a, -1), b + roll_z(b, 1))


def restrict_12(groups):
    lane, sub = lane_of(), sub_of()
    out = None
    for p, value in enumerate(groups):
        value = value + roll_x(value, 1 if p & 1 else -1)
        value = value + roll_x(value, 2 if p & 2 else -2)
        out = value if out is None else jnp.where((lane & 3) == p, value, out)
    return 0.125 * (out + jnp.where((sub & 2) == 0, roll_z(out, -2), roll_z(out, 2)))


def spread_x(tile, k, phase):
    return jnp.where((lane_of() & k) == phase, tile, roll_x(tile, -k if phase else k))


def packed_jacobian(uv, fk, level):
    scale = 0.25**level
    even = (sub_of() & 1) == 0
    u, v = jnp.where(even, uv, roll_z(uv, 1)), jnp.where(even, roll_z(uv, -1), uv)
    f, k = jnp.where(even, fk, roll_z(fk, 1)), jnp.where(even, roll_z(fk, -1), fk)
    product, squared = u * v, v * v
    diag = jnp.where(
        even,
        INV_STEP + squared + f + 6.0 * DIFF[0] * scale,
        INV_STEP + f + k - 2.0 * product + 6.0 * DIFF[1] * scale,
    )
    return 1.0 / diag, jnp.where(even, -2.0 * product, squared), diag


def packed_spread(uv, fk, level):
    scale = 0.25**level
    even = (sub_of() & 1) == 0
    inverse, other, _ = packed_jacobian(uv, fk, level)
    return jnp.where(even, 6.0 * DIFF[0] * scale - other, 6.0 * DIFF[1] * scale + other) * inverse


def packed_terms(source, g, n, level):
    k = 1 << level
    lane, sub = lane_of(), sub_of()
    even = (sub & 1) == 0
    first, last = (lane & (k - 1)) == 0, (lane & (k - 1)) == k - 1
    low, high = lane < k, lane >= X - k
    diff = jnp.where(even, DIFF[0] * 0.25**level, DIFF[1] * 0.25**level)
    wide = [source[t, pl.ds(g - 1, n + 2)] for t in (0, 1)]
    centre = [w[1 : n + 1] for w in wide]
    right = [roll_x(c, k) for c in centre]
    left = [roll_x(c, -k) for c in centre]
    out = []
    for t in (0, 1):
        c, w = centre[t], wide[t]
        total = jnp.where(low, right[1 - t], right[t]) + jnp.where(high, left[1 - t], left[t])
        if k == 2:
            ahead, back = roll_x(w, 1), roll_x(w, -1)
            total = total + jnp.where(first, back[0:n], ahead[1 : n + 1])
            total = total + jnp.where(last, ahead[2 : n + 2], back[1 : n + 1])
            total = total + roll_z(c, 2) + roll_z(c, -2)
        else:
            total = total + jnp.where(first, roll_x(w[0:n], -(k - 1)), roll_x(c, 1))
            total = total + jnp.where(last, roll_x(w[2 : n + 2], k - 1), roll_x(c, -1))
            total = total + 2.0 * roll_z(c, 4)
        other = jnp.where(even, roll_z(c, -1), roll_z(c, 1))
        out.append((c, other, diff * total))
    return out


def packed_first(coef, shift, b, target, d, g, n, gain):
    for t in (0, 1):
        value = gain * coef[0, t, pl.ds(g + shift, n)] * b[t, pl.ds(g + shift, n)]
        d[t, pl.ds(g, n)] = value
        target[t, pl.ds(g, n)] = value


def packed_step(level, coef, shift, b, source, target, d, g, n, carry, gain):
    for t, (c, other, spread) in enumerate(packed_terms(source, g, n, level)):
        at = pl.ds(g + shift, n)
        res = coef[0, t, at] * (b[t, at] + coef[1, t, at] * other + spread) - c
        delta = gain * res
        if carry is not None:
            delta = delta + carry * d[t, pl.ds(g, n)]
        d[t, pl.ds(g, n)] = delta
        target[t, pl.ds(g, n)] = c + delta


def plane(ref, f, y, rows):
    return ref[pl.ds(f * Z * rows + y, Z, stride=rows), :]


def is_even(axis):
    return lax.rem(lax.axis_index(axis), 2) == 0


def prev_of(even, first, second, at):
    return jnp.where(even, first[at], second[at])


def next_of(even, first, second, at):
    return jnp.where(even, second[at], first[at])


SOURCES = ((0, 0), (0, 1), (1, 0), (1, 1), (2, 0), (3, 0))


def first_kernel(rows, state, previous, feed, kill, first, second, coarse, *rest):
    held, sems = rest[:4], rest[4]
    copies = [
        pltpu.make_async_copy(ref, to, sems.at[i]) for i, (ref, to) in enumerate(zip((state, previous, feed, kill), held))
    ]
    for copy in copies:
        copy.start()
    for copy in copies:
        copy.wait()
    even = is_even("gy")
    values = []
    for i, (j, f) in enumerate(SOURCES):
        wanted = range(rows) if i not in (2, 3) else [*range(SENT), *range(rows - SENT, rows)]
        values.append({y: plane(held[j], f, y, rows)[None] for y in wanted})
    for i in (2, 3):
        weight = DIFF[i - 2] / INV_STEP
        values[i][SENT - 1] = values[i][SENT - 1] + weight * values[i - 2][SENT]
        values[i][rows - SENT] = values[i][rows - SENT] + weight * values[i - 2][rows - SENT - 1]
    for i in range(6):
        for y in range(SENT):
            top, bottom = values[i][y], values[i][rows - SENT + y]
            at = slice(i * SENT + y, i * SENT + y + 1)
            first[at] = jnp.where(even, top, bottom)
            second[at] = jnp.where(even, bottom, top)
    pairs = []
    for p, (i, j) in enumerate(((0, 1), (4, 5))):
        parts = []
        for g in range(OWN):
            sums = [
                jnp.concatenate([value[4 * g + 2 * q] + value[4 * g + 2 * q + 1] for q in (0, 1)], axis=0)
                for value in (values[i], values[j])
            ]
            parts.append(restrict_01(*sums))
        pairs.append(jnp.concatenate(parts, axis=0))
        coarse[p * OWN : (p + 1) * OWN] = pairs[p]
        for ref in (first, second):
            ref[FIELDS1 + p * OWN : FIELDS1 + (p + 1) * OWN] = pairs[p]
    uv, fk = (restrict_12([pair[j : j + 1] for j in range(OWN)]) for pair in pairs)
    both = jnp.where((sub_of() & 2) == 0, uv, fk)
    coarse[2 * OWN : 2 * OWN + 1] = both
    for ref in (first, second):
        ref[FIELDS2 : FIELDS2 + 1] = both


def split_fields2(both):
    low = (sub_of() & 2) == 0
    return jnp.where(low, both, roll_z(both, 2)), jnp.where(low, roll_z(both, -2), both)


def write_spread(main, coarse, out):
    lane = lax.broadcasted_iota(jnp.int32, (1, X), 1)
    u, v, f, k = (main[i] for i in (0, 1, 4, 5))
    cross, squared, inv_u, inv_v, _, _ = jacobian(u, v, f, k, 0)
    tops = [jnp.max(jnp.maximum((6.0 * DIFF[0] + cross) * inv_u, (6.0 * DIFF[1] + squared) * inv_v), axis=0)]
    tops.append(jnp.max(packed_spread(coarse[0:OWN], coarse[OWN : 2 * OWN], 1), axis=0))
    tops.append(packed_spread(*split_fields2(coarse[2 * OWN : 2 * OWN + 1]), 2)[0])
    result = jnp.zeros((1, X), jnp.float32)
    for level, top in enumerate(tops):
        top = jnp.max(jnp.max(top, axis=0, keepdims=True), axis=1, keepdims=True)
        result = jnp.where(lane == level, jnp.broadcast_to(top, (1, X)), result)
    out[...] = jnp.broadcast_to(result[None], out.shape)


GROUPS1 = HI1 - LO1
GROUPS2 = HI2 - LO2


def tiles_for(entries):
    return -(-entries // PER)


def pack_edges(entries, even, first, second):
    lane = lane_of()
    share = first.shape[0]
    left, right = None, None
    for j in range(PER):
        part = entries[j * share : (j + 1) * share]
        a, b = roll_x(part, WIDE * j), roll_x(part, WIDE + WIDE * j)
        left = a if left is None else jnp.where(lane >= WIDE * j, a, left)
        right = b if right is None else jnp.where(lane >= WIDE * j, b, right)
    first[...] = jnp.where(even, left, right)
    second[...] = jnp.where(even, right, left)


def halo_tiles(even, packets, lo, hi):
    first, second = packets
    share = first.shape[0]
    lane = lane_of()
    out = []
    for j in range(PER):
        a, b = max(lo, j * share), min(hi, (j + 1) * share)
        if a < b:
            strip = slice(a - j * share, b - j * share)
            left, right = prev_of(even, first, second, strip), next_of(even, first, second, strip)
            value = jnp.where(lane < X // 2, roll_x(right, -WIDE * j), roll_x(left, X - WIDE - WIDE * j))
            out.append((a - lo, b - lo, value))
    return out


def pack_own_kernel(
    rows, state, previous, feed, kill, coarse, first, second, spread, main, held, copies, sem
):
    inputs = (state, previous, feed, kill)
    for i, (j, f) in enumerate(SOURCES):
        for y in range(rows):
            main[i, y] = plane(inputs[j], f, y, rows)
    write_spread(main, coarse, copies)
    copy = pltpu.make_async_copy(copies, spread, sem)
    copy.start()
    for i in range(6):
        held[i * rows : (i + 1) * rows] = main[i]
    held[6 * rows : 6 * rows + 2 * OWN + 1] = coarse[...]
    pack_edges(held, is_even("gx"), first, second)
    copy.wait()


def pack_corner_kernel(y_first, y_second, first, second, held):
    even = is_even("gy")
    every = slice(0, PACKET)
    held[0:PACKET] = prev_of(even, y_first, y_second, every)
    held[PACKET : 2 * PACKET] = next_of(even, y_first, y_second, every)
    pack_edges(held, is_even("gx"), first, second)


EDGE_TILES = 2 * EDGE + 1


def level0_setup(fields, keep, diag, power, r, n):
    at = pl.ds(r, n)
    u, nb_u = neighbour_sums(lambda t, a, m: fields[0, t, pl.ds(a, m)], r, n, 1)
    v, nb_v = neighbour_sums(lambda t, a, m: fields[1, t, pl.ds(a, m)], r, n, 1)
    for t in (0, 1):
        f, k = fields[4, t, at], fields[5, t, at]
        cross, squared, inv_u, inv_v, first, second = jacobian(u[t], v[t], f, k, 0)
        react = u[t] * squared
        b_u = DIFF[0] * (nb_u[t] - 6.0 * u[t]) - INV_STEP * (u[t] - fields[2, t, at]) - react + f * (1.0 - u[t])
        b_v = DIFF[1] * (nb_v[t] - 6.0 * v[t]) - INV_STEP * (v[t] - fields[3, t, at]) + react - (f + k) * v[t]
        for i, value in enumerate((cross, squared, inv_u, inv_v, b_u, b_v)):
            keep[i, t, at] = value
        for i, value in enumerate((first, second)):
            diag[i, t, at] = value
        for i, value in enumerate((inv_u * b_u, inv_v * b_v)):
            power[i, t, at] = value


def level0_power(keep, source, target, r, n):
    for i, values in enumerate(next_power(keep, source, r, n)):
        for t in (0, 1):
            target[i, t, pl.ds(r, n)] = values[t]


def level0_down(keep, diag, y1, y2, sources, r, n):
    at = pl.ds(r, n)
    last = next_power(keep, y2, r, n)
    for t in (0, 1):
        both = [diag[i, t, at] for i in (0, 1)]
        parts = [[keep[4 + i, t, at] for i in (0, 1)]]
        parts += [[both[i] * power[i, t, at] for i in (0, 1)] for power in (y1, y2)]
        parts.append([both[i] * last[i][t] for i in (0, 1)])
        for q, part in enumerate(parts):
            u, v = (pair_rows(value) for value in part)
            for j in range(n // 4):
                value = restrict_01(u[2 * j : 2 * j + 2], v[2 * j : 2 * j + 2])
                sources[q, t, pl.ds((r - HALO0) // 4 + j, 1)] = value


def inner(rows, lost):
    return slice(HALO0 + lost, HALO0 + rows - lost)


def ends(rows, lo, hi):
    total = rows + 2 * HALO0
    return slice(lo, hi), slice(total - hi, total - lo)


def put_ends(target, rows, lo, hi, source):
    n = hi - lo
    for at, part in zip(ends(rows, lo, hi), (slice(0, n), slice(n, 2 * n))):
        for i in range(target.shape[0]):
            for t in (0, 1):
                target[i, t, at] = source[i, t, part]


def take_ends(source, rows, lo, hi, target):
    n = hi - lo
    for at, part in zip(ends(rows, lo, hi), (slice(0, n), slice(n, 2 * n))):
        for i in range(source.shape[0]):
            for t in (0, 1):
                target[i, t, part] = source[i, t, at]


def level0_inner_kernel(rows, main, own_a, own_b, keep_in, y0_in, y1_in, y2_in, diag_in, sources_in, *scratch):
    fields, keep, diag, y0, y1, y2 = scratch
    even_x = is_even("gx")
    for i in range(6):
        fields[i, 0, HALO0 : HALO0 + rows] = main[i]
        for a, b, value in halo_tiles(even_x, (own_a, own_b), i * rows, (i + 1) * rows):
            fields[i, 1, HALO0 + a : HALO0 + b] = value
    first = HALO0 + 1
    level0_setup(fields, keep, diag, y0, first, rows - 2)
    level0_power(keep, y0, y1, first + 1, rows - 4)
    level0_power(keep, y1, y2, first + 2, rows - 6)
    level0_down(keep, diag, y1, y2, sources_in, first + 3, rows - 8)
    for source, target, lost in ((keep, keep_in, 1), (y1, y1_in, 2), (y2, y2_in, 3)):
        for i in range(source.shape[0]):
            for t in (0, 1):
                target[i, t] = source[i, t, inner(rows, lost)]
    take_ends(y0, rows, HALO0 + 1, HALO0 + 3, y0_in)
    take_ends(diag, rows, HALO0 + 1, HALO0 + 4, diag_in)


def level0_outer_kernel(
    rows,
    main,
    y_first,
    y_second,
    own_a,
    own_b,
    corner_a,
    corner_b,
    keep_in,
    y0_in,
    y1_in,
    y2_in,
    diag_in,
    sources_in,
    keep_out,
    y1_out,
    y2_out,
    sources,
    edges,
    *scratch,
):
    fields, keep, diag, y0, y1, y2 = scratch
    even, even_x = is_even("gy"), is_even("gx")
    total = rows + 2 * HALO0
    near, skip = HALO0 + 2, HALO0 - SENT
    for i in range(6):
        strip = slice(i * SENT, (i + 1) * SENT)
        fields[i, 0, skip:HALO0] = prev_of(even, y_first, y_second, strip)
        fields[i, 0, HALO0:near] = main[i, 0:2]
        fields[i, 0, total - near : total - HALO0] = main[i, rows - 2 : rows]
        fields[i, 0, HALO0 + rows : total - skip] = next_of(even, y_first, y_second, strip)
        for packets, lo, n, at in (
            ((corner_a, corner_b), i * SENT, SENT, skip),
            ((own_a, own_b), i * rows, 2, HALO0),
            ((own_a, own_b), (i + 1) * rows - 2, 2, total - near),
            ((corner_a, corner_b), PACKET + i * SENT, SENT, HALO0 + rows),
        ):
            for a, b, value in halo_tiles(even_x, packets, lo, lo + n):
                fields[i, 1, at + a : at + b] = value
    for i in (0, 1):
        for t in (0, 1):
            for at in (0, total - 1):
                fields[i, t, at] = jnp.zeros((Z, X), jnp.float32)
    for at, part in zip(ends(rows, 5, 8), (slice(0, 3), slice(rows - 5, rows - 2))):
        for i in range(6):
            for t in (0, 1):
                keep[i, t, at] = keep_in[i, t, part]
    put_ends(diag, rows, 5, 8, diag_in)
    put_ends(y0, rows, 5, 7, y0_in)
    for target, source, lost in ((y1, y1_in, 2), (y2, y2_in, 3)):
        n = rows - 2 * lost
        for at, part in zip(ends(rows, HALO0 + lost, HALO0 + lost + 2), (slice(0, 2), slice(n - 2, n))):
            for i in (0, 1):
                for t in (0, 1):
                    target[i, t, at] = source[i, t, part]
    for r in (1, total - 5):
        level0_setup(fields, keep, diag, y0, r, 4)
    for r in (2, total - 6):
        level0_power(keep, y0, y1, r, 4)
    for r in (3, total - 7):
        level0_power(keep, y1, y2, r, 4)
    for r in (4, total - 8):
        level0_down(keep, diag, y1, y2, sources, r, 4)
    for q in range(4):
        for t in (0, 1):
            sources[q, t, 1 : OWN - 1] = sources_in[q, t, 1 : OWN - 1]
    take_ends(keep, rows, 1, 5, keep_out)
    take_ends(y1, rows, 4, 6, y1_out)
    take_ends(y2, rows, 4, 7, y2_out)
    for p, power in enumerate((y0, y1, y2)):
        for side, start in enumerate((HALO0, HALO0 + rows - EDGE)):
            edges[p, side] = pack_rows(power, start)


def pack_rows(x, start):
    lane = lane_of()
    halo = None
    for i in (0, 1):
        for j in range(EDGE):
            at = i * EDGE + j
            value = roll_x(x[i, 1, start + j : start + j + 1], 4 + 8 * at)
            halo = value if halo is None else jnp.where((lane >> 3) == at, value, halo)
    return jnp.concatenate([x[i, 0, start : start + EDGE] for i in (0, 1)] + [halo], axis=0)


def squeeze(halo):
    lane = lane_of()
    last = halo[OWN - 1 : OWN]
    ahead = (lane >= WIDE) & (lane < 2 * WIDE)
    parts = [jnp.where(ahead, roll_x(last, WIDE), halo[0:1]), jnp.where(ahead, roll_x(last, 2 * WIDE - X), halo[1:2])]
    return jnp.concatenate(parts + [halo[2 : OWN - 1]], axis=0)


def unsqueeze(tiles):
    last = jnp.where(lane_of() < X // 2, roll_x(tiles[0:1], -WIDE), roll_x(tiles[1:2], X - 2 * WIDE))
    return jnp.concatenate([tiles, last], axis=0)


def combine_kernel(sources, edges, spread, own, first, second, edge_first, edge_second, gain):
    write_gains(jnp.max(spread[...], axis=0)[0:1], gain)
    p0, p1, p2 = (gain[POWERS + i] for i in range(3))
    for t in (0, 1):
        value = sources[0, t] - p0 * sources[1, t] + p1 * sources[2, t] - p2 * sources[3, t]
        own[t] = value
        for ref in (first, second):
            if t == 0:
                ref[0:OWN] = value
            else:
                ref[OWN:] = squeeze(value)
    even = is_even("gy")
    top, bottom = (p0 * edges[0, side] - p1 * edges[1, side] + p2 * edges[2, side] for side in (0, 1))
    edge_first[...] = jnp.where(even, top, bottom)
    edge_second[...] = jnp.where(even, bottom, top)


def coarse1_kernel(
    rows, coarse, y_first, y_second, own_a, own_b, corner_a, corner_b, gain, keep_in, y1_in, y2_in, keep_out, y1_out, y2_out,
    coef, keep0, x0, fields
):
    even, even_x = is_even("gy"), is_even("gx")
    own_x, corner_x = (own_a, own_b), (corner_a, corner_b)
    for p in (0, 1):
        to = p * GROUPS1
        strip = slice(FIELDS1 + p * OWN, FIELDS1 + (p + 1) * OWN)
        fields[0, to : to + OWN] = prev_of(even, y_first, y_second, strip)
        fields[0, to + OWN : to + 2 * OWN] = coarse[p * OWN : (p + 1) * OWN]
        fields[0, to + 2 * OWN : to + 3 * OWN] = next_of(even, y_first, y_second, strip)
        for part, (packets, lo) in enumerate(
            ((corner_x, FIELDS1), (own_x, 6 * rows), (corner_x, PACKET + FIELDS1))
        ):
            lo += p * OWN
            for a, b, value in halo_tiles(even_x, packets, lo, lo + OWN):
                fields[1, to + part * OWN + a : to + part * OWN + b] = value
    for t in (0, 1):
        for i, value in enumerate(packed_jacobian(fields[t, 0:GROUPS1], fields[t, GROUPS1 : 2 * GROUPS1], 1)):
            coef[i, t, 1 : SIZE1 - 1] = value

    def whole(inside, outside):
        n = outside.shape[0] // 2
        return jnp.concatenate([outside[0:n], inside, outside[n:]], axis=0)

    for i in range(6):
        for t in (0, 1):
            keep0[i, t, 1 : rows + 2 * HALO0 - 1] = whole(keep_in[i, t], keep_out[i, t])
    p0, p1, p2 = (gain[POWERS + i] for i in range(3))
    for i in (0, 1):
        for t in (0, 1):
            y0 = keep0[2 + i, t, HALO0 : HALO0 + rows] * keep0[4 + i, t, HALO0 : HALO0 + rows]
            y1, y2 = (whole(a[i, t], b[i, t]) for a, b in ((y1_in, y1_out), (y2_in, y2_out)))
            x0[i, t] = p0 * y0 - p1 * y1 + p2 * y2


def fields2_kernel(rows, coarse, y_first, y_second, own_a, own_b, corner_a, corner_b, out):
    even, even_x = is_even("gy"), is_even("gx")
    own_x, corner_x = (own_a, own_b), (corner_a, corner_b)
    near = slice(FIELDS2, FIELDS2 + 1)
    out[0, 0:1] = prev_of(even, y_first, y_second, near)
    out[0, 1:2] = coarse[2 * OWN : 2 * OWN + 1]
    out[0, 2:3] = next_of(even, y_first, y_second, near)
    for q, (packets, lo) in enumerate(
        ((corner_x, FIELDS2), (own_x, 6 * rows + 2 * OWN), (corner_x, PACKET + FIELDS2))
    ):
        out[1, q : q + 1] = halo_tiles(even_x, packets, lo, lo + 1)[0][2]


def level1_kernel(
    own, first, second, edge_a, edge_b, fields2, coef1, gain, packet, to_first, to_second, to_far, keep, y1, d1
):
    b1, x1 = keep.at[0], keep.at[1]
    even = is_even("gy")
    for t in (0, 1):
        b1[t, 1 + OWN : 1 + 2 * OWN] = own[t]
        for at, take in ((1, prev_of), (1 + 2 * OWN, next_of)):
            if t == 0:
                b1[t, at : at + OWN] = take(even, first, second, slice(0, OWN))
            else:
                b1[t, at : at + OWN] = unsqueeze(take(even, first, second, slice(OWN, 2 * OWN - 1)))
    g0, g1, g2 = (gain[3 + i] for i in range(3))
    n = GROUPS1
    packed_first(coef1, 0, b1, x1, d1, 1, n, g0)
    packed_step(1, coef1, 0, b1, x1, y1, d1, 2, n - 2, CARRY1, g1)
    packed_step(1, coef1, 0, b1, y1, x1, d1, 2, n - 2, CARRY2, g2)
    here = pl.ds(1 + OWN, OWN)
    values = []
    for t, (c, other, spread) in enumerate(packed_terms(x1, 1 + OWN, OWN, 1)):
        res = b1[t, here] - coef1[2, t, here] * c + coef1[1, t, here] * other + spread
        values.append(restrict_12([res[j : j + 1] for j in range(OWN)]))
        to_far[1 + t : 2 + t] = fields2[t, 1:2]
    value = jnp.where((sub_of() & 2) == 0, values[0], values[1])
    for ref in (packet, to_first, to_second, to_far):
        ref[0:1] = value
    to_first[1:] = edge_a[...]
    to_second[1:] = edge_b[...]


def rest_kernel(
    own2, near_a, near_b, far_a, far_b, gain, coef1, fields2, keep0, iterate, keep1, out, coef2, d1, b2, x2, y2, d2, xu, yu, x0, y0, d0
):
    rows = out.shape[0] // (2 * Z)
    even = (sub_of() & 1) == 0
    b1, x1 = keep1.at[0], keep1.at[1]

    even_y, low = is_even("gy"), lax.rem(lax.axis_index("gy"), 4) < 2
    at = slice(0, 1)
    parts = [
        next_of(low, far_a, far_b, at),
        prev_of(even_y, near_a, near_b, at),
        own2[at],
        next_of(even_y, near_a, near_b, at),
        prev_of(low, far_a, far_b, at),
    ]
    for t, values in enumerate(split_fields2(jnp.concatenate(parts, axis=0))):
        b2[t, 1 : SIZE2 - 1] = values
        at = slice(1 + t, 2 + t)
        parts = [next_of(low, far_a, far_b, at), fields2[t], prev_of(low, far_a, far_b, at)]
        inverse, other, _ = packed_jacobian(*split_fields2(jnp.concatenate(parts, axis=0)), 2)
        coef2[0, t, 1 : SIZE2 - 1] = inverse
        coef2[1, t, 1 : SIZE2 - 1] = other

    n = HI2 - LO2
    g0, g1, g2 = (gain[6 + i] for i in range(3))
    packed_first(coef2, 0, b2, x2, d2, 1, n, g0)
    packed_step(2, coef2, 0, b2, x2, y2, d2, 1, n, CARRY1, g1)
    packed_step(2, coef2, 0, b2, y2, x2, d2, 1, n, CARRY2, g2)
    packed_step(2, coef2, 0, b2, x2, y2, d2, 1, n, None, g0)
    packed_step(2, coef2, 0, b2, y2, x2, d2, 2, n - 2, CARRY1, g1)
    packed_step(2, coef2, 0, b2, x2, y2, d2, 2, n - 2, CARRY2, g2)

    g0, g1, g2 = (gain[3 + i] for i in range(3))
    shift = LO_UP - LO1
    for t in (0, 1):
        for g in range(LO_UP, HI_UP):
            p = g % 4
            value = y2[t, g // 4 - LO2 + 1 : g // 4 - LO2 + 2]
            value = spread_x(spread_x(value, 1, p & 1), 2, p & 2)
            at = g - LO_UP + 1
            xu[t, at : at + 1] = x1[t, at + shift : at + shift + 1] + value
    n = HI_UP - LO_UP
    packed_step(1, coef1, shift, b1, xu, yu, d1, 2, n - 2, None, g0)
    packed_step(1, coef1, shift, b1, yu, xu, d1, 2, n - 2, CARRY1, g1)
    packed_step(1, coef1, shift, b1, xu, yu, d1, 3, n - 4, CARRY2, g2)

    g0, g1, g2 = (gain[i] for i in range(3))
    for i in (0, 1):
        for at, take in ((HALO0 - EDGE, prev_of), (HALO0 + rows, next_of)):
            whole = take(even_y, near_a, near_b, slice(1, 1 + EDGE_TILES))
            x0[i, 0, at : at + EDGE] = whole[i * EDGE : (i + 1) * EDGE]
            for j in range(EDGE):
                x0[i, 1, at + j : at + j + 1] = roll_x(whole[2 * EDGE :], -(4 + 8 * (i * EDGE + j)))
        for t in (0, 1):
            x0[i, t, HALO0 : HALO0 + rows] = iterate[i, t]
    for t in (0, 1):
        for row in range(-2, rows // 2 + 2):
            at = row // 2 - LO_UP + 1
            value = spread_x(yu[t, at : at + 1], 1, row & 1)
            for i, fine in enumerate((jnp.where(even, value, roll_z(value, 1)), jnp.where(even, roll_z(value, -1), value))):
                for y in (2 * row, 2 * row + 1):
                    if -EDGE <= y < rows + EDGE:
                        x0[i, t, y + HALO0 : y + HALO0 + 1] = x0[i, t, y + HALO0 : y + HALO0 + 1] + fine
    total = rows + 2 * HALO0
    for r, n in chunks(2, total - 2):
        cheb_step(0, keep0, x0, y0, d0, r, n, None, g0)
    for r, n in chunks(3, total - 3):
        cheb_step(0, keep0, y0, x0, d0, r, n, CARRY1, g1)
    for r, n in chunks(4, total - 4):
        last = cheb_step(0, keep0, x0, None, d0, r, n, CARRY2, g2, (0,))[0]
        for i in (0, 1):
            for j in range(n):
                out[pl.ds(i * Z * rows + r - HALO0 + j, Z, stride=rows), :] = last[i][j]


def call(kernel, out_shapes, scratch, *args, space=pltpu.VMEM, outs=None):
    out = [jax.ShapeDtypeStruct(shape, jnp.float32) for shape in out_shapes]
    return pl.pallas_call(
        kernel,
        out_shape=out,
        in_specs=[pl.BlockSpec(memory_space=space)] * len(args),
        out_specs=[pl.BlockSpec(memory_space=m) for m in outs or [pltpu.VMEM] * len(out)],
        scratch_shapes=[pltpu.VMEM(s, jnp.float32) if isinstance(s, tuple) else s for s in scratch],
        compiler_params=pltpu.CompilerParams(vmem_limit_bytes=24 * 2**20),
    )(*args)


def swap(value, axis, step):
    count = lax.axis_size(axis)
    assert count % 2 == 0
    pairs = [(i, (i + step) % count) for i in range(0, count, 2)]
    return lax.ppermute(value, axis, pairs + [(j, i) for i, j in pairs])


def swap_far(value, axis, step):
    count = lax.axis_size(axis)
    assert count % 4 == 0
    pairs = [(i + j, (i + j + 2 * step) % count) for i in range(0, count, 4) for j in (0, 1)]
    return lax.ppermute(value, axis, pairs + [(j, i) for i, j in pairs])


def exchange(first, second, axis):
    return swap(first, axis, -1), swap(second, axis, 1)


def body(state, previous, feed, kill):
    _, depth, rows, cols = state.shape
    assert depth == Z and cols == X and rows == 4 * OWN
    across, count = lax.axis_size("gx"), lax.axis_size("gy")
    total0 = rows + 2 * HALO0
    state = state.reshape(2 * Z * rows, X)
    previous = previous.reshape(2 * Z * rows, X)
    feed = feed.reshape(Z * rows, X)
    kill = kill.reshape(Z * rows, X)
    inputs = (state, previous, feed, kill)

    strip = (PACKET, Z, X)
    first, second, coarse, *inputs = call(
        functools.partial(first_kernel, rows),
        [strip, strip, (2 * OWN + 1, Z, X), *(a.shape for a in inputs)],
        [pltpu.SemaphoreType.DMA((4,))],
        *(pltpu.with_memory_space_constraint(a, pltpu.HBM) for a in inputs),
        space=pltpu.HBM,
    )
    y_packets = exchange(first, second, "gy")

    tiles = tiles_for(6 * rows + 2 * OWN + 1)
    spread_shape = (across * count, Z // 2, X)
    first, second, spread, main = call(
        functools.partial(pack_own_kernel, rows),
        [(tiles, Z, X), (tiles, Z, X), spread_shape, (6, rows, Z, X)],
        [(PER * tiles, Z, X), spread_shape, pltpu.SemaphoreType.DMA],
        *inputs,
        coarse,
        outs=[pltpu.VMEM, pltpu.VMEM, pltpu.HBM, pltpu.VMEM],
    )
    own_x = exchange(first, second, "gx")
    spread = lax.all_to_all(spread, ("gx", "gy"), 0, 0, tiled=True)
    tiles = tiles_for(2 * PACKET)
    corner_x = exchange(
        *call(pack_corner_kernel, [(tiles, Z, X), (tiles, Z, X)], [(PER * tiles, Z, X)], *y_packets), "gx"
    )

    strip, edge = (2 * OWN - 1, Z, X), (EDGE_TILES, Z, X)
    pair0 = (2, 2, total0, Z, X)
    work = [(6, 2, total0, Z, X), (6, 2, total0, Z, X), pair0, pair0, pair0, pair0]
    four = (4, 2, OWN, Z, X)
    inside = call(
        functools.partial(level0_inner_kernel, rows),
        [
            (6, 2, rows - 2, Z, X),
            (2, 2, 4, Z, X),
            (2, 2, rows - 4, Z, X),
            (2, 2, rows - 6, Z, X),
            (2, 2, 6, Z, X),
            four,
        ],
        work,
        main,
        *own_x,
    )
    keep_in, _, y1_in, y2_in, _, _ = inside
    keep_out, y1_out, y2_out, sources, edges = call(
        functools.partial(level0_outer_kernel, rows),
        [(6, 2, 8, Z, X), (2, 2, 4, Z, X), (2, 2, 6, Z, X), four, (3, 2, *edge)],
        work,
        main,
        *y_packets,
        *own_x,
        *corner_x,
        *inside,
    )
    own, first, second, edge_a, edge_b, gain = call(
        combine_kernel,
        [(2, OWN, Z, X), strip, strip, edge, edge, (POWERS + 3, Z, X)],
        [],
        sources,
        edges,
        spread,
    )
    coef1, keep0, iterate = call(
        functools.partial(coarse1_kernel, rows),
        [(3, 2, SIZE1, Z, X), (6, 2, total0, Z, X), (2, 2, rows, Z, X)],
        [(2, 2 * GROUPS1, Z, X)],
        coarse,
        *y_packets,
        *own_x,
        *corner_x,
        gain,
        keep_in,
        y1_in,
        y2_in,
        keep_out,
        y1_out,
        y2_out,
    )
    (fields2,) = call(
        functools.partial(fields2_kernel, rows), [(2, 3, Z, X)], [], coarse, *y_packets, *own_x, *corner_x
    )
    b_packets = exchange(first, second, "gy")

    one, two, up = (2, SIZE1, Z, X), (2, SIZE2, Z, X), (2, SIZE_UP, Z, X)
    near = (1 + EDGE_TILES, Z, X)
    packet, first, second, to_far, keep1 = call(
        level1_kernel,
        [(1, Z, X), near, near, (3, Z, X), (2, *one)],
        [one, one],
        own,
        *b_packets,
        edge_a,
        edge_b,
        fields2,
        coef1,
        gain,
    )
    far = (swap_far(to_far, "gy", 1), swap_far(to_far, "gy", -1))
    near = exchange(first, second, "gy")

    (out,) = call(
        rest_kernel,
        [(2 * Z * rows, X)],
        [(2, *two), one, two, two, two, two, up, up, pair0, pair0, pair0],
        packet,
        *near,
        *far,
        gain,
        coef1,
        fields2,
        keep0,
        iterate,
        keep1,
    )
    return out.reshape(2, Z, rows, X)


def solution(mesh):
    placed = (
        P(None, None, "gy", "gx"),
        P(None, None, "gy", "gx"),
        P(None, "gy", "gx"),
        P(None, "gy", "gx"),
    )
    return jax.shard_map(
        body, mesh=mesh, in_specs=placed, out_specs=P(None, None, "gy", "gx"), check_vma=False
    )
```

```python
import functools

import jax
import jax.numpy as jnp
from jax import lax
from jax.experimental import pallas as pl
from jax.experimental.pallas import tpu as pltpu
from jax.sharding import PartitionSpec as P

DIFF = (40.0, 20.0)
INV_STEP = 2.0
LOWER = 0.25

_CENTRE = (1.0 + LOWER) / 2.0
_HALF = (1.0 - LOWER) / 2.0
_SIGMA = _CENTRE / _HALF
_RHO0 = 1.0 / _SIGMA
_RHO1 = 1.0 / (2.0 * _SIGMA - _RHO0)
_RHO2 = 1.0 / (2.0 * _SIGMA - _RHO1)

Z = 8
X = 128
HALO0 = 4
SENT = 3
FIELDS1 = 6 * SENT
FIELDS2 = FIELDS1 + 8
PACKET = FIELDS2 + 1
WIDE = 42
PER = X // WIDE
EDGE = 3

LO1, HI1 = -4, 8
LO2, HI2 = -2, 3
LO_UP, HI_UP = -3, 7
SIZE1, SIZE2, SIZE_UP = HI1 - LO1 + 2, HI2 - LO2 + 2, HI_UP - LO_UP + 2
OWN = 4


def lane_of():
    return lax.broadcasted_iota(jnp.int32, (1, Z, X), 2)


def sub_of():
    return lax.broadcasted_iota(jnp.int32, (1, Z, X), 1)


def roll_x(tile, shift):
    shift = shift % X
    return pltpu.roll(tile, shift, 2) if shift else tile


def roll_z(tile, shift):
    shift = shift % Z
    return pltpu.roll(tile, shift, 1) if shift else tile


def chunks(lo, hi, step=4):
    return [(r, min(step, hi - r)) for r in range(lo, hi, step)]


def neighbour_sums(read, r, n, k, tiles=(0, 1)):
    lane = lane_of()
    low, high = lane < k, lane >= X - k
    centre = [read(t, r, n) for t in (0, 1)]
    right = [roll_x(c, k) for c in centre]
    left = [roll_x(c, -k) for c in centre]
    sums = []
    for t in tiles:
        c = centre[t]
        along_x = jnp.where(low, right[1 - t], right[t]) + jnp.where(high, left[1 - t], left[t])
        along_y = read(t, r - 1, n) + read(t, r + 1, n)
        along_z = 2.0 * roll_z(c, k) if 2 * k == Z else roll_z(c, k) + roll_z(c, -k)
        sums.append(along_x + along_y + along_z)
    return centre, sums


def jacobian(u, v, f, k, level):
    scale = 0.25**level
    product = u * v
    squared = v * v
    first = INV_STEP + squared + f + 6.0 * DIFF[0] * scale
    second = INV_STEP + f + k - 2.0 * product + 6.0 * DIFF[1] * scale
    return 2.0 * product, squared, 1.0 / first, 1.0 / second, first, second


def cheb_step(level, keep, source, target, d, r, n, carry, gain, tiles=(0, 1)):
    scale = 0.25**level
    k = 1 << level
    u, nb_u = neighbour_sums(lambda t, a, m: source[0, t, pl.ds(a, m)], r, n, k, tiles)
    v, nb_v = neighbour_sums(lambda t, a, m: source[1, t, pl.ds(a, m)], r, n, k, tiles)
    rows = pl.ds(r, n)
    out = []
    for t in tiles:
        cross, squared, inv_u, inv_v = (keep[i, t, rows] for i in range(4))
        res_u = inv_u * (keep[4, t, rows] - cross * v[t] + DIFF[0] * scale * nb_u[t]) - u[t]
        res_v = inv_v * (keep[5, t, rows] + squared * u[t] + DIFF[1] * scale * nb_v[t]) - v[t]
        du, dv = gain * res_u, gain * res_v
        if carry is not None:
            du = du + carry * d[0, t, rows]
            dv = dv + carry * d[1, t, rows]
        if target is not None:
            d[0, t, rows] = du
            d[1, t, rows] = dv
            target[0, t, rows] = u[t] + du
            target[1, t, rows] = v[t] + dv
        out.append((u[t] + du, v[t] + dv))
    return out


def next_power(keep, source, r, n):
    u, nb_u = neighbour_sums(lambda t, a, m: source[0, t, pl.ds(a, m)], r, n, 1)
    v, nb_v = neighbour_sums(lambda t, a, m: source[1, t, pl.ds(a, m)], r, n, 1)
    rows = pl.ds(r, n)
    first, second = [], []
    for t in (0, 1):
        cross, squared, inv_u, inv_v = (keep[i, t, rows] for i in range(4))
        first.append(u[t] + inv_u * (cross * v[t] - DIFF[0] * nb_u[t]))
        second.append(v[t] - inv_v * (squared * u[t] + DIFF[1] * nb_v[t]))
    return first, second


CARRY1 = _RHO1 * _RHO0
CARRY2 = _RHO2 * _RHO1


POWERS = 9


def write_gains(spread, out):
    lane = lax.broadcasted_iota(jnp.int32, (1, X), 1)
    for level in range(3):
        top = jnp.max(jnp.where(lane == level, spread, 0.0), axis=1, keepdims=True)
        tau = 1.0 / (1.0 + jnp.broadcast_to(top, (Z, X)))
        for i, factor in enumerate((1.0 / _CENTRE, 2.0 * _RHO1 / _HALF, 2.0 * _RHO2 / _HALF)):
            out[3 * level + i] = factor * tau
    g0, g1, g2 = (out[i] for i in range(3))
    first, second = g0 + CARRY1 * g0 + g1, g1 * g0
    out[POWERS] = first + CARRY2 * (CARRY1 * g0 + g1) + g2
    out[POWERS + 1] = second + CARRY2 * second + g2 * first
    out[POWERS + 2] = g2 * second


def pair_rows(value):
    n = value.shape[0] // 2
    pairs = value.reshape(n, 2, Z, X)
    return pairs[:, 0] + pairs[:, 1]


def restrict_01(first, second):
    lane, sub = lane_of(), sub_of()
    across = []
    for value in (first, second):
        a, b = value[0:1], value[1:2]
        across.append(jnp.where((lane & 1) == 0, a + roll_x(a, -1), b + roll_x(b, 1)))
    a, b = across
    return 0.125 * jnp.where((sub & 1) == 0, a + roll_z(a, -1), b + roll_z(b, 1))


def restrict_12(groups):
    lane, sub = lane_of(), sub_of()
    out = None
    for p, value in enumerate(groups):
        value = value + roll_x(value, 1 if p & 1 else -1)
        value = value + roll_x(value, 2 if p & 2 else -2)
        out = value if out is None else jnp.where((lane & 3) == p, value, out)
    return 0.125 * (out + jnp.where((sub & 2) == 0, roll_z(out, -2), roll_z(out, 2)))


def spread_x(tile, k, phase):
    return jnp.where((lane_of() & k) == phase, tile, roll_x(tile, -k if phase else k))


def packed_jacobian(uv, fk, level):
    scale = 0.25**level
    even = (sub_of() & 1) == 0
    u, v = jnp.where(even, uv, roll_z(uv, 1)), jnp.where(even, roll_z(uv, -1), uv)
    f, k = jnp.where(even, fk, roll_z(fk, 1)), jnp.where(even, roll_z(fk, -1), fk)
    product, squared = u * v, v * v
    diag = jnp.where(
        even,
        INV_STEP + squared + f + 6.0 * DIFF[0] * scale,
        INV_STEP + f + k - 2.0 * product + 6.0 * DIFF[1] * scale,
    )
    return 1.0 / diag, jnp.where(even, -2.0 * product, squared), diag


def packed_spread(uv, fk, level):
    scale = 0.25**level
    even = (sub_of() & 1) == 0
    inverse, other, _ = packed_jacobian(uv, fk, level)
    return jnp.where(even, 6.0 * DIFF[0] * scale - other, 6.0 * DIFF[1] * scale + other) * inverse


def packed_terms(source, g, n, level):
    k = 1 << level
    lane, sub = lane_of(), sub_of()
    even = (sub & 1) == 0
    first, last = (lane & (k - 1)) == 0, (lane & (k - 1)) == k - 1
    low, high = lane < k, lane >= X - k
    diff = jnp.where(even, DIFF[0] * 0.25**level, DIFF[1] * 0.25**level)
    wide = [source[t, pl.ds(g - 1, n + 2)] for t in (0, 1)]
    centre = [w[1 : n + 1] for w in wide]
    right = [roll_x(c, k) for c in centre]
    left = [roll_x(c, -k) for c in centre]
    out = []
    for t in (0, 1):
        c, w = centre[t], wide[t]
        total = jnp.where(low, right[1 - t], right[t]) + jnp.where(high, left[1 - t], left[t])
        if k == 2:
            ahead, back = roll_x(w, 1), roll_x(w, -1)
            total = total + jnp.where(first, back[0:n], ahead[1 : n + 1])
            total = total + jnp.where(last, ahead[2 : n + 2], back[1 : n + 1])
            total = total + roll_z(c, 2) + roll_z(c, -2)
        else:
            total = total + jnp.where(first, roll_x(w[0:n], -(k - 1)), roll_x(c, 1))
            total = total + jnp.where(last, roll_x(w[2 : n + 2], k - 1), roll_x(c, -1))
            total = total + 2.0 * roll_z(c, 4)
        other = jnp.where(even, roll_z(c, -1), roll_z(c, 1))
        out.append((c, other, diff * total))
    return out


def packed_first(coef, shift, b, target, d, g, n, gain):
    for t in (0, 1):
        value = gain * coef[0, t, pl.ds(g + shift, n)] * b[t, pl.ds(g + shift, n)]
        d[t, pl.ds(g, n)] = value
        target[t, pl.ds(g, n)] = value


def packed_step(level, coef, shift, b, source, target, d, g, n, carry, gain):
    for t, (c, other, spread) in enumerate(packed_terms(source, g, n, level)):
        at = pl.ds(g + shift, n)
        res = coef[0, t, at] * (b[t, at] + coef[1, t, at] * other + spread) - c
        delta = gain * res
        if carry is not None:
            delta = delta + carry * d[t, pl.ds(g, n)]
        d[t, pl.ds(g, n)] = delta
        target[t, pl.ds(g, n)] = c + delta


def plane(ref, f, y, rows):
    return ref[pl.ds(f * Z * rows + y, Z, stride=rows), :]


def is_even(axis):
    return lax.rem(lax.axis_index(axis), 2) == 0


def prev_of(even, first, second, at):
    return jnp.where(even, first[at], second[at])


def next_of(even, first, second, at):
    return jnp.where(even, second[at], first[at])


SOURCES = ((0, 0), (0, 1), (1, 0), (1, 1), (2, 0), (3, 0))


def first_kernel(rows, state, previous, feed, kill, first, second, coarse, *rest):
    held, sems = rest[:4], rest[4]
    copies = [
        pltpu.make_async_copy(ref, to, sems.at[i]) for i, (ref, to) in enumerate(zip((state, previous, feed, kill), held))
    ]
    for copy in copies:
        copy.start()
    for copy in copies:
        copy.wait()
    even = is_even("gy")
    values = []
    for i, (j, f) in enumerate(SOURCES):
        wanted = range(rows) if i not in (2, 3) else [*range(SENT), *range(rows - SENT, rows)]
        values.append({y: plane(held[j], f, y, rows)[None] for y in wanted})
    for i in (2, 3):
        weight = DIFF[i - 2] / INV_STEP
        values[i][SENT - 1] = values[i][SENT - 1] + weight * values[i - 2][SENT]
        values[i][rows - SENT] = values[i][rows - SENT] + weight * values[i - 2][rows - SENT - 1]
    for i in range(6):
        for y in range(SENT):
            top, bottom = values[i][y], values[i][rows - SENT + y]
            at = slice(i * SENT + y, i * SENT + y + 1)
            first[at] = jnp.where(even, top, bottom)
            second[at] = jnp.where(even, bottom, top)
    pairs = []
    for p, (i, j) in enumerate(((0, 1), (4, 5))):
        parts = []
        for g in range(OWN):
            sums = [
                jnp.concatenate([value[4 * g + 2 * q] + value[4 * g + 2 * q + 1] for q in (0, 1)], axis=0)
                for value in (values[i], values[j])
            ]
            parts.append(restrict_01(*sums))
        pairs.append(jnp.concatenate(parts, axis=0))
        coarse[p * OWN : (p + 1) * OWN] = pairs[p]
        for ref in (first, second):
            ref[FIELDS1 + p * OWN : FIELDS1 + (p + 1) * OWN] = pairs[p]
    uv, fk = (restrict_12([pair[j : j + 1] for j in range(OWN)]) for pair in pairs)
    both = jnp.where((sub_of() & 2) == 0, uv, fk)
    coarse[2 * OWN : 2 * OWN + 1] = both
    for ref in (first, second):
        ref[FIELDS2 : FIELDS2 + 1] = both


def split_fields2(both):
    low = (sub_of() & 2) == 0
    return jnp.where(low, both, roll_z(both, 2)), jnp.where(low, roll_z(both, -2), both)


def write_spread(main, coarse, out):
    lane = lax.broadcasted_iota(jnp.int32, (1, X), 1)
    u, v, f, k = (main[i] for i in (0, 1, 4, 5))
    cross, squared, inv_u, inv_v, _, _ = jacobian(u, v, f, k, 0)
    tops = [jnp.max(jnp.maximum((6.0 * DIFF[0] + cross) * inv_u, (6.0 * DIFF[1] + squared) * inv_v), axis=0)]
    tops.append(jnp.max(packed_spread(coarse[0:OWN], coarse[OWN : 2 * OWN], 1), axis=0))
    tops.append(packed_spread(*split_fields2(coarse[2 * OWN : 2 * OWN + 1]), 2)[0])
    result = jnp.zeros((1, X), jnp.float32)
    for level, top in enumerate(tops):
        top = jnp.max(jnp.max(top, axis=0, keepdims=True), axis=1, keepdims=True)
        result = jnp.where(lane == level, jnp.broadcast_to(top, (1, X)), result)
    out[...] = jnp.broadcast_to(result[None], out.shape)


GROUPS1 = HI1 - LO1
GROUPS2 = HI2 - LO2


def tiles_for(entries):
    return -(-entries // PER)


def pack_edges(entries, even, first, second):
    lane = lane_of()
    share = first.shape[0]
    left, right = None, None
    for j in range(PER):
        part = entries[j * share : (j + 1) * share]
        a, b = roll_x(part, WIDE * j), roll_x(part, WIDE + WIDE * j)
        left = a if left is None else jnp.where(lane >= WIDE * j, a, left)
        right = b if right is None else jnp.where(lane >= WIDE * j, b, right)
    first[...] = jnp.where(even, left, right)
    second[...] = jnp.where(even, right, left)


def halo_tiles(even, packets, lo, hi):
    first, second = packets
    share = first.shape[0]
    lane = lane_of()
    out = []
    for j in range(PER):
        a, b = max(lo, j * share), min(hi, (j + 1) * share)
        if a < b:
            strip = slice(a - j * share, b - j * share)
            left, right = prev_of(even, first, second, strip), next_of(even, first, second, strip)
            value = jnp.where(lane < X // 2, roll_x(right, -WIDE * j), roll_x(left, X - WIDE - WIDE * j))
            out.append((a - lo, b - lo, value))
    return out


def pack_own_kernel(
    rows, state, previous, feed, kill, coarse, first, second, spread, main, held, copies, sem
):
    inputs = (state, previous, feed, kill)
    for i, (j, f) in enumerate(SOURCES):
        for y in range(rows):
            main[i, y] = plane(inputs[j], f, y, rows)
    write_spread(main, coarse, copies)
    copy = pltpu.make_async_copy(copies, spread, sem)
    copy.start()
    for i in range(6):
        held[i * rows : (i + 1) * rows] = main[i]
    held[6 * rows : 6 * rows + 2 * OWN + 1] = coarse[...]
    pack_edges(held, is_even("gx"), first, second)
    copy.wait()


def pack_corner_kernel(y_first, y_second, first, second, held):
    even = is_even("gy")
    every = slice(0, PACKET)
    held[0:PACKET] = prev_of(even, y_first, y_second, every)
    held[PACKET : 2 * PACKET] = next_of(even, y_first, y_second, every)
    pack_edges(held, is_even("gx"), first, second)


EDGE_TILES = 2 * EDGE + 1


def level0_setup(fields, keep, diag, power, r, n):
    at = pl.ds(r, n)
    u, nb_u = neighbour_sums(lambda t, a, m: fields[0, t, pl.ds(a, m)], r, n, 1)
    v, nb_v = neighbour_sums(lambda t, a, m: fields[1, t, pl.ds(a, m)], r, n, 1)
    for t in (0, 1):
        f, k = fields[4, t, at], fields[5, t, at]
        cross, squared, inv_u, inv_v, first, second = jacobian(u[t], v[t], f, k, 0)
        react = u[t] * squared
        b_u = DIFF[0] * (nb_u[t] - 6.0 * u[t]) - INV_STEP * (u[t] - fields[2, t, at]) - react + f * (1.0 - u[t])
        b_v = DIFF[1] * (nb_v[t] - 6.0 * v[t]) - INV_STEP * (v[t] - fields[3, t, at]) + react - (f + k) * v[t]
        for i, value in enumerate((cross, squared, inv_u, inv_v, b_u, b_v)):
            keep[i, t, at] = value
        for i, value in enumerate((first, second)):
            diag[i, t, at] = value
        for i, value in enumerate((inv_u * b_u, inv_v * b_v)):
            power[i, t, at] = value


def level0_power(keep, source, target, r, n):
    for i, values in enumerate(next_power(keep, source, r, n)):
        for t in (0, 1):
            target[i, t, pl.ds(r, n)] = values[t]


def level0_down(keep, diag, y1, y2, sources, r, n):
    at = pl.ds(r, n)
    last = next_power(keep, y2, r, n)
    for t in (0, 1):
        both = [diag[i, t, at] for i in (0, 1)]
        parts = [[keep[4 + i, t, at] for i in (0, 1)]]
        parts += [[both[i] * power[i, t, at] for i in (0, 1)] for power in (y1, y2)]
        parts.append([both[i] * last[i][t] for i in (0, 1)])
        for q, part in enumerate(parts):
            u, v = (pair_rows(value) for value in part)
            for j in range(n // 4):
                value = restrict_01(u[2 * j : 2 * j + 2], v[2 * j : 2 * j + 2])
                sources[q, t, pl.ds((r - HALO0) // 4 + j, 1)] = value


def inner(rows, lost):
    return slice(HALO0 + lost, HALO0 + rows - lost)


def ends(rows, lo, hi):
    total = rows + 2 * HALO0
    return slice(lo, hi), slice(total - hi, total - lo)


def put_ends(target, rows, lo, hi, source):
    n = hi - lo
    for at, part in zip(ends(rows, lo, hi), (slice(0, n), slice(n, 2 * n))):
        for i in range(target.shape[0]):
            for t in (0, 1):
                target[i, t, at] = source[i, t, part]


def take_ends(source, rows, lo, hi, target):
    n = hi - lo
    for at, part in zip(ends(rows, lo, hi), (slice(0, n), slice(n, 2 * n))):
        for i in range(source.shape[0]):
            for t in (0, 1):
                target[i, t, part] = source[i, t, at]


def level0_inner_kernel(rows, main, own_a, own_b, keep_in, y0_in, y1_in, y2_in, diag_in, sources_in, *scratch):
    fields, keep, diag, y0, y1, y2 = scratch
    even_x = is_even("gx")
    for i in range(6):
        fields[i, 0, HALO0 : HALO0 + rows] = main[i]
        for a, b, value in halo_tiles(even_x, (own_a, own_b), i * rows, (i + 1) * rows):
            fields[i, 1, HALO0 + a : HALO0 + b] = value
    first = HALO0 + 1
    level0_setup(fields, keep, diag, y0, first, rows - 2)
    level0_power(keep, y0, y1, first + 1, rows - 4)
    level0_power(keep, y1, y2, first + 2, rows - 6)
    level0_down(keep, diag, y1, y2, sources_in, first + 3, rows - 8)
    for source, target, lost in ((keep, keep_in, 1), (y1, y1_in, 2), (y2, y2_in, 3)):
        for i in range(source.shape[0]):
            for t in (0, 1):
                target[i, t] = source[i, t, inner(rows, lost)]
    take_ends(y0, rows, HALO0 + 1, HALO0 + 3, y0_in)
    take_ends(diag, rows, HALO0 + 1, HALO0 + 4, diag_in)


def level0_outer_kernel(
    rows,
    main,
    y_first,
    y_second,
    own_a,
    own_b,
    corner_a,
    corner_b,
    keep_in,
    y0_in,
    y1_in,
    y2_in,
    diag_in,
    sources_in,
    keep_out,
    y1_out,
    y2_out,
    sources,
    edges,
    *scratch,
):
    fields, keep, diag, y0, y1, y2 = scratch
    even, even_x = is_even("gy"), is_even("gx")
    total = rows + 2 * HALO0
    near, skip = HALO0 + 2, HALO0 - SENT
    for i in range(6):
        strip = slice(i * SENT, (i + 1) * SENT)
        fields[i, 0, skip:HALO0] = prev_of(even, y_first, y_second, strip)
        fields[i, 0, HALO0:near] = main[i, 0:2]
        fields[i, 0, total - near : total - HALO0] = main[i, rows - 2 : rows]
        fields[i, 0, HALO0 + rows : total - skip] = next_of(even, y_first, y_second, strip)
        for packets, lo, n, at in (
            ((corner_a, corner_b), i * SENT, SENT, skip),
            ((own_a, own_b), i * rows, 2, HALO0),
            ((own_a, own_b), (i + 1) * rows - 2, 2, total - near),
            ((corner_a, corner_b), PACKET + i * SENT, SENT, HALO0 + rows),
        ):
            for a, b, value in halo_tiles(even_x, packets, lo, lo + n):
                fields[i, 1, at + a : at + b] = value
    for i in (0, 1):
        for t in (0, 1):
            for at in (0, total - 1):
                fields[i, t, at] = jnp.zeros((Z, X), jnp.float32)
    for at, part in zip(ends(rows, 5, 8), (slice(0, 3), slice(rows - 5, rows - 2))):
        for i in range(6):
            for t in (0, 1):
                keep[i, t, at] = keep_in[i, t, part]
    put_ends(diag, rows, 5, 8, diag_in)
    put_ends(y0, rows, 5, 7, y0_in)
    for target, source, lost in ((y1, y1_in, 2), (y2, y2_in, 3)):
        n = rows - 2 * lost
        for at, part in zip(ends(rows, HALO0 + lost, HALO0 + lost + 2), (slice(0, 2), slice(n - 2, n))):
            for i in (0, 1):
                for t in (0, 1):
                    target[i, t, at] = source[i, t, part]
    for r in (1, total - 5):
        level0_setup(fields, keep, diag, y0, r, 4)
    for r in (2, total - 6):
        level0_power(keep, y0, y1, r, 4)
    for r in (3, total - 7):
        level0_power(keep, y1, y2, r, 4)
    for r in (4, total - 8):
        level0_down(keep, diag, y1, y2, sources, r, 4)
    for q in range(4):
        for t in (0, 1):
            sources[q, t, 1 : OWN - 1] = sources_in[q, t, 1 : OWN - 1]
    take_ends(keep, rows, 1, 5, keep_out)
    take_ends(y1, rows, 4, 6, y1_out)
    take_ends(y2, rows, 4, 7, y2_out)
    for p, power in enumerate((y0, y1, y2)):
        for side, start in enumerate((HALO0, HALO0 + rows - EDGE)):
            edges[p, side] = pack_rows(power, start)


def pack_rows(x, start):
    lane = lane_of()
    halo = None
    for i in (0, 1):
        for j in range(EDGE):
            at = i * EDGE + j
            value = roll_x(x[i, 1, start + j : start + j + 1], 4 + 8 * at)
            halo = value if halo is None else jnp.where((lane >> 3) == at, value, halo)
    return jnp.concatenate([x[i, 0, start : start + EDGE] for i in (0, 1)] + [halo], axis=0)


def squeeze(halo):
    lane = lane_of()
    last = halo[OWN - 1 : OWN]
    ahead = (lane >= WIDE) & (lane < 2 * WIDE)
    parts = [jnp.where(ahead, roll_x(last, WIDE), halo[0:1]), jnp.where(ahead, roll_x(last, 2 * WIDE - X), halo[1:2])]
    return jnp.concatenate(parts + [halo[2 : OWN - 1]], axis=0)


def unsqueeze(tiles):
    last = jnp.where(lane_of() < X // 2, roll_x(tiles[0:1], -WIDE), roll_x(tiles[1:2], X - 2 * WIDE))
    return jnp.concatenate([tiles, last], axis=0)


def combine_kernel(sources, edges, spread, own, first, second, edge_first, edge_second, gain):
    write_gains(jnp.max(spread[...], axis=0)[0:1], gain)
    p0, p1, p2 = (gain[POWERS + i] for i in range(3))
    for t in (0, 1):
        value = sources[0, t] - p0 * sources[1, t] + p1 * sources[2, t] - p2 * sources[3, t]
        own[t] = value
        for ref in (first, second):
            if t == 0:
                ref[0:OWN] = value
            else:
                ref[OWN:] = squeeze(value)
    even = is_even("gy")
    top, bottom = (p0 * edges[0, side] - p1 * edges[1, side] + p2 * edges[2, side] for side in (0, 1))
    edge_first[...] = jnp.where(even, top, bottom)
    edge_second[...] = jnp.where(even, bottom, top)


def coarse1_kernel(
    rows, coarse, y_first, y_second, own_a, own_b, corner_a, corner_b, gain, keep_in, y1_in, y2_in, keep_out, y1_out, y2_out,
    coef, keep0, x0, fields
):
    even, even_x = is_even("gy"), is_even("gx")
    own_x, corner_x = (own_a, own_b), (corner_a, corner_b)
    for p in (0, 1):
        to = p * GROUPS1
        strip = slice(FIELDS1 + p * OWN, FIELDS1 + (p + 1) * OWN)
        fields[0, to : to + OWN] = prev_of(even, y_first, y_second, strip)
        fields[0, to + OWN : to + 2 * OWN] = coarse[p * OWN : (p + 1) * OWN]
        fields[0, to + 2 * OWN : to + 3 * OWN] = next_of(even, y_first, y_second, strip)
        for part, (packets, lo) in enumerate(
            ((corner_x, FIELDS1), (own_x, 6 * rows), (corner_x, PACKET + FIELDS1))
        ):
            lo += p * OWN
            for a, b, value in halo_tiles(even_x, packets, lo, lo + OWN):
                fields[1, to + part * OWN + a : to + part * OWN + b] = value
    for t in (0, 1):
        for i, value in enumerate(packed_jacobian(fields[t, 0:GROUPS1], fields[t, GROUPS1 : 2 * GROUPS1], 1)):
            coef[i, t, 1 : SIZE1 - 1] = value

    def whole(inside, outside):
        n = outside.shape[0] // 2
        return jnp.concatenate([outside[0:n], inside, outside[n:]], axis=0)

    for i in range(6):
        for t in (0, 1):
            keep0[i, t, 1 : rows + 2 * HALO0 - 1] = whole(keep_in[i, t], keep_out[i, t])
    p0, p1, p2 = (gain[POWERS + i] for i in range(3))
    for i in (0, 1):
        for t in (0, 1):
            y0 = keep0[2 + i, t, HALO0 : HALO0 + rows] * keep0[4 + i, t, HALO0 : HALO0 + rows]
            y1, y2 = (whole(a[i, t], b[i, t]) for a, b in ((y1_in, y1_out), (y2_in, y2_out)))
            x0[i, t] = p0 * y0 - p1 * y1 + p2 * y2


def fields2_kernel(rows, coarse, y_first, y_second, own_a, own_b, corner_a, corner_b, out):
    even, even_x = is_even("gy"), is_even("gx")
    own_x, corner_x = (own_a, own_b), (corner_a, corner_b)
    near = slice(FIELDS2, FIELDS2 + 1)
    out[0, 0:1] = prev_of(even, y_first, y_second, near)
    out[0, 1:2] = coarse[2 * OWN : 2 * OWN + 1]
    out[0, 2:3] = next_of(even, y_first, y_second, near)
    for q, (packets, lo) in enumerate(
        ((corner_x, FIELDS2), (own_x, 6 * rows + 2 * OWN), (corner_x, PACKET + FIELDS2))
    ):
        out[1, q : q + 1] = halo_tiles(even_x, packets, lo, lo + 1)[0][2]


def level1_kernel(
    own, first, second, edge_a, edge_b, fields2, coef1, gain, packet, to_first, to_second, to_far, keep, y1, d1
):
    b1, x1 = keep.at[0], keep.at[1]
    even = is_even("gy")
    for t in (0, 1):
        b1[t, 1 + OWN : 1 + 2 * OWN] = own[t]
        for at, take in ((1, prev_of), (1 + 2 * OWN, next_of)):
            if t == 0:
                b1[t, at : at + OWN] = take(even, first, second, slice(0, OWN))
            else:
                b1[t, at : at + OWN] = unsqueeze(take(even, first, second, slice(OWN, 2 * OWN - 1)))
    g0, g1, g2 = (gain[3 + i] for i in range(3))
    n = GROUPS1
    packed_first(coef1, 0, b1, x1, d1, 1, n, g0)
    packed_step(1, coef1, 0, b1, x1, y1, d1, 2, n - 2, CARRY1, g1)
    packed_step(1, coef1, 0, b1, y1, x1, d1, 2, n - 2, CARRY2, g2)
    here = pl.ds(1 + OWN, OWN)
    values = []
    for t, (c, other, spread) in enumerate(packed_terms(x1, 1 + OWN, OWN, 1)):
        res = b1[t, here] - coef1[2, t, here] * c + coef1[1, t, here] * other + spread
        values.append(restrict_12([res[j : j + 1] for j in range(OWN)]))
        to_far[1 + t : 2 + t] = fields2[t, 1:2]
    value = jnp.where((sub_of() & 2) == 0, values[0], values[1])
    for ref in (packet, to_first, to_second, to_far):
        ref[0:1] = value
    to_first[1:] = edge_a[...]
    to_second[1:] = edge_b[...]


def rest_kernel(
    own2, near_a, near_b, far_a, far_b, gain, coef1, fields2, keep0, iterate, keep1, out, coef2, d1, b2, x2, y2, d2, xu, yu, x0, y0, d0
):
    rows = out.shape[0] // (2 * Z)
    even = (sub_of() & 1) == 0
    b1, x1 = keep1.at[0], keep1.at[1]

    even_y, low = is_even("gy"), lax.rem(lax.axis_index("gy"), 4) < 2
    at = slice(0, 1)
    parts = [
        next_of(low, far_a, far_b, at),
        prev_of(even_y, near_a, near_b, at),
        own2[at],
        next_of(even_y, near_a, near_b, at),
        prev_of(low, far_a, far_b, at),
    ]
    for t, values in enumerate(split_fields2(jnp.concatenate(parts, axis=0))):
        b2[t, 1 : SIZE2 - 1] = values
        at = slice(1 + t, 2 + t)
        parts = [next_of(low, far_a, far_b, at), fields2[t], prev_of(low, far_a, far_b, at)]
        inverse, other, _ = packed_jacobian(*split_fields2(jnp.concatenate(parts, axis=0)), 2)
        coef2[0, t, 1 : SIZE2 - 1] = inverse
        coef2[1, t, 1 : SIZE2 - 1] = other

    n = HI2 - LO2
    g0, g1, g2 = (gain[6 + i] for i in range(3))
    packed_first(coef2, 0, b2, x2, d2, 1, n, g0)
    packed_step(2, coef2, 0, b2, x2, y2, d2, 1, n, CARRY1, g1)
    packed_step(2, coef2, 0, b2, y2, x2, d2, 1, n, CARRY2, g2)
    packed_step(2, coef2, 0, b2, x2, y2, d2, 1, n, None, g0)
    packed_step(2, coef2, 0, b2, y2, x2, d2, 2, n - 2, CARRY1, g1)
    packed_step(2, coef2, 0, b2, x2, y2, d2, 2, n - 2, CARRY2, g2)

    g0, g1, g2 = (gain[3 + i] for i in range(3))
    shift = LO_UP - LO1
    for t in (0, 1):
        for g in range(LO_UP, HI_UP):
            p = g % 4
            value = y2[t, g // 4 - LO2 + 1 : g // 4 - LO2 + 2]
            value = spread_x(spread_x(value, 1, p & 1), 2, p & 2)
            at = g - LO_UP + 1
            xu[t, at : at + 1] = x1[t, at + shift : at + shift + 1] + value
    n = HI_UP - LO_UP
    packed_step(1, coef1, shift, b1, xu, yu, d1, 2, n - 2, None, g0)
    packed_step(1, coef1, shift, b1, yu, xu, d1, 2, n - 2, CARRY1, g1)
    packed_step(1, coef1, shift, b1, xu, yu, d1, 3, n - 4, CARRY2, g2)

    g0, g1, g2 = (gain[i] for i in range(3))
    for i in (0, 1):
        for at, take in ((HALO0 - EDGE, prev_of), (HALO0 + rows, next_of)):
            whole = take(even_y, near_a, near_b, slice(1, 1 + EDGE_TILES))
            x0[i, 0, at : at + EDGE] = whole[i * EDGE : (i + 1) * EDGE]
            for j in range(EDGE):
                x0[i, 1, at + j : at + j + 1] = roll_x(whole[2 * EDGE :], -(4 + 8 * (i * EDGE + j)))
        for t in (0, 1):
            x0[i, t, HALO0 : HALO0 + rows] = iterate[i, t]
    for t in (0, 1):
        for row in range(-2, rows // 2 + 2):
            at = row // 2 - LO_UP + 1
            value = spread_x(yu[t, at : at + 1], 1, row & 1)
            for i, fine in enumerate((jnp.where(even, value, roll_z(value, 1)), jnp.where(even, roll_z(value, -1), value))):
                for y in (2 * row, 2 * row + 1):
                    if -EDGE <= y < rows + EDGE:
                        x0[i, t, y + HALO0 : y + HALO0 + 1] = x0[i, t, y + HALO0 : y + HALO0 + 1] + fine
    total = rows + 2 * HALO0
    for r, n in chunks(2, total - 2):
        cheb_step(0, keep0, x0, y0, d0, r, n, None, g0)
    for r, n in chunks(3, total - 3):
        cheb_step(0, keep0, y0, x0, d0, r, n, CARRY1, g1)
    for r, n in chunks(4, total - 4):
        last = cheb_step(0, keep0, x0, None, d0, r, n, CARRY2, g2, (0,))[0]
        for i in (0, 1):
            for j in range(n):
                out[pl.ds(i * Z * rows + r - HALO0 + j, Z, stride=rows), :] = last[i][j]


def call(kernel, out_shapes, scratch, *args, space=pltpu.VMEM, outs=None):
    out = [jax.ShapeDtypeStruct(shape, jnp.float32) for shape in out_shapes]
    return pl.pallas_call(
        kernel,
        out_shape=out,
        in_specs=[pl.BlockSpec(memory_space=space)] * len(args),
        out_specs=[pl.BlockSpec(memory_space=m) for m in outs or [pltpu.VMEM] * len(out)],
        scratch_shapes=[pltpu.VMEM(s, jnp.float32) if isinstance(s, tuple) else s for s in scratch],
        compiler_params=pltpu.CompilerParams(vmem_limit_bytes=24 * 2**20),
    )(*args)


def swap(value, axis, step):
    count = lax.axis_size(axis)
    assert count % 2 == 0
    pairs = [(i, (i + step) % count) for i in range(0, count, 2)]
    return lax.ppermute(value, axis, pairs + [(j, i) for i, j in pairs])


def swap_far(value, axis, step):
    count = lax.axis_size(axis)
    assert count % 4 == 0
    pairs = [(i + j, (i + j + 2 * step) % count) for i in range(0, count, 4) for j in (0, 1)]
    return lax.ppermute(value, axis, pairs + [(j, i) for i, j in pairs])


def exchange(first, second, axis):
    other = swap(second, axis, 1)
    return swap(first, axis, -1), other


def body(state, previous, feed, kill):
    _, depth, rows, cols = state.shape
    assert depth == Z and cols == X and rows == 4 * OWN
    across, count = lax.axis_size("gx"), lax.axis_size("gy")
    total0 = rows + 2 * HALO0
    state = state.reshape(2 * Z * rows, X)
    previous = previous.reshape(2 * Z * rows, X)
    feed = feed.reshape(Z * rows, X)
    kill = kill.reshape(Z * rows, X)
    inputs = (state, previous, feed, kill)

    strip = (PACKET, Z, X)
    first, second, coarse, *inputs = call(
        functools.partial(first_kernel, rows),
        [strip, strip, (2 * OWN + 1, Z, X), *(a.shape for a in inputs)],
        [pltpu.SemaphoreType.DMA((4,))],
        *(pltpu.with_memory_space_constraint(a, pltpu.HBM) for a in inputs),
        space=pltpu.HBM,
    )
    y_packets = exchange(first, second, "gy")

    tiles = tiles_for(6 * rows + 2 * OWN + 1)
    spread_shape = (across * count, Z // 2, X)
    first, second, spread, main = call(
        functools.partial(pack_own_kernel, rows),
        [(tiles, Z, X), (tiles, Z, X), spread_shape, (6, rows, Z, X)],
        [(PER * tiles, Z, X), spread_shape, pltpu.SemaphoreType.DMA],
        *inputs,
        coarse,
        outs=[pltpu.VMEM, pltpu.VMEM, pltpu.HBM, pltpu.VMEM],
    )
    own_x = exchange(first, second, "gx")
    spread = lax.all_to_all(spread, ("gx", "gy"), 0, 0, tiled=True)
    tiles = tiles_for(2 * PACKET)
    corner_x = exchange(
        *call(pack_corner_kernel, [(tiles, Z, X), (tiles, Z, X)], [(PER * tiles, Z, X)], *y_packets), "gx"
    )

    strip, edge = (2 * OWN - 1, Z, X), (EDGE_TILES, Z, X)
    pair0 = (2, 2, total0, Z, X)
    work = [(6, 2, total0, Z, X), (6, 2, total0, Z, X), pair0, pair0, pair0, pair0]
    four = (4, 2, OWN, Z, X)
    inside = call(
        functools.partial(level0_inner_kernel, rows),
        [
            (6, 2, rows - 2, Z, X),
            (2, 2, 4, Z, X),
            (2, 2, rows - 4, Z, X),
            (2, 2, rows - 6, Z, X),
            (2, 2, 6, Z, X),
            four,
        ],
        work,
        main,
        *own_x,
    )
    keep_in, _, y1_in, y2_in, _, _ = inside
    keep_out, y1_out, y2_out, sources, edges = call(
        functools.partial(level0_outer_kernel, rows),
        [(6, 2, 8, Z, X), (2, 2, 4, Z, X), (2, 2, 6, Z, X), four, (3, 2, *edge)],
        work,
        main,
        *y_packets,
        *own_x,
        *corner_x,
        *inside,
    )
    own, first, second, edge_a, edge_b, gain = call(
        combine_kernel,
        [(2, OWN, Z, X), strip, strip, edge, edge, (POWERS + 3, Z, X)],
        [],
        sources,
        edges,
        spread,
    )
    coef1, keep0, iterate = call(
        functools.partial(coarse1_kernel, rows),
        [(3, 2, SIZE1, Z, X), (6, 2, total0, Z, X), (2, 2, rows, Z, X)],
        [(2, 2 * GROUPS1, Z, X)],
        coarse,
        *y_packets,
        *own_x,
        *corner_x,
        gain,
        keep_in,
        y1_in,
        y2_in,
        keep_out,
        y1_out,
        y2_out,
    )
    (fields2,) = call(
        functools.partial(fields2_kernel, rows), [(2, 3, Z, X)], [], coarse, *y_packets, *own_x, *corner_x
    )
    b_packets = exchange(first, second, "gy")

    one, two, up = (2, SIZE1, Z, X), (2, SIZE2, Z, X), (2, SIZE_UP, Z, X)
    near = (1 + EDGE_TILES, Z, X)
    packet, first, second, to_far, keep1 = call(
        level1_kernel,
        [(1, Z, X), near, near, (3, Z, X), (2, *one)],
        [one, one],
        own,
        *b_packets,
        edge_a,
        edge_b,
        fields2,
        coef1,
        gain,
    )
    far = (swap_far(to_far, "gy", 1), swap_far(to_far, "gy", -1))
    near = exchange(first, second, "gy")

    (out,) = call(
        rest_kernel,
        [(2 * Z * rows, X)],
        [(2, *two), one, two, two, two, two, up, up, pair0, pair0, pair0],
        packet,
        *near,
        *far,
        gain,
        coef1,
        fields2,
        keep0,
        iterate,
        keep1,
    )
    return out.reshape(2, Z, rows, X)


def solution(mesh):
    placed = (
        P(None, None, "gy", "gx"),
        P(None, None, "gy", "gx"),
        P(None, "gy", "gx"),
        P(None, "gy", "gx"),
    )
    return jax.shard_map(
        body, mesh=mesh, in_specs=placed, out_specs=P(None, None, "gy", "gx"), check_vma=False
    )
```

```python
import functools

import jax
import jax.numpy as jnp
from jax import lax
from jax.experimental import pallas as pl
from jax.experimental.pallas import tpu as pltpu
from jax.sharding import PartitionSpec as P

DIFF = (40.0, 20.0)
INV_STEP = 2.0
LOWER = 0.25

_CENTRE = (1.0 + LOWER) / 2.0
_HALF = (1.0 - LOWER) / 2.0
_SIGMA = _CENTRE / _HALF
_RHO0 = 1.0 / _SIGMA
_RHO1 = 1.0 / (2.0 * _SIGMA - _RHO0)
_RHO2 = 1.0 / (2.0 * _SIGMA - _RHO1)

Z = 8
X = 128
HALO0 = 4
SENT = 3
FIELDS1 = 6 * SENT
FIELDS2 = FIELDS1 + 8
PACKET = FIELDS2 + 1
WIDE = 42
PER = X // WIDE
EDGE = 3

LO1, HI1 = -4, 8
LO2, HI2 = -2, 3
LO_UP, HI_UP = -3, 7
SIZE1, SIZE2, SIZE_UP = HI1 - LO1 + 2, HI2 - LO2 + 2, HI_UP - LO_UP + 2
OWN = 4


def lane_of():
    return lax.broadcasted_iota(jnp.int32, (1, Z, X), 2)


def sub_of():
    return lax.broadcasted_iota(jnp.int32, (1, Z, X), 1)


def roll_x(tile, shift):
    shift = shift % X
    return pltpu.roll(tile, shift, 2) if shift else tile


def roll_z(tile, shift):
    shift = shift % Z
    return pltpu.roll(tile, shift, 1) if shift else tile


def chunks(lo, hi, step=4):
    return [(r, min(step, hi - r)) for r in range(lo, hi, step)]


def neighbour_sums(read, r, n, k, tiles=(0, 1)):
    lane = lane_of()
    low, high = lane < k, lane >= X - k
    centre = [read(t, r, n) for t in (0, 1)]
    right = [roll_x(c, k) for c in centre]
    left = [roll_x(c, -k) for c in centre]
    sums = []
    for t in tiles:
        c = centre[t]
        along_x = jnp.where(low, right[1 - t], right[t]) + jnp.where(high, left[1 - t], left[t])
        along_y = read(t, r - 1, n) + read(t, r + 1, n)
        along_z = 2.0 * roll_z(c, k) if 2 * k == Z else roll_z(c, k) + roll_z(c, -k)
        sums.append(along_x + along_y + along_z)
    return centre, sums


def jacobian(u, v, f, k, level):
    scale = 0.25**level
    product = u * v
    squared = v * v
    first = INV_STEP + squared + f + 6.0 * DIFF[0] * scale
    second = INV_STEP + f + k - 2.0 * product + 6.0 * DIFF[1] * scale
    return 2.0 * product, squared, 1.0 / first, 1.0 / second, first, second


def cheb_step(level, keep, source, target, d, r, n, carry, gain, tiles=(0, 1)):
    scale = 0.25**level
    k = 1 << level
    u, nb_u = neighbour_sums(lambda t, a, m: source[0, t, pl.ds(a, m)], r, n, k, tiles)
    v, nb_v = neighbour_sums(lambda t, a, m: source[1, t, pl.ds(a, m)], r, n, k, tiles)
    rows = pl.ds(r, n)
    out = []
    for t in tiles:
        cross, squared, inv_u, inv_v = (keep[i, t, rows] for i in range(4))
        res_u = inv_u * (keep[4, t, rows] - cross * v[t] + DIFF[0] * scale * nb_u[t]) - u[t]
        res_v = inv_v * (keep[5, t, rows] + squared * u[t] + DIFF[1] * scale * nb_v[t]) - v[t]
        du, dv = gain * res_u, gain * res_v
        if carry is not None:
            du = du + carry * d[0, t, rows]
            dv = dv + carry * d[1, t, rows]
        if target is not None:
            d[0, t, rows] = du
            d[1, t, rows] = dv
            target[0, t, rows] = u[t] + du
            target[1, t, rows] = v[t] + dv
        out.append((u[t] + du, v[t] + dv))
    return out


def next_power(keep, source, r, n):
    u, nb_u = neighbour_sums(lambda t, a, m: source[0, t, pl.ds(a, m)], r, n, 1)
    v, nb_v = neighbour_sums(lambda t, a, m: source[1, t, pl.ds(a, m)], r, n, 1)
    rows = pl.ds(r, n)
    first, second = [], []
    for t in (0, 1):
        cross, squared, inv_u, inv_v = (keep[i, t, rows] for i in range(4))
        first.append(u[t] + inv_u * (cross * v[t] - DIFF[0] * nb_u[t]))
        second.append(v[t] - inv_v * (squared * u[t] + DIFF[1] * nb_v[t]))
    return first, second


CARRY1 = _RHO1 * _RHO0
CARRY2 = _RHO2 * _RHO1


POWERS = 9


def write_gains(spread, out):
    lane = lax.broadcasted_iota(jnp.int32, (1, X), 1)
    for level in range(3):
        top = jnp.max(jnp.where(lane == level, spread, 0.0), axis=1, keepdims=True)
        tau = 1.0 / (1.0 + jnp.broadcast_to(top, (Z, X)))
        for i, factor in enumerate((1.0 / _CENTRE, 2.0 * _RHO1 / _HALF, 2.0 * _RHO2 / _HALF)):
            out[3 * level + i] = factor * tau
    g0, g1, g2 = (out[i] for i in range(3))
    first, second = g0 + CARRY1 * g0 + g1, g1 * g0
    out[POWERS] = first + CARRY2 * (CARRY1 * g0 + g1) + g2
    out[POWERS + 1] = second + CARRY2 * second + g2 * first
    out[POWERS + 2] = g2 * second


def pair_rows(value):
    n = value.shape[0] // 2
    pairs = value.reshape(n, 2, Z, X)
    return pairs[:, 0] + pairs[:, 1]


def restrict_01(first, second):
    lane, sub = lane_of(), sub_of()
    across = []
    for value in (first, second):
        a, b = value[0:1], value[1:2]
        across.append(jnp.where((lane & 1) == 0, a + roll_x(a, -1), b + roll_x(b, 1)))
    a, b = across
    return 0.125 * jnp.where((sub & 1) == 0, a + roll_z(a, -1), b + roll_z(b, 1))


def restrict_12(groups):
    lane, sub = lane_of(), sub_of()
    out = None
    for p, value in enumerate(groups):
        value = value + roll_x(value, 1 if p & 1 else -1)
        value = value + roll_x(value, 2 if p & 2 else -2)
        out = value if out is None else jnp.where((lane & 3) == p, value, out)
    return 0.125 * (out + jnp.where((sub & 2) == 0, roll_z(out, -2), roll_z(out, 2)))


def spread_x(tile, k, phase):
    return jnp.where((lane_of() & k) == phase, tile, roll_x(tile, -k if phase else k))


def packed_jacobian(uv, fk, level):
    scale = 0.25**level
    even = (sub_of() & 1) == 0
    u, v = jnp.where(even, uv, roll_z(uv, 1)), jnp.where(even, roll_z(uv, -1), uv)
    f, k = jnp.where(even, fk, roll_z(fk, 1)), jnp.where(even, roll_z(fk, -1), fk)
    product, squared = u * v, v * v
    diag = jnp.where(
        even,
        INV_STEP + squared + f + 6.0 * DIFF[0] * scale,
        INV_STEP + f + k - 2.0 * product + 6.0 * DIFF[1] * scale,
    )
    return 1.0 / diag, jnp.where(even, -2.0 * product, squared), diag


def packed_spread(uv, fk, level):
    scale = 0.25**level
    even = (sub_of() & 1) == 0
    inverse, other, _ = packed_jacobian(uv, fk, level)
    return jnp.where(even, 6.0 * DIFF[0] * scale - other, 6.0 * DIFF[1] * scale + other) * inverse


def packed_terms(source, g, n, level):
    k = 1 << level
    lane, sub = lane_of(), sub_of()
    even = (sub & 1) == 0
    first, last = (lane & (k - 1)) == 0, (lane & (k - 1)) == k - 1
    low, high = lane < k, lane >= X - k
    diff = jnp.where(even, DIFF[0] * 0.25**level, DIFF[1] * 0.25**level)
    wide = [source[t, pl.ds(g - 1, n + 2)] for t in (0, 1)]
    centre = [w[1 : n + 1] for w in wide]
    right = [roll_x(c, k) for c in centre]
    left = [roll_x(c, -k) for c in centre]
    out = []
    for t in (0, 1):
        c, w = centre[t], wide[t]
        total = jnp.where(low, right[1 - t], right[t]) + jnp.where(high, left[1 - t], left[t])
        if k == 2:
            ahead, back = roll_x(w, 1), roll_x(w, -1)
            total = total + jnp.where(first, back[0:n], ahead[1 : n + 1])
            total = total + jnp.where(last, ahead[2 : n + 2], back[1 : n + 1])
            total = total + roll_z(c, 2) + roll_z(c, -2)
        else:
            total = total + jnp.where(first, roll_x(w[0:n], -(k - 1)), roll_x(c, 1))
            total = total + jnp.where(last, roll_x(w[2 : n + 2], k - 1), roll_x(c, -1))
            total = total + 2.0 * roll_z(c, 4)
        other = jnp.where(even, roll_z(c, -1), roll_z(c, 1))
        out.append((c, other, diff * total))
    return out


def packed_first(coef, shift, b, target, d, g, n, gain):
    for t in (0, 1):
        value = gain * coef[0, t, pl.ds(g + shift, n)] * b[t, pl.ds(g + shift, n)]
        d[t, pl.ds(g, n)] = value
        target[t, pl.ds(g, n)] = value


def packed_step(level, coef, shift, b, source, target, d, g, n, carry, gain):
    for t, (c, other, spread) in enumerate(packed_terms(source, g, n, level)):
        at = pl.ds(g + shift, n)
        res = coef[0, t, at] * (b[t, at] + coef[1, t, at] * other + spread) - c
        delta = gain * res
        if carry is not None:
            delta = delta + carry * d[t, pl.ds(g, n)]
        d[t, pl.ds(g, n)] = delta
        target[t, pl.ds(g, n)] = c + delta


def plane(ref, f, y, rows):
    return ref[pl.ds(f * Z * rows + y, Z, stride=rows), :]


def is_even(axis):
    return lax.rem(lax.axis_index(axis), 2) == 0


def prev_of(even, first, second, at):
    return jnp.where(even, first[at], second[at])


def next_of(even, first, second, at):
    return jnp.where(even, second[at], first[at])


SOURCES = ((0, 0), (0, 1), (1, 0), (1, 1), (2, 0), (3, 0))


def first_kernel(rows, state, previous, feed, kill, first, second, coarse, *rest):
    held, sems = rest[:4], rest[4]
    copies = [
        pltpu.make_async_copy(ref, to, sems.at[i]) for i, (ref, to) in enumerate(zip((state, previous, feed, kill), held))
    ]
    for copy in copies:
        copy.start()
    for copy in copies:
        copy.wait()
    even = is_even("gy")
    values = []
    for i, (j, f) in enumerate(SOURCES):
        wanted = range(rows) if i not in (2, 3) else [*range(SENT), *range(rows - SENT, rows)]
        values.append({y: plane(held[j], f, y, rows)[None] for y in wanted})
    for i in (2, 3):
        weight = DIFF[i - 2] / INV_STEP
        values[i][SENT - 1] = values[i][SENT - 1] + weight * values[i - 2][SENT]
        values[i][rows - SENT] = values[i][rows - SENT] + weight * values[i - 2][rows - SENT - 1]
    for i in range(6):
        for y in range(SENT):
            top, bottom = values[i][y], values[i][rows - SENT + y]
            at = slice(i * SENT + y, i * SENT + y + 1)
            first[at] = jnp.where(even, top, bottom)
            second[at] = jnp.where(even, bottom, top)
    pairs = []
    for p, (i, j) in enumerate(((0, 1), (4, 5))):
        parts = []
        for g in range(OWN):
            sums = [
                jnp.concatenate([value[4 * g + 2 * q] + value[4 * g + 2 * q + 1] for q in (0, 1)], axis=0)
                for value in (values[i], values[j])
            ]
            parts.append(restrict_01(*sums))
        pairs.append(jnp.concatenate(parts, axis=0))
        coarse[p * OWN : (p + 1) * OWN] = pairs[p]
        for ref in (first, second):
            ref[FIELDS1 + p * OWN : FIELDS1 + (p + 1) * OWN] = pairs[p]
    uv, fk = (restrict_12([pair[j : j + 1] for j in range(OWN)]) for pair in pairs)
    both = jnp.where((sub_of() & 2) == 0, uv, fk)
    coarse[2 * OWN : 2 * OWN + 1] = both
    for ref in (first, second):
        ref[FIELDS2:] = jnp.broadcast_to(both, (ref.shape[0] - FIELDS2, Z, X))


def split_fields2(both):
    low = (sub_of() & 2) == 0
    return jnp.where(low, both, roll_z(both, 2)), jnp.where(low, roll_z(both, -2), both)


def write_spread(main, coarse, out):
    lane = lax.broadcasted_iota(jnp.int32, (1, X), 1)
    u, v, f, k = (main[i] for i in (0, 1, 4, 5))
    cross, squared, inv_u, inv_v, _, _ = jacobian(u, v, f, k, 0)
    tops = [jnp.max(jnp.maximum((6.0 * DIFF[0] + cross) * inv_u, (6.0 * DIFF[1] + squared) * inv_v), axis=0)]
    tops.append(jnp.max(packed_spread(coarse[0:OWN], coarse[OWN : 2 * OWN], 1), axis=0))
    tops.append(packed_spread(*split_fields2(coarse[2 * OWN : 2 * OWN + 1]), 2)[0])
    result = jnp.zeros((1, X), jnp.float32)
    for level, top in enumerate(tops):
        top = jnp.max(jnp.max(top, axis=0, keepdims=True), axis=1, keepdims=True)
        result = jnp.where(lane == level, jnp.broadcast_to(top, (1, X)), result)
    out[...] = jnp.broadcast_to(result[None], out.shape)


GROUPS1 = HI1 - LO1
GROUPS2 = HI2 - LO2


def tiles_for(entries):
    return -(-entries // PER)


def pack_edges(entries, even, first, second):
    lane = lane_of()
    share = first.shape[0]
    left, right = None, None
    for j in range(PER):
        part = entries[j * share : (j + 1) * share]
        a, b = roll_x(part, WIDE * j), roll_x(part, WIDE + WIDE * j)
        left = a if left is None else jnp.where(lane >= WIDE * j, a, left)
        right = b if right is None else jnp.where(lane >= WIDE * j, b, right)
    first[...] = jnp.where(even, left, right)
    second[...] = jnp.where(even, right, left)


def halo_tiles(even, packets, lo, hi):
    first, second = packets
    share = first.shape[0]
    lane = lane_of()
    out = []
    for j in range(PER):
        a, b = max(lo, j * share), min(hi, (j + 1) * share)
        if a < b:
            strip = slice(a - j * share, b - j * share)
            left, right = prev_of(even, first, second, strip), next_of(even, first, second, strip)
            value = jnp.where(lane < X // 2, roll_x(right, -WIDE * j), roll_x(left, X - WIDE - WIDE * j))
            out.append((a - lo, b - lo, value))
    return out


def pack_own_kernel(
    rows, state, previous, feed, kill, coarse, first, second, spread, main, held, copies, sem
):
    inputs = (state, previous, feed, kill)
    for i, (j, f) in enumerate(SOURCES):
        for y in range(rows):
            main[i, y] = plane(inputs[j], f, y, rows)
    write_spread(main, coarse, copies)
    copy = pltpu.make_async_copy(copies, spread, sem)
    copy.start()
    for i in range(6):
        held[i * rows : (i + 1) * rows] = main[i]
    held[6 * rows : 6 * rows + 2 * OWN + 1] = coarse[...]
    pack_edges(held, is_even("gx"), first, second)
    copy.wait()


def pack_corner_kernel(y_first, y_second, first, second, held):
    even = is_even("gy")
    every = slice(0, PACKET)
    held[0:PACKET] = prev_of(even, y_first, y_second, every)
    held[PACKET : 2 * PACKET] = next_of(even, y_first, y_second, every)
    pack_edges(held, is_even("gx"), first, second)


EDGE_TILES = 2 * EDGE + 1


def level0_setup(fields, keep, diag, power, r, n):
    at = pl.ds(r, n)
    u, nb_u = neighbour_sums(lambda t, a, m: fields[0, t, pl.ds(a, m)], r, n, 1)
    v, nb_v = neighbour_sums(lambda t, a, m: fields[1, t, pl.ds(a, m)], r, n, 1)
    for t in (0, 1):
        f, k = fields[4, t, at], fields[5, t, at]
        cross, squared, inv_u, inv_v, first, second = jacobian(u[t], v[t], f, k, 0)
        react = u[t] * squared
        b_u = DIFF[0] * (nb_u[t] - 6.0 * u[t]) - INV_STEP * (u[t] - fields[2, t, at]) - react + f * (1.0 - u[t])
        b_v = DIFF[1] * (nb_v[t] - 6.0 * v[t]) - INV_STEP * (v[t] - fields[3, t, at]) + react - (f + k) * v[t]
        for i, value in enumerate((cross, squared, inv_u, inv_v, b_u, b_v)):
            keep[i, t, at] = value
        for i, value in enumerate((first, second)):
            diag[i, t, at] = value
        for i, value in enumerate((inv_u * b_u, inv_v * b_v)):
            power[i, t, at] = value


def level0_power(keep, source, target, r, n):
    for i, values in enumerate(next_power(keep, source, r, n)):
        for t in (0, 1):
            target[i, t, pl.ds(r, n)] = values[t]


def level0_down(keep, diag, y1, y2, sources, r, n):
    at = pl.ds(r, n)
    last = next_power(keep, y2, r, n)
    for t in (0, 1):
        both = [diag[i, t, at] for i in (0, 1)]
        parts = [[keep[4 + i, t, at] for i in (0, 1)]]
        parts += [[both[i] * power[i, t, at] for i in (0, 1)] for power in (y1, y2)]
        parts.append([both[i] * last[i][t] for i in (0, 1)])
        for q, part in enumerate(parts):
            u, v = (pair_rows(value) for value in part)
            for j in range(n // 4):
                value = restrict_01(u[2 * j : 2 * j + 2], v[2 * j : 2 * j + 2])
                sources[q, t, pl.ds((r - HALO0) // 4 + j, 1)] = value


def inner(rows, lost):
    return slice(HALO0 + lost, HALO0 + rows - lost)


def ends(rows, lo, hi):
    total = rows + 2 * HALO0
    return slice(lo, hi), slice(total - hi, total - lo)


def put_ends(target, rows, lo, hi, source):
    n = hi - lo
    for at, part in zip(ends(rows, lo, hi), (slice(0, n), slice(n, 2 * n))):
        for i in range(target.shape[0]):
            for t in (0, 1):
                target[i, t, at] = source[i, t, part]


def take_ends(source, rows, lo, hi, target):
    n = hi - lo
    for at, part in zip(ends(rows, lo, hi), (slice(0, n), slice(n, 2 * n))):
        for i in range(source.shape[0]):
            for t in (0, 1):
                target[i, t, part] = source[i, t, at]


def level0_inner_kernel(rows, main, own_a, own_b, keep_in, y0_in, y1_in, y2_in, diag_in, sources_in, *scratch):
    fields, keep, diag, y0, y1, y2 = scratch
    even_x = is_even("gx")
    for i in range(6):
        fields[i, 0, HALO0 : HALO0 + rows] = main[i]
        for a, b, value in halo_tiles(even_x, (own_a, own_b), i * rows, (i + 1) * rows):
            fields[i, 1, HALO0 + a : HALO0 + b] = value
    first = HALO0 + 1
    level0_setup(fields, keep, diag, y0, first, rows - 2)
    level0_power(keep, y0, y1, first + 1, rows - 4)
    level0_power(keep, y1, y2, first + 2, rows - 6)
    level0_down(keep, diag, y1, y2, sources_in, first + 3, rows - 8)
    for source, target, lost in ((keep, keep_in, 1), (y1, y1_in, 2), (y2, y2_in, 3)):
        for i in range(source.shape[0]):
            for t in (0, 1):
                target[i, t] = source[i, t, inner(rows, lost)]
    take_ends(y0, rows, HALO0 + 1, HALO0 + 3, y0_in)
    take_ends(diag, rows, HALO0 + 1, HALO0 + 4, diag_in)


def level0_outer_kernel(
    rows,
    main,
    y_first,
    y_second,
    own_a,
    own_b,
    corner_a,
    corner_b,
    keep_in,
    y0_in,
    y1_in,
    y2_in,
    diag_in,
    sources_in,
    keep_out,
    y1_out,
    y2_out,
    sources,
    edges,
    *scratch,
):
    fields, keep, diag, y0, y1, y2 = scratch
    even, even_x = is_even("gy"), is_even("gx")
    total = rows + 2 * HALO0
    near, skip = HALO0 + 2, HALO0 - SENT
    for i in range(6):
        strip = slice(i * SENT, (i + 1) * SENT)
        fields[i, 0, skip:HALO0] = prev_of(even, y_first, y_second, strip)
        fields[i, 0, HALO0:near] = main[i, 0:2]
        fields[i, 0, total - near : total - HALO0] = main[i, rows - 2 : rows]
        fields[i, 0, HALO0 + rows : total - skip] = next_of(even, y_first, y_second, strip)
        for packets, lo, n, at in (
            ((corner_a, corner_b), i * SENT, SENT, skip),
            ((own_a, own_b), i * rows, 2, HALO0),
            ((own_a, own_b), (i + 1) * rows - 2, 2, total - near),
            ((corner_a, corner_b), PACKET + i * SENT, SENT, HALO0 + rows),
        ):
            for a, b, value in halo_tiles(even_x, packets, lo, lo + n):
                fields[i, 1, at + a : at + b] = value
    for i in (0, 1):
        for t in (0, 1):
            for at in (0, total - 1):
                fields[i, t, at] = jnp.zeros((Z, X), jnp.float32)
    for at, part in zip(ends(rows, 5, 8), (slice(0, 3), slice(rows - 5, rows - 2))):
        for i in range(6):
            for t in (0, 1):
                keep[i, t, at] = keep_in[i, t, part]
    put_ends(diag, rows, 5, 8, diag_in)
    put_ends(y0, rows, 5, 7, y0_in)
    for target, source, lost in ((y1, y1_in, 2), (y2, y2_in, 3)):
        n = rows - 2 * lost
        for at, part in zip(ends(rows, HALO0 + lost, HALO0 + lost + 2), (slice(0, 2), slice(n - 2, n))):
            for i in (0, 1):
                for t in (0, 1):
                    target[i, t, at] = source[i, t, part]
    for r in (1, total - 5):
        level0_setup(fields, keep, diag, y0, r, 4)
    for r in (2, total - 6):
        level0_power(keep, y0, y1, r, 4)
    for r in (3, total - 7):
        level0_power(keep, y1, y2, r, 4)
    for r in (4, total - 8):
        level0_down(keep, diag, y1, y2, sources, r, 4)
    for q in range(4):
        for t in (0, 1):
            sources[q, t, 1 : OWN - 1] = sources_in[q, t, 1 : OWN - 1]
    take_ends(keep, rows, 1, 5, keep_out)
    take_ends(y1, rows, 4, 6, y1_out)
    take_ends(y2, rows, 4, 7, y2_out)
    for p, power in enumerate((y0, y1, y2)):
        for side, start in enumerate((HALO0, HALO0 + rows - EDGE)):
            edges[p, side] = pack_rows(power, start)


def pack_rows(x, start):
    lane = lane_of()
    halo = None
    for i in (0, 1):
        for j in range(EDGE):
            at = i * EDGE + j
            value = roll_x(x[i, 1, start + j : start + j + 1], 4 + 8 * at)
            halo = value if halo is None else jnp.where((lane >> 3) == at, value, halo)
    return jnp.concatenate([x[i, 0, start : start + EDGE] for i in (0, 1)] + [halo], axis=0)


def squeeze(halo):
    lane = lane_of()
    last = halo[OWN - 1 : OWN]
    ahead = (lane >= WIDE) & (lane < 2 * WIDE)
    parts = [jnp.where(ahead, roll_x(last, WIDE), halo[0:1]), jnp.where(ahead, roll_x(last, 2 * WIDE - X), halo[1:2])]
    return jnp.concatenate(parts + [halo[2 : OWN - 1]], axis=0)


def unsqueeze(tiles):
    last = jnp.where(lane_of() < X // 2, roll_x(tiles[0:1], -WIDE), roll_x(tiles[1:2], X - 2 * WIDE))
    return jnp.concatenate([tiles, last], axis=0)


def combine_kernel(sources, edges, spread, own, first, second, edge_first, edge_second, gain):
    write_gains(jnp.max(spread[...], axis=0)[0:1], gain)
    p0, p1, p2 = (gain[POWERS + i] for i in range(3))
    for t in (0, 1):
        value = sources[0, t] - p0 * sources[1, t] + p1 * sources[2, t] - p2 * sources[3, t]
        own[t] = value
        for ref in (first, second):
            if t == 0:
                ref[0:OWN] = value
            else:
                ref[OWN:] = squeeze(value)
    even = is_even("gy")
    top, bottom = (p0 * edges[0, side] - p1 * edges[1, side] + p2 * edges[2, side] for side in (0, 1))
    edge_first[...] = jnp.where(even, top, bottom)
    edge_second[...] = jnp.where(even, bottom, top)


def coarse1_kernel(
    rows, coarse, y_first, y_second, own_a, own_b, corner_a, corner_b, gain, keep_in, y1_in, y2_in, keep_out, y1_out, y2_out,
    coef, keep0, x0, fields
):
    even, even_x = is_even("gy"), is_even("gx")
    own_x, corner_x = (own_a, own_b), (corner_a, corner_b)
    for p in (0, 1):
        to = p * GROUPS1
        strip = slice(FIELDS1 + p * OWN, FIELDS1 + (p + 1) * OWN)
        fields[0, to : to + OWN] = prev_of(even, y_first, y_second, strip)
        fields[0, to + OWN : to + 2 * OWN] = coarse[p * OWN : (p + 1) * OWN]
        fields[0, to + 2 * OWN : to + 3 * OWN] = next_of(even, y_first, y_second, strip)
        for part, (packets, lo) in enumerate(
            ((corner_x, FIELDS1), (own_x, 6 * rows), (corner_x, PACKET + FIELDS1))
        ):
            lo += p * OWN
            for a, b, value in halo_tiles(even_x, packets, lo, lo + OWN):
                fields[1, to + part * OWN + a : to + part * OWN + b] = value
    for t in (0, 1):
        for i, value in enumerate(packed_jacobian(fields[t, 0:GROUPS1], fields[t, GROUPS1 : 2 * GROUPS1], 1)):
            coef[i, t, 1 : SIZE1 - 1] = value

    def whole(inside, outside):
        n = outside.shape[0] // 2
        return jnp.concatenate([outside[0:n], inside, outside[n:]], axis=0)

    for i in range(6):
        for t in (0, 1):
            keep0[i, t, 1 : rows + 2 * HALO0 - 1] = whole(keep_in[i, t], keep_out[i, t])
    p0, p1, p2 = (gain[POWERS + i] for i in range(3))
    for i in (0, 1):
        for t in (0, 1):
            y0 = keep0[2 + i, t, HALO0 : HALO0 + rows] * keep0[4 + i, t, HALO0 : HALO0 + rows]
            y1, y2 = (whole(a[i, t], b[i, t]) for a, b in ((y1_in, y1_out), (y2_in, y2_out)))
            x0[i, t] = p0 * y0 - p1 * y1 + p2 * y2


def fields2_kernel(rows, coarse, y_first, y_second, own_a, own_b, corner_a, corner_b, out):
    even, even_x = is_even("gy"), is_even("gx")
    own_x, corner_x = (own_a, own_b), (corner_a, corner_b)
    near = slice(FIELDS2, FIELDS2 + 1)
    out[0, 0:1] = prev_of(even, y_first, y_second, near)
    out[0, 1:2] = coarse[2 * OWN : 2 * OWN + 1]
    out[0, 2:3] = next_of(even, y_first, y_second, near)
    for q, (packets, lo) in enumerate(
        ((corner_x, FIELDS2), (own_x, 6 * rows + 2 * OWN), (corner_x, PACKET + FIELDS2))
    ):
        out[1, q : q + 1] = halo_tiles(even_x, packets, lo, lo + 1)[0][2]


def level1_kernel(
    own, first, second, edge_a, edge_b, fields2, coef1, gain, packet, to_first, to_second, to_far, keep, y1, d1
):
    b1, x1 = keep.at[0], keep.at[1]
    even = is_even("gy")
    for t in (0, 1):
        b1[t, 1 + OWN : 1 + 2 * OWN] = own[t]
        for at, take in ((1, prev_of), (1 + 2 * OWN, next_of)):
            if t == 0:
                b1[t, at : at + OWN] = take(even, first, second, slice(0, OWN))
            else:
                b1[t, at : at + OWN] = unsqueeze(take(even, first, second, slice(OWN, 2 * OWN - 1)))
    g0, g1, g2 = (gain[3 + i] for i in range(3))
    n = GROUPS1
    packed_first(coef1, 0, b1, x1, d1, 1, n, g0)
    packed_step(1, coef1, 0, b1, x1, y1, d1, 2, n - 2, CARRY1, g1)
    packed_step(1, coef1, 0, b1, y1, x1, d1, 2, n - 2, CARRY2, g2)
    here = pl.ds(1 + OWN, OWN)
    values = []
    for t, (c, other, spread) in enumerate(packed_terms(x1, 1 + OWN, OWN, 1)):
        res = b1[t, here] - coef1[2, t, here] * c + coef1[1, t, here] * other + spread
        values.append(restrict_12([res[j : j + 1] for j in range(OWN)]))
        to_far[1 + t : 2 + t] = fields2[t, 1:2]
    value = jnp.where((sub_of() & 2) == 0, values[0], values[1])
    for ref in (packet, to_first, to_second, to_far):
        ref[0:1] = value
    to_first[1:] = edge_a[...]
    to_second[1 : 1 + EDGE_TILES] = edge_b[...]
    to_second[1 + EDGE_TILES :] = value


def rest_kernel(
    own2, near_a, near_b, far_a, far_b, gain, coef1, fields2, keep0, iterate, keep1, out, coef2, d1, b2, x2, y2, d2, xu, yu, x0, y0, d0
):
    rows = out.shape[0] // (2 * Z)
    even = (sub_of() & 1) == 0
    b1, x1 = keep1.at[0], keep1.at[1]

    even_y, low = is_even("gy"), lax.rem(lax.axis_index("gy"), 4) < 2
    at = slice(0, 1)
    parts = [
        next_of(low, far_a, far_b, at),
        prev_of(even_y, near_a, near_b, at),
        own2[at],
        next_of(even_y, near_a, near_b, at),
        prev_of(low, far_a, far_b, at),
    ]
    for t, values in enumerate(split_fields2(jnp.concatenate(parts, axis=0))):
        b2[t, 1 : SIZE2 - 1] = values
        at = slice(1 + t, 2 + t)
        parts = [next_of(low, far_a, far_b, at), fields2[t], prev_of(low, far_a, far_b, at)]
        inverse, other, _ = packed_jacobian(*split_fields2(jnp.concatenate(parts, axis=0)), 2)
        coef2[0, t, 1 : SIZE2 - 1] = inverse
        coef2[1, t, 1 : SIZE2 - 1] = other

    n = HI2 - LO2
    g0, g1, g2 = (gain[6 + i] for i in range(3))
    packed_first(coef2, 0, b2, x2, d2, 1, n, g0)
    packed_step(2, coef2, 0, b2, x2, y2, d2, 1, n, CARRY1, g1)
    packed_step(2, coef2, 0, b2, y2, x2, d2, 1, n, CARRY2, g2)
    packed_step(2, coef2, 0, b2, x2, y2, d2, 1, n, None, g0)
    packed_step(2, coef2, 0, b2, y2, x2, d2, 2, n - 2, CARRY1, g1)
    packed_step(2, coef2, 0, b2, x2, y2, d2, 2, n - 2, CARRY2, g2)

    g0, g1, g2 = (gain[3 + i] for i in range(3))
    shift = LO_UP - LO1
    for t in (0, 1):
        for g in range(LO_UP, HI_UP):
            p = g % 4
            value = y2[t, g // 4 - LO2 + 1 : g // 4 - LO2 + 2]
            value = spread_x(spread_x(value, 1, p & 1), 2, p & 2)
            at = g - LO_UP + 1
            xu[t, at : at + 1] = x1[t, at + shift : at + shift + 1] + value
    n = HI_UP - LO_UP
    packed_step(1, coef1, shift, b1, xu, yu, d1, 2, n - 2, None, g0)
    packed_step(1, coef1, shift, b1, yu, xu, d1, 2, n - 2, CARRY1, g1)
    packed_step(1, coef1, shift, b1, xu, yu, d1, 3, n - 4, CARRY2, g2)

    g0, g1, g2 = (gain[i] for i in range(3))
    for i in (0, 1):
        for at, take in ((HALO0 - EDGE, prev_of), (HALO0 + rows, next_of)):
            whole = take(even_y, near_a, near_b, slice(1, 1 + EDGE_TILES))
            x0[i, 0, at : at + EDGE] = whole[i * EDGE : (i + 1) * EDGE]
            for j in range(EDGE):
                x0[i, 1, at + j : at + j + 1] = roll_x(whole[2 * EDGE :], -(4 + 8 * (i * EDGE + j)))
        for t in (0, 1):
            x0[i, t, HALO0 : HALO0 + rows] = iterate[i, t]
    for t in (0, 1):
        for row in range(-2, rows // 2 + 2):
            at = row // 2 - LO_UP + 1
            value = spread_x(yu[t, at : at + 1], 1, row & 1)
            for i, fine in enumerate((jnp.where(even, value, roll_z(value, 1)), jnp.where(even, roll_z(value, -1), value))):
                for y in (2 * row, 2 * row + 1):
                    if -EDGE <= y < rows + EDGE:
                        x0[i, t, y + HALO0 : y + HALO0 + 1] = x0[i, t, y + HALO0 : y + HALO0 + 1] + fine
    total = rows + 2 * HALO0
    for r, n in chunks(2, total - 2):
        cheb_step(0, keep0, x0, y0, d0, r, n, None, g0)
    for r, n in chunks(3, total - 3):
        cheb_step(0, keep0, y0, x0, d0, r, n, CARRY1, g1)
    for r, n in chunks(4, total - 4):
        last = cheb_step(0, keep0, x0, None, d0, r, n, CARRY2, g2, (0,))[0]
        for i in (0, 1):
            for j in range(n):
                out[pl.ds(i * Z * rows + r - HALO0 + j, Z, stride=rows), :] = last[i][j]


def call(kernel, out_shapes, scratch, *args, space=pltpu.VMEM, outs=None):
    out = [jax.ShapeDtypeStruct(shape, jnp.float32) for shape in out_shapes]
    return pl.pallas_call(
        kernel,
        out_shape=out,
        in_specs=[pl.BlockSpec(memory_space=space)] * len(args),
        out_specs=[pl.BlockSpec(memory_space=m) for m in outs or [pltpu.VMEM] * len(out)],
        scratch_shapes=[pltpu.VMEM(s, jnp.float32) if isinstance(s, tuple) else s for s in scratch],
        compiler_params=pltpu.CompilerParams(vmem_limit_bytes=24 * 2**20),
    )(*args)


def swap(value, axis, step):
    count = lax.axis_size(axis)
    assert count % 2 == 0
    pairs = [(i, (i + step) % count) for i in range(0, count, 2)]
    return lax.ppermute(value, axis, pairs + [(j, i) for i, j in pairs])


def swap_far(value, axis, step):
    count = lax.axis_size(axis)
    assert count % 4 == 0
    pairs = [(i + j, (i + j + 2 * step) % count) for i in range(0, count, 4) for j in (0, 1)]
    return lax.ppermute(value, axis, pairs + [(j, i) for i, j in pairs])


def spare(shape):
    return (shape[0] + 1, *shape[1:])


def exchange(first, second, axis):
    return swap(first, axis, -1), swap(second, axis, 1)


def body(state, previous, feed, kill):
    _, depth, rows, cols = state.shape
    assert depth == Z and cols == X and rows == 4 * OWN
    across, count = lax.axis_size("gx"), lax.axis_size("gy")
    total0 = rows + 2 * HALO0
    state = state.reshape(2 * Z * rows, X)
    previous = previous.reshape(2 * Z * rows, X)
    feed = feed.reshape(Z * rows, X)
    kill = kill.reshape(Z * rows, X)
    inputs = (state, previous, feed, kill)

    strip = (PACKET, Z, X)
    first, second, coarse, *inputs = call(
        functools.partial(first_kernel, rows),
        [strip, spare(strip), (2 * OWN + 1, Z, X), *(a.shape for a in inputs)],
        [pltpu.SemaphoreType.DMA((4,))],
        *(pltpu.with_memory_space_constraint(a, pltpu.HBM) for a in inputs),
        space=pltpu.HBM,
    )
    y_packets = exchange(first, second, "gy")

    tiles = tiles_for(6 * rows + 2 * OWN + 1)
    spread_shape = (across * count, Z // 2, X)
    first, second, spread, main = call(
        functools.partial(pack_own_kernel, rows),
        [(tiles, Z, X), (tiles, Z, X), spread_shape, (6, rows, Z, X)],
        [(PER * tiles, Z, X), spread_shape, pltpu.SemaphoreType.DMA],
        *inputs,
        coarse,
        outs=[pltpu.VMEM, pltpu.VMEM, pltpu.HBM, pltpu.VMEM],
    )
    own_x = exchange(first, second, "gx")
    spread = lax.all_to_all(spread, ("gx", "gy"), 0, 0, tiled=True)
    tiles = tiles_for(2 * PACKET)
    corner_x = exchange(
        *call(pack_corner_kernel, [(tiles, Z, X), (tiles, Z, X)], [(PER * tiles, Z, X)], *y_packets), "gx"
    )

    strip, edge = (2 * OWN - 1, Z, X), (EDGE_TILES, Z, X)
    pair0 = (2, 2, total0, Z, X)
    work = [(6, 2, total0, Z, X), (6, 2, total0, Z, X), pair0, pair0, pair0, pair0]
    four = (4, 2, OWN, Z, X)
    inside = call(
        functools.partial(level0_inner_kernel, rows),
        [
            (6, 2, rows - 2, Z, X),
            (2, 2, 4, Z, X),
            (2, 2, rows - 4, Z, X),
            (2, 2, rows - 6, Z, X),
            (2, 2, 6, Z, X),
            four,
        ],
        work,
        main,
        *own_x,
    )
    keep_in, _, y1_in, y2_in, _, _ = inside
    keep_out, y1_out, y2_out, sources, edges = call(
        functools.partial(level0_outer_kernel, rows),
        [(6, 2, 8, Z, X), (2, 2, 4, Z, X), (2, 2, 6, Z, X), four, (3, 2, *edge)],
        work,
        main,
        *y_packets,
        *own_x,
        *corner_x,
        *inside,
    )
    own, first, second, edge_a, edge_b, gain = call(
        combine_kernel,
        [(2, OWN, Z, X), strip, strip, edge, edge, (POWERS + 3, Z, X)],
        [],
        sources,
        edges,
        spread,
    )
    coef1, keep0, iterate = call(
        functools.partial(coarse1_kernel, rows),
        [(3, 2, SIZE1, Z, X), (6, 2, total0, Z, X), (2, 2, rows, Z, X)],
        [(2, 2 * GROUPS1, Z, X)],
        coarse,
        *y_packets,
        *own_x,
        *corner_x,
        gain,
        keep_in,
        y1_in,
        y2_in,
        keep_out,
        y1_out,
        y2_out,
    )
    (fields2,) = call(
        functools.partial(fields2_kernel, rows), [(2, 3, Z, X)], [], coarse, *y_packets, *own_x, *corner_x
    )
    b_packets = exchange(first, second, "gy")

    one, two, up = (2, SIZE1, Z, X), (2, SIZE2, Z, X), (2, SIZE_UP, Z, X)
    near = (1 + EDGE_TILES, Z, X)
    packet, first, second, to_far, keep1 = call(
        level1_kernel,
        [(1, Z, X), near, spare(near), (3, Z, X), (2, *one)],
        [one, one],
        own,
        *b_packets,
        edge_a,
        edge_b,
        fields2,
        coef1,
        gain,
    )
    far = (swap_far(to_far, "gy", 1), swap_far(to_far, "gy", -1))
    near = exchange(first, second, "gy")

    (out,) = call(
        rest_kernel,
        [(2 * Z * rows, X)],
        [(2, *two), one, two, two, two, two, up, up, pair0, pair0, pair0],
        packet,
        *near,
        *far,
        gain,
        coef1,
        fields2,
        keep0,
        iterate,
        keep1,
    )
    return out.reshape(2, Z, rows, X)


def solution(mesh):
    placed = (
        P(None, None, "gy", "gx"),
        P(None, None, "gy", "gx"),
        P(None, "gy", "gx"),
        P(None, "gy", "gx"),
    )
    return jax.shard_map(
        body, mesh=mesh, in_specs=placed, out_specs=P(None, None, "gy", "gx"), check_vma=False
    )
```

```python
import functools

import jax
import jax.numpy as jnp
from jax import lax
from jax.experimental import pallas as pl
from jax.experimental.pallas import tpu as pltpu
from jax.sharding import PartitionSpec as P

DIFF = (40.0, 20.0)
INV_STEP = 2.0
LOWER = 0.25

_CENTRE = (1.0 + LOWER) / 2.0
_HALF = (1.0 - LOWER) / 2.0
_SIGMA = _CENTRE / _HALF
_RHO0 = 1.0 / _SIGMA
_RHO1 = 1.0 / (2.0 * _SIGMA - _RHO0)
_RHO2 = 1.0 / (2.0 * _SIGMA - _RHO1)

Z = 8
X = 128
HALO0 = 4
SENT = 3
FIELDS1 = 6 * SENT
FIELDS2 = FIELDS1 + 8
PACKET = FIELDS2 + 1
WIDE = 42
PER = X // WIDE
EDGE = 3

LO1, HI1 = -4, 8
LO2, HI2 = -2, 3
LO_UP, HI_UP = -3, 7
SIZE1, SIZE2, SIZE_UP = HI1 - LO1 + 2, HI2 - LO2 + 2, HI_UP - LO_UP + 2
OWN = 4


def lane_of():
    return lax.broadcasted_iota(jnp.int32, (1, Z, X), 2)


def sub_of():
    return lax.broadcasted_iota(jnp.int32, (1, Z, X), 1)


def roll_x(tile, shift):
    shift = shift % X
    return pltpu.roll(tile, shift, 2) if shift else tile


def roll_z(tile, shift):
    shift = shift % Z
    return pltpu.roll(tile, shift, 1) if shift else tile


def chunks(lo, hi, step=4):
    return [(r, min(step, hi - r)) for r in range(lo, hi, step)]


def neighbour_sums(read, r, n, k, tiles=(0, 1)):
    lane = lane_of()
    low, high = lane < k, lane >= X - k
    centre = [read(t, r, n) for t in (0, 1)]
    right = [roll_x(c, k) for c in centre]
    left = [roll_x(c, -k) for c in centre]
    sums = []
    for t in tiles:
        c = centre[t]
        along_x = jnp.where(low, right[1 - t], right[t]) + jnp.where(high, left[1 - t], left[t])
        along_y = read(t, r - 1, n) + read(t, r + 1, n)
        along_z = 2.0 * roll_z(c, k) if 2 * k == Z else roll_z(c, k) + roll_z(c, -k)
        sums.append(along_x + along_y + along_z)
    return centre, sums


def jacobian(u, v, f, k, level):
    scale = 0.25**level
    product = u * v
    squared = v * v
    first = INV_STEP + squared + f + 6.0 * DIFF[0] * scale
    second = INV_STEP + f + k - 2.0 * product + 6.0 * DIFF[1] * scale
    return 2.0 * product, squared, 1.0 / first, 1.0 / second, first, second


def cheb_step(level, keep, source, target, d, r, n, carry, gain, tiles=(0, 1)):
    scale = 0.25**level
    k = 1 << level
    u, nb_u = neighbour_sums(lambda t, a, m: source[0, t, pl.ds(a, m)], r, n, k, tiles)
    v, nb_v = neighbour_sums(lambda t, a, m: source[1, t, pl.ds(a, m)], r, n, k, tiles)
    rows = pl.ds(r, n)
    out = []
    for t in tiles:
        cross, squared, inv_u, inv_v = (keep[i, t, rows] for i in range(4))
        res_u = inv_u * (keep[4, t, rows] - cross * v[t] + DIFF[0] * scale * nb_u[t]) - u[t]
        res_v = inv_v * (keep[5, t, rows] + squared * u[t] + DIFF[1] * scale * nb_v[t]) - v[t]
        du, dv = gain * res_u, gain * res_v
        if carry is not None:
            du = du + carry * d[0, t, rows]
            dv = dv + carry * d[1, t, rows]
        if target is not None:
            d[0, t, rows] = du
            d[1, t, rows] = dv
            target[0, t, rows] = u[t] + du
            target[1, t, rows] = v[t] + dv
        out.append((u[t] + du, v[t] + dv))
    return out


def next_power(keep, source, r, n):
    u, nb_u = neighbour_sums(lambda t, a, m: source[0, t, pl.ds(a, m)], r, n, 1)
    v, nb_v = neighbour_sums(lambda t, a, m: source[1, t, pl.ds(a, m)], r, n, 1)
    rows = pl.ds(r, n)
    first, second = [], []
    for t in (0, 1):
        cross, squared, inv_u, inv_v = (keep[i, t, rows] for i in range(4))
        first.append(u[t] + inv_u * (cross * v[t] - DIFF[0] * nb_u[t]))
        second.append(v[t] - inv_v * (squared * u[t] + DIFF[1] * nb_v[t]))
    return first, second


CARRY1 = _RHO1 * _RHO0
CARRY2 = _RHO2 * _RHO1


POWERS = 9


def write_gains(spread, out):
    lane = lax.broadcasted_iota(jnp.int32, (1, X), 1)
    for level in range(3):
        top = jnp.max(jnp.where(lane == level, spread, 0.0), axis=1, keepdims=True)
        tau = 1.0 / (1.0 + jnp.broadcast_to(top, (Z, X)))
        for i, factor in enumerate((1.0 / _CENTRE, 2.0 * _RHO1 / _HALF, 2.0 * _RHO2 / _HALF)):
            out[3 * level + i] = factor * tau
    g0, g1, g2 = (out[i] for i in range(3))
    first, second = g0 + CARRY1 * g0 + g1, g1 * g0
    out[POWERS] = first + CARRY2 * (CARRY1 * g0 + g1) + g2
    out[POWERS + 1] = second + CARRY2 * second + g2 * first
    out[POWERS + 2] = g2 * second


def pair_rows(value):
    n = value.shape[0] // 2
    pairs = value.reshape(n, 2, Z, X)
    return pairs[:, 0] + pairs[:, 1]


def restrict_01(first, second):
    lane, sub = lane_of(), sub_of()
    across = []
    for value in (first, second):
        a, b = value[0:1], value[1:2]
        across.append(jnp.where((lane & 1) == 0, a + roll_x(a, -1), b + roll_x(b, 1)))
    a, b = across
    return 0.125 * jnp.where((sub & 1) == 0, a + roll_z(a, -1), b + roll_z(b, 1))


def restrict_12(groups):
    lane, sub = lane_of(), sub_of()
    out = None
    for p, value in enumerate(groups):
        value = value + roll_x(value, 1 if p & 1 else -1)
        value = value + roll_x(value, 2 if p & 2 else -2)
        out = value if out is None else jnp.where((lane & 3) == p, value, out)
    return 0.125 * (out + jnp.where((sub & 2) == 0, roll_z(out, -2), roll_z(out, 2)))


def spread_x(tile, k, phase):
    return jnp.where((lane_of() & k) == phase, tile, roll_x(tile, -k if phase else k))


def packed_jacobian(uv, fk, level):
    scale = 0.25**level
    even = (sub_of() & 1) == 0
    u, v = jnp.where(even, uv, roll_z(uv, 1)), jnp.where(even, roll_z(uv, -1), uv)
    f, k = jnp.where(even, fk, roll_z(fk, 1)), jnp.where(even, roll_z(fk, -1), fk)
    product, squared = u * v, v * v
    diag = jnp.where(
        even,
        INV_STEP + squared + f + 6.0 * DIFF[0] * scale,
        INV_STEP + f + k - 2.0 * product + 6.0 * DIFF[1] * scale,
    )
    return 1.0 / diag, jnp.where(even, -2.0 * product, squared), diag


def packed_spread(uv, fk, level):
    scale = 0.25**level
    even = (sub_of() & 1) == 0
    inverse, other, _ = packed_jacobian(uv, fk, level)
    return jnp.where(even, 6.0 * DIFF[0] * scale - other, 6.0 * DIFF[1] * scale + other) * inverse


def packed_terms(source, g, n, level):
    k = 1 << level
    lane, sub = lane_of(), sub_of()
    even = (sub & 1) == 0
    first, last = (lane & (k - 1)) == 0, (lane & (k - 1)) == k - 1
    low, high = lane < k, lane >= X - k
    diff = jnp.where(even, DIFF[0] * 0.25**level, DIFF[1] * 0.25**level)
    wide = [source[t, pl.ds(g - 1, n + 2)] for t in (0, 1)]
    centre = [w[1 : n + 1] for w in wide]
    right = [roll_x(c, k) for c in centre]
    left = [roll_x(c, -k) for c in centre]
    out = []
    for t in (0, 1):
        c, w = centre[t], wide[t]
        total = jnp.where(low, right[1 - t], right[t]) + jnp.where(high, left[1 - t], left[t])
        if k == 2:
            ahead, back = roll_x(w, 1), roll_x(w, -1)
            total = total + jnp.where(first, back[0:n], ahead[1 : n + 1])
            total = total + jnp.where(last, ahead[2 : n + 2], back[1 : n + 1])
            total = total + roll_z(c, 2) + roll_z(c, -2)
        else:
            total = total + jnp.where(first, roll_x(w[0:n], -(k - 1)), roll_x(c, 1))
            total = total + jnp.where(last, roll_x(w[2 : n + 2], k - 1), roll_x(c, -1))
            total = total + 2.0 * roll_z(c, 4)
        other = jnp.where(even, roll_z(c, -1), roll_z(c, 1))
        out.append((c, other, diff * total))
    return out


def packed_first(coef, shift, b, target, d, g, n, gain):
    for t in (0, 1):
        value = gain * coef[0, t, pl.ds(g + shift, n)] * b[t, pl.ds(g + shift, n)]
        d[t, pl.ds(g, n)] = value
        target[t, pl.ds(g, n)] = value


def packed_step(level, coef, shift, b, source, target, d, g, n, carry, gain):
    for t, (c, other, spread) in enumerate(packed_terms(source, g, n, level)):
        at = pl.ds(g + shift, n)
        res = coef[0, t, at] * (b[t, at] + coef[1, t, at] * other + spread) - c
        delta = gain * res
        if carry is not None:
            delta = delta + carry * d[t, pl.ds(g, n)]
        d[t, pl.ds(g, n)] = delta
        target[t, pl.ds(g, n)] = c + delta


def plane(ref, f, y, rows):
    return ref[pl.ds(f * Z * rows + y, Z, stride=rows), :]


def is_even(axis):
    return lax.rem(lax.axis_index(axis), 2) == 0


def prev_of(even, first, second, at):
    return jnp.where(even, first[at], second[at])


def next_of(even, first, second, at):
    return jnp.where(even, second[at], first[at])


SOURCES = ((0, 0), (0, 1), (1, 0), (1, 1), (2, 0), (3, 0))


def first_kernel(rows, state, previous, feed, kill, first, second, coarse, spread, *rest):
    held, (sems, spread_held, spread_sem) = rest[:4], rest[4:]
    copies = [
        pltpu.make_async_copy(ref, to, sems.at[i]) for i, (ref, to) in enumerate(zip((state, previous, feed, kill), held))
    ]
    for copy in copies:
        copy.start()
    for copy in copies:
        copy.wait()
    even = is_even("gy")
    values = []
    for i, (j, f) in enumerate(SOURCES):
        wanted = range(rows) if i not in (2, 3) else [*range(SENT), *range(rows - SENT, rows)]
        values.append({y: plane(held[j], f, y, rows)[None] for y in wanted})
    pairs = []
    for p, (i, j) in enumerate(((0, 1), (4, 5))):
        parts = []
        for g in range(OWN):
            sums = [
                jnp.concatenate([value[4 * g + 2 * q] + value[4 * g + 2 * q + 1] for q in (0, 1)], axis=0)
                for value in (values[i], values[j])
            ]
            parts.append(restrict_01(*sums))
        pairs.append(jnp.concatenate(parts, axis=0))
    uv, fk = (restrict_12([pair[j : j + 1] for j in range(OWN)]) for pair in pairs)
    fields = [jnp.concatenate([values[i][y] for y in range(rows)], axis=0) for i in (0, 1, 4, 5)]
    write_spread(fields, pairs, (uv, fk), spread_held)
    copy = pltpu.make_async_copy(spread_held, spread, spread_sem)
    copy.start()
    for i in (2, 3):
        weight = DIFF[i - 2] / INV_STEP
        values[i][SENT - 1] = values[i][SENT - 1] + weight * values[i - 2][SENT]
        values[i][rows - SENT] = values[i][rows - SENT] + weight * values[i - 2][rows - SENT - 1]
    for i in range(6):
        for y in range(SENT):
            top, bottom = values[i][y], values[i][rows - SENT + y]
            at = slice(i * SENT + y, i * SENT + y + 1)
            first[at] = jnp.where(even, top, bottom)
            second[at] = jnp.where(even, bottom, top)
    for p in (0, 1):
        coarse[p * OWN : (p + 1) * OWN] = pairs[p]
        for ref in (first, second):
            ref[FIELDS1 + p * OWN : FIELDS1 + (p + 1) * OWN] = pairs[p]
    both = jnp.where((sub_of() & 2) == 0, uv, fk)
    coarse[2 * OWN : 2 * OWN + 1] = both
    for ref in (first, second):
        ref[FIELDS2 : FIELDS2 + 1] = both
    copy.wait()


def split_fields2(both):
    low = (sub_of() & 2) == 0
    return jnp.where(low, both, roll_z(both, 2)), jnp.where(low, roll_z(both, -2), both)


def write_spread(fields, pairs, quads, out):
    lane = lax.broadcasted_iota(jnp.int32, (1, X), 1)
    cross, squared, inv_u, inv_v, _, _ = jacobian(*fields, 0)
    tops = [jnp.max(jnp.maximum((6.0 * DIFF[0] + cross) * inv_u, (6.0 * DIFF[1] + squared) * inv_v), axis=0)]
    tops.append(jnp.max(packed_spread(*pairs, 1), axis=0))
    tops.append(packed_spread(*quads, 2)[0])
    result = jnp.zeros((1, X), jnp.float32)
    for level, top in enumerate(tops):
        top = jnp.max(jnp.max(top, axis=0, keepdims=True), axis=1, keepdims=True)
        result = jnp.where(lane == level, jnp.broadcast_to(top, (1, X)), result)
    out[...] = jnp.broadcast_to(result[None], out.shape)


GROUPS1 = HI1 - LO1
GROUPS2 = HI2 - LO2


def tiles_for(entries):
    return -(-entries // PER)


def pack_edges(entries, even, first, second):
    lane = lane_of()
    share = first.shape[0]
    left, right = None, None
    for j in range(PER):
        part = entries[j * share : (j + 1) * share]
        a, b = roll_x(part, WIDE * j), roll_x(part, WIDE + WIDE * j)
        left = a if left is None else jnp.where(lane >= WIDE * j, a, left)
        right = b if right is None else jnp.where(lane >= WIDE * j, b, right)
    first[...] = jnp.where(even, left, right)
    second[...] = jnp.where(even, right, left)


def halo_tiles(even, packets, lo, hi):
    first, second = packets
    share = first.shape[0]
    lane = lane_of()
    out = []
    for j in range(PER):
        a, b = max(lo, j * share), min(hi, (j + 1) * share)
        if a < b:
            strip = slice(a - j * share, b - j * share)
            left, right = prev_of(even, first, second, strip), next_of(even, first, second, strip)
            value = jnp.where(lane < X // 2, roll_x(right, -WIDE * j), roll_x(left, X - WIDE - WIDE * j))
            out.append((a - lo, b - lo, value))
    return out


def pack_own_kernel(rows, state, previous, feed, kill, coarse, first, second, main, held):
    inputs = (state, previous, feed, kill)
    for i, (j, f) in enumerate(SOURCES):
        for y in range(rows):
            value = plane(inputs[j], f, y, rows)
            main[i, y] = value
            held[i * rows + y] = value
    held[6 * rows : 6 * rows + 2 * OWN + 1] = coarse[...]
    pack_edges(held, is_even("gx"), first, second)


def pack_corner_kernel(y_first, y_second, first, second, held):
    even = is_even("gy")
    every = slice(0, PACKET)
    held[0:PACKET] = prev_of(even, y_first, y_second, every)
    held[PACKET : 2 * PACKET] = next_of(even, y_first, y_second, every)
    pack_edges(held, is_even("gx"), first, second)


EDGE_TILES = 2 * EDGE + 1


def level0_setup(fields, keep, diag, power, r, n):
    at = pl.ds(r, n)
    u, nb_u = neighbour_sums(lambda t, a, m: fields[0, t, pl.ds(a, m)], r, n, 1)
    v, nb_v = neighbour_sums(lambda t, a, m: fields[1, t, pl.ds(a, m)], r, n, 1)
    for t in (0, 1):
        f, k = fields[4, t, at], fields[5, t, at]
        cross, squared, inv_u, inv_v, first, second = jacobian(u[t], v[t], f, k, 0)
        react = u[t] * squared
        b_u = DIFF[0] * (nb_u[t] - 6.0 * u[t]) - INV_STEP * (u[t] - fields[2, t, at]) - react + f * (1.0 - u[t])
        b_v = DIFF[1] * (nb_v[t] - 6.0 * v[t]) - INV_STEP * (v[t] - fields[3, t, at]) + react - (f + k) * v[t]
        for i, value in enumerate((cross, squared, inv_u, inv_v, b_u, b_v)):
            keep[i, t, at] = value
        for i, value in enumerate((first, second)):
            diag[i, t, at] = value
        for i, value in enumerate((inv_u * b_u, inv_v * b_v)):
            power[i, t, at] = value


def level0_power(keep, source, target, r, n):
    for i, values in enumerate(next_power(keep, source, r, n)):
        for t in (0, 1):
            target[i, t, pl.ds(r, n)] = values[t]


def level0_down(keep, diag, y1, y2, sources, r, n):
    at = pl.ds(r, n)
    last = next_power(keep, y2, r, n)
    for t in (0, 1):
        both = [diag[i, t, at] for i in (0, 1)]
        parts = [[keep[4 + i, t, at] for i in (0, 1)]]
        parts += [[both[i] * power[i, t, at] for i in (0, 1)] for power in (y1, y2)]
        parts.append([both[i] * last[i][t] for i in (0, 1)])
        for q, part in enumerate(parts):
            u, v = (pair_rows(value) for value in part)
            for j in range(n // 4):
                value = restrict_01(u[2 * j : 2 * j + 2], v[2 * j : 2 * j + 2])
                sources[q, t, pl.ds((r - HALO0) // 4 + j, 1)] = value


def inner(rows, lost):
    return slice(HALO0 + lost, HALO0 + rows - lost)


def ends(rows, lo, hi):
    total = rows + 2 * HALO0
    return slice(lo, hi), slice(total - hi, total - lo)


def put_ends(target, rows, lo, hi, source):
    n = hi - lo
    for at, part in zip(ends(rows, lo, hi), (slice(0, n), slice(n, 2 * n))):
        for i in range(target.shape[0]):
            for t in (0, 1):
                target[i, t, at] = source[i, t, part]


def take_ends(source, rows, lo, hi, target):
    n = hi - lo
    for at, part in zip(ends(rows, lo, hi), (slice(0, n), slice(n, 2 * n))):
        for i in range(source.shape[0]):
            for t in (0, 1):
                target[i, t, part] = source[i, t, at]


def level0_inner_kernel(rows, main, own_a, own_b, keep_in, y0_in, y1_in, y2_in, diag_in, sources_in, *scratch):
    fields, keep, diag, y0, y1, y2 = scratch
    even_x = is_even("gx")
    for i in range(6):
        fields[i, 0, HALO0 : HALO0 + rows] = main[i]
        for a, b, value in halo_tiles(even_x, (own_a, own_b), i * rows, (i + 1) * rows):
            fields[i, 1, HALO0 + a : HALO0 + b] = value
    first = HALO0 + 1
    level0_setup(fields, keep, diag, y0, first, rows - 2)
    level0_power(keep, y0, y1, first + 1, rows - 4)
    level0_power(keep, y1, y2, first + 2, rows - 6)
    level0_down(keep, diag, y1, y2, sources_in, first + 3, rows - 8)
    for source, target, lost in ((keep, keep_in, 1), (y1, y1_in, 2), (y2, y2_in, 3)):
        for i in range(source.shape[0]):
            for t in (0, 1):
                target[i, t] = source[i, t, inner(rows, lost)]
    take_ends(y0, rows, HALO0 + 1, HALO0 + 3, y0_in)
    take_ends(diag, rows, HALO0 + 1, HALO0 + 4, diag_in)


def level0_outer_kernel(
    rows,
    main,
    y_first,
    y_second,
    own_a,
    own_b,
    corner_a,
    corner_b,
    keep_in,
    y0_in,
    y1_in,
    y2_in,
    diag_in,
    sources_in,
    keep_out,
    y1_out,
    y2_out,
    sources,
    edges,
    *scratch,
):
    fields, keep, diag, y0, y1, y2 = scratch
    even, even_x = is_even("gy"), is_even("gx")
    total = rows + 2 * HALO0
    near, skip = HALO0 + 2, HALO0 - SENT
    for i in range(6):
        strip = slice(i * SENT, (i + 1) * SENT)
        fields[i, 0, skip:HALO0] = prev_of(even, y_first, y_second, strip)
        fields[i, 0, HALO0:near] = main[i, 0:2]
        fields[i, 0, total - near : total - HALO0] = main[i, rows - 2 : rows]
        fields[i, 0, HALO0 + rows : total - skip] = next_of(even, y_first, y_second, strip)
        for packets, lo, n, at in (
            ((corner_a, corner_b), i * SENT, SENT, skip),
            ((own_a, own_b), i * rows, 2, HALO0),
            ((own_a, own_b), (i + 1) * rows - 2, 2, total - near),
            ((corner_a, corner_b), PACKET + i * SENT, SENT, HALO0 + rows),
        ):
            for a, b, value in halo_tiles(even_x, packets, lo, lo + n):
                fields[i, 1, at + a : at + b] = value
    for i in (0, 1):
        for t in (0, 1):
            for at in (0, total - 1):
                fields[i, t, at] = jnp.zeros((Z, X), jnp.float32)
    for at, part in zip(ends(rows, 5, 8), (slice(0, 3), slice(rows - 5, rows - 2))):
        for i in range(6):
            for t in (0, 1):
                keep[i, t, at] = keep_in[i, t, part]
    put_ends(diag, rows, 5, 8, diag_in)
    put_ends(y0, rows, 5, 7, y0_in)
    for target, source, lost in ((y1, y1_in, 2), (y2, y2_in, 3)):
        n = rows - 2 * lost
        for at, part in zip(ends(rows, HALO0 + lost, HALO0 + lost + 2), (slice(0, 2), slice(n - 2, n))):
            for i in (0, 1):
                for t in (0, 1):
                    target[i, t, at] = source[i, t, part]
    for r in (1, total - 5):
        level0_setup(fields, keep, diag, y0, r, 4)
    for r in (2, total - 6):
        level0_power(keep, y0, y1, r, 4)
    for r in (3, total - 7):
        level0_power(keep, y1, y2, r, 4)
    for r in (4, total - 8):
        level0_down(keep, diag, y1, y2, sources, r, 4)
    for q in range(4):
        for t in (0, 1):
            sources[q, t, 1 : OWN - 1] = sources_in[q, t, 1 : OWN - 1]
    take_ends(keep, rows, 1, 5, keep_out)
    take_ends(y1, rows, 4, 6, y1_out)
    take_ends(y2, rows, 4, 7, y2_out)
    for p, power in enumerate((y0, y1, y2)):
        for side, start in enumerate((HALO0, HALO0 + rows - EDGE)):
            edges[p, side] = pack_rows(power, start)


def pack_rows(x, start):
    lane = lane_of()
    halo = None
    for i in (0, 1):
        for j in range(EDGE):
            at = i * EDGE + j
            value = roll_x(x[i, 1, start + j : start + j + 1], 4 + 8 * at)
            halo = value if halo is None else jnp.where((lane >> 3) == at, value, halo)
    return jnp.concatenate([x[i, 0, start : start + EDGE] for i in (0, 1)] + [halo], axis=0)


def squeeze(halo):
    lane = lane_of()
    last = halo[OWN - 1 : OWN]
    ahead = (lane >= WIDE) & (lane < 2 * WIDE)
    parts = [jnp.where(ahead, roll_x(last, WIDE), halo[0:1]), jnp.where(ahead, roll_x(last, 2 * WIDE - X), halo[1:2])]
    return jnp.concatenate(parts + [halo[2 : OWN - 1]], axis=0)


def unsqueeze(tiles):
    last = jnp.where(lane_of() < X // 2, roll_x(tiles[0:1], -WIDE), roll_x(tiles[1:2], X - 2 * WIDE))
    return jnp.concatenate([tiles, last], axis=0)


def combine_kernel(sources, edges, spread, own, first, second, edge_first, edge_second, gain):
    write_gains(jnp.max(spread[...], axis=0)[0:1], gain)
    p0, p1, p2 = (gain[POWERS + i] for i in range(3))
    for t in (0, 1):
        value = sources[0, t] - p0 * sources[1, t] + p1 * sources[2, t] - p2 * sources[3, t]
        own[t] = value
        for ref in (first, second):
            if t == 0:
                ref[0:OWN] = value
            else:
                ref[OWN:] = squeeze(value)
    even = is_even("gy")
    top, bottom = (p0 * edges[0, side] - p1 * edges[1, side] + p2 * edges[2, side] for side in (0, 1))
    edge_first[...] = jnp.where(even, top, bottom)
    edge_second[...] = jnp.where(even, bottom, top)


def coarse1_kernel(
    rows, coarse, y_first, y_second, own_a, own_b, corner_a, corner_b, gain, keep_in, y1_in, y2_in, keep_out, y1_out, y2_out,
    coef, keep0, x0, fields
):
    even, even_x = is_even("gy"), is_even("gx")
    own_x, corner_x = (own_a, own_b), (corner_a, corner_b)
    for p in (0, 1):
        to = p * GROUPS1
        strip = slice(FIELDS1 + p * OWN, FIELDS1 + (p + 1) * OWN)
        fields[0, to : to + OWN] = prev_of(even, y_first, y_second, strip)
        fields[0, to + OWN : to + 2 * OWN] = coarse[p * OWN : (p + 1) * OWN]
        fields[0, to + 2 * OWN : to + 3 * OWN] = next_of(even, y_first, y_second, strip)
        for part, (packets, lo) in enumerate(
            ((corner_x, FIELDS1), (own_x, 6 * rows), (corner_x, PACKET + FIELDS1))
        ):
            lo += p * OWN
            for a, b, value in halo_tiles(even_x, packets, lo, lo + OWN):
                fields[1, to + part * OWN + a : to + part * OWN + b] = value
    for t in (0, 1):
        for i, value in enumerate(packed_jacobian(fields[t, 0:GROUPS1], fields[t, GROUPS1 : 2 * GROUPS1], 1)):
            coef[i, t, 1 : SIZE1 - 1] = value

    def whole(inside, outside):
        n = outside.shape[0] // 2
        return jnp.concatenate([outside[0:n], inside, outside[n:]], axis=0)

    for i in range(6):
        for t in (0, 1):
            keep0[i, t, 1 : rows + 2 * HALO0 - 1] = whole(keep_in[i, t], keep_out[i, t])
    p0, p1, p2 = (gain[POWERS + i] for i in range(3))
    for i in (0, 1):
        for t in (0, 1):
            y0 = keep0[2 + i, t, HALO0 : HALO0 + rows] * keep0[4 + i, t, HALO0 : HALO0 + rows]
            y1, y2 = (whole(a[i, t], b[i, t]) for a, b in ((y1_in, y1_out), (y2_in, y2_out)))
            x0[i, t] = p0 * y0 - p1 * y1 + p2 * y2


def fields2_kernel(rows, coarse, y_first, y_second, own_a, own_b, corner_a, corner_b, out):
    even, even_x = is_even("gy"), is_even("gx")
    own_x, corner_x = (own_a, own_b), (corner_a, corner_b)
    near = slice(FIELDS2, FIELDS2 + 1)
    out[0, 0:1] = prev_of(even, y_first, y_second, near)
    out[0, 1:2] = coarse[2 * OWN : 2 * OWN + 1]
    out[0, 2:3] = next_of(even, y_first, y_second, near)
    for q, (packets, lo) in enumerate(
        ((corner_x, FIELDS2), (own_x, 6 * rows + 2 * OWN), (corner_x, PACKET + FIELDS2))
    ):
        out[1, q : q + 1] = halo_tiles(even_x, packets, lo, lo + 1)[0][2]


def level1_kernel(
    own, first, second, edge_a, edge_b, fields2, coef1, gain, packet, to_first, to_second, to_far, keep, y1, d1
):
    b1, x1 = keep.at[0], keep.at[1]
    even = is_even("gy")
    for t in (0, 1):
        b1[t, 1 + OWN : 1 + 2 * OWN] = own[t]
        for at, take in ((1, prev_of), (1 + 2 * OWN, next_of)):
            if t == 0:
                b1[t, at : at + OWN] = take(even, first, second, slice(0, OWN))
            else:
                b1[t, at : at + OWN] = unsqueeze(take(even, first, second, slice(OWN, 2 * OWN - 1)))
    g0, g1, g2 = (gain[3 + i] for i in range(3))
    n = GROUPS1
    packed_first(coef1, 0, b1, x1, d1, 1, n, g0)
    packed_step(1, coef1, 0, b1, x1, y1, d1, 2, n - 2, CARRY1, g1)
    packed_step(1, coef1, 0, b1, y1, x1, d1, 2, n - 2, CARRY2, g2)
    here = pl.ds(1 + OWN, OWN)
    values = []
    for t, (c, other, spread) in enumerate(packed_terms(x1, 1 + OWN, OWN, 1)):
        res = b1[t, here] - coef1[2, t, here] * c + coef1[1, t, here] * other + spread
        values.append(restrict_12([res[j : j + 1] for j in range(OWN)]))
        to_far[1 + t : 2 + t] = fields2[t, 1:2]
    value = jnp.where((sub_of() & 2) == 0, values[0], values[1])
    for ref in (packet, to_first, to_second, to_far):
        ref[0:1] = value
    to_first[1:] = edge_a[...]
    to_second[1:] = edge_b[...]


def rest_kernel(
    own2, near_a, near_b, far_a, far_b, gain, coef1, fields2, keep0, iterate, keep1, out, coef2, d1, b2, x2, y2, d2, xu, yu, x0, y0, d0
):
    rows = out.shape[0] // (2 * Z)
    even = (sub_of() & 1) == 0
    b1, x1 = keep1.at[0], keep1.at[1]

    even_y, low = is_even("gy"), lax.rem(lax.axis_index("gy"), 4) < 2
    at = slice(0, 1)
    parts = [
        next_of(low, far_a, far_b, at),
        prev_of(even_y, near_a, near_b, at),
        own2[at],
        next_of(even_y, near_a, near_b, at),
        prev_of(low, far_a, far_b, at),
    ]
    for t, values in enumerate(split_fields2(jnp.concatenate(parts, axis=0))):
        b2[t, 1 : SIZE2 - 1] = values
        at = slice(1 + t, 2 + t)
        parts = [next_of(low, far_a, far_b, at), fields2[t], prev_of(low, far_a, far_b, at)]
        inverse, other, _ = packed_jacobian(*split_fields2(jnp.concatenate(parts, axis=0)), 2)
        coef2[0, t, 1 : SIZE2 - 1] = inverse
        coef2[1, t, 1 : SIZE2 - 1] = other

    n = HI2 - LO2
    g0, g1, g2 = (gain[6 + i] for i in range(3))
    packed_first(coef2, 0, b2, x2, d2, 1, n, g0)
    packed_step(2, coef2, 0, b2, x2, y2, d2, 1, n, CARRY1, g1)
    packed_step(2, coef2, 0, b2, y2, x2, d2, 1, n, CARRY2, g2)
    packed_step(2, coef2, 0, b2, x2, y2, d2, 1, n, None, g0)
    packed_step(2, coef2, 0, b2, y2, x2, d2, 2, n - 2, CARRY1, g1)
    packed_step(2, coef2, 0, b2, x2, y2, d2, 2, n - 2, CARRY2, g2)

    g0, g1, g2 = (gain[3 + i] for i in range(3))
    shift = LO_UP - LO1
    for t in (0, 1):
        for g in range(LO_UP, HI_UP):
            p = g % 4
            value = y2[t, g // 4 - LO2 + 1 : g // 4 - LO2 + 2]
            value = spread_x(spread_x(value, 1, p & 1), 2, p & 2)
            at = g - LO_UP + 1
            xu[t, at : at + 1] = x1[t, at + shift : at + shift + 1] + value
    n = HI_UP - LO_UP
    packed_step(1, coef1, shift, b1, xu, yu, d1, 2, n - 2, None, g0)
    packed_step(1, coef1, shift, b1, yu, xu, d1, 2, n - 2, CARRY1, g1)
    packed_step(1, coef1, shift, b1, xu, yu, d1, 3, n - 4, CARRY2, g2)

    g0, g1, g2 = (gain[i] for i in range(3))
    for i in (0, 1):
        for at, take in ((HALO0 - EDGE, prev_of), (HALO0 + rows, next_of)):
            whole = take(even_y, near_a, near_b, slice(1, 1 + EDGE_TILES))
            x0[i, 0, at : at + EDGE] = whole[i * EDGE : (i + 1) * EDGE]
            for j in range(EDGE):
                x0[i, 1, at + j : at + j + 1] = roll_x(whole[2 * EDGE :], -(4 + 8 * (i * EDGE + j)))
        for t in (0, 1):
            x0[i, t, HALO0 : HALO0 + rows] = iterate[i, t]
    for t in (0, 1):
        for row in range(-2, rows // 2 + 2):
            at = row // 2 - LO_UP + 1
            value = spread_x(yu[t, at : at + 1], 1, row & 1)
            for i, fine in enumerate((jnp.where(even, value, roll_z(value, 1)), jnp.where(even, roll_z(value, -1), value))):
                for y in (2 * row, 2 * row + 1):
                    if -EDGE <= y < rows + EDGE:
                        x0[i, t, y + HALO0 : y + HALO0 + 1] = x0[i, t, y + HALO0 : y + HALO0 + 1] + fine
    total = rows + 2 * HALO0
    for r, n in chunks(2, total - 2):
        cheb_step(0, keep0, x0, y0, d0, r, n, None, g0)
    for r, n in chunks(3, total - 3):
        cheb_step(0, keep0, y0, x0, d0, r, n, CARRY1, g1)
    for r, n in chunks(4, total - 4):
        last = cheb_step(0, keep0, x0, None, d0, r, n, CARRY2, g2, (0,))[0]
        for i in (0, 1):
            for j in range(n):
                out[pl.ds(i * Z * rows + r - HALO0 + j, Z, stride=rows), :] = last[i][j]


def call(kernel, out_shapes, scratch, *args, space=pltpu.VMEM, outs=None):
    out = [jax.ShapeDtypeStruct(shape, jnp.float32) for shape in out_shapes]
    return pl.pallas_call(
        kernel,
        out_shape=out,
        in_specs=[pl.BlockSpec(memory_space=space)] * len(args),
        out_specs=[pl.BlockSpec(memory_space=m) for m in outs or [pltpu.VMEM] * len(out)],
        scratch_shapes=[pltpu.VMEM(s, jnp.float32) if isinstance(s, tuple) else s for s in scratch],
        compiler_params=pltpu.CompilerParams(vmem_limit_bytes=24 * 2**20),
    )(*args)


def swap(value, axis, step):
    count = lax.axis_size(axis)
    assert count % 2 == 0
    pairs = [(i, (i + step) % count) for i in range(0, count, 2)]
    return lax.ppermute(value, axis, pairs + [(j, i) for i, j in pairs])


def swap_far(value, axis, step):
    count = lax.axis_size(axis)
    assert count % 4 == 0
    pairs = [(i + j, (i + j + 2 * step) % count) for i in range(0, count, 4) for j in (0, 1)]
    return lax.ppermute(value, axis, pairs + [(j, i) for i, j in pairs])


def exchange(first, second, axis):
    return swap(first, axis, -1), swap(second, axis, 1)


def body(state, previous, feed, kill):
    _, depth, rows, cols = state.shape
    assert depth == Z and cols == X and rows == 4 * OWN
    across, count = lax.axis_size("gx"), lax.axis_size("gy")
    total0 = rows + 2 * HALO0
    state = state.reshape(2 * Z * rows, X)
    previous = previous.reshape(2 * Z * rows, X)
    feed = feed.reshape(Z * rows, X)
    kill = kill.reshape(Z * rows, X)
    inputs = (state, previous, feed, kill)

    strip = (PACKET, Z, X)
    spread_shape = (across * count, Z // 2, X)
    first, second, coarse, spread, *inputs = call(
        functools.partial(first_kernel, rows),
        [strip, strip, (2 * OWN + 1, Z, X), spread_shape, *(a.shape for a in inputs)],
        [pltpu.SemaphoreType.DMA((4,)), spread_shape, pltpu.SemaphoreType.DMA],
        *(pltpu.with_memory_space_constraint(a, pltpu.HBM) for a in inputs),
        space=pltpu.HBM,
        outs=[pltpu.VMEM] * 3 + [pltpu.HBM] + [pltpu.VMEM] * 4,
    )
    y_packets = exchange(first, second, "gy")

    tiles = tiles_for(6 * rows + 2 * OWN + 1)
    first, second, main = call(
        functools.partial(pack_own_kernel, rows),
        [(tiles, Z, X), (tiles, Z, X), (6, rows, Z, X)],
        [(PER * tiles, Z, X)],
        *inputs,
        coarse,
    )
    own_x = exchange(first, second, "gx")
    spread = lax.all_to_all(spread, ("gx", "gy"), 0, 0, tiled=True)
    tiles = tiles_for(2 * PACKET)
    corner_x = exchange(
        *call(pack_corner_kernel, [(tiles, Z, X), (tiles, Z, X)], [(PER * tiles, Z, X)], *y_packets), "gx"
    )

    strip, edge = (2 * OWN - 1, Z, X), (EDGE_TILES, Z, X)
    pair0 = (2, 2, total0, Z, X)
    work = [(6, 2, total0, Z, X), (6, 2, total0, Z, X), pair0, pair0, pair0, pair0]
    four = (4, 2, OWN, Z, X)
    inside = call(
        functools.partial(level0_inner_kernel, rows),
        [
            (6, 2, rows - 2, Z, X),
            (2, 2, 4, Z, X),
            (2, 2, rows - 4, Z, X),
            (2, 2, rows - 6, Z, X),
            (2, 2, 6, Z, X),
            four,
        ],
        work,
        main,
        *own_x,
    )
    keep_in, _, y1_in, y2_in, _, _ = inside
    keep_out, y1_out, y2_out, sources, edges = call(
        functools.partial(level0_outer_kernel, rows),
        [(6, 2, 8, Z, X), (2, 2, 4, Z, X), (2, 2, 6, Z, X), four, (3, 2, *edge)],
        work,
        main,
        *y_packets,
        *own_x,
        *corner_x,
        *inside,
    )
    own, first, second, edge_a, edge_b, gain = call(
        combine_kernel,
        [(2, OWN, Z, X), strip, strip, edge, edge, (POWERS + 3, Z, X)],
        [],
        sources,
        edges,
        spread,
    )
    coef1, keep0, iterate = call(
        functools.partial(coarse1_kernel, rows),
        [(3, 2, SIZE1, Z, X), (6, 2, total0, Z, X), (2, 2, rows, Z, X)],
        [(2, 2 * GROUPS1, Z, X)],
        coarse,
        *y_packets,
        *own_x,
        *corner_x,
        gain,
        keep_in,
        y1_in,
        y2_in,
        keep_out,
        y1_out,
        y2_out,
    )
    (fields2,) = call(
        functools.partial(fields2_kernel, rows), [(2, 3, Z, X)], [], coarse, *y_packets, *own_x, *corner_x
    )
    b_packets = exchange(first, second, "gy")

    one, two, up = (2, SIZE1, Z, X), (2, SIZE2, Z, X), (2, SIZE_UP, Z, X)
    near = (1 + EDGE_TILES, Z, X)
    packet, first, second, to_far, keep1 = call(
        level1_kernel,
        [(1, Z, X), near, near, (3, Z, X), (2, *one)],
        [one, one],
        own,
        *b_packets,
        edge_a,
        edge_b,
        fields2,
        coef1,
        gain,
    )
    far = (swap_far(to_far, "gy", 1), swap_far(to_far, "gy", -1))
    near = exchange(first, second, "gy")

    (out,) = call(
        rest_kernel,
        [(2 * Z * rows, X)],
        [(2, *two), one, two, two, two, two, up, up, pair0, pair0, pair0],
        packet,
        *near,
        *far,
        gain,
        coef1,
        fields2,
        keep0,
        iterate,
        keep1,
    )
    return out.reshape(2, Z, rows, X)


def solution(mesh):
    placed = (
        P(None, None, "gy", "gx"),
        P(None, None, "gy", "gx"),
        P(None, "gy", "gx"),
        P(None, "gy", "gx"),
    )
    return jax.shard_map(
        body, mesh=mesh, in_specs=placed, out_specs=P(None, None, "gy", "gx"), check_vma=False
    )
```

```python
import functools

import jax
import jax.numpy as jnp
from jax import lax
from jax.experimental import pallas as pl
from jax.experimental.pallas import tpu as pltpu
from jax.sharding import PartitionSpec as P

DIFF = (40.0, 20.0)
INV_STEP = 2.0
LOWER = 0.25

_CENTRE = (1.0 + LOWER) / 2.0
_HALF = (1.0 - LOWER) / 2.0
_SIGMA = _CENTRE / _HALF
_RHO0 = 1.0 / _SIGMA
_RHO1 = 1.0 / (2.0 * _SIGMA - _RHO0)
_RHO2 = 1.0 / (2.0 * _SIGMA - _RHO1)

Z = 8
X = 128
HALO0 = 4
SENT = 3
FIELDS1 = 6 * SENT
FIELDS2 = FIELDS1 + 8
PACKET = FIELDS2 + 1
WIDE = 42
PER = X // WIDE
EDGE = 3

LO1, HI1 = -4, 8
LO2, HI2 = -2, 3
LO_UP, HI_UP = -3, 7
SIZE1, SIZE2, SIZE_UP = HI1 - LO1 + 2, HI2 - LO2 + 2, HI_UP - LO_UP + 2
OWN = 4


def lane_of():
    return lax.broadcasted_iota(jnp.int32, (1, Z, X), 2)


def sub_of():
    return lax.broadcasted_iota(jnp.int32, (1, Z, X), 1)


def roll_x(tile, shift):
    shift = shift % X
    return pltpu.roll(tile, shift, 2) if shift else tile


def roll_z(tile, shift):
    shift = shift % Z
    return pltpu.roll(tile, shift, 1) if shift else tile


def chunks(lo, hi, step=4):
    return [(r, min(step, hi - r)) for r in range(lo, hi, step)]


def neighbour_sums(read, r, n, k, tiles=(0, 1)):
    lane = lane_of()
    low, high = lane < k, lane >= X - k
    centre = [read(t, r, n) for t in (0, 1)]
    right = [roll_x(c, k) for c in centre]
    left = [roll_x(c, -k) for c in centre]
    sums = []
    for t in tiles:
        c = centre[t]
        along_x = jnp.where(low, right[1 - t], right[t]) + jnp.where(high, left[1 - t], left[t])
        along_y = read(t, r - 1, n) + read(t, r + 1, n)
        along_z = 2.0 * roll_z(c, k) if 2 * k == Z else roll_z(c, k) + roll_z(c, -k)
        sums.append(along_x + along_y + along_z)
    return centre, sums


def jacobian(u, v, f, k, level):
    scale = 0.25**level
    product = u * v
    squared = v * v
    first = INV_STEP + squared + f + 6.0 * DIFF[0] * scale
    second = INV_STEP + f + k - 2.0 * product + 6.0 * DIFF[1] * scale
    return 2.0 * product, squared, 1.0 / first, 1.0 / second, first, second


def cheb_step(level, keep, source, target, d, r, n, carry, gain, tiles=(0, 1)):
    scale = 0.25**level
    k = 1 << level
    u, nb_u = neighbour_sums(lambda t, a, m: source[0, t, pl.ds(a, m)], r, n, k, tiles)
    v, nb_v = neighbour_sums(lambda t, a, m: source[1, t, pl.ds(a, m)], r, n, k, tiles)
    rows = pl.ds(r, n)
    out = []
    for t in tiles:
        cross, squared, inv_u, inv_v = (keep[i, t, rows] for i in range(4))
        res_u = inv_u * (keep[4, t, rows] - cross * v[t] + DIFF[0] * scale * nb_u[t]) - u[t]
        res_v = inv_v * (keep[5, t, rows] + squared * u[t] + DIFF[1] * scale * nb_v[t]) - v[t]
        du, dv = gain * res_u, gain * res_v
        if carry is not None:
            du = du + carry * d[0, t, rows]
            dv = dv + carry * d[1, t, rows]
        if target is not None:
            d[0, t, rows] = du
            d[1, t, rows] = dv
            target[0, t, rows] = u[t] + du
            target[1, t, rows] = v[t] + dv
        out.append((u[t] + du, v[t] + dv))
    return out


def next_power(keep, source, r, n):
    u, nb_u = neighbour_sums(lambda t, a, m: source[0, t, pl.ds(a, m)], r, n, 1)
    v, nb_v = neighbour_sums(lambda t, a, m: source[1, t, pl.ds(a, m)], r, n, 1)
    rows = pl.ds(r, n)
    first, second = [], []
    for t in (0, 1):
        cross, squared, inv_u, inv_v = (keep[i, t, rows] for i in range(4))
        first.append(u[t] + inv_u * (cross * v[t] - DIFF[0] * nb_u[t]))
        second.append(v[t] - inv_v * (squared * u[t] + DIFF[1] * nb_v[t]))
    return first, second


CARRY1 = _RHO1 * _RHO0
CARRY2 = _RHO2 * _RHO1


POWERS = 9


def write_gains(spread, out):
    lane = lax.broadcasted_iota(jnp.int32, (1, X), 1)
    for level in range(3):
        top = jnp.max(jnp.where(lane == level, spread, 0.0), axis=1, keepdims=True)
        tau = 1.0 / (1.0 + jnp.broadcast_to(top, (Z, X)))
        for i, factor in enumerate((1.0 / _CENTRE, 2.0 * _RHO1 / _HALF, 2.0 * _RHO2 / _HALF)):
            out[3 * level + i] = factor * tau
    g0, g1, g2 = (out[i] for i in range(3))
    first, second = g0 + CARRY1 * g0 + g1, g1 * g0
    out[POWERS] = first + CARRY2 * (CARRY1 * g0 + g1) + g2
    out[POWERS + 1] = second + CARRY2 * second + g2 * first
    out[POWERS + 2] = g2 * second


def pair_rows(value):
    n = value.shape[0] // 2
    pairs = value.reshape(n, 2, Z, X)
    return pairs[:, 0] + pairs[:, 1]


def restrict_01(first, second):
    lane, sub = lane_of(), sub_of()
    across = []
    for value in (first, second):
        a, b = value[0:1], value[1:2]
        across.append(jnp.where((lane & 1) == 0, a + roll_x(a, -1), b + roll_x(b, 1)))
    a, b = across
    return 0.125 * jnp.where((sub & 1) == 0, a + roll_z(a, -1), b + roll_z(b, 1))


def restrict_12(groups):
    lane, sub = lane_of(), sub_of()
    out = None
    for p, value in enumerate(groups):
        value = value + roll_x(value, 1 if p & 1 else -1)
        value = value + roll_x(value, 2 if p & 2 else -2)
        out = value if out is None else jnp.where((lane & 3) == p, value, out)
    return 0.125 * (out + jnp.where((sub & 2) == 0, roll_z(out, -2), roll_z(out, 2)))


def spread_x(tile, k, phase):
    return jnp.where((lane_of() & k) == phase, tile, roll_x(tile, -k if phase else k))


def packed_jacobian(uv, fk, level):
    scale = 0.25**level
    even = (sub_of() & 1) == 0
    u, v = jnp.where(even, uv, roll_z(uv, 1)), jnp.where(even, roll_z(uv, -1), uv)
    f, k = jnp.where(even, fk, roll_z(fk, 1)), jnp.where(even, roll_z(fk, -1), fk)
    product, squared = u * v, v * v
    diag = jnp.where(
        even,
        INV_STEP + squared + f + 6.0 * DIFF[0] * scale,
        INV_STEP + f + k - 2.0 * product + 6.0 * DIFF[1] * scale,
    )
    return 1.0 / diag, jnp.where(even, -2.0 * product, squared), diag


def packed_spread(uv, fk, level):
    scale = 0.25**level
    even = (sub_of() & 1) == 0
    inverse, other, _ = packed_jacobian(uv, fk, level)
    return jnp.where(even, 6.0 * DIFF[0] * scale - other, 6.0 * DIFF[1] * scale + other) * inverse


def packed_terms(source, g, n, level):
    k = 1 << level
    lane, sub = lane_of(), sub_of()
    even = (sub & 1) == 0
    first, last = (lane & (k - 1)) == 0, (lane & (k - 1)) == k - 1
    low, high = lane < k, lane >= X - k
    diff = jnp.where(even, DIFF[0] * 0.25**level, DIFF[1] * 0.25**level)
    wide = [source[t, pl.ds(g - 1, n + 2)] for t in (0, 1)]
    centre = [w[1 : n + 1] for w in wide]
    right = [roll_x(c, k) for c in centre]
    left = [roll_x(c, -k) for c in centre]
    out = []
    for t in (0, 1):
        c, w = centre[t], wide[t]
        total = jnp.where(low, right[1 - t], right[t]) + jnp.where(high, left[1 - t], left[t])
        if k == 2:
            ahead, back = roll_x(w, 1), roll_x(w, -1)
            total = total + jnp.where(first, back[0:n], ahead[1 : n + 1])
            total = total + jnp.where(last, ahead[2 : n + 2], back[1 : n + 1])
            total = total + roll_z(c, 2) + roll_z(c, -2)
        else:
            total = total + jnp.where(first, roll_x(w[0:n], -(k - 1)), roll_x(c, 1))
            total = total + jnp.where(last, roll_x(w[2 : n + 2], k - 1), roll_x(c, -1))
            total = total + 2.0 * roll_z(c, 4)
        other = jnp.where(even, roll_z(c, -1), roll_z(c, 1))
        out.append((c, other, diff * total))
    return out


def packed_first(coef, shift, b, target, d, g, n, gain):
    for t in (0, 1):
        value = gain * coef[0, t, pl.ds(g + shift, n)] * b[t, pl.ds(g + shift, n)]
        d[t, pl.ds(g, n)] = value
        target[t, pl.ds(g, n)] = value


def packed_step(level, coef, shift, b, source, target, d, g, n, carry, gain):
    for t, (c, other, spread) in enumerate(packed_terms(source, g, n, level)):
        at = pl.ds(g + shift, n)
        res = coef[0, t, at] * (b[t, at] + coef[1, t, at] * other + spread) - c
        delta = gain * res
        if carry is not None:
            delta = delta + carry * d[t, pl.ds(g, n)]
        d[t, pl.ds(g, n)] = delta
        target[t, pl.ds(g, n)] = c + delta


def plane(ref, f, y, rows):
    return ref[pl.ds(f * Z * rows + y, Z, stride=rows), :]


def is_even(axis):
    return lax.rem(lax.axis_index(axis), 2) == 0


def prev_of(even, first, second, at):
    return jnp.where(even, first[at], second[at])


def next_of(even, first, second, at):
    return jnp.where(even, second[at], first[at])


SOURCES = ((0, 0), (0, 1), (1, 0), (1, 1), (2, 0), (3, 0))


def first_kernel(rows, state, previous, feed, kill, first, second, coarse, *rest):
    held, sems = rest[:4], rest[4]
    copies = [
        pltpu.make_async_copy(ref, to, sems.at[i]) for i, (ref, to) in enumerate(zip((state, previous, feed, kill), held))
    ]
    for copy in copies:
        copy.start()
    for copy in copies:
        copy.wait()
    even = is_even("gy")
    values = []
    for i, (j, f) in enumerate(SOURCES):
        wanted = range(rows) if i not in (2, 3) else [*range(SENT), *range(rows - SENT, rows)]
        values.append({y: plane(held[j], f, y, rows)[None] for y in wanted})
    for i in (2, 3):
        weight = DIFF[i - 2] / INV_STEP
        values[i][SENT - 1] = values[i][SENT - 1] + weight * values[i - 2][SENT]
        values[i][rows - SENT] = values[i][rows - SENT] + weight * values[i - 2][rows - SENT - 1]
    for i in range(6):
        for y in range(SENT):
            top, bottom = values[i][y], values[i][rows - SENT + y]
            at = slice(i * SENT + y, i * SENT + y + 1)
            first[at] = jnp.where(even, top, bottom)
            second[at] = jnp.where(even, bottom, top)
    pairs = []
    for p, (i, j) in enumerate(((0, 1), (4, 5))):
        parts = []
        for g in range(OWN):
            sums = [
                jnp.concatenate([value[4 * g + 2 * q] + value[4 * g + 2 * q + 1] for q in (0, 1)], axis=0)
                for value in (values[i], values[j])
            ]
            parts.append(restrict_01(*sums))
        pairs.append(jnp.concatenate(parts, axis=0))
        coarse[p * OWN : (p + 1) * OWN] = pairs[p]
        for ref in (first, second):
            ref[FIELDS1 + p * OWN : FIELDS1 + (p + 1) * OWN] = pairs[p]
    uv, fk = (restrict_12([pair[j : j + 1] for j in range(OWN)]) for pair in pairs)
    both = jnp.where((sub_of() & 2) == 0, uv, fk)
    coarse[2 * OWN : 2 * OWN + 1] = both
    for ref in (first, second):
        ref[FIELDS2 : FIELDS2 + 1] = both


def split_fields2(both):
    low = (sub_of() & 2) == 0
    return jnp.where(low, both, roll_z(both, 2)), jnp.where(low, roll_z(both, -2), both)


def write_spread(fields, coarse, out):
    lane = lax.broadcasted_iota(jnp.int32, (1, X), 1)
    cross, squared, inv_u, inv_v, _, _ = jacobian(*fields, 0)
    tops = [jnp.max(jnp.maximum((6.0 * DIFF[0] + cross) * inv_u, (6.0 * DIFF[1] + squared) * inv_v), axis=0)]
    tops.append(jnp.max(packed_spread(coarse[0:OWN], coarse[OWN : 2 * OWN], 1), axis=0))
    tops.append(packed_spread(*split_fields2(coarse[2 * OWN : 2 * OWN + 1]), 2)[0])
    result = jnp.zeros((1, X), jnp.float32)
    for level, top in enumerate(tops):
        top = jnp.max(jnp.max(top, axis=0, keepdims=True), axis=1, keepdims=True)
        result = jnp.where(lane == level, jnp.broadcast_to(top, (1, X)), result)
    out[...] = jnp.broadcast_to(result[None], out.shape)


GROUPS1 = HI1 - LO1
GROUPS2 = HI2 - LO2


def tiles_for(entries):
    return -(-entries // PER)


def pack_edges(entries, even, first, second):
    lane = lane_of()
    share = first.shape[0]
    left, right = None, None
    for j in range(PER):
        part = entries[j * share : (j + 1) * share]
        a, b = roll_x(part, WIDE * j), roll_x(part, WIDE + WIDE * j)
        left = a if left is None else jnp.where(lane >= WIDE * j, a, left)
        right = b if right is None else jnp.where(lane >= WIDE * j, b, right)
    first[...] = jnp.where(even, left, right)
    second[...] = jnp.where(even, right, left)


def halo_tiles(even, packets, lo, hi):
    first, second = packets
    share = first.shape[0]
    lane = lane_of()
    out = []
    for j in range(PER):
        a, b = max(lo, j * share), min(hi, (j + 1) * share)
        if a < b:
            strip = slice(a - j * share, b - j * share)
            left, right = prev_of(even, first, second, strip), next_of(even, first, second, strip)
            value = jnp.where(lane < X // 2, roll_x(right, -WIDE * j), roll_x(left, X - WIDE - WIDE * j))
            out.append((a - lo, b - lo, value))
    return out


def pack_own_kernel(
    rows, state, previous, feed, kill, coarse, first, second, spread, main, held, copies, sem
):
    inputs = (state, previous, feed, kill)

    def field(i):
        j, f = SOURCES[i]
        return jnp.stack([plane(inputs[j], f, y, rows) for y in range(rows)])

    fields = {i: field(i) for i in (0, 1, 4, 5)}
    write_spread([fields[i] for i in (0, 1, 4, 5)], coarse, copies)
    copy = pltpu.make_async_copy(copies, spread, sem)
    copy.start()
    for i in range(6):
        value = fields[i] if i in fields else field(i)
        main[i] = value
        held[i * rows : (i + 1) * rows] = value
    held[6 * rows : 6 * rows + 2 * OWN + 1] = coarse[...]
    pack_edges(held, is_even("gx"), first, second)
    copy.wait()


def pack_corner_kernel(y_first, y_second, first, second, held):
    even = is_even("gy")
    every = slice(0, PACKET)
    held[0:PACKET] = prev_of(even, y_first, y_second, every)
    held[PACKET : 2 * PACKET] = next_of(even, y_first, y_second, every)
    pack_edges(held, is_even("gx"), first, second)


EDGE_TILES = 2 * EDGE + 1


def level0_setup(fields, keep, diag, power, r, n):
    at = pl.ds(r, n)
    u, nb_u = neighbour_sums(lambda t, a, m: fields[0, t, pl.ds(a, m)], r, n, 1)
    v, nb_v = neighbour_sums(lambda t, a, m: fields[1, t, pl.ds(a, m)], r, n, 1)
    for t in (0, 1):
        f, k = fields[4, t, at], fields[5, t, at]
        cross, squared, inv_u, inv_v, first, second = jacobian(u[t], v[t], f, k, 0)
        react = u[t] * squared
        b_u = DIFF[0] * (nb_u[t] - 6.0 * u[t]) - INV_STEP * (u[t] - fields[2, t, at]) - react + f * (1.0 - u[t])
        b_v = DIFF[1] * (nb_v[t] - 6.0 * v[t]) - INV_STEP * (v[t] - fields[3, t, at]) + react - (f + k) * v[t]
        for i, value in enumerate((cross, squared, inv_u, inv_v, b_u, b_v)):
            keep[i, t, at] = value
        for i, value in enumerate((first, second)):
            diag[i, t, at] = value
        for i, value in enumerate((inv_u * b_u, inv_v * b_v)):
            power[i, t, at] = value


def level0_power(keep, source, target, r, n):
    for i, values in enumerate(next_power(keep, source, r, n)):
        for t in (0, 1):
            target[i, t, pl.ds(r, n)] = values[t]


def level0_down(keep, diag, y1, y2, sources, r, n):
    at = pl.ds(r, n)
    last = next_power(keep, y2, r, n)
    for t in (0, 1):
        both = [diag[i, t, at] for i in (0, 1)]
        parts = [[keep[4 + i, t, at] for i in (0, 1)]]
        parts += [[both[i] * power[i, t, at] for i in (0, 1)] for power in (y1, y2)]
        parts.append([both[i] * last[i][t] for i in (0, 1)])
        for q, part in enumerate(parts):
            u, v = (pair_rows(value) for value in part)
            for j in range(n // 4):
                value = restrict_01(u[2 * j : 2 * j + 2], v[2 * j : 2 * j + 2])
                sources[q, t, pl.ds((r - HALO0) // 4 + j, 1)] = value


def inner(rows, lost):
    return slice(HALO0 + lost, HALO0 + rows - lost)


def ends(rows, lo, hi):
    total = rows + 2 * HALO0
    return slice(lo, hi), slice(total - hi, total - lo)


def put_ends(target, rows, lo, hi, source):
    n = hi - lo
    for at, part in zip(ends(rows, lo, hi), (slice(0, n), slice(n, 2 * n))):
        for i in range(target.shape[0]):
            for t in (0, 1):
                target[i, t, at] = source[i, t, part]


def take_ends(source, rows, lo, hi, target):
    n = hi - lo
    for at, part in zip(ends(rows, lo, hi), (slice(0, n), slice(n, 2 * n))):
        for i in range(source.shape[0]):
            for t in (0, 1):
                target[i, t, part] = source[i, t, at]


def level0_inner_kernel(rows, main, own_a, own_b, keep_in, y0_in, y1_in, y2_in, diag_in, sources_in, *scratch):
    fields, keep, diag, y0, y1, y2 = scratch
    even_x = is_even("gx")
    for i in range(6):
        fields[i, 0, HALO0 : HALO0 + rows] = main[i]
        for a, b, value in halo_tiles(even_x, (own_a, own_b), i * rows, (i + 1) * rows):
            fields[i, 1, HALO0 + a : HALO0 + b] = value
    first = HALO0 + 1
    level0_setup(fields, keep, diag, y0, first, rows - 2)
    level0_power(keep, y0, y1, first + 1, rows - 4)
    level0_power(keep, y1, y2, first + 2, rows - 6)
    level0_down(keep, diag, y1, y2, sources_in, first + 3, rows - 8)
    for source, target, lost in ((keep, keep_in, 1), (y1, y1_in, 2), (y2, y2_in, 3)):
        for i in range(source.shape[0]):
            for t in (0, 1):
                target[i, t] = source[i, t, inner(rows, lost)]
    take_ends(y0, rows, HALO0 + 1, HALO0 + 3, y0_in)
    take_ends(diag, rows, HALO0 + 1, HALO0 + 4, diag_in)


def level0_outer_kernel(
    rows,
    main,
    y_first,
    y_second,
    own_a,
    own_b,
    corner_a,
    corner_b,
    keep_in,
    y0_in,
    y1_in,
    y2_in,
    diag_in,
    sources_in,
    keep_out,
    y1_out,
    y2_out,
    sources,
    edges,
    *scratch,
):
    fields, keep, diag, y0, y1, y2 = scratch
    even, even_x = is_even("gy"), is_even("gx")
    total = rows + 2 * HALO0
    near, skip = HALO0 + 2, HALO0 - SENT
    for i in range(6):
        strip = slice(i * SENT, (i + 1) * SENT)
        fields[i, 0, skip:HALO0] = prev_of(even, y_first, y_second, strip)
        fields[i, 0, HALO0:near] = main[i, 0:2]
        fields[i, 0, total - near : total - HALO0] = main[i, rows - 2 : rows]
        fields[i, 0, HALO0 + rows : total - skip] = next_of(even, y_first, y_second, strip)
        for packets, lo, n, at in (
            ((corner_a, corner_b), i * SENT, SENT, skip),
            ((own_a, own_b), i * rows, 2, HALO0),
            ((own_a, own_b), (i + 1) * rows - 2, 2, total - near),
            ((corner_a, corner_b), PACKET + i * SENT, SENT, HALO0 + rows),
        ):
            for a, b, value in halo_tiles(even_x, packets, lo, lo + n):
                fields[i, 1, at + a : at + b] = value
    for i in (0, 1):
        for t in (0, 1):
            for at in (0, total - 1):
                fields[i, t, at] = jnp.zeros((Z, X), jnp.float32)
    for at, part in zip(ends(rows, 5, 8), (slice(0, 3), slice(rows - 5, rows - 2))):
        for i in range(6):
            for t in (0, 1):
                keep[i, t, at] = keep_in[i, t, part]
    put_ends(diag, rows, 5, 8, diag_in)
    put_ends(y0, rows, 5, 7, y0_in)
    for target, source, lost in ((y1, y1_in, 2), (y2, y2_in, 3)):
        n = rows - 2 * lost
        for at, part in zip(ends(rows, HALO0 + lost, HALO0 + lost + 2), (slice(0, 2), slice(n - 2, n))):
            for i in (0, 1):
                for t in (0, 1):
                    target[i, t, at] = source[i, t, part]
    for r in (1, total - 5):
        level0_setup(fields, keep, diag, y0, r, 4)
    for r in (2, total - 6):
        level0_power(keep, y0, y1, r, 4)
    for r in (3, total - 7):
        level0_power(keep, y1, y2, r, 4)
    for r in (4, total - 8):
        level0_down(keep, diag, y1, y2, sources, r, 4)
    for q in range(4):
        for t in (0, 1):
            sources[q, t, 1 : OWN - 1] = sources_in[q, t, 1 : OWN - 1]
    take_ends(keep, rows, 1, 5, keep_out)
    take_ends(y1, rows, 4, 6, y1_out)
    take_ends(y2, rows, 4, 7, y2_out)
    for p, power in enumerate((y0, y1, y2)):
        for side, start in enumerate((HALO0, HALO0 + rows - EDGE)):
            edges[p, side] = pack_rows(power, start)


def pack_rows(x, start):
    lane = lane_of()
    halo = None
    for i in (0, 1):
        for j in range(EDGE):
            at = i * EDGE + j
            value = roll_x(x[i, 1, start + j : start + j + 1], 4 + 8 * at)
            halo = value if halo is None else jnp.where((lane >> 3) == at, value, halo)
    return jnp.concatenate([x[i, 0, start : start + EDGE] for i in (0, 1)] + [halo], axis=0)


def squeeze(halo):
    lane = lane_of()
    last = halo[OWN - 1 : OWN]
    ahead = (lane >= WIDE) & (lane < 2 * WIDE)
    parts = [jnp.where(ahead, roll_x(last, WIDE), halo[0:1]), jnp.where(ahead, roll_x(last, 2 * WIDE - X), halo[1:2])]
    return jnp.concatenate(parts + [halo[2 : OWN - 1]], axis=0)


def unsqueeze(tiles):
    last = jnp.where(lane_of() < X // 2, roll_x(tiles[0:1], -WIDE), roll_x(tiles[1:2], X - 2 * WIDE))
    return jnp.concatenate([tiles, last], axis=0)


def combine_kernel(sources, edges, spread, own, first, second, edge_first, edge_second, gain):
    write_gains(jnp.max(spread[...], axis=0)[0:1], gain)
    p0, p1, p2 = (gain[POWERS + i] for i in range(3))
    for t in (0, 1):
        value = sources[0, t] - p0 * sources[1, t] + p1 * sources[2, t] - p2 * sources[3, t]
        own[t] = value
        for ref in (first, second):
            if t == 0:
                ref[0:OWN] = value
            else:
                ref[OWN:] = squeeze(value)
    even = is_even("gy")
    top, bottom = (p0 * edges[0, side] - p1 * edges[1, side] + p2 * edges[2, side] for side in (0, 1))
    edge_first[...] = jnp.where(even, top, bottom)
    edge_second[...] = jnp.where(even, bottom, top)


def coarse1_kernel(
    rows, coarse, y_first, y_second, own_a, own_b, corner_a, corner_b, gain, keep_in, y1_in, y2_in, keep_out, y1_out, y2_out,
    coef, keep0, x0, fields
):
    even, even_x = is_even("gy"), is_even("gx")
    own_x, corner_x = (own_a, own_b), (corner_a, corner_b)
    for p in (0, 1):
        to = p * GROUPS1
        strip = slice(FIELDS1 + p * OWN, FIELDS1 + (p + 1) * OWN)
        fields[0, to : to + OWN] = prev_of(even, y_first, y_second, strip)
        fields[0, to + OWN : to + 2 * OWN] = coarse[p * OWN : (p + 1) * OWN]
        fields[0, to + 2 * OWN : to + 3 * OWN] = next_of(even, y_first, y_second, strip)
        for part, (packets, lo) in enumerate(
            ((corner_x, FIELDS1), (own_x, 6 * rows), (corner_x, PACKET + FIELDS1))
        ):
            lo += p * OWN
            for a, b, value in halo_tiles(even_x, packets, lo, lo + OWN):
                fields[1, to + part * OWN + a : to + part * OWN + b] = value
    for t in (0, 1):
        for i, value in enumerate(packed_jacobian(fields[t, 0:GROUPS1], fields[t, GROUPS1 : 2 * GROUPS1], 1)):
            coef[i, t, 1 : SIZE1 - 1] = value

    def whole(inside, outside):
        n = outside.shape[0] // 2
        return jnp.concatenate([outside[0:n], inside, outside[n:]], axis=0)

    for i in range(6):
        for t in (0, 1):
            keep0[i, t, 1 : rows + 2 * HALO0 - 1] = whole(keep_in[i, t], keep_out[i, t])
    p0, p1, p2 = (gain[POWERS + i] for i in range(3))
    for i in (0, 1):
        for t in (0, 1):
            y0 = keep0[2 + i, t, HALO0 : HALO0 + rows] * keep0[4 + i, t, HALO0 : HALO0 + rows]
            y1, y2 = (whole(a[i, t], b[i, t]) for a, b in ((y1_in, y1_out), (y2_in, y2_out)))
            x0[i, t] = p0 * y0 - p1 * y1 + p2 * y2


def fields2_kernel(rows, coarse, y_first, y_second, own_a, own_b, corner_a, corner_b, out):
    even, even_x = is_even("gy"), is_even("gx")
    own_x, corner_x = (own_a, own_b), (corner_a, corner_b)
    near = slice(FIELDS2, FIELDS2 + 1)
    out[0, 0:1] = prev_of(even, y_first, y_second, near)
    out[0, 1:2] = coarse[2 * OWN : 2 * OWN + 1]
    out[0, 2:3] = next_of(even, y_first, y_second, near)
    for q, (packets, lo) in enumerate(
        ((corner_x, FIELDS2), (own_x, 6 * rows + 2 * OWN), (corner_x, PACKET + FIELDS2))
    ):
        out[1, q : q + 1] = halo_tiles(even_x, packets, lo, lo + 1)[0][2]


def level1_kernel(
    own, first, second, edge_a, edge_b, fields2, coef1, gain, packet, to_first, to_second, to_far, keep, y1, d1
):
    b1, x1 = keep.at[0], keep.at[1]
    even = is_even("gy")
    for t in (0, 1):
        b1[t, 1 + OWN : 1 + 2 * OWN] = own[t]
        for at, take in ((1, prev_of), (1 + 2 * OWN, next_of)):
            if t == 0:
                b1[t, at : at + OWN] = take(even, first, second, slice(0, OWN))
            else:
                b1[t, at : at + OWN] = unsqueeze(take(even, first, second, slice(OWN, 2 * OWN - 1)))
    g0, g1, g2 = (gain[3 + i] for i in range(3))
    n = GROUPS1
    packed_first(coef1, 0, b1, x1, d1, 1, n, g0)
    packed_step(1, coef1, 0, b1, x1, y1, d1, 2, n - 2, CARRY1, g1)
    packed_step(1, coef1, 0, b1, y1, x1, d1, 2, n - 2, CARRY2, g2)
    here = pl.ds(1 + OWN, OWN)
    values = []
    for t, (c, other, spread) in enumerate(packed_terms(x1, 1 + OWN, OWN, 1)):
        res = b1[t, here] - coef1[2, t, here] * c + coef1[1, t, here] * other + spread
        values.append(restrict_12([res[j : j + 1] for j in range(OWN)]))
        to_far[1 + t : 2 + t] = fields2[t, 1:2]
    value = jnp.where((sub_of() & 2) == 0, values[0], values[1])
    for ref in (packet, to_first, to_second, to_far):
        ref[0:1] = value
    to_first[1:] = edge_a[...]
    to_second[1:] = edge_b[...]


def rest_kernel(
    own2, near_a, near_b, far_a, far_b, gain, coef1, fields2, keep0, iterate, keep1, out, coef2, d1, b2, x2, y2, d2, xu, yu, x0, y0, d0
):
    rows = out.shape[0] // (2 * Z)
    even = (sub_of() & 1) == 0
    b1, x1 = keep1.at[0], keep1.at[1]

    even_y, low = is_even("gy"), lax.rem(lax.axis_index("gy"), 4) < 2
    at = slice(0, 1)
    parts = [
        next_of(low, far_a, far_b, at),
        prev_of(even_y, near_a, near_b, at),
        own2[at],
        next_of(even_y, near_a, near_b, at),
        prev_of(low, far_a, far_b, at),
    ]
    for t, values in enumerate(split_fields2(jnp.concatenate(parts, axis=0))):
        b2[t, 1 : SIZE2 - 1] = values
        at = slice(1 + t, 2 + t)
        parts = [next_of(low, far_a, far_b, at), fields2[t], prev_of(low, far_a, far_b, at)]
        inverse, other, _ = packed_jacobian(*split_fields2(jnp.concatenate(parts, axis=0)), 2)
        coef2[0, t, 1 : SIZE2 - 1] = inverse
        coef2[1, t, 1 : SIZE2 - 1] = other

    n = HI2 - LO2
    g0, g1, g2 = (gain[6 + i] for i in range(3))
    packed_first(coef2, 0, b2, x2, d2, 1, n, g0)
    packed_step(2, coef2, 0, b2, x2, y2, d2, 1, n, CARRY1, g1)
    packed_step(2, coef2, 0, b2, y2, x2, d2, 1, n, CARRY2, g2)
    packed_step(2, coef2, 0, b2, x2, y2, d2, 1, n, None, g0)
    packed_step(2, coef2, 0, b2, y2, x2, d2, 2, n - 2, CARRY1, g1)
    packed_step(2, coef2, 0, b2, x2, y2, d2, 2, n - 2, CARRY2, g2)

    g0, g1, g2 = (gain[3 + i] for i in range(3))
    shift = LO_UP - LO1
    for t in (0, 1):
        for g in range(LO_UP, HI_UP):
            p = g % 4
            value = y2[t, g // 4 - LO2 + 1 : g // 4 - LO2 + 2]
            value = spread_x(spread_x(value, 1, p & 1), 2, p & 2)
            at = g - LO_UP + 1
            xu[t, at : at + 1] = x1[t, at + shift : at + shift + 1] + value
    n = HI_UP - LO_UP
    packed_step(1, coef1, shift, b1, xu, yu, d1, 2, n - 2, None, g0)
    packed_step(1, coef1, shift, b1, yu, xu, d1, 2, n - 2, CARRY1, g1)
    packed_step(1, coef1, shift, b1, xu, yu, d1, 3, n - 4, CARRY2, g2)

    g0, g1, g2 = (gain[i] for i in range(3))
    sides = [take(even_y, near_a, near_b, slice(1, 1 + EDGE_TILES)) for take in (prev_of, next_of)]

    def before(i, t, y):
        if 0 <= y < rows:
            return iterate[i, t, y : y + 1]
        side, j = (sides[0], y + EDGE) if y < 0 else (sides[1], y - rows)
        if t == 0:
            return side[i * EDGE + j : i * EDGE + j + 1]
        return roll_x(side[2 * EDGE :], -(4 + 8 * (i * EDGE + j)))

    for t in (0, 1):
        for row in range(-2, rows // 2 + 2):
            at = row // 2 - LO_UP + 1
            value = spread_x(yu[t, at : at + 1], 1, row & 1)
            for i, fine in enumerate((jnp.where(even, value, roll_z(value, 1)), jnp.where(even, roll_z(value, -1), value))):
                for y in (2 * row, 2 * row + 1):
                    if -EDGE <= y < rows + EDGE:
                        x0[i, t, y + HALO0 : y + HALO0 + 1] = before(i, t, y) + fine
    total = rows + 2 * HALO0
    for r, n in chunks(2, total - 2):
        cheb_step(0, keep0, x0, y0, d0, r, n, None, g0)
    for r, n in chunks(3, total - 3):
        cheb_step(0, keep0, y0, x0, d0, r, n, CARRY1, g1)
    for r, n in chunks(4, total - 4):
        last = cheb_step(0, keep0, x0, None, d0, r, n, CARRY2, g2, (0,))[0]
        for i in (0, 1):
            for j in range(n):
                out[pl.ds(i * Z * rows + r - HALO0 + j, Z, stride=rows), :] = last[i][j]


def call(kernel, out_shapes, scratch, *args, space=pltpu.VMEM, outs=None):
    out = [jax.ShapeDtypeStruct(shape, jnp.float32) for shape in out_shapes]
    return pl.pallas_call(
        kernel,
        out_shape=out,
        in_specs=[pl.BlockSpec(memory_space=space)] * len(args),
        out_specs=[pl.BlockSpec(memory_space=m) for m in outs or [pltpu.VMEM] * len(out)],
        scratch_shapes=[pltpu.VMEM(s, jnp.float32) if isinstance(s, tuple) else s for s in scratch],
        compiler_params=pltpu.CompilerParams(vmem_limit_bytes=24 * 2**20),
    )(*args)


def swap(value, axis, step):
    count = lax.axis_size(axis)
    assert count % 2 == 0
    pairs = [(i, (i + step) % count) for i in range(0, count, 2)]
    return lax.ppermute(value, axis, pairs + [(j, i) for i, j in pairs])


def swap_far(value, axis, step):
    count = lax.axis_size(axis)
    assert count % 4 == 0
    pairs = [(i + j, (i + j + 2 * step) % count) for i in range(0, count, 4) for j in (0, 1)]
    return lax.ppermute(value, axis, pairs + [(j, i) for i, j in pairs])


def exchange(first, second, axis):
    return swap(first, axis, -1), swap(second, axis, 1)


def body(state, previous, feed, kill):
    _, depth, rows, cols = state.shape
    assert depth == Z and cols == X and rows == 4 * OWN
    across, count = lax.axis_size("gx"), lax.axis_size("gy")
    total0 = rows + 2 * HALO0
    state = state.reshape(2 * Z * rows, X)
    previous = previous.reshape(2 * Z * rows, X)
    feed = feed.reshape(Z * rows, X)
    kill = kill.reshape(Z * rows, X)
    inputs = (state, previous, feed, kill)

    strip = (PACKET, Z, X)
    first, second, coarse, *inputs = call(
        functools.partial(first_kernel, rows),
        [strip, strip, (2 * OWN + 1, Z, X), *(a.shape for a in inputs)],
        [pltpu.SemaphoreType.DMA((4,))],
        *(pltpu.with_memory_space_constraint(a, pltpu.HBM) for a in inputs),
        space=pltpu.HBM,
    )
    y_packets = exchange(first, second, "gy")

    tiles = tiles_for(6 * rows + 2 * OWN + 1)
    spread_shape = (across * count, Z // 2, X)
    first, second, spread, main = call(
        functools.partial(pack_own_kernel, rows),
        [(tiles, Z, X), (tiles, Z, X), spread_shape, (6, rows, Z, X)],
        [(PER * tiles, Z, X), spread_shape, pltpu.SemaphoreType.DMA],
        *inputs,
        coarse,
        outs=[pltpu.VMEM, pltpu.VMEM, pltpu.HBM, pltpu.VMEM],
    )
    own_x = exchange(first, second, "gx")
    spread = lax.all_to_all(spread, ("gx", "gy"), 0, 0, tiled=True)
    tiles = tiles_for(2 * PACKET)
    corner_x = exchange(
        *call(pack_corner_kernel, [(tiles, Z, X), (tiles, Z, X)], [(PER * tiles, Z, X)], *y_packets), "gx"
    )

    strip, edge = (2 * OWN - 1, Z, X), (EDGE_TILES, Z, X)
    pair0 = (2, 2, total0, Z, X)
    work = [(6, 2, total0, Z, X), (6, 2, total0, Z, X), pair0, pair0, pair0, pair0]
    four = (4, 2, OWN, Z, X)
    inside = call(
        functools.partial(level0_inner_kernel, rows),
        [
            (6, 2, rows - 2, Z, X),
            (2, 2, 4, Z, X),
            (2, 2, rows - 4, Z, X),
            (2, 2, rows - 6, Z, X),
            (2, 2, 6, Z, X),
            four,
        ],
        work,
        main,
        *own_x,
    )
    keep_in, _, y1_in, y2_in, _, _ = inside
    keep_out, y1_out, y2_out, sources, edges = call(
        functools.partial(level0_outer_kernel, rows),
        [(6, 2, 8, Z, X), (2, 2, 4, Z, X), (2, 2, 6, Z, X), four, (3, 2, *edge)],
        work,
        main,
        *y_packets,
        *own_x,
        *corner_x,
        *inside,
    )
    own, first, second, edge_a, edge_b, gain = call(
        combine_kernel,
        [(2, OWN, Z, X), strip, strip, edge, edge, (POWERS + 3, Z, X)],
        [],
        sources,
        edges,
        spread,
    )
    coef1, keep0, iterate = call(
        functools.partial(coarse1_kernel, rows),
        [(3, 2, SIZE1, Z, X), (6, 2, total0, Z, X), (2, 2, rows, Z, X)],
        [(2, 2 * GROUPS1, Z, X)],
        coarse,
        *y_packets,
        *own_x,
        *corner_x,
        gain,
        keep_in,
        y1_in,
        y2_in,
        keep_out,
        y1_out,
        y2_out,
    )
    (fields2,) = call(
        functools.partial(fields2_kernel, rows), [(2, 3, Z, X)], [], coarse, *y_packets, *own_x, *corner_x
    )
    b_packets = exchange(first, second, "gy")

    one, two, up = (2, SIZE1, Z, X), (2, SIZE2, Z, X), (2, SIZE_UP, Z, X)
    near = (1 + EDGE_TILES, Z, X)
    packet, first, second, to_far, keep1 = call(
        level1_kernel,
        [(1, Z, X), near, near, (3, Z, X), (2, *one)],
        [one, one],
        own,
        *b_packets,
        edge_a,
        edge_b,
        fields2,
        coef1,
        gain,
    )
    far = (swap_far(to_far, "gy", 1), swap_far(to_far, "gy", -1))
    near = exchange(first, second, "gy")

    (out,) = call(
        rest_kernel,
        [(2 * Z * rows, X)],
        [(2, *two), one, two, two, two, two, up, up, pair0, pair0, pair0],
        packet,
        *near,
        *far,
        gain,
        coef1,
        fields2,
        keep0,
        iterate,
        keep1,
    )
    return out.reshape(2, Z, rows, X)


def solution(mesh):
    placed = (
        P(None, None, "gy", "gx"),
        P(None, None, "gy", "gx"),
        P(None, "gy", "gx"),
        P(None, "gy", "gx"),
    )
    return jax.shard_map(
        body, mesh=mesh, in_specs=placed, out_specs=P(None, None, "gy", "gx"), check_vma=False
    )
```

```python
import functools

import jax
import jax.numpy as jnp
from jax import lax
from jax.experimental import pallas as pl
from jax.experimental.pallas import tpu as pltpu
from jax.sharding import PartitionSpec as P

DIFF = (40.0, 20.0)
INV_STEP = 2.0
LOWER = 0.25

_CENTRE = (1.0 + LOWER) / 2.0
_HALF = (1.0 - LOWER) / 2.0
_SIGMA = _CENTRE / _HALF
_RHO0 = 1.0 / _SIGMA
_RHO1 = 1.0 / (2.0 * _SIGMA - _RHO0)
_RHO2 = 1.0 / (2.0 * _SIGMA - _RHO1)

Z = 8
X = 128
HALO0 = 4
SENT = 3
FIELDS1 = 6 * SENT
FIELDS2 = FIELDS1 + 8
PACKET = FIELDS2 + 1
WIDE = 42
PER = X // WIDE
EDGE = 3

LO1, HI1 = -4, 8
LO2, HI2 = -2, 3
LO_UP, HI_UP = -3, 7
SIZE1, SIZE2, SIZE_UP = HI1 - LO1 + 2, HI2 - LO2 + 2, HI_UP - LO_UP + 2
OWN = 4


def lane_of():
    return lax.broadcasted_iota(jnp.int32, (1, Z, X), 2)


def sub_of():
    return lax.broadcasted_iota(jnp.int32, (1, Z, X), 1)


def roll_x(tile, shift):
    shift = shift % X
    return pltpu.roll(tile, shift, 2) if shift else tile


def roll_z(tile, shift):
    shift = shift % Z
    return pltpu.roll(tile, shift, 1) if shift else tile


def chunks(lo, hi, step=4):
    return [(r, min(step, hi - r)) for r in range(lo, hi, step)]


def neighbour_sums(read, r, n, k, tiles=(0, 1)):
    lane = lane_of()
    low, high = lane < k, lane >= X - k
    centre = [read(t, r, n) for t in (0, 1)]
    right = [roll_x(c, k) for c in centre]
    left = [roll_x(c, -k) for c in centre]
    sums = []
    for t in tiles:
        c = centre[t]
        along_x = jnp.where(low, right[1 - t], right[t]) + jnp.where(high, left[1 - t], left[t])
        along_y = read(t, r - 1, n) + read(t, r + 1, n)
        along_z = 2.0 * roll_z(c, k) if 2 * k == Z else roll_z(c, k) + roll_z(c, -k)
        sums.append(along_x + along_y + along_z)
    return centre, sums


def jacobian(u, v, f, k, level):
    scale = 0.25**level
    product = u * v
    squared = v * v
    first = INV_STEP + squared + f + 6.0 * DIFF[0] * scale
    second = INV_STEP + f + k - 2.0 * product + 6.0 * DIFF[1] * scale
    return 2.0 * product, squared, 1.0 / first, 1.0 / second, first, second


def cheb_step(level, keep, source, target, d, r, n, carry, gain, tiles=(0, 1)):
    scale = 0.25**level
    k = 1 << level
    u, nb_u = neighbour_sums(lambda t, a, m: source[0, t, pl.ds(a, m)], r, n, k, tiles)
    v, nb_v = neighbour_sums(lambda t, a, m: source[1, t, pl.ds(a, m)], r, n, k, tiles)
    rows = pl.ds(r, n)
    out = []
    for t in tiles:
        cross, squared, inv_u, inv_v = (keep[i, t, rows] for i in range(4))
        res_u = inv_u * (keep[4, t, rows] - cross * v[t] + DIFF[0] * scale * nb_u[t]) - u[t]
        res_v = inv_v * (keep[5, t, rows] + squared * u[t] + DIFF[1] * scale * nb_v[t]) - v[t]
        du, dv = gain * res_u, gain * res_v
        if carry is not None:
            du = du + carry * d[0, t, rows]
            dv = dv + carry * d[1, t, rows]
        if target is not None:
            d[0, t, rows] = du
            d[1, t, rows] = dv
            target[0, t, rows] = u[t] + du
            target[1, t, rows] = v[t] + dv
        out.append((u[t] + du, v[t] + dv))
    return out


def next_power(keep, source, r, n):
    u, nb_u = neighbour_sums(lambda t, a, m: source[0, t, pl.ds(a, m)], r, n, 1)
    v, nb_v = neighbour_sums(lambda t, a, m: source[1, t, pl.ds(a, m)], r, n, 1)
    rows = pl.ds(r, n)
    first, second = [], []
    for t in (0, 1):
        cross, squared, inv_u, inv_v = (keep[i, t, rows] for i in range(4))
        first.append(u[t] + inv_u * (cross * v[t] - DIFF[0] * nb_u[t]))
        second.append(v[t] - inv_v * (squared * u[t] + DIFF[1] * nb_v[t]))
    return first, second


CARRY1 = _RHO1 * _RHO0
CARRY2 = _RHO2 * _RHO1


POWERS = 9


def write_gains(spread, out):
    lane = lax.broadcasted_iota(jnp.int32, (1, X), 1)
    for level in range(3):
        top = jnp.max(jnp.where(lane == level, spread, 0.0), axis=1, keepdims=True)
        tau = 1.0 / (1.0 + jnp.broadcast_to(top, (Z, X)))
        for i, factor in enumerate((1.0 / _CENTRE, 2.0 * _RHO1 / _HALF, 2.0 * _RHO2 / _HALF)):
            out[3 * level + i] = factor * tau
    g0, g1, g2 = (out[i] for i in range(3))
    first, second = g0 + CARRY1 * g0 + g1, g1 * g0
    out[POWERS] = first + CARRY2 * (CARRY1 * g0 + g1) + g2
    out[POWERS + 1] = second + CARRY2 * second + g2 * first
    out[POWERS + 2] = g2 * second


def pair_rows(value):
    n = value.shape[0] // 2
    pairs = value.reshape(n, 2, Z, X)
    return pairs[:, 0] + pairs[:, 1]


def restrict_01(first, second):
    lane, sub = lane_of(), sub_of()
    across = []
    for value in (first, second):
        a, b = value[0:1], value[1:2]
        across.append(jnp.where((lane & 1) == 0, a + roll_x(a, -1), b + roll_x(b, 1)))
    a, b = across
    return 0.125 * jnp.where((sub & 1) == 0, a + roll_z(a, -1), b + roll_z(b, 1))


def restrict_12(groups):
    lane, sub = lane_of(), sub_of()
    out = None
    for p, value in enumerate(groups):
        value = value + roll_x(value, 1 if p & 1 else -1)
        value = value + roll_x(value, 2 if p & 2 else -2)
        out = value if out is None else jnp.where((lane & 3) == p, value, out)
    return 0.125 * (out + jnp.where((sub & 2) == 0, roll_z(out, -2), roll_z(out, 2)))


def spread_x(tile, k, phase):
    return jnp.where((lane_of() & k) == phase, tile, roll_x(tile, -k if phase else k))


def packed_jacobian(uv, fk, level):
    scale = 0.25**level
    even = (sub_of() & 1) == 0
    u, v = jnp.where(even, uv, roll_z(uv, 1)), jnp.where(even, roll_z(uv, -1), uv)
    f, k = jnp.where(even, fk, roll_z(fk, 1)), jnp.where(even, roll_z(fk, -1), fk)
    product, squared = u * v, v * v
    diag = jnp.where(
        even,
        INV_STEP + squared + f + 6.0 * DIFF[0] * scale,
        INV_STEP + f + k - 2.0 * product + 6.0 * DIFF[1] * scale,
    )
    return 1.0 / diag, jnp.where(even, -2.0 * product, squared), diag


def packed_spread(uv, fk, level):
    scale = 0.25**level
    even = (sub_of() & 1) == 0
    inverse, other, _ = packed_jacobian(uv, fk, level)
    return jnp.where(even, 6.0 * DIFF[0] * scale - other, 6.0 * DIFF[1] * scale + other) * inverse


def packed_terms(source, g, n, level):
    k = 1 << level
    lane, sub = lane_of(), sub_of()
    even = (sub & 1) == 0
    first, last = (lane & (k - 1)) == 0, (lane & (k - 1)) == k - 1
    low, high = lane < k, lane >= X - k
    diff = jnp.where(even, DIFF[0] * 0.25**level, DIFF[1] * 0.25**level)
    wide = [source[t, pl.ds(g - 1, n + 2)] for t in (0, 1)]
    centre = [w[1 : n + 1] for w in wide]
    right = [roll_x(c, k) for c in centre]
    left = [roll_x(c, -k) for c in centre]
    out = []
    for t in (0, 1):
        c, w = centre[t], wide[t]
        total = jnp.where(low, right[1 - t], right[t]) + jnp.where(high, left[1 - t], left[t])
        if k == 2:
            ahead, back = roll_x(w, 1), roll_x(w, -1)
            total = total + jnp.where(first, back[0:n], ahead[1 : n + 1])
            total = total + jnp.where(last, ahead[2 : n + 2], back[1 : n + 1])
            total = total + roll_z(c, 2) + roll_z(c, -2)
        else:
            total = total + jnp.where(first, roll_x(w[0:n], -(k - 1)), roll_x(c, 1))
            total = total + jnp.where(last, roll_x(w[2 : n + 2], k - 1), roll_x(c, -1))
            total = total + 2.0 * roll_z(c, 4)
        other = jnp.where(even, roll_z(c, -1), roll_z(c, 1))
        out.append((c, other, diff * total))
    return out


def packed_first(coef, shift, b, target, d, g, n, gain):
    for t in (0, 1):
        value = gain * coef[0, t, pl.ds(g + shift, n)] * b[t, pl.ds(g + shift, n)]
        d[t, pl.ds(g, n)] = value
        target[t, pl.ds(g, n)] = value


def packed_step(level, coef, shift, b, source, target, d, g, n, carry, gain):
    for t, (c, other, spread) in enumerate(packed_terms(source, g, n, level)):
        at = pl.ds(g + shift, n)
        res = coef[0, t, at] * (b[t, at] + coef[1, t, at] * other + spread) - c
        delta = gain * res
        if carry is not None:
            delta = delta + carry * d[t, pl.ds(g, n)]
        d[t, pl.ds(g, n)] = delta
        target[t, pl.ds(g, n)] = c + delta


def plane(ref, f, y, rows):
    return ref[pl.ds(f * Z * rows + y, Z, stride=rows), :]


def is_even(axis):
    return lax.rem(lax.axis_index(axis), 2) == 0


def prev_of(even, first, second, at):
    return jnp.where(even, first[at], second[at])


def next_of(even, first, second, at):
    return jnp.where(even, second[at], first[at])


SOURCES = ((0, 0), (0, 1), (1, 0), (1, 1), (2, 0), (3, 0))


def first_kernel(rows, state, previous, feed, kill, first, second, coarse, *rest):
    held, sems = rest[:4], rest[4]
    copies = [
        pltpu.make_async_copy(ref, to, sems.at[i]) for i, (ref, to) in enumerate(zip((state, previous, feed, kill), held))
    ]
    for copy in copies:
        copy.start()
    for copy in copies:
        copy.wait()
    even = is_even("gy")
    values = []
    for i, (j, f) in enumerate(SOURCES):
        wanted = range(rows) if i not in (2, 3) else [*range(SENT), *range(rows - SENT, rows)]
        values.append({y: plane(held[j], f, y, rows)[None] for y in wanted})
    for i in (2, 3):
        weight = DIFF[i - 2] / INV_STEP
        values[i][SENT - 1] = values[i][SENT - 1] + weight * values[i - 2][SENT]
        values[i][rows - SENT] = values[i][rows - SENT] + weight * values[i - 2][rows - SENT - 1]
    for i in range(6):
        for y in range(SENT):
            top, bottom = values[i][y], values[i][rows - SENT + y]
            at = slice(i * SENT + y, i * SENT + y + 1)
            first[at] = jnp.where(even, top, bottom)
            second[at] = jnp.where(even, bottom, top)
    pairs = []
    for p, (i, j) in enumerate(((0, 1), (4, 5))):
        parts = []
        for g in range(OWN):
            sums = [
                jnp.concatenate([value[4 * g + 2 * q] + value[4 * g + 2 * q + 1] for q in (0, 1)], axis=0)
                for value in (values[i], values[j])
            ]
            parts.append(restrict_01(*sums))
        pairs.append(jnp.concatenate(parts, axis=0))
        coarse[p * OWN : (p + 1) * OWN] = pairs[p]
        for ref in (first, second):
            ref[FIELDS1 + p * OWN : FIELDS1 + (p + 1) * OWN] = pairs[p]
    uv, fk = (restrict_12([pair[j : j + 1] for j in range(OWN)]) for pair in pairs)
    both = jnp.where((sub_of() & 2) == 0, uv, fk)
    coarse[2 * OWN : 2 * OWN + 1] = both
    for ref in (first, second):
        ref[FIELDS2 : FIELDS2 + 1] = both


def split_fields2(both):
    low = (sub_of() & 2) == 0
    return jnp.where(low, both, roll_z(both, 2)), jnp.where(low, roll_z(both, -2), both)


def write_spread(fields, coarse, out):
    lane = lax.broadcasted_iota(jnp.int32, (1, X), 1)
    cross, squared, inv_u, inv_v, _, _ = jacobian(*fields, 0)
    tops = [jnp.max(jnp.maximum((6.0 * DIFF[0] + cross) * inv_u, (6.0 * DIFF[1] + squared) * inv_v), axis=0)]
    tops.append(jnp.max(packed_spread(coarse[0:OWN], coarse[OWN : 2 * OWN], 1), axis=0))
    tops.append(packed_spread(*split_fields2(coarse[2 * OWN : 2 * OWN + 1]), 2)[0])
    result = jnp.zeros((1, X), jnp.float32)
    for level, top in enumerate(tops):
        top = jnp.max(jnp.max(top, axis=0, keepdims=True), axis=1, keepdims=True)
        result = jnp.where(lane == level, jnp.broadcast_to(top, (1, X)), result)
    out[...] = jnp.broadcast_to(result[None], out.shape)


GROUPS1 = HI1 - LO1
GROUPS2 = HI2 - LO2


def tiles_for(entries):
    return -(-entries // PER)


def pack_edges(entries, even, first, second):
    lane = lane_of()
    share = first.shape[0]
    left, right = None, None
    for j in range(PER):
        part = entries[j * share : (j + 1) * share]
        a, b = roll_x(part, WIDE * j), roll_x(part, WIDE + WIDE * j)
        left = a if left is None else jnp.where(lane >= WIDE * j, a, left)
        right = b if right is None else jnp.where(lane >= WIDE * j, b, right)
    first[...] = jnp.where(even, left, right)
    second[...] = jnp.where(even, right, left)


def halo_tiles(even, packets, lo, hi):
    first, second = packets
    share = first.shape[0]
    lane = lane_of()
    out = []
    for j in range(PER):
        a, b = max(lo, j * share), min(hi, (j + 1) * share)
        if a < b:
            strip = slice(a - j * share, b - j * share)
            left, right = prev_of(even, first, second, strip), next_of(even, first, second, strip)
            value = jnp.where(lane < X // 2, roll_x(right, -WIDE * j), roll_x(left, X - WIDE - WIDE * j))
            out.append((a - lo, b - lo, value))
    return out


def pack_own_kernel(
    rows, state, previous, feed, kill, coarse, first, second, spread, main, held, copies, sem
):
    inputs = (state, previous, feed, kill)

    def field(i):
        j, f = SOURCES[i]
        return jnp.stack([plane(inputs[j], f, y, rows) for y in range(rows)])

    fields = {i: field(i) for i in (0, 1, 4, 5)}
    write_spread([fields[i] for i in (0, 1, 4, 5)], coarse, copies)
    copy = pltpu.make_async_copy(copies, spread, sem)
    copy.start()

    @pl.when(lax.axis_index("gx") >= 0)
    def _():
        for i in range(6):
            value = field(i)
            main[i] = value
            held[i * rows : (i + 1) * rows] = value
        held[6 * rows : 6 * rows + 2 * OWN + 1] = coarse[...]
        pack_edges(held, is_even("gx"), first, second)

    copy.wait()


def pack_corner_kernel(y_first, y_second, first, second, held):
    even = is_even("gy")
    every = slice(0, PACKET)
    held[0:PACKET] = prev_of(even, y_first, y_second, every)
    held[PACKET : 2 * PACKET] = next_of(even, y_first, y_second, every)
    pack_edges(held, is_even("gx"), first, second)


EDGE_TILES = 2 * EDGE + 1


def level0_setup(fields, keep, diag, power, r, n):
    at = pl.ds(r, n)
    u, nb_u = neighbour_sums(lambda t, a, m: fields[0, t, pl.ds(a, m)], r, n, 1)
    v, nb_v = neighbour_sums(lambda t, a, m: fields[1, t, pl.ds(a, m)], r, n, 1)
    for t in (0, 1):
        f, k = fields[4, t, at], fields[5, t, at]
        cross, squared, inv_u, inv_v, first, second = jacobian(u[t], v[t], f, k, 0)
        react = u[t] * squared
        b_u = DIFF[0] * (nb_u[t] - 6.0 * u[t]) - INV_STEP * (u[t] - fields[2, t, at]) - react + f * (1.0 - u[t])
        b_v = DIFF[1] * (nb_v[t] - 6.0 * v[t]) - INV_STEP * (v[t] - fields[3, t, at]) + react - (f + k) * v[t]
        for i, value in enumerate((cross, squared, inv_u, inv_v, b_u, b_v)):
            keep[i, t, at] = value
        for i, value in enumerate((first, second)):
            diag[i, t, at] = value
        for i, value in enumerate((inv_u * b_u, inv_v * b_v)):
            power[i, t, at] = value


def level0_power(keep, source, target, r, n):
    for i, values in enumerate(next_power(keep, source, r, n)):
        for t in (0, 1):
            target[i, t, pl.ds(r, n)] = values[t]


def level0_down(keep, diag, y1, y2, sources, r, n):
    at = pl.ds(r, n)
    last = next_power(keep, y2, r, n)
    for t in (0, 1):
        both = [diag[i, t, at] for i in (0, 1)]
        parts = [[keep[4 + i, t, at] for i in (0, 1)]]
        parts += [[both[i] * power[i, t, at] for i in (0, 1)] for power in (y1, y2)]
        parts.append([both[i] * last[i][t] for i in (0, 1)])
        for q, part in enumerate(parts):
            u, v = (pair_rows(value) for value in part)
            for j in range(n // 4):
                value = restrict_01(u[2 * j : 2 * j + 2], v[2 * j : 2 * j + 2])
                sources[q, t, pl.ds((r - HALO0) // 4 + j, 1)] = value


def inner(rows, lost):
    return slice(HALO0 + lost, HALO0 + rows - lost)


def ends(rows, lo, hi):
    total = rows + 2 * HALO0
    return slice(lo, hi), slice(total - hi, total - lo)


def put_ends(target, rows, lo, hi, source):
    n = hi - lo
    for at, part in zip(ends(rows, lo, hi), (slice(0, n), slice(n, 2 * n))):
        for i in range(target.shape[0]):
            for t in (0, 1):
                target[i, t, at] = source[i, t, part]


def take_ends(source, rows, lo, hi, target):
    n = hi - lo
    for at, part in zip(ends(rows, lo, hi), (slice(0, n), slice(n, 2 * n))):
        for i in range(source.shape[0]):
            for t in (0, 1):
                target[i, t, part] = source[i, t, at]


def level0_inner_kernel(rows, main, own_a, own_b, keep_in, y0_in, y1_in, y2_in, diag_in, sources_in, *scratch):
    fields, keep, diag, y0, y1, y2 = scratch
    even_x = is_even("gx")
    for i in range(6):
        fields[i, 0, HALO0 : HALO0 + rows] = main[i]
        for a, b, value in halo_tiles(even_x, (own_a, own_b), i * rows, (i + 1) * rows):
            fields[i, 1, HALO0 + a : HALO0 + b] = value
    first = HALO0 + 1
    level0_setup(fields, keep, diag, y0, first, rows - 2)
    level0_power(keep, y0, y1, first + 1, rows - 4)
    level0_power(keep, y1, y2, first + 2, rows - 6)
    level0_down(keep, diag, y1, y2, sources_in, first + 3, rows - 8)
    for source, target, lost in ((keep, keep_in, 1), (y1, y1_in, 2), (y2, y2_in, 3)):
        for i in range(source.shape[0]):
            for t in (0, 1):
                target[i, t] = source[i, t, inner(rows, lost)]
    take_ends(y0, rows, HALO0 + 1, HALO0 + 3, y0_in)
    take_ends(diag, rows, HALO0 + 1, HALO0 + 4, diag_in)


def level0_outer_kernel(
    rows,
    main,
    y_first,
    y_second,
    own_a,
    own_b,
    corner_a,
    corner_b,
    keep_in,
    y0_in,
    y1_in,
    y2_in,
    diag_in,
    sources_in,
    keep_out,
    y1_out,
    y2_out,
    sources,
    edges,
    *scratch,
):
    fields, keep, diag, y0, y1, y2 = scratch
    even, even_x = is_even("gy"), is_even("gx")
    total = rows + 2 * HALO0
    near, skip = HALO0 + 2, HALO0 - SENT
    for i in range(6):
        strip = slice(i * SENT, (i + 1) * SENT)
        fields[i, 0, skip:HALO0] = prev_of(even, y_first, y_second, strip)
        fields[i, 0, HALO0:near] = main[i, 0:2]
        fields[i, 0, total - near : total - HALO0] = main[i, rows - 2 : rows]
        fields[i, 0, HALO0 + rows : total - skip] = next_of(even, y_first, y_second, strip)
        for packets, lo, n, at in (
            ((corner_a, corner_b), i * SENT, SENT, skip),
            ((own_a, own_b), i * rows, 2, HALO0),
            ((own_a, own_b), (i + 1) * rows - 2, 2, total - near),
            ((corner_a, corner_b), PACKET + i * SENT, SENT, HALO0 + rows),
        ):
            for a, b, value in halo_tiles(even_x, packets, lo, lo + n):
                fields[i, 1, at + a : at + b] = value
    for i in (0, 1):
        for t in (0, 1):
            for at in (0, total - 1):
                fields[i, t, at] = jnp.zeros((Z, X), jnp.float32)
    for at, part in zip(ends(rows, 5, 8), (slice(0, 3), slice(rows - 5, rows - 2))):
        for i in range(6):
            for t in (0, 1):
                keep[i, t, at] = keep_in[i, t, part]
    put_ends(diag, rows, 5, 8, diag_in)
    put_ends(y0, rows, 5, 7, y0_in)
    for target, source, lost in ((y1, y1_in, 2), (y2, y2_in, 3)):
        n = rows - 2 * lost
        for at, part in zip(ends(rows, HALO0 + lost, HALO0 + lost + 2), (slice(0, 2), slice(n - 2, n))):
            for i in (0, 1):
                for t in (0, 1):
                    target[i, t, at] = source[i, t, part]
    for r in (1, total - 5):
        level0_setup(fields, keep, diag, y0, r, 4)
    for r in (2, total - 6):
        level0_power(keep, y0, y1, r, 4)
    for r in (3, total - 7):
        level0_power(keep, y1, y2, r, 4)
    for r in (4, total - 8):
        level0_down(keep, diag, y1, y2, sources, r, 4)
    for q in range(4):
        for t in (0, 1):
            sources[q, t, 1 : OWN - 1] = sources_in[q, t, 1 : OWN - 1]
    take_ends(keep, rows, 1, 5, keep_out)
    take_ends(y1, rows, 4, 6, y1_out)
    take_ends(y2, rows, 4, 7, y2_out)
    for p, power in enumerate((y0, y1, y2)):
        for side, start in enumerate((HALO0, HALO0 + rows - EDGE)):
            edges[p, side] = pack_rows(power, start)


def pack_rows(x, start):
    lane = lane_of()
    halo = None
    for i in (0, 1):
        for j in range(EDGE):
            at = i * EDGE + j
            value = roll_x(x[i, 1, start + j : start + j + 1], 4 + 8 * at)
            halo = value if halo is None else jnp.where((lane >> 3) == at, value, halo)
    return jnp.concatenate([x[i, 0, start : start + EDGE] for i in (0, 1)] + [halo], axis=0)


def squeeze(halo):
    lane = lane_of()
    last = halo[OWN - 1 : OWN]
    ahead = (lane >= WIDE) & (lane < 2 * WIDE)
    parts = [jnp.where(ahead, roll_x(last, WIDE), halo[0:1]), jnp.where(ahead, roll_x(last, 2 * WIDE - X), halo[1:2])]
    return jnp.concatenate(parts + [halo[2 : OWN - 1]], axis=0)


def unsqueeze(tiles):
    last = jnp.where(lane_of() < X // 2, roll_x(tiles[0:1], -WIDE), roll_x(tiles[1:2], X - 2 * WIDE))
    return jnp.concatenate([tiles, last], axis=0)


def combine_kernel(sources, edges, spread, own, first, second, edge_first, edge_second, gain):
    write_gains(jnp.max(spread[...], axis=0)[0:1], gain)
    p0, p1, p2 = (gain[POWERS + i] for i in range(3))
    for t in (0, 1):
        value = sources[0, t] - p0 * sources[1, t] + p1 * sources[2, t] - p2 * sources[3, t]
        own[t] = value
        for ref in (first, second):
            if t == 0:
                ref[0:OWN] = value
            else:
                ref[OWN:] = squeeze(value)
    even = is_even("gy")
    top, bottom = (p0 * edges[0, side] - p1 * edges[1, side] + p2 * edges[2, side] for side in (0, 1))
    edge_first[...] = jnp.where(even, top, bottom)
    edge_second[...] = jnp.where(even, bottom, top)


def coarse1_kernel(
    rows, coarse, y_first, y_second, own_a, own_b, corner_a, corner_b, gain, keep_in, y1_in, y2_in, keep_out, y1_out, y2_out,
    coef, keep0, x0, fields
):
    even, even_x = is_even("gy"), is_even("gx")
    own_x, corner_x = (own_a, own_b), (corner_a, corner_b)
    for p in (0, 1):
        to = p * GROUPS1
        strip = slice(FIELDS1 + p * OWN, FIELDS1 + (p + 1) * OWN)
        fields[0, to : to + OWN] = prev_of(even, y_first, y_second, strip)
        fields[0, to + OWN : to + 2 * OWN] = coarse[p * OWN : (p + 1) * OWN]
        fields[0, to + 2 * OWN : to + 3 * OWN] = next_of(even, y_first, y_second, strip)
        for part, (packets, lo) in enumerate(
            ((corner_x, FIELDS1), (own_x, 6 * rows), (corner_x, PACKET + FIELDS1))
        ):
            lo += p * OWN
            for a, b, value in halo_tiles(even_x, packets, lo, lo + OWN):
                fields[1, to + part * OWN + a : to + part * OWN + b] = value
    for t in (0, 1):
        for i, value in enumerate(packed_jacobian(fields[t, 0:GROUPS1], fields[t, GROUPS1 : 2 * GROUPS1], 1)):
            coef[i, t, 1 : SIZE1 - 1] = value

    def whole(inside, outside):
        n = outside.shape[0] // 2
        return jnp.concatenate([outside[0:n], inside, outside[n:]], axis=0)

    for i in range(6):
        for t in (0, 1):
            keep0[i, t, 1 : rows + 2 * HALO0 - 1] = whole(keep_in[i, t], keep_out[i, t])
    p0, p1, p2 = (gain[POWERS + i] for i in range(3))
    for i in (0, 1):
        for t in (0, 1):
            y0 = keep0[2 + i, t, HALO0 : HALO0 + rows] * keep0[4 + i, t, HALO0 : HALO0 + rows]
            y1, y2 = (whole(a[i, t], b[i, t]) for a, b in ((y1_in, y1_out), (y2_in, y2_out)))
            x0[i, t] = p0 * y0 - p1 * y1 + p2 * y2


def fields2_kernel(rows, coarse, y_first, y_second, own_a, own_b, corner_a, corner_b, out):
    even, even_x = is_even("gy"), is_even("gx")
    own_x, corner_x = (own_a, own_b), (corner_a, corner_b)
    near = slice(FIELDS2, FIELDS2 + 1)
    out[0, 0:1] = prev_of(even, y_first, y_second, near)
    out[0, 1:2] = coarse[2 * OWN : 2 * OWN + 1]
    out[0, 2:3] = next_of(even, y_first, y_second, near)
    for q, (packets, lo) in enumerate(
        ((corner_x, FIELDS2), (own_x, 6 * rows + 2 * OWN), (corner_x, PACKET + FIELDS2))
    ):
        out[1, q : q + 1] = halo_tiles(even_x, packets, lo, lo + 1)[0][2]


def level1_kernel(
    own, first, second, edge_a, edge_b, fields2, coef1, gain, packet, to_first, to_second, to_far, keep, y1, d1
):
    b1, x1 = keep.at[0], keep.at[1]
    even = is_even("gy")
    for t in (0, 1):
        b1[t, 1 + OWN : 1 + 2 * OWN] = own[t]
        for at, take in ((1, prev_of), (1 + 2 * OWN, next_of)):
            if t == 0:
                b1[t, at : at + OWN] = take(even, first, second, slice(0, OWN))
            else:
                b1[t, at : at + OWN] = unsqueeze(take(even, first, second, slice(OWN, 2 * OWN - 1)))
    g0, g1, g2 = (gain[3 + i] for i in range(3))
    n = GROUPS1
    packed_first(coef1, 0, b1, x1, d1, 1, n, g0)
    packed_step(1, coef1, 0, b1, x1, y1, d1, 2, n - 2, CARRY1, g1)
    packed_step(1, coef1, 0, b1, y1, x1, d1, 2, n - 2, CARRY2, g2)
    here = pl.ds(1 + OWN, OWN)
    values = []
    for t, (c, other, spread) in enumerate(packed_terms(x1, 1 + OWN, OWN, 1)):
        res = b1[t, here] - coef1[2, t, here] * c + coef1[1, t, here] * other + spread
        values.append(restrict_12([res[j : j + 1] for j in range(OWN)]))
        to_far[1 + t : 2 + t] = fields2[t, 1:2]
    value = jnp.where((sub_of() & 2) == 0, values[0], values[1])
    for ref in (packet, to_first, to_second, to_far):
        ref[0:1] = value
    to_first[1:] = edge_a[...]
    to_second[1:] = edge_b[...]


def rest_kernel(
    own2, near_a, near_b, far_a, far_b, gain, coef1, fields2, keep0, iterate, keep1, out, coef2, d1, b2, x2, y2, d2, xu, yu, x0, y0, d0
):
    rows = out.shape[0] // (2 * Z)
    even = (sub_of() & 1) == 0
    b1, x1 = keep1.at[0], keep1.at[1]

    even_y, low = is_even("gy"), lax.rem(lax.axis_index("gy"), 4) < 2
    at = slice(0, 1)
    parts = [
        next_of(low, far_a, far_b, at),
        prev_of(even_y, near_a, near_b, at),
        own2[at],
        next_of(even_y, near_a, near_b, at),
        prev_of(low, far_a, far_b, at),
    ]
    for t, values in enumerate(split_fields2(jnp.concatenate(parts, axis=0))):
        b2[t, 1 : SIZE2 - 1] = values
        at = slice(1 + t, 2 + t)
        parts = [next_of(low, far_a, far_b, at), fields2[t], prev_of(low, far_a, far_b, at)]
        inverse, other, _ = packed_jacobian(*split_fields2(jnp.concatenate(parts, axis=0)), 2)
        coef2[0, t, 1 : SIZE2 - 1] = inverse
        coef2[1, t, 1 : SIZE2 - 1] = other

    n = HI2 - LO2
    g0, g1, g2 = (gain[6 + i] for i in range(3))
    packed_first(coef2, 0, b2, x2, d2, 1, n, g0)
    packed_step(2, coef2, 0, b2, x2, y2, d2, 1, n, CARRY1, g1)
    packed_step(2, coef2, 0, b2, y2, x2, d2, 1, n, CARRY2, g2)
    packed_step(2, coef2, 0, b2, x2, y2, d2, 1, n, None, g0)
    packed_step(2, coef2, 0, b2, y2, x2, d2, 2, n - 2, CARRY1, g1)
    packed_step(2, coef2, 0, b2, x2, y2, d2, 2, n - 2, CARRY2, g2)

    g0, g1, g2 = (gain[3 + i] for i in range(3))
    shift = LO_UP - LO1
    for t in (0, 1):
        for g in range(LO_UP, HI_UP):
            p = g % 4
            value = y2[t, g // 4 - LO2 + 1 : g // 4 - LO2 + 2]
            value = spread_x(spread_x(value, 1, p & 1), 2, p & 2)
            at = g - LO_UP + 1
            xu[t, at : at + 1] = x1[t, at + shift : at + shift + 1] + value
    n = HI_UP - LO_UP
    packed_step(1, coef1, shift, b1, xu, yu, d1, 2, n - 2, None, g0)
    packed_step(1, coef1, shift, b1, yu, xu, d1, 2, n - 2, CARRY1, g1)
    packed_step(1, coef1, shift, b1, xu, yu, d1, 3, n - 4, CARRY2, g2)

    g0, g1, g2 = (gain[i] for i in range(3))
    sides = [take(even_y, near_a, near_b, slice(1, 1 + EDGE_TILES)) for take in (prev_of, next_of)]

    def before(i, t, y):
        if 0 <= y < rows:
            return iterate[i, t, y : y + 1]
        side, j = (sides[0], y + EDGE) if y < 0 else (sides[1], y - rows)
        if t == 0:
            return side[i * EDGE + j : i * EDGE + j + 1]
        return roll_x(side[2 * EDGE :], -(4 + 8 * (i * EDGE + j)))

    for t in (0, 1):
        for row in range(-2, rows // 2 + 2):
            at = row // 2 - LO_UP + 1
            value = spread_x(yu[t, at : at + 1], 1, row & 1)
            for i, fine in enumerate((jnp.where(even, value, roll_z(value, 1)), jnp.where(even, roll_z(value, -1), value))):
                for y in (2 * row, 2 * row + 1):
                    if -EDGE <= y < rows + EDGE:
                        x0[i, t, y + HALO0 : y + HALO0 + 1] = before(i, t, y) + fine
    total = rows + 2 * HALO0
    for r, n in chunks(2, total - 2):
        cheb_step(0, keep0, x0, y0, d0, r, n, None, g0)
    for r, n in chunks(3, total - 3):
        cheb_step(0, keep0, y0, x0, d0, r, n, CARRY1, g1)
    for r, n in chunks(4, total - 4):
        last = cheb_step(0, keep0, x0, None, d0, r, n, CARRY2, g2, (0,))[0]
        for i in (0, 1):
            for j in range(n):
                out[pl.ds(i * Z * rows + r - HALO0 + j, Z, stride=rows), :] = last[i][j]


def call(kernel, out_shapes, scratch, *args, space=pltpu.VMEM, outs=None):
    out = [jax.ShapeDtypeStruct(shape, jnp.float32) for shape in out_shapes]
    return pl.pallas_call(
        kernel,
        out_shape=out,
        in_specs=[pl.BlockSpec(memory_space=space)] * len(args),
        out_specs=[pl.BlockSpec(memory_space=m) for m in outs or [pltpu.VMEM] * len(out)],
        scratch_shapes=[pltpu.VMEM(s, jnp.float32) if isinstance(s, tuple) else s for s in scratch],
        compiler_params=pltpu.CompilerParams(vmem_limit_bytes=24 * 2**20),
    )(*args)


def swap(value, axis, step):
    count = lax.axis_size(axis)
    assert count % 2 == 0
    pairs = [(i, (i + step) % count) for i in range(0, count, 2)]
    return lax.ppermute(value, axis, pairs + [(j, i) for i, j in pairs])


def swap_far(value, axis, step):
    count = lax.axis_size(axis)
    assert count % 4 == 0
    pairs = [(i + j, (i + j + 2 * step) % count) for i in range(0, count, 4) for j in (0, 1)]
    return lax.ppermute(value, axis, pairs + [(j, i) for i, j in pairs])


def exchange(first, second, axis):
    return swap(first, axis, -1), swap(second, axis, 1)


def body(state, previous, feed, kill):
    _, depth, rows, cols = state.shape
    assert depth == Z and cols == X and rows == 4 * OWN
    across, count = lax.axis_size("gx"), lax.axis_size("gy")
    total0 = rows + 2 * HALO0
    state = state.reshape(2 * Z * rows, X)
    previous = previous.reshape(2 * Z * rows, X)
    feed = feed.reshape(Z * rows, X)
    kill = kill.reshape(Z * rows, X)
    inputs = (state, previous, feed, kill)

    strip = (PACKET, Z, X)
    first, second, coarse, *inputs = call(
        functools.partial(first_kernel, rows),
        [strip, strip, (2 * OWN + 1, Z, X), *(a.shape for a in inputs)],
        [pltpu.SemaphoreType.DMA((4,))],
        *(pltpu.with_memory_space_constraint(a, pltpu.HBM) for a in inputs),
        space=pltpu.HBM,
    )
    y_packets = exchange(first, second, "gy")

    tiles = tiles_for(6 * rows + 2 * OWN + 1)
    spread_shape = (across * count, Z // 2, X)
    first, second, spread, main = call(
        functools.partial(pack_own_kernel, rows),
        [(tiles, Z, X), (tiles, Z, X), spread_shape, (6, rows, Z, X)],
        [(PER * tiles, Z, X), spread_shape, pltpu.SemaphoreType.DMA],
        *inputs,
        coarse,
        outs=[pltpu.VMEM, pltpu.VMEM, pltpu.HBM, pltpu.VMEM],
    )
    own_x = exchange(first, second, "gx")
    spread = lax.all_to_all(spread, ("gx", "gy"), 0, 0, tiled=True)
    tiles = tiles_for(2 * PACKET)
    corner_x = exchange(
        *call(pack_corner_kernel, [(tiles, Z, X), (tiles, Z, X)], [(PER * tiles, Z, X)], *y_packets), "gx"
    )

    strip, edge = (2 * OWN - 1, Z, X), (EDGE_TILES, Z, X)
    pair0 = (2, 2, total0, Z, X)
    work = [(6, 2, total0, Z, X), (6, 2, total0, Z, X), pair0, pair0, pair0, pair0]
    four = (4, 2, OWN, Z, X)
    inside = call(
        functools.partial(level0_inner_kernel, rows),
        [
            (6, 2, rows - 2, Z, X),
            (2, 2, 4, Z, X),
            (2, 2, rows - 4, Z, X),
            (2, 2, rows - 6, Z, X),
            (2, 2, 6, Z, X),
            four,
        ],
        work,
        main,
        *own_x,
    )
    keep_in, _, y1_in, y2_in, _, _ = inside
    keep_out, y1_out, y2_out, sources, edges = call(
        functools.partial(level0_outer_kernel, rows),
        [(6, 2, 8, Z, X), (2, 2, 4, Z, X), (2, 2, 6, Z, X), four, (3, 2, *edge)],
        work,
        main,
        *y_packets,
        *own_x,
        *corner_x,
        *inside,
    )
    own, first, second, edge_a, edge_b, gain = call(
        combine_kernel,
        [(2, OWN, Z, X), strip, strip, edge, edge, (POWERS + 3, Z, X)],
        [],
        sources,
        edges,
        spread,
    )
    coef1, keep0, iterate = call(
        functools.partial(coarse1_kernel, rows),
        [(3, 2, SIZE1, Z, X), (6, 2, total0, Z, X), (2, 2, rows, Z, X)],
        [(2, 2 * GROUPS1, Z, X)],
        coarse,
        *y_packets,
        *own_x,
        *corner_x,
        gain,
        keep_in,
        y1_in,
        y2_in,
        keep_out,
        y1_out,
        y2_out,
    )
    (fields2,) = call(
        functools.partial(fields2_kernel, rows), [(2, 3, Z, X)], [], coarse, *y_packets, *own_x, *corner_x
    )
    b_packets = exchange(first, second, "gy")

    one, two, up = (2, SIZE1, Z, X), (2, SIZE2, Z, X), (2, SIZE_UP, Z, X)
    near = (1 + EDGE_TILES, Z, X)
    packet, first, second, to_far, keep1 = call(
        level1_kernel,
        [(1, Z, X), near, near, (3, Z, X), (2, *one)],
        [one, one],
        own,
        *b_packets,
        edge_a,
        edge_b,
        fields2,
        coef1,
        gain,
    )
    far = (swap_far(to_far, "gy", 1), swap_far(to_far, "gy", -1))
    near = exchange(first, second, "gy")

    (out,) = call(
        rest_kernel,
        [(2 * Z * rows, X)],
        [(2, *two), one, two, two, two, two, up, up, pair0, pair0, pair0],
        packet,
        *near,
        *far,
        gain,
        coef1,
        fields2,
        keep0,
        iterate,
        keep1,
    )
    return out.reshape(2, Z, rows, X)


def solution(mesh):
    placed = (
        P(None, None, "gy", "gx"),
        P(None, None, "gy", "gx"),
        P(None, "gy", "gx"),
        P(None, "gy", "gx"),
    )
    return jax.shard_map(
        body, mesh=mesh, in_specs=placed, out_specs=P(None, None, "gy", "gx"), check_vma=False
    )
```

```python
import functools

import jax
import jax.numpy as jnp
from jax import lax
from jax.experimental import pallas as pl
from jax.experimental.pallas import tpu as pltpu
from jax.sharding import PartitionSpec as P

DIFF = (40.0, 20.0)
INV_STEP = 2.0
LOWER = 0.25

_CENTRE = (1.0 + LOWER) / 2.0
_HALF = (1.0 - LOWER) / 2.0
_SIGMA = _CENTRE / _HALF
_RHO0 = 1.0 / _SIGMA
_RHO1 = 1.0 / (2.0 * _SIGMA - _RHO0)
_RHO2 = 1.0 / (2.0 * _SIGMA - _RHO1)

Z = 8
X = 128
HALO0 = 4
SENT = 3
FIELDS1 = 6 * SENT
FIELDS2 = FIELDS1 + 8
PACKET = FIELDS2 + 1
WIDE = 42
PER = X // WIDE
EDGE = 3

LO1, HI1 = -4, 8
LO2, HI2 = -2, 3
LO_UP, HI_UP = -3, 7
SIZE1, SIZE2, SIZE_UP = HI1 - LO1 + 2, HI2 - LO2 + 2, HI_UP - LO_UP + 2
OWN = 4


def lane_of():
    return lax.broadcasted_iota(jnp.int32, (1, Z, X), 2)


def sub_of():
    return lax.broadcasted_iota(jnp.int32, (1, Z, X), 1)


def roll_x(tile, shift):
    shift = shift % X
    return pltpu.roll(tile, shift, 2) if shift else tile


def roll_z(tile, shift):
    shift = shift % Z
    return pltpu.roll(tile, shift, 1) if shift else tile


def chunks(lo, hi, step=4):
    return [(r, min(step, hi - r)) for r in range(lo, hi, step)]


def neighbour_sums(read, r, n, k, tiles=(0, 1)):
    lane = lane_of()
    low, high = lane < k, lane >= X - k
    centre = [read(t, r, n) for t in (0, 1)]
    right = [roll_x(c, k) for c in centre]
    left = [roll_x(c, -k) for c in centre]
    sums = []
    for t in tiles:
        c = centre[t]
        along_x = jnp.where(low, right[1 - t], right[t]) + jnp.where(high, left[1 - t], left[t])
        along_y = read(t, r - 1, n) + read(t, r + 1, n)
        along_z = 2.0 * roll_z(c, k) if 2 * k == Z else roll_z(c, k) + roll_z(c, -k)
        sums.append(along_x + along_y + along_z)
    return centre, sums


def jacobian(u, v, f, k, level):
    scale = 0.25**level
    product = u * v
    squared = v * v
    first = INV_STEP + squared + f + 6.0 * DIFF[0] * scale
    second = INV_STEP + f + k - 2.0 * product + 6.0 * DIFF[1] * scale
    return 2.0 * product, squared, 1.0 / first, 1.0 / second, first, second


def cheb_step(level, keep, source, target, d, r, n, carry, gain, tiles=(0, 1)):
    scale = 0.25**level
    k = 1 << level
    u, nb_u = neighbour_sums(lambda t, a, m: source[0, t, pl.ds(a, m)], r, n, k, tiles)
    v, nb_v = neighbour_sums(lambda t, a, m: source[1, t, pl.ds(a, m)], r, n, k, tiles)
    rows = pl.ds(r, n)
    out = []
    for t in tiles:
        cross, squared, inv_u, inv_v = (keep[i, t, rows] for i in range(4))
        res_u = inv_u * (keep[4, t, rows] - cross * v[t] + DIFF[0] * scale * nb_u[t]) - u[t]
        res_v = inv_v * (keep[5, t, rows] + squared * u[t] + DIFF[1] * scale * nb_v[t]) - v[t]
        du, dv = gain * res_u, gain * res_v
        if carry is not None:
            du = du + carry * d[0, t, rows]
            dv = dv + carry * d[1, t, rows]
        if target is not None:
            d[0, t, rows] = du
            d[1, t, rows] = dv
            target[0, t, rows] = u[t] + du
            target[1, t, rows] = v[t] + dv
        out.append((u[t] + du, v[t] + dv))
    return out


def next_power(keep, source, r, n):
    u, nb_u = neighbour_sums(lambda t, a, m: source[0, t, pl.ds(a, m)], r, n, 1)
    v, nb_v = neighbour_sums(lambda t, a, m: source[1, t, pl.ds(a, m)], r, n, 1)
    rows = pl.ds(r, n)
    first, second = [], []
    for t in (0, 1):
        cross, squared, inv_u, inv_v = (keep[i, t, rows] for i in range(4))
        first.append(u[t] + inv_u * (cross * v[t] - DIFF[0] * nb_u[t]))
        second.append(v[t] - inv_v * (squared * u[t] + DIFF[1] * nb_v[t]))
    return first, second


CARRY1 = _RHO1 * _RHO0
CARRY2 = _RHO2 * _RHO1


POWERS = 9


def write_gains(spread, out):
    lane = lax.broadcasted_iota(jnp.int32, (1, X), 1)
    for level in range(3):
        top = jnp.max(jnp.where(lane == level, spread, 0.0), axis=1, keepdims=True)
        tau = 1.0 / (1.0 + jnp.broadcast_to(top, (Z, X)))
        for i, factor in enumerate((1.0 / _CENTRE, 2.0 * _RHO1 / _HALF, 2.0 * _RHO2 / _HALF)):
            out[3 * level + i] = factor * tau
    g0, g1, g2 = (out[i] for i in range(3))
    first, second = g0 + CARRY1 * g0 + g1, g1 * g0
    out[POWERS] = first + CARRY2 * (CARRY1 * g0 + g1) + g2
    out[POWERS + 1] = second + CARRY2 * second + g2 * first
    out[POWERS + 2] = g2 * second


def pair_rows(value):
    n = value.shape[0] // 2
    pairs = value.reshape(n, 2, Z, X)
    return pairs[:, 0] + pairs[:, 1]


def restrict_01(first, second):
    lane, sub = lane_of(), sub_of()
    across = []
    for value in (first, second):
        a, b = value[0:1], value[1:2]
        across.append(jnp.where((lane & 1) == 0, a + roll_x(a, -1), b + roll_x(b, 1)))
    a, b = across
    return 0.125 * jnp.where((sub & 1) == 0, a + roll_z(a, -1), b + roll_z(b, 1))


def restrict_12(groups):
    lane, sub = lane_of(), sub_of()
    out = None
    for p, value in enumerate(groups):
        value = value + roll_x(value, 1 if p & 1 else -1)
        value = value + roll_x(value, 2 if p & 2 else -2)
        out = value if out is None else jnp.where((lane & 3) == p, value, out)
    return 0.125 * (out + jnp.where((sub & 2) == 0, roll_z(out, -2), roll_z(out, 2)))


def spread_x(tile, k, phase):
    return jnp.where((lane_of() & k) == phase, tile, roll_x(tile, -k if phase else k))


def packed_jacobian(uv, fk, level):
    scale = 0.25**level
    even = (sub_of() & 1) == 0
    u, v = jnp.where(even, uv, roll_z(uv, 1)), jnp.where(even, roll_z(uv, -1), uv)
    f, k = jnp.where(even, fk, roll_z(fk, 1)), jnp.where(even, roll_z(fk, -1), fk)
    product, squared = u * v, v * v
    diag = jnp.where(
        even,
        INV_STEP + squared + f + 6.0 * DIFF[0] * scale,
        INV_STEP + f + k - 2.0 * product + 6.0 * DIFF[1] * scale,
    )
    return 1.0 / diag, jnp.where(even, -2.0 * product, squared), diag


def packed_spread(uv, fk, level):
    scale = 0.25**level
    even = (sub_of() & 1) == 0
    inverse, other, _ = packed_jacobian(uv, fk, level)
    return jnp.where(even, 6.0 * DIFF[0] * scale - other, 6.0 * DIFF[1] * scale + other) * inverse


def packed_terms(source, g, n, level):
    k = 1 << level
    lane, sub = lane_of(), sub_of()
    even = (sub & 1) == 0
    first, last = (lane & (k - 1)) == 0, (lane & (k - 1)) == k - 1
    low, high = lane < k, lane >= X - k
    diff = jnp.where(even, DIFF[0] * 0.25**level, DIFF[1] * 0.25**level)
    wide = [source[t, pl.ds(g - 1, n + 2)] for t in (0, 1)]
    centre = [w[1 : n + 1] for w in wide]
    right = [roll_x(c, k) for c in centre]
    left = [roll_x(c, -k) for c in centre]
    out = []
    for t in (0, 1):
        c, w = centre[t], wide[t]
        total = jnp.where(low, right[1 - t], right[t]) + jnp.where(high, left[1 - t], left[t])
        if k == 2:
            ahead, back = roll_x(w, 1), roll_x(w, -1)
            total = total + jnp.where(first, back[0:n], ahead[1 : n + 1])
            total = total + jnp.where(last, ahead[2 : n + 2], back[1 : n + 1])
            total = total + roll_z(c, 2) + roll_z(c, -2)
        else:
            total = total + jnp.where(first, roll_x(w[0:n], -(k - 1)), roll_x(c, 1))
            total = total + jnp.where(last, roll_x(w[2 : n + 2], k - 1), roll_x(c, -1))
            total = total + 2.0 * roll_z(c, 4)
        other = jnp.where(even, roll_z(c, -1), roll_z(c, 1))
        out.append((c, other, diff * total))
    return out


def packed_first(coef, shift, b, target, d, g, n, gain):
    for t in (0, 1):
        value = gain * coef[0, t, pl.ds(g + shift, n)] * b[t, pl.ds(g + shift, n)]
        d[t, pl.ds(g, n)] = value
        target[t, pl.ds(g, n)] = value


def packed_step(level, coef, shift, b, source, target, d, g, n, carry, gain):
    for t, (c, other, spread) in enumerate(packed_terms(source, g, n, level)):
        at = pl.ds(g + shift, n)
        res = coef[0, t, at] * (b[t, at] + coef[1, t, at] * other + spread) - c
        delta = gain * res
        if carry is not None:
            delta = delta + carry * d[t, pl.ds(g, n)]
        d[t, pl.ds(g, n)] = delta
        target[t, pl.ds(g, n)] = c + delta


def plane(ref, f, y, rows):
    return ref[pl.ds(f * Z * rows + y, Z, stride=rows), :]


def is_even(axis):
    return lax.rem(lax.axis_index(axis), 2) == 0


def prev_of(even, first, second, at):
    return jnp.where(even, first[at], second[at])


def next_of(even, first, second, at):
    return jnp.where(even, second[at], first[at])


SOURCES = ((0, 0), (0, 1), (1, 0), (1, 1), (2, 0), (3, 0))


def first_kernel(rows, state, previous, feed, kill, first, second, coarse, *rest):
    held, sems = rest[:4], rest[4]
    copies = [
        pltpu.make_async_copy(ref, to, sems.at[i]) for i, (ref, to) in enumerate(zip((state, previous, feed, kill), held))
    ]
    for copy in copies:
        copy.start()
    for copy in copies:
        copy.wait()
    even = is_even("gy")
    values = []
    for i, (j, f) in enumerate(SOURCES):
        wanted = range(rows) if i not in (2, 3) else [*range(SENT), *range(rows - SENT, rows)]
        values.append({y: plane(held[j], f, y, rows)[None] for y in wanted})
    for i in (2, 3):
        weight = DIFF[i - 2] / INV_STEP
        values[i][SENT - 1] = values[i][SENT - 1] + weight * values[i - 2][SENT]
        values[i][rows - SENT] = values[i][rows - SENT] + weight * values[i - 2][rows - SENT - 1]
    for i in range(6):
        for y in range(SENT):
            top, bottom = values[i][y], values[i][rows - SENT + y]
            at = slice(i * SENT + y, i * SENT + y + 1)
            first[at] = jnp.where(even, top, bottom)
            second[at] = jnp.where(even, bottom, top)
    pairs = []
    for p, (i, j) in enumerate(((0, 1), (4, 5))):
        parts = []
        for g in range(OWN):
            sums = [
                jnp.concatenate([value[4 * g + 2 * q] + value[4 * g + 2 * q + 1] for q in (0, 1)], axis=0)
                for value in (values[i], values[j])
            ]
            parts.append(restrict_01(*sums))
        pairs.append(jnp.concatenate(parts, axis=0))
        coarse[p * OWN : (p + 1) * OWN] = pairs[p]
        for ref in (first, second):
            ref[FIELDS1 + p * OWN : FIELDS1 + (p + 1) * OWN] = pairs[p]
    uv, fk = (restrict_12([pair[j : j + 1] for j in range(OWN)]) for pair in pairs)
    both = jnp.where((sub_of() & 2) == 0, uv, fk)
    coarse[2 * OWN : 2 * OWN + 1] = both
    for ref in (first, second):
        ref[FIELDS2 : FIELDS2 + 1] = both


def split_fields2(both):
    low = (sub_of() & 2) == 0
    return jnp.where(low, both, roll_z(both, 2)), jnp.where(low, roll_z(both, -2), both)


def write_spread(fields, coarse, out):
    lane = lax.broadcasted_iota(jnp.int32, (1, X), 1)
    cross, squared, inv_u, inv_v, _, _ = jacobian(*fields, 0)
    tops = [jnp.max(jnp.maximum((6.0 * DIFF[0] + cross) * inv_u, (6.0 * DIFF[1] + squared) * inv_v), axis=0)]
    tops.append(jnp.max(packed_spread(coarse[0:OWN], coarse[OWN : 2 * OWN], 1), axis=0))
    tops.append(packed_spread(*split_fields2(coarse[2 * OWN : 2 * OWN + 1]), 2)[0])
    result = jnp.zeros((1, X), jnp.float32)
    for level, top in enumerate(tops):
        top = jnp.max(jnp.max(top, axis=0, keepdims=True), axis=1, keepdims=True)
        result = jnp.where(lane == level, jnp.broadcast_to(top, (1, X)), result)
    out[...] = jnp.broadcast_to(result[None], out.shape)


GROUPS1 = HI1 - LO1
GROUPS2 = HI2 - LO2


def tiles_for(entries):
    return -(-entries // PER)


def pack_edges(entries, even, first, second):
    lane = lane_of()
    share = first.shape[0]
    left, right = None, None
    for j in range(PER):
        part = entries[j * share : (j + 1) * share]
        a, b = roll_x(part, WIDE * j), roll_x(part, WIDE + WIDE * j)
        left = a if left is None else jnp.where(lane >= WIDE * j, a, left)
        right = b if right is None else jnp.where(lane >= WIDE * j, b, right)
    first[...] = jnp.where(even, left, right)
    second[...] = jnp.where(even, right, left)


def halo_tiles(even, packets, lo, hi):
    first, second = packets
    share = first.shape[0]
    lane = lane_of()
    out = []
    for j in range(PER):
        a, b = max(lo, j * share), min(hi, (j + 1) * share)
        if a < b:
            strip = slice(a - j * share, b - j * share)
            left, right = prev_of(even, first, second, strip), next_of(even, first, second, strip)
            value = jnp.where(lane < X // 2, roll_x(right, -WIDE * j), roll_x(left, X - WIDE - WIDE * j))
            out.append((a - lo, b - lo, value))
    return out


def spread_kernel(rows, state, feed, kill, coarse, out):
    inputs = (state, None, feed, kill)
    fields = [jnp.stack([plane(inputs[j], f, y, rows) for y in range(rows)]) for j, f in ((0, 0), (0, 1), (2, 0), (3, 0))]
    write_spread(fields, coarse, out)


def pack_own_kernel(rows, state, previous, feed, kill, coarse, first, second, main, held):
    inputs = (state, previous, feed, kill)
    for i, (j, f) in enumerate(SOURCES):
        for y in range(rows):
            value = plane(inputs[j], f, y, rows)
            main[i, y] = value
            held[i * rows + y] = value
    held[6 * rows : 6 * rows + 2 * OWN + 1] = coarse[...]
    pack_edges(held, is_even("gx"), first, second)


def pack_corner_kernel(y_first, y_second, first, second, held):
    even = is_even("gy")
    every = slice(0, PACKET)
    held[0:PACKET] = prev_of(even, y_first, y_second, every)
    held[PACKET : 2 * PACKET] = next_of(even, y_first, y_second, every)
    pack_edges(held, is_even("gx"), first, second)


EDGE_TILES = 2 * EDGE + 1


def level0_setup(fields, keep, diag, power, r, n):
    at = pl.ds(r, n)
    u, nb_u = neighbour_sums(lambda t, a, m: fields[0, t, pl.ds(a, m)], r, n, 1)
    v, nb_v = neighbour_sums(lambda t, a, m: fields[1, t, pl.ds(a, m)], r, n, 1)
    for t in (0, 1):
        f, k = fields[4, t, at], fields[5, t, at]
        cross, squared, inv_u, inv_v, first, second = jacobian(u[t], v[t], f, k, 0)
        react = u[t] * squared
        b_u = DIFF[0] * (nb_u[t] - 6.0 * u[t]) - INV_STEP * (u[t] - fields[2, t, at]) - react + f * (1.0 - u[t])
        b_v = DIFF[1] * (nb_v[t] - 6.0 * v[t]) - INV_STEP * (v[t] - fields[3, t, at]) + react - (f + k) * v[t]
        for i, value in enumerate((cross, squared, inv_u, inv_v, b_u, b_v)):
            keep[i, t, at] = value
        for i, value in enumerate((first, second)):
            diag[i, t, at] = value
        for i, value in enumerate((inv_u * b_u, inv_v * b_v)):
            power[i, t, at] = value


def level0_power(keep, source, target, r, n):
    for i, values in enumerate(next_power(keep, source, r, n)):
        for t in (0, 1):
            target[i, t, pl.ds(r, n)] = values[t]


def level0_down(keep, diag, y1, y2, sources, r, n):
    at = pl.ds(r, n)
    last = next_power(keep, y2, r, n)
    for t in (0, 1):
        both = [diag[i, t, at] for i in (0, 1)]
        parts = [[keep[4 + i, t, at] for i in (0, 1)]]
        parts += [[both[i] * power[i, t, at] for i in (0, 1)] for power in (y1, y2)]
        parts.append([both[i] * last[i][t] for i in (0, 1)])
        for q, part in enumerate(parts):
            u, v = (pair_rows(value) for value in part)
            for j in range(n // 4):
                value = restrict_01(u[2 * j : 2 * j + 2], v[2 * j : 2 * j + 2])
                sources[q, t, pl.ds((r - HALO0) // 4 + j, 1)] = value


def inner(rows, lost):
    return slice(HALO0 + lost, HALO0 + rows - lost)


def ends(rows, lo, hi):
    total = rows + 2 * HALO0
    return slice(lo, hi), slice(total - hi, total - lo)


def put_ends(target, rows, lo, hi, source):
    n = hi - lo
    for at, part in zip(ends(rows, lo, hi), (slice(0, n), slice(n, 2 * n))):
        for i in range(target.shape[0]):
            for t in (0, 1):
                target[i, t, at] = source[i, t, part]


def take_ends(source, rows, lo, hi, target):
    n = hi - lo
    for at, part in zip(ends(rows, lo, hi), (slice(0, n), slice(n, 2 * n))):
        for i in range(source.shape[0]):
            for t in (0, 1):
                target[i, t, part] = source[i, t, at]


def level0_inner_kernel(rows, main, own_a, own_b, keep_in, y0_in, y1_in, y2_in, diag_in, sources_in, *scratch):
    fields, keep, diag, y0, y1, y2 = scratch
    even_x = is_even("gx")
    for i in range(6):
        fields[i, 0, HALO0 : HALO0 + rows] = main[i]
        for a, b, value in halo_tiles(even_x, (own_a, own_b), i * rows, (i + 1) * rows):
            fields[i, 1, HALO0 + a : HALO0 + b] = value
    first = HALO0 + 1
    level0_setup(fields, keep, diag, y0, first, rows - 2)
    level0_power(keep, y0, y1, first + 1, rows - 4)
    level0_power(keep, y1, y2, first + 2, rows - 6)
    level0_down(keep, diag, y1, y2, sources_in, first + 3, rows - 8)
    for source, target, lost in ((keep, keep_in, 1), (y1, y1_in, 2), (y2, y2_in, 3)):
        for i in range(source.shape[0]):
            for t in (0, 1):
                target[i, t] = source[i, t, inner(rows, lost)]
    take_ends(y0, rows, HALO0 + 1, HALO0 + 3, y0_in)
    take_ends(diag, rows, HALO0 + 1, HALO0 + 4, diag_in)


def level0_outer_kernel(
    rows,
    main,
    y_first,
    y_second,
    own_a,
    own_b,
    corner_a,
    corner_b,
    keep_in,
    y0_in,
    y1_in,
    y2_in,
    diag_in,
    sources_in,
    keep_out,
    y1_out,
    y2_out,
    sources,
    edges,
    *scratch,
):
    fields, keep, diag, y0, y1, y2 = scratch
    even, even_x = is_even("gy"), is_even("gx")
    total = rows + 2 * HALO0
    near, skip = HALO0 + 2, HALO0 - SENT
    for i in range(6):
        strip = slice(i * SENT, (i + 1) * SENT)
        fields[i, 0, skip:HALO0] = prev_of(even, y_first, y_second, strip)
        fields[i, 0, HALO0:near] = main[i, 0:2]
        fields[i, 0, total - near : total - HALO0] = main[i, rows - 2 : rows]
        fields[i, 0, HALO0 + rows : total - skip] = next_of(even, y_first, y_second, strip)
        for packets, lo, n, at in (
            ((corner_a, corner_b), i * SENT, SENT, skip),
            ((own_a, own_b), i * rows, 2, HALO0),
            ((own_a, own_b), (i + 1) * rows - 2, 2, total - near),
            ((corner_a, corner_b), PACKET + i * SENT, SENT, HALO0 + rows),
        ):
            for a, b, value in halo_tiles(even_x, packets, lo, lo + n):
                fields[i, 1, at + a : at + b] = value
    for i in (0, 1):
        for t in (0, 1):
            for at in (0, total - 1):
                fields[i, t, at] = jnp.zeros((Z, X), jnp.float32)
    for at, part in zip(ends(rows, 5, 8), (slice(0, 3), slice(rows - 5, rows - 2))):
        for i in range(6):
            for t in (0, 1):
                keep[i, t, at] = keep_in[i, t, part]
    put_ends(diag, rows, 5, 8, diag_in)
    put_ends(y0, rows, 5, 7, y0_in)
    for target, source, lost in ((y1, y1_in, 2), (y2, y2_in, 3)):
        n = rows - 2 * lost
        for at, part in zip(ends(rows, HALO0 + lost, HALO0 + lost + 2), (slice(0, 2), slice(n - 2, n))):
            for i in (0, 1):
                for t in (0, 1):
                    target[i, t, at] = source[i, t, part]
    for r in (1, total - 5):
        level0_setup(fields, keep, diag, y0, r, 4)
    for r in (2, total - 6):
        level0_power(keep, y0, y1, r, 4)
    for r in (3, total - 7):
        level0_power(keep, y1, y2, r, 4)
    for r in (4, total - 8):
        level0_down(keep, diag, y1, y2, sources, r, 4)
    for q in range(4):
        for t in (0, 1):
            sources[q, t, 1 : OWN - 1] = sources_in[q, t, 1 : OWN - 1]
    take_ends(keep, rows, 1, 5, keep_out)
    take_ends(y1, rows, 4, 6, y1_out)
    take_ends(y2, rows, 4, 7, y2_out)
    for p, power in enumerate((y0, y1, y2)):
        for side, start in enumerate((HALO0, HALO0 + rows - EDGE)):
            edges[p, side] = pack_rows(power, start)


def pack_rows(x, start):
    lane = lane_of()
    halo = None
    for i in (0, 1):
        for j in range(EDGE):
            at = i * EDGE + j
            value = roll_x(x[i, 1, start + j : start + j + 1], 4 + 8 * at)
            halo = value if halo is None else jnp.where((lane >> 3) == at, value, halo)
    return jnp.concatenate([x[i, 0, start : start + EDGE] for i in (0, 1)] + [halo], axis=0)


def squeeze(halo):
    lane = lane_of()
    last = halo[OWN - 1 : OWN]
    ahead = (lane >= WIDE) & (lane < 2 * WIDE)
    parts = [jnp.where(ahead, roll_x(last, WIDE), halo[0:1]), jnp.where(ahead, roll_x(last, 2 * WIDE - X), halo[1:2])]
    return jnp.concatenate(parts + [halo[2 : OWN - 1]], axis=0)


def unsqueeze(tiles):
    last = jnp.where(lane_of() < X // 2, roll_x(tiles[0:1], -WIDE), roll_x(tiles[1:2], X - 2 * WIDE))
    return jnp.concatenate([tiles, last], axis=0)


def combine_kernel(sources, edges, spread, own, first, second, edge_first, edge_second, gain):
    write_gains(jnp.max(spread[...], axis=0)[0:1], gain)
    p0, p1, p2 = (gain[POWERS + i] for i in range(3))
    for t in (0, 1):
        value = sources[0, t] - p0 * sources[1, t] + p1 * sources[2, t] - p2 * sources[3, t]
        own[t] = value
        for ref in (first, second):
            if t == 0:
                ref[0:OWN] = value
            else:
                ref[OWN:] = squeeze(value)
    even = is_even("gy")
    top, bottom = (p0 * edges[0, side] - p1 * edges[1, side] + p2 * edges[2, side] for side in (0, 1))
    edge_first[...] = jnp.where(even, top, bottom)
    edge_second[...] = jnp.where(even, bottom, top)


def coarse1_kernel(
    rows, coarse, y_first, y_second, own_a, own_b, corner_a, corner_b, gain, keep_in, y1_in, y2_in, keep_out, y1_out, y2_out,
    coef, keep0, x0, fields
):
    even, even_x = is_even("gy"), is_even("gx")
    own_x, corner_x = (own_a, own_b), (corner_a, corner_b)
    for p in (0, 1):
        to = p * GROUPS1
        strip = slice(FIELDS1 + p * OWN, FIELDS1 + (p + 1) * OWN)
        fields[0, to : to + OWN] = prev_of(even, y_first, y_second, strip)
        fields[0, to + OWN : to + 2 * OWN] = coarse[p * OWN : (p + 1) * OWN]
        fields[0, to + 2 * OWN : to + 3 * OWN] = next_of(even, y_first, y_second, strip)
        for part, (packets, lo) in enumerate(
            ((corner_x, FIELDS1), (own_x, 6 * rows), (corner_x, PACKET + FIELDS1))
        ):
            lo += p * OWN
            for a, b, value in halo_tiles(even_x, packets, lo, lo + OWN):
                fields[1, to + part * OWN + a : to + part * OWN + b] = value
    for t in (0, 1):
        for i, value in enumerate(packed_jacobian(fields[t, 0:GROUPS1], fields[t, GROUPS1 : 2 * GROUPS1], 1)):
            coef[i, t, 1 : SIZE1 - 1] = value

    def whole(inside, outside):
        n = outside.shape[0] // 2
        return jnp.concatenate([outside[0:n], inside, outside[n:]], axis=0)

    for i in range(6):
        for t in (0, 1):
            keep0[i, t, 1 : rows + 2 * HALO0 - 1] = whole(keep_in[i, t], keep_out[i, t])
    p0, p1, p2 = (gain[POWERS + i] for i in range(3))
    for i in (0, 1):
        for t in (0, 1):
            y0 = keep0[2 + i, t, HALO0 : HALO0 + rows] * keep0[4 + i, t, HALO0 : HALO0 + rows]
            y1, y2 = (whole(a[i, t], b[i, t]) for a, b in ((y1_in, y1_out), (y2_in, y2_out)))
            x0[i, t] = p0 * y0 - p1 * y1 + p2 * y2


def fields2_kernel(rows, coarse, y_first, y_second, own_a, own_b, corner_a, corner_b, out):
    even, even_x = is_even("gy"), is_even("gx")
    own_x, corner_x = (own_a, own_b), (corner_a, corner_b)
    near = slice(FIELDS2, FIELDS2 + 1)
    out[0, 0:1] = prev_of(even, y_first, y_second, near)
    out[0, 1:2] = coarse[2 * OWN : 2 * OWN + 1]
    out[0, 2:3] = next_of(even, y_first, y_second, near)
    for q, (packets, lo) in enumerate(
        ((corner_x, FIELDS2), (own_x, 6 * rows + 2 * OWN), (corner_x, PACKET + FIELDS2))
    ):
        out[1, q : q + 1] = halo_tiles(even_x, packets, lo, lo + 1)[0][2]


def level1_kernel(
    own, first, second, edge_a, edge_b, fields2, coef1, gain, packet, to_first, to_second, to_far_a, to_far_b, keep, y1, d1
):
    b1, x1 = keep.at[0], keep.at[1]
    even = is_even("gy")
    for t in (0, 1):
        b1[t, 1 + OWN : 1 + 2 * OWN] = own[t]
        for at, take in ((1, prev_of), (1 + 2 * OWN, next_of)):
            if t == 0:
                b1[t, at : at + OWN] = take(even, first, second, slice(0, OWN))
            else:
                b1[t, at : at + OWN] = unsqueeze(take(even, first, second, slice(OWN, 2 * OWN - 1)))
    g0, g1, g2 = (gain[3 + i] for i in range(3))
    n = GROUPS1
    packed_first(coef1, 0, b1, x1, d1, 1, n, g0)
    packed_step(1, coef1, 0, b1, x1, y1, d1, 2, n - 2, CARRY1, g1)
    packed_step(1, coef1, 0, b1, y1, x1, d1, 2, n - 2, CARRY2, g2)
    here = pl.ds(1 + OWN, OWN)
    values = []
    for t, (c, other, spread) in enumerate(packed_terms(x1, 1 + OWN, OWN, 1)):
        res = b1[t, here] - coef1[2, t, here] * c + coef1[1, t, here] * other + spread
        values.append(restrict_12([res[j : j + 1] for j in range(OWN)]))
        for ref in (to_far_a, to_far_b):
            ref[1 + t : 2 + t] = fields2[t, 1:2]
    value = jnp.where((sub_of() & 2) == 0, values[0], values[1])
    for ref in (packet, to_first, to_second, to_far_a, to_far_b):
        ref[0:1] = value
    for ref in (to_far_a, to_far_b):
        ref[3:] = jnp.broadcast_to(value, (ref.shape[0] - 3, Z, X))
    to_first[1:] = edge_a[...]
    to_second[1:] = edge_b[...]


def rest_kernel(
    own2, near_a, near_b, far_a, far_b, gain, coef1, fields2, keep0, iterate, keep1, out, coef2, d1, b2, x2, y2, d2, xu, yu, x0, y0, d0
):
    rows = out.shape[0] // (2 * Z)
    even = (sub_of() & 1) == 0
    b1, x1 = keep1.at[0], keep1.at[1]

    even_y, low = is_even("gy"), lax.rem(lax.axis_index("gy"), 4) < 2
    at = slice(0, 1)
    parts = [
        next_of(low, far_a, far_b, at),
        prev_of(even_y, near_a, near_b, at),
        own2[at],
        next_of(even_y, near_a, near_b, at),
        prev_of(low, far_a, far_b, at),
    ]
    for t, values in enumerate(split_fields2(jnp.concatenate(parts, axis=0))):
        b2[t, 1 : SIZE2 - 1] = values
        at = slice(1 + t, 2 + t)
        parts = [next_of(low, far_a, far_b, at), fields2[t], prev_of(low, far_a, far_b, at)]
        inverse, other, _ = packed_jacobian(*split_fields2(jnp.concatenate(parts, axis=0)), 2)
        coef2[0, t, 1 : SIZE2 - 1] = inverse
        coef2[1, t, 1 : SIZE2 - 1] = other

    n = HI2 - LO2
    g0, g1, g2 = (gain[6 + i] for i in range(3))
    packed_first(coef2, 0, b2, x2, d2, 1, n, g0)
    packed_step(2, coef2, 0, b2, x2, y2, d2, 1, n, CARRY1, g1)
    packed_step(2, coef2, 0, b2, y2, x2, d2, 1, n, CARRY2, g2)
    packed_step(2, coef2, 0, b2, x2, y2, d2, 1, n, None, g0)
    packed_step(2, coef2, 0, b2, y2, x2, d2, 2, n - 2, CARRY1, g1)
    packed_step(2, coef2, 0, b2, x2, y2, d2, 2, n - 2, CARRY2, g2)

    g0, g1, g2 = (gain[3 + i] for i in range(3))
    shift = LO_UP - LO1
    for t in (0, 1):
        for g in range(LO_UP, HI_UP):
            p = g % 4
            value = y2[t, g // 4 - LO2 + 1 : g // 4 - LO2 + 2]
            value = spread_x(spread_x(value, 1, p & 1), 2, p & 2)
            at = g - LO_UP + 1
            xu[t, at : at + 1] = x1[t, at + shift : at + shift + 1] + value
    n = HI_UP - LO_UP
    packed_step(1, coef1, shift, b1, xu, yu, d1, 2, n - 2, None, g0)
    packed_step(1, coef1, shift, b1, yu, xu, d1, 2, n - 2, CARRY1, g1)
    packed_step(1, coef1, shift, b1, xu, yu, d1, 3, n - 4, CARRY2, g2)

    g0, g1, g2 = (gain[i] for i in range(3))
    sides = [take(even_y, near_a, near_b, slice(1, 1 + EDGE_TILES)) for take in (prev_of, next_of)]

    def before(i, t, y):
        if 0 <= y < rows:
            return iterate[i, t, y : y + 1]
        side, j = (sides[0], y + EDGE) if y < 0 else (sides[1], y - rows)
        if t == 0:
            return side[i * EDGE + j : i * EDGE + j + 1]
        return roll_x(side[2 * EDGE :], -(4 + 8 * (i * EDGE + j)))

    for t in (0, 1):
        for row in range(-2, rows // 2 + 2):
            at = row // 2 - LO_UP + 1
            value = spread_x(yu[t, at : at + 1], 1, row & 1)
            for i, fine in enumerate((jnp.where(even, value, roll_z(value, 1)), jnp.where(even, roll_z(value, -1), value))):
                for y in (2 * row, 2 * row + 1):
                    if -EDGE <= y < rows + EDGE:
                        x0[i, t, y + HALO0 : y + HALO0 + 1] = before(i, t, y) + fine
    total = rows + 2 * HALO0
    for r, n in chunks(2, total - 2):
        cheb_step(0, keep0, x0, y0, d0, r, n, None, g0)
    for r, n in chunks(3, total - 3):
        cheb_step(0, keep0, y0, x0, d0, r, n, CARRY1, g1)
    for r, n in chunks(4, total - 4):
        last = cheb_step(0, keep0, x0, None, d0, r, n, CARRY2, g2, (0,))[0]
        for i in (0, 1):
            for j in range(n):
                out[pl.ds(i * Z * rows + r - HALO0 + j, Z, stride=rows), :] = last[i][j]


def call(kernel, out_shapes, scratch, *args, space=pltpu.VMEM, outs=None):
    out = [jax.ShapeDtypeStruct(shape, jnp.float32) for shape in out_shapes]
    return pl.pallas_call(
        kernel,
        out_shape=out,
        in_specs=[pl.BlockSpec(memory_space=space)] * len(args),
        out_specs=[pl.BlockSpec(memory_space=m) for m in outs or [pltpu.VMEM] * len(out)],
        scratch_shapes=[pltpu.VMEM(s, jnp.float32) if isinstance(s, tuple) else s for s in scratch],
        compiler_params=pltpu.CompilerParams(vmem_limit_bytes=24 * 2**20),
    )(*args)


def swap(value, axis, step):
    count = lax.axis_size(axis)
    assert count % 2 == 0
    pairs = [(i, (i + step) % count) for i in range(0, count, 2)]
    return lax.ppermute(value, axis, pairs + [(j, i) for i, j in pairs])


def swap_far(value, axis, step):
    count = lax.axis_size(axis)
    assert count % 4 == 0
    pairs = [(i + j, (i + j + 2 * step) % count) for i in range(0, count, 4) for j in (0, 1)]
    return lax.ppermute(value, axis, pairs + [(j, i) for i, j in pairs])


def exchange(first, second, axis):
    return swap(first, axis, -1), swap(second, axis, 1)


def body(state, previous, feed, kill):
    _, depth, rows, cols = state.shape
    assert depth == Z and cols == X and rows == 4 * OWN
    across, count = lax.axis_size("gx"), lax.axis_size("gy")
    total0 = rows + 2 * HALO0
    state = state.reshape(2 * Z * rows, X)
    previous = previous.reshape(2 * Z * rows, X)
    feed = feed.reshape(Z * rows, X)
    kill = kill.reshape(Z * rows, X)
    inputs = (state, previous, feed, kill)

    strip = (PACKET, Z, X)
    first, second, coarse, *inputs = call(
        functools.partial(first_kernel, rows),
        [strip, strip, (2 * OWN + 1, Z, X), *(a.shape for a in inputs)],
        [pltpu.SemaphoreType.DMA((4,))],
        *(pltpu.with_memory_space_constraint(a, pltpu.HBM) for a in inputs),
        space=pltpu.HBM,
    )
    y_packets = exchange(first, second, "gy")

    tiles = tiles_for(6 * rows + 2 * OWN + 1)
    state, _, feed, kill = inputs
    (spread,) = call(
        functools.partial(spread_kernel, rows), [(across * count, 6, X)], [], state, feed, kill, coarse
    )
    spread = lax.all_to_all(spread, ("gx", "gy"), 0, 0, tiled=True)
    first, second, main = call(
        functools.partial(pack_own_kernel, rows),
        [(tiles, Z, X), (tiles, Z, X), (6, rows, Z, X)],
        [(PER * tiles, Z, X)],
        *inputs,
        coarse,
    )
    own_x = exchange(first, second, "gx")
    tiles = tiles_for(2 * PACKET)
    corner_x = exchange(
        *call(pack_corner_kernel, [(tiles, Z, X), (tiles, Z, X)], [(PER * tiles, Z, X)], *y_packets), "gx"
    )

    strip, edge = (2 * OWN - 1, Z, X), (EDGE_TILES, Z, X)
    pair0 = (2, 2, total0, Z, X)
    work = [(6, 2, total0, Z, X), (6, 2, total0, Z, X), pair0, pair0, pair0, pair0]
    four = (4, 2, OWN, Z, X)
    inside = call(
        functools.partial(level0_inner_kernel, rows),
        [
            (6, 2, rows - 2, Z, X),
            (2, 2, 4, Z, X),
            (2, 2, rows - 4, Z, X),
            (2, 2, rows - 6, Z, X),
            (2, 2, 6, Z, X),
            four,
        ],
        work,
        main,
        *own_x,
    )
    keep_in, _, y1_in, y2_in, _, _ = inside
    keep_out, y1_out, y2_out, sources, edges = call(
        functools.partial(level0_outer_kernel, rows),
        [(6, 2, 8, Z, X), (2, 2, 4, Z, X), (2, 2, 6, Z, X), four, (3, 2, *edge)],
        work,
        main,
        *y_packets,
        *own_x,
        *corner_x,
        *inside,
    )
    own, first, second, edge_a, edge_b, gain = call(
        combine_kernel,
        [(2, OWN, Z, X), strip, strip, edge, edge, (POWERS + 3, Z, X)],
        [],
        sources,
        edges,
        spread,
    )
    coef1, keep0, iterate = call(
        functools.partial(coarse1_kernel, rows),
        [(3, 2, SIZE1, Z, X), (6, 2, total0, Z, X), (2, 2, rows, Z, X)],
        [(2, 2 * GROUPS1, Z, X)],
        coarse,
        *y_packets,
        *own_x,
        *corner_x,
        gain,
        keep_in,
        y1_in,
        y2_in,
        keep_out,
        y1_out,
        y2_out,
    )
    (fields2,) = call(
        functools.partial(fields2_kernel, rows), [(2, 3, Z, X)], [], coarse, *y_packets, *own_x, *corner_x
    )
    b_packets = exchange(first, second, "gy")

    one, two, up = (2, SIZE1, Z, X), (2, SIZE2, Z, X), (2, SIZE_UP, Z, X)
    near = (1 + EDGE_TILES, Z, X)
    packet, first, second, far_a, far_b, keep1 = call(
        level1_kernel,
        [(1, Z, X), near, near, (near[0] + 2, Z, X), (near[0] + 1, Z, X), (2, *one)],
        [one, one],
        own,
        *b_packets,
        edge_a,
        edge_b,
        fields2,
        coef1,
        gain,
    )
    far = (swap_far(far_a, "gy", 1), swap_far(far_b, "gy", -1))
    near = exchange(first, second, "gy")

    (out,) = call(
        rest_kernel,
        [(2 * Z * rows, X)],
        [(2, *two), one, two, two, two, two, up, up, pair0, pair0, pair0],
        packet,
        *near,
        *far,
        gain,
        coef1,
        fields2,
        keep0,
        iterate,
        keep1,
    )
    return out.reshape(2, Z, rows, X)


def solution(mesh):
    placed = (
        P(None, None, "gy", "gx"),
        P(None, None, "gy", "gx"),
        P(None, "gy", "gx"),
        P(None, "gy", "gx"),
    )
    return jax.shard_map(
        body, mesh=mesh, in_specs=placed, out_specs=P(None, None, "gy", "gx"), check_vma=False
    )
```

```python
import functools

import jax
import jax.numpy as jnp
from jax import lax
from jax.experimental import pallas as pl
from jax.experimental.pallas import tpu as pltpu
from jax.sharding import PartitionSpec as P

DIFF = (40.0, 20.0)
INV_STEP = 2.0
LOWER = 0.25

_CENTRE = (1.0 + LOWER) / 2.0
_HALF = (1.0 - LOWER) / 2.0
_SIGMA = _CENTRE / _HALF
_RHO0 = 1.0 / _SIGMA
_RHO1 = 1.0 / (2.0 * _SIGMA - _RHO0)
_RHO2 = 1.0 / (2.0 * _SIGMA - _RHO1)

Z = 8
X = 128
HALO0 = 4
SENT = 3
FIELDS1 = 6 * SENT
FIELDS2 = FIELDS1 + 8
PACKET = FIELDS2 + 1
WIDE = 42
PER = X // WIDE
EDGE = 3

LO1, HI1 = -4, 8
LO2, HI2 = -2, 3
LO_UP, HI_UP = -3, 7
SIZE1, SIZE2, SIZE_UP = HI1 - LO1 + 2, HI2 - LO2 + 2, HI_UP - LO_UP + 2
OWN = 4


def lane_of():
    return lax.broadcasted_iota(jnp.int32, (1, Z, X), 2)


def sub_of():
    return lax.broadcasted_iota(jnp.int32, (1, Z, X), 1)


def roll_x(tile, shift):
    shift = shift % X
    return pltpu.roll(tile, shift, 2) if shift else tile


def roll_z(tile, shift):
    shift = shift % Z
    return pltpu.roll(tile, shift, 1) if shift else tile


def chunks(lo, hi, step=4):
    return [(r, min(step, hi - r)) for r in range(lo, hi, step)]


def neighbour_sums(read, r, n, k, tiles=(0, 1)):
    lane = lane_of()
    low, high = lane < k, lane >= X - k
    centre = [read(t, r, n) for t in (0, 1)]
    right = [roll_x(c, k) for c in centre]
    left = [roll_x(c, -k) for c in centre]
    sums = []
    for t in tiles:
        c = centre[t]
        along_x = jnp.where(low, right[1 - t], right[t]) + jnp.where(high, left[1 - t], left[t])
        along_y = read(t, r - 1, n) + read(t, r + 1, n)
        along_z = 2.0 * roll_z(c, k) if 2 * k == Z else roll_z(c, k) + roll_z(c, -k)
        sums.append(along_x + along_y + along_z)
    return centre, sums


def jacobian(u, v, f, k, level):
    scale = 0.25**level
    product = u * v
    squared = v * v
    first = INV_STEP + squared + f + 6.0 * DIFF[0] * scale
    second = INV_STEP + f + k - 2.0 * product + 6.0 * DIFF[1] * scale
    return 2.0 * product, squared, 1.0 / first, 1.0 / second, first, second


def cheb_step(level, keep, source, target, d, r, n, carry, gain, tiles=(0, 1)):
    scale = 0.25**level
    k = 1 << level
    u, nb_u = neighbour_sums(lambda t, a, m: source[0, t, pl.ds(a, m)], r, n, k, tiles)
    v, nb_v = neighbour_sums(lambda t, a, m: source[1, t, pl.ds(a, m)], r, n, k, tiles)
    rows = pl.ds(r, n)
    out = []
    for t in tiles:
        cross, squared, inv_u, inv_v = (keep[i, t, rows] for i in range(4))
        res_u = inv_u * (keep[4, t, rows] - cross * v[t] + DIFF[0] * scale * nb_u[t]) - u[t]
        res_v = inv_v * (keep[5, t, rows] + squared * u[t] + DIFF[1] * scale * nb_v[t]) - v[t]
        du, dv = gain * res_u, gain * res_v
        if carry is not None:
            du = du + carry * d[0, t, rows]
            dv = dv + carry * d[1, t, rows]
        if target is not None:
            d[0, t, rows] = du
            d[1, t, rows] = dv
            target[0, t, rows] = u[t] + du
            target[1, t, rows] = v[t] + dv
        out.append((u[t] + du, v[t] + dv))
    return out


def next_power(keep, source, r, n):
    u, nb_u = neighbour_sums(lambda t, a, m: source[0, t, pl.ds(a, m)], r, n, 1)
    v, nb_v = neighbour_sums(lambda t, a, m: source[1, t, pl.ds(a, m)], r, n, 1)
    rows = pl.ds(r, n)
    first, second = [], []
    for t in (0, 1):
        cross, squared, inv_u, inv_v = (keep[i, t, rows] for i in range(4))
        first.append(u[t] + inv_u * (cross * v[t] - DIFF[0] * nb_u[t]))
        second.append(v[t] - inv_v * (squared * u[t] + DIFF[1] * nb_v[t]))
    return first, second


CARRY1 = _RHO1 * _RHO0
CARRY2 = _RHO2 * _RHO1


POWERS = 9


def write_gains(spread, out):
    lane = lax.broadcasted_iota(jnp.int32, (1, X), 1)
    for level in range(3):
        top = jnp.max(jnp.where(lane == level, spread, 0.0), axis=1, keepdims=True)
        tau = 1.0 / (1.0 + jnp.broadcast_to(top, (Z, X)))
        for i, factor in enumerate((1.0 / _CENTRE, 2.0 * _RHO1 / _HALF, 2.0 * _RHO2 / _HALF)):
            out[3 * level + i] = factor * tau
    g0, g1, g2 = (out[i] for i in range(3))
    first, second = g0 + CARRY1 * g0 + g1, g1 * g0
    out[POWERS] = first + CARRY2 * (CARRY1 * g0 + g1) + g2
    out[POWERS + 1] = second + CARRY2 * second + g2 * first
    out[POWERS + 2] = g2 * second


def pair_rows(value):
    n = value.shape[0] // 2
    pairs = value.reshape(n, 2, Z, X)
    return pairs[:, 0] + pairs[:, 1]


def restrict_01(first, second):
    lane, sub = lane_of(), sub_of()
    across = []
    for value in (first, second):
        a, b = value[0:1], value[1:2]
        across.append(jnp.where((lane & 1) == 0, a + roll_x(a, -1), b + roll_x(b, 1)))
    a, b = across
    return 0.125 * jnp.where((sub & 1) == 0, a + roll_z(a, -1), b + roll_z(b, 1))


def restrict_12(groups):
    lane, sub = lane_of(), sub_of()
    out = None
    for p, value in enumerate(groups):
        value = value + roll_x(value, 1 if p & 1 else -1)
        value = value + roll_x(value, 2 if p & 2 else -2)
        out = value if out is None else jnp.where((lane & 3) == p, value, out)
    return 0.125 * (out + jnp.where((sub & 2) == 0, roll_z(out, -2), roll_z(out, 2)))


def spread_x(tile, k, phase):
    return jnp.where((lane_of() & k) == phase, tile, roll_x(tile, -k if phase else k))


def packed_jacobian(uv, fk, level):
    scale = 0.25**level
    even = (sub_of() & 1) == 0
    u, v = jnp.where(even, uv, roll_z(uv, 1)), jnp.where(even, roll_z(uv, -1), uv)
    f, k = jnp.where(even, fk, roll_z(fk, 1)), jnp.where(even, roll_z(fk, -1), fk)
    product, squared = u * v, v * v
    diag = jnp.where(
        even,
        INV_STEP + squared + f + 6.0 * DIFF[0] * scale,
        INV_STEP + f + k - 2.0 * product + 6.0 * DIFF[1] * scale,
    )
    return 1.0 / diag, jnp.where(even, -2.0 * product, squared), diag


def packed_spread(uv, fk, level):
    scale = 0.25**level
    even = (sub_of() & 1) == 0
    inverse, other, _ = packed_jacobian(uv, fk, level)
    return jnp.where(even, 6.0 * DIFF[0] * scale - other, 6.0 * DIFF[1] * scale + other) * inverse


def packed_terms(source, g, n, level):
    k = 1 << level
    lane, sub = lane_of(), sub_of()
    even = (sub & 1) == 0
    first, last = (lane & (k - 1)) == 0, (lane & (k - 1)) == k - 1
    low, high = lane < k, lane >= X - k
    diff = jnp.where(even, DIFF[0] * 0.25**level, DIFF[1] * 0.25**level)
    wide = [source[t, pl.ds(g - 1, n + 2)] for t in (0, 1)]
    centre = [w[1 : n + 1] for w in wide]
    right = [roll_x(c, k) for c in centre]
    left = [roll_x(c, -k) for c in centre]
    out = []
    for t in (0, 1):
        c, w = centre[t], wide[t]
        total = jnp.where(low, right[1 - t], right[t]) + jnp.where(high, left[1 - t], left[t])
        if k == 2:
            ahead, back = roll_x(w, 1), roll_x(w, -1)
            total = total + jnp.where(first, back[0:n], ahead[1 : n + 1])
            total = total + jnp.where(last, ahead[2 : n + 2], back[1 : n + 1])
            total = total + roll_z(c, 2) + roll_z(c, -2)
        else:
            total = total + jnp.where(first, roll_x(w[0:n], -(k - 1)), roll_x(c, 1))
            total = total + jnp.where(last, roll_x(w[2 : n + 2], k - 1), roll_x(c, -1))
            total = total + 2.0 * roll_z(c, 4)
        other = jnp.where(even, roll_z(c, -1), roll_z(c, 1))
        out.append((c, other, diff * total))
    return out


def packed_first(coef, shift, b, target, d, g, n, gain):
    for t in (0, 1):
        value = gain * coef[0, t, pl.ds(g + shift, n)] * b[t, pl.ds(g + shift, n)]
        d[t, pl.ds(g, n)] = value
        target[t, pl.ds(g, n)] = value


def packed_step(level, coef, shift, b, source, target, d, g, n, carry, gain):
    for t, (c, other, spread) in enumerate(packed_terms(source, g, n, level)):
        at = pl.ds(g + shift, n)
        res = coef[0, t, at] * (b[t, at] + coef[1, t, at] * other + spread) - c
        delta = gain * res
        if carry is not None:
            delta = delta + carry * d[t, pl.ds(g, n)]
        d[t, pl.ds(g, n)] = delta
        target[t, pl.ds(g, n)] = c + delta


def plane(ref, f, y, rows):
    return ref[pl.ds(f * Z * rows + y, Z, stride=rows), :]


def is_even(axis):
    return lax.rem(lax.axis_index(axis), 2) == 0


def prev_of(even, first, second, at):
    return jnp.where(even, first[at], second[at])


def next_of(even, first, second, at):
    return jnp.where(even, second[at], first[at])


SOURCES = ((0, 0), (0, 1), (1, 0), (1, 1), (2, 0), (3, 0))


def first_kernel(rows, state, previous, feed, kill, first, second, coarse, *rest):
    held, sems = rest[:4], rest[4]
    copies = [
        pltpu.make_async_copy(ref, to, sems.at[i]) for i, (ref, to) in enumerate(zip((state, previous, feed, kill), held))
    ]
    for copy in copies:
        copy.start()
    for copy in copies:
        copy.wait()
    even = is_even("gy")
    values = []
    for i, (j, f) in enumerate(SOURCES):
        wanted = range(rows) if i not in (2, 3) else [*range(SENT), *range(rows - SENT, rows)]
        values.append({y: plane(held[j], f, y, rows)[None] for y in wanted})
    for i in (2, 3):
        weight = DIFF[i - 2] / INV_STEP
        values[i][SENT - 1] = values[i][SENT - 1] + weight * values[i - 2][SENT]
        values[i][rows - SENT] = values[i][rows - SENT] + weight * values[i - 2][rows - SENT - 1]
    for i in range(6):
        for y in range(SENT):
            top, bottom = values[i][y], values[i][rows - SENT + y]
            at = slice(i * SENT + y, i * SENT + y + 1)
            first[at] = jnp.where(even, top, bottom)
            second[at] = jnp.where(even, bottom, top)
    pairs = []
    for p, (i, j) in enumerate(((0, 1), (4, 5))):
        parts = []
        for g in range(OWN):
            sums = [
                jnp.concatenate([value[4 * g + 2 * q] + value[4 * g + 2 * q + 1] for q in (0, 1)], axis=0)
                for value in (values[i], values[j])
            ]
            parts.append(restrict_01(*sums))
        pairs.append(jnp.concatenate(parts, axis=0))
        coarse[p * OWN : (p + 1) * OWN] = pairs[p]
        for ref in (first, second):
            ref[FIELDS1 + p * OWN : FIELDS1 + (p + 1) * OWN] = pairs[p]
    uv, fk = (restrict_12([pair[j : j + 1] for j in range(OWN)]) for pair in pairs)
    both = jnp.where((sub_of() & 2) == 0, uv, fk)
    coarse[2 * OWN : 2 * OWN + 1] = both
    for ref in (first, second):
        ref[FIELDS2 : FIELDS2 + 1] = both


def split_fields2(both):
    low = (sub_of() & 2) == 0
    return jnp.where(low, both, roll_z(both, 2)), jnp.where(low, roll_z(both, -2), both)


def write_spread(fields, coarse, out):
    lane = lax.broadcasted_iota(jnp.int32, (1, X), 1)
    cross, squared, inv_u, inv_v, _, _ = jacobian(*fields, 0)
    tops = [jnp.max(jnp.maximum((6.0 * DIFF[0] + cross) * inv_u, (6.0 * DIFF[1] + squared) * inv_v), axis=0)]
    tops.append(jnp.max(packed_spread(coarse[0:OWN], coarse[OWN : 2 * OWN], 1), axis=0))
    tops.append(packed_spread(*split_fields2(coarse[2 * OWN : 2 * OWN + 1]), 2)[0])
    result = jnp.zeros((1, X), jnp.float32)
    for level, top in enumerate(tops):
        top = jnp.max(jnp.max(top, axis=0, keepdims=True), axis=1, keepdims=True)
        result = jnp.where(lane == level, jnp.broadcast_to(top, (1, X)), result)
    out[...] = jnp.broadcast_to(result[None], out.shape)


GROUPS1 = HI1 - LO1
GROUPS2 = HI2 - LO2


def tiles_for(entries):
    return -(-entries // PER)


def pack_edges(entries, even, first, second):
    lane = lane_of()
    share = first.shape[0]
    left, right = None, None
    for j in range(PER):
        part = entries[j * share : (j + 1) * share]
        a, b = roll_x(part, WIDE * j), roll_x(part, WIDE + WIDE * j)
        left = a if left is None else jnp.where(lane >= WIDE * j, a, left)
        right = b if right is None else jnp.where(lane >= WIDE * j, b, right)
    first[...] = jnp.where(even, left, right)
    second[...] = jnp.where(even, right, left)


def halo_tiles(even, packets, lo, hi):
    first, second = packets
    share = first.shape[0]
    lane = lane_of()
    out = []
    for j in range(PER):
        a, b = max(lo, j * share), min(hi, (j + 1) * share)
        if a < b:
            strip = slice(a - j * share, b - j * share)
            left, right = prev_of(even, first, second, strip), next_of(even, first, second, strip)
            value = jnp.where(lane < X // 2, roll_x(right, -WIDE * j), roll_x(left, X - WIDE - WIDE * j))
            out.append((a - lo, b - lo, value))
    return out


def spread_kernel(rows, state, feed, kill, coarse, out):
    inputs = (state, None, feed, kill)
    fields = [jnp.stack([plane(inputs[j], f, y, rows) for y in range(rows)]) for j, f in ((0, 0), (0, 1), (2, 0), (3, 0))]
    write_spread(fields, coarse, out)


def pack_own_kernel(rows, state, previous, feed, kill, coarse, first, second, main, held):
    inputs = (state, previous, feed, kill)
    for i, (j, f) in enumerate(SOURCES):
        for y in range(rows):
            value = plane(inputs[j], f, y, rows)
            main[i, y] = value
            held[i * rows + y] = value
    held[6 * rows : 6 * rows + 2 * OWN + 1] = coarse[...]
    pack_edges(held, is_even("gx"), first, second)


def pack_corner_kernel(y_first, y_second, first, second, held):
    even = is_even("gy")
    every = slice(0, PACKET)
    held[0:PACKET] = prev_of(even, y_first, y_second, every)
    held[PACKET : 2 * PACKET] = next_of(even, y_first, y_second, every)
    pack_edges(held, is_even("gx"), first, second)


EDGE_TILES = 2 * EDGE + 1


def level0_setup(fields, keep, diag, power, r, n):
    at = pl.ds(r, n)
    u, nb_u = neighbour_sums(lambda t, a, m: fields[0, t, pl.ds(a, m)], r, n, 1)
    v, nb_v = neighbour_sums(lambda t, a, m: fields[1, t, pl.ds(a, m)], r, n, 1)
    for t in (0, 1):
        f, k = fields[4, t, at], fields[5, t, at]
        cross, squared, inv_u, inv_v, first, second = jacobian(u[t], v[t], f, k, 0)
        react = u[t] * squared
        b_u = DIFF[0] * (nb_u[t] - 6.0 * u[t]) - INV_STEP * (u[t] - fields[2, t, at]) - react + f * (1.0 - u[t])
        b_v = DIFF[1] * (nb_v[t] - 6.0 * v[t]) - INV_STEP * (v[t] - fields[3, t, at]) + react - (f + k) * v[t]
        for i, value in enumerate((cross, squared, inv_u, inv_v, b_u, b_v)):
            keep[i, t, at] = value
        for i, value in enumerate((first, second)):
            diag[i, t, at] = value
        for i, value in enumerate((inv_u * b_u, inv_v * b_v)):
            power[i, t, at] = value


def level0_power(keep, source, target, r, n):
    for i, values in enumerate(next_power(keep, source, r, n)):
        for t in (0, 1):
            target[i, t, pl.ds(r, n)] = values[t]


def level0_down(keep, diag, y1, y2, sources, r, n):
    at = pl.ds(r, n)
    last = next_power(keep, y2, r, n)
    for t in (0, 1):
        both = [diag[i, t, at] for i in (0, 1)]
        parts = [[keep[4 + i, t, at] for i in (0, 1)]]
        parts += [[both[i] * power[i, t, at] for i in (0, 1)] for power in (y1, y2)]
        parts.append([both[i] * last[i][t] for i in (0, 1)])
        for q, part in enumerate(parts):
            u, v = (pair_rows(value) for value in part)
            for j in range(n // 4):
                value = restrict_01(u[2 * j : 2 * j + 2], v[2 * j : 2 * j + 2])
                sources[q, t, pl.ds((r - HALO0) // 4 + j, 1)] = value


def inner(rows, lost):
    return slice(HALO0 + lost, HALO0 + rows - lost)


def ends(rows, lo, hi):
    total = rows + 2 * HALO0
    return slice(lo, hi), slice(total - hi, total - lo)


def put_ends(target, rows, lo, hi, source):
    n = hi - lo
    for at, part in zip(ends(rows, lo, hi), (slice(0, n), slice(n, 2 * n))):
        for i in range(target.shape[0]):
            for t in (0, 1):
                target[i, t, at] = source[i, t, part]


def take_ends(source, rows, lo, hi, target):
    n = hi - lo
    for at, part in zip(ends(rows, lo, hi), (slice(0, n), slice(n, 2 * n))):
        for i in range(source.shape[0]):
            for t in (0, 1):
                target[i, t, part] = source[i, t, at]


def level0_inner_kernel(rows, main, own_a, own_b, keep_in, y0_in, y1_in, y2_in, diag_in, sources_in, *scratch):
    fields, keep, diag, y0, y1, y2 = scratch
    even_x = is_even("gx")
    for i in range(6):
        fields[i, 0, HALO0 : HALO0 + rows] = main[i]
        for a, b, value in halo_tiles(even_x, (own_a, own_b), i * rows, (i + 1) * rows):
            fields[i, 1, HALO0 + a : HALO0 + b] = value
    first = HALO0 + 1
    level0_setup(fields, keep, diag, y0, first, rows - 2)
    level0_power(keep, y0, y1, first + 1, rows - 4)
    level0_power(keep, y1, y2, first + 2, rows - 6)
    level0_down(keep, diag, y1, y2, sources_in, first + 3, rows - 8)
    for source, target, lost in ((keep, keep_in, 1), (y1, y1_in, 2), (y2, y2_in, 3)):
        for i in range(source.shape[0]):
            for t in (0, 1):
                target[i, t] = source[i, t, inner(rows, lost)]
    take_ends(y0, rows, HALO0 + 1, HALO0 + 3, y0_in)
    take_ends(diag, rows, HALO0 + 1, HALO0 + 4, diag_in)


def level0_outer_kernel(
    rows,
    main,
    y_first,
    y_second,
    own_a,
    own_b,
    corner_a,
    corner_b,
    keep_in,
    y0_in,
    y1_in,
    y2_in,
    diag_in,
    sources_in,
    keep_out,
    y1_out,
    y2_out,
    sources,
    edges,
    *scratch,
):
    fields, keep, diag, y0, y1, y2 = scratch
    even, even_x = is_even("gy"), is_even("gx")
    total = rows + 2 * HALO0
    near, skip = HALO0 + 2, HALO0 - SENT
    for i in range(6):
        strip = slice(i * SENT, (i + 1) * SENT)
        fields[i, 0, skip:HALO0] = prev_of(even, y_first, y_second, strip)
        fields[i, 0, HALO0:near] = main[i, 0:2]
        fields[i, 0, total - near : total - HALO0] = main[i, rows - 2 : rows]
        fields[i, 0, HALO0 + rows : total - skip] = next_of(even, y_first, y_second, strip)
        for packets, lo, n, at in (
            ((corner_a, corner_b), i * SENT, SENT, skip),
            ((own_a, own_b), i * rows, 2, HALO0),
            ((own_a, own_b), (i + 1) * rows - 2, 2, total - near),
            ((corner_a, corner_b), PACKET + i * SENT, SENT, HALO0 + rows),
        ):
            for a, b, value in halo_tiles(even_x, packets, lo, lo + n):
                fields[i, 1, at + a : at + b] = value
    for i in (0, 1):
        for t in (0, 1):
            for at in (0, total - 1):
                fields[i, t, at] = jnp.zeros((Z, X), jnp.float32)
    for at, part in zip(ends(rows, 5, 8), (slice(0, 3), slice(rows - 5, rows - 2))):
        for i in range(6):
            for t in (0, 1):
                keep[i, t, at] = keep_in[i, t, part]
    put_ends(diag, rows, 5, 8, diag_in)
    put_ends(y0, rows, 5, 7, y0_in)
    for target, source, lost in ((y1, y1_in, 2), (y2, y2_in, 3)):
        n = rows - 2 * lost
        for at, part in zip(ends(rows, HALO0 + lost, HALO0 + lost + 2), (slice(0, 2), slice(n - 2, n))):
            for i in (0, 1):
                for t in (0, 1):
                    target[i, t, at] = source[i, t, part]
    for r in (1, total - 5):
        level0_setup(fields, keep, diag, y0, r, 4)
    for r in (2, total - 6):
        level0_power(keep, y0, y1, r, 4)
    for r in (3, total - 7):
        level0_power(keep, y1, y2, r, 4)
    for r in (4, total - 8):
        level0_down(keep, diag, y1, y2, sources, r, 4)
    for q in range(4):
        for t in (0, 1):
            sources[q, t, 1 : OWN - 1] = sources_in[q, t, 1 : OWN - 1]
    take_ends(keep, rows, 1, 5, keep_out)
    take_ends(y1, rows, 4, 6, y1_out)
    take_ends(y2, rows, 4, 7, y2_out)
    for p, power in enumerate((y0, y1, y2)):
        for side, start in enumerate((HALO0, HALO0 + rows - EDGE)):
            edges[p, side] = pack_rows(power, start)


def pack_rows(x, start):
    lane = lane_of()
    halo = None
    for i in (0, 1):
        for j in range(EDGE):
            at = i * EDGE + j
            value = roll_x(x[i, 1, start + j : start + j + 1], 4 + 8 * at)
            halo = value if halo is None else jnp.where((lane >> 3) == at, value, halo)
    return jnp.concatenate([x[i, 0, start : start + EDGE] for i in (0, 1)] + [halo], axis=0)


def squeeze(halo):
    lane = lane_of()
    last = halo[OWN - 1 : OWN]
    ahead = (lane >= WIDE) & (lane < 2 * WIDE)
    parts = [jnp.where(ahead, roll_x(last, WIDE), halo[0:1]), jnp.where(ahead, roll_x(last, 2 * WIDE - X), halo[1:2])]
    return jnp.concatenate(parts + [halo[2 : OWN - 1]], axis=0)


def unsqueeze(tiles):
    last = jnp.where(lane_of() < X // 2, roll_x(tiles[0:1], -WIDE), roll_x(tiles[1:2], X - 2 * WIDE))
    return jnp.concatenate([tiles, last], axis=0)


def combine_kernel(sources, edges, spread, own, first, second, edge_first, edge_second, gain):
    write_gains(jnp.max(spread[...], axis=0)[0:1], gain)
    p0, p1, p2 = (gain[POWERS + i] for i in range(3))
    for t in (0, 1):
        value = sources[0, t] - p0 * sources[1, t] + p1 * sources[2, t] - p2 * sources[3, t]
        own[t] = value
        for ref in (first, second):
            if t == 0:
                ref[0:OWN] = value
            else:
                ref[OWN:] = squeeze(value)
    even = is_even("gy")
    top, bottom = (p0 * edges[0, side] - p1 * edges[1, side] + p2 * edges[2, side] for side in (0, 1))
    edge_first[...] = jnp.where(even, top, bottom)
    edge_second[...] = jnp.where(even, bottom, top)


def coarse1_kernel(
    rows, coarse, y_first, y_second, own_a, own_b, corner_a, corner_b, gain, keep_in, y1_in, y2_in, keep_out, y1_out, y2_out,
    coef, keep0, x0, fields
):
    even, even_x = is_even("gy"), is_even("gx")
    own_x, corner_x = (own_a, own_b), (corner_a, corner_b)
    for p in (0, 1):
        to = p * GROUPS1
        strip = slice(FIELDS1 + p * OWN, FIELDS1 + (p + 1) * OWN)
        fields[0, to : to + OWN] = prev_of(even, y_first, y_second, strip)
        fields[0, to + OWN : to + 2 * OWN] = coarse[p * OWN : (p + 1) * OWN]
        fields[0, to + 2 * OWN : to + 3 * OWN] = next_of(even, y_first, y_second, strip)
        for part, (packets, lo) in enumerate(
            ((corner_x, FIELDS1), (own_x, 6 * rows), (corner_x, PACKET + FIELDS1))
        ):
            lo += p * OWN
            for a, b, value in halo_tiles(even_x, packets, lo, lo + OWN):
                fields[1, to + part * OWN + a : to + part * OWN + b] = value
    for t in (0, 1):
        for i, value in enumerate(packed_jacobian(fields[t, 0:GROUPS1], fields[t, GROUPS1 : 2 * GROUPS1], 1)):
            coef[i, t, 1 : SIZE1 - 1] = value

    def whole(inside, outside):
        n = outside.shape[0] // 2
        return jnp.concatenate([outside[0:n], inside, outside[n:]], axis=0)

    for i in range(6):
        for t in (0, 1):
            keep0[i, t, 1 : rows + 2 * HALO0 - 1] = whole(keep_in[i, t], keep_out[i, t])
    p0, p1, p2 = (gain[POWERS + i] for i in range(3))
    for i in (0, 1):
        for t in (0, 1):
            y0 = keep0[2 + i, t, HALO0 : HALO0 + rows] * keep0[4 + i, t, HALO0 : HALO0 + rows]
            y1, y2 = (whole(a[i, t], b[i, t]) for a, b in ((y1_in, y1_out), (y2_in, y2_out)))
            x0[i, t] = p0 * y0 - p1 * y1 + p2 * y2


def fields2_kernel(rows, coarse, y_first, y_second, own_a, own_b, corner_a, corner_b, out):
    even, even_x = is_even("gy"), is_even("gx")
    own_x, corner_x = (own_a, own_b), (corner_a, corner_b)
    near = slice(FIELDS2, FIELDS2 + 1)
    out[0, 0:1] = prev_of(even, y_first, y_second, near)
    out[0, 1:2] = coarse[2 * OWN : 2 * OWN + 1]
    out[0, 2:3] = next_of(even, y_first, y_second, near)
    for q, (packets, lo) in enumerate(
        ((corner_x, FIELDS2), (own_x, 6 * rows + 2 * OWN), (corner_x, PACKET + FIELDS2))
    ):
        out[1, q : q + 1] = halo_tiles(even_x, packets, lo, lo + 1)[0][2]


def level1_kernel(
    own, first, second, edge_a, edge_b, fields2, coef1, gain, packet, to_first, to_second, to_far_a, to_far_b, keep, y1, d1
):
    b1, x1 = keep.at[0], keep.at[1]
    even = is_even("gy")
    for t in (0, 1):
        b1[t, 1 + OWN : 1 + 2 * OWN] = own[t]
        for at, take in ((1, prev_of), (1 + 2 * OWN, next_of)):
            if t == 0:
                b1[t, at : at + OWN] = take(even, first, second, slice(0, OWN))
            else:
                b1[t, at : at + OWN] = unsqueeze(take(even, first, second, slice(OWN, 2 * OWN - 1)))
    g0, g1, g2 = (gain[3 + i] for i in range(3))
    n = GROUPS1
    packed_first(coef1, 0, b1, x1, d1, 1, n, g0)
    packed_step(1, coef1, 0, b1, x1, y1, d1, 2, n - 2, CARRY1, g1)
    packed_step(1, coef1, 0, b1, y1, x1, d1, 2, n - 2, CARRY2, g2)
    here = pl.ds(1 + OWN, OWN)
    values = []
    for t, (c, other, spread) in enumerate(packed_terms(x1, 1 + OWN, OWN, 1)):
        res = b1[t, here] - coef1[2, t, here] * c + coef1[1, t, here] * other + spread
        values.append(restrict_12([res[j : j + 1] for j in range(OWN)]))
        for ref in (to_far_a, to_far_b):
            ref[1 + t : 2 + t] = fields2[t, 1:2]
    value = jnp.where((sub_of() & 2) == 0, values[0], values[1])
    for ref in (packet, to_first, to_second, to_far_a, to_far_b):
        ref[0:1] = value
    for ref in (to_far_a, to_far_b):
        ref[3:] = jnp.broadcast_to(value, (ref.shape[0] - 3, Z, X))
    to_first[1:] = edge_a[...]
    to_second[1:] = edge_b[...]


def rest_kernel(
    own2, near_a, near_b, far_a, far_b, gain, coef1, fields2, keep0, iterate, keep1, out, coef2, d1, b2, x2, y2, d2, xu, yu, x0, y0, d0
):
    rows = out.shape[0] // (2 * Z)
    even = (sub_of() & 1) == 0
    b1, x1 = keep1.at[0], keep1.at[1]

    even_y, low = is_even("gy"), lax.rem(lax.axis_index("gy"), 4) < 2
    at = slice(0, 1)
    parts = [
        next_of(low, far_a, far_b, at),
        prev_of(even_y, near_a, near_b, at),
        own2[at],
        next_of(even_y, near_a, near_b, at),
        prev_of(low, far_a, far_b, at),
    ]
    for t, values in enumerate(split_fields2(jnp.concatenate(parts, axis=0))):
        b2[t, 1 : SIZE2 - 1] = values
        at = slice(1 + t, 2 + t)
        parts = [next_of(low, far_a, far_b, at), fields2[t], prev_of(low, far_a, far_b, at)]
        inverse, other, _ = packed_jacobian(*split_fields2(jnp.concatenate(parts, axis=0)), 2)
        coef2[0, t, 1 : SIZE2 - 1] = inverse
        coef2[1, t, 1 : SIZE2 - 1] = other

    n = HI2 - LO2
    g0, g1, g2 = (gain[6 + i] for i in range(3))
    packed_first(coef2, 0, b2, x2, d2, 1, n, g0)
    packed_step(2, coef2, 0, b2, x2, y2, d2, 1, n, CARRY1, g1)
    packed_step(2, coef2, 0, b2, y2, x2, d2, 1, n, CARRY2, g2)
    packed_step(2, coef2, 0, b2, x2, y2, d2, 1, n, None, g0)
    packed_step(2, coef2, 0, b2, y2, x2, d2, 2, n - 2, CARRY1, g1)
    packed_step(2, coef2, 0, b2, x2, y2, d2, 2, n - 2, CARRY2, g2)

    g0, g1, g2 = (gain[3 + i] for i in range(3))
    shift = LO_UP - LO1
    for t in (0, 1):
        for g in range(LO_UP, HI_UP):
            p = g % 4
            value = y2[t, g // 4 - LO2 + 1 : g // 4 - LO2 + 2]
            value = spread_x(spread_x(value, 1, p & 1), 2, p & 2)
            at = g - LO_UP + 1
            xu[t, at : at + 1] = x1[t, at + shift : at + shift + 1] + value
    n = HI_UP - LO_UP
    packed_step(1, coef1, shift, b1, xu, yu, d1, 2, n - 2, None, g0)
    packed_step(1, coef1, shift, b1, yu, xu, d1, 2, n - 2, CARRY1, g1)
    packed_step(1, coef1, shift, b1, xu, yu, d1, 3, n - 4, CARRY2, g2)

    g0, g1, g2 = (gain[i] for i in range(3))
    sides = [take(even_y, near_a, near_b, slice(1, 1 + EDGE_TILES)) for take in (prev_of, next_of)]

    def before(i, t, y):
        if 0 <= y < rows:
            return iterate[i, t, y : y + 1]
        side, j = (sides[0], y + EDGE) if y < 0 else (sides[1], y - rows)
        if t == 0:
            return side[i * EDGE + j : i * EDGE + j + 1]
        return roll_x(side[2 * EDGE :], -(4 + 8 * (i * EDGE + j)))

    for t in (0, 1):
        for row in range(-2, rows // 2 + 2):
            at = row // 2 - LO_UP + 1
            value = spread_x(yu[t, at : at + 1], 1, row & 1)
            for i, fine in enumerate((jnp.where(even, value, roll_z(value, 1)), jnp.where(even, roll_z(value, -1), value))):
                for y in (2 * row, 2 * row + 1):
                    if -EDGE <= y < rows + EDGE:
                        x0[i, t, y + HALO0 : y + HALO0 + 1] = before(i, t, y) + fine
    total = rows + 2 * HALO0
    for r, n in chunks(2, total - 2):
        cheb_step(0, keep0, x0, y0, d0, r, n, None, g0)
    for r, n in chunks(3, total - 3):
        cheb_step(0, keep0, y0, x0, d0, r, n, CARRY1, g1)
    for r, n in chunks(4, total - 4):
        last = cheb_step(0, keep0, x0, None, d0, r, n, CARRY2, g2, (0,))[0]
        for i in (0, 1):
            for j in range(n):
                out[pl.ds(i * Z * rows + r - HALO0 + j, Z, stride=rows), :] = last[i][j]


def call(kernel, out_shapes, scratch, *args, space=pltpu.VMEM, outs=None):
    out = [jax.ShapeDtypeStruct(shape, jnp.float32) for shape in out_shapes]
    return pl.pallas_call(
        kernel,
        out_shape=out,
        in_specs=[pl.BlockSpec(memory_space=space)] * len(args),
        out_specs=[pl.BlockSpec(memory_space=m) for m in outs or [pltpu.VMEM] * len(out)],
        scratch_shapes=[pltpu.VMEM(s, jnp.float32) if isinstance(s, tuple) else s for s in scratch],
        compiler_params=pltpu.CompilerParams(vmem_limit_bytes=24 * 2**20),
    )(*args)


def swap(value, axis, step):
    count = lax.axis_size(axis)
    assert count % 2 == 0
    pairs = [(i, (i + step) % count) for i in range(0, count, 2)]
    return lax.ppermute(value, axis, pairs + [(j, i) for i, j in pairs])


def swap_far(value, axis, step):
    count = lax.axis_size(axis)
    assert count % 4 == 0
    pairs = [(i + j, (i + j + 2 * step) % count) for i in range(0, count, 4) for j in (0, 1)]
    return lax.ppermute(value, axis, pairs + [(j, i) for i, j in pairs])


def exchange(first, second, axis):
    return swap(first, axis, -1), swap(second, axis, 1)


def body(state, previous, feed, kill):
    _, depth, rows, cols = state.shape
    assert depth == Z and cols == X and rows == 4 * OWN
    across, count = lax.axis_size("gx"), lax.axis_size("gy")
    total0 = rows + 2 * HALO0
    state = state.reshape(2 * Z * rows, X)
    previous = previous.reshape(2 * Z * rows, X)
    feed = feed.reshape(Z * rows, X)
    kill = kill.reshape(Z * rows, X)
    inputs = (state, previous, feed, kill)

    strip = (PACKET, Z, X)
    first, second, coarse, *inputs = call(
        functools.partial(first_kernel, rows),
        [strip, strip, (2 * OWN + 1, Z, X), *(a.shape for a in inputs)],
        [pltpu.SemaphoreType.DMA((4,))],
        *(pltpu.with_memory_space_constraint(a, pltpu.HBM) for a in inputs),
        space=pltpu.HBM,
    )
    y_packets = exchange(first, second, "gy")

    tiles = tiles_for(6 * rows + 2 * OWN + 1)
    state, _, feed, kill = inputs
    (spread,) = call(
        functools.partial(spread_kernel, rows), [(across * count, 5, X)], [], state, feed, kill, coarse
    )
    spread = lax.all_to_all(spread, ("gx", "gy"), 0, 0, tiled=True)
    first, second, main = call(
        functools.partial(pack_own_kernel, rows),
        [(tiles, Z, X), (tiles, Z, X), (6, rows, Z, X)],
        [(PER * tiles, Z, X)],
        *inputs,
        coarse,
    )
    own_x = exchange(first, second, "gx")
    tiles = tiles_for(2 * PACKET)
    corner_x = exchange(
        *call(pack_corner_kernel, [(tiles, Z, X), (tiles, Z, X)], [(PER * tiles, Z, X)], *y_packets), "gx"
    )

    strip, edge = (2 * OWN - 1, Z, X), (EDGE_TILES, Z, X)
    pair0 = (2, 2, total0, Z, X)
    work = [(6, 2, total0, Z, X), (6, 2, total0, Z, X), pair0, pair0, pair0, pair0]
    four = (4, 2, OWN, Z, X)
    inside = call(
        functools.partial(level0_inner_kernel, rows),
        [
            (6, 2, rows - 2, Z, X),
            (2, 2, 4, Z, X),
            (2, 2, rows - 4, Z, X),
            (2, 2, rows - 6, Z, X),
            (2, 2, 6, Z, X),
            four,
        ],
        work,
        main,
        *own_x,
    )
    keep_in, _, y1_in, y2_in, _, _ = inside
    keep_out, y1_out, y2_out, sources, edges = call(
        functools.partial(level0_outer_kernel, rows),
        [(6, 2, 8, Z, X), (2, 2, 4, Z, X), (2, 2, 6, Z, X), four, (3, 2, *edge)],
        work,
        main,
        *y_packets,
        *own_x,
        *corner_x,
        *inside,
    )
    own, first, second, edge_a, edge_b, gain = call(
        combine_kernel,
        [(2, OWN, Z, X), strip, strip, edge, edge, (POWERS + 3, Z, X)],
        [],
        sources,
        edges,
        spread,
    )
    coef1, keep0, iterate = call(
        functools.partial(coarse1_kernel, rows),
        [(3, 2, SIZE1, Z, X), (6, 2, total0, Z, X), (2, 2, rows, Z, X)],
        [(2, 2 * GROUPS1, Z, X)],
        coarse,
        *y_packets,
        *own_x,
        *corner_x,
        gain,
        keep_in,
        y1_in,
        y2_in,
        keep_out,
        y1_out,
        y2_out,
    )
    (fields2,) = call(
        functools.partial(fields2_kernel, rows), [(2, 3, Z, X)], [], coarse, *y_packets, *own_x, *corner_x
    )
    b_packets = exchange(first, second, "gy")

    one, two, up = (2, SIZE1, Z, X), (2, SIZE2, Z, X), (2, SIZE_UP, Z, X)
    near = (1 + EDGE_TILES, Z, X)
    packet, first, second, far_a, far_b, keep1 = call(
        level1_kernel,
        [(1, Z, X), near, near, (near[0] + 2, Z, X), (near[0] + 1, Z, X), (2, *one)],
        [one, one],
        own,
        *b_packets,
        edge_a,
        edge_b,
        fields2,
        coef1,
        gain,
    )
    far = (swap_far(far_a, "gy", 1), swap_far(far_b, "gy", -1))
    near = exchange(first, second, "gy")

    (out,) = call(
        rest_kernel,
        [(2 * Z * rows, X)],
        [(2, *two), one, two, two, two, two, up, up, pair0, pair0, pair0],
        packet,
        *near,
        *far,
        gain,
        coef1,
        fields2,
        keep0,
        iterate,
        keep1,
    )
    return out.reshape(2, Z, rows, X)


def solution(mesh):
    placed = (
        P(None, None, "gy", "gx"),
        P(None, None, "gy", "gx"),
        P(None, "gy", "gx"),
        P(None, "gy", "gx"),
    )
    return jax.shard_map(
        body, mesh=mesh, in_specs=placed, out_specs=P(None, None, "gy", "gx"), check_vma=False
    )
```

```python
import functools

import jax
import jax.numpy as jnp
from jax import lax
from jax.experimental import pallas as pl
from jax.experimental.pallas import tpu as pltpu
from jax.sharding import PartitionSpec as P

DIFF = (40.0, 20.0)
INV_STEP = 2.0
LOWER = 0.25

_CENTRE = (1.0 + LOWER) / 2.0
_HALF = (1.0 - LOWER) / 2.0
_SIGMA = _CENTRE / _HALF
_RHO0 = 1.0 / _SIGMA
_RHO1 = 1.0 / (2.0 * _SIGMA - _RHO0)
_RHO2 = 1.0 / (2.0 * _SIGMA - _RHO1)

Z = 8
X = 128
HALO0 = 4
SENT = 3
FIELDS1 = 6 * SENT
FIELDS2 = FIELDS1 + 8
PACKET = FIELDS2 + 1
WIDE = 42
PER = X // WIDE
EDGE = 3

LO1, HI1 = -4, 8
LO2, HI2 = -2, 3
LO_UP, HI_UP = -3, 7
SIZE1, SIZE2, SIZE_UP = HI1 - LO1 + 2, HI2 - LO2 + 2, HI_UP - LO_UP + 2
OWN = 4


def lane_of():
    return lax.broadcasted_iota(jnp.int32, (1, Z, X), 2)


def sub_of():
    return lax.broadcasted_iota(jnp.int32, (1, Z, X), 1)


def roll_x(tile, shift):
    shift = shift % X
    return pltpu.roll(tile, shift, 2) if shift else tile


def roll_z(tile, shift):
    shift = shift % Z
    return pltpu.roll(tile, shift, 1) if shift else tile


def chunks(lo, hi, step=4):
    return [(r, min(step, hi - r)) for r in range(lo, hi, step)]


def neighbour_sums(read, r, n, k, tiles=(0, 1)):
    lane = lane_of()
    low, high = lane < k, lane >= X - k
    centre = [read(t, r, n) for t in (0, 1)]
    right = [roll_x(c, k) for c in centre]
    left = [roll_x(c, -k) for c in centre]
    sums = []
    for t in tiles:
        c = centre[t]
        along_x = jnp.where(low, right[1 - t], right[t]) + jnp.where(high, left[1 - t], left[t])
        along_y = read(t, r - 1, n) + read(t, r + 1, n)
        along_z = 2.0 * roll_z(c, k) if 2 * k == Z else roll_z(c, k) + roll_z(c, -k)
        sums.append(along_x + along_y + along_z)
    return centre, sums


def jacobian(u, v, f, k, level):
    scale = 0.25**level
    product = u * v
    squared = v * v
    first = INV_STEP + squared + f + 6.0 * DIFF[0] * scale
    second = INV_STEP + f + k - 2.0 * product + 6.0 * DIFF[1] * scale
    return 2.0 * product, squared, 1.0 / first, 1.0 / second, first, second


def cheb_step(level, keep, source, target, d, r, n, carry, gain, tiles=(0, 1)):
    scale = 0.25**level
    k = 1 << level
    u, nb_u = neighbour_sums(lambda t, a, m: source[0, t, pl.ds(a, m)], r, n, k, tiles)
    v, nb_v = neighbour_sums(lambda t, a, m: source[1, t, pl.ds(a, m)], r, n, k, tiles)
    rows = pl.ds(r, n)
    out = []
    for t in tiles:
        cross, squared, inv_u, inv_v = (keep[i, t, rows] for i in range(4))
        res_u = inv_u * (keep[4, t, rows] - cross * v[t] + DIFF[0] * scale * nb_u[t]) - u[t]
        res_v = inv_v * (keep[5, t, rows] + squared * u[t] + DIFF[1] * scale * nb_v[t]) - v[t]
        du, dv = gain * res_u, gain * res_v
        if carry is not None:
            du = du + carry * d[0, t, rows]
            dv = dv + carry * d[1, t, rows]
        if target is not None:
            d[0, t, rows] = du
            d[1, t, rows] = dv
            target[0, t, rows] = u[t] + du
            target[1, t, rows] = v[t] + dv
        out.append((u[t] + du, v[t] + dv))
    return out


def next_power(keep, source, r, n):
    u, nb_u = neighbour_sums(lambda t, a, m: source[0, t, pl.ds(a, m)], r, n, 1)
    v, nb_v = neighbour_sums(lambda t, a, m: source[1, t, pl.ds(a, m)], r, n, 1)
    rows = pl.ds(r, n)
    first, second = [], []
    for t in (0, 1):
        cross, squared, inv_u, inv_v = (keep[i, t, rows] for i in range(4))
        first.append(u[t] + inv_u * (cross * v[t] - DIFF[0] * nb_u[t]))
        second.append(v[t] - inv_v * (squared * u[t] + DIFF[1] * nb_v[t]))
    return first, second


CARRY1 = _RHO1 * _RHO0
CARRY2 = _RHO2 * _RHO1


POWERS = 9


def write_gains(spread, out):
    lane = lax.broadcasted_iota(jnp.int32, (1, X), 1)
    for level in range(3):
        top = jnp.max(jnp.where(lane == level, spread, 0.0), axis=1, keepdims=True)
        tau = 1.0 / (1.0 + jnp.broadcast_to(top, (Z, X)))
        for i, factor in enumerate((1.0 / _CENTRE, 2.0 * _RHO1 / _HALF, 2.0 * _RHO2 / _HALF)):
            out[3 * level + i] = factor * tau
    g0, g1, g2 = (out[i] for i in range(3))
    first, second = g0 + CARRY1 * g0 + g1, g1 * g0
    out[POWERS] = first + CARRY2 * (CARRY1 * g0 + g1) + g2
    out[POWERS + 1] = second + CARRY2 * second + g2 * first
    out[POWERS + 2] = g2 * second


def pair_rows(value):
    n = value.shape[0] // 2
    pairs = value.reshape(n, 2, Z, X)
    return pairs[:, 0] + pairs[:, 1]


def restrict_01(first, second):
    lane, sub = lane_of(), sub_of()
    across = []
    for value in (first, second):
        a, b = value[0:1], value[1:2]
        across.append(jnp.where((lane & 1) == 0, a + roll_x(a, -1), b + roll_x(b, 1)))
    a, b = across
    return 0.125 * jnp.where((sub & 1) == 0, a + roll_z(a, -1), b + roll_z(b, 1))


def restrict_12(groups):
    lane, sub = lane_of(), sub_of()
    out = None
    for p, value in enumerate(groups):
        value = value + roll_x(value, 1 if p & 1 else -1)
        value = value + roll_x(value, 2 if p & 2 else -2)
        out = value if out is None else jnp.where((lane & 3) == p, value, out)
    return 0.125 * (out + jnp.where((sub & 2) == 0, roll_z(out, -2), roll_z(out, 2)))


def spread_x(tile, k, phase):
    return jnp.where((lane_of() & k) == phase, tile, roll_x(tile, -k if phase else k))


def packed_jacobian(uv, fk, level):
    scale = 0.25**level
    even = (sub_of() & 1) == 0
    u, v = jnp.where(even, uv, roll_z(uv, 1)), jnp.where(even, roll_z(uv, -1), uv)
    f, k = jnp.where(even, fk, roll_z(fk, 1)), jnp.where(even, roll_z(fk, -1), fk)
    product, squared = u * v, v * v
    diag = jnp.where(
        even,
        INV_STEP + squared + f + 6.0 * DIFF[0] * scale,
        INV_STEP + f + k - 2.0 * product + 6.0 * DIFF[1] * scale,
    )
    return 1.0 / diag, jnp.where(even, -2.0 * product, squared), diag


def packed_spread(uv, fk, level):
    scale = 0.25**level
    even = (sub_of() & 1) == 0
    inverse, other, _ = packed_jacobian(uv, fk, level)
    return jnp.where(even, 6.0 * DIFF[0] * scale - other, 6.0 * DIFF[1] * scale + other) * inverse


def packed_terms(source, g, n, level):
    k = 1 << level
    lane, sub = lane_of(), sub_of()
    even = (sub & 1) == 0
    first, last = (lane & (k - 1)) == 0, (lane & (k - 1)) == k - 1
    low, high = lane < k, lane >= X - k
    diff = jnp.where(even, DIFF[0] * 0.25**level, DIFF[1] * 0.25**level)
    wide = [source[t, pl.ds(g - 1, n + 2)] for t in (0, 1)]
    centre = [w[1 : n + 1] for w in wide]
    right = [roll_x(c, k) for c in centre]
    left = [roll_x(c, -k) for c in centre]
    out = []
    for t in (0, 1):
        c, w = centre[t], wide[t]
        total = jnp.where(low, right[1 - t], right[t]) + jnp.where(high, left[1 - t], left[t])
        if k == 2:
            ahead, back = roll_x(w, 1), roll_x(w, -1)
            total = total + jnp.where(first, back[0:n], ahead[1 : n + 1])
            total = total + jnp.where(last, ahead[2 : n + 2], back[1 : n + 1])
            total = total + roll_z(c, 2) + roll_z(c, -2)
        else:
            total = total + jnp.where(first, roll_x(w[0:n], -(k - 1)), roll_x(c, 1))
            total = total + jnp.where(last, roll_x(w[2 : n + 2], k - 1), roll_x(c, -1))
            total = total + 2.0 * roll_z(c, 4)
        other = jnp.where(even, roll_z(c, -1), roll_z(c, 1))
        out.append((c, other, diff * total))
    return out


def packed_first(coef, shift, b, target, d, g, n, gain):
    for t in (0, 1):
        value = gain * coef[0, t, pl.ds(g + shift, n)] * b[t, pl.ds(g + shift, n)]
        d[t, pl.ds(g, n)] = value
        target[t, pl.ds(g, n)] = value


def packed_step(level, coef, shift, b, source, target, d, g, n, carry, gain):
    for t, (c, other, spread) in enumerate(packed_terms(source, g, n, level)):
        at = pl.ds(g + shift, n)
        res = coef[0, t, at] * (b[t, at] + coef[1, t, at] * other + spread) - c
        delta = gain * res
        if carry is not None:
            delta = delta + carry * d[t, pl.ds(g, n)]
        d[t, pl.ds(g, n)] = delta
        target[t, pl.ds(g, n)] = c + delta


def plane(ref, f, y, rows):
    return ref[pl.ds(f * Z * rows + y, Z, stride=rows), :]


def is_even(axis):
    return lax.rem(lax.axis_index(axis), 2) == 0


def prev_of(even, first, second, at):
    return jnp.where(even, first[at], second[at])


def next_of(even, first, second, at):
    return jnp.where(even, second[at], first[at])


SOURCES = ((0, 0), (0, 1), (1, 0), (1, 1), (2, 0), (3, 0))


def first_kernel(rows, state, previous, feed, kill, first, second, coarse, *rest):
    held, sems = rest[:4], rest[4]
    copies = [
        pltpu.make_async_copy(ref, to, sems.at[i]) for i, (ref, to) in enumerate(zip((state, previous, feed, kill), held))
    ]
    for copy in copies:
        copy.start()
    for copy in copies:
        copy.wait()
    even = is_even("gy")
    values = []
    for i, (j, f) in enumerate(SOURCES):
        wanted = range(rows) if i not in (2, 3) else [*range(SENT), *range(rows - SENT, rows)]
        values.append({y: plane(held[j], f, y, rows)[None] for y in wanted})
    for i in (2, 3):
        weight = DIFF[i - 2] / INV_STEP
        values[i][SENT - 1] = values[i][SENT - 1] + weight * values[i - 2][SENT]
        values[i][rows - SENT] = values[i][rows - SENT] + weight * values[i - 2][rows - SENT - 1]
    for i in range(6):
        for y in range(SENT):
            top, bottom = values[i][y], values[i][rows - SENT + y]
            at = slice(i * SENT + y, i * SENT + y + 1)
            first[at] = jnp.where(even, top, bottom)
            second[at] = jnp.where(even, bottom, top)
    pairs = []
    for p, (i, j) in enumerate(((0, 1), (4, 5))):
        parts = []
        for g in range(OWN):
            sums = [
                jnp.concatenate([value[4 * g + 2 * q] + value[4 * g + 2 * q + 1] for q in (0, 1)], axis=0)
                for value in (values[i], values[j])
            ]
            parts.append(restrict_01(*sums))
        pairs.append(jnp.concatenate(parts, axis=0))
        coarse[p * OWN : (p + 1) * OWN] = pairs[p]
        for ref in (first, second):
            ref[FIELDS1 + p * OWN : FIELDS1 + (p + 1) * OWN] = pairs[p]
    uv, fk = (restrict_12([pair[j : j + 1] for j in range(OWN)]) for pair in pairs)
    both = jnp.where((sub_of() & 2) == 0, uv, fk)
    coarse[2 * OWN : 2 * OWN + 1] = both
    for ref in (first, second):
        ref[FIELDS2 : FIELDS2 + 1] = both


def split_fields2(both):
    low = (sub_of() & 2) == 0
    return jnp.where(low, both, roll_z(both, 2)), jnp.where(low, roll_z(both, -2), both)


def write_spread(fields, coarse, out):
    lane = lax.broadcasted_iota(jnp.int32, (1, X), 1)
    cross, squared, inv_u, inv_v, _, _ = jacobian(*fields, 0)
    tops = [jnp.max(jnp.maximum((6.0 * DIFF[0] + cross) * inv_u, (6.0 * DIFF[1] + squared) * inv_v), axis=0)]
    tops.append(jnp.max(packed_spread(coarse[0:OWN], coarse[OWN : 2 * OWN], 1), axis=0))
    tops.append(packed_spread(*split_fields2(coarse[2 * OWN : 2 * OWN + 1]), 2)[0])
    result = jnp.zeros((1, X), jnp.float32)
    for level, top in enumerate(tops):
        top = jnp.max(jnp.max(top, axis=0, keepdims=True), axis=1, keepdims=True)
        result = jnp.where(lane == level, jnp.broadcast_to(top, (1, X)), result)
    out[...] = jnp.broadcast_to(result[None], out.shape)


GROUPS1 = HI1 - LO1
GROUPS2 = HI2 - LO2


def tiles_for(entries):
    return -(-entries // PER)


def pack_edges(entries, even, first, second):
    lane = lane_of()
    share = first.shape[0]
    left, right = None, None
    for j in range(PER):
        part = entries[j * share : (j + 1) * share]
        a, b = roll_x(part, WIDE * j), roll_x(part, WIDE + WIDE * j)
        left = a if left is None else jnp.where(lane >= WIDE * j, a, left)
        right = b if right is None else jnp.where(lane >= WIDE * j, b, right)
    first[...] = jnp.where(even, left, right)
    second[...] = jnp.where(even, right, left)


def halo_tiles(even, packets, lo, hi):
    first, second = packets
    share = first.shape[0]
    lane = lane_of()
    out = []
    for j in range(PER):
        a, b = max(lo, j * share), min(hi, (j + 1) * share)
        if a < b:
            strip = slice(a - j * share, b - j * share)
            left, right = prev_of(even, first, second, strip), next_of(even, first, second, strip)
            value = jnp.where(lane < X // 2, roll_x(right, -WIDE * j), roll_x(left, X - WIDE - WIDE * j))
            out.append((a - lo, b - lo, value))
    return out


def pack_own_kernel(
    rows, state, previous, feed, kill, coarse, first, second, spread, main, held, copies, sem
):
    inputs = (state, previous, feed, kill)

    def field(i):
        j, f = SOURCES[i]
        return jnp.stack([plane(inputs[j], f, y, rows) for y in range(rows)])

    fields = {i: field(i) for i in (0, 1, 4, 5)}
    write_spread([fields[i] for i in (0, 1, 4, 5)], coarse, copies)
    copy = pltpu.make_async_copy(copies, spread, sem)
    copy.start()

    @pl.when(lax.axis_index("gx") >= 0)
    def _():
        for i in range(6):
            value = field(i)
            main[i] = value
            held[i * rows : (i + 1) * rows] = value
        held[6 * rows : 6 * rows + 2 * OWN + 1] = coarse[...]
        pack_edges(held, is_even("gx"), first, second)

    copy.wait()


def pack_corner_kernel(y_first, y_second, first, second, held):
    even = is_even("gy")
    every = slice(0, PACKET)
    held[0:PACKET] = prev_of(even, y_first, y_second, every)
    held[PACKET : 2 * PACKET] = next_of(even, y_first, y_second, every)
    pack_edges(held, is_even("gx"), first, second)


EDGE_TILES = 2 * EDGE + 1


def level0_setup(fields, keep, diag, power, r, n):
    at = pl.ds(r, n)
    u, nb_u = neighbour_sums(lambda t, a, m: fields[0, t, pl.ds(a, m)], r, n, 1)
    v, nb_v = neighbour_sums(lambda t, a, m: fields[1, t, pl.ds(a, m)], r, n, 1)
    for t in (0, 1):
        f, k = fields[4, t, at], fields[5, t, at]
        cross, squared, inv_u, inv_v, first, second = jacobian(u[t], v[t], f, k, 0)
        react = u[t] * squared
        b_u = DIFF[0] * (nb_u[t] - 6.0 * u[t]) - INV_STEP * (u[t] - fields[2, t, at]) - react + f * (1.0 - u[t])
        b_v = DIFF[1] * (nb_v[t] - 6.0 * v[t]) - INV_STEP * (v[t] - fields[3, t, at]) + react - (f + k) * v[t]
        for i, value in enumerate((cross, squared, inv_u, inv_v, b_u, b_v)):
            keep[i, t, at] = value
        for i, value in enumerate((first, second)):
            diag[i, t, at] = value
        for i, value in enumerate((inv_u * b_u, inv_v * b_v)):
            power[i, t, at] = value


def level0_power(keep, source, target, r, n):
    for i, values in enumerate(next_power(keep, source, r, n)):
        for t in (0, 1):
            target[i, t, pl.ds(r, n)] = values[t]


def level0_down(keep, diag, y1, y2, sources, r, n):
    at = pl.ds(r, n)
    last = next_power(keep, y2, r, n)
    for t in (0, 1):
        both = [diag[i, t, at] for i in (0, 1)]
        parts = [[keep[4 + i, t, at] for i in (0, 1)]]
        parts += [[both[i] * power[i, t, at] for i in (0, 1)] for power in (y1, y2)]
        parts.append([both[i] * last[i][t] for i in (0, 1)])
        for q, part in enumerate(parts):
            u, v = (pair_rows(value) for value in part)
            for j in range(n // 4):
                value = restrict_01(u[2 * j : 2 * j + 2], v[2 * j : 2 * j + 2])
                sources[q, t, pl.ds((r - HALO0) // 4 + j, 1)] = value


def inner(rows, lost):
    return slice(HALO0 + lost, HALO0 + rows - lost)


def ends(rows, lo, hi):
    total = rows + 2 * HALO0
    return slice(lo, hi), slice(total - hi, total - lo)


def put_ends(target, rows, lo, hi, source):
    n = hi - lo
    for at, part in zip(ends(rows, lo, hi), (slice(0, n), slice(n, 2 * n))):
        for i in range(target.shape[0]):
            for t in (0, 1):
                target[i, t, at] = source[i, t, part]


def take_ends(source, rows, lo, hi, target):
    n = hi - lo
    for at, part in zip(ends(rows, lo, hi), (slice(0, n), slice(n, 2 * n))):
        for i in range(source.shape[0]):
            for t in (0, 1):
                target[i, t, part] = source[i, t, at]


def level0_inner_kernel(rows, main, own_a, own_b, keep_in, y0_in, y1_in, y2_in, diag_in, sources_in, *scratch):
    fields, keep, diag, y0, y1, y2 = scratch
    even_x = is_even("gx")
    for i in range(6):
        fields[i, 0, HALO0 : HALO0 + rows] = main[i]
        for a, b, value in halo_tiles(even_x, (own_a, own_b), i * rows, (i + 1) * rows):
            fields[i, 1, HALO0 + a : HALO0 + b] = value
    first = HALO0 + 1
    level0_setup(fields, keep, diag, y0, first, rows - 2)
    level0_power(keep, y0, y1, first + 1, rows - 4)
    level0_power(keep, y1, y2, first + 2, rows - 6)
    level0_down(keep, diag, y1, y2, sources_in, first + 3, rows - 8)
    for source, target, lost in ((keep, keep_in, 1), (y1, y1_in, 2), (y2, y2_in, 3)):
        for i in range(source.shape[0]):
            for t in (0, 1):
                target[i, t] = source[i, t, inner(rows, lost)]
    take_ends(y0, rows, HALO0 + 1, HALO0 + 3, y0_in)
    take_ends(diag, rows, HALO0 + 1, HALO0 + 4, diag_in)


def level0_outer_kernel(
    rows,
    main,
    y_first,
    y_second,
    own_a,
    own_b,
    corner_a,
    corner_b,
    keep_in,
    y0_in,
    y1_in,
    y2_in,
    diag_in,
    sources_in,
    keep_out,
    y1_out,
    y2_out,
    sources,
    edges,
    *scratch,
):
    fields, keep, diag, y0, y1, y2 = scratch
    even, even_x = is_even("gy"), is_even("gx")
    total = rows + 2 * HALO0
    near, skip = HALO0 + 2, HALO0 - SENT
    for i in range(6):
        strip = slice(i * SENT, (i + 1) * SENT)
        fields[i, 0, skip:HALO0] = prev_of(even, y_first, y_second, strip)
        fields[i, 0, HALO0:near] = main[i, 0:2]
        fields[i, 0, total - near : total - HALO0] = main[i, rows - 2 : rows]
        fields[i, 0, HALO0 + rows : total - skip] = next_of(even, y_first, y_second, strip)
        for packets, lo, n, at in (
            ((corner_a, corner_b), i * SENT, SENT, skip),
            ((own_a, own_b), i * rows, 2, HALO0),
            ((own_a, own_b), (i + 1) * rows - 2, 2, total - near),
            ((corner_a, corner_b), PACKET + i * SENT, SENT, HALO0 + rows),
        ):
            for a, b, value in halo_tiles(even_x, packets, lo, lo + n):
                fields[i, 1, at + a : at + b] = value
    for i in (0, 1):
        for t in (0, 1):
            for at in (0, total - 1):
                fields[i, t, at] = jnp.zeros((Z, X), jnp.float32)
    for at, part in zip(ends(rows, 5, 8), (slice(0, 3), slice(rows - 5, rows - 2))):
        for i in range(6):
            for t in (0, 1):
                keep[i, t, at] = keep_in[i, t, part]
    put_ends(diag, rows, 5, 8, diag_in)
    put_ends(y0, rows, 5, 7, y0_in)
    for target, source, lost in ((y1, y1_in, 2), (y2, y2_in, 3)):
        n = rows - 2 * lost
        for at, part in zip(ends(rows, HALO0 + lost, HALO0 + lost + 2), (slice(0, 2), slice(n - 2, n))):
            for i in (0, 1):
                for t in (0, 1):
                    target[i, t, at] = source[i, t, part]
    for r in (1, total - 5):
        level0_setup(fields, keep, diag, y0, r, 4)
    for r in (2, total - 6):
        level0_power(keep, y0, y1, r, 4)
    for r in (3, total - 7):
        level0_power(keep, y1, y2, r, 4)
    for r in (4, total - 8):
        level0_down(keep, diag, y1, y2, sources, r, 4)
    for q in range(4):
        for t in (0, 1):
            sources[q, t, 1 : OWN - 1] = sources_in[q, t, 1 : OWN - 1]
    take_ends(keep, rows, 1, 5, keep_out)
    take_ends(y1, rows, 4, 6, y1_out)
    take_ends(y2, rows, 4, 7, y2_out)
    for p, power in enumerate((y0, y1, y2)):
        for side, start in enumerate((HALO0, HALO0 + rows - EDGE)):
            edges[p, side] = pack_rows(power, start)


def pack_rows(x, start):
    lane = lane_of()
    halo = None
    for i in (0, 1):
        for j in range(EDGE):
            at = i * EDGE + j
            value = roll_x(x[i, 1, start + j : start + j + 1], 4 + 8 * at)
            halo = value if halo is None else jnp.where((lane >> 3) == at, value, halo)
    return jnp.concatenate([x[i, 0, start : start + EDGE] for i in (0, 1)] + [halo], axis=0)


def squeeze(halo):
    lane = lane_of()
    last = halo[OWN - 1 : OWN]
    ahead = (lane >= WIDE) & (lane < 2 * WIDE)
    parts = [jnp.where(ahead, roll_x(last, WIDE), halo[0:1]), jnp.where(ahead, roll_x(last, 2 * WIDE - X), halo[1:2])]
    return jnp.concatenate(parts + [halo[2 : OWN - 1]], axis=0)


def unsqueeze(tiles):
    last = jnp.where(lane_of() < X // 2, roll_x(tiles[0:1], -WIDE), roll_x(tiles[1:2], X - 2 * WIDE))
    return jnp.concatenate([tiles, last], axis=0)


def combine_kernel(sources, edges, spread, own, first, second, edge_first, edge_second, gain):
    write_gains(jnp.max(spread[...], axis=0)[0:1], gain)
    p0, p1, p2 = (gain[POWERS + i] for i in range(3))
    for t in (0, 1):
        value = sources[0, t] - p0 * sources[1, t] + p1 * sources[2, t] - p2 * sources[3, t]
        own[t] = value
        for ref in (first, second):
            if t == 0:
                ref[0:OWN] = value
            else:
                ref[OWN:] = squeeze(value)
    even = is_even("gy")
    top, bottom = (p0 * edges[0, side] - p1 * edges[1, side] + p2 * edges[2, side] for side in (0, 1))
    edge_first[...] = jnp.where(even, top, bottom)
    edge_second[...] = jnp.where(even, bottom, top)


def coarse1_kernel(
    rows, coarse, y_first, y_second, own_a, own_b, corner_a, corner_b, gain, keep_in, y1_in, y2_in, keep_out, y1_out, y2_out,
    coef, keep0, x0, fields
):
    even, even_x = is_even("gy"), is_even("gx")
    own_x, corner_x = (own_a, own_b), (corner_a, corner_b)
    for p in (0, 1):
        to = p * GROUPS1
        strip = slice(FIELDS1 + p * OWN, FIELDS1 + (p + 1) * OWN)
        fields[0, to : to + OWN] = prev_of(even, y_first, y_second, strip)
        fields[0, to + OWN : to + 2 * OWN] = coarse[p * OWN : (p + 1) * OWN]
        fields[0, to + 2 * OWN : to + 3 * OWN] = next_of(even, y_first, y_second, strip)
        for part, (packets, lo) in enumerate(
            ((corner_x, FIELDS1), (own_x, 6 * rows), (corner_x, PACKET + FIELDS1))
        ):
            lo += p * OWN
            for a, b, value in halo_tiles(even_x, packets, lo, lo + OWN):
                fields[1, to + part * OWN + a : to + part * OWN + b] = value
    for t in (0, 1):
        for i, value in enumerate(packed_jacobian(fields[t, 0:GROUPS1], fields[t, GROUPS1 : 2 * GROUPS1], 1)):
            coef[i, t, 1 : SIZE1 - 1] = value

    def whole(inside, outside):
        n = outside.shape[0] // 2
        return jnp.concatenate([outside[0:n], inside, outside[n:]], axis=0)

    for i in range(6):
        for t in (0, 1):
            keep0[i, t, 1 : rows + 2 * HALO0 - 1] = whole(keep_in[i, t], keep_out[i, t])
    p0, p1, p2 = (gain[POWERS + i] for i in range(3))
    for i in (0, 1):
        for t in (0, 1):
            y0 = keep0[2 + i, t, HALO0 : HALO0 + rows] * keep0[4 + i, t, HALO0 : HALO0 + rows]
            y1, y2 = (whole(a[i, t], b[i, t]) for a, b in ((y1_in, y1_out), (y2_in, y2_out)))
            x0[i, t] = p0 * y0 - p1 * y1 + p2 * y2


def fields2_kernel(rows, coarse, y_first, y_second, own_a, own_b, corner_a, corner_b, out):
    even, even_x = is_even("gy"), is_even("gx")
    own_x, corner_x = (own_a, own_b), (corner_a, corner_b)
    near = slice(FIELDS2, FIELDS2 + 1)
    out[0, 0:1] = prev_of(even, y_first, y_second, near)
    out[0, 1:2] = coarse[2 * OWN : 2 * OWN + 1]
    out[0, 2:3] = next_of(even, y_first, y_second, near)
    for q, (packets, lo) in enumerate(
        ((corner_x, FIELDS2), (own_x, 6 * rows + 2 * OWN), (corner_x, PACKET + FIELDS2))
    ):
        out[1, q : q + 1] = halo_tiles(even_x, packets, lo, lo + 1)[0][2]


def level1_kernel(
    own, first, second, edge_a, edge_b, fields2, coef1, gain, packet, to_first, to_second, to_far_a, to_far_b, keep, y1, d1
):
    b1, x1 = keep.at[0], keep.at[1]
    even = is_even("gy")
    for t in (0, 1):
        b1[t, 1 + OWN : 1 + 2 * OWN] = own[t]
        for at, take in ((1, prev_of), (1 + 2 * OWN, next_of)):
            if t == 0:
                b1[t, at : at + OWN] = take(even, first, second, slice(0, OWN))
            else:
                b1[t, at : at + OWN] = unsqueeze(take(even, first, second, slice(OWN, 2 * OWN - 1)))
    g0, g1, g2 = (gain[3 + i] for i in range(3))
    n = GROUPS1
    packed_first(coef1, 0, b1, x1, d1, 1, n, g0)
    packed_step(1, coef1, 0, b1, x1, y1, d1, 2, n - 2, CARRY1, g1)
    packed_step(1, coef1, 0, b1, y1, x1, d1, 2, n - 2, CARRY2, g2)
    here = pl.ds(1 + OWN, OWN)
    values = []
    for t, (c, other, spread) in enumerate(packed_terms(x1, 1 + OWN, OWN, 1)):
        res = b1[t, here] - coef1[2, t, here] * c + coef1[1, t, here] * other + spread
        values.append(restrict_12([res[j : j + 1] for j in range(OWN)]))
        for ref in (to_far_a, to_far_b):
            ref[1 + t : 2 + t] = fields2[t, 1:2]
    value = jnp.where((sub_of() & 2) == 0, values[0], values[1])
    for ref in (packet, to_first, to_second, to_far_a, to_far_b):
        ref[0:1] = value
    for ref in (to_far_a, to_far_b):
        ref[3:] = jnp.broadcast_to(value, (ref.shape[0] - 3, Z, X))
    to_first[1:] = edge_a[...]
    to_second[1:] = edge_b[...]


def rest_kernel(
    own2, near_a, near_b, far_a, far_b, gain, coef1, fields2, keep0, iterate, keep1, out, coef2, d1, b2, x2, y2, d2, xu, yu, x0, y0, d0
):
    rows = out.shape[0] // (2 * Z)
    even = (sub_of() & 1) == 0
    b1, x1 = keep1.at[0], keep1.at[1]

    even_y, low = is_even("gy"), lax.rem(lax.axis_index("gy"), 4) < 2
    at = slice(0, 1)
    parts = [
        next_of(low, far_a, far_b, at),
        prev_of(even_y, near_a, near_b, at),
        own2[at],
        next_of(even_y, near_a, near_b, at),
        prev_of(low, far_a, far_b, at),
    ]
    for t, values in enumerate(split_fields2(jnp.concatenate(parts, axis=0))):
        b2[t, 1 : SIZE2 - 1] = values
        at = slice(1 + t, 2 + t)
        parts = [next_of(low, far_a, far_b, at), fields2[t], prev_of(low, far_a, far_b, at)]
        inverse, other, _ = packed_jacobian(*split_fields2(jnp.concatenate(parts, axis=0)), 2)
        coef2[0, t, 1 : SIZE2 - 1] = inverse
        coef2[1, t, 1 : SIZE2 - 1] = other

    n = HI2 - LO2
    g0, g1, g2 = (gain[6 + i] for i in range(3))
    packed_first(coef2, 0, b2, x2, d2, 1, n, g0)
    packed_step(2, coef2, 0, b2, x2, y2, d2, 1, n, CARRY1, g1)
    packed_step(2, coef2, 0, b2, y2, x2, d2, 1, n, CARRY2, g2)
    packed_step(2, coef2, 0, b2, x2, y2, d2, 1, n, None, g0)
    packed_step(2, coef2, 0, b2, y2, x2, d2, 2, n - 2, CARRY1, g1)
    packed_step(2, coef2, 0, b2, x2, y2, d2, 2, n - 2, CARRY2, g2)

    g0, g1, g2 = (gain[3 + i] for i in range(3))
    shift = LO_UP - LO1
    for t in (0, 1):
        for g in range(LO_UP, HI_UP):
            p = g % 4
            value = y2[t, g // 4 - LO2 + 1 : g // 4 - LO2 + 2]
            value = spread_x(spread_x(value, 1, p & 1), 2, p & 2)
            at = g - LO_UP + 1
            xu[t, at : at + 1] = x1[t, at + shift : at + shift + 1] + value
    n = HI_UP - LO_UP
    packed_step(1, coef1, shift, b1, xu, yu, d1, 2, n - 2, None, g0)
    packed_step(1, coef1, shift, b1, yu, xu, d1, 2, n - 2, CARRY1, g1)
    packed_step(1, coef1, shift, b1, xu, yu, d1, 3, n - 4, CARRY2, g2)

    g0, g1, g2 = (gain[i] for i in range(3))
    sides = [take(even_y, near_a, near_b, slice(1, 1 + EDGE_TILES)) for take in (prev_of, next_of)]

    def before(i, t, y):
        if 0 <= y < rows:
            return iterate[i, t, y : y + 1]
        side, j = (sides[0], y + EDGE) if y < 0 else (sides[1], y - rows)
        if t == 0:
            return side[i * EDGE + j : i * EDGE + j + 1]
        return roll_x(side[2 * EDGE :], -(4 + 8 * (i * EDGE + j)))

    for t in (0, 1):
        for row in range(-2, rows // 2 + 2):
            at = row // 2 - LO_UP + 1
            value = spread_x(yu[t, at : at + 1], 1, row & 1)
            for i, fine in enumerate((jnp.where(even, value, roll_z(value, 1)), jnp.where(even, roll_z(value, -1), value))):
                for y in (2 * row, 2 * row + 1):
                    if -EDGE <= y < rows + EDGE:
                        x0[i, t, y + HALO0 : y + HALO0 + 1] = before(i, t, y) + fine
    total = rows + 2 * HALO0
    for r, n in chunks(2, total - 2):
        cheb_step(0, keep0, x0, y0, d0, r, n, None, g0)
    for r, n in chunks(3, total - 3):
        cheb_step(0, keep0, y0, x0, d0, r, n, CARRY1, g1)
    for r, n in chunks(4, total - 4):
        last = cheb_step(0, keep0, x0, None, d0, r, n, CARRY2, g2, (0,))[0]
        for i in (0, 1):
            for j in range(n):
                out[pl.ds(i * Z * rows + r - HALO0 + j, Z, stride=rows), :] = last[i][j]


def call(kernel, out_shapes, scratch, *args, space=pltpu.VMEM, outs=None):
    out = [jax.ShapeDtypeStruct(shape, jnp.float32) for shape in out_shapes]
    return pl.pallas_call(
        kernel,
        out_shape=out,
        in_specs=[pl.BlockSpec(memory_space=space)] * len(args),
        out_specs=[pl.BlockSpec(memory_space=m) for m in outs or [pltpu.VMEM] * len(out)],
        scratch_shapes=[pltpu.VMEM(s, jnp.float32) if isinstance(s, tuple) else s for s in scratch],
        compiler_params=pltpu.CompilerParams(vmem_limit_bytes=24 * 2**20),
    )(*args)


def swap(value, axis, step):
    count = lax.axis_size(axis)
    assert count % 2 == 0
    pairs = [(i, (i + step) % count) for i in range(0, count, 2)]
    return lax.ppermute(value, axis, pairs + [(j, i) for i, j in pairs])


def swap_far(value, axis, step):
    count = lax.axis_size(axis)
    assert count % 4 == 0
    pairs = [(i + j, (i + j + 2 * step) % count) for i in range(0, count, 4) for j in (0, 1)]
    return lax.ppermute(value, axis, pairs + [(j, i) for i, j in pairs])


def exchange(first, second, axis):
    return swap(first, axis, -1), swap(second, axis, 1)


def body(state, previous, feed, kill):
    _, depth, rows, cols = state.shape
    assert depth == Z and cols == X and rows == 4 * OWN
    across, count = lax.axis_size("gx"), lax.axis_size("gy")
    total0 = rows + 2 * HALO0
    state = state.reshape(2 * Z * rows, X)
    previous = previous.reshape(2 * Z * rows, X)
    feed = feed.reshape(Z * rows, X)
    kill = kill.reshape(Z * rows, X)
    inputs = (state, previous, feed, kill)

    strip = (PACKET, Z, X)
    first, second, coarse, *inputs = call(
        functools.partial(first_kernel, rows),
        [strip, strip, (2 * OWN + 1, Z, X), *(a.shape for a in inputs)],
        [pltpu.SemaphoreType.DMA((4,))],
        *(pltpu.with_memory_space_constraint(a, pltpu.HBM) for a in inputs),
        space=pltpu.HBM,
    )
    y_packets = exchange(first, second, "gy")

    tiles = tiles_for(6 * rows + 2 * OWN + 1)
    spread_shape = (across * count, Z // 2, X)
    first, second, spread, main = call(
        functools.partial(pack_own_kernel, rows),
        [(tiles, Z, X), (tiles, Z, X), spread_shape, (6, rows, Z, X)],
        [(PER * tiles, Z, X), spread_shape, pltpu.SemaphoreType.DMA],
        *inputs,
        coarse,
        outs=[pltpu.VMEM, pltpu.VMEM, pltpu.HBM, pltpu.VMEM],
    )
    own_x = exchange(first, second, "gx")
    spread = lax.all_to_all(spread, ("gx", "gy"), 0, 0, tiled=True)
    tiles = tiles_for(2 * PACKET)
    corner_x = exchange(
        *call(pack_corner_kernel, [(tiles, Z, X), (tiles, Z, X)], [(PER * tiles, Z, X)], *y_packets), "gx"
    )

    strip, edge = (2 * OWN - 1, Z, X), (EDGE_TILES, Z, X)
    pair0 = (2, 2, total0, Z, X)
    work = [(6, 2, total0, Z, X), (6, 2, total0, Z, X), pair0, pair0, pair0, pair0]
    four = (4, 2, OWN, Z, X)
    inside = call(
        functools.partial(level0_inner_kernel, rows),
        [
            (6, 2, rows - 2, Z, X),
            (2, 2, 4, Z, X),
            (2, 2, rows - 4, Z, X),
            (2, 2, rows - 6, Z, X),
            (2, 2, 6, Z, X),
            four,
        ],
        work,
        main,
        *own_x,
    )
    keep_in, _, y1_in, y2_in, _, _ = inside
    keep_out, y1_out, y2_out, sources, edges = call(
        functools.partial(level0_outer_kernel, rows),
        [(6, 2, 8, Z, X), (2, 2, 4, Z, X), (2, 2, 6, Z, X), four, (3, 2, *edge)],
        work,
        main,
        *y_packets,
        *own_x,
        *corner_x,
        *inside,
    )
    own, first, second, edge_a, edge_b, gain = call(
        combine_kernel,
        [(2, OWN, Z, X), strip, strip, edge, edge, (POWERS + 3, Z, X)],
        [],
        sources,
        edges,
        spread,
    )
    coef1, keep0, iterate = call(
        functools.partial(coarse1_kernel, rows),
        [(3, 2, SIZE1, Z, X), (6, 2, total0, Z, X), (2, 2, rows, Z, X)],
        [(2, 2 * GROUPS1, Z, X)],
        coarse,
        *y_packets,
        *own_x,
        *corner_x,
        gain,
        keep_in,
        y1_in,
        y2_in,
        keep_out,
        y1_out,
        y2_out,
    )
    (fields2,) = call(
        functools.partial(fields2_kernel, rows), [(2, 3, Z, X)], [], coarse, *y_packets, *own_x, *corner_x
    )
    b_packets = exchange(first, second, "gy")

    one, two, up = (2, SIZE1, Z, X), (2, SIZE2, Z, X), (2, SIZE_UP, Z, X)
    near = (1 + EDGE_TILES, Z, X)
    packet, first, second, far_a, far_b, keep1 = call(
        level1_kernel,
        [(1, Z, X), near, near, (near[0] + 2, Z, X), (near[0] + 1, Z, X), (2, *one)],
        [one, one],
        own,
        *b_packets,
        edge_a,
        edge_b,
        fields2,
        coef1,
        gain,
    )
    far = (swap_far(far_a, "gy", 1), swap_far(far_b, "gy", -1))
    near = exchange(first, second, "gy")

    (out,) = call(
        rest_kernel,
        [(2 * Z * rows, X)],
        [(2, *two), one, two, two, two, two, up, up, pair0, pair0, pair0],
        packet,
        *near,
        *far,
        gain,
        coef1,
        fields2,
        keep0,
        iterate,
        keep1,
    )
    return out.reshape(2, Z, rows, X)


def solution(mesh):
    placed = (
        P(None, None, "gy", "gx"),
        P(None, None, "gy", "gx"),
        P(None, "gy", "gx"),
        P(None, "gy", "gx"),
    )
    return jax.shard_map(
        body, mesh=mesh, in_specs=placed, out_specs=P(None, None, "gy", "gx"), check_vma=False
    )
```

```python
import functools

import jax
import jax.numpy as jnp
from jax import lax
from jax.experimental import pallas as pl
from jax.experimental.pallas import tpu as pltpu
from jax.sharding import PartitionSpec as P

DIFF = (40.0, 20.0)
INV_STEP = 2.0
LOWER = 0.25

_CENTRE = (1.0 + LOWER) / 2.0
_HALF = (1.0 - LOWER) / 2.0
_SIGMA = _CENTRE / _HALF
_RHO0 = 1.0 / _SIGMA
_RHO1 = 1.0 / (2.0 * _SIGMA - _RHO0)
_RHO2 = 1.0 / (2.0 * _SIGMA - _RHO1)

Z = 8
X = 128
HALO0 = 4
SENT = 3
FIELDS1 = 6 * SENT
FIELDS2 = FIELDS1 + 8
PACKET = FIELDS2 + 1
WIDE = 42
PER = X // WIDE
EDGE = 3

LO1, HI1 = -4, 8
LO2, HI2 = -2, 3
LO_UP, HI_UP = -3, 7
SIZE1, SIZE2, SIZE_UP = HI1 - LO1 + 2, HI2 - LO2 + 2, HI_UP - LO_UP + 2
OWN = 4


def lane_of():
    return lax.broadcasted_iota(jnp.int32, (1, Z, X), 2)


def sub_of():
    return lax.broadcasted_iota(jnp.int32, (1, Z, X), 1)


def roll_x(tile, shift):
    shift = shift % X
    return pltpu.roll(tile, shift, 2) if shift else tile


def roll_z(tile, shift):
    shift = shift % Z
    return pltpu.roll(tile, shift, 1) if shift else tile


def chunks(lo, hi, step=4):
    return [(r, min(step, hi - r)) for r in range(lo, hi, step)]


def neighbour_sums(read, r, n, k, tiles=(0, 1)):
    lane = lane_of()
    low, high = lane < k, lane >= X - k
    centre = [read(t, r, n) for t in (0, 1)]
    right = [roll_x(c, k) for c in centre]
    left = [roll_x(c, -k) for c in centre]
    sums = []
    for t in tiles:
        c = centre[t]
        along_x = jnp.where(low, right[1 - t], right[t]) + jnp.where(high, left[1 - t], left[t])
        along_y = read(t, r - 1, n) + read(t, r + 1, n)
        along_z = 2.0 * roll_z(c, k) if 2 * k == Z else roll_z(c, k) + roll_z(c, -k)
        sums.append(along_x + along_y + along_z)
    return centre, sums


def jacobian(u, v, f, k, level):
    scale = 0.25**level
    product = u * v
    squared = v * v
    first = INV_STEP + squared + f + 6.0 * DIFF[0] * scale
    second = INV_STEP + f + k - 2.0 * product + 6.0 * DIFF[1] * scale
    return 2.0 * product, squared, 1.0 / first, 1.0 / second, first, second


def cheb_step(level, keep, source, target, d, r, n, carry, gain, tiles=(0, 1)):
    scale = 0.25**level
    k = 1 << level
    u, nb_u = neighbour_sums(lambda t, a, m: source[0, t, pl.ds(a, m)], r, n, k, tiles)
    v, nb_v = neighbour_sums(lambda t, a, m: source[1, t, pl.ds(a, m)], r, n, k, tiles)
    rows = pl.ds(r, n)
    out = []
    for t in tiles:
        cross, squared, inv_u, inv_v = (keep[i, t, rows] for i in range(4))
        res_u = inv_u * (keep[4, t, rows] - cross * v[t] + DIFF[0] * scale * nb_u[t]) - u[t]
        res_v = inv_v * (keep[5, t, rows] + squared * u[t] + DIFF[1] * scale * nb_v[t]) - v[t]
        du, dv = gain * res_u, gain * res_v
        if carry is not None:
            du = du + carry * d[0, t, rows]
            dv = dv + carry * d[1, t, rows]
        if target is not None:
            d[0, t, rows] = du
            d[1, t, rows] = dv
            target[0, t, rows] = u[t] + du
            target[1, t, rows] = v[t] + dv
        out.append((u[t] + du, v[t] + dv))
    return out


def next_power(keep, source, r, n):
    u, nb_u = neighbour_sums(lambda t, a, m: source[0, t, pl.ds(a, m)], r, n, 1)
    v, nb_v = neighbour_sums(lambda t, a, m: source[1, t, pl.ds(a, m)], r, n, 1)
    rows = pl.ds(r, n)
    first, second = [], []
    for t in (0, 1):
        cross, squared, inv_u, inv_v = (keep[i, t, rows] for i in range(4))
        first.append(u[t] + inv_u * (cross * v[t] - DIFF[0] * nb_u[t]))
        second.append(v[t] - inv_v * (squared * u[t] + DIFF[1] * nb_v[t]))
    return first, second


CARRY1 = _RHO1 * _RHO0
CARRY2 = _RHO2 * _RHO1


POWERS = 9


def write_gains(spread, out):
    lane = lax.broadcasted_iota(jnp.int32, (1, X), 1)
    for level in range(3):
        top = jnp.max(jnp.where(lane == level, spread, 0.0), axis=1, keepdims=True)
        tau = 1.0 / (1.0 + jnp.broadcast_to(top, (Z, X)))
        for i, factor in enumerate((1.0 / _CENTRE, 2.0 * _RHO1 / _HALF, 2.0 * _RHO2 / _HALF)):
            out[3 * level + i] = factor * tau
    g0, g1, g2 = (out[i] for i in range(3))
    first, second = g0 + CARRY1 * g0 + g1, g1 * g0
    out[POWERS] = first + CARRY2 * (CARRY1 * g0 + g1) + g2
    out[POWERS + 1] = second + CARRY2 * second + g2 * first
    out[POWERS + 2] = g2 * second


def pair_rows(value):
    n = value.shape[0] // 2
    pairs = value.reshape(n, 2, Z, X)
    return pairs[:, 0] + pairs[:, 1]


def restrict_01(first, second):
    lane, sub = lane_of(), sub_of()
    across = []
    for value in (first, second):
        a, b = value[0:1], value[1:2]
        across.append(jnp.where((lane & 1) == 0, a + roll_x(a, -1), b + roll_x(b, 1)))
    a, b = across
    return 0.125 * jnp.where((sub & 1) == 0, a + roll_z(a, -1), b + roll_z(b, 1))


def restrict_12(groups):
    lane, sub = lane_of(), sub_of()
    out = None
    for p, value in enumerate(groups):
        value = value + roll_x(value, 1 if p & 1 else -1)
        value = value + roll_x(value, 2 if p & 2 else -2)
        out = value if out is None else jnp.where((lane & 3) == p, value, out)
    return 0.125 * (out + jnp.where((sub & 2) == 0, roll_z(out, -2), roll_z(out, 2)))


def spread_x(tile, k, phase):
    return jnp.where((lane_of() & k) == phase, tile, roll_x(tile, -k if phase else k))


def packed_jacobian(uv, fk, level):
    scale = 0.25**level
    even = (sub_of() & 1) == 0
    u, v = jnp.where(even, uv, roll_z(uv, 1)), jnp.where(even, roll_z(uv, -1), uv)
    f, k = jnp.where(even, fk, roll_z(fk, 1)), jnp.where(even, roll_z(fk, -1), fk)
    product, squared = u * v, v * v
    diag = jnp.where(
        even,
        INV_STEP + squared + f + 6.0 * DIFF[0] * scale,
        INV_STEP + f + k - 2.0 * product + 6.0 * DIFF[1] * scale,
    )
    return 1.0 / diag, jnp.where(even, -2.0 * product, squared), diag


def packed_spread(uv, fk, level):
    scale = 0.25**level
    even = (sub_of() & 1) == 0
    inverse, other, _ = packed_jacobian(uv, fk, level)
    return jnp.where(even, 6.0 * DIFF[0] * scale - other, 6.0 * DIFF[1] * scale + other) * inverse


def packed_terms(source, g, n, level):
    k = 1 << level
    lane, sub = lane_of(), sub_of()
    even = (sub & 1) == 0
    first, last = (lane & (k - 1)) == 0, (lane & (k - 1)) == k - 1
    low, high = lane < k, lane >= X - k
    diff = jnp.where(even, DIFF[0] * 0.25**level, DIFF[1] * 0.25**level)
    wide = [source[t, pl.ds(g - 1, n + 2)] for t in (0, 1)]
    centre = [w[1 : n + 1] for w in wide]
    right = [roll_x(c, k) for c in centre]
    left = [roll_x(c, -k) for c in centre]
    out = []
    for t in (0, 1):
        c, w = centre[t], wide[t]
        total = jnp.where(low, right[1 - t], right[t]) + jnp.where(high, left[1 - t], left[t])
        if k == 2:
            ahead, back = roll_x(w, 1), roll_x(w, -1)
            total = total + jnp.where(first, back[0:n], ahead[1 : n + 1])
            total = total + jnp.where(last, ahead[2 : n + 2], back[1 : n + 1])
            total = total + roll_z(c, 2) + roll_z(c, -2)
        else:
            total = total + jnp.where(first, roll_x(w[0:n], -(k - 1)), roll_x(c, 1))
            total = total + jnp.where(last, roll_x(w[2 : n + 2], k - 1), roll_x(c, -1))
            total = total + 2.0 * roll_z(c, 4)
        other = jnp.where(even, roll_z(c, -1), roll_z(c, 1))
        out.append((c, other, diff * total))
    return out


def packed_first(coef, shift, b, target, d, g, n, gain):
    for t in (0, 1):
        value = gain * coef[0, t, pl.ds(g + shift, n)] * b[t, pl.ds(g + shift, n)]
        d[t, pl.ds(g, n)] = value
        target[t, pl.ds(g, n)] = value


def packed_step(level, coef, shift, b, source, target, d, g, n, carry, gain):
    for t, (c, other, spread) in enumerate(packed_terms(source, g, n, level)):
        at = pl.ds(g + shift, n)
        res = coef[0, t, at] * (b[t, at] + coef[1, t, at] * other + spread) - c
        delta = gain * res
        if carry is not None:
            delta = delta + carry * d[t, pl.ds(g, n)]
        d[t, pl.ds(g, n)] = delta
        target[t, pl.ds(g, n)] = c + delta


def plane(ref, f, y, rows):
    return ref[pl.ds(f * Z * rows + y, Z, stride=rows), :]


def is_even(axis):
    return lax.rem(lax.axis_index(axis), 2) == 0


def prev_of(even, first, second, at):
    return jnp.where(even, first[at], second[at])


def next_of(even, first, second, at):
    return jnp.where(even, second[at], first[at])


SOURCES = ((0, 0), (0, 1), (1, 0), (1, 1), (2, 0), (3, 0))


def first_kernel(rows, state, previous, feed, kill, first, second, coarse, *rest):
    held, sems = rest[:4], rest[4]
    copies = [
        pltpu.make_async_copy(ref, to, sems.at[i]) for i, (ref, to) in enumerate(zip((state, previous, feed, kill), held))
    ]
    for copy in copies:
        copy.start()
    for copy in copies:
        copy.wait()
    even = is_even("gy")
    values = []
    for i, (j, f) in enumerate(SOURCES):
        wanted = range(rows) if i not in (2, 3) else [*range(SENT), *range(rows - SENT, rows)]
        values.append({y: plane(held[j], f, y, rows)[None] for y in wanted})
    for i in (2, 3):
        weight = DIFF[i - 2] / INV_STEP
        values[i][SENT - 1] = values[i][SENT - 1] + weight * values[i - 2][SENT]
        values[i][rows - SENT] = values[i][rows - SENT] + weight * values[i - 2][rows - SENT - 1]
    for i in range(6):
        for y in range(SENT):
            top, bottom = values[i][y], values[i][rows - SENT + y]
            at = slice(i * SENT + y, i * SENT + y + 1)
            first[at] = jnp.where(even, top, bottom)
            second[at] = jnp.where(even, bottom, top)
    pairs = []
    for p, (i, j) in enumerate(((0, 1), (4, 5))):
        parts = []
        for g in range(OWN):
            sums = [
                jnp.concatenate([value[4 * g + 2 * q] + value[4 * g + 2 * q + 1] for q in (0, 1)], axis=0)
                for value in (values[i], values[j])
            ]
            parts.append(restrict_01(*sums))
        pairs.append(jnp.concatenate(parts, axis=0))
        coarse[p * OWN : (p + 1) * OWN] = pairs[p]
        for ref in (first, second):
            ref[FIELDS1 + p * OWN : FIELDS1 + (p + 1) * OWN] = pairs[p]
    uv, fk = (restrict_12([pair[j : j + 1] for j in range(OWN)]) for pair in pairs)
    both = jnp.where((sub_of() & 2) == 0, uv, fk)
    coarse[2 * OWN : 2 * OWN + 1] = both
    for ref in (first, second):
        ref[FIELDS2 : FIELDS2 + 1] = both


def split_fields2(both):
    low = (sub_of() & 2) == 0
    return jnp.where(low, both, roll_z(both, 2)), jnp.where(low, roll_z(both, -2), both)


def write_spread(fields, coarse, out):
    lane = lax.broadcasted_iota(jnp.int32, (1, X), 1)
    cross, squared, inv_u, inv_v, _, _ = jacobian(*fields, 0)
    tops = [jnp.max(jnp.maximum((6.0 * DIFF[0] + cross) * inv_u, (6.0 * DIFF[1] + squared) * inv_v), axis=0)]
    tops.append(jnp.max(packed_spread(coarse[0:OWN], coarse[OWN : 2 * OWN], 1), axis=0))
    tops.append(packed_spread(*split_fields2(coarse[2 * OWN : 2 * OWN + 1]), 2)[0])
    result = jnp.zeros((1, X), jnp.float32)
    for level, top in enumerate(tops):
        top = jnp.max(jnp.max(top, axis=0, keepdims=True), axis=1, keepdims=True)
        result = jnp.where(lane == level, jnp.broadcast_to(top, (1, X)), result)
    out[...] = jnp.broadcast_to(result[None], out.shape)


GROUPS1 = HI1 - LO1
GROUPS2 = HI2 - LO2


def tiles_for(entries):
    return -(-entries // PER)


def pack_edges(entries, even, first, second):
    lane = lane_of()
    share = first.shape[0]
    left, right = None, None
    for j in range(PER):
        part = entries[j * share : (j + 1) * share]
        a, b = roll_x(part, WIDE * j), roll_x(part, WIDE + WIDE * j)
        left = a if left is None else jnp.where(lane >= WIDE * j, a, left)
        right = b if right is None else jnp.where(lane >= WIDE * j, b, right)
    first[...] = jnp.where(even, left, right)
    second[...] = jnp.where(even, right, left)


def halo_tiles(even, packets, lo, hi):
    first, second = packets
    share = first.shape[0]
    lane = lane_of()
    out = []
    for j in range(PER):
        a, b = max(lo, j * share), min(hi, (j + 1) * share)
        if a < b:
            strip = slice(a - j * share, b - j * share)
            left, right = prev_of(even, first, second, strip), next_of(even, first, second, strip)
            value = jnp.where(lane < X // 2, roll_x(right, -WIDE * j), roll_x(left, X - WIDE - WIDE * j))
            out.append((a - lo, b - lo, value))
    return out


def pack_own_kernel(
    rows, state, previous, feed, kill, coarse, first, second, spread, main, held, copies, sem
):
    inputs = (state, previous, feed, kill)

    def field(i):
        j, f = SOURCES[i]
        return jnp.stack([plane(inputs[j], f, y, rows) for y in range(rows)])

    fields = {i: field(i) for i in (0, 1, 4, 5)}
    write_spread([fields[i] for i in (0, 1, 4, 5)], coarse, copies)
    copy = pltpu.make_async_copy(copies, spread, sem)
    copy.start()

    @pl.when(lax.axis_index("gx") >= 0)
    def _():
        for i in range(6):
            value = field(i)
            main[i] = value
            held[i * rows : (i + 1) * rows] = value
        held[6 * rows : 6 * rows + 2 * OWN + 1] = coarse[...]
        pack_edges(held, is_even("gx"), first, second)

    copy.wait()


def pack_corner_kernel(y_first, y_second, first, second, held):
    even = is_even("gy")
    every = slice(0, PACKET)
    held[0:PACKET] = prev_of(even, y_first, y_second, every)
    held[PACKET : 2 * PACKET] = next_of(even, y_first, y_second, every)
    pack_edges(held, is_even("gx"), first, second)


EDGE_TILES = 2 * EDGE + 1


def level0_setup(fields, keep, diag, power, r, n):
    at = pl.ds(r, n)
    u, nb_u = neighbour_sums(lambda t, a, m: fields[0, t, pl.ds(a, m)], r, n, 1)
    v, nb_v = neighbour_sums(lambda t, a, m: fields[1, t, pl.ds(a, m)], r, n, 1)
    for t in (0, 1):
        f, k = fields[4, t, at], fields[5, t, at]
        cross, squared, inv_u, inv_v, first, second = jacobian(u[t], v[t], f, k, 0)
        react = u[t] * squared
        b_u = DIFF[0] * (nb_u[t] - 6.0 * u[t]) - INV_STEP * (u[t] - fields[2, t, at]) - react + f * (1.0 - u[t])
        b_v = DIFF[1] * (nb_v[t] - 6.0 * v[t]) - INV_STEP * (v[t] - fields[3, t, at]) + react - (f + k) * v[t]
        for i, value in enumerate((cross, squared, inv_u, inv_v, b_u, b_v)):
            keep[i, t, at] = value
        for i, value in enumerate((first, second)):
            diag[i, t, at] = value
        for i, value in enumerate((inv_u * b_u, inv_v * b_v)):
            power[i, t, at] = value


def level0_power(keep, source, target, r, n):
    for i, values in enumerate(next_power(keep, source, r, n)):
        for t in (0, 1):
            target[i, t, pl.ds(r, n)] = values[t]


def level0_down(keep, diag, y1, y2, sources, r, n):
    at = pl.ds(r, n)
    last = next_power(keep, y2, r, n)
    for t in (0, 1):
        both = [diag[i, t, at] for i in (0, 1)]
        parts = [[keep[4 + i, t, at] for i in (0, 1)]]
        parts += [[both[i] * power[i, t, at] for i in (0, 1)] for power in (y1, y2)]
        parts.append([both[i] * last[i][t] for i in (0, 1)])
        for q, part in enumerate(parts):
            u, v = (pair_rows(value) for value in part)
            for j in range(n // 4):
                value = restrict_01(u[2 * j : 2 * j + 2], v[2 * j : 2 * j + 2])
                sources[q, t, pl.ds((r - HALO0) // 4 + j, 1)] = value


def inner(rows, lost):
    return slice(HALO0 + lost, HALO0 + rows - lost)


def ends(rows, lo, hi):
    total = rows + 2 * HALO0
    return slice(lo, hi), slice(total - hi, total - lo)


def put_ends(target, rows, lo, hi, source):
    n = hi - lo
    for at, part in zip(ends(rows, lo, hi), (slice(0, n), slice(n, 2 * n))):
        for i in range(target.shape[0]):
            for t in (0, 1):
                target[i, t, at] = source[i, t, part]


def take_ends(source, rows, lo, hi, target):
    n = hi - lo
    for at, part in zip(ends(rows, lo, hi), (slice(0, n), slice(n, 2 * n))):
        for i in range(source.shape[0]):
            for t in (0, 1):
                target[i, t, part] = source[i, t, at]


def level0_inner_kernel(rows, main, own_a, own_b, keep_in, y0_in, y1_in, y2_in, diag_in, sources_in, *scratch):
    fields, keep, diag, y0, y1, y2 = scratch
    even_x = is_even("gx")
    for i in range(6):
        fields[i, 0, HALO0 : HALO0 + rows] = main[i]
        for a, b, value in halo_tiles(even_x, (own_a, own_b), i * rows, (i + 1) * rows):
            fields[i, 1, HALO0 + a : HALO0 + b] = value
    first = HALO0 + 1
    level0_setup(fields, keep, diag, y0, first, rows - 2)
    level0_power(keep, y0, y1, first + 1, rows - 4)
    level0_power(keep, y1, y2, first + 2, rows - 6)
    level0_down(keep, diag, y1, y2, sources_in, first + 3, rows - 8)
    for source, target, lost in ((keep, keep_in, 1), (y1, y1_in, 2), (y2, y2_in, 3)):
        for i in range(source.shape[0]):
            for t in (0, 1):
                target[i, t] = source[i, t, inner(rows, lost)]
    take_ends(y0, rows, HALO0 + 1, HALO0 + 3, y0_in)
    take_ends(diag, rows, HALO0 + 1, HALO0 + 4, diag_in)


def level0_outer_kernel(
    rows,
    main,
    y_first,
    y_second,
    own_a,
    own_b,
    corner_a,
    corner_b,
    keep_in,
    y0_in,
    y1_in,
    y2_in,
    diag_in,
    sources_in,
    keep_out,
    y1_out,
    y2_out,
    sources,
    edges,
    *scratch,
):
    fields, keep, diag, y0, y1, y2 = scratch
    even, even_x = is_even("gy"), is_even("gx")
    total = rows + 2 * HALO0
    near, skip = HALO0 + 2, HALO0 - SENT
    for i in range(6):
        strip = slice(i * SENT, (i + 1) * SENT)
        fields[i, 0, skip:HALO0] = prev_of(even, y_first, y_second, strip)
        fields[i, 0, HALO0:near] = main[i, 0:2]
        fields[i, 0, total - near : total - HALO0] = main[i, rows - 2 : rows]
        fields[i, 0, HALO0 + rows : total - skip] = next_of(even, y_first, y_second, strip)
        for packets, lo, n, at in (
            ((corner_a, corner_b), i * SENT, SENT, skip),
            ((own_a, own_b), i * rows, 2, HALO0),
            ((own_a, own_b), (i + 1) * rows - 2, 2, total - near),
            ((corner_a, corner_b), PACKET + i * SENT, SENT, HALO0 + rows),
        ):
            for a, b, value in halo_tiles(even_x, packets, lo, lo + n):
                fields[i, 1, at + a : at + b] = value
    for i in (0, 1):
        for t in (0, 1):
            for at in (0, total - 1):
                fields[i, t, at] = jnp.zeros((Z, X), jnp.float32)
    for at, part in zip(ends(rows, 5, 8), (slice(0, 3), slice(rows - 5, rows - 2))):
        for i in range(6):
            for t in (0, 1):
                keep[i, t, at] = keep_in[i, t, part]
    put_ends(diag, rows, 5, 8, diag_in)
    put_ends(y0, rows, 5, 7, y0_in)
    for target, source, lost in ((y1, y1_in, 2), (y2, y2_in, 3)):
        n = rows - 2 * lost
        for at, part in zip(ends(rows, HALO0 + lost, HALO0 + lost + 2), (slice(0, 2), slice(n - 2, n))):
            for i in (0, 1):
                for t in (0, 1):
                    target[i, t, at] = source[i, t, part]
    for r in (1, total - 5):
        level0_setup(fields, keep, diag, y0, r, 4)
    for r in (2, total - 6):
        level0_power(keep, y0, y1, r, 4)
    for r in (3, total - 7):
        level0_power(keep, y1, y2, r, 4)
    for r in (4, total - 8):
        level0_down(keep, diag, y1, y2, sources, r, 4)
    for q in range(4):
        for t in (0, 1):
            sources[q, t, 1 : OWN - 1] = sources_in[q, t, 1 : OWN - 1]
    take_ends(keep, rows, 1, 5, keep_out)
    take_ends(y1, rows, 4, 6, y1_out)
    take_ends(y2, rows, 4, 7, y2_out)
    for p, power in enumerate((y0, y1, y2)):
        for side, start in enumerate((HALO0, HALO0 + rows - EDGE)):
            edges[p, side] = pack_rows(power, start)


def pack_rows(x, start):
    lane = lane_of()
    halo = None
    for i in (0, 1):
        for j in range(EDGE):
            at = i * EDGE + j
            value = roll_x(x[i, 1, start + j : start + j + 1], 4 + 8 * at)
            halo = value if halo is None else jnp.where((lane >> 3) == at, value, halo)
    return jnp.concatenate([x[i, 0, start : start + EDGE] for i in (0, 1)] + [halo], axis=0)


def squeeze(halo):
    lane = lane_of()
    last = halo[OWN - 1 : OWN]
    ahead = (lane >= WIDE) & (lane < 2 * WIDE)
    parts = [jnp.where(ahead, roll_x(last, WIDE), halo[0:1]), jnp.where(ahead, roll_x(last, 2 * WIDE - X), halo[1:2])]
    return jnp.concatenate(parts + [halo[2 : OWN - 1]], axis=0)


def unsqueeze(tiles):
    last = jnp.where(lane_of() < X // 2, roll_x(tiles[0:1], -WIDE), roll_x(tiles[1:2], X - 2 * WIDE))
    return jnp.concatenate([tiles, last], axis=0)


def combine_kernel(sources, edges, spread, own, first, second, edge_first, edge_second, gain):
    write_gains(jnp.max(spread[...], axis=0)[0:1], gain)
    p0, p1, p2 = (gain[POWERS + i] for i in range(3))
    for t in (0, 1):
        value = sources[0, t] - p0 * sources[1, t] + p1 * sources[2, t] - p2 * sources[3, t]
        own[t] = value
        for ref in (first, second):
            if t == 0:
                ref[0:OWN] = value
            else:
                ref[OWN:] = squeeze(value)
    even = is_even("gy")
    top, bottom = (p0 * edges[0, side] - p1 * edges[1, side] + p2 * edges[2, side] for side in (0, 1))
    edge_first[...] = jnp.where(even, top, bottom)
    edge_second[...] = jnp.where(even, bottom, top)


def coarse1_kernel(
    rows, coarse, y_first, y_second, own_a, own_b, corner_a, corner_b, gain, keep_in, y1_in, y2_in, keep_out, y1_out, y2_out,
    coef, keep0, x0, fields
):
    even, even_x = is_even("gy"), is_even("gx")
    own_x, corner_x = (own_a, own_b), (corner_a, corner_b)
    for p in (0, 1):
        to = p * GROUPS1
        strip = slice(FIELDS1 + p * OWN, FIELDS1 + (p + 1) * OWN)
        fields[0, to : to + OWN] = prev_of(even, y_first, y_second, strip)
        fields[0, to + OWN : to + 2 * OWN] = coarse[p * OWN : (p + 1) * OWN]
        fields[0, to + 2 * OWN : to + 3 * OWN] = next_of(even, y_first, y_second, strip)
        for part, (packets, lo) in enumerate(
            ((corner_x, FIELDS1), (own_x, 6 * rows), (corner_x, PACKET + FIELDS1))
        ):
            lo += p * OWN
            for a, b, value in halo_tiles(even_x, packets, lo, lo + OWN):
                fields[1, to + part * OWN + a : to + part * OWN + b] = value
    for t in (0, 1):
        for i, value in enumerate(packed_jacobian(fields[t, 0:GROUPS1], fields[t, GROUPS1 : 2 * GROUPS1], 1)):
            coef[i, t, 1 : SIZE1 - 1] = value

    def whole(inside, outside):
        n = outside.shape[0] // 2
        return jnp.concatenate([outside[0:n], inside, outside[n:]], axis=0)

    for i in range(6):
        for t in (0, 1):
            keep0[i, t, 1 : rows + 2 * HALO0 - 1] = whole(keep_in[i, t], keep_out[i, t])
    p0, p1, p2 = (gain[POWERS + i] for i in range(3))
    for i in (0, 1):
        for t in (0, 1):
            y0 = keep0[2 + i, t, HALO0 : HALO0 + rows] * keep0[4 + i, t, HALO0 : HALO0 + rows]
            y1, y2 = (whole(a[i, t], b[i, t]) for a, b in ((y1_in, y1_out), (y2_in, y2_out)))
            x0[i, t] = p0 * y0 - p1 * y1 + p2 * y2


def fields2_kernel(rows, coarse, y_first, y_second, own_a, own_b, corner_a, corner_b, out):
    even, even_x = is_even("gy"), is_even("gx")
    own_x, corner_x = (own_a, own_b), (corner_a, corner_b)
    near = slice(FIELDS2, FIELDS2 + 1)
    out[0, 0:1] = prev_of(even, y_first, y_second, near)
    out[0, 1:2] = coarse[2 * OWN : 2 * OWN + 1]
    out[0, 2:3] = next_of(even, y_first, y_second, near)
    for q, (packets, lo) in enumerate(
        ((corner_x, FIELDS2), (own_x, 6 * rows + 2 * OWN), (corner_x, PACKET + FIELDS2))
    ):
        out[1, q : q + 1] = halo_tiles(even_x, packets, lo, lo + 1)[0][2]


def level1_kernel(
    own, first, second, edge_a, edge_b, fields2, coef1, gain, packet, to_first, to_second, to_far_a, to_far_b, keep, y1, d1
):
    b1, x1 = keep.at[0], keep.at[1]
    even = is_even("gy")
    for t in (0, 1):
        b1[t, 1 + OWN : 1 + 2 * OWN] = own[t]
        for at, take in ((1, prev_of), (1 + 2 * OWN, next_of)):
            if t == 0:
                b1[t, at : at + OWN] = take(even, first, second, slice(0, OWN))
            else:
                b1[t, at : at + OWN] = unsqueeze(take(even, first, second, slice(OWN, 2 * OWN - 1)))
    g0, g1, g2 = (gain[3 + i] for i in range(3))
    n = GROUPS1
    packed_first(coef1, 0, b1, x1, d1, 1, n, g0)
    packed_step(1, coef1, 0, b1, x1, y1, d1, 2, n - 2, CARRY1, g1)
    packed_step(1, coef1, 0, b1, y1, x1, d1, 2, n - 2, CARRY2, g2)
    here = pl.ds(1 + OWN, OWN)
    values = []
    for t, (c, other, spread) in enumerate(packed_terms(x1, 1 + OWN, OWN, 1)):
        res = b1[t, here] - coef1[2, t, here] * c + coef1[1, t, here] * other + spread
        values.append(restrict_12([res[j : j + 1] for j in range(OWN)]))
        for ref in (to_far_a, to_far_b):
            ref[1 + t : 2 + t] = fields2[t, 1:2]
    value = jnp.where((sub_of() & 2) == 0, values[0], values[1])
    for ref in (packet, to_first, to_second, to_far_a, to_far_b):
        ref[0:1] = value
    for ref in (to_far_a, to_far_b):
        ref[3:] = jnp.broadcast_to(value, (ref.shape[0] - 3, Z, X))
    to_first[1 : 1 + EDGE_TILES] = edge_a[...]
    to_first[1 + EDGE_TILES :] = jnp.broadcast_to(value, (to_first.shape[0] - 1 - EDGE_TILES, Z, X))
    to_second[1:] = edge_b[...]


def rest_kernel(
    own2, near_a, near_b, far_a, far_b, gain, coef1, fields2, keep0, iterate, keep1, out, coef2, d1, b2, x2, y2, d2, xu, yu, x0, y0, d0
):
    rows = out.shape[0] // (2 * Z)
    even = (sub_of() & 1) == 0
    b1, x1 = keep1.at[0], keep1.at[1]

    even_y, low = is_even("gy"), lax.rem(lax.axis_index("gy"), 4) < 2
    at = slice(0, 1)
    parts = [
        next_of(low, far_a, far_b, at),
        prev_of(even_y, near_a, near_b, at),
        own2[at],
        next_of(even_y, near_a, near_b, at),
        prev_of(low, far_a, far_b, at),
    ]
    for t, values in enumerate(split_fields2(jnp.concatenate(parts, axis=0))):
        b2[t, 1 : SIZE2 - 1] = values
        at = slice(1 + t, 2 + t)
        parts = [next_of(low, far_a, far_b, at), fields2[t], prev_of(low, far_a, far_b, at)]
        inverse, other, _ = packed_jacobian(*split_fields2(jnp.concatenate(parts, axis=0)), 2)
        coef2[0, t, 1 : SIZE2 - 1] = inverse
        coef2[1, t, 1 : SIZE2 - 1] = other

    n = HI2 - LO2
    g0, g1, g2 = (gain[6 + i] for i in range(3))
    packed_first(coef2, 0, b2, x2, d2, 1, n, g0)
    packed_step(2, coef2, 0, b2, x2, y2, d2, 1, n, CARRY1, g1)
    packed_step(2, coef2, 0, b2, y2, x2, d2, 1, n, CARRY2, g2)
    packed_step(2, coef2, 0, b2, x2, y2, d2, 1, n, None, g0)
    packed_step(2, coef2, 0, b2, y2, x2, d2, 2, n - 2, CARRY1, g1)
    packed_step(2, coef2, 0, b2, x2, y2, d2, 2, n - 2, CARRY2, g2)

    g0, g1, g2 = (gain[3 + i] for i in range(3))
    shift = LO_UP - LO1
    for t in (0, 1):
        for g in range(LO_UP, HI_UP):
            p = g % 4
            value = y2[t, g // 4 - LO2 + 1 : g // 4 - LO2 + 2]
            value = spread_x(spread_x(value, 1, p & 1), 2, p & 2)
            at = g - LO_UP + 1
            xu[t, at : at + 1] = x1[t, at + shift : at + shift + 1] + value
    n = HI_UP - LO_UP
    packed_step(1, coef1, shift, b1, xu, yu, d1, 2, n - 2, None, g0)
    packed_step(1, coef1, shift, b1, yu, xu, d1, 2, n - 2, CARRY1, g1)
    packed_step(1, coef1, shift, b1, xu, yu, d1, 3, n - 4, CARRY2, g2)

    g0, g1, g2 = (gain[i] for i in range(3))
    sides = [take(even_y, near_a, near_b, slice(1, 1 + EDGE_TILES)) for take in (prev_of, next_of)]

    def before(i, t, y):
        if 0 <= y < rows:
            return iterate[i, t, y : y + 1]
        side, j = (sides[0], y + EDGE) if y < 0 else (sides[1], y - rows)
        if t == 0:
            return side[i * EDGE + j : i * EDGE + j + 1]
        return roll_x(side[2 * EDGE :], -(4 + 8 * (i * EDGE + j)))

    for t in (0, 1):
        for row in range(-2, rows // 2 + 2):
            at = row // 2 - LO_UP + 1
            value = spread_x(yu[t, at : at + 1], 1, row & 1)
            for i, fine in enumerate((jnp.where(even, value, roll_z(value, 1)), jnp.where(even, roll_z(value, -1), value))):
                for y in (2 * row, 2 * row + 1):
                    if -EDGE <= y < rows + EDGE:
                        x0[i, t, y + HALO0 : y + HALO0 + 1] = before(i, t, y) + fine
    total = rows + 2 * HALO0
    for r, n in chunks(2, total - 2):
        cheb_step(0, keep0, x0, y0, d0, r, n, None, g0)
    for r, n in chunks(3, total - 3):
        cheb_step(0, keep0, y0, x0, d0, r, n, CARRY1, g1)
    for r, n in chunks(4, total - 4):
        last = cheb_step(0, keep0, x0, None, d0, r, n, CARRY2, g2, (0,))[0]
        for i in (0, 1):
            for j in range(n):
                out[pl.ds(i * Z * rows + r - HALO0 + j, Z, stride=rows), :] = last[i][j]


def call(kernel, out_shapes, scratch, *args, space=pltpu.VMEM, outs=None):
    out = [jax.ShapeDtypeStruct(shape, jnp.float32) for shape in out_shapes]
    return pl.pallas_call(
        kernel,
        out_shape=out,
        in_specs=[pl.BlockSpec(memory_space=space)] * len(args),
        out_specs=[pl.BlockSpec(memory_space=m) for m in outs or [pltpu.VMEM] * len(out)],
        scratch_shapes=[pltpu.VMEM(s, jnp.float32) if isinstance(s, tuple) else s for s in scratch],
        compiler_params=pltpu.CompilerParams(vmem_limit_bytes=24 * 2**20),
    )(*args)


def swap(value, axis, step):
    count = lax.axis_size(axis)
    assert count % 2 == 0
    pairs = [(i, (i + step) % count) for i in range(0, count, 2)]
    return lax.ppermute(value, axis, pairs + [(j, i) for i, j in pairs])


def swap_far(value, axis, step):
    count = lax.axis_size(axis)
    assert count % 4 == 0
    pairs = [(i + j, (i + j + 2 * step) % count) for i in range(0, count, 4) for j in (0, 1)]
    return lax.ppermute(value, axis, pairs + [(j, i) for i, j in pairs])


def exchange(first, second, axis):
    return swap(first, axis, -1), swap(second, axis, 1)


def body(state, previous, feed, kill):
    _, depth, rows, cols = state.shape
    assert depth == Z and cols == X and rows == 4 * OWN
    across, count = lax.axis_size("gx"), lax.axis_size("gy")
    total0 = rows + 2 * HALO0
    state = state.reshape(2 * Z * rows, X)
    previous = previous.reshape(2 * Z * rows, X)
    feed = feed.reshape(Z * rows, X)
    kill = kill.reshape(Z * rows, X)
    inputs = (state, previous, feed, kill)

    strip = (PACKET, Z, X)
    first, second, coarse, *inputs = call(
        functools.partial(first_kernel, rows),
        [strip, strip, (2 * OWN + 1, Z, X), *(a.shape for a in inputs)],
        [pltpu.SemaphoreType.DMA((4,))],
        *(pltpu.with_memory_space_constraint(a, pltpu.HBM) for a in inputs),
        space=pltpu.HBM,
    )
    y_packets = exchange(first, second, "gy")

    tiles = tiles_for(6 * rows + 2 * OWN + 1)
    spread_shape = (across * count, Z // 2, X)
    first, second, spread, main = call(
        functools.partial(pack_own_kernel, rows),
        [(tiles, Z, X), (tiles, Z, X), spread_shape, (6, rows, Z, X)],
        [(PER * tiles, Z, X), spread_shape, pltpu.SemaphoreType.DMA],
        *inputs,
        coarse,
        outs=[pltpu.VMEM, pltpu.VMEM, pltpu.HBM, pltpu.VMEM],
    )
    own_x = exchange(first, second, "gx")
    spread = lax.all_to_all(spread, ("gx", "gy"), 0, 0, tiled=True)
    tiles = tiles_for(2 * PACKET)
    corner_x = exchange(
        *call(pack_corner_kernel, [(tiles, Z, X), (tiles, Z, X)], [(PER * tiles, Z, X)], *y_packets), "gx"
    )

    strip, edge = (2 * OWN - 1, Z, X), (EDGE_TILES, Z, X)
    pair0 = (2, 2, total0, Z, X)
    work = [(6, 2, total0, Z, X), (6, 2, total0, Z, X), pair0, pair0, pair0, pair0]
    four = (4, 2, OWN, Z, X)
    inside = call(
        functools.partial(level0_inner_kernel, rows),
        [
            (6, 2, rows - 2, Z, X),
            (2, 2, 4, Z, X),
            (2, 2, rows - 4, Z, X),
            (2, 2, rows - 6, Z, X),
            (2, 2, 6, Z, X),
            four,
        ],
        work,
        main,
        *own_x,
    )
    keep_in, _, y1_in, y2_in, _, _ = inside
    keep_out, y1_out, y2_out, sources, edges = call(
        functools.partial(level0_outer_kernel, rows),
        [(6, 2, 8, Z, X), (2, 2, 4, Z, X), (2, 2, 6, Z, X), four, (3, 2, *edge)],
        work,
        main,
        *y_packets,
        *own_x,
        *corner_x,
        *inside,
    )
    own, first, second, edge_a, edge_b, gain = call(
        combine_kernel,
        [(2, OWN, Z, X), strip, strip, edge, edge, (POWERS + 3, Z, X)],
        [],
        sources,
        edges,
        spread,
    )
    coef1, keep0, iterate = call(
        functools.partial(coarse1_kernel, rows),
        [(3, 2, SIZE1, Z, X), (6, 2, total0, Z, X), (2, 2, rows, Z, X)],
        [(2, 2 * GROUPS1, Z, X)],
        coarse,
        *y_packets,
        *own_x,
        *corner_x,
        gain,
        keep_in,
        y1_in,
        y2_in,
        keep_out,
        y1_out,
        y2_out,
    )
    (fields2,) = call(
        functools.partial(fields2_kernel, rows), [(2, 3, Z, X)], [], coarse, *y_packets, *own_x, *corner_x
    )
    b_packets = exchange(first, second, "gy")

    one, two, up = (2, SIZE1, Z, X), (2, SIZE2, Z, X), (2, SIZE_UP, Z, X)
    near = (1 + EDGE_TILES, Z, X)
    packet, first, second, far_a, far_b, keep1 = call(
        level1_kernel,
        [(1, Z, X), (near[0] + 2, Z, X), near, (near[0] + 3, Z, X), (near[0] + 1, Z, X), (2, *one)],
        [one, one],
        own,
        *b_packets,
        edge_a,
        edge_b,
        fields2,
        coef1,
        gain,
    )
    far = (swap_far(far_a, "gy", 1), swap_far(far_b, "gy", -1))
    near = exchange(first, second, "gy")

    (out,) = call(
        rest_kernel,
        [(2 * Z * rows, X)],
        [(2, *two), one, two, two, two, two, up, up, pair0, pair0, pair0],
        packet,
        *near,
        *far,
        gain,
        coef1,
        fields2,
        keep0,
        iterate,
        keep1,
    )
    return out.reshape(2, Z, rows, X)


def solution(mesh):
    placed = (
        P(None, None, "gy", "gx"),
        P(None, None, "gy", "gx"),
        P(None, "gy", "gx"),
        P(None, "gy", "gx"),
    )
    return jax.shard_map(
        body, mesh=mesh, in_specs=placed, out_specs=P(None, None, "gy", "gx"), check_vma=False
    )
```

```python
import functools

import jax
import jax.numpy as jnp
from jax import lax
from jax.experimental import pallas as pl
from jax.experimental.pallas import tpu as pltpu
from jax.sharding import PartitionSpec as P

DIFF = (40.0, 20.0)
INV_STEP = 2.0
LOWER = 0.25

_CENTRE = (1.0 + LOWER) / 2.0
_HALF = (1.0 - LOWER) / 2.0
_SIGMA = _CENTRE / _HALF
_RHO0 = 1.0 / _SIGMA
_RHO1 = 1.0 / (2.0 * _SIGMA - _RHO0)
_RHO2 = 1.0 / (2.0 * _SIGMA - _RHO1)

Z = 8
X = 128
HALO0 = 4
SENT = 3
FIELDS1 = 6 * SENT
FIELDS2 = FIELDS1 + 8
PACKET = FIELDS2 + 1
WIDE = 42
PER = X // WIDE
EDGE = 3

LO1, HI1 = -4, 8
LO2, HI2 = -2, 3
LO_UP, HI_UP = -3, 7
SIZE1, SIZE2, SIZE_UP = HI1 - LO1 + 2, HI2 - LO2 + 2, HI_UP - LO_UP + 2
OWN = 4


def lane_of():
    return lax.broadcasted_iota(jnp.int32, (1, Z, X), 2)


def sub_of():
    return lax.broadcasted_iota(jnp.int32, (1, Z, X), 1)


def roll_x(tile, shift):
    shift = shift % X
    return pltpu.roll(tile, shift, 2) if shift else tile


def roll_z(tile, shift):
    shift = shift % Z
    return pltpu.roll(tile, shift, 1) if shift else tile


def chunks(lo, hi, step=4):
    return [(r, min(step, hi - r)) for r in range(lo, hi, step)]


def neighbour_sums(read, r, n, k, tiles=(0, 1)):
    lane = lane_of()
    low, high = lane < k, lane >= X - k
    centre = [read(t, r, n) for t in (0, 1)]
    right = [roll_x(c, k) for c in centre]
    left = [roll_x(c, -k) for c in centre]
    sums = []
    for t in tiles:
        c = centre[t]
        along_x = jnp.where(low, right[1 - t], right[t]) + jnp.where(high, left[1 - t], left[t])
        along_y = read(t, r - 1, n) + read(t, r + 1, n)
        along_z = 2.0 * roll_z(c, k) if 2 * k == Z else roll_z(c, k) + roll_z(c, -k)
        sums.append(along_x + along_y + along_z)
    return centre, sums


def jacobian(u, v, f, k, level):
    scale = 0.25**level
    product = u * v
    squared = v * v
    first = INV_STEP + squared + f + 6.0 * DIFF[0] * scale
    second = INV_STEP + f + k - 2.0 * product + 6.0 * DIFF[1] * scale
    return 2.0 * product, squared, 1.0 / first, 1.0 / second, first, second


def cheb_step(level, keep, source, target, d, r, n, carry, gain, tiles=(0, 1)):
    scale = 0.25**level
    k = 1 << level
    u, nb_u = neighbour_sums(lambda t, a, m: source[0, t, pl.ds(a, m)], r, n, k, tiles)
    v, nb_v = neighbour_sums(lambda t, a, m: source[1, t, pl.ds(a, m)], r, n, k, tiles)
    rows = pl.ds(r, n)
    out = []
    for t in tiles:
        cross, squared, inv_u, inv_v = (keep[i, t, rows] for i in range(4))
        res_u = inv_u * (keep[4, t, rows] - cross * v[t] + DIFF[0] * scale * nb_u[t]) - u[t]
        res_v = inv_v * (keep[5, t, rows] + squared * u[t] + DIFF[1] * scale * nb_v[t]) - v[t]
        du, dv = gain * res_u, gain * res_v
        if carry is not None:
            du = du + carry * d[0, t, rows]
            dv = dv + carry * d[1, t, rows]
        if target is not None:
            d[0, t, rows] = du
            d[1, t, rows] = dv
            target[0, t, rows] = u[t] + du
            target[1, t, rows] = v[t] + dv
        out.append((u[t] + du, v[t] + dv))
    return out


def next_power(keep, source, r, n):
    u, nb_u = neighbour_sums(lambda t, a, m: source[0, t, pl.ds(a, m)], r, n, 1)
    v, nb_v = neighbour_sums(lambda t, a, m: source[1, t, pl.ds(a, m)], r, n, 1)
    rows = pl.ds(r, n)
    first, second = [], []
    for t in (0, 1):
        cross, squared, inv_u, inv_v = (keep[i, t, rows] for i in range(4))
        first.append(u[t] + inv_u * (cross * v[t] - DIFF[0] * nb_u[t]))
        second.append(v[t] - inv_v * (squared * u[t] + DIFF[1] * nb_v[t]))
    return first, second


CARRY1 = _RHO1 * _RHO0
CARRY2 = _RHO2 * _RHO1


POWERS = 9


def write_gains(spread, out):
    lane = lax.broadcasted_iota(jnp.int32, (1, X), 1)
    for level in range(3):
        top = jnp.max(jnp.where(lane == level, spread, 0.0), axis=1, keepdims=True)
        tau = 1.0 / (1.0 + jnp.broadcast_to(top, (Z, X)))
        for i, factor in enumerate((1.0 / _CENTRE, 2.0 * _RHO1 / _HALF, 2.0 * _RHO2 / _HALF)):
            out[3 * level + i] = factor * tau
    g0, g1, g2 = (out[i] for i in range(3))
    first, second = g0 + CARRY1 * g0 + g1, g1 * g0
    out[POWERS] = first + CARRY2 * (CARRY1 * g0 + g1) + g2
    out[POWERS + 1] = second + CARRY2 * second + g2 * first
    out[POWERS + 2] = g2 * second


def pair_rows(value):
    n = value.shape[0] // 2
    pairs = value.reshape(n, 2, Z, X)
    return pairs[:, 0] + pairs[:, 1]


def restrict_01(first, second):
    lane, sub = lane_of(), sub_of()
    across = []
    for value in (first, second):
        a, b = value[0:1], value[1:2]
        across.append(jnp.where((lane & 1) == 0, a + roll_x(a, -1), b + roll_x(b, 1)))
    a, b = across
    return 0.125 * jnp.where((sub & 1) == 0, a + roll_z(a, -1), b + roll_z(b, 1))


def restrict_12(groups):
    lane, sub = lane_of(), sub_of()
    out = None
    for p, value in enumerate(groups):
        value = value + roll_x(value, 1 if p & 1 else -1)
        value = value + roll_x(value, 2 if p & 2 else -2)
        out = value if out is None else jnp.where((lane & 3) == p, value, out)
    return 0.125 * (out + jnp.where((sub & 2) == 0, roll_z(out, -2), roll_z(out, 2)))


def spread_x(tile, k, phase):
    return jnp.where((lane_of() & k) == phase, tile, roll_x(tile, -k if phase else k))


def packed_jacobian(uv, fk, level):
    scale = 0.25**level
    even = (sub_of() & 1) == 0
    u, v = jnp.where(even, uv, roll_z(uv, 1)), jnp.where(even, roll_z(uv, -1), uv)
    f, k = jnp.where(even, fk, roll_z(fk, 1)), jnp.where(even, roll_z(fk, -1), fk)
    product, squared = u * v, v * v
    diag = jnp.where(
        even,
        INV_STEP + squared + f + 6.0 * DIFF[0] * scale,
        INV_STEP + f + k - 2.0 * product + 6.0 * DIFF[1] * scale,
    )
    return 1.0 / diag, jnp.where(even, -2.0 * product, squared), diag


def packed_spread(uv, fk, level):
    scale = 0.25**level
    even = (sub_of() & 1) == 0
    inverse, other, _ = packed_jacobian(uv, fk, level)
    return jnp.where(even, 6.0 * DIFF[0] * scale - other, 6.0 * DIFF[1] * scale + other) * inverse


def packed_terms(source, g, n, level):
    k = 1 << level
    lane, sub = lane_of(), sub_of()
    even = (sub & 1) == 0
    first, last = (lane & (k - 1)) == 0, (lane & (k - 1)) == k - 1
    low, high = lane < k, lane >= X - k
    diff = jnp.where(even, DIFF[0] * 0.25**level, DIFF[1] * 0.25**level)
    wide = [source[t, pl.ds(g - 1, n + 2)] for t in (0, 1)]
    centre = [w[1 : n + 1] for w in wide]
    right = [roll_x(c, k) for c in centre]
    left = [roll_x(c, -k) for c in centre]
    out = []
    for t in (0, 1):
        c, w = centre[t], wide[t]
        total = jnp.where(low, right[1 - t], right[t]) + jnp.where(high, left[1 - t], left[t])
        if k == 2:
            ahead, back = roll_x(w, 1), roll_x(w, -1)
            total = total + jnp.where(first, back[0:n], ahead[1 : n + 1])
            total = total + jnp.where(last, ahead[2 : n + 2], back[1 : n + 1])
            total = total + roll_z(c, 2) + roll_z(c, -2)
        else:
            total = total + jnp.where(first, roll_x(w[0:n], -(k - 1)), roll_x(c, 1))
            total = total + jnp.where(last, roll_x(w[2 : n + 2], k - 1), roll_x(c, -1))
            total = total + 2.0 * roll_z(c, 4)
        other = jnp.where(even, roll_z(c, -1), roll_z(c, 1))
        out.append((c, other, diff * total))
    return out


def packed_first(coef, shift, b, target, d, g, n, gain):
    for t in (0, 1):
        value = gain * coef[0, t, pl.ds(g + shift, n)] * b[t, pl.ds(g + shift, n)]
        d[t, pl.ds(g, n)] = value
        target[t, pl.ds(g, n)] = value


def packed_step(level, coef, shift, b, source, target, d, g, n, carry, gain):
    for t, (c, other, spread) in enumerate(packed_terms(source, g, n, level)):
        at = pl.ds(g + shift, n)
        res = coef[0, t, at] * (b[t, at] + coef[1, t, at] * other + spread) - c
        delta = gain * res
        if carry is not None:
            delta = delta + carry * d[t, pl.ds(g, n)]
        d[t, pl.ds(g, n)] = delta
        target[t, pl.ds(g, n)] = c + delta


def plane(ref, f, y, rows):
    return ref[pl.ds(f * Z * rows + y, Z, stride=rows), :]


def is_even(axis):
    return lax.rem(lax.axis_index(axis), 2) == 0


def prev_of(even, first, second, at):
    return jnp.where(even, first[at], second[at])


def next_of(even, first, second, at):
    return jnp.where(even, second[at], first[at])


SOURCES = ((0, 0), (0, 1), (1, 0), (1, 1), (2, 0), (3, 0))


def first_kernel(rows, state, previous, feed, kill, first, second, coarse, *rest):
    held, sems = rest[:4], rest[4]
    copies = [
        pltpu.make_async_copy(ref, to, sems.at[i]) for i, (ref, to) in enumerate(zip((state, previous, feed, kill), held))
    ]
    for copy in copies:
        copy.start()
    for copy in copies:
        copy.wait()
    even = is_even("gy")
    values = []
    for i, (j, f) in enumerate(SOURCES):
        wanted = range(rows) if i not in (2, 3) else [*range(SENT), *range(rows - SENT, rows)]
        values.append({y: plane(held[j], f, y, rows)[None] for y in wanted})
    for i in (2, 3):
        weight = DIFF[i - 2] / INV_STEP
        values[i][SENT - 1] = values[i][SENT - 1] + weight * values[i - 2][SENT]
        values[i][rows - SENT] = values[i][rows - SENT] + weight * values[i - 2][rows - SENT - 1]
    for i in range(6):
        for y in range(SENT):
            top, bottom = values[i][y], values[i][rows - SENT + y]
            at = slice(i * SENT + y, i * SENT + y + 1)
            first[at] = jnp.where(even, top, bottom)
            second[at] = jnp.where(even, bottom, top)
    pairs = []
    for p, (i, j) in enumerate(((0, 1), (4, 5))):
        parts = []
        for g in range(OWN):
            sums = [
                jnp.concatenate([value[4 * g + 2 * q] + value[4 * g + 2 * q + 1] for q in (0, 1)], axis=0)
                for value in (values[i], values[j])
            ]
            parts.append(restrict_01(*sums))
        pairs.append(jnp.concatenate(parts, axis=0))
        coarse[p * OWN : (p + 1) * OWN] = pairs[p]
        for ref in (first, second):
            ref[FIELDS1 + p * OWN : FIELDS1 + (p + 1) * OWN] = pairs[p]
    uv, fk = (restrict_12([pair[j : j + 1] for j in range(OWN)]) for pair in pairs)
    both = jnp.where((sub_of() & 2) == 0, uv, fk)
    coarse[2 * OWN : 2 * OWN + 1] = both
    for ref in (first, second):
        ref[FIELDS2 : FIELDS2 + 1] = both


def split_fields2(both):
    low = (sub_of() & 2) == 0
    return jnp.where(low, both, roll_z(both, 2)), jnp.where(low, roll_z(both, -2), both)


def write_spread(fields, coarse, out):
    lane = lax.broadcasted_iota(jnp.int32, (1, X), 1)
    cross, squared, inv_u, inv_v, _, _ = jacobian(*fields, 0)
    tops = [jnp.max(jnp.maximum((6.0 * DIFF[0] + cross) * inv_u, (6.0 * DIFF[1] + squared) * inv_v), axis=0)]
    tops.append(jnp.max(packed_spread(coarse[0:OWN], coarse[OWN : 2 * OWN], 1), axis=0))
    tops.append(packed_spread(*split_fields2(coarse[2 * OWN : 2 * OWN + 1]), 2)[0])
    result = jnp.zeros((1, X), jnp.float32)
    for level, top in enumerate(tops):
        top = jnp.max(jnp.max(top, axis=0, keepdims=True), axis=1, keepdims=True)
        result = jnp.where(lane == level, jnp.broadcast_to(top, (1, X)), result)
    out[...] = jnp.broadcast_to(result[None], out.shape)


GROUPS1 = HI1 - LO1
GROUPS2 = HI2 - LO2


def tiles_for(entries):
    return -(-entries // PER)


def pack_edges(entries, even, first, second):
    lane = lane_of()
    share = first.shape[0]
    left, right = None, None
    for j in range(PER):
        part = entries[j * share : (j + 1) * share]
        a, b = roll_x(part, WIDE * j), roll_x(part, WIDE + WIDE * j)
        left = a if left is None else jnp.where(lane >= WIDE * j, a, left)
        right = b if right is None else jnp.where(lane >= WIDE * j, b, right)
    first[...] = jnp.where(even, left, right)
    second[...] = jnp.where(even, right, left)


def halo_tiles(even, packets, lo, hi):
    first, second = packets
    share = first.shape[0]
    lane = lane_of()
    out = []
    for j in range(PER):
        a, b = max(lo, j * share), min(hi, (j + 1) * share)
        if a < b:
            strip = slice(a - j * share, b - j * share)
            left, right = prev_of(even, first, second, strip), next_of(even, first, second, strip)
            value = jnp.where(lane < X // 2, roll_x(right, -WIDE * j), roll_x(left, X - WIDE - WIDE * j))
            out.append((a - lo, b - lo, value))
    return out


def pack_own_kernel(
    rows, state, previous, feed, kill, coarse, first, second, spread, main, held, copies, sem
):
    inputs = (state, previous, feed, kill)

    def field(i):
        j, f = SOURCES[i]
        return jnp.stack([plane(inputs[j], f, y, rows) for y in range(rows)])

    fields = {i: field(i) for i in (0, 1, 4, 5)}
    write_spread([fields[i] for i in (0, 1, 4, 5)], coarse, copies)
    copy = pltpu.make_async_copy(copies, spread, sem)
    copy.start()

    @pl.when(lax.axis_index("gx") >= 0)
    def _():
        for i in range(6):
            value = field(i)
            main[i] = value
            held[i * rows : (i + 1) * rows] = value
        held[6 * rows : 6 * rows + 2 * OWN + 1] = coarse[...]
        pack_edges(held, is_even("gx"), first, second)

    copy.wait()


def pack_corner_kernel(y_first, y_second, first, second, held):
    even = is_even("gy")
    every = slice(0, PACKET)
    held[0:PACKET] = prev_of(even, y_first, y_second, every)
    held[PACKET : 2 * PACKET] = next_of(even, y_first, y_second, every)
    pack_edges(held, is_even("gx"), first, second)


EDGE_TILES = 2 * EDGE + 1


def level0_setup(fields, keep, diag, power, r, n):
    at = pl.ds(r, n)
    u, nb_u = neighbour_sums(lambda t, a, m: fields[0, t, pl.ds(a, m)], r, n, 1)
    v, nb_v = neighbour_sums(lambda t, a, m: fields[1, t, pl.ds(a, m)], r, n, 1)
    for t in (0, 1):
        f, k = fields[4, t, at], fields[5, t, at]
        cross, squared, inv_u, inv_v, first, second = jacobian(u[t], v[t], f, k, 0)
        react = u[t] * squared
        b_u = DIFF[0] * (nb_u[t] - 6.0 * u[t]) - INV_STEP * (u[t] - fields[2, t, at]) - react + f * (1.0 - u[t])
        b_v = DIFF[1] * (nb_v[t] - 6.0 * v[t]) - INV_STEP * (v[t] - fields[3, t, at]) + react - (f + k) * v[t]
        for i, value in enumerate((cross, squared, inv_u, inv_v, b_u, b_v)):
            keep[i, t, at] = value
        for i, value in enumerate((first, second)):
            diag[i, t, at] = value
        for i, value in enumerate((inv_u * b_u, inv_v * b_v)):
            power[i, t, at] = value


def level0_power(keep, source, target, r, n):
    for i, values in enumerate(next_power(keep, source, r, n)):
        for t in (0, 1):
            target[i, t, pl.ds(r, n)] = values[t]


def level0_down(keep, diag, y1, y2, sources, r, n):
    at = pl.ds(r, n)
    last = next_power(keep, y2, r, n)
    for t in (0, 1):
        both = [diag[i, t, at] for i in (0, 1)]
        parts = [[keep[4 + i, t, at] for i in (0, 1)]]
        parts += [[both[i] * power[i, t, at] for i in (0, 1)] for power in (y1, y2)]
        parts.append([both[i] * last[i][t] for i in (0, 1)])
        for q, part in enumerate(parts):
            u, v = (pair_rows(value) for value in part)
            for j in range(n // 4):
                value = restrict_01(u[2 * j : 2 * j + 2], v[2 * j : 2 * j + 2])
                sources[q, t, pl.ds((r - HALO0) // 4 + j, 1)] = value


def inner(rows, lost):
    return slice(HALO0 + lost, HALO0 + rows - lost)


def ends(rows, lo, hi):
    total = rows + 2 * HALO0
    return slice(lo, hi), slice(total - hi, total - lo)


def put_ends(target, rows, lo, hi, source):
    n = hi - lo
    for at, part in zip(ends(rows, lo, hi), (slice(0, n), slice(n, 2 * n))):
        for i in range(target.shape[0]):
            for t in (0, 1):
                target[i, t, at] = source[i, t, part]


def take_ends(source, rows, lo, hi, target):
    n = hi - lo
    for at, part in zip(ends(rows, lo, hi), (slice(0, n), slice(n, 2 * n))):
        for i in range(source.shape[0]):
            for t in (0, 1):
                target[i, t, part] = source[i, t, at]


def level0_inner_kernel(rows, main, own_a, own_b, keep_in, y0_in, y1_in, y2_in, diag_in, sources_in, *scratch):
    fields, keep, diag, y0, y1, y2 = scratch
    even_x = is_even("gx")
    for i in range(6):
        fields[i, 0, HALO0 : HALO0 + rows] = main[i]
        for a, b, value in halo_tiles(even_x, (own_a, own_b), i * rows, (i + 1) * rows):
            fields[i, 1, HALO0 + a : HALO0 + b] = value
    first = HALO0 + 1
    level0_setup(fields, keep, diag, y0, first, rows - 2)
    level0_power(keep, y0, y1, first + 1, rows - 4)
    level0_power(keep, y1, y2, first + 2, rows - 6)
    level0_down(keep, diag, y1, y2, sources_in, first + 3, rows - 8)
    for source, target, lost in ((keep, keep_in, 1), (y1, y1_in, 2), (y2, y2_in, 3)):
        for i in range(source.shape[0]):
            for t in (0, 1):
                target[i, t] = source[i, t, inner(rows, lost)]
    take_ends(y0, rows, HALO0 + 1, HALO0 + 3, y0_in)
    take_ends(diag, rows, HALO0 + 1, HALO0 + 4, diag_in)


def level0_outer_kernel(
    rows,
    main,
    y_first,
    y_second,
    own_a,
    own_b,
    corner_a,
    corner_b,
    keep_in,
    y0_in,
    y1_in,
    y2_in,
    diag_in,
    sources_in,
    keep_out,
    y1_out,
    y2_out,
    sources,
    edges,
    *scratch,
):
    fields, keep, diag, y0, y1, y2 = scratch
    even, even_x = is_even("gy"), is_even("gx")
    total = rows + 2 * HALO0
    near, skip = HALO0 + 2, HALO0 - SENT
    for i in range(6):
        strip = slice(i * SENT, (i + 1) * SENT)
        fields[i, 0, skip:HALO0] = prev_of(even, y_first, y_second, strip)
        fields[i, 0, HALO0:near] = main[i, 0:2]
        fields[i, 0, total - near : total - HALO0] = main[i, rows - 2 : rows]
        fields[i, 0, HALO0 + rows : total - skip] = next_of(even, y_first, y_second, strip)
        for packets, lo, n, at in (
            ((corner_a, corner_b), i * SENT, SENT, skip),
            ((own_a, own_b), i * rows, 2, HALO0),
            ((own_a, own_b), (i + 1) * rows - 2, 2, total - near),
            ((corner_a, corner_b), PACKET + i * SENT, SENT, HALO0 + rows),
        ):
            for a, b, value in halo_tiles(even_x, packets, lo, lo + n):
                fields[i, 1, at + a : at + b] = value
    for i in (0, 1):
        for t in (0, 1):
            for at in (0, total - 1):
                fields[i, t, at] = jnp.zeros((Z, X), jnp.float32)
    for at, part in zip(ends(rows, 5, 8), (slice(0, 3), slice(rows - 5, rows - 2))):
        for i in range(6):
            for t in (0, 1):
                keep[i, t, at] = keep_in[i, t, part]
    put_ends(diag, rows, 5, 8, diag_in)
    put_ends(y0, rows, 5, 7, y0_in)
    for target, source, lost in ((y1, y1_in, 2), (y2, y2_in, 3)):
        n = rows - 2 * lost
        for at, part in zip(ends(rows, HALO0 + lost, HALO0 + lost + 2), (slice(0, 2), slice(n - 2, n))):
            for i in (0, 1):
                for t in (0, 1):
                    target[i, t, at] = source[i, t, part]
    for r in (1, total - 5):
        level0_setup(fields, keep, diag, y0, r, 4)
    for r in (2, total - 6):
        level0_power(keep, y0, y1, r, 4)
    for r in (3, total - 7):
        level0_power(keep, y1, y2, r, 4)
    for r in (4, total - 8):
        level0_down(keep, diag, y1, y2, sources, r, 4)
    for q in range(4):
        for t in (0, 1):
            sources[q, t, 1 : OWN - 1] = sources_in[q, t, 1 : OWN - 1]
    take_ends(keep, rows, 1, 5, keep_out)
    take_ends(y1, rows, 4, 6, y1_out)
    take_ends(y2, rows, 4, 7, y2_out)
    for p, power in enumerate((y0, y1, y2)):
        for side, start in enumerate((HALO0, HALO0 + rows - EDGE)):
            edges[p, side] = pack_rows(power, start)


def pack_rows(x, start):
    lane = lane_of()
    halo = None
    for i in (0, 1):
        for j in range(EDGE):
            at = i * EDGE + j
            value = roll_x(x[i, 1, start + j : start + j + 1], 4 + 8 * at)
            halo = value if halo is None else jnp.where((lane >> 3) == at, value, halo)
    return jnp.concatenate([x[i, 0, start : start + EDGE] for i in (0, 1)] + [halo], axis=0)


def squeeze(halo):
    lane = lane_of()
    last = halo[OWN - 1 : OWN]
    ahead = (lane >= WIDE) & (lane < 2 * WIDE)
    parts = [jnp.where(ahead, roll_x(last, WIDE), halo[0:1]), jnp.where(ahead, roll_x(last, 2 * WIDE - X), halo[1:2])]
    return jnp.concatenate(parts + [halo[2 : OWN - 1]], axis=0)


def unsqueeze(tiles):
    last = jnp.where(lane_of() < X // 2, roll_x(tiles[0:1], -WIDE), roll_x(tiles[1:2], X - 2 * WIDE))
    return jnp.concatenate([tiles, last], axis=0)


def combine_kernel(sources, edges, spread, own, first, second, edge_first, edge_second, gain):
    write_gains(jnp.max(spread[...], axis=0)[0:1], gain)
    p0, p1, p2 = (gain[POWERS + i] for i in range(3))
    for t in (0, 1):
        value = sources[0, t] - p0 * sources[1, t] + p1 * sources[2, t] - p2 * sources[3, t]
        own[t] = value
        for ref in (first, second):
            if t == 0:
                ref[0:OWN] = value
            else:
                ref[OWN:] = squeeze(value)
    even = is_even("gy")
    top, bottom = (p0 * edges[0, side] - p1 * edges[1, side] + p2 * edges[2, side] for side in (0, 1))
    edge_first[...] = jnp.where(even, top, bottom)
    edge_second[...] = jnp.where(even, bottom, top)


def coarse1_kernel(
    rows, coarse, y_first, y_second, own_a, own_b, corner_a, corner_b, gain, keep_in, y1_in, y2_in, keep_out, y1_out, y2_out,
    coef, keep0, x0, fields
):
    even, even_x = is_even("gy"), is_even("gx")
    own_x, corner_x = (own_a, own_b), (corner_a, corner_b)
    for p in (0, 1):
        to = p * GROUPS1
        strip = slice(FIELDS1 + p * OWN, FIELDS1 + (p + 1) * OWN)
        fields[0, to : to + OWN] = prev_of(even, y_first, y_second, strip)
        fields[0, to + OWN : to + 2 * OWN] = coarse[p * OWN : (p + 1) * OWN]
        fields[0, to + 2 * OWN : to + 3 * OWN] = next_of(even, y_first, y_second, strip)
        for part, (packets, lo) in enumerate(
            ((corner_x, FIELDS1), (own_x, 6 * rows), (corner_x, PACKET + FIELDS1))
        ):
            lo += p * OWN
            for a, b, value in halo_tiles(even_x, packets, lo, lo + OWN):
                fields[1, to + part * OWN + a : to + part * OWN + b] = value
    for t in (0, 1):
        for i, value in enumerate(packed_jacobian(fields[t, 0:GROUPS1], fields[t, GROUPS1 : 2 * GROUPS1], 1)):
            coef[i, t, 1 : SIZE1 - 1] = value

    def whole(inside, outside):
        n = outside.shape[0] // 2
        return jnp.concatenate([outside[0:n], inside, outside[n:]], axis=0)

    for i in range(6):
        for t in (0, 1):
            keep0[i, t, 1 : rows + 2 * HALO0 - 1] = whole(keep_in[i, t], keep_out[i, t])
    p0, p1, p2 = (gain[POWERS + i] for i in range(3))
    for i in (0, 1):
        for t in (0, 1):
            y0 = keep0[2 + i, t, HALO0 : HALO0 + rows] * keep0[4 + i, t, HALO0 : HALO0 + rows]
            y1, y2 = (whole(a[i, t], b[i, t]) for a, b in ((y1_in, y1_out), (y2_in, y2_out)))
            x0[i, t] = p0 * y0 - p1 * y1 + p2 * y2


def fields2_kernel(rows, coarse, y_first, y_second, own_a, own_b, corner_a, corner_b, out):
    even, even_x = is_even("gy"), is_even("gx")
    own_x, corner_x = (own_a, own_b), (corner_a, corner_b)
    near = slice(FIELDS2, FIELDS2 + 1)
    out[0, 0:1] = prev_of(even, y_first, y_second, near)
    out[0, 1:2] = coarse[2 * OWN : 2 * OWN + 1]
    out[0, 2:3] = next_of(even, y_first, y_second, near)
    for q, (packets, lo) in enumerate(
        ((corner_x, FIELDS2), (own_x, 6 * rows + 2 * OWN), (corner_x, PACKET + FIELDS2))
    ):
        out[1, q : q + 1] = halo_tiles(even_x, packets, lo, lo + 1)[0][2]


def level1_kernel(
    own, first, second, edge_a, edge_b, fields2, coef1, gain, packet, to_first, to_second, to_far_a, to_far_b, keep, y1, d1
):
    b1, x1 = keep.at[0], keep.at[1]
    even = is_even("gy")
    for t in (0, 1):
        b1[t, 1 + OWN : 1 + 2 * OWN] = own[t]
        for at, take in ((1, prev_of), (1 + 2 * OWN, next_of)):
            if t == 0:
                b1[t, at : at + OWN] = take(even, first, second, slice(0, OWN))
            else:
                b1[t, at : at + OWN] = unsqueeze(take(even, first, second, slice(OWN, 2 * OWN - 1)))
    g0, g1, g2 = (gain[3 + i] for i in range(3))
    n = GROUPS1
    packed_first(coef1, 0, b1, x1, d1, 1, n, g0)
    packed_step(1, coef1, 0, b1, x1, y1, d1, 2, n - 2, CARRY1, g1)
    packed_step(1, coef1, 0, b1, y1, x1, d1, 2, n - 2, CARRY2, g2)
    here = pl.ds(1 + OWN, OWN)
    values = []
    for t, (c, other, spread) in enumerate(packed_terms(x1, 1 + OWN, OWN, 1)):
        res = b1[t, here] - coef1[2, t, here] * c + coef1[1, t, here] * other + spread
        values.append(restrict_12([res[j : j + 1] for j in range(OWN)]))
        for ref in (to_far_a, to_far_b):
            ref[1 + t : 2 + t] = fields2[t, 1:2]
    value = jnp.where((sub_of() & 2) == 0, values[0], values[1])
    for ref in (packet, to_first, to_second, to_far_a, to_far_b):
        ref[0:1] = value
    for ref in (to_far_a, to_far_b):
        ref[3:] = jnp.broadcast_to(value, (ref.shape[0] - 3, Z, X))
    to_first[1:] = edge_a[...]
    to_second[1:] = edge_b[...]


def rest_kernel(
    own2, near_a, near_b, far_a, far_b, gain, coef1, fields2, keep0, iterate, keep1, out, coef2, d1, b2, x2, y2, d2, xu, yu, x0, y0, d0
):
    rows = out.shape[0] // (2 * Z)
    even = (sub_of() & 1) == 0
    b1, x1 = keep1.at[0], keep1.at[1]

    even_y, low = is_even("gy"), lax.rem(lax.axis_index("gy"), 4) < 2
    at = slice(0, 1)
    parts = [
        next_of(low, far_a, far_b, at),
        prev_of(even_y, near_a, near_b, at),
        own2[at],
        next_of(even_y, near_a, near_b, at),
        prev_of(low, far_a, far_b, at),
    ]
    for t, values in enumerate(split_fields2(jnp.concatenate(parts, axis=0))):
        b2[t, 1 : SIZE2 - 1] = values
        at = slice(1 + t, 2 + t)
        parts = [next_of(low, far_a, far_b, at), fields2[t], prev_of(low, far_a, far_b, at)]
        inverse, other, _ = packed_jacobian(*split_fields2(jnp.concatenate(parts, axis=0)), 2)
        coef2[0, t, 1 : SIZE2 - 1] = inverse
        coef2[1, t, 1 : SIZE2 - 1] = other

    n = HI2 - LO2
    g0, g1, g2 = (gain[6 + i] for i in range(3))
    packed_first(coef2, 0, b2, x2, d2, 1, n, g0)
    packed_step(2, coef2, 0, b2, x2, y2, d2, 1, n, CARRY1, g1)
    packed_step(2, coef2, 0, b2, y2, x2, d2, 1, n, CARRY2, g2)
    packed_step(2, coef2, 0, b2, x2, y2, d2, 1, n, None, g0)
    packed_step(2, coef2, 0, b2, y2, x2, d2, 2, n - 2, CARRY1, g1)
    packed_step(2, coef2, 0, b2, x2, y2, d2, 2, n - 2, CARRY2, g2)

    g0, g1, g2 = (gain[3 + i] for i in range(3))
    shift = LO_UP - LO1
    for t in (0, 1):
        for g in range(LO_UP, HI_UP):
            p = g % 4
            value = y2[t, g // 4 - LO2 + 1 : g // 4 - LO2 + 2]
            value = spread_x(spread_x(value, 1, p & 1), 2, p & 2)
            at = g - LO_UP + 1
            xu[t, at : at + 1] = x1[t, at + shift : at + shift + 1] + value
    n = HI_UP - LO_UP
    packed_step(1, coef1, shift, b1, xu, yu, d1, 2, n - 2, None, g0)
    packed_step(1, coef1, shift, b1, yu, xu, d1, 2, n - 2, CARRY1, g1)
    packed_step(1, coef1, shift, b1, xu, yu, d1, 3, n - 4, CARRY2, g2)

    g0, g1, g2 = (gain[i] for i in range(3))
    sides = [take(even_y, near_a, near_b, slice(1, 1 + EDGE_TILES)) for take in (prev_of, next_of)]

    def before(i, t, y):
        if 0 <= y < rows:
            return iterate[i, t, y : y + 1]
        side, j = (sides[0], y + EDGE) if y < 0 else (sides[1], y - rows)
        if t == 0:
            return side[i * EDGE + j : i * EDGE + j + 1]
        return roll_x(side[2 * EDGE :], -(4 + 8 * (i * EDGE + j)))

    for t in (0, 1):
        for row in range(-2, rows // 2 + 2):
            at = row // 2 - LO_UP + 1
            value = spread_x(yu[t, at : at + 1], 1, row & 1)
            for i, fine in enumerate((jnp.where(even, value, roll_z(value, 1)), jnp.where(even, roll_z(value, -1), value))):
                for y in (2 * row, 2 * row + 1):
                    if -EDGE <= y < rows + EDGE:
                        x0[i, t, y + HALO0 : y + HALO0 + 1] = before(i, t, y) + fine
    total = rows + 2 * HALO0
    for r, n in chunks(2, total - 2):
        cheb_step(0, keep0, x0, y0, d0, r, n, None, g0)
    for r, n in chunks(3, total - 3):
        cheb_step(0, keep0, y0, x0, d0, r, n, CARRY1, g1)
    for r, n in chunks(4, total - 4):
        last = cheb_step(0, keep0, x0, None, d0, r, n, CARRY2, g2, (0,))[0]
        for i in (0, 1):
            for j in range(n):
                out[pl.ds(i * Z * rows + r - HALO0 + j, Z, stride=rows), :] = last[i][j]


def call(kernel, out_shapes, scratch, *args, space=pltpu.VMEM, outs=None):
    out = [jax.ShapeDtypeStruct(shape, jnp.float32) for shape in out_shapes]
    return pl.pallas_call(
        kernel,
        out_shape=out,
        in_specs=[pl.BlockSpec(memory_space=space)] * len(args),
        out_specs=[pl.BlockSpec(memory_space=m) for m in outs or [pltpu.VMEM] * len(out)],
        scratch_shapes=[pltpu.VMEM(s, jnp.float32) if isinstance(s, tuple) else s for s in scratch],
        compiler_params=pltpu.CompilerParams(vmem_limit_bytes=24 * 2**20),
    )(*args)


def swap(value, axis, step):
    count = lax.axis_size(axis)
    assert count % 2 == 0
    pairs = [(i, (i + step) % count) for i in range(0, count, 2)]
    return lax.ppermute(value, axis, pairs + [(j, i) for i, j in pairs])


def swap_far(value, axis, step):
    count = lax.axis_size(axis)
    assert count % 4 == 0
    pairs = [(i + j, (i + j + 2 * step) % count) for i in range(0, count, 4) for j in (0, 1)]
    return lax.ppermute(value, axis, pairs + [(j, i) for i, j in pairs])


def exchange(first, second, axis):
    return swap(first, axis, -1), swap(second, axis, 1)


def body(state, previous, feed, kill):
    _, depth, rows, cols = state.shape
    assert depth == Z and cols == X and rows == 4 * OWN
    across, count = lax.axis_size("gx"), lax.axis_size("gy")
    total0 = rows + 2 * HALO0
    state = state.reshape(2 * Z * rows, X)
    previous = previous.reshape(2 * Z * rows, X)
    feed = feed.reshape(Z * rows, X)
    kill = kill.reshape(Z * rows, X)
    inputs = (state, previous, feed, kill)

    strip = (PACKET, Z, X)
    first, second, coarse, *inputs = call(
        functools.partial(first_kernel, rows),
        [strip, strip, (2 * OWN + 1, Z, X), *(a.shape for a in inputs)],
        [pltpu.SemaphoreType.DMA((4,))],
        *(pltpu.with_memory_space_constraint(a, pltpu.HBM) for a in inputs),
        space=pltpu.HBM,
    )
    y_packets = exchange(first, second, "gy")

    tiles = tiles_for(6 * rows + 2 * OWN + 1)
    spread_shape = (across * count, Z // 2, X)
    first, second, spread, main = call(
        functools.partial(pack_own_kernel, rows),
        [(tiles, Z, X), (tiles, Z, X), spread_shape, (6, rows, Z, X)],
        [(PER * tiles, Z, X), spread_shape, pltpu.SemaphoreType.DMA],
        *inputs,
        coarse,
        outs=[pltpu.VMEM, pltpu.VMEM, pltpu.HBM, pltpu.VMEM],
    )
    own_x = exchange(first, second, "gx")
    spread = lax.all_to_all(spread, ("gx", "gy"), 0, 0, tiled=True)
    tiles = tiles_for(2 * PACKET)
    corner_x = exchange(
        *call(pack_corner_kernel, [(tiles, Z, X), (tiles, Z, X)], [(PER * tiles, Z, X)], *y_packets), "gx"
    )

    strip, edge = (2 * OWN - 1, Z, X), (EDGE_TILES, Z, X)
    pair0 = (2, 2, total0, Z, X)
    work = [(6, 2, total0, Z, X), (6, 2, total0, Z, X), pair0, pair0, pair0, pair0]
    four = (4, 2, OWN, Z, X)
    inside = call(
        functools.partial(level0_inner_kernel, rows),
        [
            (6, 2, rows - 2, Z, X),
            (2, 2, 4, Z, X),
            (2, 2, rows - 4, Z, X),
            (2, 2, rows - 6, Z, X),
            (2, 2, 6, Z, X),
            four,
        ],
        work,
        main,
        *own_x,
    )
    keep_in, _, y1_in, y2_in, _, _ = inside
    keep_out, y1_out, y2_out, sources, edges = call(
        functools.partial(level0_outer_kernel, rows),
        [(6, 2, 8, Z, X), (2, 2, 4, Z, X), (2, 2, 6, Z, X), four, (3, 2, *edge)],
        work,
        main,
        *y_packets,
        *own_x,
        *corner_x,
        *inside,
    )
    own, first, second, edge_a, edge_b, gain = call(
        combine_kernel,
        [(2, OWN, Z, X), strip, strip, edge, edge, (POWERS + 3, Z, X)],
        [],
        sources,
        edges,
        spread,
    )
    coef1, keep0, iterate = call(
        functools.partial(coarse1_kernel, rows),
        [(3, 2, SIZE1, Z, X), (6, 2, total0, Z, X), (2, 2, rows, Z, X)],
        [(2, 2 * GROUPS1, Z, X)],
        coarse,
        *y_packets,
        *own_x,
        *corner_x,
        gain,
        keep_in,
        y1_in,
        y2_in,
        keep_out,
        y1_out,
        y2_out,
    )
    (fields2,) = call(
        functools.partial(fields2_kernel, rows), [(2, 3, Z, X)], [], coarse, *y_packets, *own_x, *corner_x
    )
    b_packets = exchange(first, second, "gy")

    one, two, up = (2, SIZE1, Z, X), (2, SIZE2, Z, X), (2, SIZE_UP, Z, X)
    near = (1 + EDGE_TILES, Z, X)
    packet, first, second, far_a, far_b, keep1 = call(
        level1_kernel,
        [(1, Z, X), near, near, (near[0] + 1, Z, X), (near[0] + 2, Z, X), (2, *one)],
        [one, one],
        own,
        *b_packets,
        edge_a,
        edge_b,
        fields2,
        coef1,
        gain,
    )
    far = (swap_far(far_a, "gy", 1), swap_far(far_b, "gy", -1))
    near = exchange(first, second, "gy")

    (out,) = call(
        rest_kernel,
        [(2 * Z * rows, X)],
        [(2, *two), one, two, two, two, two, up, up, pair0, pair0, pair0],
        packet,
        *near,
        *far,
        gain,
        coef1,
        fields2,
        keep0,
        iterate,
        keep1,
    )
    return out.reshape(2, Z, rows, X)


def solution(mesh):
    placed = (
        P(None, None, "gy", "gx"),
        P(None, None, "gy", "gx"),
        P(None, "gy", "gx"),
        P(None, "gy", "gx"),
    )
    return jax.shard_map(
        body, mesh=mesh, in_specs=placed, out_specs=P(None, None, "gy", "gx"), check_vma=False
    )
```
